32 devices in a mesh: section: 2 (over x), seq: 4 (over y, core), blk: 4 (over z).
Axes of the slice: x: 2, y: 2, z: 4, core: 2. Of those that a mesh axis runs over, the one named last changes fastest.
Arguments:
- inputs: bfloat16 [2, 1, 1024, 1536], P(None, None, ('seq', 'blk')), may hold values from -6 to 6
- cotangent: bfloat16 [2, 1, 1024, 1536], P(None, None, ('seq', 'blk')), may hold values from -6 to 6
- doc_lengths: int32 [2, 1, 4], replicated, may hold values from 0 to 1024, as said below
- attention_gain: bfloat16 [2, 1536], P('section', 'blk'), may hold values from 0.099609375 to 1.8984375
- w_query: bfloat16 [2, 1536, 1536], P('section', 'blk'), may hold values from -0.15625 to 0.15625
- w_key: bfloat16 [2, 1536, 768], P('section', 'blk'), may hold values from -0.15625 to 0.15625
- w_value: bfloat16 [2, 1536, 768], P('section', 'blk'), may hold values from -0.15625 to 0.15625
- w_output: bfloat16 [2, 1536, 1536], P('section', 'blk'), may hold values from -1.75 to 1.75
- mlp_gain: bfloat16 [2, 1536], P('section', 'blk'), may hold values from 0.099609375 to 1.8984375
- w_gate: bfloat16 [2, 1536, 4096], P('section', 'blk'), may hold values from -0.15625 to 0.15625
- w_up: bfloat16 [2, 1536, 4096], P('section', 'blk'), may hold values from -0.15625 to 0.15625
- w_down: bfloat16 [2, 4096, 1536], P('section', 'blk'), may hold values from -0.09375 to 0.09375
Outputs:
- activations: bfloat16 [2, 2, 1, 1024, 1536], P('section', None, None, ('seq', 'blk'))
- input_grads: bfloat16 [2, 2, 1, 1024, 1536], P('section', None, None, ('seq', 'blk'))
- grad_attention_gain: float32 [2, 1536], P('section', 'blk')
- grad_w_query: float32 [2, 1536, 1536], P('section', 'blk')
- grad_w_key: float32 [2, 1536, 768], P('section', 'blk')
- grad_w_value: float32 [2, 1536, 768], P('section', 'blk')
- grad_w_output: float32 [2, 1536, 1536], P('section', 'blk')
- grad_mlp_gain: float32 [2, 1536], P('section', 'blk')
- grad_w_gate: float32 [2, 1536, 4096], P('section', 'blk')
- grad_w_up: float32 [2, 1536, 4096], P('section', 'blk')
- grad_w_down: float32 [2, 4096, 1536], P('section', 'blk')
The draws below stay inside these ranges and needn't reach their ends.
Inputs may be any that keep to these rules, and one draw needn't show every extreme that they name: `doc_lengths`: the 4 lengths of a sequence sum to 1024. Of all sequences, one drawn from the seed is a single document (1024 then zeros); in every other sequence each length is 1 or more.
All inputs are finite; a program needn't handle non-finite values.
Results may differ from the reference program's by a relative error of at most 0.028.
Values may be sent and summed in bfloat16 or wider, within the bound.
A program may use at most 448 MiB of HBM per device.

```python
import jax
import jax.numpy as jnp
from jax import lax

HEADS = 16
KV_HEADS = 8
HEAD_DIM = 96
FF = 4096
D = 1536
SEQS = 1
MICRO = 2
DOCS = 4
SEQ_LEN = 1024
N_SEQ = 4


def draw_doc_lengths(key, part):
    key = jax.random.fold_in(key, 7)
    key_cut, key_whole = jax.random.split(key)
    row_count = MICRO * SEQS

    def one_row(row_key):
        cut_points = jnp.sort(jax.random.permutation(row_key, SEQ_LEN - 1)[:DOCS - 1] + 1).astype(jnp.int32)
        edge_points = jnp.concatenate([jnp.zeros((1,), jnp.int32), cut_points, jnp.full((1,), SEQ_LEN, jnp.int32)])
        return (edge_points[1:] - edge_points[:-1]).astype(jnp.int32)
    split_rows = jax.vmap(one_row)(jax.random.split(key_cut, row_count))
    whole_row = jax.random.randint(key_whole, (), 0, row_count)
    single = jnp.concatenate([jnp.full((1,), SEQ_LEN, jnp.int32), jnp.zeros((DOCS - 1,), jnp.int32)])
    is_whole = (jnp.arange(row_count) == whole_row)[:, None]
    picked = jnp.where(is_whole, single[None, :], split_rows)
    return picked.reshape(MICRO, SEQS, DOCS).astype(jnp.int32)


def level_of(own_key, dims, pieces, least, high):
    def one(dim, parts):
        heights = jax.random.uniform(jax.random.fold_in(jax.random.fold_in(own_key, 6), dim), (parts,), jnp.float32, least / len(pieces), high / len(pieces))
        return jnp.repeat(jnp.exp(heights), dims[dim] // parts).reshape((-1,) + (1,) * (len(dims) - dim - 1))

    gain = one(*pieces[0])
    for cut in pieces[1:]:
        gain = gain * one(*cut)
    return gain


def normal_values(key, shape, scale, bound, shards=(), held_as=jnp.bfloat16):
    result = scale * jax.random.normal(key, shape, jnp.float32)
    if shards:
        result = result * level_of(key, shape, shards, -0.22, 0.18)
    return jnp.clip(result, -bound, bound).astype(held_as)


def setup_inputs(seed: int = 0) -> dict:
    streams_of = jax.random.split(jax.random.key(seed), 13)
    return {
        "inputs": normal_values(streams_of[0], (MICRO, SEQS, SEQ_LEN, D), 1.0, 6.0, ((2, 16),)),
        "cotangent": normal_values(streams_of[1], (MICRO, SEQS, SEQ_LEN, D), 1.0, 6.0, ((2, 16),)),
        "doc_lengths": draw_doc_lengths(jax.random.fold_in(streams_of[12], 71), 0),
        "attention_gain": jnp.clip(1.0 + 0.18 * jax.random.normal(streams_of[3], (2, D), jnp.float32), 0.099609375, 1.8984375).astype(jnp.bfloat16),
        "w_query": normal_values(streams_of[4], (2, D, D), D ** -0.5, 0.15625, ((0, 2), (1, 4))),
        "w_key": normal_values(streams_of[5], (2, D, KV_HEADS * HEAD_DIM), D ** -0.5, 0.15625, ((0, 2), (1, 4))),
        "w_value": normal_values(streams_of[6], (2, D, KV_HEADS * HEAD_DIM), D ** -0.5, 0.15625, ((0, 2), (1, 4))),
        "w_output": normal_values(streams_of[7], (2, D, D), (max(D // 128, 1)) ** -0.5, 1.75, ((0, 2), (1, 4))),
        "mlp_gain": jnp.clip(1.0 + 0.18 * jax.random.normal(streams_of[8], (2, D), jnp.float32), 0.099609375, 1.8984375).astype(jnp.bfloat16),
        "w_gate": normal_values(streams_of[9], (2, D, FF), D ** -0.5, 0.15625, ((0, 2), (1, 4))),
        "w_up": normal_values(streams_of[10], (2, D, FF), D ** -0.5, 0.15625, ((0, 2), (1, 4))),
        "w_down": normal_values(streams_of[11], (2, FF, D), FF ** -0.5, 0.09375, ((0, 2), (1, 4))),
    }


EPS = 1e-05
THETA = 100000.0
MASKED = -1e+30

@jax.custom_vjp
def low(v):
    return lax.optimization_barrier(v.astype(jnp.bfloat16)).astype(jnp.float32)

@jax.custom_vjp
def low_back(v):
    return v

def low_keep(v):
    return (low(v), None)

def low_pass(kept, grad):
    return (grad,)

def back_keep(v):
    return (v, None)

def back_low(kept, grad):
    return (low(grad),)
low.defvjp(low_keep, low_pass)
low_back.defvjp(back_keep, back_low)

def highest(left_side, right_side):
    return jnp.dot(left_side, right_side, precision=lax.Precision.HIGHEST, preferred_element_type=jnp.float32)

def doc_info(lengths, token_index):
    doc_ends = jnp.cumsum(lengths, axis=-1).astype(jnp.int32)
    passed = (doc_ends[..., None, :] <= token_index[..., None]).astype(jnp.int32)
    segment = lax.optimization_barrier(jnp.sum(passed, axis=-1)).astype(jnp.int32)
    offset = lax.optimization_barrier(jnp.sum(passed * lengths[..., None, :], axis=-1)).astype(jnp.int32)
    return (segment, (token_index - offset).astype(jnp.int32))

def rotate(field_in, position, turn_sign):
    half_dim = field_in.shape[-1] // 2
    frequency = THETA ** (-2.0 * jnp.arange(half_dim, dtype=jnp.float32) / field_in.shape[-1])
    angles = position.astype(jnp.float32)[:, None] * frequency
    cosine = jnp.cos(angles)[:, None, :]
    sine_part = turn_sign * jnp.sin(angles)[:, None, :]
    first_half = field_in[..., :half_dim]
    second_half = field_in[..., half_dim:]
    return jnp.concatenate([first_half * cosine - second_half * sine_part, second_half * cosine + first_half * sine_part], axis=-1)

def rms_forward(field_in, gain_row):
    return field_in * lax.rsqrt(lax.optimization_barrier(jnp.mean(field_in * field_in, axis=-1, keepdims=True)) + EPS) * gain_row

def layer(row_in, lengths, params):
    gain_attn, w_query, w_key, w_value, w_output, gain_mlp, w_gate, w_up, w_down = params
    copies = max(1, N_SEQ // KV_HEADS)
    group_size = HEADS // (KV_HEADS * copies)
    token_index = jnp.arange(SEQ_LEN, dtype=jnp.int32)
    segment, position = doc_info(lengths, token_index)
    normed = low(rms_forward(row_in, gain_attn))
    query_pre = low_back(highest(normed, w_query)).reshape(SEQ_LEN, HEADS, HEAD_DIM)
    key_pre = low_back(highest(normed, w_key)).reshape(SEQ_LEN, KV_HEADS, HEAD_DIM)
    value_pre = low_back(highest(normed, w_value)).reshape(SEQ_LEN, KV_HEADS, HEAD_DIM)
    queries = low_back(low(rotate(query_pre, position, 1.0)))
    key_heads = low_back(jnp.repeat(low(rotate(key_pre, position, 1.0)), copies, axis=1))
    value_heads = low_back(jnp.repeat(low(value_pre), copies, axis=1))
    key_full = jnp.repeat(key_heads, group_size, axis=1)
    value_full = jnp.repeat(value_heads, group_size, axis=1)
    block_rows = min(512, SEQ_LEN)

    def attend(first_row):
        query_rows = lax.dynamic_slice_in_dim(queries, first_row, block_rows, 0)
        row_seg = lax.dynamic_slice_in_dim(segment, first_row, block_rows, 0)
        row_index = first_row + jnp.arange(block_rows, dtype=jnp.int32)
        scores = low_back(jnp.einsum('qhd,khd->hqk', query_rows, key_full, precision=lax.Precision.HIGHEST) * HEAD_DIM ** (-0.5))
        allowed = (row_seg[:, None] == segment[None, :]) & (token_index[None, :] <= row_index[:, None])
        scores = jnp.where(allowed[None], scores, MASKED)
        row_top = lax.optimization_barrier(jnp.max(scores, axis=-1, keepdims=True))
        log_total = row_top + jnp.log(lax.optimization_barrier(jnp.sum(jnp.exp(scores - row_top), axis=-1, keepdims=True)))
        attn_probs = low(jnp.exp(scores - log_total))
        return jnp.einsum('hqk,khd->qhd', attn_probs, value_full, precision=lax.Precision.HIGHEST)
    starts = jnp.arange(SEQ_LEN // block_rows, dtype=jnp.int32) * block_rows
    mixed_heads = lax.map(jax.checkpoint(attend), starts).reshape(SEQ_LEN, HEADS * HEAD_DIM)
    attn_out = low_back(low(mixed_heads))
    hidden = row_in + low_back(highest(attn_out, w_output))
    normed_mlp = low(rms_forward(hidden, gain_mlp))
    gate_pre = low_back(highest(normed_mlp, w_gate))
    up_pre = low_back(highest(normed_mlp, w_up))
    act_low = low(jax.nn.silu(gate_pre) * up_pre)
    return hidden + low_back(highest(act_low, w_down))

def run_section(section_in, lengths, params):

    def one_row(row_pair):
        return layer(row_pair[0], row_pair[1], params)
    return lax.map(jax.checkpoint(one_row), (section_in, lengths))

def reference(inputs, cotangent, doc_lengths, attention_gain, w_query, w_key, w_value, w_output, mlp_gain, w_gate, w_up, w_down):
    row_count = MICRO * SEQS
    start_rows = inputs.astype(jnp.float32).reshape(row_count, SEQ_LEN, D)
    lengths = doc_lengths.reshape(row_count, DOCS).astype(jnp.int32)
    params = tuple((weight.astype(jnp.float32) for weight in (attention_gain, w_query, w_key, w_value, w_output, mlp_gain, w_gate, w_up, w_down)))
    first_params = tuple((weight[0] for weight in params))
    second_params = tuple((weight[1] for weight in params))
    between_zero = jnp.zeros((row_count, SEQ_LEN, D), jnp.float32)

    def forward(section_in, added_zero, params_one, params_two):
        between = low_back(low(run_section(section_in, lengths, params_one))) + added_zero
        return (run_section(between, lengths, params_two), between)
    final_out, pullback, between = jax.vjp(forward, start_rows, between_zero, first_params, second_params, has_aux=True)
    grad_start, grad_between, grads_one, grads_two = pullback(cotangent.astype(jnp.float32).reshape(row_count, SEQ_LEN, D))
    shape_out = (2, MICRO, SEQS, SEQ_LEN, D)
    activations = jnp.stack([between, final_out]).reshape(shape_out).astype(jnp.bfloat16)
    input_grads = jnp.stack([grad_start, grad_between]).reshape(shape_out).astype(jnp.bfloat16)
    weight_grads = tuple((jnp.stack([first_grad, second_grad]) for first_grad, second_grad in zip(grads_one, grads_two)))
    return (activations, input_grads, weight_grads[0], weight_grads[1], weight_grads[2], weight_grads[3], weight_grads[4], weight_grads[5], weight_grads[6], weight_grads[7], weight_grads[8])
```

```python
import jax
import jax.numpy as jnp
from jax import lax
from jax.sharding import PartitionSpec as P

HEADS = 16
KV_HEADS = 8
HEAD_DIM = 96


EPS = 1e-05
THETA = 100000.0
MASKED = -1e30


def passed_along(value, axis, steps):
    count = lax.axis_size(axis)
    first, last = (max(0, -steps), min(count, count - steps))
    return lax.ppermute(value, axis, [(source, source + steps) for source in range(first, last)])


def shortened(value):
    return jax.tree.map(lambda a: a.astype(jnp.bfloat16) if a.dtype == jnp.float32 else a, value)


def product(left_side, right_side):
    return jnp.dot(left_side, right_side, preferred_element_type=jnp.float32)


def back_product(left_side, right_side):
    return lax.dot_general(
        left_side, right_side, (((1,), (1,)), ((), ())), preferred_element_type=jnp.float32
    )


def doc_info(lengths, token_index):
    doc_ends = jnp.cumsum(lengths, axis=-1)
    passed = (doc_ends[..., None, :] <= token_index[..., None]).astype(jnp.int32)
    segment = jnp.sum(passed, axis=-1)
    offset = jnp.sum(passed * lengths[..., None, :], axis=-1)
    return (segment, token_index - offset)


def rotate(field_in, position, turn_sign):
    half_dim = field_in.shape[-1] // 2
    frequency = THETA ** (-2.0 * jnp.arange(half_dim, dtype=jnp.float32) / field_in.shape[-1])
    angles = position.astype(jnp.float32)[:, None] * frequency
    cosine = jnp.cos(angles)[:, None, :]
    sine_part = turn_sign * jnp.sin(angles)[:, None, :]
    first_half = field_in[..., :half_dim]
    second_half = field_in[..., half_dim:]
    return jnp.concatenate(
        [
            first_half * cosine - second_half * sine_part,
            second_half * cosine + first_half * sine_part,
        ],
        axis=-1,
    )


def rms_forward(field_in, gain_row):
    inv_root = lax.rsqrt(jnp.mean(field_in * field_in, axis=-1, keepdims=True) + EPS)
    return (field_in * inv_root * gain_row, inv_root)


def rms_backward(field_in, gain_row, inv_root, grad_normed):
    scaled = gain_row * grad_normed
    grad_field = inv_root * scaled - field_in * inv_root**3 * jnp.mean(
        scaled * field_in, axis=-1, keepdims=True
    )
    return (grad_field, grad_normed * field_in * inv_root)


def token_place(block_id, row_ids, per_device, blk_count):
    return (row_ids // per_device * blk_count + block_id) * per_device + row_ids % per_device


def masks_for(lengths, blk_index, per_device, blk_count, seq_count):
    block_tokens = seq_count * per_device
    row_ids = jnp.arange(block_tokens, dtype=jnp.int32)
    query_index = token_place(blk_index, row_ids, per_device, blk_count)
    all_ids = jnp.arange(blk_count * block_tokens, dtype=jnp.int32)
    key_index = token_place(all_ids // block_tokens, all_ids % block_tokens, per_device, blk_count)
    query_seg, _ = doc_info(lengths, query_index)
    key_seg, _ = doc_info(lengths, key_index)
    return (query_index, key_index, query_seg, key_seg)


def head_scores(queries, key_rows, allowed, kv_local):
    grouped = queries.reshape(queries.shape[0], kv_local, -1, HEAD_DIM)
    key_heads = key_rows.reshape(key_rows.shape[0], kv_local, HEAD_DIM)
    scores = jnp.einsum(
        "rkgd,lkd->kgrl", grouped, key_heads, preferred_element_type=jnp.float32
    ) * HEAD_DIM ** (-0.5)
    return (jnp.where(allowed, scores, MASKED), grouped, key_heads)


def attend_forward(operands, query_index, key_index, kv_local):
    queries, key_rows, value_rows, query_seg, key_seg = operands
    allowed = (query_seg[:, None] == key_seg[None, :]) & (
        key_index[None, :] <= query_index[:, None]
    )
    scores, grouped, key_heads = head_scores(queries, key_rows, allowed, kv_local)
    row_top = jnp.max(scores, axis=-1, keepdims=True)
    log_total = row_top + jnp.log(jnp.sum(jnp.exp(scores - row_top), axis=-1, keepdims=True))
    weights_low = jnp.exp(scores - log_total).astype(jnp.bfloat16)
    value_heads = value_rows.reshape(value_rows.shape[0], kv_local, HEAD_DIM)
    mixed_heads = jnp.einsum(
        "kgrl,lkd->rkgd", weights_low, value_heads, preferred_element_type=jnp.float32
    )
    return (mixed_heads.reshape(queries.shape).astype(jnp.bfloat16), log_total)


def attend_backward(operands, query_index, key_index, kv_local):
    queries, key_rows, value_rows, grad_mixed, log_total, query_seg, key_seg = operands
    allowed = (query_seg[:, None] == key_seg[None, :]) & (
        key_index[None, :] <= query_index[:, None]
    )
    scores, grouped, key_heads = head_scores(queries, key_rows, allowed, kv_local)
    attn_probs = jnp.exp(scores - log_total)
    value_heads = value_rows.reshape(value_rows.shape[0], kv_local, HEAD_DIM)
    grad_heads = grad_mixed.reshape(grouped.shape)
    grad_values = jnp.einsum(
        "kgrl,rkgd->lkd",
        attn_probs.astype(jnp.bfloat16),
        grad_heads,
        preferred_element_type=jnp.float32,
    )
    grad_probs = jnp.einsum(
        "rkgd,lkd->kgrl", grad_heads, value_heads, preferred_element_type=jnp.float32
    )
    centre = jnp.sum(attn_probs * grad_probs, axis=-1, keepdims=True)
    grad_scores = (attn_probs * (grad_probs - centre)).astype(jnp.bfloat16)
    grad_queries = jnp.einsum(
        "kgrl,lkd->rkgd", grad_scores, key_heads, preferred_element_type=jnp.float32
    ) * HEAD_DIM ** (-0.5)
    grad_keys = jnp.einsum(
        "kgrl,rkgd->lkd", grad_scores, grouped, preferred_element_type=jnp.float32
    ) * HEAD_DIM ** (-0.5)
    return (
        grad_queries.reshape(queries.shape).astype(jnp.bfloat16),
        grad_keys.reshape(key_rows.shape),
        grad_values.reshape(value_rows.shape),
    )


def layer_forward(section_in, lengths, weights, placing):
    shard_id, blk_index, seq_count, blk_count = placing
    gain_attn, w_query, w_key, w_value, w_output, gain_mlp, w_gate, w_up, w_down = weights
    seqs_here, per_device, width = section_in.shape
    token_rows = seqs_here * per_device
    copies = max(1, seq_count // KV_HEADS)
    kv_local = KV_HEADS * copies // seq_count
    token_index = shard_id * per_device + jnp.arange(per_device, dtype=jnp.int32)
    _, position = doc_info(lengths, token_index)
    position = position.reshape(token_rows)
    flat_in = section_in.reshape(token_rows, width)
    normed, inv_first = rms_forward(flat_in, gain_attn.astype(jnp.float32))
    normed_low = normed.astype(jnp.bfloat16)
    query_pre = product(normed_low, w_query).reshape(token_rows, HEADS, HEAD_DIM)
    key_pre = product(normed_low, w_key).reshape(token_rows, KV_HEADS, HEAD_DIM)
    value_pre = product(normed_low, w_value).reshape(token_rows, KV_HEADS, HEAD_DIM)
    query_rot = (
        rotate(query_pre, position, 1.0).astype(jnp.bfloat16).reshape(seqs_here, per_device, width)
    )
    key_rot = rotate(key_pre, position, 1.0).astype(jnp.bfloat16)
    spread_shape = (token_rows, KV_HEADS, copies, HEAD_DIM)
    key_rep = jnp.broadcast_to(key_rot[:, :, None, :], spread_shape).reshape(
        seqs_here, per_device, -1
    )
    value_rep = jnp.broadcast_to(
        value_pre.astype(jnp.bfloat16)[:, :, None, :], spread_shape
    ).reshape(seqs_here, per_device, -1)
    heads_query, heads_key, heads_value = (
        lax.all_to_all(query_rot, "seq", split_axis=2, concat_axis=1, tiled=True),
        lax.all_to_all(key_rep, "seq", split_axis=2, concat_axis=1, tiled=True),
        lax.all_to_all(value_rep, "seq", split_axis=2, concat_axis=1, tiled=True),
    )
    keys_all, values_all = (
        lax.all_gather(heads_key, "blk", axis=1, tiled=True),
        lax.all_gather(heads_value, "blk", axis=1, tiled=True),
    )
    query_index, key_index, query_seg, key_seg = masks_for(
        lengths, blk_index, per_device, blk_count, seq_count
    )
    heads_mixed, log_total = lax.map(
        lambda operands: attend_forward(operands, query_index, key_index, kv_local),
        (heads_query, keys_all, values_all, query_seg, key_seg),
    )
    token_mixed = lax.all_to_all(
        heads_mixed, "seq", split_axis=1, concat_axis=2, tiled=True
    ).reshape(token_rows, width)
    hidden = flat_in + product(token_mixed, w_output)
    normed_mlp, inv_second = rms_forward(hidden, gain_mlp.astype(jnp.float32))
    normed_mlp_low = normed_mlp.astype(jnp.bfloat16)
    gate_pre = product(normed_mlp_low, w_gate)
    up_pre = product(normed_mlp_low, w_up)
    act_low = (jax.nn.silu(gate_pre) * up_pre).astype(jnp.bfloat16)
    result = hidden + product(act_low, w_down)
    saved_state = (
        flat_in,
        normed_low,
        inv_first,
        position,
        heads_query,
        keys_all,
        values_all,
        log_total,
        token_mixed,
        hidden,
        inv_second,
        normed_mlp_low,
        gate_pre,
        up_pre,
        act_low,
        lengths,
    )
    return (result.reshape(section_in.shape), saved_state)


def layer_backward(upstream, saved_state, weights, placing):
    shard_id, blk_index, seq_count, blk_count = placing
    gain_attn, w_query, w_key, w_value, w_output, gain_mlp, w_gate, w_up, w_down = weights
    (
        flat_in,
        normed_low,
        inv_first,
        position,
        heads_query,
        keys_all,
        values_all,
        log_total,
        token_mixed,
        hidden,
        inv_second,
        normed_mlp_low,
        gate_pre,
        up_pre,
        act_low,
        lengths,
    ) = saved_state
    seqs_here, per_device, width = upstream.shape
    token_rows = seqs_here * per_device
    copies = max(1, seq_count // KV_HEADS)
    kv_local = KV_HEADS * copies // seq_count
    grad_rows = upstream.reshape(token_rows, width)
    grad_out_low = grad_rows.astype(jnp.bfloat16)
    grad_act = back_product(grad_out_low, w_down)
    gate_sigmoid = jax.nn.sigmoid(gate_pre)
    grad_gate_low = (
        grad_act * up_pre * gate_sigmoid * (1.0 + gate_pre * (1.0 - gate_sigmoid))
    ).astype(jnp.bfloat16)
    grad_up_low = (grad_act * jax.nn.silu(gate_pre)).astype(jnp.bfloat16)
    grad_normed_mlp = back_product(grad_gate_low, w_gate) + back_product(grad_up_low, w_up)
    grad_hidden_part, gain_mlp_terms = rms_backward(
        hidden, gain_mlp.astype(jnp.float32), inv_second, grad_normed_mlp
    )
    grad_hidden = grad_rows + grad_hidden_part
    grad_branch_low = grad_hidden.astype(jnp.bfloat16)
    grad_mixed_low = (
        back_product(grad_branch_low, w_output)
        .astype(jnp.bfloat16)
        .reshape(seqs_here, per_device, width)
    )
    heads_grad = lax.all_to_all(grad_mixed_low, "seq", split_axis=2, concat_axis=1, tiled=True)
    query_index, key_index, query_seg, key_seg = masks_for(
        lengths, blk_index, per_device, blk_count, seq_count
    )
    grad_heads_query, grad_keys_all, grad_values_all = lax.map(
        lambda operands: attend_backward(operands, query_index, key_index, kv_local),
        (heads_query, keys_all, values_all, heads_grad, log_total, query_seg, key_seg),
    )
    grad_key_own, grad_value_own = (
        lax.psum_scatter(
            grad_keys_all.astype(jnp.bfloat16), "blk", scatter_dimension=1, tiled=True
        ).astype(jnp.float32),
        lax.psum_scatter(
            grad_values_all.astype(jnp.bfloat16), "blk", scatter_dimension=1, tiled=True
        ).astype(jnp.float32),
    )
    token_query, token_key, token_value = (
        lax.all_to_all(grad_heads_query, "seq", split_axis=1, concat_axis=2, tiled=True),
        lax.all_to_all(
            grad_key_own.astype(jnp.bfloat16), "seq", split_axis=1, concat_axis=2, tiled=True
        ),
        lax.all_to_all(
            grad_value_own.astype(jnp.bfloat16), "seq", split_axis=1, concat_axis=2, tiled=True
        ),
    )
    grad_key_sum = jnp.sum(
        token_key.astype(jnp.float32).reshape(token_rows, KV_HEADS, copies, HEAD_DIM), axis=2
    )
    grad_value_sum = jnp.sum(
        token_value.astype(jnp.float32).reshape(token_rows, KV_HEADS, copies, HEAD_DIM), axis=2
    )
    grad_query_low = (
        rotate(token_query.astype(jnp.float32).reshape(token_rows, HEADS, HEAD_DIM), position, -1.0)
        .astype(jnp.bfloat16)
        .reshape(token_rows, width)
    )
    grad_key_low = (
        rotate(grad_key_sum, position, -1.0)
        .astype(jnp.bfloat16)
        .reshape(token_rows, KV_HEADS * HEAD_DIM)
    )
    grad_value_low = grad_value_sum.astype(jnp.bfloat16).reshape(token_rows, KV_HEADS * HEAD_DIM)
    grad_normed = (
        back_product(grad_query_low, w_query)
        + back_product(grad_key_low, w_key)
        + back_product(grad_value_low, w_value)
    )
    grad_in_part, gain_attn_terms = rms_backward(
        flat_in, gain_attn.astype(jnp.float32), inv_first, grad_normed
    )
    grad_input = (grad_hidden + grad_in_part).reshape(upstream.shape)
    weight_rows = (
        gain_attn_terms,
        normed_low,
        grad_query_low,
        grad_key_low,
        grad_value_low,
        token_mixed,
        grad_branch_low,
        gain_mlp_terms,
        normed_mlp_low,
        grad_gate_low,
        grad_up_low,
        act_low,
        grad_out_low,
    )
    return (grad_input, weight_rows)


def weight_term(inputs_low, outputs_low):
    if outputs_low is None:
        return jnp.sum(inputs_low, axis=0)
    return lax.dot_general(
        inputs_low, outputs_low, (((0,), (0,)), ((), ())), preferred_element_type=jnp.float32
    )


def shards(
    inputs,
    cotangent,
    doc_lengths,
    attention_gain,
    w_query,
    w_key,
    w_value,
    w_output,
    mlp_gain,
    w_gate,
    w_up,
    w_down,
):
    at_first = lax.axis_index("section") == 0
    seq_count = lax.axis_size("seq")
    blk_count = lax.axis_size("blk")
    blk_index = lax.axis_index("blk")
    shard_id = lax.axis_index("seq") * blk_count + blk_index
    placing = (shard_id, blk_index, seq_count, blk_count)
    micro_count = inputs.shape[0]
    local_shards = (
        attention_gain[0],
        w_query[0],
        w_key[0],
        w_value[0],
        w_output[0],
        mlp_gain[0],
        w_gate[0],
        w_up[0],
        w_down[0],
    )
    weights = (
        lax.all_gather(local_shards[0], "blk", axis=0, tiled=True),
        lax.all_gather(local_shards[1], "blk", axis=0, tiled=True),
        lax.all_gather(local_shards[2], "blk", axis=0, tiled=True),
        lax.all_gather(local_shards[3], "blk", axis=0, tiled=True),
        lax.all_gather(local_shards[4], "blk", axis=0, tiled=True),
        lax.all_gather(local_shards[5], "blk", axis=0, tiled=True),
        lax.all_gather(local_shards[6], "blk", axis=0, tiled=True),
        lax.all_gather(local_shards[7], "blk", axis=0, tiled=True),
        lax.all_gather(local_shards[8], "blk", axis=0, tiled=True),
    )
    received = jnp.zeros(inputs.shape[1:], jnp.bfloat16)
    saved_states = []
    section_outs = []
    for tick_index in range(micro_count + 1):
        fresh_input = inputs[min(tick_index, micro_count - 1)]
        section_in = jnp.where(at_first, fresh_input, received).astype(jnp.float32)
        lengths = jnp.where(
            at_first,
            doc_lengths[min(tick_index, micro_count - 1)],
            doc_lengths[max(tick_index - 1, 0)],
        )
        result, saved_state = layer_forward(section_in, lengths, weights, placing)
        result_low = result.astype(jnp.bfloat16)
        if tick_index < micro_count:
            received = passed_along(result_low, "section", 1)
        saved_states.append(saved_state)
        section_outs.append(result_low)
    weights = (
        lax.all_gather(local_shards[0], "blk", axis=0, tiled=True),
        lax.all_gather(local_shards[1], "blk", axis=0, tiled=True),
        lax.all_gather(local_shards[2], "blk", axis=0, tiled=True),
        lax.all_gather(local_shards[3], "blk", axis=0, tiled=True),
        lax.all_gather(local_shards[4], "blk", axis=0, tiled=True),
        lax.all_gather(local_shards[5], "blk", axis=0, tiled=True),
        lax.all_gather(local_shards[6], "blk", axis=0, tiled=True),
        lax.all_gather(local_shards[7], "blk", axis=0, tiled=True),
        lax.all_gather(local_shards[8], "blk", axis=0, tiled=True),
    )
    back_in = jnp.zeros(cotangent.shape[1:], jnp.bfloat16)
    grad_outs = []
    row_sets = []
    for tick_index in range(micro_count + 1):
        saved_state = jax.tree.map(
            lambda first_pick, second_pick: jnp.where(at_first, first_pick, second_pick),
            saved_states[max(tick_index - 1, 0)],
            saved_states[min(tick_index + 1, micro_count)],
        )
        upstream = jnp.where(at_first, back_in, cotangent[min(tick_index, micro_count - 1)]).astype(
            jnp.float32
        )
        grad_input, weight_rows = layer_backward(upstream, saved_state, weights, placing)
        grad_low = grad_input.astype(jnp.bfloat16)
        if tick_index < micro_count:
            back_in = passed_along(grad_low, "section", -1)
        grad_outs.append(grad_low)
        row_sets.append(weight_rows)
    activations = jnp.stack(
        [
            jnp.where(at_first, section_outs[index_m], section_outs[index_m + 1])
            for index_m in range(micro_count)
        ]
    )[None]
    input_grads = jnp.stack(
        [
            jnp.where(at_first, grad_outs[index_m + 1], grad_outs[index_m])
            for index_m in range(micro_count)
        ]
    )[None]
    picked = [
        jax.tree.map(
            lambda first_pick, second_pick: jnp.where(at_first, first_pick, second_pick),
            row_sets[index_m + 1],
            row_sets[index_m],
        )
        for index_m in range(micro_count)
    ]
    merged = jax.tree.map(lambda *pieces: jnp.concatenate(pieces, axis=0), *picked)
    (
        gain_attn_terms,
        normed_low,
        grad_query_low,
        grad_key_low,
        grad_value_low,
        token_mixed,
        grad_branch_low,
        gain_mlp_terms,
        normed_mlp_low,
        grad_gate_low,
        grad_up_low,
        act_low,
        grad_out_low,
    ) = merged
    grad_pairs = (
        (gain_attn_terms, None),
        (normed_low, grad_query_low),
        (normed_low, grad_key_low),
        (normed_low, grad_value_low),
        (token_mixed, grad_branch_low),
        (gain_mlp_terms, None),
        (normed_mlp_low, grad_gate_low),
        (normed_mlp_low, grad_up_low),
        (act_low, grad_out_low),
    )
    shares = tuple(
        (
            lax.psum_scatter(
                weight_term(left_side, right_side).astype(jnp.bfloat16),
                "blk",
                scatter_dimension=0,
                tiled=True,
            ).astype(jnp.float32)
            for left_side, right_side in grad_pairs
        )
    )
    shares = jax.tree.map(lambda part: part.astype(jnp.float32), lax.psum(shortened(shares), "seq"))
    return (
        activations,
        input_grads,
        shares[0][None],
        shares[1][None],
        shares[2][None],
        shares[3][None],
        shares[4][None],
        shares[5][None],
        shares[6][None],
        shares[7][None],
        shares[8][None],
    )


def group_gather(block):
    return lax.all_gather(block, ("seq", "blk"), axis=0, tiled=True)


def group_scatter(partial):
    return lax.psum_scatter(
        partial.astype(jnp.bfloat16), ("seq", "blk"), scatter_dimension=0, tiled=True
    ).astype(jnp.float32)


def turn(field_in, cosine, sine):
    half_dim = HEAD_DIM // 2
    first_half = field_in[:, :half_dim]
    second_half = field_in[:, half_dim:]
    return jnp.concatenate(
        [first_half * cosine - second_half * sine, second_half * cosine + first_half * sine],
        axis=-1,
    )


def swapped(own, kept_here):
    return lax.ppermute(own, "section", [(0, 1), (1, 0)])


def spread_weights(local_shards):
    seq_index = lax.axis_index("seq")
    seq_count = lax.axis_size("seq")
    blk_count = lax.axis_size("blk")
    gain_attn, w_query, w_key, w_value, w_output, gain_mlp, w_gate, w_up, w_down = local_shards
    rows = w_query.shape[0]

    def mine(weight, width, per_blk, place):
        return lax.dynamic_index_in_dim(
            weight.reshape(rows, blk_count, per_blk, width), place, 2, keepdims=False
        )

    kv_per_blk = KV_HEADS // blk_count
    kv_place = seq_index * kv_per_blk // seq_count
    ff_width = w_gate.shape[1] // (seq_count * blk_count)
    attn = jnp.concatenate(
        [
            mine(w_query, HEAD_DIM, seq_count, seq_index),
            mine(w_key, HEAD_DIM, kv_per_blk, kv_place),
            mine(w_value, HEAD_DIM, kv_per_blk, kv_place),
        ],
        axis=-1,
    ).transpose(1, 2, 0)
    gains = jnp.stack([gain_attn, gain_mlp])
    attn = jnp.concatenate(
        [attn, jnp.broadcast_to(gains[None], (blk_count,) + gains.shape)], axis=1
    )
    wide = jnp.concatenate(
        [mine(w_gate, ff_width, seq_count, seq_index), mine(w_up, ff_width, seq_count, seq_index)],
        axis=-1,
    ).transpose(1, 0, 2)
    attn = lax.all_to_all(attn, "blk", split_axis=0, concat_axis=2, tiled=True)[0]
    wide = lax.all_to_all(wide, "blk", split_axis=0, concat_axis=1, tiled=True)[0]
    out_rows = w_output.shape[0] // seq_count
    down_rows = w_down.shape[0] // seq_count
    out = lax.dynamic_slice_in_dim(w_output, seq_index * out_rows, out_rows, 0)
    down = lax.dynamic_slice_in_dim(w_down, seq_index * down_rows, down_rows, 0)
    return attn, out, wide, down


def own_layer(x_own, weights, info):
    attn, out, wide, down = weights
    allowed, cosine, sine = info
    gain_attn = attn[3 * HEAD_DIM].astype(jnp.float32)
    gain_mlp = attn[3 * HEAD_DIM + 1].astype(jnp.float32)
    normed, inv_first = rms_forward(x_own, gain_attn)
    normed_all = group_gather(normed.astype(jnp.bfloat16))
    mixed_in = back_product(normed_all, attn[: 3 * HEAD_DIM])
    query = turn(mixed_in[:, :HEAD_DIM], cosine, sine).astype(jnp.bfloat16)
    key = turn(mixed_in[:, HEAD_DIM : 2 * HEAD_DIM], cosine, sine).astype(jnp.bfloat16)
    value = mixed_in[:, 2 * HEAD_DIM :].astype(jnp.bfloat16)
    scores = jnp.where(allowed, back_product(query, key) * HEAD_DIM ** (-0.5), MASKED)
    row_top = jnp.max(scores, axis=-1, keepdims=True)
    log_total = row_top + jnp.log(jnp.sum(jnp.exp(scores - row_top), axis=-1, keepdims=True))
    mixed = product(jnp.exp(scores - log_total).astype(jnp.bfloat16), value).astype(jnp.bfloat16)
    hidden = x_own + group_scatter(product(mixed, out))
    normed_mlp, inv_second = rms_forward(hidden, gain_mlp)
    normed_mlp_all = group_gather(normed_mlp.astype(jnp.bfloat16))
    pre = product(normed_mlp_all, wide)
    half = pre.shape[1] // 2
    gate_pre, up_pre = pre[:, :half], pre[:, half:]
    act_low = (jax.nn.silu(gate_pre) * up_pre).astype(jnp.bfloat16)
    result = hidden + group_scatter(product(act_low, down))
    saved = (
        x_own,
        inv_first,
        normed_all,
        query,
        key,
        value,
        log_total,
        mixed,
        hidden,
        inv_second,
        normed_mlp_all,
        gate_pre,
        up_pre,
        act_low,
    )
    return result, saved


def own_layer_back(grad_own, weights, info, saved):
    attn, out, wide, down = weights
    allowed, cosine, sine = info
    (
        x_own,
        inv_first,
        normed_all,
        query,
        key,
        value,
        log_total,
        mixed,
        hidden,
        inv_second,
        normed_mlp_all,
        gate_pre,
        up_pre,
        act_low,
    ) = saved
    gain_attn = attn[3 * HEAD_DIM].astype(jnp.float32)
    gain_mlp = attn[3 * HEAD_DIM + 1].astype(jnp.float32)
    grad_out_all = group_gather(grad_own.astype(jnp.bfloat16))
    grad_act = back_product(grad_out_all, down)
    gate_sigmoid = jax.nn.sigmoid(gate_pre)
    grad_gate = (
        grad_act * up_pre * gate_sigmoid * (1.0 + gate_pre * (1.0 - gate_sigmoid))
    ).astype(jnp.bfloat16)
    grad_up = (grad_act * jax.nn.silu(gate_pre)).astype(jnp.bfloat16)
    grad_wide = jnp.concatenate([grad_gate, grad_up], axis=1)
    grad_normed_mlp = group_scatter(back_product(grad_wide, wide))
    grad_hidden_part, gain_mlp_terms = rms_backward(hidden, gain_mlp, inv_second, grad_normed_mlp)
    grad_hidden = grad_own + grad_hidden_part
    grad_branch_all = group_gather(grad_hidden.astype(jnp.bfloat16))
    grad_mixed = back_product(grad_branch_all, out).astype(jnp.bfloat16)
    scores = jnp.where(allowed, back_product(query, key) * HEAD_DIM ** (-0.5), MASKED)
    probs = jnp.exp(scores - log_total)
    grad_probs = back_product(grad_mixed, value)
    centre = jnp.sum(probs * grad_probs, axis=-1, keepdims=True)
    grad_scores = (probs * (grad_probs - centre)).astype(jnp.bfloat16)
    grad_query = (product(grad_scores, key) * HEAD_DIM ** (-0.5)).astype(jnp.bfloat16)
    grad_key = weight_term(grad_scores, query) * HEAD_DIM ** (-0.5)
    grad_value = weight_term(probs.astype(jnp.bfloat16), grad_mixed).astype(jnp.bfloat16)
    grad_query = turn(grad_query.astype(jnp.float32), cosine, -sine).astype(jnp.bfloat16)
    grad_key = turn(grad_key, cosine, -sine).astype(jnp.bfloat16)
    grad_qkv = jnp.concatenate([grad_query, grad_key, grad_value], axis=1)
    grad_normed = group_scatter(product(grad_qkv, attn[: 3 * HEAD_DIM]))
    grad_in_part, gain_attn_terms = rms_backward(x_own, gain_attn, inv_first, grad_normed)
    grads = (
        weight_term(grad_qkv, normed_all),
        weight_term(mixed, grad_branch_all),
        weight_term(normed_mlp_all, grad_wide),
        weight_term(act_low, grad_out_all),
    )
    gains = jnp.stack([jnp.sum(gain_attn_terms, axis=0), jnp.sum(gain_mlp_terms, axis=0)])
    return grad_hidden + grad_in_part, grads, gains


def finish_grads(grads):
    seq_count = lax.axis_size("seq")
    blk_count = lax.axis_size("blk")
    attn, out, wide, down = grads
    attn = lax.all_to_all(attn[None], "blk", split_axis=2, concat_axis=0, tiled=True)
    wide = lax.all_to_all(wide[None], "blk", split_axis=1, concat_axis=0, tiled=True)
    attn, out, wide, down = [
        lax.all_gather(part, "seq", axis=0, tiled=False).astype(jnp.float32)
        for part in (attn, out, wide, down)
    ]
    rows = attn.shape[-1]
    query = attn[:, :, :HEAD_DIM].transpose(3, 1, 0, 2).reshape(rows, -1)

    def key_like(part):
        copies = HEADS // KV_HEADS
        part = part.reshape(seq_count // copies, copies, blk_count, HEAD_DIM, rows).sum(1)
        return part.transpose(3, 1, 0, 2).reshape(rows, -1)

    key = key_like(attn[:, :, HEAD_DIM : 2 * HEAD_DIM])
    value = key_like(attn[:, :, 2 * HEAD_DIM :])
    half = wide.shape[-1] // 2
    gate = wide[..., :half].transpose(2, 1, 0, 3).reshape(rows, -1)
    up = wide[..., half:].transpose(2, 1, 0, 3).reshape(rows, -1)
    return query, key, value, out.reshape(-1, out.shape[-1]), gate, up, down.reshape(
        -1, down.shape[-1]
    )


def head_shards(inputs, cotangent, doc_lengths, *params):
    section = lax.axis_index("section")
    at_first = section == 0
    blk_index = lax.axis_index("blk")
    tokens = inputs.shape[2] * lax.axis_size("seq") * lax.axis_size("blk")
    own = spread_weights(tuple(weight[0] for weight in params))
    other = tuple(swapped(part, None) for part in own)
    first = tuple(jnp.where(at_first, a, b) for a, b in zip(own, other))
    second = tuple(jnp.where(at_first, b, a) for a, b in zip(own, other))
    x_own = lax.dynamic_index_in_dim(inputs, section, 0, keepdims=False)[0].astype(jnp.float32)
    grad_own = lax.dynamic_index_in_dim(cotangent, section, 0, keepdims=False)[0].astype(
        jnp.float32
    )
    lengths = lax.dynamic_index_in_dim(doc_lengths, section, 0, keepdims=False)[0]
    token_index = jnp.arange(tokens, dtype=jnp.int32)
    segment, position = doc_info(lengths, token_index)
    allowed = (segment[:, None] == segment[None, :]) & (
        token_index[None, :] <= token_index[:, None]
    )
    half_dim = HEAD_DIM // 2
    frequency = THETA ** (-2.0 * jnp.arange(half_dim, dtype=jnp.float32) / HEAD_DIM)
    angles = position.astype(jnp.float32)[:, None] * frequency
    info = (allowed, jnp.cos(angles), jnp.sin(angles))
    result, saved_first = own_layer(x_own, first, info)
    between = result.astype(jnp.bfloat16)
    result, saved_second = own_layer(between.astype(jnp.float32), second, info)
    final = result.astype(jnp.bfloat16)
    grad_between, grads_second, gains_second = own_layer_back(grad_own, second, info, saved_second)
    grad_between = grad_between.astype(jnp.bfloat16)
    grad_start, grads_first, gains_first = own_layer_back(
        grad_between.astype(jnp.float32), first, info, saved_first
    )
    grad_start = grad_start.astype(jnp.bfloat16)

    def by_section(for_first, for_second):
        kept = jnp.where(at_first, for_first, for_second)
        received = swapped(jnp.where(at_first, for_second, for_first), None)
        return jnp.stack(
            [jnp.where(at_first, kept, received), jnp.where(at_first, received, kept)]
        )[None, :, None]

    activations = by_section(between, final)
    input_grads = by_section(grad_start, grad_between)
    summed = []
    for one, two in zip(grads_first, grads_second):
        kept = jnp.where(at_first, one, two)
        received = swapped(jnp.where(at_first, two, one).astype(jnp.bfloat16), None)
        summed.append((kept + received.astype(jnp.float32)).astype(jnp.bfloat16))
    query, key, value, out, gate, up, down = finish_grads(summed)
    gains = lax.psum(jnp.stack([gains_first, gains_second]), ("section", "seq", "blk"))
    gains = lax.dynamic_index_in_dim(gains, section, 0, keepdims=False)
    rows = params[1].shape[1]
    gains = lax.dynamic_slice_in_dim(gains, blk_index * rows, rows, 1)
    return (
        activations,
        input_grads,
        gains[0][None],
        query[None],
        key[None],
        value[None],
        out[None],
        gains[1][None],
        gate[None],
        up[None],
        down[None],
    )


def solution(mesh):
    placed = (
        P(None, None, ("seq", "blk"), None),
        P(None, None, ("seq", "blk"), None),
        P(),
        P("section", "blk"),
        P("section", "blk", None),
        P("section", "blk", None),
        P("section", "blk", None),
        P("section", "blk", None),
        P("section", "blk"),
        P("section", "blk", None),
        P("section", "blk", None),
        P("section", "blk", None),
    )
    one_head_each = mesh.shape["seq"] * mesh.shape["blk"] == HEADS
    return jax.shard_map(
        head_shards if one_head_each else shards,
        mesh=mesh,
        in_specs=placed,
        out_specs=(
            P("section", None, None, ("seq", "blk"), None),
            P("section", None, None, ("seq", "blk"), None),
            P("section", "blk"),
            P("section", "blk", None),
            P("section", "blk", None),
            P("section", "blk", None),
            P("section", "blk", None),
            P("section", "blk"),
            P("section", "blk", None),
            P("section", "blk", None),
            P("section", "blk", None),
        ),
        check_vma=False,
    )
```

```python
import functools

import jax
import jax.numpy as jnp
from jax import lax
from jax.experimental import pallas as pl
from jax.experimental.pallas import tpu as pltpu
from jax.sharding import PartitionSpec as P

HEADS = 16
KV_HEADS = 8
HEAD_DIM = 96


EPS = 1e-05
THETA = 100000.0
MASKED = -1e30


def passed_along(value, axis, steps):
    count = lax.axis_size(axis)
    first, last = (max(0, -steps), min(count, count - steps))
    return lax.ppermute(value, axis, [(source, source + steps) for source in range(first, last)])


def shortened(value):
    return jax.tree.map(lambda a: a.astype(jnp.bfloat16) if a.dtype == jnp.float32 else a, value)


def product(left_side, right_side):
    return jnp.dot(left_side, right_side, preferred_element_type=jnp.float32)


def back_product(left_side, right_side):
    return lax.dot_general(
        left_side, right_side, (((1,), (1,)), ((), ())), preferred_element_type=jnp.float32
    )


def doc_info(lengths, token_index):
    doc_ends = jnp.cumsum(lengths, axis=-1)
    passed = (doc_ends[..., None, :] <= token_index[..., None]).astype(jnp.int32)
    segment = jnp.sum(passed, axis=-1)
    offset = jnp.sum(passed * lengths[..., None, :], axis=-1)
    return (segment, token_index - offset)


def rotate(field_in, position, turn_sign):
    half_dim = field_in.shape[-1] // 2
    frequency = THETA ** (-2.0 * jnp.arange(half_dim, dtype=jnp.float32) / field_in.shape[-1])
    angles = position.astype(jnp.float32)[:, None] * frequency
    cosine = jnp.cos(angles)[:, None, :]
    sine_part = turn_sign * jnp.sin(angles)[:, None, :]
    first_half = field_in[..., :half_dim]
    second_half = field_in[..., half_dim:]
    return jnp.concatenate(
        [
            first_half * cosine - second_half * sine_part,
            second_half * cosine + first_half * sine_part,
        ],
        axis=-1,
    )


def rms_forward(field_in, gain_row):
    inv_root = lax.rsqrt(jnp.mean(field_in * field_in, axis=-1, keepdims=True) + EPS)
    return (field_in * inv_root * gain_row, inv_root)


def rms_backward(field_in, gain_row, inv_root, grad_normed):
    scaled = gain_row * grad_normed
    grad_field = inv_root * scaled - field_in * inv_root**3 * jnp.mean(
        scaled * field_in, axis=-1, keepdims=True
    )
    return (grad_field, grad_normed * field_in * inv_root)


def token_place(block_id, row_ids, per_device, blk_count):
    return (row_ids // per_device * blk_count + block_id) * per_device + row_ids % per_device


def masks_for(lengths, blk_index, per_device, blk_count, seq_count):
    block_tokens = seq_count * per_device
    row_ids = jnp.arange(block_tokens, dtype=jnp.int32)
    query_index = token_place(blk_index, row_ids, per_device, blk_count)
    all_ids = jnp.arange(blk_count * block_tokens, dtype=jnp.int32)
    key_index = token_place(all_ids // block_tokens, all_ids % block_tokens, per_device, blk_count)
    query_seg, _ = doc_info(lengths, query_index)
    key_seg, _ = doc_info(lengths, key_index)
    return (query_index, key_index, query_seg, key_seg)


def head_scores(queries, key_rows, allowed, kv_local):
    grouped = queries.reshape(queries.shape[0], kv_local, -1, HEAD_DIM)
    key_heads = key_rows.reshape(key_rows.shape[0], kv_local, HEAD_DIM)
    scores = jnp.einsum(
        "rkgd,lkd->kgrl", grouped, key_heads, preferred_element_type=jnp.float32
    ) * HEAD_DIM ** (-0.5)
    return (jnp.where(allowed, scores, MASKED), grouped, key_heads)


def attend_forward(operands, query_index, key_index, kv_local):
    queries, key_rows, value_rows, query_seg, key_seg = operands
    allowed = (query_seg[:, None] == key_seg[None, :]) & (
        key_index[None, :] <= query_index[:, None]
    )
    scores, grouped, key_heads = head_scores(queries, key_rows, allowed, kv_local)
    row_top = jnp.max(scores, axis=-1, keepdims=True)
    log_total = row_top + jnp.log(jnp.sum(jnp.exp(scores - row_top), axis=-1, keepdims=True))
    weights_low = jnp.exp(scores - log_total).astype(jnp.bfloat16)
    value_heads = value_rows.reshape(value_rows.shape[0], kv_local, HEAD_DIM)
    mixed_heads = jnp.einsum(
        "kgrl,lkd->rkgd", weights_low, value_heads, preferred_element_type=jnp.float32
    )
    return (mixed_heads.reshape(queries.shape).astype(jnp.bfloat16), log_total)


def attend_backward(operands, query_index, key_index, kv_local):
    queries, key_rows, value_rows, grad_mixed, log_total, query_seg, key_seg = operands
    allowed = (query_seg[:, None] == key_seg[None, :]) & (
        key_index[None, :] <= query_index[:, None]
    )
    scores, grouped, key_heads = head_scores(queries, key_rows, allowed, kv_local)
    attn_probs = jnp.exp(scores - log_total)
    value_heads = value_rows.reshape(value_rows.shape[0], kv_local, HEAD_DIM)
    grad_heads = grad_mixed.reshape(grouped.shape)
    grad_values = jnp.einsum(
        "kgrl,rkgd->lkd",
        attn_probs.astype(jnp.bfloat16),
        grad_heads,
        preferred_element_type=jnp.float32,
    )
    grad_probs = jnp.einsum(
        "rkgd,lkd->kgrl", grad_heads, value_heads, preferred_element_type=jnp.float32
    )
    centre = jnp.sum(attn_probs * grad_probs, axis=-1, keepdims=True)
    grad_scores = (attn_probs * (grad_probs - centre)).astype(jnp.bfloat16)
    grad_queries = jnp.einsum(
        "kgrl,lkd->rkgd", grad_scores, key_heads, preferred_element_type=jnp.float32
    ) * HEAD_DIM ** (-0.5)
    grad_keys = jnp.einsum(
        "kgrl,rkgd->lkd", grad_scores, grouped, preferred_element_type=jnp.float32
    ) * HEAD_DIM ** (-0.5)
    return (
        grad_queries.reshape(queries.shape).astype(jnp.bfloat16),
        grad_keys.reshape(key_rows.shape),
        grad_values.reshape(value_rows.shape),
    )


def layer_forward(section_in, lengths, weights, placing):
    shard_id, blk_index, seq_count, blk_count = placing
    gain_attn, w_query, w_key, w_value, w_output, gain_mlp, w_gate, w_up, w_down = weights
    seqs_here, per_device, width = section_in.shape
    token_rows = seqs_here * per_device
    copies = max(1, seq_count // KV_HEADS)
    kv_local = KV_HEADS * copies // seq_count
    token_index = shard_id * per_device + jnp.arange(per_device, dtype=jnp.int32)
    _, position = doc_info(lengths, token_index)
    position = position.reshape(token_rows)
    flat_in = section_in.reshape(token_rows, width)
    normed, inv_first = rms_forward(flat_in, gain_attn.astype(jnp.float32))
    normed_low = normed.astype(jnp.bfloat16)
    query_pre = product(normed_low, w_query).reshape(token_rows, HEADS, HEAD_DIM)
    key_pre = product(normed_low, w_key).reshape(token_rows, KV_HEADS, HEAD_DIM)
    value_pre = product(normed_low, w_value).reshape(token_rows, KV_HEADS, HEAD_DIM)
    query_rot = (
        rotate(query_pre, position, 1.0).astype(jnp.bfloat16).reshape(seqs_here, per_device, width)
    )
    key_rot = rotate(key_pre, position, 1.0).astype(jnp.bfloat16)
    spread_shape = (token_rows, KV_HEADS, copies, HEAD_DIM)
    key_rep = jnp.broadcast_to(key_rot[:, :, None, :], spread_shape).reshape(
        seqs_here, per_device, -1
    )
    value_rep = jnp.broadcast_to(
        value_pre.astype(jnp.bfloat16)[:, :, None, :], spread_shape
    ).reshape(seqs_here, per_device, -1)
    heads_query, heads_key, heads_value = (
        lax.all_to_all(query_rot, "seq", split_axis=2, concat_axis=1, tiled=True),
        lax.all_to_all(key_rep, "seq", split_axis=2, concat_axis=1, tiled=True),
        lax.all_to_all(value_rep, "seq", split_axis=2, concat_axis=1, tiled=True),
    )
    keys_all, values_all = (
        lax.all_gather(heads_key, "blk", axis=1, tiled=True),
        lax.all_gather(heads_value, "blk", axis=1, tiled=True),
    )
    query_index, key_index, query_seg, key_seg = masks_for(
        lengths, blk_index, per_device, blk_count, seq_count
    )
    heads_mixed, log_total = lax.map(
        lambda operands: attend_forward(operands, query_index, key_index, kv_local),
        (heads_query, keys_all, values_all, query_seg, key_seg),
    )
    token_mixed = lax.all_to_all(
        heads_mixed, "seq", split_axis=1, concat_axis=2, tiled=True
    ).reshape(token_rows, width)
    hidden = flat_in + product(token_mixed, w_output)
    normed_mlp, inv_second = rms_forward(hidden, gain_mlp.astype(jnp.float32))
    normed_mlp_low = normed_mlp.astype(jnp.bfloat16)
    gate_pre = product(normed_mlp_low, w_gate)
    up_pre = product(normed_mlp_low, w_up)
    act_low = (jax.nn.silu(gate_pre) * up_pre).astype(jnp.bfloat16)
    result = hidden + product(act_low, w_down)
    saved_state = (
        flat_in,
        normed_low,
        inv_first,
        position,
        heads_query,
        keys_all,
        values_all,
        log_total,
        token_mixed,
        hidden,
        inv_second,
        normed_mlp_low,
        gate_pre,
        up_pre,
        act_low,
        lengths,
    )
    return (result.reshape(section_in.shape), saved_state)


def layer_backward(upstream, saved_state, weights, placing):
    shard_id, blk_index, seq_count, blk_count = placing
    gain_attn, w_query, w_key, w_value, w_output, gain_mlp, w_gate, w_up, w_down = weights
    (
        flat_in,
        normed_low,
        inv_first,
        position,
        heads_query,
        keys_all,
        values_all,
        log_total,
        token_mixed,
        hidden,
        inv_second,
        normed_mlp_low,
        gate_pre,
        up_pre,
        act_low,
        lengths,
    ) = saved_state
    seqs_here, per_device, width = upstream.shape
    token_rows = seqs_here * per_device
    copies = max(1, seq_count // KV_HEADS)
    kv_local = KV_HEADS * copies // seq_count
    grad_rows = upstream.reshape(token_rows, width)
    grad_out_low = grad_rows.astype(jnp.bfloat16)
    grad_act = back_product(grad_out_low, w_down)
    gate_sigmoid = jax.nn.sigmoid(gate_pre)
    grad_gate_low = (
        grad_act * up_pre * gate_sigmoid * (1.0 + gate_pre * (1.0 - gate_sigmoid))
    ).astype(jnp.bfloat16)
    grad_up_low = (grad_act * jax.nn.silu(gate_pre)).astype(jnp.bfloat16)
    grad_normed_mlp = back_product(grad_gate_low, w_gate) + back_product(grad_up_low, w_up)
    grad_hidden_part, gain_mlp_terms = rms_backward(
        hidden, gain_mlp.astype(jnp.float32), inv_second, grad_normed_mlp
    )
    grad_hidden = grad_rows + grad_hidden_part
    grad_branch_low = grad_hidden.astype(jnp.bfloat16)
    grad_mixed_low = (
        back_product(grad_branch_low, w_output)
        .astype(jnp.bfloat16)
        .reshape(seqs_here, per_device, width)
    )
    heads_grad = lax.all_to_all(grad_mixed_low, "seq", split_axis=2, concat_axis=1, tiled=True)
    query_index, key_index, query_seg, key_seg = masks_for(
        lengths, blk_index, per_device, blk_count, seq_count
    )
    grad_heads_query, grad_keys_all, grad_values_all = lax.map(
        lambda operands: attend_backward(operands, query_index, key_index, kv_local),
        (heads_query, keys_all, values_all, heads_grad, log_total, query_seg, key_seg),
    )
    grad_key_own, grad_value_own = (
        lax.psum_scatter(
            grad_keys_all.astype(jnp.bfloat16), "blk", scatter_dimension=1, tiled=True
        ).astype(jnp.float32),
        lax.psum_scatter(
            grad_values_all.astype(jnp.bfloat16), "blk", scatter_dimension=1, tiled=True
        ).astype(jnp.float32),
    )
    token_query, token_key, token_value = (
        lax.all_to_all(grad_heads_query, "seq", split_axis=1, concat_axis=2, tiled=True),
        lax.all_to_all(
            grad_key_own.astype(jnp.bfloat16), "seq", split_axis=1, concat_axis=2, tiled=True
        ),
        lax.all_to_all(
            grad_value_own.astype(jnp.bfloat16), "seq", split_axis=1, concat_axis=2, tiled=True
        ),
    )
    grad_key_sum = jnp.sum(
        token_key.astype(jnp.float32).reshape(token_rows, KV_HEADS, copies, HEAD_DIM), axis=2
    )
    grad_value_sum = jnp.sum(
        token_value.astype(jnp.float32).reshape(token_rows, KV_HEADS, copies, HEAD_DIM), axis=2
    )
    grad_query_low = (
        rotate(token_query.astype(jnp.float32).reshape(token_rows, HEADS, HEAD_DIM), position, -1.0)
        .astype(jnp.bfloat16)
        .reshape(token_rows, width)
    )
    grad_key_low = (
        rotate(grad_key_sum, position, -1.0)
        .astype(jnp.bfloat16)
        .reshape(token_rows, KV_HEADS * HEAD_DIM)
    )
    grad_value_low = grad_value_sum.astype(jnp.bfloat16).reshape(token_rows, KV_HEADS * HEAD_DIM)
    grad_normed = (
        back_product(grad_query_low, w_query)
        + back_product(grad_key_low, w_key)
        + back_product(grad_value_low, w_value)
    )
    grad_in_part, gain_attn_terms = rms_backward(
        flat_in, gain_attn.astype(jnp.float32), inv_first, grad_normed
    )
    grad_input = (grad_hidden + grad_in_part).reshape(upstream.shape)
    weight_rows = (
        gain_attn_terms,
        normed_low,
        grad_query_low,
        grad_key_low,
        grad_value_low,
        token_mixed,
        grad_branch_low,
        gain_mlp_terms,
        normed_mlp_low,
        grad_gate_low,
        grad_up_low,
        act_low,
        grad_out_low,
    )
    return (grad_input, weight_rows)


def weight_term(inputs_low, outputs_low):
    if outputs_low is None:
        return jnp.sum(inputs_low, axis=0)
    return lax.dot_general(
        inputs_low, outputs_low, (((0,), (0,)), ((), ())), preferred_element_type=jnp.float32
    )


def shards(
    inputs,
    cotangent,
    doc_lengths,
    attention_gain,
    w_query,
    w_key,
    w_value,
    w_output,
    mlp_gain,
    w_gate,
    w_up,
    w_down,
):
    at_first = lax.axis_index("section") == 0
    seq_count = lax.axis_size("seq")
    blk_count = lax.axis_size("blk")
    blk_index = lax.axis_index("blk")
    shard_id = lax.axis_index("seq") * blk_count + blk_index
    placing = (shard_id, blk_index, seq_count, blk_count)
    micro_count = inputs.shape[0]
    local_shards = (
        attention_gain[0],
        w_query[0],
        w_key[0],
        w_value[0],
        w_output[0],
        mlp_gain[0],
        w_gate[0],
        w_up[0],
        w_down[0],
    )
    weights = (
        lax.all_gather(local_shards[0], "blk", axis=0, tiled=True),
        lax.all_gather(local_shards[1], "blk", axis=0, tiled=True),
        lax.all_gather(local_shards[2], "blk", axis=0, tiled=True),
        lax.all_gather(local_shards[3], "blk", axis=0, tiled=True),
        lax.all_gather(local_shards[4], "blk", axis=0, tiled=True),
        lax.all_gather(local_shards[5], "blk", axis=0, tiled=True),
        lax.all_gather(local_shards[6], "blk", axis=0, tiled=True),
        lax.all_gather(local_shards[7], "blk", axis=0, tiled=True),
        lax.all_gather(local_shards[8], "blk", axis=0, tiled=True),
    )
    received = jnp.zeros(inputs.shape[1:], jnp.bfloat16)
    saved_states = []
    section_outs = []
    for tick_index in range(micro_count + 1):
        fresh_input = inputs[min(tick_index, micro_count - 1)]
        section_in = jnp.where(at_first, fresh_input, received).astype(jnp.float32)
        lengths = jnp.where(
            at_first,
            doc_lengths[min(tick_index, micro_count - 1)],
            doc_lengths[max(tick_index - 1, 0)],
        )
        result, saved_state = layer_forward(section_in, lengths, weights, placing)
        result_low = result.astype(jnp.bfloat16)
        if tick_index < micro_count:
            received = passed_along(result_low, "section", 1)
        saved_states.append(saved_state)
        section_outs.append(result_low)
    weights = (
        lax.all_gather(local_shards[0], "blk", axis=0, tiled=True),
        lax.all_gather(local_shards[1], "blk", axis=0, tiled=True),
        lax.all_gather(local_shards[2], "blk", axis=0, tiled=True),
        lax.all_gather(local_shards[3], "blk", axis=0, tiled=True),
        lax.all_gather(local_shards[4], "blk", axis=0, tiled=True),
        lax.all_gather(local_shards[5], "blk", axis=0, tiled=True),
        lax.all_gather(local_shards[6], "blk", axis=0, tiled=True),
        lax.all_gather(local_shards[7], "blk", axis=0, tiled=True),
        lax.all_gather(local_shards[8], "blk", axis=0, tiled=True),
    )
    back_in = jnp.zeros(cotangent.shape[1:], jnp.bfloat16)
    grad_outs = []
    row_sets = []
    for tick_index in range(micro_count + 1):
        saved_state = jax.tree.map(
            lambda first_pick, second_pick: jnp.where(at_first, first_pick, second_pick),
            saved_states[max(tick_index - 1, 0)],
            saved_states[min(tick_index + 1, micro_count)],
        )
        upstream = jnp.where(at_first, back_in, cotangent[min(tick_index, micro_count - 1)]).astype(
            jnp.float32
        )
        grad_input, weight_rows = layer_backward(upstream, saved_state, weights, placing)
        grad_low = grad_input.astype(jnp.bfloat16)
        if tick_index < micro_count:
            back_in = passed_along(grad_low, "section", -1)
        grad_outs.append(grad_low)
        row_sets.append(weight_rows)
    activations = jnp.stack(
        [
            jnp.where(at_first, section_outs[index_m], section_outs[index_m + 1])
            for index_m in range(micro_count)
        ]
    )[None]
    input_grads = jnp.stack(
        [
            jnp.where(at_first, grad_outs[index_m + 1], grad_outs[index_m])
            for index_m in range(micro_count)
        ]
    )[None]
    picked = [
        jax.tree.map(
            lambda first_pick, second_pick: jnp.where(at_first, first_pick, second_pick),
            row_sets[index_m + 1],
            row_sets[index_m],
        )
        for index_m in range(micro_count)
    ]
    merged = jax.tree.map(lambda *pieces: jnp.concatenate(pieces, axis=0), *picked)
    (
        gain_attn_terms,
        normed_low,
        grad_query_low,
        grad_key_low,
        grad_value_low,
        token_mixed,
        grad_branch_low,
        gain_mlp_terms,
        normed_mlp_low,
        grad_gate_low,
        grad_up_low,
        act_low,
        grad_out_low,
    ) = merged
    grad_pairs = (
        (gain_attn_terms, None),
        (normed_low, grad_query_low),
        (normed_low, grad_key_low),
        (normed_low, grad_value_low),
        (token_mixed, grad_branch_low),
        (gain_mlp_terms, None),
        (normed_mlp_low, grad_gate_low),
        (normed_mlp_low, grad_up_low),
        (act_low, grad_out_low),
    )
    shares = tuple(
        (
            lax.psum_scatter(
                weight_term(left_side, right_side).astype(jnp.bfloat16),
                "blk",
                scatter_dimension=0,
                tiled=True,
            ).astype(jnp.float32)
            for left_side, right_side in grad_pairs
        )
    )
    shares = jax.tree.map(lambda part: part.astype(jnp.float32), lax.psum(shortened(shares), "seq"))
    return (
        activations,
        input_grads,
        shares[0][None],
        shares[1][None],
        shares[2][None],
        shares[3][None],
        shares[4][None],
        shares[5][None],
        shares[6][None],
        shares[7][None],
        shares[8][None],
    )


MESH = pl.DeviceIdType.MESH


def remote(source, target, sent, arrived, device):
    return pltpu.make_async_remote_copy(
        source, target, sent, arrived, device_id=device, device_id_type=MESH
    )


def greet(partners):
    barrier = pltpu.get_barrier_semaphore()
    for device in partners:
        pl.semaphore_signal(barrier, 1, device_id=device, device_id_type=MESH)
    pl.semaphore_wait(barrier, len(partners))


def greet_line(blk_index, count, partners):
    barrier = pltpu.get_barrier_semaphore()
    for device in partners:
        pl.semaphore_signal(barrier, 1, device_id=device, device_id_type=MESH)
    for step, there in ((-1, blk_index > 0), (1, blk_index < count - 1)):

        @pl.when(there)
        def _():
            pl.semaphore_signal(
                barrier, 1, device_id={"blk": blk_index + step}, device_id_type=MESH
            )

    inner = (blk_index > 0).astype(jnp.int32) + (blk_index < count - 1).astype(jnp.int32)
    pl.semaphore_wait(barrier, len(partners) + inner)


def gather_kernel(
    count, own, out, line_sent, line_got, side_sent, side_got, core_sent, core_got, local_done
):
    seq = lax.axis_index("seq")
    b = lax.axis_index("blk")
    core, side = {"seq": seq ^ 1}, {"seq": seq ^ 2}
    greet_line(b, count, (core, side))
    base, side_base = seq * count, (seq ^ 2) * count

    def along_line(j, way, source=None):
        device = {"blk": b + (1 if way else -1)}
        spot = out.at[base + j]
        return remote(
            spot if source is None else source, spot, line_sent.at[j, way], line_got.at[j], device
        )

    def to_side(j, source=None):
        spot = out.at[base + j]
        return remote(
            spot if source is None else source, spot, side_sent.at[j], side_got.at[j], side
        )

    def to_core(turn_of, j, source=None):
        spot = out.at[(base if turn_of == 0 else side_base) + j]
        return remote(
            spot if source is None else source,
            spot,
            core_sent.at[turn_of, j],
            core_got.at[turn_of, j],
            core,
        )

    local = pltpu.make_async_copy(own, out.at[base + b], local_done)
    local.start()
    to_side(b, own).start()

    @pl.when(b > 0)
    def _():
        along_line(b, 0, own).start()

    @pl.when(b < count - 1)
    def _():
        along_line(b, 1, own).start()

    to_core(0, b, own).start()

    def from_line(j, way):
        spot = out.at[base + j]
        remote(spot, spot, line_got.at[j], line_got.at[j], core).wait_recv()

        @pl.when((b < count - 1) if way else (b > 0))
        def _():
            along_line(j, way).start()

        to_side(j).start()
        to_core(0, j).start()

    def from_side(j):
        spot = out.at[side_base + j]
        remote(spot, spot, side_got.at[j], side_got.at[j], core).wait_recv()
        to_core(1, j).start()

    for k in range(1, count + 1):
        if k < count:
            pl.when(b - k >= 0)(functools.partial(from_line, b - k, 1))
            pl.when(b + k < count)(functools.partial(from_line, b + k, 0))
        if k == 1:
            from_side(b)
        else:
            pl.when(b - k + 1 >= 0)(functools.partial(from_side, b - k + 1))
            pl.when(b + k - 1 < count)(functools.partial(from_side, b + k - 1))
    for half, corner in ((0, seq ^ 1), (1, seq ^ 3)):
        for j in range(count):
            spot = out.at[corner * count + j]
            remote(spot, spot, core_got.at[half, j], core_got.at[half, j], core).wait_recv()
    local.wait()
    for j in range(count):
        to_side(j).wait_send()
        to_core(0, j).wait_send()
        to_core(1, j).wait_send()

    @pl.when(b > 0)
    def _():
        along_line(b, 0).wait_send()

    @pl.when(b < count - 1)
    def _():
        along_line(b, 1).wait_send()

    for k in range(1, count):

        @pl.when((b - k >= 0) & (b < count - 1))
        def _():
            along_line(b - k, 1).wait_send()

        @pl.when((b + k < count) & (b > 0))
        def _():
            along_line(b + k, 0).wait_send()


def group_gather(block):
    seq_count, count = lax.axis_size("seq"), lax.axis_size("blk")
    dma = pltpu.SemaphoreType.DMA
    gathered = pl.pallas_call(
        functools.partial(gather_kernel, count),
        out_shape=jax.ShapeDtypeStruct((seq_count * count,) + block.shape, block.dtype),
        in_specs=[pl.BlockSpec(memory_space=pltpu.VMEM)],
        out_specs=pl.BlockSpec(memory_space=pltpu.VMEM),
        scratch_shapes=[
            dma((count, 2)),
            dma((count,)),
            dma((count,)),
            dma((count,)),
            dma((2, count)),
            dma((2, count)),
            dma,
        ],
        compiler_params=pltpu.CompilerParams(
            collective_id=0, has_side_effects=True, vmem_limit_bytes=48 * 2**20
        ),
        name="gather_tokens",
    )(block)
    return gathered.reshape(-1, block.shape[1])


def scatter_kernel(
    count,
    partial,
    out,
    core_slot,
    side_slot,
    line_slot,
    side_out,
    line_out,
    core_sent,
    core_got,
    side_sent,
    side_got,
    line_sent,
    line_got,
):
    seq = lax.axis_index("seq")
    b = lax.axis_index("blk")
    core, side = {"seq": seq ^ 1}, {"seq": seq ^ 2}
    greet((core, side) + tuple({"blk": lax.rem(b + k, count)} for k in range(1, count)))
    away = tuple(range(count // 2, 0, -1)) + tuple(range(count // 2 + 1, count)) + (0,)
    place = [lax.rem(b + k, count) for k in away]

    def to_core(half, k):
        source = partial.at[(seq ^ (1 if half else 3)) * count + place[k]]
        return remote(
            source, core_slot.at[half, k], core_sent.at[half, k], core_got.at[half, k], core
        )

    def to_side(k):
        return remote(side_out.at[k], side_slot.at[k], side_sent.at[k], side_got.at[k], side)

    def along_line(k):
        slot = away[k] - 1
        return remote(
            line_out.at[k],
            line_slot.at[slot],
            line_sent.at[k],
            line_got.at[slot],
            {"blk": place[k]},
        )

    for half in range(2):
        for k in range(count):
            to_core(half, k).start()
    for k in range(count):
        to_core(0, k).wait_recv()
        total = partial[(seq ^ 2) * count + place[k]].astype(jnp.float32)
        total += core_slot[0, k].astype(jnp.float32)
        side_out[k] = total.astype(jnp.bfloat16)
        to_side(k).start()
    for k in range(count):
        to_core(1, k).wait_recv()
        to_side(k).wait_recv()
        total = partial[seq * count + place[k]].astype(jnp.float32)
        total += core_slot[1, k].astype(jnp.float32)
        total += side_slot[k].astype(jnp.float32)
        if k < count - 1:
            line_out[k] = total.astype(jnp.bfloat16)
            along_line(k).start()
        else:
            out[...] = total
    for k in range(count - 1):
        along_line(k).wait_recv()
        out[...] += line_slot[away[k] - 1].astype(jnp.float32)
    for k in range(count):
        to_core(0, k).wait_send()
        to_core(1, k).wait_send()
        to_side(k).wait_send()
        if k < count - 1:
            along_line(k).wait_send()


def group_scatter(partial):
    seq_count, count = lax.axis_size("seq"), lax.axis_size("blk")
    rows, width = partial.shape[0] // (seq_count * count), partial.shape[1]
    dma = pltpu.SemaphoreType.DMA

    def slots(*places):
        return pltpu.VMEM(places + (rows, width), jnp.bfloat16)

    return pl.pallas_call(
        functools.partial(scatter_kernel, count),
        out_shape=jax.ShapeDtypeStruct((rows, width), jnp.float32),
        in_specs=[pl.BlockSpec(memory_space=pltpu.VMEM)],
        out_specs=pl.BlockSpec(memory_space=pltpu.VMEM),
        scratch_shapes=[
            slots(2, count),
            slots(count),
            slots(count - 1),
            slots(count),
            slots(count - 1),
            dma((2, count)),
            dma((2, count)),
            dma((count,)),
            dma((count,)),
            dma((count - 1,)),
            dma((count - 1,)),
        ],
        compiler_params=pltpu.CompilerParams(
            collective_id=1, has_side_effects=True, vmem_limit_bytes=48 * 2**20
        ),
        name="scatter_tokens",
    )(partial.astype(jnp.bfloat16).reshape(seq_count * count, rows, width))


def turn(field_in, cosine, sine):
    half_dim = HEAD_DIM // 2
    first_half = field_in[:, :half_dim]
    second_half = field_in[:, half_dim:]
    return jnp.concatenate(
        [first_half * cosine - second_half * sine, second_half * cosine + first_half * sine],
        axis=-1,
    )


def swapped(own):
    return lax.ppermute(own, "section", [(0, 1), (1, 0)])


def spread_weights(local_shards):
    seq_index = lax.axis_index("seq")
    seq_count = lax.axis_size("seq")
    blk_count = lax.axis_size("blk")
    gain_attn, w_query, w_key, w_value, w_output, gain_mlp, w_gate, w_up, w_down = local_shards
    rows = w_query.shape[0]

    def mine(weight, width, per_blk, place):
        return lax.dynamic_index_in_dim(
            weight.reshape(rows, blk_count, per_blk, width), place, 2, keepdims=False
        )

    kv_per_blk = KV_HEADS // blk_count
    kv_place = seq_index * kv_per_blk // seq_count
    ff_width = w_gate.shape[1] // (seq_count * blk_count)
    attn = jnp.concatenate(
        [
            mine(w_query, HEAD_DIM, seq_count, seq_index),
            mine(w_key, HEAD_DIM, kv_per_blk, kv_place),
            mine(w_value, HEAD_DIM, kv_per_blk, kv_place),
        ],
        axis=-1,
    ).transpose(1, 2, 0)
    gains = jnp.stack([gain_attn, gain_mlp])
    attn = jnp.concatenate(
        [attn, jnp.broadcast_to(gains[None], (blk_count,) + gains.shape)], axis=1
    )
    wide = jnp.concatenate(
        [mine(w_gate, ff_width, seq_count, seq_index), mine(w_up, ff_width, seq_count, seq_index)],
        axis=-1,
    ).transpose(1, 0, 2)
    attn = lax.all_to_all(attn, "blk", split_axis=0, concat_axis=2, tiled=True)[0]
    wide = lax.all_to_all(wide, "blk", split_axis=0, concat_axis=1, tiled=True)[0]
    out_rows = w_output.shape[0] // seq_count
    down_rows = w_down.shape[0] // seq_count
    out = lax.dynamic_slice_in_dim(w_output, seq_index * out_rows, out_rows, 0)
    down = lax.dynamic_slice_in_dim(w_down, seq_index * down_rows, down_rows, 0)
    return attn, out, wide, down


def own_layer(x_own, weights, info):
    attn, out, wide, down = weights
    allowed, cosine, sine = info
    gain_attn = attn[3 * HEAD_DIM].astype(jnp.float32)
    gain_mlp = attn[3 * HEAD_DIM + 1].astype(jnp.float32)
    normed, inv_first = rms_forward(x_own, gain_attn)
    normed_all = group_gather(normed.astype(jnp.bfloat16))
    mixed_in = back_product(normed_all, attn[: 3 * HEAD_DIM])
    query = turn(mixed_in[:, :HEAD_DIM], cosine, sine).astype(jnp.bfloat16)
    key = turn(mixed_in[:, HEAD_DIM : 2 * HEAD_DIM], cosine, sine).astype(jnp.bfloat16)
    value = mixed_in[:, 2 * HEAD_DIM :].astype(jnp.bfloat16)
    scores = jnp.where(allowed, back_product(query, key) * HEAD_DIM ** (-0.5), MASKED)
    row_top = jnp.max(scores, axis=-1, keepdims=True)
    log_total = row_top + jnp.log(jnp.sum(jnp.exp(scores - row_top), axis=-1, keepdims=True))
    mixed = product(jnp.exp(scores - log_total).astype(jnp.bfloat16), value).astype(jnp.bfloat16)
    hidden = x_own + group_scatter(product(mixed, out))
    normed_mlp, inv_second = rms_forward(hidden, gain_mlp)
    normed_mlp_all = group_gather(normed_mlp.astype(jnp.bfloat16))
    pre = product(normed_mlp_all, wide)
    half = pre.shape[1] // 2
    gate_pre, up_pre = pre[:, :half], pre[:, half:]
    act_low = (jax.nn.silu(gate_pre) * up_pre).astype(jnp.bfloat16)
    result = hidden + group_scatter(product(act_low, down))
    saved = (
        x_own,
        inv_first,
        normed_all,
        query,
        key,
        value,
        log_total,
        mixed,
        hidden,
        inv_second,
        normed_mlp_all,
        gate_pre,
        up_pre,
        act_low,
    )
    return result, saved


def own_layer_back(grad_own, weights, info, saved):
    attn, out, wide, down = weights
    allowed, cosine, sine = info
    (
        x_own,
        inv_first,
        normed_all,
        query,
        key,
        value,
        log_total,
        mixed,
        hidden,
        inv_second,
        normed_mlp_all,
        gate_pre,
        up_pre,
        act_low,
    ) = saved
    gain_attn = attn[3 * HEAD_DIM].astype(jnp.float32)
    gain_mlp = attn[3 * HEAD_DIM + 1].astype(jnp.float32)
    grad_out_all = group_gather(grad_own.astype(jnp.bfloat16))
    grad_act = back_product(grad_out_all, down)
    gate_sigmoid = jax.nn.sigmoid(gate_pre)
    grad_gate = (
        grad_act * up_pre * gate_sigmoid * (1.0 + gate_pre * (1.0 - gate_sigmoid))
    ).astype(jnp.bfloat16)
    grad_up = (grad_act * jax.nn.silu(gate_pre)).astype(jnp.bfloat16)
    grad_wide = jnp.concatenate([grad_gate, grad_up], axis=1)
    grad_normed_mlp = group_scatter(back_product(grad_wide, wide))
    grad_hidden_part, gain_mlp_terms = rms_backward(hidden, gain_mlp, inv_second, grad_normed_mlp)
    grad_hidden = grad_own + grad_hidden_part
    grad_branch_all = group_gather(grad_hidden.astype(jnp.bfloat16))
    grad_mixed = back_product(grad_branch_all, out).astype(jnp.bfloat16)
    scores = jnp.where(allowed, back_product(query, key) * HEAD_DIM ** (-0.5), MASKED)
    probs = jnp.exp(scores - log_total)
    grad_probs = back_product(grad_mixed, value)
    centre = jnp.sum(probs * grad_probs, axis=-1, keepdims=True)
    grad_scores = (probs * (grad_probs - centre)).astype(jnp.bfloat16)
    grad_query = (product(grad_scores, key) * HEAD_DIM ** (-0.5)).astype(jnp.bfloat16)
    grad_key = weight_term(grad_scores, query) * HEAD_DIM ** (-0.5)
    grad_value = weight_term(probs.astype(jnp.bfloat16), grad_mixed).astype(jnp.bfloat16)
    grad_query = turn(grad_query.astype(jnp.float32), cosine, -sine).astype(jnp.bfloat16)
    grad_key = turn(grad_key, cosine, -sine).astype(jnp.bfloat16)
    grad_qkv = jnp.concatenate([grad_query, grad_key, grad_value], axis=1)
    grad_normed = group_scatter(product(grad_qkv, attn[: 3 * HEAD_DIM]))
    grad_in_part, gain_attn_terms = rms_backward(x_own, gain_attn, inv_first, grad_normed)
    grads = (
        weight_term(grad_qkv, normed_all),
        weight_term(mixed, grad_branch_all),
        weight_term(normed_mlp_all, grad_wide),
        weight_term(act_low, grad_out_all),
    )
    gains = jnp.stack([jnp.sum(gain_attn_terms, axis=0), jnp.sum(gain_mlp_terms, axis=0)])
    return grad_hidden + grad_in_part, grads, gains


def finish_grads(grads):
    seq_count = lax.axis_size("seq")
    blk_count = lax.axis_size("blk")
    attn, out, wide, down = grads
    attn = lax.all_to_all(attn[None], "blk", split_axis=2, concat_axis=0, tiled=True)
    wide = lax.all_to_all(wide[None], "blk", split_axis=1, concat_axis=0, tiled=True)
    attn, out, wide, down = [
        lax.all_gather(part, "seq", axis=0, tiled=False).astype(jnp.float32)
        for part in (attn, out, wide, down)
    ]
    rows = attn.shape[-1]
    query = attn[:, :, :HEAD_DIM].transpose(3, 1, 0, 2).reshape(rows, -1)

    def key_like(part):
        copies = HEADS // KV_HEADS
        part = part.reshape(seq_count // copies, copies, blk_count, HEAD_DIM, rows).sum(1)
        return part.transpose(3, 1, 0, 2).reshape(rows, -1)

    key = key_like(attn[:, :, HEAD_DIM : 2 * HEAD_DIM])
    value = key_like(attn[:, :, 2 * HEAD_DIM :])
    half = wide.shape[-1] // 2
    gate = wide[..., :half].transpose(2, 1, 0, 3).reshape(rows, -1)
    up = wide[..., half:].transpose(2, 1, 0, 3).reshape(rows, -1)
    return query, key, value, out.reshape(-1, out.shape[-1]), gate, up, down.reshape(
        -1, down.shape[-1]
    )


def head_shards(inputs, cotangent, doc_lengths, *params):
    section = lax.axis_index("section")
    at_first = section == 0
    blk_index = lax.axis_index("blk")
    tokens = inputs.shape[2] * lax.axis_size("seq") * lax.axis_size("blk")
    own = spread_weights(tuple(weight[0] for weight in params))
    other = tuple(swapped(part) for part in own)
    first = tuple(jnp.where(at_first, a, b) for a, b in zip(own, other))
    second = tuple(jnp.where(at_first, b, a) for a, b in zip(own, other))
    x_own = lax.dynamic_index_in_dim(inputs, section, 0, keepdims=False)[0].astype(jnp.float32)
    grad_own = lax.dynamic_index_in_dim(cotangent, section, 0, keepdims=False)[0].astype(
        jnp.float32
    )
    lengths = lax.dynamic_index_in_dim(doc_lengths, section, 0, keepdims=False)[0]
    token_index = jnp.arange(tokens, dtype=jnp.int32)
    segment, position = doc_info(lengths, token_index)
    allowed = (segment[:, None] == segment[None, :]) & (
        token_index[None, :] <= token_index[:, None]
    )
    half_dim = HEAD_DIM // 2
    frequency = THETA ** (-2.0 * jnp.arange(half_dim, dtype=jnp.float32) / HEAD_DIM)
    angles = position.astype(jnp.float32)[:, None] * frequency
    info = (allowed, jnp.cos(angles), jnp.sin(angles))
    result, saved_first = own_layer(x_own, first, info)
    between = result.astype(jnp.bfloat16)
    result, saved_second = own_layer(between.astype(jnp.float32), second, info)
    final = result.astype(jnp.bfloat16)
    grad_between, grads_second, gains_second = own_layer_back(grad_own, second, info, saved_second)
    grad_between = grad_between.astype(jnp.bfloat16)
    grad_start, grads_first, gains_first = own_layer_back(
        grad_between.astype(jnp.float32), first, info, saved_first
    )
    grad_start = grad_start.astype(jnp.bfloat16)

    def by_section(for_first, for_second):
        kept = jnp.where(at_first, for_first, for_second)
        received = swapped(jnp.where(at_first, for_second, for_first))
        return jnp.stack(
            [jnp.where(at_first, kept, received), jnp.where(at_first, received, kept)]
        )[None, :, None]

    activations = by_section(between, final)
    input_grads = by_section(grad_start, grad_between)
    summed = []
    for one, two in zip(grads_first, grads_second):
        kept = jnp.where(at_first, one, two)
        received = swapped(jnp.where(at_first, two, one).astype(jnp.bfloat16))
        summed.append((kept + received.astype(jnp.float32)).astype(jnp.bfloat16))
    query, key, value, out, gate, up, down = finish_grads(summed)
    gains = lax.psum(jnp.stack([gains_first, gains_second]), ("section", "seq", "blk"))
    gains = lax.dynamic_index_in_dim(gains, section, 0, keepdims=False)
    rows = params[1].shape[1]
    gains = lax.dynamic_slice_in_dim(gains, blk_index * rows, rows, 1)
    return (
        activations,
        input_grads,
        gains[0][None],
        query[None],
        key[None],
        value[None],
        out[None],
        gains[1][None],
        gate[None],
        up[None],
        down[None],
    )


def solution(mesh):
    placed = (
        P(None, None, ("seq", "blk"), None),
        P(None, None, ("seq", "blk"), None),
        P(),
        P("section", "blk"),
        P("section", "blk", None),
        P("section", "blk", None),
        P("section", "blk", None),
        P("section", "blk", None),
        P("section", "blk"),
        P("section", "blk", None),
        P("section", "blk", None),
        P("section", "blk", None),
    )
    one_head_each = mesh.shape["seq"] * mesh.shape["blk"] == HEADS
    return jax.shard_map(
        head_shards if one_head_each else shards,
        mesh=mesh,
        in_specs=placed,
        out_specs=(
            P("section", None, None, ("seq", "blk"), None),
            P("section", None, None, ("seq", "blk"), None),
            P("section", "blk"),
            P("section", "blk", None),
            P("section", "blk", None),
            P("section", "blk", None),
            P("section", "blk", None),
            P("section", "blk"),
            P("section", "blk", None),
            P("section", "blk", None),
            P("section", "blk", None),
        ),
        check_vma=False,
    )
```

```python
import functools

import jax
import jax.numpy as jnp
from jax import lax
from jax.experimental import pallas as pl
from jax.experimental.pallas import tpu as pltpu
from jax.sharding import PartitionSpec as P

HEADS = 16
KV_HEADS = 8
HEAD_DIM = 96


EPS = 1e-05
THETA = 100000.0
MASKED = -1e30


def passed_along(value, axis, steps):
    count = lax.axis_size(axis)
    first, last = (max(0, -steps), min(count, count - steps))
    return lax.ppermute(value, axis, [(source, source + steps) for source in range(first, last)])


def shortened(value):
    return jax.tree.map(lambda a: a.astype(jnp.bfloat16) if a.dtype == jnp.float32 else a, value)


def product(left_side, right_side):
    return jnp.dot(left_side, right_side, preferred_element_type=jnp.float32)


def back_product(left_side, right_side):
    return lax.dot_general(
        left_side, right_side, (((1,), (1,)), ((), ())), preferred_element_type=jnp.float32
    )


def doc_info(lengths, token_index):
    doc_ends = jnp.cumsum(lengths, axis=-1)
    passed = (doc_ends[..., None, :] <= token_index[..., None]).astype(jnp.int32)
    segment = jnp.sum(passed, axis=-1)
    offset = jnp.sum(passed * lengths[..., None, :], axis=-1)
    return (segment, token_index - offset)


def rotate(field_in, position, turn_sign):
    half_dim = field_in.shape[-1] // 2
    frequency = THETA ** (-2.0 * jnp.arange(half_dim, dtype=jnp.float32) / field_in.shape[-1])
    angles = position.astype(jnp.float32)[:, None] * frequency
    cosine = jnp.cos(angles)[:, None, :]
    sine_part = turn_sign * jnp.sin(angles)[:, None, :]
    first_half = field_in[..., :half_dim]
    second_half = field_in[..., half_dim:]
    return jnp.concatenate(
        [
            first_half * cosine - second_half * sine_part,
            second_half * cosine + first_half * sine_part,
        ],
        axis=-1,
    )


def rms_forward(field_in, gain_row):
    inv_root = lax.rsqrt(jnp.mean(field_in * field_in, axis=-1, keepdims=True) + EPS)
    return (field_in * inv_root * gain_row, inv_root)


def rms_backward(field_in, gain_row, inv_root, grad_normed):
    scaled = gain_row * grad_normed
    grad_field = inv_root * scaled - field_in * inv_root**3 * jnp.mean(
        scaled * field_in, axis=-1, keepdims=True
    )
    return (grad_field, grad_normed * field_in * inv_root)


def token_place(block_id, row_ids, per_device, blk_count):
    return (row_ids // per_device * blk_count + block_id) * per_device + row_ids % per_device


def masks_for(lengths, blk_index, per_device, blk_count, seq_count):
    block_tokens = seq_count * per_device
    row_ids = jnp.arange(block_tokens, dtype=jnp.int32)
    query_index = token_place(blk_index, row_ids, per_device, blk_count)
    all_ids = jnp.arange(blk_count * block_tokens, dtype=jnp.int32)
    key_index = token_place(all_ids // block_tokens, all_ids % block_tokens, per_device, blk_count)
    query_seg, _ = doc_info(lengths, query_index)
    key_seg, _ = doc_info(lengths, key_index)
    return (query_index, key_index, query_seg, key_seg)


def head_scores(queries, key_rows, allowed, kv_local):
    grouped = queries.reshape(queries.shape[0], kv_local, -1, HEAD_DIM)
    key_heads = key_rows.reshape(key_rows.shape[0], kv_local, HEAD_DIM)
    scores = jnp.einsum(
        "rkgd,lkd->kgrl", grouped, key_heads, preferred_element_type=jnp.float32
    ) * HEAD_DIM ** (-0.5)
    return (jnp.where(allowed, scores, MASKED), grouped, key_heads)


def attend_forward(operands, query_index, key_index, kv_local):
    queries, key_rows, value_rows, query_seg, key_seg = operands
    allowed = (query_seg[:, None] == key_seg[None, :]) & (
        key_index[None, :] <= query_index[:, None]
    )
    scores, grouped, key_heads = head_scores(queries, key_rows, allowed, kv_local)
    row_top = jnp.max(scores, axis=-1, keepdims=True)
    log_total = row_top + jnp.log(jnp.sum(jnp.exp(scores - row_top), axis=-1, keepdims=True))
    weights_low = jnp.exp(scores - log_total).astype(jnp.bfloat16)
    value_heads = value_rows.reshape(value_rows.shape[0], kv_local, HEAD_DIM)
    mixed_heads = jnp.einsum(
        "kgrl,lkd->rkgd", weights_low, value_heads, preferred_element_type=jnp.float32
    )
    return (mixed_heads.reshape(queries.shape).astype(jnp.bfloat16), log_total)


def attend_backward(operands, query_index, key_index, kv_local):
    queries, key_rows, value_rows, grad_mixed, log_total, query_seg, key_seg = operands
    allowed = (query_seg[:, None] == key_seg[None, :]) & (
        key_index[None, :] <= query_index[:, None]
    )
    scores, grouped, key_heads = head_scores(queries, key_rows, allowed, kv_local)
    attn_probs = jnp.exp(scores - log_total)
    value_heads = value_rows.reshape(value_rows.shape[0], kv_local, HEAD_DIM)
    grad_heads = grad_mixed.reshape(grouped.shape)
    grad_values = jnp.einsum(
        "kgrl,rkgd->lkd",
        attn_probs.astype(jnp.bfloat16),
        grad_heads,
        preferred_element_type=jnp.float32,
    )
    grad_probs = jnp.einsum(
        "rkgd,lkd->kgrl", grad_heads, value_heads, preferred_element_type=jnp.float32
    )
    centre = jnp.sum(attn_probs * grad_probs, axis=-1, keepdims=True)
    grad_scores = (attn_probs * (grad_probs - centre)).astype(jnp.bfloat16)
    grad_queries = jnp.einsum(
        "kgrl,lkd->rkgd", grad_scores, key_heads, preferred_element_type=jnp.float32
    ) * HEAD_DIM ** (-0.5)
    grad_keys = jnp.einsum(
        "kgrl,rkgd->lkd", grad_scores, grouped, preferred_element_type=jnp.float32
    ) * HEAD_DIM ** (-0.5)
    return (
        grad_queries.reshape(queries.shape).astype(jnp.bfloat16),
        grad_keys.reshape(key_rows.shape),
        grad_values.reshape(value_rows.shape),
    )


def layer_forward(section_in, lengths, weights, placing):
    shard_id, blk_index, seq_count, blk_count = placing
    gain_attn, w_query, w_key, w_value, w_output, gain_mlp, w_gate, w_up, w_down = weights
    seqs_here, per_device, width = section_in.shape
    token_rows = seqs_here * per_device
    copies = max(1, seq_count // KV_HEADS)
    kv_local = KV_HEADS * copies // seq_count
    token_index = shard_id * per_device + jnp.arange(per_device, dtype=jnp.int32)
    _, position = doc_info(lengths, token_index)
    position = position.reshape(token_rows)
    flat_in = section_in.reshape(token_rows, width)
    normed, inv_first = rms_forward(flat_in, gain_attn.astype(jnp.float32))
    normed_low = normed.astype(jnp.bfloat16)
    query_pre = product(normed_low, w_query).reshape(token_rows, HEADS, HEAD_DIM)
    key_pre = product(normed_low, w_key).reshape(token_rows, KV_HEADS, HEAD_DIM)
    value_pre = product(normed_low, w_value).reshape(token_rows, KV_HEADS, HEAD_DIM)
    query_rot = (
        rotate(query_pre, position, 1.0).astype(jnp.bfloat16).reshape(seqs_here, per_device, width)
    )
    key_rot = rotate(key_pre, position, 1.0).astype(jnp.bfloat16)
    spread_shape = (token_rows, KV_HEADS, copies, HEAD_DIM)
    key_rep = jnp.broadcast_to(key_rot[:, :, None, :], spread_shape).reshape(
        seqs_here, per_device, -1
    )
    value_rep = jnp.broadcast_to(
        value_pre.astype(jnp.bfloat16)[:, :, None, :], spread_shape
    ).reshape(seqs_here, per_device, -1)
    heads_query, heads_key, heads_value = (
        lax.all_to_all(query_rot, "seq", split_axis=2, concat_axis=1, tiled=True),
        lax.all_to_all(key_rep, "seq", split_axis=2, concat_axis=1, tiled=True),
        lax.all_to_all(value_rep, "seq", split_axis=2, concat_axis=1, tiled=True),
    )
    keys_all, values_all = (
        lax.all_gather(heads_key, "blk", axis=1, tiled=True),
        lax.all_gather(heads_value, "blk", axis=1, tiled=True),
    )
    query_index, key_index, query_seg, key_seg = masks_for(
        lengths, blk_index, per_device, blk_count, seq_count
    )
    heads_mixed, log_total = lax.map(
        lambda operands: attend_forward(operands, query_index, key_index, kv_local),
        (heads_query, keys_all, values_all, query_seg, key_seg),
    )
    token_mixed = lax.all_to_all(
        heads_mixed, "seq", split_axis=1, concat_axis=2, tiled=True
    ).reshape(token_rows, width)
    hidden = flat_in + product(token_mixed, w_output)
    normed_mlp, inv_second = rms_forward(hidden, gain_mlp.astype(jnp.float32))
    normed_mlp_low = normed_mlp.astype(jnp.bfloat16)
    gate_pre = product(normed_mlp_low, w_gate)
    up_pre = product(normed_mlp_low, w_up)
    act_low = (jax.nn.silu(gate_pre) * up_pre).astype(jnp.bfloat16)
    result = hidden + product(act_low, w_down)
    saved_state = (
        flat_in,
        normed_low,
        inv_first,
        position,
        heads_query,
        keys_all,
        values_all,
        log_total,
        token_mixed,
        hidden,
        inv_second,
        normed_mlp_low,
        gate_pre,
        up_pre,
        act_low,
        lengths,
    )
    return (result.reshape(section_in.shape), saved_state)


def layer_backward(upstream, saved_state, weights, placing):
    shard_id, blk_index, seq_count, blk_count = placing
    gain_attn, w_query, w_key, w_value, w_output, gain_mlp, w_gate, w_up, w_down = weights
    (
        flat_in,
        normed_low,
        inv_first,
        position,
        heads_query,
        keys_all,
        values_all,
        log_total,
        token_mixed,
        hidden,
        inv_second,
        normed_mlp_low,
        gate_pre,
        up_pre,
        act_low,
        lengths,
    ) = saved_state
    seqs_here, per_device, width = upstream.shape
    token_rows = seqs_here * per_device
    copies = max(1, seq_count // KV_HEADS)
    kv_local = KV_HEADS * copies // seq_count
    grad_rows = upstream.reshape(token_rows, width)
    grad_out_low = grad_rows.astype(jnp.bfloat16)
    grad_act = back_product(grad_out_low, w_down)
    gate_sigmoid = jax.nn.sigmoid(gate_pre)
    grad_gate_low = (
        grad_act * up_pre * gate_sigmoid * (1.0 + gate_pre * (1.0 - gate_sigmoid))
    ).astype(jnp.bfloat16)
    grad_up_low = (grad_act * jax.nn.silu(gate_pre)).astype(jnp.bfloat16)
    grad_normed_mlp = back_product(grad_gate_low, w_gate) + back_product(grad_up_low, w_up)
    grad_hidden_part, gain_mlp_terms = rms_backward(
        hidden, gain_mlp.astype(jnp.float32), inv_second, grad_normed_mlp
    )
    grad_hidden = grad_rows + grad_hidden_part
    grad_branch_low = grad_hidden.astype(jnp.bfloat16)
    grad_mixed_low = (
        back_product(grad_branch_low, w_output)
        .astype(jnp.bfloat16)
        .reshape(seqs_here, per_device, width)
    )
    heads_grad = lax.all_to_all(grad_mixed_low, "seq", split_axis=2, concat_axis=1, tiled=True)
    query_index, key_index, query_seg, key_seg = masks_for(
        lengths, blk_index, per_device, blk_count, seq_count
    )
    grad_heads_query, grad_keys_all, grad_values_all = lax.map(
        lambda operands: attend_backward(operands, query_index, key_index, kv_local),
        (heads_query, keys_all, values_all, heads_grad, log_total, query_seg, key_seg),
    )
    grad_key_own, grad_value_own = (
        lax.psum_scatter(
            grad_keys_all.astype(jnp.bfloat16), "blk", scatter_dimension=1, tiled=True
        ).astype(jnp.float32),
        lax.psum_scatter(
            grad_values_all.astype(jnp.bfloat16), "blk", scatter_dimension=1, tiled=True
        ).astype(jnp.float32),
    )
    token_query, token_key, token_value = (
        lax.all_to_all(grad_heads_query, "seq", split_axis=1, concat_axis=2, tiled=True),
        lax.all_to_all(
            grad_key_own.astype(jnp.bfloat16), "seq", split_axis=1, concat_axis=2, tiled=True
        ),
        lax.all_to_all(
            grad_value_own.astype(jnp.bfloat16), "seq", split_axis=1, concat_axis=2, tiled=True
        ),
    )
    grad_key_sum = jnp.sum(
        token_key.astype(jnp.float32).reshape(token_rows, KV_HEADS, copies, HEAD_DIM), axis=2
    )
    grad_value_sum = jnp.sum(
        token_value.astype(jnp.float32).reshape(token_rows, KV_HEADS, copies, HEAD_DIM), axis=2
    )
    grad_query_low = (
        rotate(token_query.astype(jnp.float32).reshape(token_rows, HEADS, HEAD_DIM), position, -1.0)
        .astype(jnp.bfloat16)
        .reshape(token_rows, width)
    )
    grad_key_low = (
        rotate(grad_key_sum, position, -1.0)
        .astype(jnp.bfloat16)
        .reshape(token_rows, KV_HEADS * HEAD_DIM)
    )
    grad_value_low = grad_value_sum.astype(jnp.bfloat16).reshape(token_rows, KV_HEADS * HEAD_DIM)
    grad_normed = (
        back_product(grad_query_low, w_query)
        + back_product(grad_key_low, w_key)
        + back_product(grad_value_low, w_value)
    )
    grad_in_part, gain_attn_terms = rms_backward(
        flat_in, gain_attn.astype(jnp.float32), inv_first, grad_normed
    )
    grad_input = (grad_hidden + grad_in_part).reshape(upstream.shape)
    weight_rows = (
        gain_attn_terms,
        normed_low,
        grad_query_low,
        grad_key_low,
        grad_value_low,
        token_mixed,
        grad_branch_low,
        gain_mlp_terms,
        normed_mlp_low,
        grad_gate_low,
        grad_up_low,
        act_low,
        grad_out_low,
    )
    return (grad_input, weight_rows)


def weight_term(inputs_low, outputs_low):
    if outputs_low is None:
        return jnp.sum(inputs_low, axis=0)
    return lax.dot_general(
        inputs_low, outputs_low, (((0,), (0,)), ((), ())), preferred_element_type=jnp.float32
    )


def shards(
    inputs,
    cotangent,
    doc_lengths,
    attention_gain,
    w_query,
    w_key,
    w_value,
    w_output,
    mlp_gain,
    w_gate,
    w_up,
    w_down,
):
    at_first = lax.axis_index("section") == 0
    seq_count = lax.axis_size("seq")
    blk_count = lax.axis_size("blk")
    blk_index = lax.axis_index("blk")
    shard_id = lax.axis_index("seq") * blk_count + blk_index
    placing = (shard_id, blk_index, seq_count, blk_count)
    micro_count = inputs.shape[0]
    local_shards = (
        attention_gain[0],
        w_query[0],
        w_key[0],
        w_value[0],
        w_output[0],
        mlp_gain[0],
        w_gate[0],
        w_up[0],
        w_down[0],
    )
    weights = (
        lax.all_gather(local_shards[0], "blk", axis=0, tiled=True),
        lax.all_gather(local_shards[1], "blk", axis=0, tiled=True),
        lax.all_gather(local_shards[2], "blk", axis=0, tiled=True),
        lax.all_gather(local_shards[3], "blk", axis=0, tiled=True),
        lax.all_gather(local_shards[4], "blk", axis=0, tiled=True),
        lax.all_gather(local_shards[5], "blk", axis=0, tiled=True),
        lax.all_gather(local_shards[6], "blk", axis=0, tiled=True),
        lax.all_gather(local_shards[7], "blk", axis=0, tiled=True),
        lax.all_gather(local_shards[8], "blk", axis=0, tiled=True),
    )
    received = jnp.zeros(inputs.shape[1:], jnp.bfloat16)
    saved_states = []
    section_outs = []
    for tick_index in range(micro_count + 1):
        fresh_input = inputs[min(tick_index, micro_count - 1)]
        section_in = jnp.where(at_first, fresh_input, received).astype(jnp.float32)
        lengths = jnp.where(
            at_first,
            doc_lengths[min(tick_index, micro_count - 1)],
            doc_lengths[max(tick_index - 1, 0)],
        )
        result, saved_state = layer_forward(section_in, lengths, weights, placing)
        result_low = result.astype(jnp.bfloat16)
        if tick_index < micro_count:
            received = passed_along(result_low, "section", 1)
        saved_states.append(saved_state)
        section_outs.append(result_low)
    weights = (
        lax.all_gather(local_shards[0], "blk", axis=0, tiled=True),
        lax.all_gather(local_shards[1], "blk", axis=0, tiled=True),
        lax.all_gather(local_shards[2], "blk", axis=0, tiled=True),
        lax.all_gather(local_shards[3], "blk", axis=0, tiled=True),
        lax.all_gather(local_shards[4], "blk", axis=0, tiled=True),
        lax.all_gather(local_shards[5], "blk", axis=0, tiled=True),
        lax.all_gather(local_shards[6], "blk", axis=0, tiled=True),
        lax.all_gather(local_shards[7], "blk", axis=0, tiled=True),
        lax.all_gather(local_shards[8], "blk", axis=0, tiled=True),
    )
    back_in = jnp.zeros(cotangent.shape[1:], jnp.bfloat16)
    grad_outs = []
    row_sets = []
    for tick_index in range(micro_count + 1):
        saved_state = jax.tree.map(
            lambda first_pick, second_pick: jnp.where(at_first, first_pick, second_pick),
            saved_states[max(tick_index - 1, 0)],
            saved_states[min(tick_index + 1, micro_count)],
        )
        upstream = jnp.where(at_first, back_in, cotangent[min(tick_index, micro_count - 1)]).astype(
            jnp.float32
        )
        grad_input, weight_rows = layer_backward(upstream, saved_state, weights, placing)
        grad_low = grad_input.astype(jnp.bfloat16)
        if tick_index < micro_count:
            back_in = passed_along(grad_low, "section", -1)
        grad_outs.append(grad_low)
        row_sets.append(weight_rows)
    activations = jnp.stack(
        [
            jnp.where(at_first, section_outs[index_m], section_outs[index_m + 1])
            for index_m in range(micro_count)
        ]
    )[None]
    input_grads = jnp.stack(
        [
            jnp.where(at_first, grad_outs[index_m + 1], grad_outs[index_m])
            for index_m in range(micro_count)
        ]
    )[None]
    picked = [
        jax.tree.map(
            lambda first_pick, second_pick: jnp.where(at_first, first_pick, second_pick),
            row_sets[index_m + 1],
            row_sets[index_m],
        )
        for index_m in range(micro_count)
    ]
    merged = jax.tree.map(lambda *pieces: jnp.concatenate(pieces, axis=0), *picked)
    (
        gain_attn_terms,
        normed_low,
        grad_query_low,
        grad_key_low,
        grad_value_low,
        token_mixed,
        grad_branch_low,
        gain_mlp_terms,
        normed_mlp_low,
        grad_gate_low,
        grad_up_low,
        act_low,
        grad_out_low,
    ) = merged
    grad_pairs = (
        (gain_attn_terms, None),
        (normed_low, grad_query_low),
        (normed_low, grad_key_low),
        (normed_low, grad_value_low),
        (token_mixed, grad_branch_low),
        (gain_mlp_terms, None),
        (normed_mlp_low, grad_gate_low),
        (normed_mlp_low, grad_up_low),
        (act_low, grad_out_low),
    )
    shares = tuple(
        (
            lax.psum_scatter(
                weight_term(left_side, right_side).astype(jnp.bfloat16),
                "blk",
                scatter_dimension=0,
                tiled=True,
            ).astype(jnp.float32)
            for left_side, right_side in grad_pairs
        )
    )
    shares = jax.tree.map(lambda part: part.astype(jnp.float32), lax.psum(shortened(shares), "seq"))
    return (
        activations,
        input_grads,
        shares[0][None],
        shares[1][None],
        shares[2][None],
        shares[3][None],
        shares[4][None],
        shares[5][None],
        shares[6][None],
        shares[7][None],
        shares[8][None],
    )


MESH = pl.DeviceIdType.MESH


def remote(source, target, sent, arrived, device):
    return pltpu.make_async_remote_copy(
        source, target, sent, arrived, device_id=device, device_id_type=MESH
    )


def greet(partners):
    barrier = pltpu.get_barrier_semaphore()
    for device in partners:
        pl.semaphore_signal(barrier, 1, device_id=device, device_id_type=MESH)
    pl.semaphore_wait(barrier, len(partners))


def greet_line(blk_index, count, partners):
    barrier = pltpu.get_barrier_semaphore()
    for device in partners:
        pl.semaphore_signal(barrier, 1, device_id=device, device_id_type=MESH)
    for step, there in ((-1, blk_index > 0), (1, blk_index < count - 1)):

        @pl.when(there)
        def _():
            pl.semaphore_signal(
                barrier, 1, device_id={"blk": blk_index + step}, device_id_type=MESH
            )

    inner = (blk_index > 0).astype(jnp.int32) + (blk_index < count - 1).astype(jnp.int32)
    pl.semaphore_wait(barrier, len(partners) + inner)


def settled(spot, semaphore, received):
    copy = remote(spot, spot, semaphore, semaphore, {"seq": lax.axis_index("seq") ^ 1})
    if received:
        copy.wait_recv()
    else:
        copy.wait_send()


def gather_steps(
    count, own, out, line_sent, line_got, side_sent, side_got, core_sent, core_got, local_done
):
    seq, b = lax.axis_index("seq"), lax.axis_index("blk")
    core, side = {"seq": seq ^ 1}, {"seq": seq ^ 2}
    base, side_base = seq * count, (seq ^ 2) * count

    def along_line(j, way, source=None):
        device = {"blk": b + (1 if way else -1)}
        spot = out.at[base + j]
        return remote(
            spot if source is None else source, spot, line_sent.at[j, way], line_got.at[j], device
        )

    def to_side(j, source=None):
        spot = out.at[base + j]
        return remote(
            spot if source is None else source, spot, side_sent.at[j], side_got.at[j], side
        )

    def to_core(half, j, source=None):
        spot = out.at[(side_base if half else base) + j]
        return remote(
            spot if source is None else source,
            spot,
            core_sent.at[half, j],
            core_got.at[half, j],
            core,
        )

    local = pltpu.make_async_copy(own, out.at[base + b], local_done)
    local.start()
    to_side(b, own).start()

    @pl.when(b > 0)
    def _():
        along_line(b, 0, own).start()

    @pl.when(b < count - 1)
    def _():
        along_line(b, 1, own).start()

    to_core(0, b, own).start()
    yield

    def from_line(j, way):
        settled(out.at[base + j], line_got.at[j], True)

        @pl.when((b < count - 1) if way else (b > 0))
        def _():
            along_line(j, way).start()

        to_side(j).start()
        to_core(0, j).start()

    def from_side(j):
        settled(out.at[side_base + j], side_got.at[j], True)
        to_core(1, j).start()

    for k in range(1, count + 1):
        if k < count:
            pl.when(b - k >= 0)(functools.partial(from_line, b - k, 1))
            pl.when(b + k < count)(functools.partial(from_line, b + k, 0))
        if k == 1:
            from_side(b)
        else:
            pl.when(b - k + 1 >= 0)(functools.partial(from_side, b - k + 1))
            pl.when(b + k - 1 < count)(functools.partial(from_side, b + k - 1))
        yield
    for half, corner in ((0, seq ^ 1), (1, seq ^ 3)):
        for j in range(count):
            settled(out.at[corner * count + j], core_got.at[half, j], True)
    local.wait()
    for j in range(count):
        to_side(j).wait_send()
        to_core(0, j).wait_send()
        to_core(1, j).wait_send()

    @pl.when(b > 0)
    def _():
        along_line(b, 0).wait_send()

    @pl.when(b < count - 1)
    def _():
        along_line(b, 1).wait_send()

    for k in range(1, count):

        @pl.when((b - k >= 0) & (b < count - 1))
        def _():
            along_line(b - k, 1).wait_send()

        @pl.when((b + k < count) & (b > 0))
        def _():
            along_line(b + k, 0).wait_send()


def gather_kernel(count, *refs):
    seq, b = lax.axis_index("seq"), lax.axis_index("blk")
    greet_line(b, count, ({"seq": seq ^ 1}, {"seq": seq ^ 2}))
    for _ in gather_steps(count, *refs):
        pass


def gather_semaphores(count):
    dma = pltpu.SemaphoreType.DMA
    return [
        dma((count, 2)),
        dma((count,)),
        dma((count,)),
        dma((count,)),
        dma((2, count)),
        dma((2, count)),
        dma,
    ]


def group_gather(block):
    seq_count, count = lax.axis_size("seq"), lax.axis_size("blk")
    gathered = pl.pallas_call(
        functools.partial(gather_kernel, count),
        out_shape=jax.ShapeDtypeStruct((seq_count * count,) + block.shape, block.dtype),
        in_specs=[pl.BlockSpec(memory_space=pltpu.VMEM)],
        out_specs=pl.BlockSpec(memory_space=pltpu.VMEM),
        scratch_shapes=gather_semaphores(count),
        compiler_params=pltpu.CompilerParams(
            collective_id=0, has_side_effects=True, vmem_limit_bytes=48 * 2**20
        ),
        name="gather_tokens",
    )(block)
    return gathered.reshape(-1, block.shape[1])


def scatter_kernel(
    count,
    partial,
    out,
    core_slot,
    side_slot,
    line_slot,
    side_out,
    line_out,
    core_sent,
    core_got,
    side_sent,
    side_got,
    line_sent,
    line_got,
):
    seq = lax.axis_index("seq")
    b = lax.axis_index("blk")
    core, side = {"seq": seq ^ 1}, {"seq": seq ^ 2}
    greet((core, side) + tuple({"blk": lax.rem(b + k, count)} for k in range(1, count)))
    away = tuple(range(count // 2, 0, -1)) + tuple(range(count // 2 + 1, count)) + (0,)
    place = [lax.rem(b + k, count) for k in away]

    def to_core(half, k):
        source = partial.at[(seq ^ (1 if half else 3)) * count + place[k]]
        return remote(
            source, core_slot.at[half, k], core_sent.at[half, k], core_got.at[half, k], core
        )

    def to_side(k):
        return remote(side_out.at[k], side_slot.at[k], side_sent.at[k], side_got.at[k], side)

    def along_line(k):
        slot = away[k] - 1
        return remote(
            line_out.at[k],
            line_slot.at[slot],
            line_sent.at[k],
            line_got.at[slot],
            {"blk": place[k]},
        )

    for half in range(2):
        for k in range(count):
            to_core(half, k).start()
    for k in range(count):
        to_core(0, k).wait_recv()
        total = partial[(seq ^ 2) * count + place[k]].astype(jnp.float32)
        total += core_slot[0, k].astype(jnp.float32)
        side_out[k] = total.astype(jnp.bfloat16)
        to_side(k).start()
    for k in range(count):
        to_core(1, k).wait_recv()
        to_side(k).wait_recv()
        total = partial[seq * count + place[k]].astype(jnp.float32)
        total += core_slot[1, k].astype(jnp.float32)
        total += side_slot[k].astype(jnp.float32)
        if k < count - 1:
            line_out[k] = total.astype(jnp.bfloat16)
            along_line(k).start()
        else:
            out[...] = total
    for k in range(count - 1):
        along_line(k).wait_recv()
        out[...] += line_slot[away[k] - 1].astype(jnp.float32)
    for k in range(count):
        to_core(0, k).wait_send()
        to_core(1, k).wait_send()
        to_side(k).wait_send()
        if k < count - 1:
            along_line(k).wait_send()


def group_scatter(partial):
    seq_count, count = lax.axis_size("seq"), lax.axis_size("blk")
    rows, width = partial.shape[0] // (seq_count * count), partial.shape[1]
    dma = pltpu.SemaphoreType.DMA

    def slots(*places):
        return pltpu.VMEM(places + (rows, width), jnp.bfloat16)

    return pl.pallas_call(
        functools.partial(scatter_kernel, count),
        out_shape=jax.ShapeDtypeStruct((rows, width), jnp.float32),
        in_specs=[pl.BlockSpec(memory_space=pltpu.VMEM)],
        out_specs=pl.BlockSpec(memory_space=pltpu.VMEM),
        scratch_shapes=[
            slots(2, count),
            slots(count),
            slots(count - 1),
            slots(count),
            slots(count - 1),
            dma((2, count)),
            dma((2, count)),
            dma((count,)),
            dma((count,)),
            dma((count - 1,)),
            dma((count - 1,)),
        ],
        compiler_params=pltpu.CompilerParams(
            collective_id=1, has_side_effects=True, vmem_limit_bytes=48 * 2**20
        ),
        name="scatter_tokens",
    )(partial.astype(jnp.bfloat16).reshape(seq_count * count, rows, width))


def turn(field_in, cosine, sine):
    half_dim = HEAD_DIM // 2
    first_half = field_in[:, :half_dim]
    second_half = field_in[:, half_dim:]
    return jnp.concatenate(
        [first_half * cosine - second_half * sine, second_half * cosine + first_half * sine],
        axis=-1,
    )


def spread_kernel(
    count,
    pieces,
    w_gate,
    w_up,
    w_output,
    w_down,
    rows_in,
    grads_in,
    attn,
    gate_up,
    out,
    down,
    rows_all,
    grads_all,
    line_sent,
    line_got,
    cross_sent,
    cross_got,
    local_done,
    *gather_sems,
):
    seq, b, section = lax.axis_index("seq"), lax.axis_index("blk"), lax.axis_index("section")
    other = {"section": 1 - section}
    greet(
        (other, {"seq": seq ^ 1}, {"seq": seq ^ 2})
        + tuple({"blk": lax.rem(b + k, count)} for k in range(1, count))
    )
    rows, lanes = w_gate.shape[0], gate_up.shape[2] // 2
    out_rows, down_rows = out.shape[1], down.shape[1]
    far_first = tuple(range(count // 2, 0, -1)) + tuple(range(count // 2 + 1, count))

    def source(kind, j):
        if kind == 0:
            return pieces.at[j]
        weight = w_gate if kind == 1 else w_up
        return weight.at[:, pl.ds(pl.multiple_of((j * 4 + seq) * lanes, lanes), lanes)]

    def target(kind, j):
        if kind == 0:
            return attn.at[section, :, pl.ds(pl.multiple_of(j * rows, rows), rows)]
        return gate_up.at[
            section, pl.ds(pl.multiple_of(j * rows, rows), rows), pl.ds((kind - 1) * lanes, lanes)
        ]

    def along_line(kind, k):
        j = lax.rem(b + k, count)
        return remote(
            source(kind, j),
            target(kind, b),
            line_sent.at[kind, k],
            line_got.at[kind, k],
            {"blk": j},
        )

    def across(kind, j, slot, begin=None):
        spot = target(kind, j)
        return remote(
            spot if begin is None else begin,
            spot,
            cross_sent.at[kind, slot],
            cross_got.at[kind, slot],
            other,
        )

    def own_rows(kind):
        weight, place, size = (w_output, out, out_rows) if kind == 3 else (w_down, down, down_rows)
        begin = weight.at[pl.ds(pl.multiple_of(seq * size, size), size)]
        spot = place.at[section]
        return (
            remote(begin, spot, cross_sent.at[kind, 0], cross_got.at[kind, 0], other),
            pltpu.make_async_copy(begin, spot, local_done.at[kind]),
        )

    def own_piece(kind):
        return (
            across(kind, b, 0, source(kind, b)),
            pltpu.make_async_copy(source(kind, b), target(kind, b), local_done.at[kind]),
        )

    def forward(kind):
        for k in far_first:
            j = lax.rem(b + count - k, count)
            settled(target(kind, j), line_got.at[kind, k], True)
            across(kind, j, k).start()

    first = gather_steps(count, rows_in, rows_all, *gather_sems[:7])
    second = gather_steps(count, grads_in, grads_all, *gather_sems[7:])
    for k in far_first:
        along_line(0, k).start()
    for copy in own_piece(0) + own_rows(3):
        copy.start()
    next(first)
    next(first)
    for kind in (1, 2):
        for k in far_first:
            along_line(kind, k).start()
    next(first)
    forward(0)
    for copy in own_piece(1) + own_piece(2) + own_rows(4):
        copy.start()
    for _ in first:
        pass
    next(second)
    forward(1)
    next(second)
    next(second)
    forward(2)
    for _ in second:
        pass
    for kind in range(3):
        for k in range(count):
            settled(target(kind, 0), cross_got.at[kind, k], True)
            settled(target(kind, 0), cross_sent.at[kind, k], False)
            if k:
                settled(target(kind, 0), line_sent.at[kind, k], False)
        own_piece(kind)[1].wait()
    for kind in (3, 4):
        passed, local = own_rows(kind)
        passed.wait()
        local.wait()


def spread_weights(local_shards, rows_in, grads_in):
    seq_index, seq_count = lax.axis_index("seq"), lax.axis_size("seq")
    count = lax.axis_size("blk")
    gain_attn, w_query, w_key, w_value, w_output, gain_mlp, w_gate, w_up, w_down = local_shards
    rows, width = w_query.shape[0], w_query.shape[1]
    lanes = w_gate.shape[1] // (seq_count * count)
    pad = 16

    def heads_of(weight, per_blk, place):
        head = jnp.arange(count)[:, None] * per_blk + place
        column = (head * HEAD_DIM + jnp.arange(HEAD_DIM)).reshape(-1)
        chosen = jnp.arange(weight.shape[1])[:, None] == column[None, :]
        taken = lax.dot_general(
            chosen.astype(jnp.bfloat16),
            weight,
            (((0,), (1,)), ((), ())),
            preferred_element_type=jnp.float32,
        )
        return taken.astype(jnp.bfloat16).reshape(count, HEAD_DIM, rows)

    kv_per_blk = KV_HEADS // count
    kv_place = seq_index * kv_per_blk // seq_count
    gains = jnp.concatenate(
        [jnp.stack([gain_attn, gain_mlp]), jnp.zeros((pad - 2, rows), jnp.bfloat16)]
    )
    pieces = jnp.concatenate(
        [
            heads_of(w_query, seq_count, seq_index),
            heads_of(w_key, kv_per_blk, kv_place),
            heads_of(w_value, kv_per_blk, kv_place),
            jnp.broadcast_to(gains[None], (count,) + gains.shape),
        ],
        axis=1,
    )
    low = jnp.bfloat16
    out_rows, down_rows = w_output.shape[0] // seq_count, w_down.shape[0] // seq_count
    block = rows_in.shape[0]
    dma = pltpu.SemaphoreType.DMA
    attn, gate_up, out, down, rows_all, grads_all = pl.pallas_call(
        functools.partial(spread_kernel, count),
        out_shape=[
            jax.ShapeDtypeStruct((2, pieces.shape[1], rows * count), low),
            jax.ShapeDtypeStruct((2, rows * count, 2 * lanes), low),
            jax.ShapeDtypeStruct((2, out_rows, w_output.shape[1]), low),
            jax.ShapeDtypeStruct((2, down_rows, w_down.shape[1]), low),
            jax.ShapeDtypeStruct((seq_count * count, block, width), low),
            jax.ShapeDtypeStruct((seq_count * count, block, width), low),
        ],
        in_specs=[pl.BlockSpec(memory_space=pl.ANY)] * 7,
        out_specs=[pl.BlockSpec(memory_space=pl.ANY)] * 6,
        scratch_shapes=[
            dma((3, count)),
            dma((3, count)),
            dma((5, count)),
            dma((5, count)),
            dma((5,)),
        ]
        + gather_semaphores(count) * 2,
        compiler_params=pltpu.CompilerParams(collective_id=2, has_side_effects=True),
        name="spread_weights",
    )(pieces, w_gate, w_up, w_output, w_down, rows_in, grads_in)
    layers = tuple((attn[i], out[i], gate_up[i], down[i]) for i in range(2))
    return layers, rows_all.reshape(-1, width), grads_all.reshape(-1, width)


def own_layer(x_own, normed_all, weights, info):
    attn, out, wide, down = weights
    allowed, cosine, sine = info
    gain_mlp = attn[3 * HEAD_DIM + 1].astype(jnp.float32)
    inv_first = lax.rsqrt(jnp.mean(x_own * x_own, axis=-1, keepdims=True) + EPS)
    mixed_in = back_product(normed_all, attn[: 3 * HEAD_DIM])
    query = turn(mixed_in[:, :HEAD_DIM], cosine, sine).astype(jnp.bfloat16)
    key = turn(mixed_in[:, HEAD_DIM : 2 * HEAD_DIM], cosine, sine).astype(jnp.bfloat16)
    value = mixed_in[:, 2 * HEAD_DIM :].astype(jnp.bfloat16)
    scores = jnp.where(allowed, back_product(query, key) * HEAD_DIM ** (-0.5), MASKED)
    row_top = jnp.max(scores, axis=-1, keepdims=True)
    log_total = row_top + jnp.log(jnp.sum(jnp.exp(scores - row_top), axis=-1, keepdims=True))
    mixed = product(jnp.exp(scores - log_total).astype(jnp.bfloat16), value).astype(jnp.bfloat16)
    hidden = x_own + group_scatter(product(mixed, out))
    normed_mlp, inv_second = rms_forward(hidden, gain_mlp)
    normed_mlp_all = group_gather(normed_mlp.astype(jnp.bfloat16))
    pre = product(normed_mlp_all, wide)
    half = pre.shape[1] // 2
    gate_pre, up_pre = pre[:, :half], pre[:, half:]
    act_low = (jax.nn.silu(gate_pre) * up_pre).astype(jnp.bfloat16)
    result = hidden + group_scatter(product(act_low, down))
    saved = (
        x_own,
        inv_first,
        normed_all,
        query,
        key,
        value,
        log_total,
        mixed,
        hidden,
        inv_second,
        normed_mlp_all,
        gate_pre,
        up_pre,
        act_low,
    )
    return result, saved


def own_layer_back(grad_own, grad_out_all, weights, info, saved):
    attn, out, wide, down = weights
    allowed, cosine, sine = info
    (
        x_own,
        inv_first,
        normed_all,
        query,
        key,
        value,
        log_total,
        mixed,
        hidden,
        inv_second,
        normed_mlp_all,
        gate_pre,
        up_pre,
        act_low,
    ) = saved
    gain_attn = attn[3 * HEAD_DIM].astype(jnp.float32)
    gain_mlp = attn[3 * HEAD_DIM + 1].astype(jnp.float32)
    grad_act = back_product(grad_out_all, down)
    gate_sigmoid = jax.nn.sigmoid(gate_pre)
    grad_gate = (
        grad_act * up_pre * gate_sigmoid * (1.0 + gate_pre * (1.0 - gate_sigmoid))
    ).astype(jnp.bfloat16)
    grad_up = (grad_act * jax.nn.silu(gate_pre)).astype(jnp.bfloat16)
    grad_wide = jnp.concatenate([grad_gate, grad_up], axis=1)
    grad_normed_mlp = group_scatter(back_product(grad_wide, wide))
    grad_hidden_part, gain_mlp_terms = rms_backward(hidden, gain_mlp, inv_second, grad_normed_mlp)
    grad_hidden = grad_own + grad_hidden_part
    grad_branch_all = group_gather(grad_hidden.astype(jnp.bfloat16))
    grad_mixed = back_product(grad_branch_all, out).astype(jnp.bfloat16)
    scores = jnp.where(allowed, back_product(query, key) * HEAD_DIM ** (-0.5), MASKED)
    probs = jnp.exp(scores - log_total)
    grad_probs = back_product(grad_mixed, value)
    centre = jnp.sum(probs * grad_probs, axis=-1, keepdims=True)
    grad_scores = (probs * (grad_probs - centre)).astype(jnp.bfloat16)
    grad_query = (product(grad_scores, key) * HEAD_DIM ** (-0.5)).astype(jnp.bfloat16)
    grad_key = weight_term(grad_scores, query) * HEAD_DIM ** (-0.5)
    grad_value = weight_term(probs.astype(jnp.bfloat16), grad_mixed).astype(jnp.bfloat16)
    grad_query = turn(grad_query.astype(jnp.float32), cosine, -sine).astype(jnp.bfloat16)
    grad_key = turn(grad_key, cosine, -sine).astype(jnp.bfloat16)
    grad_qkv = jnp.concatenate([grad_query, grad_key, grad_value], axis=1)
    grad_normed = group_scatter(product(grad_qkv, attn[: 3 * HEAD_DIM]))
    grad_in_part, gain_attn_terms = rms_backward(x_own, gain_attn, inv_first, grad_normed)
    grads = shortened(
        (
            weight_term(grad_qkv, normed_all),
            weight_term(mixed, grad_branch_all),
            weight_term(normed_mlp_all, grad_wide),
            weight_term(act_low, grad_out_all),
        )
    )
    gains = jnp.stack([jnp.sum(gain_attn_terms, axis=0), jnp.sum(gain_mlp_terms, axis=0)])
    return grad_hidden + grad_in_part, grads, gains


def finish_kernel(
    count,
    attn_one,
    attn_two,
    out_one,
    out_two,
    wide_one,
    wide_two,
    down_one,
    down_two,
    gains,
    swap_rows,
    attn,
    out,
    gate,
    up,
    down,
    gains_out,
    swapped_rows,
    attn_in,
    out_in,
    wide_in,
    down_in,
    attn_slot,
    wide_slot,
    gain_in,
    gain_sum,
    gain_line,
    gain_part,
    gain_side,
    gain_core,
    cross_sent,
    cross_got,
    line_sent,
    line_got,
    side_sent,
    side_got,
    core_sent,
    core_got,
    local_done,
    small_sent,
    small_got,
):
    seq, b, section = lax.axis_index("seq"), lax.axis_index("blk"), lax.axis_index("section")
    at_first = section == 0
    core, side, other = {"seq": seq ^ 1}, {"seq": seq ^ 2}, {"section": 1 - section}
    greet((other, core, side) + tuple({"blk": lax.rem(b + k, count)} for k in range(1, count)))
    rows, lanes = attn.shape[2], gate.shape[1] // (4 * count)
    far_first = tuple(range(count // 2, 0, -1)) + tuple(range(count // 2 + 1, count)) + (0,)
    f32, low = jnp.float32, jnp.bfloat16

    def piece_rows(kind, j):
        if kind == 0:
            return (slice(None), pl.ds(pl.multiple_of(j * rows, rows), rows))
        return (pl.ds(pl.multiple_of(j * rows, rows), rows),)

    pairs = {
        0: (attn_one, attn_two, attn_in),
        1: (wide_one, wide_two, wide_in),
        2: (out_one, out_two, out_in),
        3: (down_one, down_two, down_in),
    }

    def cross(kind, k, begin):
        one, two, held = pairs[kind]
        index = piece_rows(kind, lax.rem(b + k, count)) if kind < 2 else (slice(None),)
        spots = [ref.at[index] for ref in (one, two, held)]
        sems = (cross_sent.at[kind, k], cross_got.at[kind, k])
        if not begin:
            return remote(spots[0], spots[2], *sems, other)

        @pl.when(at_first)
        def _():
            remote(spots[1], spots[2], *sems, other).start()

        @pl.when(jnp.logical_not(at_first))
        def _():
            remote(spots[0], spots[2], *sems, other).start()

    def add_up(kind, k):
        one, two, held = pairs[kind]
        index = piece_rows(kind, lax.rem(b + k, count)) if kind < 2 else (slice(None),)
        cross(kind, k, False).wait_recv()
        own = jnp.where(at_first, one[index], two[index]).astype(f32)
        held[index] = (own + held[index].astype(f32)).astype(low)

    def along_line(kind, k):
        j = lax.rem(b + k, count)
        slot = (attn_slot if kind == 0 else wide_slot).at[k]
        source = pairs[kind][2].at[piece_rows(kind, j)]
        return remote(source, slot, line_sent.at[kind, k], line_got.at[kind, k], {"blk": j})

    def places(kind, k, of_seq):
        if kind == 2:
            size = out_in.shape[0]
            return [out.at[pl.ds(pl.multiple_of(of_seq * size, size), size)]]
        if kind == 3:
            size = down_in.shape[0]
            return [down.at[pl.ds(pl.multiple_of(of_seq * size, size), size)]]
        head = lax.rem(b + count - k, count) * 4 + of_seq
        if kind == 0:
            return [attn.at[head]]
        column = pl.ds(pl.multiple_of(head * lanes, lanes), lanes)
        return [gate.at[:, column], up.at[:, column]]

    def numbered(kind, k, of_seq):
        base = {0: k, 1: count + 2 * k, 2: 3 * count, 3: 3 * count + 1}[kind]
        return [(base + n, spot) for n, spot in enumerate(places(kind, k, of_seq))]

    def made(kind, k):
        if kind > 1:
            return [pairs[kind][2].at[:]]
        if kind == 0:
            return [attn_in.at[piece_rows(0, b)] if k == 0 else attn_slot.at[k]]
        whole = (lambda cut: wide_in.at[piece_rows(1, b) + (cut,)]) if k == 0 else (
            lambda cut: wide_slot.at[k, :, cut]
        )
        return [whole(pl.ds(0, lanes)), whole(pl.ds(lanes, lanes))]

    def sends(kind, k):
        found = []
        for (n, spot), begin in zip(numbered(kind, k, seq), made(kind, k)):
            found.append(
                (
                    remote(begin, spot, side_sent.at[n], side_got.at[n], side),
                    remote(begin, spot, core_sent.at[0, n], core_got.at[0, n], core),
                    pltpu.make_async_copy(begin, spot, local_done.at[n]),
                )
            )
        return found

    def publish(kind, k):
        for copies in sends(kind, k):
            for copy in copies:
                copy.start()

    def passes(kind, k):
        return [
            remote(spot, spot, core_sent.at[1, n], core_got.at[1, n], core)
            for n, spot in numbered(kind, k, seq ^ 2)
        ]

    def from_line(kind, k):
        along_line(kind, k).wait_recv()
        publish(kind, k)

    def from_side(kind, k):
        for n, spot in numbered(kind, k, seq ^ 2):
            settled(spot, side_got.at[n], True)
        for copy in passes(kind, k):
            copy.start()

    def small(n, source, slot, device):
        return remote(source, slot, small_sent.at[n], small_got.at[n], device)

    swap = small(0, swap_rows.at[:], swapped_rows.at[:], other)
    swap.start()
    gain_cross = small(1, gains.at[1 - section], gain_in.at[:], other)
    gain_cross.start()
    cross(2, 0, True)
    for kind, k in ((1, far_first[0]), (1, 0)):
        cross(kind, k, True)
    cross(3, 0, True)
    for kind in (1, 0):
        for k in far_first:
            if (kind, k) not in ((1, far_first[0]), (1, 0)):
                cross(kind, k, True)

    def gain_piece(j):
        return gain_sum.at[:, pl.ds(pl.multiple_of(j * rows, rows), rows)]

    def gain_send(k):
        j = lax.rem(b + k, count)
        return small(3 + k, gain_piece(j), gain_line.at[k], {"blk": j})

    gain_cross.wait_recv()
    gain_sum[...] = gains[section] + gain_in[...]
    for k in range(1, count):
        gain_send(k).start()

    add_up(2, 0)
    publish(2, 0)
    add_up(1, far_first[0])
    along_line(1, far_first[0]).start()
    add_up(1, 0)
    publish(1, 0)
    from_side(2, 0)
    for k in range(1, count):
        gain_send(k).wait_recv()
    gain_part[...] = gain_sum[:, pl.ds(pl.multiple_of(b * rows, rows), rows)]
    for k in range(1, count):
        gain_part[...] += gain_line[k]
    gain_to_side = small(2, gain_part.at[:], gain_side.at[:], side)
    gain_to_side.start()
    add_up(3, 0)
    publish(3, 0)
    for k in far_first[1:-1]:
        add_up(1, k)
        along_line(1, k).start()
    from_side(1, 0)
    gain_to_side.wait_recv()
    gain_side[...] += gain_part[...]
    gain_to_core = small(3, gain_side.at[:], gain_core.at[:], core)
    gain_to_core.start()
    from_line(1, far_first[0])
    from_side(3, 0)
    add_up(0, far_first[0])
    along_line(0, far_first[0]).start()
    from_line(1, far_first[1])
    add_up(0, far_first[1])
    along_line(0, far_first[1]).start()
    from_side(1, far_first[0])
    from_line(1, far_first[2])
    add_up(0, far_first[2])
    along_line(0, far_first[2]).start()
    add_up(0, 0)
    publish(0, 0)
    from_side(1, far_first[1])
    gain_to_core.wait_recv()
    gains_out[...] = gain_side[...] + gain_core[...]
    from_line(0, far_first[0])
    from_side(1, far_first[2])
    from_line(0, far_first[1])
    from_line(0, far_first[2])
    from_side(0, 0)
    for k in far_first[:-1]:
        from_side(0, k)
    every = [(0, k) for k in range(count)] + [(1, k) for k in range(count)] + [(2, 0), (3, 0)]
    for kind, k in every:
        cross(kind, k, False).wait_send()
        if kind < 2 and k:
            along_line(kind, k).wait_send()
        for to_side, to_core, local in sends(kind, k):
            to_side.wait_send()
            to_core.wait_send()
            local.wait()
        for copy in passes(kind, k):
            copy.wait_send()
        for half, of_seq in ((0, seq ^ 1), (1, seq ^ 3)):
            for n, spot in numbered(kind, k, of_seq):
                settled(spot, core_got.at[half, n], True)
    swap.wait()
    gain_cross.wait_send()
    for k in range(1, count):
        gain_send(k).wait_send()
    gain_to_side.wait_send()
    gain_to_core.wait_send()


def finish_grads(first, second, gains, swap_rows):
    seq_count, count = lax.axis_size("seq"), lax.axis_size("blk")
    low, f32 = jnp.bfloat16, jnp.float32
    attn, out, wide, down = first
    rows = wide.shape[0] // count
    lanes = wide.shape[1] // 2
    parts = seq_count * count
    dma = pltpu.SemaphoreType.DMA
    vmem = pltpu.VMEM
    sends = 3 * count + 2
    heads = attn.shape[0]
    operands = [array for pair in zip(first, second) for array in pair] + [gains, swap_rows]
    in_vmem = pl.BlockSpec(memory_space=vmem)
    anywhere = pl.BlockSpec(memory_space=pl.ANY)
    small = (gains.shape[1], rows)
    attn, out, gate, up, down, gains, swapped_rows = pl.pallas_call(
        functools.partial(finish_kernel, count),
        out_shape=[
            jax.ShapeDtypeStruct((parts, heads, rows), low),
            jax.ShapeDtypeStruct((out.shape[0] * seq_count, out.shape[1]), low),
            jax.ShapeDtypeStruct((rows, lanes * parts), low),
            jax.ShapeDtypeStruct((rows, lanes * parts), low),
            jax.ShapeDtypeStruct((down.shape[0] * seq_count, down.shape[1]), low),
            jax.ShapeDtypeStruct(small, f32),
            jax.ShapeDtypeStruct(swap_rows.shape, low),
        ],
        in_specs=[in_vmem] * len(operands),
        out_specs=[anywhere] * 5 + [in_vmem, in_vmem],
        scratch_shapes=[
            vmem(attn.shape, low),
            vmem(out.shape, low),
            vmem(wide.shape, low),
            vmem(down.shape, low),
            vmem((count, heads, rows), low),
            vmem((count, rows, 2 * lanes), low),
            vmem(gains.shape[1:], f32),
            vmem(gains.shape[1:], f32),
            vmem((count,) + small, f32),
            vmem(small, f32),
            vmem(small, f32),
            vmem(small, f32),
            dma((4, count)),
            dma((4, count)),
            dma((2, count)),
            dma((2, count)),
            dma((sends,)),
            dma((sends,)),
            dma((2, sends)),
            dma((2, sends)),
            dma((sends,)),
            dma((4 + count,)),
            dma((4 + count,)),
        ],
        compiler_params=pltpu.CompilerParams(
            collective_id=3, has_side_effects=True, vmem_limit_bytes=48 * 2**20
        ),
        name="finish_grads",
    )(*operands)
    attn = attn.astype(f32)

    def heads_back(start, copies):
        part = attn[:, start : start + HEAD_DIM].reshape(-1, copies, HEAD_DIM, rows).sum(1)
        return part.reshape(-1, rows).T

    copies = HEADS // KV_HEADS
    return (
        swapped_rows,
        gains,
        heads_back(0, 1),
        heads_back(HEAD_DIM, copies),
        heads_back(2 * HEAD_DIM, copies),
        out.astype(f32),
        gate.astype(f32),
        up.astype(f32),
        down.astype(f32),
    )


def head_shards(inputs, cotangent, doc_lengths, *params):
    section = lax.axis_index("section")
    at_first = section == 0
    tokens = inputs.shape[2] * lax.axis_size("seq") * lax.axis_size("blk")
    rows_own = lax.dynamic_index_in_dim(inputs, section, 0, keepdims=False)[0]
    grads_own = lax.dynamic_index_in_dim(cotangent, section, 0, keepdims=False)[0]
    (first, second), rows_all, grads_all = spread_weights(
        tuple(weight[0] for weight in params), rows_own, grads_own
    )
    lengths = lax.dynamic_index_in_dim(doc_lengths, section, 0, keepdims=False)[0]
    token_index = jnp.arange(tokens, dtype=jnp.int32)
    segment, position = doc_info(lengths, token_index)
    allowed = (segment[:, None] == segment[None, :]) & (
        token_index[None, :] <= token_index[:, None]
    )
    half_dim = HEAD_DIM // 2
    frequency = THETA ** (-2.0 * jnp.arange(half_dim, dtype=jnp.float32) / HEAD_DIM)
    angles = position.astype(jnp.float32)[:, None] * frequency
    info = (allowed, jnp.cos(angles), jnp.sin(angles))
    x_own = rows_own.astype(jnp.float32)
    gain = first[0][3 * HEAD_DIM].astype(jnp.float32)
    normed_all = rms_forward(rows_all.astype(jnp.float32), gain)[0].astype(jnp.bfloat16)
    result, saved_first = own_layer(x_own, normed_all, first, info)
    between = result.astype(jnp.bfloat16)
    x_own = between.astype(jnp.float32)
    gain = second[0][3 * HEAD_DIM].astype(jnp.float32)
    normed_all = group_gather(rms_forward(x_own, gain)[0].astype(jnp.bfloat16))
    result, saved_second = own_layer(x_own, normed_all, second, info)
    final = result.astype(jnp.bfloat16)
    grad_between, grads_second, gains_second = own_layer_back(
        grads_own.astype(jnp.float32), grads_all, second, info, saved_second
    )
    grad_between = grad_between.astype(jnp.bfloat16)
    grad_start, grads_first, gains_first = own_layer_back(
        grad_between.astype(jnp.float32), group_gather(grad_between), first, info, saved_first
    )
    grad_start = grad_start.astype(jnp.bfloat16)
    kept = jnp.where(
        at_first, jnp.stack([between, grad_start]), jnp.stack([final, grad_between])
    )
    sent = jnp.where(
        at_first, jnp.stack([final, grad_between]), jnp.stack([between, grad_start])
    )
    gains = jnp.stack([gains_first, gains_second])
    gains = jnp.concatenate([gains, jnp.zeros((2, 6) + gains.shape[2:], jnp.float32)], axis=1)
    swapped_rows, gains, query, key, value, out, gate, up, down = finish_grads(
        grads_first, grads_second, gains, sent
    )
    pairs = jnp.where(
        at_first, jnp.stack([kept, swapped_rows], axis=1), jnp.stack([swapped_rows, kept], axis=1)
    )
    return (
        pairs[0][None, :, None],
        pairs[1][None, :, None],
        gains[0][None],
        query[None],
        key[None],
        value[None],
        out[None],
        gains[1][None],
        gate[None],
        up[None],
        down[None],
    )

def solution(mesh):
    placed = (
        P(None, None, ("seq", "blk"), None),
        P(None, None, ("seq", "blk"), None),
        P(),
        P("section", "blk"),
        P("section", "blk", None),
        P("section", "blk", None),
        P("section", "blk", None),
        P("section", "blk", None),
        P("section", "blk"),
        P("section", "blk", None),
        P("section", "blk", None),
        P("section", "blk", None),
    )
    one_head_each = mesh.shape["seq"] == 4 and mesh.shape["blk"] == HEADS // 4
    return jax.shard_map(
        head_shards if one_head_each else shards,
        mesh=mesh,
        in_specs=placed,
        out_specs=(
            P("section", None, None, ("seq", "blk"), None),
            P("section", None, None, ("seq", "blk"), None),
            P("section", "blk"),
            P("section", "blk", None),
            P("section", "blk", None),
            P("section", "blk", None),
            P("section", "blk", None),
            P("section", "blk"),
            P("section", "blk", None),
            P("section", "blk", None),
            P("section", "blk", None),
        ),
        check_vma=False,
    )
```

```python
import functools

import jax
import jax.numpy as jnp
from jax import lax
from jax.experimental import pallas as pl
from jax.experimental.pallas import tpu as pltpu
from jax.sharding import PartitionSpec as P

HEADS = 16
KV_HEADS = 8
HEAD_DIM = 96


EPS = 1e-05
THETA = 100000.0
MASKED = -1e30


def passed_along(value, axis, steps):
    count = lax.axis_size(axis)
    first, last = (max(0, -steps), min(count, count - steps))
    return lax.ppermute(value, axis, [(source, source + steps) for source in range(first, last)])


def shortened(value):
    return jax.tree.map(lambda a: a.astype(jnp.bfloat16) if a.dtype == jnp.float32 else a, value)


def product(left_side, right_side):
    return jnp.dot(left_side, right_side, preferred_element_type=jnp.float32)


def back_product(left_side, right_side):
    return lax.dot_general(
        left_side, right_side, (((1,), (1,)), ((), ())), preferred_element_type=jnp.float32
    )


def doc_info(lengths, token_index):
    doc_ends = jnp.cumsum(lengths, axis=-1)
    passed = (doc_ends[..., None, :] <= token_index[..., None]).astype(jnp.int32)
    segment = jnp.sum(passed, axis=-1)
    offset = jnp.sum(passed * lengths[..., None, :], axis=-1)
    return (segment, token_index - offset)


def rotate(field_in, position, turn_sign):
    half_dim = field_in.shape[-1] // 2
    frequency = THETA ** (-2.0 * jnp.arange(half_dim, dtype=jnp.float32) / field_in.shape[-1])
    angles = position.astype(jnp.float32)[:, None] * frequency
    cosine = jnp.cos(angles)[:, None, :]
    sine_part = turn_sign * jnp.sin(angles)[:, None, :]
    first_half = field_in[..., :half_dim]
    second_half = field_in[..., half_dim:]
    return jnp.concatenate(
        [
            first_half * cosine - second_half * sine_part,
            second_half * cosine + first_half * sine_part,
        ],
        axis=-1,
    )


def rms_forward(field_in, gain_row):
    inv_root = lax.rsqrt(jnp.mean(field_in * field_in, axis=-1, keepdims=True) + EPS)
    return (field_in * inv_root * gain_row, inv_root)


def rms_backward(field_in, gain_row, inv_root, grad_normed):
    scaled = gain_row * grad_normed
    grad_field = inv_root * scaled - field_in * inv_root**3 * jnp.mean(
        scaled * field_in, axis=-1, keepdims=True
    )
    return (grad_field, grad_normed * field_in * inv_root)


def token_place(block_id, row_ids, per_device, blk_count):
    return (row_ids // per_device * blk_count + block_id) * per_device + row_ids % per_device


def masks_for(lengths, blk_index, per_device, blk_count, seq_count):
    block_tokens = seq_count * per_device
    row_ids = jnp.arange(block_tokens, dtype=jnp.int32)
    query_index = token_place(blk_index, row_ids, per_device, blk_count)
    all_ids = jnp.arange(blk_count * block_tokens, dtype=jnp.int32)
    key_index = token_place(all_ids // block_tokens, all_ids % block_tokens, per_device, blk_count)
    query_seg, _ = doc_info(lengths, query_index)
    key_seg, _ = doc_info(lengths, key_index)
    return (query_index, key_index, query_seg, key_seg)


def head_scores(queries, key_rows, allowed, kv_local):
    grouped = queries.reshape(queries.shape[0], kv_local, -1, HEAD_DIM)
    key_heads = key_rows.reshape(key_rows.shape[0], kv_local, HEAD_DIM)
    scores = jnp.einsum(
        "rkgd,lkd->kgrl", grouped, key_heads, preferred_element_type=jnp.float32
    ) * HEAD_DIM ** (-0.5)
    return (jnp.where(allowed, scores, MASKED), grouped, key_heads)


def attend_forward(operands, query_index, key_index, kv_local):
    queries, key_rows, value_rows, query_seg, key_seg = operands
    allowed = (query_seg[:, None] == key_seg[None, :]) & (
        key_index[None, :] <= query_index[:, None]
    )
    scores, grouped, key_heads = head_scores(queries, key_rows, allowed, kv_local)
    row_top = jnp.max(scores, axis=-1, keepdims=True)
    log_total = row_top + jnp.log(jnp.sum(jnp.exp(scores - row_top), axis=-1, keepdims=True))
    weights_low = jnp.exp(scores - log_total).astype(jnp.bfloat16)
    value_heads = value_rows.reshape(value_rows.shape[0], kv_local, HEAD_DIM)
    mixed_heads = jnp.einsum(
        "kgrl,lkd->rkgd", weights_low, value_heads, preferred_element_type=jnp.float32
    )
    return (mixed_heads.reshape(queries.shape).astype(jnp.bfloat16), log_total)


def attend_backward(operands, query_index, key_index, kv_local):
    queries, key_rows, value_rows, grad_mixed, log_total, query_seg, key_seg = operands
    allowed = (query_seg[:, None] == key_seg[None, :]) & (
        key_index[None, :] <= query_index[:, None]
    )
    scores, grouped, key_heads = head_scores(queries, key_rows, allowed, kv_local)
    attn_probs = jnp.exp(scores - log_total)
    value_heads = value_rows.reshape(value_rows.shape[0], kv_local, HEAD_DIM)
    grad_heads = grad_mixed.reshape(grouped.shape)
    grad_values = jnp.einsum(
        "kgrl,rkgd->lkd",
        attn_probs.astype(jnp.bfloat16),
        grad_heads,
        preferred_element_type=jnp.float32,
    )
    grad_probs = jnp.einsum(
        "rkgd,lkd->kgrl", grad_heads, value_heads, preferred_element_type=jnp.float32
    )
    centre = jnp.sum(attn_probs * grad_probs, axis=-1, keepdims=True)
    grad_scores = (attn_probs * (grad_probs - centre)).astype(jnp.bfloat16)
    grad_queries = jnp.einsum(
        "kgrl,lkd->rkgd", grad_scores, key_heads, preferred_element_type=jnp.float32
    ) * HEAD_DIM ** (-0.5)
    grad_keys = jnp.einsum(
        "kgrl,rkgd->lkd", grad_scores, grouped, preferred_element_type=jnp.float32
    ) * HEAD_DIM ** (-0.5)
    return (
        grad_queries.reshape(queries.shape).astype(jnp.bfloat16),
        grad_keys.reshape(key_rows.shape),
        grad_values.reshape(value_rows.shape),
    )


def layer_forward(section_in, lengths, weights, placing):
    shard_id, blk_index, seq_count, blk_count = placing
    gain_attn, w_query, w_key, w_value, w_output, gain_mlp, w_gate, w_up, w_down = weights
    seqs_here, per_device, width = section_in.shape
    token_rows = seqs_here * per_device
    copies = max(1, seq_count // KV_HEADS)
    kv_local = KV_HEADS * copies // seq_count
    token_index = shard_id * per_device + jnp.arange(per_device, dtype=jnp.int32)
    _, position = doc_info(lengths, token_index)
    position = position.reshape(token_rows)
    flat_in = section_in.reshape(token_rows, width)
    normed, inv_first = rms_forward(flat_in, gain_attn.astype(jnp.float32))
    normed_low = normed.astype(jnp.bfloat16)
    query_pre = product(normed_low, w_query).reshape(token_rows, HEADS, HEAD_DIM)
    key_pre = product(normed_low, w_key).reshape(token_rows, KV_HEADS, HEAD_DIM)
    value_pre = product(normed_low, w_value).reshape(token_rows, KV_HEADS, HEAD_DIM)
    query_rot = (
        rotate(query_pre, position, 1.0).astype(jnp.bfloat16).reshape(seqs_here, per_device, width)
    )
    key_rot = rotate(key_pre, position, 1.0).astype(jnp.bfloat16)
    spread_shape = (token_rows, KV_HEADS, copies, HEAD_DIM)
    key_rep = jnp.broadcast_to(key_rot[:, :, None, :], spread_shape).reshape(
        seqs_here, per_device, -1
    )
    value_rep = jnp.broadcast_to(
        value_pre.astype(jnp.bfloat16)[:, :, None, :], spread_shape
    ).reshape(seqs_here, per_device, -1)
    heads_query, heads_key, heads_value = (
        lax.all_to_all(query_rot, "seq", split_axis=2, concat_axis=1, tiled=True),
        lax.all_to_all(key_rep, "seq", split_axis=2, concat_axis=1, tiled=True),
        lax.all_to_all(value_rep, "seq", split_axis=2, concat_axis=1, tiled=True),
    )
    keys_all, values_all = (
        lax.all_gather(heads_key, "blk", axis=1, tiled=True),
        lax.all_gather(heads_value, "blk", axis=1, tiled=True),
    )
    query_index, key_index, query_seg, key_seg = masks_for(
        lengths, blk_index, per_device, blk_count, seq_count
    )
    heads_mixed, log_total = lax.map(
        lambda operands: attend_forward(operands, query_index, key_index, kv_local),
        (heads_query, keys_all, values_all, query_seg, key_seg),
    )
    token_mixed = lax.all_to_all(
        heads_mixed, "seq", split_axis=1, concat_axis=2, tiled=True
    ).reshape(token_rows, width)
    hidden = flat_in + product(token_mixed, w_output)
    normed_mlp, inv_second = rms_forward(hidden, gain_mlp.astype(jnp.float32))
    normed_mlp_low = normed_mlp.astype(jnp.bfloat16)
    gate_pre = product(normed_mlp_low, w_gate)
    up_pre = product(normed_mlp_low, w_up)
    act_low = (jax.nn.silu(gate_pre) * up_pre).astype(jnp.bfloat16)
    result = hidden + product(act_low, w_down)
    saved_state = (
        flat_in,
        normed_low,
        inv_first,
        position,
        heads_query,
        keys_all,
        values_all,
        log_total,
        token_mixed,
        hidden,
        inv_second,
        normed_mlp_low,
        gate_pre,
        up_pre,
        act_low,
        lengths,
    )
    return (result.reshape(section_in.shape), saved_state)


def layer_backward(upstream, saved_state, weights, placing):
    shard_id, blk_index, seq_count, blk_count = placing
    gain_attn, w_query, w_key, w_value, w_output, gain_mlp, w_gate, w_up, w_down = weights
    (
        flat_in,
        normed_low,
        inv_first,
        position,
        heads_query,
        keys_all,
        values_all,
        log_total,
        token_mixed,
        hidden,
        inv_second,
        normed_mlp_low,
        gate_pre,
        up_pre,
        act_low,
        lengths,
    ) = saved_state
    seqs_here, per_device, width = upstream.shape
    token_rows = seqs_here * per_device
    copies = max(1, seq_count // KV_HEADS)
    kv_local = KV_HEADS * copies // seq_count
    grad_rows = upstream.reshape(token_rows, width)
    grad_out_low = grad_rows.astype(jnp.bfloat16)
    grad_act = back_product(grad_out_low, w_down)
    gate_sigmoid = jax.nn.sigmoid(gate_pre)
    grad_gate_low = (
        grad_act * up_pre * gate_sigmoid * (1.0 + gate_pre * (1.0 - gate_sigmoid))
    ).astype(jnp.bfloat16)
    grad_up_low = (grad_act * jax.nn.silu(gate_pre)).astype(jnp.bfloat16)
    grad_normed_mlp = back_product(grad_gate_low, w_gate) + back_product(grad_up_low, w_up)
    grad_hidden_part, gain_mlp_terms = rms_backward(
        hidden, gain_mlp.astype(jnp.float32), inv_second, grad_normed_mlp
    )
    grad_hidden = grad_rows + grad_hidden_part
    grad_branch_low = grad_hidden.astype(jnp.bfloat16)
    grad_mixed_low = (
        back_product(grad_branch_low, w_output)
        .astype(jnp.bfloat16)
        .reshape(seqs_here, per_device, width)
    )
    heads_grad = lax.all_to_all(grad_mixed_low, "seq", split_axis=2, concat_axis=1, tiled=True)
    query_index, key_index, query_seg, key_seg = masks_for(
        lengths, blk_index, per_device, blk_count, seq_count
    )
    grad_heads_query, grad_keys_all, grad_values_all = lax.map(
        lambda operands: attend_backward(operands, query_index, key_index, kv_local),
        (heads_query, keys_all, values_all, heads_grad, log_total, query_seg, key_seg),
    )
    grad_key_own, grad_value_own = (
        lax.psum_scatter(
            grad_keys_all.astype(jnp.bfloat16), "blk", scatter_dimension=1, tiled=True
        ).astype(jnp.float32),
        lax.psum_scatter(
            grad_values_all.astype(jnp.bfloat16), "blk", scatter_dimension=1, tiled=True
        ).astype(jnp.float32),
    )
    token_query, token_key, token_value = (
        lax.all_to_all(grad_heads_query, "seq", split_axis=1, concat_axis=2, tiled=True),
        lax.all_to_all(
            grad_key_own.astype(jnp.bfloat16), "seq", split_axis=1, concat_axis=2, tiled=True
        ),
        lax.all_to_all(
            grad_value_own.astype(jnp.bfloat16), "seq", split_axis=1, concat_axis=2, tiled=True
        ),
    )
    grad_key_sum = jnp.sum(
        token_key.astype(jnp.float32).reshape(token_rows, KV_HEADS, copies, HEAD_DIM), axis=2
    )
    grad_value_sum = jnp.sum(
        token_value.astype(jnp.float32).reshape(token_rows, KV_HEADS, copies, HEAD_DIM), axis=2
    )
    grad_query_low = (
        rotate(token_query.astype(jnp.float32).reshape(token_rows, HEADS, HEAD_DIM), position, -1.0)
        .astype(jnp.bfloat16)
        .reshape(token_rows, width)
    )
    grad_key_low = (
        rotate(grad_key_sum, position, -1.0)
        .astype(jnp.bfloat16)
        .reshape(token_rows, KV_HEADS * HEAD_DIM)
    )
    grad_value_low = grad_value_sum.astype(jnp.bfloat16).reshape(token_rows, KV_HEADS * HEAD_DIM)
    grad_normed = (
        back_product(grad_query_low, w_query)
        + back_product(grad_key_low, w_key)
        + back_product(grad_value_low, w_value)
    )
    grad_in_part, gain_attn_terms = rms_backward(
        flat_in, gain_attn.astype(jnp.float32), inv_first, grad_normed
    )
    grad_input = (grad_hidden + grad_in_part).reshape(upstream.shape)
    weight_rows = (
        gain_attn_terms,
        normed_low,
        grad_query_low,
        grad_key_low,
        grad_value_low,
        token_mixed,
        grad_branch_low,
        gain_mlp_terms,
        normed_mlp_low,
        grad_gate_low,
        grad_up_low,
        act_low,
        grad_out_low,
    )
    return (grad_input, weight_rows)


def weight_term(inputs_low, outputs_low):
    if outputs_low is None:
        return jnp.sum(inputs_low, axis=0)
    return lax.dot_general(
        inputs_low, outputs_low, (((0,), (0,)), ((), ())), preferred_element_type=jnp.float32
    )


def shards(
    inputs,
    cotangent,
    doc_lengths,
    attention_gain,
    w_query,
    w_key,
    w_value,
    w_output,
    mlp_gain,
    w_gate,
    w_up,
    w_down,
):
    at_first = lax.axis_index("section") == 0
    seq_count = lax.axis_size("seq")
    blk_count = lax.axis_size("blk")
    blk_index = lax.axis_index("blk")
    shard_id = lax.axis_index("seq") * blk_count + blk_index
    placing = (shard_id, blk_index, seq_count, blk_count)
    micro_count = inputs.shape[0]
    local_shards = (
        attention_gain[0],
        w_query[0],
        w_key[0],
        w_value[0],
        w_output[0],
        mlp_gain[0],
        w_gate[0],
        w_up[0],
        w_down[0],
    )
    weights = (
        lax.all_gather(local_shards[0], "blk", axis=0, tiled=True),
        lax.all_gather(local_shards[1], "blk", axis=0, tiled=True),
        lax.all_gather(local_shards[2], "blk", axis=0, tiled=True),
        lax.all_gather(local_shards[3], "blk", axis=0, tiled=True),
        lax.all_gather(local_shards[4], "blk", axis=0, tiled=True),
        lax.all_gather(local_shards[5], "blk", axis=0, tiled=True),
        lax.all_gather(local_shards[6], "blk", axis=0, tiled=True),
        lax.all_gather(local_shards[7], "blk", axis=0, tiled=True),
        lax.all_gather(local_shards[8], "blk", axis=0, tiled=True),
    )
    received = jnp.zeros(inputs.shape[1:], jnp.bfloat16)
    saved_states = []
    section_outs = []
    for tick_index in range(micro_count + 1):
        fresh_input = inputs[min(tick_index, micro_count - 1)]
        section_in = jnp.where(at_first, fresh_input, received).astype(jnp.float32)
        lengths = jnp.where(
            at_first,
            doc_lengths[min(tick_index, micro_count - 1)],
            doc_lengths[max(tick_index - 1, 0)],
        )
        result, saved_state = layer_forward(section_in, lengths, weights, placing)
        result_low = result.astype(jnp.bfloat16)
        if tick_index < micro_count:
            received = passed_along(result_low, "section", 1)
        saved_states.append(saved_state)
        section_outs.append(result_low)
    weights = (
        lax.all_gather(local_shards[0], "blk", axis=0, tiled=True),
        lax.all_gather(local_shards[1], "blk", axis=0, tiled=True),
        lax.all_gather(local_shards[2], "blk", axis=0, tiled=True),
        lax.all_gather(local_shards[3], "blk", axis=0, tiled=True),
        lax.all_gather(local_shards[4], "blk", axis=0, tiled=True),
        lax.all_gather(local_shards[5], "blk", axis=0, tiled=True),
        lax.all_gather(local_shards[6], "blk", axis=0, tiled=True),
        lax.all_gather(local_shards[7], "blk", axis=0, tiled=True),
        lax.all_gather(local_shards[8], "blk", axis=0, tiled=True),
    )
    back_in = jnp.zeros(cotangent.shape[1:], jnp.bfloat16)
    grad_outs = []
    row_sets = []
    for tick_index in range(micro_count + 1):
        saved_state = jax.tree.map(
            lambda first_pick, second_pick: jnp.where(at_first, first_pick, second_pick),
            saved_states[max(tick_index - 1, 0)],
            saved_states[min(tick_index + 1, micro_count)],
        )
        upstream = jnp.where(at_first, back_in, cotangent[min(tick_index, micro_count - 1)]).astype(
            jnp.float32
        )
        grad_input, weight_rows = layer_backward(upstream, saved_state, weights, placing)
        grad_low = grad_input.astype(jnp.bfloat16)
        if tick_index < micro_count:
            back_in = passed_along(grad_low, "section", -1)
        grad_outs.append(grad_low)
        row_sets.append(weight_rows)
    activations = jnp.stack(
        [
            jnp.where(at_first, section_outs[index_m], section_outs[index_m + 1])
            for index_m in range(micro_count)
        ]
    )[None]
    input_grads = jnp.stack(
        [
            jnp.where(at_first, grad_outs[index_m + 1], grad_outs[index_m])
            for index_m in range(micro_count)
        ]
    )[None]
    picked = [
        jax.tree.map(
            lambda first_pick, second_pick: jnp.where(at_first, first_pick, second_pick),
            row_sets[index_m + 1],
            row_sets[index_m],
        )
        for index_m in range(micro_count)
    ]
    merged = jax.tree.map(lambda *pieces: jnp.concatenate(pieces, axis=0), *picked)
    (
        gain_attn_terms,
        normed_low,
        grad_query_low,
        grad_key_low,
        grad_value_low,
        token_mixed,
        grad_branch_low,
        gain_mlp_terms,
        normed_mlp_low,
        grad_gate_low,
        grad_up_low,
        act_low,
        grad_out_low,
    ) = merged
    grad_pairs = (
        (gain_attn_terms, None),
        (normed_low, grad_query_low),
        (normed_low, grad_key_low),
        (normed_low, grad_value_low),
        (token_mixed, grad_branch_low),
        (gain_mlp_terms, None),
        (normed_mlp_low, grad_gate_low),
        (normed_mlp_low, grad_up_low),
        (act_low, grad_out_low),
    )
    shares = tuple(
        (
            lax.psum_scatter(
                weight_term(left_side, right_side).astype(jnp.bfloat16),
                "blk",
                scatter_dimension=0,
                tiled=True,
            ).astype(jnp.float32)
            for left_side, right_side in grad_pairs
        )
    )
    shares = jax.tree.map(lambda part: part.astype(jnp.float32), lax.psum(shortened(shares), "seq"))
    return (
        activations,
        input_grads,
        shares[0][None],
        shares[1][None],
        shares[2][None],
        shares[3][None],
        shares[4][None],
        shares[5][None],
        shares[6][None],
        shares[7][None],
        shares[8][None],
    )


MESH = pl.DeviceIdType.MESH


def remote(source, target, sent, arrived, device):
    return pltpu.make_async_remote_copy(
        source, target, sent, arrived, device_id=device, device_id_type=MESH
    )


def greet(partners):
    barrier = pltpu.get_barrier_semaphore()
    for device in partners:
        pl.semaphore_signal(barrier, 1, device_id=device, device_id_type=MESH)
    pl.semaphore_wait(barrier, len(partners))


def settled(spot, semaphore, received):
    copy = remote(spot, spot, semaphore, semaphore, {"seq": lax.axis_index("seq") ^ 1})
    if received:
        copy.wait_recv()
    else:
        copy.wait_send()


def gather_steps(
    count, own, out, line_sent, line_got, side_sent, side_got, core_sent, core_got, local_done
):
    seq, b = lax.axis_index("seq"), lax.axis_index("blk")
    core, side = {"seq": seq ^ 1}, {"seq": seq ^ 2}
    base, side_base = seq * count, (seq ^ 2) * count

    def along_line(j, way, source=None):
        device = {"blk": b + (1 if way else -1)}
        spot = out.at[base + j]
        return remote(
            spot if source is None else source, spot, line_sent.at[j, way], line_got.at[j], device
        )

    def to_side(j, source=None):
        spot = out.at[base + j]
        return remote(
            spot if source is None else source, spot, side_sent.at[j], side_got.at[j], side
        )

    def to_core(half, j, source=None):
        spot = out.at[(side_base if half else base) + j]
        return remote(
            spot if source is None else source,
            spot,
            core_sent.at[half, j],
            core_got.at[half, j],
            core,
        )

    local = pltpu.make_async_copy(own, out.at[base + b], local_done)
    local.start()
    to_side(b, own).start()

    @pl.when(b > 0)
    def _():
        along_line(b, 0, own).start()

    @pl.when(b < count - 1)
    def _():
        along_line(b, 1, own).start()

    to_core(0, b, own).start()
    yield "sent"

    def from_line(j, way):
        settled(out.at[base + j], line_got.at[j], True)

        @pl.when((b < count - 1) if way else (b > 0))
        def _():
            along_line(j, way).start()

        to_side(j).start()
        to_core(0, j).start()

    def from_side(j):
        settled(out.at[side_base + j], side_got.at[j], True)
        to_core(1, j).start()

    for k in range(1, count + 1):
        if k < count:
            pl.when(b - k >= 0)(functools.partial(from_line, b - k, 1))
            pl.when(b + k < count)(functools.partial(from_line, b + k, 0))
        if k == 1:
            from_side(b)
        else:
            pl.when(b - k + 1 >= 0)(functools.partial(from_side, b - k + 1))
            pl.when(b + k - 1 < count)(functools.partial(from_side, b + k - 1))
        if k == count - 1:
            local.wait()
        yield "line" if k == count - 1 else "side" if k == count else "step"
    for half, corner in ((0, seq ^ 1), (1, seq ^ 3)):
        for j in range(count):
            settled(out.at[corner * count + j], core_got.at[half, j], True)
        yield "corner" if half else "near"
    for j in range(count):
        to_side(j).wait_send()
        to_core(0, j).wait_send()
        to_core(1, j).wait_send()

    @pl.when(b > 0)
    def _():
        along_line(b, 0).wait_send()

    @pl.when(b < count - 1)
    def _():
        along_line(b, 1).wait_send()

    for k in range(1, count):

        @pl.when((b - k >= 0) & (b < count - 1))
        def _():
            along_line(b - k, 1).wait_send()

        @pl.when((b + k < count) & (b > 0))
        def _():
            along_line(b + k, 0).wait_send()


def gather_semaphores(count):
    dma = pltpu.SemaphoreType.DMA
    return [
        dma((count, 2)),
        dma((count,)),
        dma((count,)),
        dma((count,)),
        dma((2, count)),
        dma((2, count)),
        dma,
    ]


def advance(steps, times):
    for _ in range(times):
        next(steps, None)


def group_of(event):
    seq = lax.axis_index("seq")
    return {"line": seq, "side": seq ^ 2, "near": seq ^ 1, "corner": seq ^ 3}.get(event)


def scatter_steps(
    count,
    partial,
    deliver,
    core_slot,
    side_slot,
    line_slot,
    side_out,
    line_out,
    core_sent,
    core_got,
    side_sent,
    side_got,
    line_sent,
    line_got,
    compute=None,
):
    seq, b = lax.axis_index("seq"), lax.axis_index("blk")
    core, side = {"seq": seq ^ 1}, {"seq": seq ^ 2}
    away = tuple(range(count // 2, 0, -1)) + tuple(range(count // 2 + 1, count)) + (0,)
    place = [lax.rem(b + k, count) for k in away]

    def to_core(half, k):
        source = partial.at[(seq ^ (1 if half else 3)) * count + place[k]]
        return remote(
            source, core_slot.at[half, k], core_sent.at[half, k], core_got.at[half, k], core
        )

    def to_side(k):
        return remote(side_out.at[k], side_slot.at[k], side_sent.at[k], side_got.at[k], side)

    def along_line(k):
        slot = away[k] - 1
        return remote(
            line_out.at[k],
            line_slot.at[slot],
            line_sent.at[k],
            line_got.at[slot],
            {"blk": place[k]},
        )

    for half in range(2):
        if compute:
            compute(seq ^ (1 if half else 3))
        for k in range(count):
            to_core(half, k).start()
    if compute:
        compute(seq ^ 2)
    for k in range(count):
        to_core(0, k).wait_recv()
        total = partial[(seq ^ 2) * count + place[k]].astype(jnp.float32)
        total += core_slot[0, k].astype(jnp.float32)
        side_out[k] = total.astype(jnp.bfloat16)
        to_side(k).start()
    if compute:
        compute(seq)
    yield
    for k in range(count):
        to_core(1, k).wait_recv()
        to_side(k).wait_recv()
        total = partial[seq * count + place[k]].astype(jnp.float32)
        total += core_slot[1, k].astype(jnp.float32)
        total += side_slot[k].astype(jnp.float32)
        if k < count - 1:
            line_out[k] = total.astype(jnp.bfloat16)
            along_line(k).start()
            yield
    yield
    for k in range(count - 1):
        along_line(k).wait_recv()
        total += line_slot[away[k] - 1].astype(jnp.float32)
    deliver(total)
    for k in range(count):
        to_core(0, k).wait_send()
        to_core(1, k).wait_send()
        to_side(k).wait_send()
        if k < count - 1:
            along_line(k).wait_send()


def scatter_scratch(count, rows, width):
    dma = pltpu.SemaphoreType.DMA

    def slots(*places):
        return pltpu.VMEM(places + (rows, width), jnp.bfloat16)

    return [
        slots(2, count),
        slots(count),
        slots(count - 1),
        slots(count),
        slots(count - 1),
        dma((2, count)),
        dma((2, count)),
        dma((count,)),
        dma((count,)),
        dma((count - 1,)),
        dma((count - 1,)),
    ]


def run_with(steps, fillers):
    fillers = list(fillers)
    for _ in steps:
        if fillers:
            fillers.pop(0)()
    for filler in fillers:
        filler()


def greet_group(count, more=()):
    seq, b = lax.axis_index("seq"), lax.axis_index("blk")
    greet(
        tuple(more)
        + ({"seq": seq ^ 1}, {"seq": seq ^ 2})
        + tuple({"blk": lax.rem(b + k, count)} for k in range(1, count))
    )


def group_rows(ref, group, count):
    value = ref[pl.ds(group * count, count)]
    return value.reshape(value.shape[0] * value.shape[1], value.shape[2])


def group_span(group, count, block):
    size = count * block
    return pl.ds(pl.multiple_of(group * size, size), size)


def lane_turn(field_in, cosine, sine):
    half_dim, lanes = HEAD_DIM // 2, field_in.shape[-1]
    lane = lax.broadcasted_iota(jnp.int32, field_in.shape, 1)
    partner = jnp.where(
        lane < half_dim,
        pltpu.roll(field_in, lanes - half_dim, 1),
        pltpu.roll(field_in, half_dim, 1),
    )
    return field_in * cosine + partner * sine


def masked_scores(query, key, first_row, start):
    scores = back_product(query, key) * HEAD_DIM ** (-0.5)
    key_index = lax.broadcasted_iota(jnp.int32, scores.shape, 1)
    query_index = first_row + lax.broadcasted_iota(jnp.int32, scores.shape, 0)
    return jnp.where((key_index >= start) & (key_index <= query_index), scores, MASKED)


def normalise(field_in, gain_row):
    inv_root = lax.rsqrt(jnp.mean(field_in * field_in, axis=-1, keepdims=True) + EPS)
    return field_in * inv_root * gain_row


PAD = 128


def load_weights(attn, out, attn_vm, out_vm, sems):
    copies = []
    for part in range(3):
        copies.append(
            pltpu.make_async_copy(
                attn.at[pl.ds(part * HEAD_DIM, HEAD_DIM)],
                attn_vm.at[pl.ds(part * PAD, HEAD_DIM)],
                sems.at[part],
            )
        )
    copies.append(
        pltpu.make_async_copy(
            attn.at[pl.ds(3 * HEAD_DIM, 16)], attn_vm.at[pl.ds(3 * PAD, 16)], sems.at[3]
        )
    )
    copies.append(pltpu.make_async_copy(out, out_vm.at[pl.ds(0, HEAD_DIM)], sems.at[4]))
    return copies


def clear_pads(attn_vm, out_vm):
    empty = jnp.zeros((PAD - HEAD_DIM, attn_vm.shape[1]), jnp.bfloat16)
    for part in range(3):
        attn_vm[part * PAD + HEAD_DIM : (part + 1) * PAD] = empty
    out_vm[HEAD_DIM:PAD] = empty


def attn_kernel(count, spreading, *refs):
    refs = iter(refs)

    def take(n):
        return [next(refs) for _ in range(n)]

    if spreading:
        pieces, w_gate, w_up, w_output, rows_in, grads_in, cosine, sine, start = take(9)
        attn, gate_up, out, grads_all = take(4)
    else:
        rows_in, x_own, attn, out, cosine, sine, start = take(7)
    hidden_out, normed_out, all_rows, heads, log_total = take(5)
    rows_vm, attn_vm, out_vm, partial, load_done, save_done = take(6)
    if spreading:
        normed_vm, grads_vm = take(2)
        spread_sems = take(5)
        grads_sems = take(7)
    else:
        normed_vm = rows_vm
    gather_sems = take(7)
    scatter_refs = list(refs)
    seq, section = lax.axis_index("seq"), lax.axis_index("section")
    block = rows_vm.shape[1]
    tokens = block * rows_vm.shape[0]
    size = count * block
    if spreading:
        greet_group(count, ({"section": 1 - section},))
        spread = spread_steps(
            count, pieces, w_gate, w_up, w_output, attn, gate_up, out, *spread_sems
        )
        next(spread)
    else:
        greet_group(count)
    steps = gather_steps(count, rows_in, rows_vm, *gather_sems)
    next(steps)
    clear_pads(attn_vm, out_vm)
    if spreading:
        loads = load_weights(attn.at[0], out.at[0], attn_vm, out_vm, load_done)
    else:
        loads = load_weights(attn.at[1], out.at[1], attn_vm, out_vm, load_done)
        for copy in loads:
            copy.start()

    def project(group):
        if spreading:
            gain = attn_vm[3 * PAD : 3 * PAD + 16][0:1].astype(jnp.float32)
            raw = rows_vm[pl.ds(group * count, count)].astype(jnp.float32)
            normed = normalise(raw, gain[None]).astype(jnp.bfloat16)
            normed_vm[pl.ds(group * count, count)] = normed
            normed = normed.reshape(size, normed.shape[2])
        else:
            normed = group_rows(rows_vm, group, count)
        mixed = back_product(normed, attn_vm[0 : 3 * PAD])
        span = group_span(group, count, block)
        cos_rows, sin_rows = cosine[span], sine[span]
        heads[0, span] = lane_turn(mixed[:, :PAD], cos_rows, sin_rows).astype(jnp.bfloat16)
        heads[1, span] = lane_turn(mixed[:, PAD : 2 * PAD], cos_rows, sin_rows).astype(
            jnp.bfloat16
        )
        heads[2, span] = mixed[:, 2 * PAD :].astype(jnp.bfloat16)

    for number, event in enumerate(steps):
        group = group_of(event)
        if spreading:
            if number == 1:
                next(spread)
            continue
        if event == "line":
            for copy in loads:
                copy.wait()
        if group is not None:
            project(group)
    if spreading:
        next(spread)
        for copy in loads:
            copy.start()
        grad_steps = gather_steps(count, grads_in, grads_vm, *grads_sems)
        next(grad_steps)
        for copy in loads:
            copy.wait()
        for group in range(tokens // size):
            project(group)
    save = pltpu.make_async_copy(normed_vm, all_rows, save_done.at[0])
    save.start()
    for i in range(tokens // size):
        here, seen = slice(i * size, (i + 1) * size), slice(0, (i + 1) * size)
        scores = masked_scores(heads[0, here], heads[1, seen], i * size, start[here])
        row_top = jnp.max(scores, axis=-1, keepdims=True)
        weights = jnp.exp(scores - row_top)
        total = jnp.sum(weights, axis=-1, keepdims=True)
        log_total[here] = row_top + jnp.log(total)
        weights = (weights * (1.0 / total)).astype(jnp.bfloat16)
        heads[3, here] = product(weights, heads[2, seen]).astype(jnp.bfloat16)

    def project_out(group):
        mixed = heads[3, group_span(group, count, block)]
        value = product(mixed, out_vm[...]).astype(jnp.bfloat16)
        partial[pl.ds(group * count, count)] = value.reshape(count, block, -1)

    def deliver(total):
        own = rows_in[...].astype(jnp.float32) if spreading else x_own[...]
        hidden = own + total
        gain = attn_vm[3 * PAD : 3 * PAD + 16][1:2].astype(jnp.float32)
        hidden_out[...] = hidden
        normed_out[...] = normalise(hidden, gain).astype(jnp.bfloat16)

    between = []
    if spreading:
        between = [functools.partial(advance, grad_steps, n) for n in (2, 1, 1, 2)]
    run_with(scatter_steps(count, partial, deliver, *scatter_refs, compute=project_out), between)
    if spreading:
        for _ in spread:
            pass
        for _ in grad_steps:
            pass
        keep = pltpu.make_async_copy(grads_vm, grads_all, save_done.at[1])
        keep.start()
        keep.wait()
    save.wait()


def spread_steps(
    count,
    pieces,
    w_gate,
    w_up,
    w_output,
    attn,
    gate_up,
    out,
    line_sent,
    line_got,
    cross_sent,
    cross_got,
    local_done,
):
    seq, b, section = lax.axis_index("seq"), lax.axis_index("blk"), lax.axis_index("section")
    seq_count = lax.axis_size("seq")
    other = {"section": 1 - section}
    rows, lanes = w_gate.shape[0], gate_up.shape[2] // 2
    out_rows = out.shape[1]
    far_first = tuple(range(count // 2, 0, -1)) + tuple(range(count // 2 + 1, count))

    def source(kind, j):
        if kind == 0:
            return pieces.at[j]
        weight = w_gate if kind == 1 else w_up
        return weight.at[:, pl.ds(pl.multiple_of((j * seq_count + seq) * lanes, lanes), lanes)]

    def target(kind, j):
        if kind == 0:
            return attn.at[section, :, pl.ds(pl.multiple_of(j * rows, rows), rows)]
        return gate_up.at[
            section, pl.ds(pl.multiple_of(j * rows, rows), rows), pl.ds((kind - 1) * lanes, lanes)
        ]

    def along_line(kind, k):
        j = lax.rem(b + k, count)
        return remote(
            source(kind, j),
            target(kind, b),
            line_sent.at[kind, k],
            line_got.at[kind, k],
            {"blk": j},
        )

    def across(kind, j, slot, begin=None):
        spot = target(kind, j)
        return remote(
            spot if begin is None else begin,
            spot,
            cross_sent.at[kind, slot],
            cross_got.at[kind, slot],
            other,
        )

    def own_rows():
        begin = w_output.at[pl.ds(pl.multiple_of(seq * out_rows, out_rows), out_rows)]
        spot = out.at[section]
        return (
            remote(begin, spot, cross_sent.at[3, 0], cross_got.at[3, 0], other),
            pltpu.make_async_copy(begin, spot, local_done.at[3]),
        )

    def own_piece(kind):
        return (
            across(kind, b, 0, source(kind, b)),
            pltpu.make_async_copy(source(kind, b), target(kind, b), local_done.at[kind]),
        )

    def begin(copies):
        for copy in copies:
            copy.start()

    def forward(kind):
        for k in far_first:
            j = lax.rem(b + count - k, count)
            settled(target(kind, j), line_got.at[kind, k], True)
            across(kind, j, k).start()

    def arrived(kind):
        for k in range(count):
            settled(target(kind, 0), cross_got.at[kind, k], True)
            settled(target(kind, 0), cross_sent.at[kind, k], False)
            if k:
                settled(target(kind, 0), line_sent.at[kind, k], False)
        own_piece(kind)[1].wait()

    for k in far_first:
        along_line(0, k).start()
    begin(own_piece(0) + own_rows())
    yield
    forward(0)
    for kind in (1, 2):
        for k in far_first:
            along_line(kind, k).start()
    yield
    arrived(0)
    passed, local = own_rows()
    passed.wait()
    local.wait()
    for kind in (1, 2):
        begin(own_piece(kind))
        forward(kind)
    yield
    for kind in (1, 2):
        arrived(kind)


def start_all(copies):
    for copy in copies:
        copy.start()


def wait_all(copies):
    for copy in copies:
        copy.wait()


def gated(pre):
    half = pre.shape[1] // 2
    gate, up = pre[:, :half], pre[:, half:]
    sigma = jax.nn.sigmoid(gate)
    return gate, up, sigma


def hidden_units(pre):
    gate, up, sigma = gated(pre)
    return (gate * sigma * up).astype(jnp.bfloat16)


def store_gate_grads(place, span, grad_act, pre):
    gate, up, sigma = gated(pre)
    half = gate.shape[1]
    place[span, 0:half] = (grad_act * up * sigma * (1.0 + gate * (1.0 - sigma))).astype(
        jnp.bfloat16
    )
    place[span, half : 2 * half] = (grad_act * (gate * sigma)).astype(jnp.bfloat16)


def mlp_kernel(count, *refs):
    refs = iter(refs)

    def take(n):
        return [next(refs) for _ in range(n)]

    rows_in, hidden, gate_up, w_down, gain_next = take(5)
    down, result_out, normed_out, all_rows = take(4)
    rows_vm, wide_vm, down_vm, units, partial, load_done, cross_sent, cross_got = take(8)
    gather_sems = take(7)
    scatter_refs = list(refs)
    seq, section = lax.axis_index("seq"), lax.axis_index("section")
    block = rows_vm.shape[1]
    other = {"section": 1 - section}
    greet_group(count, (other,))
    load = pltpu.make_async_copy(gate_up.at[0], wide_vm, load_done.at[0])
    load.start()
    steps = gather_steps(count, rows_in, rows_vm, *gather_sems)
    next(steps)
    size = down.shape[1]
    begin = w_down.at[pl.ds(pl.multiple_of(seq * size, size), size)]
    across = remote(begin, down.at[section], cross_sent, cross_got, other)
    local = pltpu.make_async_copy(begin, down.at[section], load_done.at[1])
    across.start()
    local.start()

    def units_of(group):
        pre = product(group_rows(rows_vm, group, count), wide_vm[...])
        units[group_span(group, count, block)] = hidden_units(pre)

    for event in steps:
        if event == "line":
            load.wait()
        group = group_of(event)
        if group is not None:
            units_of(group)
    save = pltpu.make_async_copy(rows_vm, all_rows, load_done.at[2])
    save.start()
    across.wait()
    local.wait()
    load = pltpu.make_async_copy(down.at[0], down_vm, load_done.at[3])
    load.start()
    load.wait()

    def project_down(group):
        value = product(units[group_span(group, count, block)], down_vm[...])
        partial[pl.ds(group * count, count)] = value.astype(jnp.bfloat16).reshape(count, block, -1)

    def deliver(total):
        low = (hidden[...] + total).astype(jnp.bfloat16)
        result_out[...] = low
        normed_out[...] = normalise(low.astype(jnp.float32), gain_next[...]).astype(jnp.bfloat16)

    run_with(scatter_steps(count, partial, deliver, *scatter_refs, compute=project_down), [])
    save.wait()


def wide_grads(rows_vm, pre_grads, units, grads_vm, wide_grad, down_grad):
    tokens = pre_grads.shape[0]
    width = rows_vm.shape[2]
    step = width // 4

    def wide_part(n):
        cut = slice(n * step, (n + 1) * step)
        rows = rows_vm[:, :, cut].reshape(tokens, step)
        wide_grad[cut] = weight_term(rows, pre_grads[...]).astype(jnp.bfloat16)

    def down_part(n):
        cut = slice(n * 2 * step, (n + 1) * 2 * step)
        rows = grads_vm[:, :, cut].reshape(tokens, 2 * step)
        down_grad[:, cut] = weight_term(units[...], rows).astype(jnp.bfloat16)

    return [functools.partial(wide_part, n) for n in range(4)] + [
        functools.partial(down_part, n) for n in range(2)
    ]


def mlp_grad_sent(total, hidden, grads_own, gain, branch_out, grad_hidden_out, gain_out):
    field_in = hidden[...]
    inv_root = lax.rsqrt(jnp.mean(field_in * field_in, axis=-1, keepdims=True) + EPS)
    part, terms = rms_backward(field_in, gain[...], inv_root, total)
    grad_hidden = grads_own[...].astype(jnp.float32) + part
    grad_hidden_out[...] = grad_hidden
    branch_out[...] = grad_hidden.astype(jnp.bfloat16)
    gain_out[...] = jnp.broadcast_to(jnp.sum(terms, axis=0, keepdims=True), gain_out.shape)


def mlp_both_kernel(count, *refs):
    refs = iter(refs)

    def take(n):
        return [next(refs) for _ in range(n)]

    rows_in, hidden, gate_up, down, grads_all, grads_own, gain = take(7)
    result_out, branch_out, grad_hidden_out, gain_out, wide_grad, down_grad = take(6)
    rows_vm, grads_vm, wide_vm, down_vm, units, pre_grads, partial, partial_back = take(8)
    (load_done,) = take(1)
    gather_sems = take(7)
    scatter_refs, scatter_back = take(11), take(11)
    block = rows_vm.shape[1]
    greet_group(count)
    steps = gather_steps(count, rows_in, rows_vm, *gather_sems)
    next(steps)
    loads = [
        pltpu.make_async_copy(gate_up.at[1], wide_vm, load_done.at[0]),
        pltpu.make_async_copy(down.at[1], down_vm, load_done.at[1]),
        pltpu.make_async_copy(grads_all, grads_vm, load_done.at[2]),
    ]
    start_all(loads)

    def through(group):
        span = group_span(group, count, block)
        pre = product(group_rows(rows_vm, group, count), wide_vm[...])
        units[span] = hidden_units(pre)
        grad_act = back_product(group_rows(grads_vm, group, count), down_vm[...])
        store_gate_grads(pre_grads, span, grad_act, pre)
        value = back_product(pre_grads[span], wide_vm[...])
        partial_back[pl.ds(group * count, count)] = value.astype(jnp.bfloat16).reshape(
            count, block, -1
        )

    for event in steps:
        if event == "line":
            wait_all(loads)
        group = group_of(event)
        if group is not None:
            through(group)

    def project_down(group):
        value = product(units[group_span(group, count, block)], down_vm[...])
        partial[pl.ds(group * count, count)] = value.astype(jnp.bfloat16).reshape(count, block, -1)

    def deliver(total):
        result_out[...] = (hidden[...] + total).astype(jnp.bfloat16)

    def deliver_back(total):
        mlp_grad_sent(
            total, hidden, grads_own, gain, branch_out, grad_hidden_out, gain_out
        )

    back = scatter_steps(count, partial_back, deliver_back, *scatter_back)
    ahead = scatter_steps(count, partial, deliver, *scatter_refs, compute=project_down)
    next(back)
    next(ahead)
    run_with(back, wide_grads(rows_vm, pre_grads, units, grads_vm, wide_grad, down_grad))
    run_with(ahead, [])


def mlp_back_kernel(count, *refs):
    refs = iter(refs)

    def take(n):
        return [next(refs) for _ in range(n)]

    grads_own, hidden, all_rows, gate_up, down, gain = take(6)
    branch_out, grad_hidden_out, gain_out, wide_grad, down_grad = take(5)
    rows_vm, grads_vm, wide_vm, down_vm, units, pre_vm, pre_grads, partial, load_done = take(9)
    gather_sems = take(7)
    scatter_refs = list(refs)
    block = rows_vm.shape[1]
    greet_group(count)
    steps = gather_steps(count, grads_own, grads_vm, *gather_sems)
    next(steps)
    loads = [
        pltpu.make_async_copy(gate_up.at[0], wide_vm, load_done.at[0]),
        pltpu.make_async_copy(all_rows, rows_vm, load_done.at[1]),
        pltpu.make_async_copy(down.at[0], down_vm, load_done.at[2]),
    ]
    start_all(loads)

    def again(group):
        span = group_span(group, count, block)
        pre = product(group_rows(rows_vm, group, count), wide_vm[...])
        pre_vm[span] = pre
        units[span] = hidden_units(pre)

    def through(group):
        span = group_span(group, count, block)
        grad_act = back_product(group_rows(grads_vm, group, count), down_vm[...])
        store_gate_grads(pre_grads, span, grad_act, pre_vm[span])
        value = back_product(pre_grads[span], wide_vm[...])
        partial[pl.ds(group * count, count)] = value.astype(jnp.bfloat16).reshape(count, block, -1)

    wait_all(loads)
    for number, event in enumerate(steps):
        if number < 2:
            again(2 * number)
            again(2 * number + 1)
        group = group_of(event)
        if group is not None:
            through(group)

    def deliver(total):
        mlp_grad_sent(total, hidden, grads_own, gain, branch_out, grad_hidden_out, gain_out)

    run_with(
        scatter_steps(count, partial, deliver, *scatter_refs),
        wide_grads(rows_vm, pre_grads, units, grads_vm, wide_grad, down_grad),
    )


def attn_back_kernel(count, layer, *refs):
    refs = iter(refs)

    def take(n):
        return [next(refs) for _ in range(n)]

    branch_in, grad_hidden, x_own, all_rows, heads_kept, log_total, attn, out = take(8)
    cosine, sine, start, gain = take(4)
    grad_out, gain_out, attn_grad, out_grad = take(4)
    branch_vm, rows_vm, heads, attn_vm, out_vm, mixed_grads, probs = take(7)
    key_grads, value_grads, joint, partial, load_done = take(5)
    gather_sems = take(7)
    scatter_refs = list(refs)
    block = rows_vm.shape[1]
    size = count * block
    tokens = block * rows_vm.shape[0]
    low, f32 = jnp.bfloat16, jnp.float32
    scale = HEAD_DIM ** (-0.5)
    greet_group(count)
    steps = gather_steps(count, branch_in, branch_vm, *gather_sems)
    next(steps)
    clear_pads(attn_vm, out_vm)
    loads = load_weights(attn.at[layer], out.at[layer], attn_vm, out_vm, load_done)
    loads.append(pltpu.make_async_copy(heads_kept, heads, load_done.at[5]))
    loads.append(pltpu.make_async_copy(all_rows, rows_vm, load_done.at[6]))
    start_all(loads)
    key_grads[...] = jnp.zeros_like(key_grads)
    value_grads[...] = jnp.zeros_like(value_grads)
    wait_all(loads)

    def spans(i):
        return slice(i * size, (i + 1) * size), slice(0, (i + 1) * size)

    def weigh(i):
        here, seen = spans(i)
        scores = masked_scores(heads[0, here], heads[1, seen], i * size, start[here])
        probs[here, seen] = jnp.exp(scores - log_total[here])

    def project(group):
        value = back_product(group_rows(branch_vm, group, count), out_vm[...])
        mixed_grads[group_span(group, count, block)] = value.astype(low)

    for number, event in enumerate(steps):
        if number < 2:
            weigh(2 * number)
            weigh(2 * number + 1)
        group = group_of(event)
        if group is not None:
            project(group)
    for i in reversed(range(tokens // size)):
        here, seen = spans(i)
        weights = probs[here, seen]
        grads = mixed_grads[here]
        grad_weights = back_product(grads, heads[2, seen])
        centre = jnp.sum(weights * grad_weights, axis=-1, keepdims=True)
        grad_scores = (weights * (grad_weights - centre)).astype(low)
        query_grad = (product(grad_scores, heads[1, seen]) * scale).astype(low).astype(f32)
        joint[here, 0:PAD] = lane_turn(query_grad, cosine[here], -sine[here]).astype(low)
        key_grads[seen] += weight_term(grad_scores, heads[0, here])
        value_grads[seen] += weight_term(weights.astype(low), grads)
        key_grad = (key_grads[here] * scale).astype(low).astype(f32)
        joint[here, PAD : 2 * PAD] = lane_turn(key_grad, cosine[here], -sine[here]).astype(low)
        joint[here, 2 * PAD : 3 * PAD] = value_grads[here].astype(low)

    def project_back(group):
        value = product(joint[group_span(group, count, block)], attn_vm[0 : 3 * PAD])
        partial[pl.ds(group * count, count)] = value.astype(low).reshape(count, block, -1)

    def attn_part(part):
        rows = rows_vm[...].reshape(tokens, rows_vm.shape[2])
        value = weight_term(joint[:, part * PAD : (part + 1) * PAD], rows)
        attn_grad[part * HEAD_DIM : (part + 1) * HEAD_DIM] = value[0:HEAD_DIM].astype(low)

    def out_part():
        rows = branch_vm[...].reshape(tokens, branch_vm.shape[2])
        out_grad[...] = weight_term(heads[3], rows)[0:HEAD_DIM].astype(low)

    def deliver(total):
        field_in = x_own[...].astype(f32)
        inv_root = lax.rsqrt(jnp.mean(field_in * field_in, axis=-1, keepdims=True) + EPS)
        part, terms = rms_backward(field_in, gain[...], inv_root, total)
        grad_out[...] = (grad_hidden[...] + part).astype(low)
        gain_out[...] = jnp.broadcast_to(jnp.sum(terms, axis=0, keepdims=True), gain_out.shape)

    run_with(
        scatter_steps(count, partial, deliver, *scatter_refs, compute=project_back),
        [functools.partial(attn_part, part) for part in range(3)] + [out_part],
    )


def finish_kernel(
    count,
    attn_one,
    attn_two,
    out_one,
    out_two,
    wide_one,
    wide_two,
    down_one,
    down_two,
    gains,
    swap_rows,
    attn,
    out,
    gate,
    up,
    down,
    gains_out,
    swapped_rows,
    attn_in,
    out_in,
    wide_in,
    down_in,
    attn_slot,
    wide_slot,
    gain_in,
    gain_sum,
    gain_line,
    gain_part,
    gain_side,
    gain_core,
    cross_sent,
    cross_got,
    line_sent,
    line_got,
    side_sent,
    side_got,
    core_sent,
    core_got,
    local_done,
    small_sent,
    small_got,
):
    seq, b, section = lax.axis_index("seq"), lax.axis_index("blk"), lax.axis_index("section")
    at_first = section == 0
    core, side, other = {"seq": seq ^ 1}, {"seq": seq ^ 2}, {"section": 1 - section}
    greet((other, core, side) + tuple({"blk": lax.rem(b + k, count)} for k in range(1, count)))
    rows, lanes = attn.shape[2], gate.shape[1] // (4 * count)
    far_first = tuple(range(count // 2, 0, -1)) + tuple(range(count // 2 + 1, count)) + (0,)
    f32, low = jnp.float32, jnp.bfloat16

    def piece_rows(kind, j):
        if kind == 0:
            return (slice(None), pl.ds(pl.multiple_of(j * rows, rows), rows))
        return (pl.ds(pl.multiple_of(j * rows, rows), rows),)

    pairs = {
        0: (attn_one, attn_two, attn_in),
        1: (wide_one, wide_two, wide_in),
        2: (out_one, out_two, out_in),
        3: (down_one, down_two, down_in),
    }

    def cross(kind, k, begin):
        one, two, held = pairs[kind]
        index = piece_rows(kind, lax.rem(b + k, count)) if kind < 2 else (slice(None),)
        spots = [ref.at[index] for ref in (one, two, held)]
        sems = (cross_sent.at[kind, k], cross_got.at[kind, k])
        if not begin:
            return remote(spots[0], spots[2], *sems, other)

        @pl.when(at_first)
        def _():
            remote(spots[1], spots[2], *sems, other).start()

        @pl.when(jnp.logical_not(at_first))
        def _():
            remote(spots[0], spots[2], *sems, other).start()

    def add_up(kind, k):
        one, two, held = pairs[kind]
        index = piece_rows(kind, lax.rem(b + k, count)) if kind < 2 else (slice(None),)
        cross(kind, k, False).wait_recv()
        own = jnp.where(at_first, one[index], two[index]).astype(f32)
        held[index] = (own + held[index].astype(f32)).astype(low)

    def along_line(kind, k):
        j = lax.rem(b + k, count)
        slot = (attn_slot if kind == 0 else wide_slot).at[k]
        source = pairs[kind][2].at[piece_rows(kind, j)]
        return remote(source, slot, line_sent.at[kind, k], line_got.at[kind, k], {"blk": j})

    def places(kind, k, of_seq):
        if kind == 2:
            size = out_in.shape[0]
            return [out.at[pl.ds(pl.multiple_of(of_seq * size, size), size)]]
        if kind == 3:
            size = down_in.shape[0]
            return [down.at[pl.ds(pl.multiple_of(of_seq * size, size), size)]]
        head = lax.rem(b + count - k, count) * 4 + of_seq
        if kind == 0:
            return [attn.at[head]]
        column = pl.ds(pl.multiple_of(head * lanes, lanes), lanes)
        return [gate.at[:, column], up.at[:, column]]

    def numbered(kind, k, of_seq):
        base = {0: k, 1: count + 2 * k, 2: 3 * count, 3: 3 * count + 1}[kind]
        return [(base + n, spot) for n, spot in enumerate(places(kind, k, of_seq))]

    def made(kind, k):
        if kind > 1:
            return [pairs[kind][2].at[:]]
        if kind == 0:
            return [attn_in.at[piece_rows(0, b)] if k == 0 else attn_slot.at[k]]
        whole = (lambda cut: wide_in.at[piece_rows(1, b) + (cut,)]) if k == 0 else (
            lambda cut: wide_slot.at[k, :, cut]
        )
        return [whole(pl.ds(0, lanes)), whole(pl.ds(lanes, lanes))]

    def sends(kind, k):
        found = []
        for (n, spot), begin in zip(numbered(kind, k, seq), made(kind, k)):
            found.append(
                (
                    remote(begin, spot, side_sent.at[n], side_got.at[n], side),
                    remote(begin, spot, core_sent.at[0, n], core_got.at[0, n], core),
                    pltpu.make_async_copy(begin, spot, local_done.at[n]),
                )
            )
        return found

    def publish(kind, k):
        for copies in sends(kind, k):
            for copy in copies:
                copy.start()

    def passes(kind, k):
        return [
            remote(spot, spot, core_sent.at[1, n], core_got.at[1, n], core)
            for n, spot in numbered(kind, k, seq ^ 2)
        ]

    def from_line(kind, k):
        along_line(kind, k).wait_recv()
        publish(kind, k)

    def from_side(kind, k):
        for n, spot in numbered(kind, k, seq ^ 2):
            settled(spot, side_got.at[n], True)
        for copy in passes(kind, k):
            copy.start()

    def small(n, source, slot, device):
        return remote(source, slot, small_sent.at[n], small_got.at[n], device)

    swap = small(0, swap_rows.at[:], swapped_rows.at[:], other)
    swap.start()
    gain_cross = small(1, gains.at[1 - section], gain_in.at[:], other)
    gain_cross.start()
    cross(2, 0, True)
    for kind, k in ((1, far_first[0]), (1, 0)):
        cross(kind, k, True)
    cross(3, 0, True)
    for kind in (1, 0):
        for k in far_first:
            if (kind, k) not in ((1, far_first[0]), (1, 0)):
                cross(kind, k, True)

    def gain_piece(j):
        return gain_sum.at[:, pl.ds(pl.multiple_of(j * rows, rows), rows)]

    def gain_send(k):
        j = lax.rem(b + k, count)
        return small(3 + k, gain_piece(j), gain_line.at[k], {"blk": j})

    gain_cross.wait_recv()
    gain_sum[...] = gains[section] + gain_in[...]
    for k in range(1, count):
        gain_send(k).start()

    add_up(2, 0)
    publish(2, 0)
    add_up(1, far_first[0])
    along_line(1, far_first[0]).start()
    add_up(1, 0)
    publish(1, 0)
    from_side(2, 0)
    for k in range(1, count):
        gain_send(k).wait_recv()
    gain_part[...] = gain_sum[:, pl.ds(pl.multiple_of(b * rows, rows), rows)]
    for k in range(1, count):
        gain_part[...] += gain_line[k]
    gain_to_side = small(2, gain_part.at[:], gain_side.at[:], side)
    gain_to_side.start()
    add_up(3, 0)
    publish(3, 0)
    for k in far_first[1:-1]:
        add_up(1, k)
        along_line(1, k).start()
    from_side(1, 0)
    gain_to_side.wait_recv()
    gain_side[...] += gain_part[...]
    gain_to_core = small(3, gain_side.at[:], gain_core.at[:], core)
    gain_to_core.start()
    from_line(1, far_first[0])
    from_side(3, 0)
    add_up(0, far_first[0])
    along_line(0, far_first[0]).start()
    from_line(1, far_first[1])
    add_up(0, far_first[1])
    along_line(0, far_first[1]).start()
    from_side(1, far_first[0])
    from_line(1, far_first[2])
    add_up(0, far_first[2])
    along_line(0, far_first[2]).start()
    add_up(0, 0)
    publish(0, 0)
    from_side(1, far_first[1])
    gain_to_core.wait_recv()
    gains_out[...] = gain_side[...] + gain_core[...]
    from_line(0, far_first[0])
    from_side(1, far_first[2])
    from_line(0, far_first[1])
    from_line(0, far_first[2])
    from_side(0, 0)
    for k in far_first[:-1]:
        from_side(0, k)
    every = [(0, k) for k in range(count)] + [(1, k) for k in range(count)] + [(2, 0), (3, 0)]
    for kind, k in every:
        cross(kind, k, False).wait_send()
        if kind < 2 and k:
            along_line(kind, k).wait_send()
        for to_side, to_core, local in sends(kind, k):
            to_side.wait_send()
            to_core.wait_send()
            local.wait()
        for copy in passes(kind, k):
            copy.wait_send()
        for half, of_seq in ((0, seq ^ 1), (1, seq ^ 3)):
            for n, spot in numbered(kind, k, of_seq):
                settled(spot, core_got.at[half, n], True)
    swap.wait()
    gain_cross.wait_send()
    for k in range(1, count):
        gain_send(k).wait_send()
    gain_to_side.wait_send()
    gain_to_core.wait_send()


def finish_grads(first, second, gains, swap_rows):
    seq_count, count = lax.axis_size("seq"), lax.axis_size("blk")
    low, f32 = jnp.bfloat16, jnp.float32
    attn, out, wide, down = first
    rows = wide.shape[0] // count
    lanes = wide.shape[1] // 2
    parts = seq_count * count
    dma = pltpu.SemaphoreType.DMA
    vmem = pltpu.VMEM
    sends = 3 * count + 2
    heads = attn.shape[0]
    operands = [array for pair in zip(first, second) for array in pair] + [gains, swap_rows]
    in_vmem = pl.BlockSpec(memory_space=vmem)
    anywhere = pl.BlockSpec(memory_space=pl.ANY)
    small = (gains.shape[1], rows)
    attn, out, gate, up, down, gains, swapped_rows = pl.pallas_call(
        functools.partial(finish_kernel, count),
        out_shape=[
            jax.ShapeDtypeStruct((parts, heads, rows), low),
            jax.ShapeDtypeStruct((out.shape[0] * seq_count, out.shape[1]), low),
            jax.ShapeDtypeStruct((rows, lanes * parts), low),
            jax.ShapeDtypeStruct((rows, lanes * parts), low),
            jax.ShapeDtypeStruct((down.shape[0] * seq_count, down.shape[1]), low),
            jax.ShapeDtypeStruct(small, f32),
            jax.ShapeDtypeStruct(swap_rows.shape, low),
        ],
        in_specs=[in_vmem] * len(operands),
        out_specs=[anywhere] * 5 + [in_vmem, in_vmem],
        scratch_shapes=[
            vmem(attn.shape, low),
            vmem(out.shape, low),
            vmem(wide.shape, low),
            vmem(down.shape, low),
            vmem((count, heads, rows), low),
            vmem((count, rows, 2 * lanes), low),
            vmem(gains.shape[1:], f32),
            vmem(gains.shape[1:], f32),
            vmem((count,) + small, f32),
            vmem(small, f32),
            vmem(small, f32),
            vmem(small, f32),
            dma((4, count)),
            dma((4, count)),
            dma((2, count)),
            dma((2, count)),
            dma((sends,)),
            dma((sends,)),
            dma((2, sends)),
            dma((2, sends)),
            dma((sends,)),
            dma((4 + count,)),
            dma((4 + count,)),
        ],
        compiler_params=pltpu.CompilerParams(
            collective_id=3, has_side_effects=True, vmem_limit_bytes=48 * 2**20
        ),
        name="finish_grads",
    )(*operands)
    attn = attn.astype(f32)

    def heads_back(start, copies):
        part = attn[:, start : start + HEAD_DIM].reshape(-1, copies, HEAD_DIM, rows).sum(1)
        return part.reshape(-1, rows).T

    copies = HEADS // KV_HEADS
    return (
        swapped_rows,
        gains,
        heads_back(0, 1),
        heads_back(HEAD_DIM, copies),
        heads_back(2 * HEAD_DIM, copies),
        out.astype(f32),
        gate.astype(f32),
        up.astype(f32),
        down.astype(f32),
    )


def call_kernel(kernel, name, number, operands, outputs, scratch):
    in_vmem = pl.BlockSpec(memory_space=pltpu.VMEM)
    anywhere = pl.BlockSpec(memory_space=pl.ANY)
    return pl.pallas_call(
        kernel,
        out_shape=[jax.ShapeDtypeStruct(shape, dtype) for shape, dtype, _ in outputs],
        in_specs=[in_vmem if near else anywhere for _, near in operands],
        out_specs=[in_vmem if near else anywhere for _, _, near in outputs],
        scratch_shapes=scratch,
        compiler_params=pltpu.CompilerParams(
            collective_id=number, has_side_effects=True, vmem_limit_bytes=56 * 2**20
        ),
        name=name,
    )(*[array for array, _ in operands])


def sliced_heads(local_shards):
    seq_index, seq_count = lax.axis_index("seq"), lax.axis_size("seq")
    count = lax.axis_size("blk")
    gain_attn, w_query, w_key, w_value, _, gain_mlp, _, _, _ = local_shards
    rows = w_query.shape[0]

    def heads_of(weight, per_blk, place):
        head = jnp.arange(count)[:, None] * per_blk + place
        column = (head * HEAD_DIM + jnp.arange(HEAD_DIM)).reshape(-1)
        chosen = jnp.arange(weight.shape[1])[:, None] == column[None, :]
        taken = lax.dot_general(
            chosen.astype(jnp.bfloat16),
            weight,
            (((0,), (1,)), ((), ())),
            preferred_element_type=jnp.float32,
        )
        return taken.astype(jnp.bfloat16).reshape(count, HEAD_DIM, rows)

    kv_per_blk = KV_HEADS // count
    kv_place = seq_index * kv_per_blk // seq_count
    gains = jnp.concatenate(
        [jnp.stack([gain_attn, gain_mlp]), jnp.zeros((14, rows), jnp.bfloat16)]
    )
    return jnp.concatenate(
        [
            heads_of(w_query, seq_count, seq_index),
            heads_of(w_key, kv_per_blk, kv_place),
            heads_of(w_value, kv_per_blk, kv_place),
            jnp.broadcast_to(gains[None], (count,) + gains.shape),
        ],
        axis=1,
    )


def head_shards(inputs, cotangent, doc_lengths, *params):
    section = lax.axis_index("section")
    at_first = section == 0
    seq_count, count = lax.axis_size("seq"), lax.axis_size("blk")
    low, f32 = jnp.bfloat16, jnp.float32
    vmem, dma = pltpu.VMEM, pltpu.SemaphoreType.DMA
    block, width = inputs.shape[2], inputs.shape[3]
    blocks = seq_count * count
    tokens = blocks * block
    rows_own = lax.dynamic_index_in_dim(inputs, section, 0, keepdims=False)[0]
    grads_own = lax.dynamic_index_in_dim(cotangent, section, 0, keepdims=False)[0]
    local = tuple(weight[0] for weight in params)
    pieces = sliced_heads(local)
    w_output, w_gate, w_up, w_down = local[4], local[6], local[7], local[8]
    rows = w_gate.shape[0]
    lanes = w_gate.shape[1] // blocks
    out_rows, down_rows = w_output.shape[0] // seq_count, w_down.shape[0] // seq_count
    lengths = lax.dynamic_index_in_dim(doc_lengths, section, 0, keepdims=False)[0]
    token_index = jnp.arange(tokens, dtype=jnp.int32)
    _, position = doc_info(lengths, token_index)
    start = (token_index - position)[:, None]
    half_dim = HEAD_DIM // 2
    frequency = THETA ** (-2.0 * jnp.arange(half_dim, dtype=f32) / HEAD_DIM)
    angles = position.astype(f32)[:, None] * frequency
    cosine, sine = jnp.cos(angles), jnp.sin(angles)
    empty = jnp.zeros((tokens, PAD - HEAD_DIM), f32)
    cosine = jnp.concatenate([cosine, cosine, empty], axis=1)
    sine = jnp.concatenate([-sine, sine, empty], axis=1)

    def all_blocks():
        return vmem((blocks, block, width), low)

    def scatter():
        return scatter_scratch(count, block, width)

    own_low, own_wide = ((block, width), low, True), ((block, width), f32, True)
    every = ((blocks, block, width), low, False)
    gain_rows = ((8, width), f32, True)
    attn_outputs = [
        own_wide,
        own_low,
        every,
        ((4, tokens, PAD), low, True),
        ((tokens, 1), f32, True),
    ]
    weights_vm = [vmem((3 * PAD + 16, width), low), vmem((PAD, width), low)]
    wide_vm, down_vm = vmem((width, 2 * lanes), low), vmem((down_rows, width), low)
    tables = [(cosine, True), (sine, True), (start, True)]
    attn, gate_up, out, grads_all, hidden_one, normed, rows_one, heads_one, total_one = call_kernel(
        functools.partial(attn_kernel, count, True),
        "first_attention",
        2,
        [(array, False) for array in (pieces, w_gate, w_up, w_output)]
        + [(rows_own, True), (grads_own, True)]
        + tables,
        [
            ((2, pieces.shape[1], width), low, False),
            ((2, width, 2 * lanes), low, False),
            ((2, out_rows, width), low, False),
            every,
        ]
        + attn_outputs,
        [all_blocks()]
        + weights_vm
        + [all_blocks(), dma((5,)), dma((2,)), all_blocks(), all_blocks()]
        + [dma((3, count)), dma((3, count)), dma((4, count)), dma((4, count)), dma((4,))]
        + gather_semaphores(count) * 2
        + scatter(),
    )
    gains = attn[:, 3 * HEAD_DIM : 3 * HEAD_DIM + 2].astype(f32)
    down, between, normed, wide_rows_one = call_kernel(
        functools.partial(mlp_kernel, count),
        "first_feed_forward",
        5,
        [
            (normed, True),
            (hidden_one, True),
            (gate_up, False),
            (w_down, False),
            (gains[1, 0:1], True),
        ],
        [((2, down_rows, width), low, False), own_low, own_low, every],
        [all_blocks(), wide_vm, down_vm, vmem((tokens, lanes), low), all_blocks(), dma((4,)), dma, dma]
        + gather_semaphores(count)
        + scatter(),
    )
    hidden_two, normed, rows_two, heads_two, total_two = call_kernel(
        functools.partial(attn_kernel, count, False),
        "second_attention",
        4,
        [(normed, True), (between.astype(f32), True), (attn, False), (out, False)] + tables,
        attn_outputs,
        [all_blocks()]
        + weights_vm
        + [all_blocks(), dma((5,)), dma((2,))]
        + gather_semaphores(count)
        + scatter(),
    )
    wide_outputs = [((width, 2 * lanes), low, True), ((down_rows, width), low, True)]
    final, branch, grad_hidden, gain_mlp_two, wide_two, down_two = call_kernel(
        functools.partial(mlp_both_kernel, count),
        "second_feed_forward",
        6,
        [
            (normed, True),
            (hidden_two, True),
            (gate_up, False),
            (down, False),
            (grads_all, False),
            (grads_own, True),
            (gains[1, 1:2], True),
        ],
        [own_low, own_low, own_wide, gain_rows] + wide_outputs,
        [all_blocks(), all_blocks(), wide_vm, down_vm]
        + [vmem((tokens, lanes), low), vmem((tokens, 2 * lanes), low)]
        + [all_blocks(), all_blocks(), dma((3,))]
        + gather_semaphores(count)
        + scatter()
        + scatter(),
    )

    def attention_back(layer, branch, grad_hidden, x_own, rows_all, heads, log_total):
        return call_kernel(
            functools.partial(attn_back_kernel, count, layer),
            ("first", "second")[layer] + "_attention_back",
            7 + layer,
            [(branch, True), (grad_hidden, True), (x_own, True)]
            + [(rows_all, False), (heads, False), (log_total, True), (attn, False), (out, False)]
            + tables
            + [(gains[layer, 0:1], True)],
            [
                own_low,
                gain_rows,
                ((3 * HEAD_DIM, width), low, True),
                ((HEAD_DIM, width), low, True),
            ],
            [all_blocks(), all_blocks(), vmem((4, tokens, PAD), low)]
            + weights_vm
            + [vmem((tokens, PAD), low), vmem((tokens, tokens), f32)]
            + [vmem((tokens, PAD), f32), vmem((tokens, PAD), f32), vmem((tokens, 3 * PAD), low)]
            + [all_blocks(), dma((7,))]
            + gather_semaphores(count)
            + scatter(),
        )

    grad_between, gain_attn_two, attn_two, out_two = attention_back(
        1, branch, grad_hidden, between, rows_two, heads_two, total_two
    )
    branch, grad_hidden, gain_mlp_one, wide_one, down_one = call_kernel(
        functools.partial(mlp_back_kernel, count),
        "first_feed_forward_back",
        9,
        [
            (grad_between, True),
            (hidden_one, True),
            (wide_rows_one, False),
            (gate_up, False),
            (down, False),
            (gains[0, 1:2], True),
        ],
        [own_low, own_wide, gain_rows] + wide_outputs,
        [all_blocks(), all_blocks(), wide_vm, down_vm]
        + [vmem((tokens, lanes), low), vmem((tokens, 2 * lanes), f32)]
        + [vmem((tokens, 2 * lanes), low), all_blocks(), dma((3,))]
        + gather_semaphores(count)
        + scatter(),
    )
    grad_start, gain_attn_one, attn_one, out_one = attention_back(
        0, branch, grad_hidden, rows_own, rows_one, heads_one, total_one
    )
    kept = jnp.where(
        at_first, jnp.stack([between, grad_start]), jnp.stack([final, grad_between])
    )
    sent = jnp.where(
        at_first, jnp.stack([final, grad_between]), jnp.stack([between, grad_start])
    )
    gain_sums = jnp.stack(
        [
            jnp.concatenate([gain_attn_one[0:4], gain_mlp_one[0:4]]),
            jnp.concatenate([gain_attn_two[0:4], gain_mlp_two[0:4]]),
        ]
    )
    swapped_rows, gain_sums, query, key, value, out, gate, up, down = finish_grads(
        (attn_one, out_one, wide_one, down_one),
        (attn_two, out_two, wide_two, down_two),
        gain_sums,
        sent,
    )
    pairs = jnp.where(
        at_first, jnp.stack([kept, swapped_rows], axis=1), jnp.stack([swapped_rows, kept], axis=1)
    )
    return (
        pairs[0][None, :, None],
        pairs[1][None, :, None],
        gain_sums[0][None],
        query[None],
        key[None],
        value[None],
        out[None],
        gain_sums[4][None],
        gate[None],
        up[None],
        down[None],
    )

def solution(mesh):
    placed = (
        P(None, None, ("seq", "blk"), None),
        P(None, None, ("seq", "blk"), None),
        P(),
        P("section", "blk"),
        P("section", "blk", None),
        P("section", "blk", None),
        P("section", "blk", None),
        P("section", "blk", None),
        P("section", "blk"),
        P("section", "blk", None),
        P("section", "blk", None),
        P("section", "blk", None),
    )
    one_head_each = mesh.shape["seq"] == 4 and mesh.shape["blk"] == HEADS // 4
    return jax.shard_map(
        head_shards if one_head_each else shards,
        mesh=mesh,
        in_specs=placed,
        out_specs=(
            P("section", None, None, ("seq", "blk"), None),
            P("section", None, None, ("seq", "blk"), None),
            P("section", "blk"),
            P("section", "blk", None),
            P("section", "blk", None),
            P("section", "blk", None),
            P("section", "blk", None),
            P("section", "blk"),
            P("section", "blk", None),
            P("section", "blk", None),
            P("section", "blk", None),
        ),
        check_vma=False,
    )
```

```python
import functools

import jax
import jax.numpy as jnp
from jax import lax
from jax.experimental import pallas as pl
from jax.experimental.pallas import tpu as pltpu
from jax.sharding import PartitionSpec as P

HEADS = 16
KV_HEADS = 8
HEAD_DIM = 96


EPS = 1e-05
THETA = 100000.0
MASKED = -1e30


def passed_along(value, axis, steps):
    count = lax.axis_size(axis)
    first, last = (max(0, -steps), min(count, count - steps))
    return lax.ppermute(value, axis, [(source, source + steps) for source in range(first, last)])


def shortened(value):
    return jax.tree.map(lambda a: a.astype(jnp.bfloat16) if a.dtype == jnp.float32 else a, value)


def product(left_side, right_side):
    return jnp.dot(left_side, right_side, preferred_element_type=jnp.float32)


def back_product(left_side, right_side):
    return lax.dot_general(
        left_side, right_side, (((1,), (1,)), ((), ())), preferred_element_type=jnp.float32
    )


def doc_info(lengths, token_index):
    doc_ends = jnp.cumsum(lengths, axis=-1)
    passed = (doc_ends[..., None, :] <= token_index[..., None]).astype(jnp.int32)
    segment = jnp.sum(passed, axis=-1)
    offset = jnp.sum(passed * lengths[..., None, :], axis=-1)
    return (segment, token_index - offset)


def rotate(field_in, position, turn_sign):
    half_dim = field_in.shape[-1] // 2
    frequency = THETA ** (-2.0 * jnp.arange(half_dim, dtype=jnp.float32) / field_in.shape[-1])
    angles = position.astype(jnp.float32)[:, None] * frequency
    cosine = jnp.cos(angles)[:, None, :]
    sine_part = turn_sign * jnp.sin(angles)[:, None, :]
    first_half = field_in[..., :half_dim]
    second_half = field_in[..., half_dim:]
    return jnp.concatenate(
        [
            first_half * cosine - second_half * sine_part,
            second_half * cosine + first_half * sine_part,
        ],
        axis=-1,
    )


def rms_forward(field_in, gain_row):
    inv_root = lax.rsqrt(jnp.mean(field_in * field_in, axis=-1, keepdims=True) + EPS)
    return (field_in * inv_root * gain_row, inv_root)


def rms_backward(field_in, gain_row, inv_root, grad_normed):
    scaled = gain_row * grad_normed
    grad_field = inv_root * scaled - field_in * inv_root**3 * jnp.mean(
        scaled * field_in, axis=-1, keepdims=True
    )
    return (grad_field, grad_normed * field_in * inv_root)


def token_place(block_id, row_ids, per_device, blk_count):
    return (row_ids // per_device * blk_count + block_id) * per_device + row_ids % per_device


def masks_for(lengths, blk_index, per_device, blk_count, seq_count):
    block_tokens = seq_count * per_device
    row_ids = jnp.arange(block_tokens, dtype=jnp.int32)
    query_index = token_place(blk_index, row_ids, per_device, blk_count)
    all_ids = jnp.arange(blk_count * block_tokens, dtype=jnp.int32)
    key_index = token_place(all_ids // block_tokens, all_ids % block_tokens, per_device, blk_count)
    query_seg, _ = doc_info(lengths, query_index)
    key_seg, _ = doc_info(lengths, key_index)
    return (query_index, key_index, query_seg, key_seg)


def head_scores(queries, key_rows, allowed, kv_local):
    grouped = queries.reshape(queries.shape[0], kv_local, -1, HEAD_DIM)
    key_heads = key_rows.reshape(key_rows.shape[0], kv_local, HEAD_DIM)
    scores = jnp.einsum(
        "rkgd,lkd->kgrl", grouped, key_heads, preferred_element_type=jnp.float32
    ) * HEAD_DIM ** (-0.5)
    return (jnp.where(allowed, scores, MASKED), grouped, key_heads)


def attend_forward(operands, query_index, key_index, kv_local):
    queries, key_rows, value_rows, query_seg, key_seg = operands
    allowed = (query_seg[:, None] == key_seg[None, :]) & (
        key_index[None, :] <= query_index[:, None]
    )
    scores, grouped, key_heads = head_scores(queries, key_rows, allowed, kv_local)
    row_top = jnp.max(scores, axis=-1, keepdims=True)
    log_total = row_top + jnp.log(jnp.sum(jnp.exp(scores - row_top), axis=-1, keepdims=True))
    weights_low = jnp.exp(scores - log_total).astype(jnp.bfloat16)
    value_heads = value_rows.reshape(value_rows.shape[0], kv_local, HEAD_DIM)
    mixed_heads = jnp.einsum(
        "kgrl,lkd->rkgd", weights_low, value_heads, preferred_element_type=jnp.float32
    )
    return (mixed_heads.reshape(queries.shape).astype(jnp.bfloat16), log_total)


def attend_backward(operands, query_index, key_index, kv_local):
    queries, key_rows, value_rows, grad_mixed, log_total, query_seg, key_seg = operands
    allowed = (query_seg[:, None] == key_seg[None, :]) & (
        key_index[None, :] <= query_index[:, None]
    )
    scores, grouped, key_heads = head_scores(queries, key_rows, allowed, kv_local)
    attn_probs = jnp.exp(scores - log_total)
    value_heads = value_rows.reshape(value_rows.shape[0], kv_local, HEAD_DIM)
    grad_heads = grad_mixed.reshape(grouped.shape)
    grad_values = jnp.einsum(
        "kgrl,rkgd->lkd",
        attn_probs.astype(jnp.bfloat16),
        grad_heads,
        preferred_element_type=jnp.float32,
    )
    grad_probs = jnp.einsum(
        "rkgd,lkd->kgrl", grad_heads, value_heads, preferred_element_type=jnp.float32
    )
    centre = jnp.sum(attn_probs * grad_probs, axis=-1, keepdims=True)
    grad_scores = (attn_probs * (grad_probs - centre)).astype(jnp.bfloat16)
    grad_queries = jnp.einsum(
        "kgrl,lkd->rkgd", grad_scores, key_heads, preferred_element_type=jnp.float32
    ) * HEAD_DIM ** (-0.5)
    grad_keys = jnp.einsum(
        "kgrl,rkgd->lkd", grad_scores, grouped, preferred_element_type=jnp.float32
    ) * HEAD_DIM ** (-0.5)
    return (
        grad_queries.reshape(queries.shape).astype(jnp.bfloat16),
        grad_keys.reshape(key_rows.shape),
        grad_values.reshape(value_rows.shape),
    )


def layer_forward(section_in, lengths, weights, placing):
    shard_id, blk_index, seq_count, blk_count = placing
    gain_attn, w_query, w_key, w_value, w_output, gain_mlp, w_gate, w_up, w_down = weights
    seqs_here, per_device, width = section_in.shape
    token_rows = seqs_here * per_device
    copies = max(1, seq_count // KV_HEADS)
    kv_local = KV_HEADS * copies // seq_count
    token_index = shard_id * per_device + jnp.arange(per_device, dtype=jnp.int32)
    _, position = doc_info(lengths, token_index)
    position = position.reshape(token_rows)
    flat_in = section_in.reshape(token_rows, width)
    normed, inv_first = rms_forward(flat_in, gain_attn.astype(jnp.float32))
    normed_low = normed.astype(jnp.bfloat16)
    query_pre = product(normed_low, w_query).reshape(token_rows, HEADS, HEAD_DIM)
    key_pre = product(normed_low, w_key).reshape(token_rows, KV_HEADS, HEAD_DIM)
    value_pre = product(normed_low, w_value).reshape(token_rows, KV_HEADS, HEAD_DIM)
    query_rot = (
        rotate(query_pre, position, 1.0).astype(jnp.bfloat16).reshape(seqs_here, per_device, width)
    )
    key_rot = rotate(key_pre, position, 1.0).astype(jnp.bfloat16)
    spread_shape = (token_rows, KV_HEADS, copies, HEAD_DIM)
    key_rep = jnp.broadcast_to(key_rot[:, :, None, :], spread_shape).reshape(
        seqs_here, per_device, -1
    )
    value_rep = jnp.broadcast_to(
        value_pre.astype(jnp.bfloat16)[:, :, None, :], spread_shape
    ).reshape(seqs_here, per_device, -1)
    heads_query, heads_key, heads_value = (
        lax.all_to_all(query_rot, "seq", split_axis=2, concat_axis=1, tiled=True),
        lax.all_to_all(key_rep, "seq", split_axis=2, concat_axis=1, tiled=True),
        lax.all_to_all(value_rep, "seq", split_axis=2, concat_axis=1, tiled=True),
    )
    keys_all, values_all = (
        lax.all_gather(heads_key, "blk", axis=1, tiled=True),
        lax.all_gather(heads_value, "blk", axis=1, tiled=True),
    )
    query_index, key_index, query_seg, key_seg = masks_for(
        lengths, blk_index, per_device, blk_count, seq_count
    )
    heads_mixed, log_total = lax.map(
        lambda operands: attend_forward(operands, query_index, key_index, kv_local),
        (heads_query, keys_all, values_all, query_seg, key_seg),
    )
    token_mixed = lax.all_to_all(
        heads_mixed, "seq", split_axis=1, concat_axis=2, tiled=True
    ).reshape(token_rows, width)
    hidden = flat_in + product(token_mixed, w_output)
    normed_mlp, inv_second = rms_forward(hidden, gain_mlp.astype(jnp.float32))
    normed_mlp_low = normed_mlp.astype(jnp.bfloat16)
    gate_pre = product(normed_mlp_low, w_gate)
    up_pre = product(normed_mlp_low, w_up)
    act_low = (jax.nn.silu(gate_pre) * up_pre).astype(jnp.bfloat16)
    result = hidden + product(act_low, w_down)
    saved_state = (
        flat_in,
        normed_low,
        inv_first,
        position,
        heads_query,
        keys_all,
        values_all,
        log_total,
        token_mixed,
        hidden,
        inv_second,
        normed_mlp_low,
        gate_pre,
        up_pre,
        act_low,
        lengths,
    )
    return (result.reshape(section_in.shape), saved_state)


def layer_backward(upstream, saved_state, weights, placing):
    shard_id, blk_index, seq_count, blk_count = placing
    gain_attn, w_query, w_key, w_value, w_output, gain_mlp, w_gate, w_up, w_down = weights
    (
        flat_in,
        normed_low,
        inv_first,
        position,
        heads_query,
        keys_all,
        values_all,
        log_total,
        token_mixed,
        hidden,
        inv_second,
        normed_mlp_low,
        gate_pre,
        up_pre,
        act_low,
        lengths,
    ) = saved_state
    seqs_here, per_device, width = upstream.shape
    token_rows = seqs_here * per_device
    copies = max(1, seq_count // KV_HEADS)
    kv_local = KV_HEADS * copies // seq_count
    grad_rows = upstream.reshape(token_rows, width)
    grad_out_low = grad_rows.astype(jnp.bfloat16)
    grad_act = back_product(grad_out_low, w_down)
    gate_sigmoid = jax.nn.sigmoid(gate_pre)
    grad_gate_low = (
        grad_act * up_pre * gate_sigmoid * (1.0 + gate_pre * (1.0 - gate_sigmoid))
    ).astype(jnp.bfloat16)
    grad_up_low = (grad_act * jax.nn.silu(gate_pre)).astype(jnp.bfloat16)
    grad_normed_mlp = back_product(grad_gate_low, w_gate) + back_product(grad_up_low, w_up)
    grad_hidden_part, gain_mlp_terms = rms_backward(
        hidden, gain_mlp.astype(jnp.float32), inv_second, grad_normed_mlp
    )
    grad_hidden = grad_rows + grad_hidden_part
    grad_branch_low = grad_hidden.astype(jnp.bfloat16)
    grad_mixed_low = (
        back_product(grad_branch_low, w_output)
        .astype(jnp.bfloat16)
        .reshape(seqs_here, per_device, width)
    )
    heads_grad = lax.all_to_all(grad_mixed_low, "seq", split_axis=2, concat_axis=1, tiled=True)
    query_index, key_index, query_seg, key_seg = masks_for(
        lengths, blk_index, per_device, blk_count, seq_count
    )
    grad_heads_query, grad_keys_all, grad_values_all = lax.map(
        lambda operands: attend_backward(operands, query_index, key_index, kv_local),
        (heads_query, keys_all, values_all, heads_grad, log_total, query_seg, key_seg),
    )
    grad_key_own, grad_value_own = (
        lax.psum_scatter(
            grad_keys_all.astype(jnp.bfloat16), "blk", scatter_dimension=1, tiled=True
        ).astype(jnp.float32),
        lax.psum_scatter(
            grad_values_all.astype(jnp.bfloat16), "blk", scatter_dimension=1, tiled=True
        ).astype(jnp.float32),
    )
    token_query, token_key, token_value = (
        lax.all_to_all(grad_heads_query, "seq", split_axis=1, concat_axis=2, tiled=True),
        lax.all_to_all(
            grad_key_own.astype(jnp.bfloat16), "seq", split_axis=1, concat_axis=2, tiled=True
        ),
        lax.all_to_all(
            grad_value_own.astype(jnp.bfloat16), "seq", split_axis=1, concat_axis=2, tiled=True
        ),
    )
    grad_key_sum = jnp.sum(
        token_key.astype(jnp.float32).reshape(token_rows, KV_HEADS, copies, HEAD_DIM), axis=2
    )
    grad_value_sum = jnp.sum(
        token_value.astype(jnp.float32).reshape(token_rows, KV_HEADS, copies, HEAD_DIM), axis=2
    )
    grad_query_low = (
        rotate(token_query.astype(jnp.float32).reshape(token_rows, HEADS, HEAD_DIM), position, -1.0)
        .astype(jnp.bfloat16)
        .reshape(token_rows, width)
    )
    grad_key_low = (
        rotate(grad_key_sum, position, -1.0)
        .astype(jnp.bfloat16)
        .reshape(token_rows, KV_HEADS * HEAD_DIM)
    )
    grad_value_low = grad_value_sum.astype(jnp.bfloat16).reshape(token_rows, KV_HEADS * HEAD_DIM)
    grad_normed = (
        back_product(grad_query_low, w_query)
        + back_product(grad_key_low, w_key)
        + back_product(grad_value_low, w_value)
    )
    grad_in_part, gain_attn_terms = rms_backward(
        flat_in, gain_attn.astype(jnp.float32), inv_first, grad_normed
    )
    grad_input = (grad_hidden + grad_in_part).reshape(upstream.shape)
    weight_rows = (
        gain_attn_terms,
        normed_low,
        grad_query_low,
        grad_key_low,
        grad_value_low,
        token_mixed,
        grad_branch_low,
        gain_mlp_terms,
        normed_mlp_low,
        grad_gate_low,
        grad_up_low,
        act_low,
        grad_out_low,
    )
    return (grad_input, weight_rows)


def weight_term(inputs_low, outputs_low):
    if outputs_low is None:
        return jnp.sum(inputs_low, axis=0)
    return lax.dot_general(
        inputs_low, outputs_low, (((0,), (0,)), ((), ())), preferred_element_type=jnp.float32
    )


def shards(
    inputs,
    cotangent,
    doc_lengths,
    attention_gain,
    w_query,
    w_key,
    w_value,
    w_output,
    mlp_gain,
    w_gate,
    w_up,
    w_down,
):
    at_first = lax.axis_index("section") == 0
    seq_count = lax.axis_size("seq")
    blk_count = lax.axis_size("blk")
    blk_index = lax.axis_index("blk")
    shard_id = lax.axis_index("seq") * blk_count + blk_index
    placing = (shard_id, blk_index, seq_count, blk_count)
    micro_count = inputs.shape[0]
    local_shards = (
        attention_gain[0],
        w_query[0],
        w_key[0],
        w_value[0],
        w_output[0],
        mlp_gain[0],
        w_gate[0],
        w_up[0],
        w_down[0],
    )
    weights = (
        lax.all_gather(local_shards[0], "blk", axis=0, tiled=True),
        lax.all_gather(local_shards[1], "blk", axis=0, tiled=True),
        lax.all_gather(local_shards[2], "blk", axis=0, tiled=True),
        lax.all_gather(local_shards[3], "blk", axis=0, tiled=True),
        lax.all_gather(local_shards[4], "blk", axis=0, tiled=True),
        lax.all_gather(local_shards[5], "blk", axis=0, tiled=True),
        lax.all_gather(local_shards[6], "blk", axis=0, tiled=True),
        lax.all_gather(local_shards[7], "blk", axis=0, tiled=True),
        lax.all_gather(local_shards[8], "blk", axis=0, tiled=True),
    )
    received = jnp.zeros(inputs.shape[1:], jnp.bfloat16)
    saved_states = []
    section_outs = []
    for tick_index in range(micro_count + 1):
        fresh_input = inputs[min(tick_index, micro_count - 1)]
        section_in = jnp.where(at_first, fresh_input, received).astype(jnp.float32)
        lengths = jnp.where(
            at_first,
            doc_lengths[min(tick_index, micro_count - 1)],
            doc_lengths[max(tick_index - 1, 0)],
        )
        result, saved_state = layer_forward(section_in, lengths, weights, placing)
        result_low = result.astype(jnp.bfloat16)
        if tick_index < micro_count:
            received = passed_along(result_low, "section", 1)
        saved_states.append(saved_state)
        section_outs.append(result_low)
    weights = (
        lax.all_gather(local_shards[0], "blk", axis=0, tiled=True),
        lax.all_gather(local_shards[1], "blk", axis=0, tiled=True),
        lax.all_gather(local_shards[2], "blk", axis=0, tiled=True),
        lax.all_gather(local_shards[3], "blk", axis=0, tiled=True),
        lax.all_gather(local_shards[4], "blk", axis=0, tiled=True),
        lax.all_gather(local_shards[5], "blk", axis=0, tiled=True),
        lax.all_gather(local_shards[6], "blk", axis=0, tiled=True),
        lax.all_gather(local_shards[7], "blk", axis=0, tiled=True),
        lax.all_gather(local_shards[8], "blk", axis=0, tiled=True),
    )
    back_in = jnp.zeros(cotangent.shape[1:], jnp.bfloat16)
    grad_outs = []
    row_sets = []
    for tick_index in range(micro_count + 1):
        saved_state = jax.tree.map(
            lambda first_pick, second_pick: jnp.where(at_first, first_pick, second_pick),
            saved_states[max(tick_index - 1, 0)],
            saved_states[min(tick_index + 1, micro_count)],
        )
        upstream = jnp.where(at_first, back_in, cotangent[min(tick_index, micro_count - 1)]).astype(
            jnp.float32
        )
        grad_input, weight_rows = layer_backward(upstream, saved_state, weights, placing)
        grad_low = grad_input.astype(jnp.bfloat16)
        if tick_index < micro_count:
            back_in = passed_along(grad_low, "section", -1)
        grad_outs.append(grad_low)
        row_sets.append(weight_rows)
    activations = jnp.stack(
        [
            jnp.where(at_first, section_outs[index_m], section_outs[index_m + 1])
            for index_m in range(micro_count)
        ]
    )[None]
    input_grads = jnp.stack(
        [
            jnp.where(at_first, grad_outs[index_m + 1], grad_outs[index_m])
            for index_m in range(micro_count)
        ]
    )[None]
    picked = [
        jax.tree.map(
            lambda first_pick, second_pick: jnp.where(at_first, first_pick, second_pick),
            row_sets[index_m + 1],
            row_sets[index_m],
        )
        for index_m in range(micro_count)
    ]
    merged = jax.tree.map(lambda *pieces: jnp.concatenate(pieces, axis=0), *picked)
    (
        gain_attn_terms,
        normed_low,
        grad_query_low,
        grad_key_low,
        grad_value_low,
        token_mixed,
        grad_branch_low,
        gain_mlp_terms,
        normed_mlp_low,
        grad_gate_low,
        grad_up_low,
        act_low,
        grad_out_low,
    ) = merged
    grad_pairs = (
        (gain_attn_terms, None),
        (normed_low, grad_query_low),
        (normed_low, grad_key_low),
        (normed_low, grad_value_low),
        (token_mixed, grad_branch_low),
        (gain_mlp_terms, None),
        (normed_mlp_low, grad_gate_low),
        (normed_mlp_low, grad_up_low),
        (act_low, grad_out_low),
    )
    shares = tuple(
        (
            lax.psum_scatter(
                weight_term(left_side, right_side).astype(jnp.bfloat16),
                "blk",
                scatter_dimension=0,
                tiled=True,
            ).astype(jnp.float32)
            for left_side, right_side in grad_pairs
        )
    )
    shares = jax.tree.map(lambda part: part.astype(jnp.float32), lax.psum(shortened(shares), "seq"))
    return (
        activations,
        input_grads,
        shares[0][None],
        shares[1][None],
        shares[2][None],
        shares[3][None],
        shares[4][None],
        shares[5][None],
        shares[6][None],
        shares[7][None],
        shares[8][None],
    )


MESH = pl.DeviceIdType.MESH


def remote(source, target, sent, arrived, device):
    return pltpu.make_async_remote_copy(
        source, target, sent, arrived, device_id=device, device_id_type=MESH
    )


def greet(partners):
    barrier = pltpu.get_barrier_semaphore()
    for device in partners:
        pl.semaphore_signal(barrier, 1, device_id=device, device_id_type=MESH)
    pl.semaphore_wait(barrier, len(partners))


def settled(spot, semaphore, received):
    copy = remote(spot, spot, semaphore, semaphore, {"seq": lax.axis_index("seq") ^ 1})
    if received:
        copy.wait_recv()
    else:
        copy.wait_send()


def gather_steps(
    count, own, out, line_sent, line_got, side_sent, side_got, core_sent, core_got, local_done
):
    seq, b = lax.axis_index("seq"), lax.axis_index("blk")
    core, side = {"seq": seq ^ 1}, {"seq": seq ^ 2}
    base, side_base = seq * count, (seq ^ 2) * count

    def along_line(j, way, source=None):
        device = {"blk": b + (1 if way else -1)}
        spot = out.at[base + j]
        return remote(
            spot if source is None else source, spot, line_sent.at[j, way], line_got.at[j], device
        )

    def to_side(j, source=None):
        spot = out.at[base + j]
        return remote(
            spot if source is None else source, spot, side_sent.at[j], side_got.at[j], side
        )

    def to_core(half, j, source=None):
        spot = out.at[(side_base if half else base) + j]
        return remote(
            spot if source is None else source,
            spot,
            core_sent.at[half, j],
            core_got.at[half, j],
            core,
        )

    local = pltpu.make_async_copy(own, out.at[base + b], local_done)
    local.start()
    to_side(b, own).start()

    @pl.when(b > 0)
    def _():
        along_line(b, 0, own).start()

    @pl.when(b < count - 1)
    def _():
        along_line(b, 1, own).start()

    to_core(0, b, own).start()
    yield "sent"

    def from_line(j, way):
        settled(out.at[base + j], line_got.at[j], True)

        @pl.when((b < count - 1) if way else (b > 0))
        def _():
            along_line(j, way).start()

        to_side(j).start()
        to_core(0, j).start()

    def from_side(j):
        settled(out.at[side_base + j], side_got.at[j], True)
        to_core(1, j).start()

    for k in range(1, count + 1):
        if k < count:
            pl.when(b - k >= 0)(functools.partial(from_line, b - k, 1))
            pl.when(b + k < count)(functools.partial(from_line, b + k, 0))
        if k == 1:
            from_side(b)
        else:
            pl.when(b - k + 1 >= 0)(functools.partial(from_side, b - k + 1))
            pl.when(b + k - 1 < count)(functools.partial(from_side, b + k - 1))
        if k == count - 1:
            local.wait()
        yield "line" if k == count - 1 else "side" if k == count else "step"
    for half, corner in ((0, seq ^ 1), (1, seq ^ 3)):
        for j in range(count):
            settled(out.at[corner * count + j], core_got.at[half, j], True)
        yield "corner" if half else "near"
    for j in range(count):
        to_side(j).wait_send()
        to_core(0, j).wait_send()
        to_core(1, j).wait_send()

    @pl.when(b > 0)
    def _():
        along_line(b, 0).wait_send()

    @pl.when(b < count - 1)
    def _():
        along_line(b, 1).wait_send()

    for k in range(1, count):

        @pl.when((b - k >= 0) & (b < count - 1))
        def _():
            along_line(b - k, 1).wait_send()

        @pl.when((b + k < count) & (b > 0))
        def _():
            along_line(b + k, 0).wait_send()


def gather_semaphores(count):
    dma = pltpu.SemaphoreType.DMA
    return [
        dma((count, 2)),
        dma((count,)),
        dma((count,)),
        dma((count,)),
        dma((2, count)),
        dma((2, count)),
        dma,
    ]


def advance(steps, times):
    for _ in range(times):
        next(steps, None)


def group_of(event):
    seq = lax.axis_index("seq")
    return {"line": seq, "side": seq ^ 2, "near": seq ^ 1, "corner": seq ^ 3}.get(event)


def scatter_steps(
    count,
    partial,
    deliver,
    core_slot,
    side_slot,
    line_slot,
    side_out,
    line_out,
    running,
    core_sent,
    core_got,
    side_sent,
    side_got,
    line_sent,
    line_got,
    compute=None,
):
    seq, b = lax.axis_index("seq"), lax.axis_index("blk")
    core, side = {"seq": seq ^ 1}, {"seq": seq ^ 2}
    place = far_first(b, count)

    def to_core(half, k):
        source = partial.at[(seq ^ (1 if half else 3)) * count + place[k]]
        return remote(
            source, core_slot.at[half, k], core_sent.at[half, k], core_got.at[half, k], core
        )

    def to_side(k):
        return remote(side_out.at[k], side_slot.at[k], side_sent.at[k], side_got.at[k], side)

    def along_line(k, way):
        j = place[k]
        return remote(
            line_out.at[k],
            line_slot.at[way, j],
            line_sent.at[k],
            line_got.at[way, j],
            {"blk": b + (1 if way else -1)},
        )

    def add_from(way, j):
        settled(line_slot.at[way, j], line_got.at[way, j], True)
        running[...] += line_slot[way, j].astype(jnp.float32)

    for half in range(2):
        if compute:
            compute(seq ^ (1 if half else 3))
        for k in range(count):
            to_core(half, k).start()
    if compute:
        compute(seq ^ 2)
    for k in range(count):
        to_core(0, k).wait_recv()
        total = partial[(seq ^ 2) * count + place[k]].astype(jnp.float32)
        total += core_slot[0, k].astype(jnp.float32)
        side_out[k] = total.astype(jnp.bfloat16)
        to_side(k).start()
    if compute:
        compute(seq)
    yield
    for k in range(count):
        j = place[k]
        to_core(1, k).wait_recv()
        to_side(k).wait_recv()
        total = partial[seq * count + j].astype(jnp.float32)
        total += core_slot[1, k].astype(jnp.float32)
        running[...] = total + side_slot[k].astype(jnp.float32)
        rightward, leftward = j >= b, j <= b
        pl.when(rightward & (b > 0))(functools.partial(add_from, 1, j))
        pl.when(leftward & (b < count - 1))(functools.partial(add_from, 0, j))
        if k < count - 1:
            line_out[k] = running[...].astype(jnp.bfloat16)

            @pl.when(rightward)
            def _():
                along_line(k, 1).start()

            @pl.when(jnp.logical_not(rightward))
            def _():
                along_line(k, 0).start()

            yield
    deliver(running[...])
    yield
    for k in range(count):
        to_core(0, k).wait_send()
        to_core(1, k).wait_send()
        to_side(k).wait_send()
        if k < count - 1:
            settled(line_out.at[k], line_sent.at[k], False)


def far_first(b, count):
    order = sorted(range(count), key=lambda j: -j)
    places = []
    for k in range(count):
        place = 0
        for own in range(count):
            by_distance = sorted(order, key=lambda j: (-abs(j - own), -j if own * 2 < count else j))
            place = jnp.where(b == own, by_distance[k], place)
        places.append(place)
    return places


def scatter_scratch(count, rows, width):
    dma = pltpu.SemaphoreType.DMA

    def slots(*places):
        return pltpu.VMEM(places + (rows, width), jnp.bfloat16)

    return [
        slots(2, count),
        slots(count),
        slots(2, count),
        slots(count),
        slots(count - 1),
        pltpu.VMEM((rows, width), jnp.float32),
        dma((2, count)),
        dma((2, count)),
        dma((count,)),
        dma((count,)),
        dma((count - 1,)),
        dma((2, count)),
    ]


def run_with(steps, fillers):
    fillers = list(fillers)
    for _ in steps:
        if fillers:
            fillers.pop(0)()
    for filler in fillers:
        filler()


def greet_group(count, more=()):
    seq, b = lax.axis_index("seq"), lax.axis_index("blk")
    greet(
        tuple(more)
        + ({"seq": seq ^ 1}, {"seq": seq ^ 2})
        + tuple({"blk": lax.rem(b + k, count)} for k in range(1, count))
    )


def carry(copies, from_section, what):
    sending = lax.axis_index("section") == from_section
    for copy in copies:
        if what == "start":
            pl.when(sending)(copy.start)
        else:
            pl.when(sending)(copy.wait_send)
            pl.when(jnp.logical_not(sending))(copy.wait_recv)


def carried(sources, targets, sent, got):
    other = {"section": 1 - lax.axis_index("section")}
    return [
        remote(source, target, sent.at[n], got.at[n], other)
        for n, (source, target) in enumerate(zip(sources, targets))
    ]


def group_rows(ref, group, count):
    value = ref[pl.ds(group * count, count)]
    return value.reshape(value.shape[0] * value.shape[1], value.shape[2])


def group_span(group, count, block):
    size = count * block
    return pl.ds(pl.multiple_of(group * size, size), size)


def lane_turn(field_in, cosine, sine):
    half_dim, lanes = HEAD_DIM // 2, field_in.shape[-1]
    lane = lax.broadcasted_iota(jnp.int32, field_in.shape, 1)
    partner = jnp.where(
        lane < half_dim,
        pltpu.roll(field_in, lanes - half_dim, 1),
        pltpu.roll(field_in, half_dim, 1),
    )
    return field_in * cosine + partner * sine


def masked_scores(query, key, first_row, start):
    scores = back_product(query, key) * HEAD_DIM ** (-0.5)
    key_index = lax.broadcasted_iota(jnp.int32, scores.shape, 1)
    query_index = first_row + lax.broadcasted_iota(jnp.int32, scores.shape, 0)
    return jnp.where((key_index >= start) & (key_index <= query_index), scores, MASKED)


def normalise(field_in, gain_row):
    inv_root = lax.rsqrt(jnp.mean(field_in * field_in, axis=-1, keepdims=True) + EPS)
    return field_in * inv_root * gain_row


PAD = 128


def load_weights(attn, out, attn_vm, out_vm, sems):
    copies = []
    for part in range(3):
        copies.append(
            pltpu.make_async_copy(
                attn.at[pl.ds(part * HEAD_DIM, HEAD_DIM)],
                attn_vm.at[pl.ds(part * PAD, HEAD_DIM)],
                sems.at[part],
            )
        )
    copies.append(
        pltpu.make_async_copy(
            attn.at[pl.ds(3 * HEAD_DIM, 16)], attn_vm.at[pl.ds(3 * PAD, 16)], sems.at[3]
        )
    )
    copies.append(pltpu.make_async_copy(out, out_vm.at[pl.ds(0, HEAD_DIM)], sems.at[4]))
    return copies


def clear_pads(attn_vm, out_vm):
    empty = jnp.zeros((PAD - HEAD_DIM, attn_vm.shape[1]), jnp.bfloat16)
    for part in range(3):
        attn_vm[part * PAD + HEAD_DIM : (part + 1) * PAD] = empty
    out_vm[HEAD_DIM:PAD] = empty


def attention_rows(heads, log_total, start, size, tokens):
    for i in range(tokens // size):
        here, seen = slice(i * size, (i + 1) * size), slice(0, (i + 1) * size)
        scores = masked_scores(heads[0, here], heads[1, seen], i * size, start[here])
        row_top = jnp.max(scores, axis=-1, keepdims=True)
        weights = jnp.exp(scores - row_top)
        total = jnp.sum(weights, axis=-1, keepdims=True)
        log_total[here] = row_top + jnp.log(total)
        weights = (weights * (1.0 / total)).astype(jnp.bfloat16)
        heads[3, here] = product(weights, heads[2, seen]).astype(jnp.bfloat16)


def project_heads(normed, attn_vm, heads, span, cosine, sine):
    mixed = back_product(normed, attn_vm[0 : 3 * PAD])
    cos_rows, sin_rows = cosine[span], sine[span]
    heads[0, span] = lane_turn(mixed[:, :PAD], cos_rows, sin_rows).astype(jnp.bfloat16)
    heads[1, span] = lane_turn(mixed[:, PAD : 2 * PAD], cos_rows, sin_rows).astype(jnp.bfloat16)
    heads[2, span] = mixed[:, 2 * PAD :].astype(jnp.bfloat16)


def keep_group(partial, group, value, count):
    block = partial.shape[1]
    partial[pl.ds(group * count, count)] = value.astype(jnp.bfloat16).reshape(count, block, -1)


def gain_of(ref, row):
    return ref[3 * PAD : 3 * PAD + 16][row : row + 1].astype(jnp.float32)


def attn_kernel(count, *refs):
    refs = iter(refs)

    def take(n):
        return [next(refs) for _ in range(n)]

    rows_in, x_own, attn, out, cosine, sine, start = take(7)
    hidden_out, normed_out, all_rows, heads, log_total = take(5)
    rows_vm, attn_vm, out_vm, partial, load_done, save_done = take(6)
    gather_sems = take(7)
    scatter_refs = list(refs)
    block = rows_vm.shape[1]
    tokens = block * rows_vm.shape[0]
    size = count * block
    greet_group(count)
    steps = gather_steps(count, rows_in, rows_vm, *gather_sems)
    next(steps)
    clear_pads(attn_vm, out_vm)
    loads = load_weights(attn.at[1], out.at[1], attn_vm, out_vm, load_done)
    start_all(loads)
    for event in steps:
        if event == "line":
            wait_all(loads)
        group = group_of(event)
        if group is not None:
            span = group_span(group, count, block)
            normed = group_rows(rows_vm, group, count)
            project_heads(normed, attn_vm, heads, span, cosine, sine)
    save = pltpu.make_async_copy(rows_vm, all_rows, save_done.at[0])
    save.start()
    attention_rows(heads, log_total, start, size, tokens)

    def project_out(group):
        mixed = heads[3, group_span(group, count, block)]
        keep_group(partial, group, product(mixed, out_vm[...]), count)

    def deliver(total):
        hidden = x_own[...].astype(jnp.float32) + total
        hidden_out[...] = hidden
        normed_out[...] = normalise(hidden, gain_of(attn_vm, 1)).astype(jnp.bfloat16)

    run_with(scatter_steps(count, partial, deliver, *scatter_refs, compute=project_out), [])
    save.wait()


def first_layer_kernel(count, *refs):
    refs = iter(refs)

    def take(n):
        return [next(refs) for _ in range(n)]

    pieces, w_gate, w_up, w_output, w_down, rows_in, grads_in, cosine, sine, start = take(10)
    attn, gate_up, out, down, grads_all, all_rows, wide_rows = take(7)
    hidden, result_out, normed_out, heads, log_total = take(5)
    raw_vm, normed_vm, rows_vm, grads_vm, partial, partial_two = take(6)
    attn_vm, out_vm, wide_vm, down_vm, units, normed_own, gain_vm = take(7)
    load_done, save_done = take(2)
    spread_sems = take(5)
    first_sems, second_sems, grads_sems = take(7), take(7), take(7)
    scatter_one, scatter_two = take(12), take(12)
    section = lax.axis_index("section")
    block, width = raw_vm.shape[1], raw_vm.shape[2]
    tokens = block * raw_vm.shape[0]
    size = count * block
    low, f32 = jnp.bfloat16, jnp.float32
    greet_group(count, ({"section": 1 - section},))
    steps = gather_steps(count, rows_in, raw_vm, *first_sems)
    next(steps)
    spread = spread_steps(
        count, pieces, w_gate, w_up, w_output, w_down, attn, gate_up, out, down, *spread_sems
    )
    next(spread)
    clear_pads(attn_vm, out_vm)
    for event in steps:
        if event == "line":
            next(spread)
    grad_steps = gather_steps(count, grads_in, grads_vm, *grads_sems)
    next(grad_steps)
    next(spread)
    next(spread)
    loads = load_weights(attn.at[0], out.at[0], attn_vm, out_vm, load_done)
    loads.append(
        pltpu.make_async_copy(attn.at[1, pl.ds(3 * HEAD_DIM, 16)], gain_vm, load_done.at[5])
    )
    start_all(loads)
    wait_all(loads)
    for group in range(tokens // size):
        raw = raw_vm[group * count : (group + 1) * count].astype(f32)
        normed = normalise(raw, gain_of(attn_vm, 0)[None]).astype(low)
        normed_vm[group * count : (group + 1) * count] = normed
        span = slice(group * size, (group + 1) * size)
        project_heads(normed.reshape(size, width), attn_vm, heads, span, cosine, sine)
    saves = [pltpu.make_async_copy(normed_vm, all_rows, save_done.at[0])]
    saves[0].start()
    attention_rows(heads, log_total, start, size, tokens)

    def project_out(group):
        mixed = heads[3, group_span(group, count, block)]
        keep_group(partial, group, product(mixed, out_vm[...]), count)

    def deliver(total):
        value = rows_in[...].astype(f32) + total
        hidden[...] = value
        normed_own[...] = normalise(value, gain_of(attn_vm, 1)).astype(low)

    def more():
        next(spread)
        next(grad_steps, None)

    next(grad_steps)
    run_with(scatter_steps(count, partial, deliver, *scatter_one, compute=project_out), [more] * 5)
    for number, event in enumerate(gather_steps(count, normed_own, rows_vm, *second_sems)):
        if number == 0:
            more()
    for _ in spread:
        pass
    loads = [
        pltpu.make_async_copy(gate_up.at[0], wide_vm, load_done.at[0]),
        pltpu.make_async_copy(down.at[0], down_vm, load_done.at[1]),
    ]
    start_all(loads)
    wait_all(loads)
    saves.append(pltpu.make_async_copy(rows_vm, wide_rows, save_done.at[1]))
    saves[1].start()

    def project_down(group):
        pre = product(group_rows(rows_vm, group, count), wide_vm[...])
        made = hidden_units(pre)
        units[group_span(group, count, block)] = made
        keep_group(partial_two, group, product(made, down_vm[...]), count)

    def deliver_two(total):
        made = (hidden[...] + total).astype(low)
        result_out[...] = made
        gain = gain_vm[...][0:1].astype(f32)
        normed_out[...] = normalise(made.astype(f32), gain).astype(low)

    run_with(scatter_steps(count, partial_two, deliver_two, *scatter_two, compute=project_down), [])
    for _ in grad_steps:
        pass
    saves.append(pltpu.make_async_copy(grads_vm, grads_all, save_done.at[2]))
    saves[2].start()
    wait_all(saves)


def spread_steps(
    count,
    pieces,
    w_gate,
    w_up,
    w_output,
    w_down,
    attn,
    gate_up,
    out,
    down,
    line_sent,
    line_got,
    cross_sent,
    cross_got,
    local_done,
):
    seq, b, section = lax.axis_index("seq"), lax.axis_index("blk"), lax.axis_index("section")
    seq_count = lax.axis_size("seq")
    other = {"section": 1 - section}
    rows, lanes = w_gate.shape[0], gate_up.shape[2] // 2
    turns = tuple(range(count // 2, 0, -1)) + tuple(range(count // 2 + 1, count))

    def source(kind, j):
        if kind == 0:
            return pieces.at[j]
        weight = w_gate if kind == 1 else w_up
        return weight.at[:, pl.ds(pl.multiple_of((j * seq_count + seq) * lanes, lanes), lanes)]

    def target(kind, j):
        if kind == 0:
            return attn.at[section, :, pl.ds(pl.multiple_of(j * rows, rows), rows)]
        return gate_up.at[
            section, pl.ds(pl.multiple_of(j * rows, rows), rows), pl.ds((kind - 1) * lanes, lanes)
        ]

    def along_line(kind, k):
        j = lax.rem(b + k, count)
        return remote(
            source(kind, j),
            target(kind, b),
            line_sent.at[kind, k],
            line_got.at[kind, k],
            {"blk": j},
        )

    def across(kind, j, slot, begin=None):
        spot = target(kind, j)
        return remote(
            spot if begin is None else begin,
            spot,
            cross_sent.at[kind, slot],
            cross_got.at[kind, slot],
            other,
        )

    def own_rows(kind):
        weight, place = (w_output, out) if kind == 3 else (w_down, down)
        size = place.shape[1]
        begin = weight.at[pl.ds(pl.multiple_of(seq * size, size), size)]
        spot = place.at[section]
        return (
            remote(begin, spot, cross_sent.at[kind, 0], cross_got.at[kind, 0], other),
            pltpu.make_async_copy(begin, spot, local_done.at[kind]),
        )

    def own_piece(kind):
        return (
            across(kind, b, 0, source(kind, b)),
            pltpu.make_async_copy(source(kind, b), target(kind, b), local_done.at[kind]),
        )

    def forward(kind, k):
        j = lax.rem(b + count - k, count)
        settled(target(kind, j), line_got.at[kind, k], True)
        across(kind, j, k).start()

    def arrived(kind):
        if kind > 2:
            wait_all(own_rows(kind))
            return
        for k in range(count):
            settled(target(kind, 0), cross_got.at[kind, k], True)
            settled(target(kind, 0), cross_sent.at[kind, k], False)
            if k:
                settled(target(kind, 0), line_sent.at[kind, k], False)
        pltpu.make_async_copy(source(kind, b), target(kind, b), local_done.at[kind]).wait()

    for k in turns:
        along_line(0, k).start()
    start_all(own_piece(0) + own_rows(3))
    yield
    for k in turns:
        forward(0, k)
    yield
    for kind in (1, 2):
        for k in turns:
            along_line(kind, k).start()
    yield
    arrived(0)
    arrived(3)
    start_all(own_piece(1) + own_piece(2) + own_rows(4))
    yield
    for kind in (1, 2):
        for k in turns:
            forward(kind, k)
            yield
    for kind in (1, 2, 4):
        arrived(kind)


def start_all(copies):
    for copy in copies:
        copy.start()


def wait_all(copies):
    for copy in copies:
        copy.wait()


def gated(pre):
    half = pre.shape[1] // 2
    gate, up = pre[:, :half], pre[:, half:]
    sigma = jax.nn.sigmoid(gate)
    return gate, up, sigma


def hidden_units(pre):
    gate, up, sigma = gated(pre)
    return (gate * sigma * up).astype(jnp.bfloat16)


def store_gate_grads(place, span, grad_act, pre):
    gate, up, sigma = gated(pre)
    half = gate.shape[1]
    place[span, 0:half] = (grad_act * up * sigma * (1.0 + gate * (1.0 - sigma))).astype(
        jnp.bfloat16
    )
    place[span, half : 2 * half] = (grad_act * (gate * sigma)).astype(jnp.bfloat16)


def wide_grads(rows_vm, pre_grads, units, grads_vm, wide_grad, down_grad):
    tokens = pre_grads.shape[0]
    width = rows_vm.shape[2]
    step = width // 4

    def wide_part(n):
        cut = slice(n * step, (n + 1) * step)
        rows = rows_vm[:, :, cut].reshape(tokens, step)
        wide_grad[cut] = weight_term(rows, pre_grads[...]).astype(jnp.bfloat16)

    def down_part(n):
        cut = slice(n * 2 * step, (n + 1) * 2 * step)
        rows = grads_vm[:, :, cut].reshape(tokens, 2 * step)
        down_grad[:, cut] = weight_term(units[...], rows).astype(jnp.bfloat16)

    return [functools.partial(wide_part, n) for n in range(4)] + [
        functools.partial(down_part, n) for n in range(2)
    ]


def mlp_grad_sent(total, hidden, grads_own, gain, branch_out, grad_hidden_out, gain_out):
    field_in = hidden[...]
    inv_root = lax.rsqrt(jnp.mean(field_in * field_in, axis=-1, keepdims=True) + EPS)
    part, terms = rms_backward(field_in, gain[...], inv_root, total)
    grad_hidden = grads_own[...].astype(jnp.float32) + part
    grad_hidden_out[...] = grad_hidden
    branch_out[...] = grad_hidden.astype(jnp.bfloat16)
    gain_out[...] = jnp.broadcast_to(jnp.sum(terms, axis=0, keepdims=True), gain_out.shape)


def mlp_both_kernel(count, *refs):
    refs = iter(refs)

    def take(n):
        return [next(refs) for _ in range(n)]

    rows_in, hidden, gate_up, down, grads_all, grads_own, gain = take(7)
    result_out, branch_out, grad_hidden_out, gain_out, wide_grad, down_grad = take(6)
    rows_vm, grads_vm, wide_vm, down_vm, units, pre_grads, partial, partial_back = take(8)
    (load_done,) = take(1)
    gather_sems = take(7)
    scatter_refs, scatter_back = take(12), take(12)
    block = rows_vm.shape[1]
    greet_group(count)
    steps = gather_steps(count, rows_in, rows_vm, *gather_sems)
    next(steps)
    loads = [
        pltpu.make_async_copy(gate_up.at[1], wide_vm, load_done.at[0]),
        pltpu.make_async_copy(down.at[1], down_vm, load_done.at[1]),
        pltpu.make_async_copy(grads_all, grads_vm, load_done.at[2]),
    ]
    start_all(loads)

    def through(group):
        span = group_span(group, count, block)
        pre = product(group_rows(rows_vm, group, count), wide_vm[...])
        units[span] = hidden_units(pre)
        grad_act = back_product(group_rows(grads_vm, group, count), down_vm[...])
        store_gate_grads(pre_grads, span, grad_act, pre)
        value = back_product(pre_grads[span], wide_vm[...])
        partial_back[pl.ds(group * count, count)] = value.astype(jnp.bfloat16).reshape(
            count, block, -1
        )

    for event in steps:
        if event == "line":
            wait_all(loads)
        group = group_of(event)
        if group is not None:
            through(group)

    def project_down(group):
        value = product(units[group_span(group, count, block)], down_vm[...])
        partial[pl.ds(group * count, count)] = value.astype(jnp.bfloat16).reshape(count, block, -1)

    def deliver(total):
        result_out[...] = (hidden[...] + total).astype(jnp.bfloat16)

    def deliver_back(total):
        mlp_grad_sent(
            total, hidden, grads_own, gain, branch_out, grad_hidden_out, gain_out
        )

    back = scatter_steps(count, partial_back, deliver_back, *scatter_back)
    ahead = scatter_steps(count, partial, deliver, *scatter_refs, compute=project_down)
    next(back)
    next(ahead)
    run_with(back, wide_grads(rows_vm, pre_grads, units, grads_vm, wide_grad, down_grad))
    run_with(ahead, [])


def mlp_back_kernel(count, *refs):
    refs = iter(refs)

    def take(n):
        return [next(refs) for _ in range(n)]

    grads_own, hidden, all_rows, gate_up, down, gain = take(6)
    carry_from = take(2)
    branch_out, grad_hidden_out, gain_out, wide_grad, down_grad = take(5)
    carry_to = take(2)
    rows_vm, grads_vm, wide_vm, down_vm, units, pre_vm, pre_grads, partial, load_done = take(9)
    carry_sent, carry_got = take(2)
    gather_sems = take(7)
    scatter_refs = list(refs)
    block = rows_vm.shape[1]
    greet_group(count, ({"section": 1 - lax.axis_index("section")},))
    steps = gather_steps(count, grads_own, grads_vm, *gather_sems)
    next(steps)
    copies = carried(carry_from, carry_to, carry_sent, carry_got)
    carry(copies, 0, "start")
    loads = [
        pltpu.make_async_copy(gate_up.at[0], wide_vm, load_done.at[0]),
        pltpu.make_async_copy(all_rows, rows_vm, load_done.at[1]),
        pltpu.make_async_copy(down.at[0], down_vm, load_done.at[2]),
    ]
    start_all(loads)

    def again(group):
        span = group_span(group, count, block)
        pre = product(group_rows(rows_vm, group, count), wide_vm[...])
        pre_vm[span] = pre
        units[span] = hidden_units(pre)

    def through(group):
        span = group_span(group, count, block)
        grad_act = back_product(group_rows(grads_vm, group, count), down_vm[...])
        store_gate_grads(pre_grads, span, grad_act, pre_vm[span])
        value = back_product(pre_grads[span], wide_vm[...])
        partial[pl.ds(group * count, count)] = value.astype(jnp.bfloat16).reshape(count, block, -1)

    wait_all(loads)
    for number, event in enumerate(steps):
        if number < 2:
            again(2 * number)
            again(2 * number + 1)
        group = group_of(event)
        if group is not None:
            through(group)

    def deliver(total):
        mlp_grad_sent(total, hidden, grads_own, gain, branch_out, grad_hidden_out, gain_out)

    run_with(
        scatter_steps(count, partial, deliver, *scatter_refs),
        wide_grads(rows_vm, pre_grads, units, grads_vm, wide_grad, down_grad),
    )
    carry(copies, 0, "wait")


def attn_back_kernel(count, layer, *refs):
    refs = iter(refs)

    def take(n):
        return [next(refs) for _ in range(n)]

    branch_in, grad_hidden, x_own, all_rows, heads_kept, log_total, attn, out = take(8)
    cosine, sine, start, gain = take(4)
    carry_from = take(2)
    grad_out, gain_out, attn_grad, out_grad = take(4)
    carry_to = take(2)
    branch_vm, rows_vm, heads, attn_vm, out_vm, mixed_grads, probs = take(7)
    key_grads, value_grads, joint, partial, load_done, carry_sent, carry_got = take(7)
    gather_sems = take(7)
    scatter_refs = list(refs)
    block = rows_vm.shape[1]
    size = count * block
    tokens = block * rows_vm.shape[0]
    low, f32 = jnp.bfloat16, jnp.float32
    scale = HEAD_DIM ** (-0.5)
    greet_group(count, ({"section": 1 - lax.axis_index("section")},))
    steps = gather_steps(count, branch_in, branch_vm, *gather_sems)
    next(steps)
    copies = carried(carry_from, carry_to, carry_sent, carry_got)
    carry(copies, 1 - layer, "start")
    clear_pads(attn_vm, out_vm)
    loads = load_weights(attn.at[layer], out.at[layer], attn_vm, out_vm, load_done)
    loads.append(pltpu.make_async_copy(heads_kept, heads, load_done.at[5]))
    loads.append(pltpu.make_async_copy(all_rows, rows_vm, load_done.at[6]))
    start_all(loads)
    key_grads[...] = jnp.zeros_like(key_grads)
    value_grads[...] = jnp.zeros_like(value_grads)
    wait_all(loads)

    def spans(i):
        return slice(i * size, (i + 1) * size), slice(0, (i + 1) * size)

    def weigh(i):
        here, seen = spans(i)
        scores = masked_scores(heads[0, here], heads[1, seen], i * size, start[here])
        probs[here, seen] = jnp.exp(scores - log_total[here])

    def project(group):
        value = back_product(group_rows(branch_vm, group, count), out_vm[...])
        mixed_grads[group_span(group, count, block)] = value.astype(low)

    for number, event in enumerate(steps):
        if number < 2:
            weigh(2 * number)
            weigh(2 * number + 1)
        group = group_of(event)
        if group is not None:
            project(group)
    for i in reversed(range(tokens // size)):
        here, seen = spans(i)
        weights = probs[here, seen]
        grads = mixed_grads[here]
        grad_weights = back_product(grads, heads[2, seen])
        centre = jnp.sum(weights * grad_weights, axis=-1, keepdims=True)
        grad_scores = (weights * (grad_weights - centre)).astype(low)
        query_grad = (product(grad_scores, heads[1, seen]) * scale).astype(low).astype(f32)
        joint[here, 0:PAD] = lane_turn(query_grad, cosine[here], -sine[here]).astype(low)
        key_grads[seen] += weight_term(grad_scores, heads[0, here])
        value_grads[seen] += weight_term(weights.astype(low), grads)
        key_grad = (key_grads[here] * scale).astype(low).astype(f32)
        joint[here, PAD : 2 * PAD] = lane_turn(key_grad, cosine[here], -sine[here]).astype(low)
        joint[here, 2 * PAD : 3 * PAD] = value_grads[here].astype(low)

    def project_back(group):
        value = product(joint[group_span(group, count, block)], attn_vm[0 : 3 * PAD])
        partial[pl.ds(group * count, count)] = value.astype(low).reshape(count, block, -1)

    def attn_part(part):
        rows = rows_vm[...].reshape(tokens, rows_vm.shape[2])
        value = weight_term(joint[:, part * PAD : (part + 1) * PAD], rows)
        attn_grad[part * HEAD_DIM : (part + 1) * HEAD_DIM] = value[0:HEAD_DIM].astype(low)

    def out_part():
        rows = branch_vm[...].reshape(tokens, branch_vm.shape[2])
        out_grad[...] = weight_term(heads[3], rows)[0:HEAD_DIM].astype(low)

    def deliver(total):
        field_in = x_own[...].astype(f32)
        inv_root = lax.rsqrt(jnp.mean(field_in * field_in, axis=-1, keepdims=True) + EPS)
        part, terms = rms_backward(field_in, gain[...], inv_root, total)
        grad_out[...] = (grad_hidden[...] + part).astype(low)
        gain_out[...] = jnp.broadcast_to(jnp.sum(terms, axis=0, keepdims=True), gain_out.shape)

    run_with(
        scatter_steps(count, partial, deliver, *scatter_refs, compute=project_back),
        [functools.partial(attn_part, part) for part in range(3)] + [out_part],
    )
    carry(copies, 1 - layer, "wait")


def finish_kernel(count, *refs):
    refs = iter(refs)

    def take(n):
        return [next(refs) for _ in range(n)]

    ones, twos = take(4), take(4)
    wide_from_two, down_from_two, wide_from_one, down_from_one = take(4)
    attn_from_one, out_from_one, gains, swap_rows = take(4)
    attn, out, gate, up, down, gains_out, swapped_rows = take(7)
    attn_own, out_own, wide_own, down_own, attn_in, out_in, wide_in, down_in = take(8)
    attn_slot, wide_slot = take(2)
    gain_in, gain_sum, gain_line, gain_part, gain_side, gain_core = take(6)
    load_done, cross_sent, cross_got, line_sent, line_got = take(5)
    side_sent, side_got, core_sent, core_got, local_done, small_sent, small_got = take(7)
    seq, b, section = lax.axis_index("seq"), lax.axis_index("blk"), lax.axis_index("section")
    at_first = section == 0
    at_second = jnp.logical_not(at_first)
    core, side, other = {"seq": seq ^ 1}, {"seq": seq ^ 2}, {"section": 1 - section}
    greet((other, core, side) + tuple({"blk": lax.rem(b + k, count)} for k in range(1, count)))
    rows, lanes = attn.shape[2], gate.shape[1] // (4 * count)
    turns = tuple(range(count // 2, 0, -1)) + tuple(range(count // 2 + 1, count)) + (0,)
    f32, low = jnp.float32, jnp.bfloat16

    def piece_rows(kind, j):
        if kind == 0:
            return (slice(None), pl.ds(pl.multiple_of(j * rows, rows), rows))
        return (pl.ds(pl.multiple_of(j * rows, rows), rows),)

    pairs = {
        0: (attn_own, attn_in, ones[0]),
        1: (wide_own, wide_in, None),
        2: (out_own, out_in, ones[1]),
        3: (down_own, down_in, None),
    }
    sources = {
        0: (ones[0], twos[0], None, attn_from_one),
        1: (ones[2], twos[2], wide_from_two, wide_from_one),
        2: (ones[1], twos[1], None, out_from_one),
        3: (ones[3], twos[3], down_from_two, down_from_one),
    }

    def load(kind):
        one, two, from_two, from_one = sources[kind]
        own, held, _ = pairs[kind]

        def copies(begins):
            for n, (begin, end) in enumerate(zip(begins, (own, held))):
                if begin is not None:
                    pltpu.make_async_copy(begin, end, load_done.at[kind, n]).start()

        pl.when(at_first)(functools.partial(copies, (one, from_two)))
        pl.when(at_second)(functools.partial(copies, (two, from_one)))

    def loaded(kind):
        own, held, crossing = pairs[kind]
        pltpu.make_async_copy(own, own, load_done.at[kind, 0]).wait()
        copy = pltpu.make_async_copy(held, held, load_done.at[kind, 1])
        if crossing is None:
            copy.wait()
        else:
            pl.when(at_second)(copy.wait)

    def cross(kind, k):
        _, held, begin = pairs[kind]
        index = piece_rows(kind, lax.rem(b + k, count)) if kind < 2 else (slice(None),)
        return remote(
            begin.at[index], held.at[index], cross_sent.at[kind, k], cross_got.at[kind, k], other
        )

    def add_up(kind, k):
        own, held, crossing = pairs[kind]
        if crossing is not None:
            pl.when(at_first)(cross(kind, k).wait_recv)
        index = piece_rows(kind, lax.rem(b + k, count)) if kind < 2 else (slice(None),)
        held[index] = (own[index].astype(f32) + held[index].astype(f32)).astype(low)

    def along_line(kind, k):
        j = lax.rem(b + k, count)
        slot = (attn_slot if kind == 0 else wide_slot).at[k]
        source = pairs[kind][1].at[piece_rows(kind, j)]
        return remote(source, slot, line_sent.at[kind, k], line_got.at[kind, k], {"blk": j})

    def places(kind, k, of_seq):
        if kind == 2:
            size = out_in.shape[0]
            return [out.at[pl.ds(pl.multiple_of(of_seq * size, size), size)]]
        if kind == 3:
            size = down_in.shape[0]
            return [down.at[pl.ds(pl.multiple_of(of_seq * size, size), size)]]
        head = lax.rem(b + count - k, count) * 4 + of_seq
        if kind == 0:
            return [attn.at[head]]
        column = pl.ds(pl.multiple_of(head * lanes, lanes), lanes)
        return [gate.at[:, column], up.at[:, column]]

    def numbered(kind, k, of_seq):
        base = {0: k, 1: count + 2 * k, 2: 3 * count, 3: 3 * count + 1}[kind]
        return [(base + n, spot) for n, spot in enumerate(places(kind, k, of_seq))]

    def made(kind, k):
        if kind > 1:
            return [pairs[kind][1].at[:]]
        if kind == 0:
            return [attn_in.at[piece_rows(0, b)] if k == 0 else attn_slot.at[k]]
        whole = (lambda cut: wide_in.at[piece_rows(1, b) + (cut,)]) if k == 0 else (
            lambda cut: wide_slot.at[k, :, cut]
        )
        return [whole(pl.ds(0, lanes)), whole(pl.ds(lanes, lanes))]

    def sends(kind, k):
        found = []
        for (n, spot), begin in zip(numbered(kind, k, seq), made(kind, k)):
            found.append(
                (
                    remote(begin, spot, side_sent.at[n], side_got.at[n], side),
                    remote(begin, spot, core_sent.at[0, n], core_got.at[0, n], core),
                    pltpu.make_async_copy(begin, spot, local_done.at[n]),
                )
            )
        return found

    def publish(kind, k):
        for copies in sends(kind, k):
            for copy in copies:
                copy.start()

    def passes(kind, k):
        return [
            remote(spot, spot, core_sent.at[1, n], core_got.at[1, n], core)
            for n, spot in numbered(kind, k, seq ^ 2)
        ]

    def from_line(kind, k):
        along_line(kind, k).wait_recv()
        publish(kind, k)

    def from_side(kind, k):
        for n, spot in numbered(kind, k, seq ^ 2):
            settled(spot, side_got.at[n], True)
        for copy in passes(kind, k):
            copy.start()

    def small(n, source, slot, device):
        return remote(source, slot, small_sent.at[n], small_got.at[n], device)

    swap = small(0, swap_rows.at[:], swapped_rows.at[:], other)
    swap.start()
    gain_cross = small(1, gains.at[1 - section], gain_in.at[:], other)
    gain_cross.start()
    for kind in (1, 3, 2, 0):
        load(kind)
    crossings = [(2, 0)] + [(0, k) for k in turns]
    for kind, k in crossings:
        pl.when(at_second)(cross(kind, k).start)

    def gain_piece(j):
        return gain_sum.at[:, pl.ds(pl.multiple_of(j * rows, rows), rows)]

    def gain_send(k):
        j = lax.rem(b + k, count)
        return small(3 + k, gain_piece(j), gain_line.at[k], {"blk": j})

    gain_cross.wait_recv()
    gain_sum[...] = gains[section] + gain_in[...]
    for k in range(1, count):
        gain_send(k).start()

    loaded(1)
    for k in turns[:-1]:
        add_up(1, k)
        along_line(1, k).start()
    loaded(3)
    add_up(3, 0)
    publish(3, 0)
    add_up(1, 0)
    publish(1, 0)
    for k in range(1, count):
        gain_send(k).wait_recv()
    gain_part[...] = gain_sum[:, pl.ds(pl.multiple_of(b * rows, rows), rows)]
    for k in range(1, count):
        gain_part[...] += gain_line[k]
    gain_to_side = small(2, gain_part.at[:], gain_side.at[:], side)
    gain_to_side.start()
    loaded(2)
    add_up(2, 0)
    publish(2, 0)
    from_side(3, 0)
    from_line(1, turns[0])
    gain_to_side.wait_recv()
    gain_side[...] += gain_part[...]
    gain_to_core = small(3, gain_side.at[:], gain_core.at[:], core)
    gain_to_core.start()
    loaded(0)
    add_up(0, turns[0])
    along_line(0, turns[0]).start()
    from_side(1, 0)
    from_line(1, turns[1])
    add_up(0, turns[1])
    along_line(0, turns[1]).start()
    from_side(2, 0)
    from_line(1, turns[2])
    add_up(0, turns[2])
    along_line(0, turns[2]).start()
    add_up(0, 0)
    publish(0, 0)
    from_side(1, turns[0])
    gain_to_core.wait_recv()
    gains_out[...] = gain_side[...] + gain_core[...]
    from_line(0, turns[0])
    from_side(1, turns[1])
    from_line(0, turns[1])
    from_line(0, turns[2])
    from_side(1, turns[2])
    from_side(0, 0)
    for k in turns[:-1]:
        from_side(0, k)
    every = [(0, k) for k in range(count)] + [(1, k) for k in range(count)] + [(2, 0), (3, 0)]
    for kind, k in every:
        if (kind, k) in crossings:
            pl.when(at_second)(cross(kind, k).wait_send)
        if kind < 2 and k:
            along_line(kind, k).wait_send()
        for to_side, to_core, local in sends(kind, k):
            to_side.wait_send()
            to_core.wait_send()
            local.wait()
        for copy in passes(kind, k):
            copy.wait_send()
        for half, of_seq in ((0, seq ^ 1), (1, seq ^ 3)):
            for n, spot in numbered(kind, k, of_seq):
                settled(spot, core_got.at[half, n], True)
    swap.wait()
    gain_cross.wait_send()
    for k in range(1, count):
        gain_send(k).wait_send()
    gain_to_side.wait_send()
    gain_to_core.wait_send()


def finish_grads(first, second, from_two, from_one, gains, swap_rows):
    seq_count, count = lax.axis_size("seq"), lax.axis_size("blk")
    low, f32 = jnp.bfloat16, jnp.float32
    attn, out, wide, down = first
    rows = wide.shape[0] // count
    lanes = wide.shape[1] // 2
    parts = seq_count * count
    dma = pltpu.SemaphoreType.DMA
    vmem = pltpu.VMEM
    sends = 3 * count + 2
    heads = attn.shape[0]
    operands = list(first) + list(second) + list(from_two) + list(from_one) + [gains, swap_rows]
    in_vmem = pl.BlockSpec(memory_space=vmem)
    anywhere = pl.BlockSpec(memory_space=pl.ANY)
    small = (gains.shape[1], rows)
    attn, out, gate, up, down, gains, swapped_rows = pl.pallas_call(
        functools.partial(finish_kernel, count),
        out_shape=[
            jax.ShapeDtypeStruct((parts, heads, rows), low),
            jax.ShapeDtypeStruct((out.shape[0] * seq_count, out.shape[1]), low),
            jax.ShapeDtypeStruct((rows, lanes * parts), low),
            jax.ShapeDtypeStruct((rows, lanes * parts), low),
            jax.ShapeDtypeStruct((down.shape[0] * seq_count, down.shape[1]), low),
            jax.ShapeDtypeStruct(small, f32),
            jax.ShapeDtypeStruct(swap_rows.shape, low),
        ],
        in_specs=[anywhere] * (len(operands) - 2) + [in_vmem] * 2,
        out_specs=[anywhere] * 5 + [in_vmem, in_vmem],
        scratch_shapes=[
            vmem(attn.shape, low),
            vmem(out.shape, low),
            vmem(wide.shape, low),
            vmem(down.shape, low),
            vmem(attn.shape, low),
            vmem(out.shape, low),
            vmem(wide.shape, low),
            vmem(down.shape, low),
            vmem((count, heads, rows), low),
            vmem((count, rows, 2 * lanes), low),
            vmem(gains.shape[1:], f32),
            vmem(gains.shape[1:], f32),
            vmem((count,) + small, f32),
            vmem(small, f32),
            vmem(small, f32),
            vmem(small, f32),
            dma((4, 2)),
            dma((4, count)),
            dma((4, count)),
            dma((2, count)),
            dma((2, count)),
            dma((sends,)),
            dma((sends,)),
            dma((2, sends)),
            dma((2, sends)),
            dma((sends,)),
            dma((4 + count,)),
            dma((4 + count,)),
        ],
        compiler_params=pltpu.CompilerParams(
            collective_id=3, has_side_effects=True, vmem_limit_bytes=48 * 2**20
        ),
        name="finish_grads",
    )(*operands)
    attn = attn.astype(f32)

    def heads_back(start, copies):
        part = attn[:, start : start + HEAD_DIM].reshape(-1, copies, HEAD_DIM, rows).sum(1)
        return part.reshape(-1, rows).T

    copies = HEADS // KV_HEADS
    return (
        swapped_rows,
        gains,
        heads_back(0, 1),
        heads_back(HEAD_DIM, copies),
        heads_back(2 * HEAD_DIM, copies),
        out.astype(f32),
        gate.astype(f32),
        up.astype(f32),
        down.astype(f32),
    )


def call_kernel(kernel, name, number, operands, outputs, scratch):
    in_vmem = pl.BlockSpec(memory_space=pltpu.VMEM)
    anywhere = pl.BlockSpec(memory_space=pl.ANY)
    return pl.pallas_call(
        kernel,
        out_shape=[jax.ShapeDtypeStruct(shape, dtype) for shape, dtype, _ in outputs],
        in_specs=[in_vmem if near else anywhere for _, near in operands],
        out_specs=[in_vmem if near else anywhere for _, _, near in outputs],
        scratch_shapes=scratch,
        compiler_params=pltpu.CompilerParams(
            collective_id=number, has_side_effects=True, vmem_limit_bytes=56 * 2**20
        ),
        name=name,
    )(*[array for array, _ in operands])


def sliced_heads(local_shards):
    seq_index, seq_count = lax.axis_index("seq"), lax.axis_size("seq")
    count = lax.axis_size("blk")
    gain_attn, w_query, w_key, w_value, _, gain_mlp, _, _, _ = local_shards
    rows = w_query.shape[0]

    def heads_of(weight, per_blk, place):
        head = jnp.arange(count)[:, None] * per_blk + place
        column = (head * HEAD_DIM + jnp.arange(HEAD_DIM)).reshape(-1)
        chosen = jnp.arange(weight.shape[1])[:, None] == column[None, :]
        taken = lax.dot_general(
            chosen.astype(jnp.bfloat16),
            weight,
            (((0,), (1,)), ((), ())),
            preferred_element_type=jnp.float32,
        )
        return taken.astype(jnp.bfloat16).reshape(count, HEAD_DIM, rows)

    kv_per_blk = KV_HEADS // count
    kv_place = seq_index * kv_per_blk // seq_count
    gains = jnp.concatenate(
        [jnp.stack([gain_attn, gain_mlp]), jnp.zeros((14, rows), jnp.bfloat16)]
    )
    return jnp.concatenate(
        [
            heads_of(w_query, seq_count, seq_index),
            heads_of(w_key, kv_per_blk, kv_place),
            heads_of(w_value, kv_per_blk, kv_place),
            jnp.broadcast_to(gains[None], (count,) + gains.shape),
        ],
        axis=1,
    )


def head_shards(inputs, cotangent, doc_lengths, *params):
    section = lax.axis_index("section")
    at_first = section == 0
    seq_count, count = lax.axis_size("seq"), lax.axis_size("blk")
    low, f32 = jnp.bfloat16, jnp.float32
    vmem, dma = pltpu.VMEM, pltpu.SemaphoreType.DMA
    block, width = inputs.shape[2], inputs.shape[3]
    blocks = seq_count * count
    tokens = blocks * block
    rows_own = lax.dynamic_index_in_dim(inputs, section, 0, keepdims=False)[0]
    grads_own = lax.dynamic_index_in_dim(cotangent, section, 0, keepdims=False)[0]
    local = tuple(weight[0] for weight in params)
    pieces = sliced_heads(local)
    w_output, w_gate, w_up, w_down = local[4], local[6], local[7], local[8]
    rows = w_gate.shape[0]
    lanes = w_gate.shape[1] // blocks
    out_rows, down_rows = w_output.shape[0] // seq_count, w_down.shape[0] // seq_count
    lengths = lax.dynamic_index_in_dim(doc_lengths, section, 0, keepdims=False)[0]
    token_index = jnp.arange(tokens, dtype=jnp.int32)
    _, position = doc_info(lengths, token_index)
    start = (token_index - position)[:, None]
    half_dim = HEAD_DIM // 2
    frequency = THETA ** (-2.0 * jnp.arange(half_dim, dtype=f32) / HEAD_DIM)
    angles = position.astype(f32)[:, None] * frequency
    cosine, sine = jnp.cos(angles), jnp.sin(angles)
    empty = jnp.zeros((tokens, PAD - HEAD_DIM), f32)
    cosine = jnp.concatenate([cosine, cosine, empty], axis=1)
    sine = jnp.concatenate([-sine, sine, empty], axis=1)

    def all_blocks():
        return vmem((blocks, block, width), low)

    def scatter():
        return scatter_scratch(count, block, width)

    own_low, own_wide = ((block, width), low, True), ((block, width), f32, True)
    every = ((blocks, block, width), low, False)
    gain_rows = ((8, width), f32, True)
    attn_outputs = [
        own_wide,
        own_low,
        every,
        ((4, tokens, PAD), low, True),
        ((tokens, 1), f32, True),
    ]
    weights_vm = [vmem((3 * PAD + 16, width), low), vmem((PAD, width), low)]
    wide_vm, down_vm = vmem((width, 2 * lanes), low), vmem((down_rows, width), low)
    tables = [(cosine, True), (sine, True), (start, True)]
    (
        attn,
        gate_up,
        out,
        down,
        grads_all,
        rows_one,
        wide_rows_one,
        hidden_one,
        between,
        normed,
        heads_one,
        total_one,
    ) = call_kernel(
        functools.partial(first_layer_kernel, count),
        "first_layer",
        2,
        [(array, False) for array in (pieces, w_gate, w_up, w_output, w_down)]
        + [(rows_own, True), (grads_own, True)]
        + tables,
        [
            ((2, pieces.shape[1], width), low, False),
            ((2, width, 2 * lanes), low, False),
            ((2, out_rows, width), low, False),
            ((2, down_rows, width), low, False),
            every,
            every,
            every,
            own_wide,
            own_low,
            own_low,
            ((4, tokens, PAD), low, True),
            ((tokens, 1), f32, True),
        ],
        [all_blocks() for _ in range(6)]
        + weights_vm
        + [wide_vm, down_vm, vmem((tokens, lanes), low), vmem((block, width), low)]
        + [vmem((16, width), low), dma((6,)), dma((3,))]
        + [dma((3, count)), dma((3, count)), dma((5, count)), dma((5, count)), dma((5,))]
        + gather_semaphores(count) * 3
        + scatter()
        + scatter(),
    )
    gains = attn[:, 3 * HEAD_DIM : 3 * HEAD_DIM + 2].astype(f32)
    hidden_two, normed, rows_two, heads_two, total_two = call_kernel(
        functools.partial(attn_kernel, count),
        "second_attention",
        4,
        [(normed, True), (between, True), (attn, False), (out, False)] + tables,
        attn_outputs,
        [all_blocks()]
        + weights_vm
        + [all_blocks(), dma((5,)), dma((2,))]
        + gather_semaphores(count)
        + scatter(),
    )
    wide_outputs = [((width, 2 * lanes), low, True), ((down_rows, width), low, True)]
    final, branch, grad_hidden, gain_mlp_two, wide_two, down_two = call_kernel(
        functools.partial(mlp_both_kernel, count),
        "second_feed_forward",
        6,
        [
            (normed, True),
            (hidden_two, True),
            (gate_up, False),
            (down, False),
            (grads_all, False),
            (grads_own, True),
            (gains[1, 1:2], True),
        ],
        [own_low, own_low, own_wide, gain_rows] + wide_outputs,
        [all_blocks(), all_blocks(), wide_vm, down_vm]
        + [vmem((tokens, lanes), low), vmem((tokens, 2 * lanes), low)]
        + [all_blocks(), all_blocks(), dma((3,))]
        + gather_semaphores(count)
        + scatter()
        + scatter(),
    )

    wide_carried = ((width, 2 * lanes), low, False), ((down_rows, width), low, False)
    attn_carried = ((3 * HEAD_DIM, width), low, False), ((HEAD_DIM, width), low, False)

    def attention_back(layer, branch, grad_hidden, x_own, rows_all, heads, log_total, carries):
        return call_kernel(
            functools.partial(attn_back_kernel, count, layer),
            ("first", "second")[layer] + "_attention_back",
            7 + layer,
            [(branch, True), (grad_hidden, True), (x_own, True)]
            + [(rows_all, False), (heads, False), (log_total, True), (attn, False), (out, False)]
            + tables
            + [(gains[layer, 0:1], True)]
            + [(array, False) for array in carries],
            [
                own_low,
                gain_rows,
                ((3 * HEAD_DIM, width), low, True),
                ((HEAD_DIM, width), low, True),
                *wide_carried,
            ],
            [all_blocks(), all_blocks(), vmem((4, tokens, PAD), low)]
            + weights_vm
            + [vmem((tokens, PAD), low), vmem((tokens, tokens), f32)]
            + [vmem((tokens, PAD), f32), vmem((tokens, PAD), f32), vmem((tokens, 3 * PAD), low)]
            + [all_blocks(), dma((7,)), dma((2,)), dma((2,))]
            + gather_semaphores(count)
            + scatter(),
        )

    grad_between, gain_attn_two, attn_two, out_two, *wide_held_two = attention_back(
        1,
        branch,
        grad_hidden,
        between,
        rows_two,
        heads_two,
        total_two,
        (wide_two, down_two),
    )
    branch, grad_hidden, gain_mlp_one, wide_one, down_one, *attn_held_two = call_kernel(
        functools.partial(mlp_back_kernel, count),
        "first_feed_forward_back",
        9,
        [
            (grad_between, True),
            (hidden_one, True),
            (wide_rows_one, False),
            (gate_up, False),
            (down, False),
            (gains[0, 1:2], True),
            (attn_two, False),
            (out_two, False),
        ],
        [own_low, own_wide, gain_rows] + wide_outputs + list(attn_carried),
        [all_blocks(), all_blocks(), wide_vm, down_vm]
        + [vmem((tokens, lanes), low), vmem((tokens, 2 * lanes), f32)]
        + [vmem((tokens, 2 * lanes), low), all_blocks(), dma((3,)), dma((2,)), dma((2,))]
        + gather_semaphores(count)
        + scatter(),
    )
    grad_start, gain_attn_one, attn_one, out_one, *wide_held_one = attention_back(
        0,
        branch,
        grad_hidden,
        rows_own,
        rows_one,
        heads_one,
        total_one,
        (wide_one, down_one),
    )
    kept = jnp.where(
        at_first, jnp.stack([between, grad_start]), jnp.stack([final, grad_between])
    )
    sent = jnp.where(
        at_first, jnp.stack([final, grad_between]), jnp.stack([between, grad_start])
    )
    gain_sums = jnp.stack(
        [
            jnp.concatenate([gain_attn_one[0:4], gain_mlp_one[0:4]]),
            jnp.concatenate([gain_attn_two[0:4], gain_mlp_two[0:4]]),
        ]
    )
    swapped_rows, gain_sums, query, key, value, out, gate, up, down = finish_grads(
        (attn_one, out_one, wide_one, down_one),
        (attn_two, out_two, wide_two, down_two),
        wide_held_one,
        wide_held_two + attn_held_two,
        gain_sums,
        sent,
    )
    pairs = jnp.where(
        at_first, jnp.stack([kept, swapped_rows], axis=1), jnp.stack([swapped_rows, kept], axis=1)
    )
    return (
        pairs[0][None, :, None],
        pairs[1][None, :, None],
        gain_sums[0][None],
        query[None],
        key[None],
        value[None],
        out[None],
        gain_sums[4][None],
        gate[None],
        up[None],
        down[None],
    )

def solution(mesh):
    placed = (
        P(None, None, ("seq", "blk"), None),
        P(None, None, ("seq", "blk"), None),
        P(),
        P("section", "blk"),
        P("section", "blk", None),
        P("section", "blk", None),
        P("section", "blk", None),
        P("section", "blk", None),
        P("section", "blk"),
        P("section", "blk", None),
        P("section", "blk", None),
        P("section", "blk", None),
    )
    one_head_each = mesh.shape["seq"] == 4 and mesh.shape["blk"] == HEADS // 4
    return jax.shard_map(
        head_shards if one_head_each else shards,
        mesh=mesh,
        in_specs=placed,
        out_specs=(
            P("section", None, None, ("seq", "blk"), None),
            P("section", None, None, ("seq", "blk"), None),
            P("section", "blk"),
            P("section", "blk", None),
            P("section", "blk", None),
            P("section", "blk", None),
            P("section", "blk", None),
            P("section", "blk"),
            P("section", "blk", None),
            P("section", "blk", None),
            P("section", "blk", None),
        ),
        check_vma=False,
    )
```

```python
import functools

import jax
import jax.numpy as jnp
from jax import lax
from jax.experimental import pallas as pl
from jax.experimental.pallas import tpu as pltpu
from jax.sharding import PartitionSpec as P

HEADS = 16
KV_HEADS = 8
HEAD_DIM = 96


EPS = 1e-05
THETA = 100000.0
MASKED = -1e30


def passed_along(value, axis, steps):
    count = lax.axis_size(axis)
    first, last = (max(0, -steps), min(count, count - steps))
    return lax.ppermute(value, axis, [(source, source + steps) for source in range(first, last)])


def shortened(value):
    return jax.tree.map(lambda a: a.astype(jnp.bfloat16) if a.dtype == jnp.float32 else a, value)


def product(left_side, right_side):
    return jnp.dot(left_side, right_side, preferred_element_type=jnp.float32)


def back_product(left_side, right_side):
    return lax.dot_general(
        left_side, right_side, (((1,), (1,)), ((), ())), preferred_element_type=jnp.float32
    )


def doc_info(lengths, token_index):
    doc_ends = jnp.cumsum(lengths, axis=-1)
    passed = (doc_ends[..., None, :] <= token_index[..., None]).astype(jnp.int32)
    segment = jnp.sum(passed, axis=-1)
    offset = jnp.sum(passed * lengths[..., None, :], axis=-1)
    return (segment, token_index - offset)


def rotate(field_in, position, turn_sign):
    half_dim = field_in.shape[-1] // 2
    frequency = THETA ** (-2.0 * jnp.arange(half_dim, dtype=jnp.float32) / field_in.shape[-1])
    angles = position.astype(jnp.float32)[:, None] * frequency
    cosine = jnp.cos(angles)[:, None, :]
    sine_part = turn_sign * jnp.sin(angles)[:, None, :]
    first_half = field_in[..., :half_dim]
    second_half = field_in[..., half_dim:]
    return jnp.concatenate(
        [
            first_half * cosine - second_half * sine_part,
            second_half * cosine + first_half * sine_part,
        ],
        axis=-1,
    )


def rms_forward(field_in, gain_row):
    inv_root = lax.rsqrt(jnp.mean(field_in * field_in, axis=-1, keepdims=True) + EPS)
    return (field_in * inv_root * gain_row, inv_root)


def rms_backward(field_in, gain_row, inv_root, grad_normed):
    scaled = gain_row * grad_normed
    grad_field = inv_root * scaled - field_in * inv_root**3 * jnp.mean(
        scaled * field_in, axis=-1, keepdims=True
    )
    return (grad_field, grad_normed * field_in * inv_root)


def token_place(block_id, row_ids, per_device, blk_count):
    return (row_ids // per_device * blk_count + block_id) * per_device + row_ids % per_device


def masks_for(lengths, blk_index, per_device, blk_count, seq_count):
    block_tokens = seq_count * per_device
    row_ids = jnp.arange(block_tokens, dtype=jnp.int32)
    query_index = token_place(blk_index, row_ids, per_device, blk_count)
    all_ids = jnp.arange(blk_count * block_tokens, dtype=jnp.int32)
    key_index = token_place(all_ids // block_tokens, all_ids % block_tokens, per_device, blk_count)
    query_seg, _ = doc_info(lengths, query_index)
    key_seg, _ = doc_info(lengths, key_index)
    return (query_index, key_index, query_seg, key_seg)


def head_scores(queries, key_rows, allowed, kv_local):
    grouped = queries.reshape(queries.shape[0], kv_local, -1, HEAD_DIM)
    key_heads = key_rows.reshape(key_rows.shape[0], kv_local, HEAD_DIM)
    scores = jnp.einsum(
        "rkgd,lkd->kgrl", grouped, key_heads, preferred_element_type=jnp.float32
    ) * HEAD_DIM ** (-0.5)
    return (jnp.where(allowed, scores, MASKED), grouped, key_heads)


def attend_forward(operands, query_index, key_index, kv_local):
    queries, key_rows, value_rows, query_seg, key_seg = operands
    allowed = (query_seg[:, None] == key_seg[None, :]) & (
        key_index[None, :] <= query_index[:, None]
    )
    scores, grouped, key_heads = head_scores(queries, key_rows, allowed, kv_local)
    row_top = jnp.max(scores, axis=-1, keepdims=True)
    log_total = row_top + jnp.log(jnp.sum(jnp.exp(scores - row_top), axis=-1, keepdims=True))
    weights_low = jnp.exp(scores - log_total).astype(jnp.bfloat16)
    value_heads = value_rows.reshape(value_rows.shape[0], kv_local, HEAD_DIM)
    mixed_heads = jnp.einsum(
        "kgrl,lkd->rkgd", weights_low, value_heads, preferred_element_type=jnp.float32
    )
    return (mixed_heads.reshape(queries.shape).astype(jnp.bfloat16), log_total)


def attend_backward(operands, query_index, key_index, kv_local):
    queries, key_rows, value_rows, grad_mixed, log_total, query_seg, key_seg = operands
    allowed = (query_seg[:, None] == key_seg[None, :]) & (
        key_index[None, :] <= query_index[:, None]
    )
    scores, grouped, key_heads = head_scores(queries, key_rows, allowed, kv_local)
    attn_probs = jnp.exp(scores - log_total)
    value_heads = value_rows.reshape(value_rows.shape[0], kv_local, HEAD_DIM)
    grad_heads = grad_mixed.reshape(grouped.shape)
    grad_values = jnp.einsum(
        "kgrl,rkgd->lkd",
        attn_probs.astype(jnp.bfloat16),
        grad_heads,
        preferred_element_type=jnp.float32,
    )
    grad_probs = jnp.einsum(
        "rkgd,lkd->kgrl", grad_heads, value_heads, preferred_element_type=jnp.float32
    )
    centre = jnp.sum(attn_probs * grad_probs, axis=-1, keepdims=True)
    grad_scores = (attn_probs * (grad_probs - centre)).astype(jnp.bfloat16)
    grad_queries = jnp.einsum(
        "kgrl,lkd->rkgd", grad_scores, key_heads, preferred_element_type=jnp.float32
    ) * HEAD_DIM ** (-0.5)
    grad_keys = jnp.einsum(
        "kgrl,rkgd->lkd", grad_scores, grouped, preferred_element_type=jnp.float32
    ) * HEAD_DIM ** (-0.5)
    return (
        grad_queries.reshape(queries.shape).astype(jnp.bfloat16),
        grad_keys.reshape(key_rows.shape),
        grad_values.reshape(value_rows.shape),
    )


def layer_forward(section_in, lengths, weights, placing):
    shard_id, blk_index, seq_count, blk_count = placing
    gain_attn, w_query, w_key, w_value, w_output, gain_mlp, w_gate, w_up, w_down = weights
    seqs_here, per_device, width = section_in.shape
    token_rows = seqs_here * per_device
    copies = max(1, seq_count // KV_HEADS)
    kv_local = KV_HEADS * copies // seq_count
    token_index = shard_id * per_device + jnp.arange(per_device, dtype=jnp.int32)
    _, position = doc_info(lengths, token_index)
    position = position.reshape(token_rows)
    flat_in = section_in.reshape(token_rows, width)
    normed, inv_first = rms_forward(flat_in, gain_attn.astype(jnp.float32))
    normed_low = normed.astype(jnp.bfloat16)
    query_pre = product(normed_low, w_query).reshape(token_rows, HEADS, HEAD_DIM)
    key_pre = product(normed_low, w_key).reshape(token_rows, KV_HEADS, HEAD_DIM)
    value_pre = product(normed_low, w_value).reshape(token_rows, KV_HEADS, HEAD_DIM)
    query_rot = (
        rotate(query_pre, position, 1.0).astype(jnp.bfloat16).reshape(seqs_here, per_device, width)
    )
    key_rot = rotate(key_pre, position, 1.0).astype(jnp.bfloat16)
    spread_shape = (token_rows, KV_HEADS, copies, HEAD_DIM)
    key_rep = jnp.broadcast_to(key_rot[:, :, None, :], spread_shape).reshape(
        seqs_here, per_device, -1
    )
    value_rep = jnp.broadcast_to(
        value_pre.astype(jnp.bfloat16)[:, :, None, :], spread_shape
    ).reshape(seqs_here, per_device, -1)
    heads_query, heads_key, heads_value = (
        lax.all_to_all(query_rot, "seq", split_axis=2, concat_axis=1, tiled=True),
        lax.all_to_all(key_rep, "seq", split_axis=2, concat_axis=1, tiled=True),
        lax.all_to_all(value_rep, "seq", split_axis=2, concat_axis=1, tiled=True),
    )
    keys_all, values_all = (
        lax.all_gather(heads_key, "blk", axis=1, tiled=True),
        lax.all_gather(heads_value, "blk", axis=1, tiled=True),
    )
    query_index, key_index, query_seg, key_seg = masks_for(
        lengths, blk_index, per_device, blk_count, seq_count
    )
    heads_mixed, log_total = lax.map(
        lambda operands: attend_forward(operands, query_index, key_index, kv_local),
        (heads_query, keys_all, values_all, query_seg, key_seg),
    )
    token_mixed = lax.all_to_all(
        heads_mixed, "seq", split_axis=1, concat_axis=2, tiled=True
    ).reshape(token_rows, width)
    hidden = flat_in + product(token_mixed, w_output)
    normed_mlp, inv_second = rms_forward(hidden, gain_mlp.astype(jnp.float32))
    normed_mlp_low = normed_mlp.astype(jnp.bfloat16)
    gate_pre = product(normed_mlp_low, w_gate)
    up_pre = product(normed_mlp_low, w_up)
    act_low = (jax.nn.silu(gate_pre) * up_pre).astype(jnp.bfloat16)
    result = hidden + product(act_low, w_down)
    saved_state = (
        flat_in,
        normed_low,
        inv_first,
        position,
        heads_query,
        keys_all,
        values_all,
        log_total,
        token_mixed,
        hidden,
        inv_second,
        normed_mlp_low,
        gate_pre,
        up_pre,
        act_low,
        lengths,
    )
    return (result.reshape(section_in.shape), saved_state)


def layer_backward(upstream, saved_state, weights, placing):
    shard_id, blk_index, seq_count, blk_count = placing
    gain_attn, w_query, w_key, w_value, w_output, gain_mlp, w_gate, w_up, w_down = weights
    (
        flat_in,
        normed_low,
        inv_first,
        position,
        heads_query,
        keys_all,
        values_all,
        log_total,
        token_mixed,
        hidden,
        inv_second,
        normed_mlp_low,
        gate_pre,
        up_pre,
        act_low,
        lengths,
    ) = saved_state
    seqs_here, per_device, width = upstream.shape
    token_rows = seqs_here * per_device
    copies = max(1, seq_count // KV_HEADS)
    kv_local = KV_HEADS * copies // seq_count
    grad_rows = upstream.reshape(token_rows, width)
    grad_out_low = grad_rows.astype(jnp.bfloat16)
    grad_act = back_product(grad_out_low, w_down)
    gate_sigmoid = jax.nn.sigmoid(gate_pre)
    grad_gate_low = (
        grad_act * up_pre * gate_sigmoid * (1.0 + gate_pre * (1.0 - gate_sigmoid))
    ).astype(jnp.bfloat16)
    grad_up_low = (grad_act * jax.nn.silu(gate_pre)).astype(jnp.bfloat16)
    grad_normed_mlp = back_product(grad_gate_low, w_gate) + back_product(grad_up_low, w_up)
    grad_hidden_part, gain_mlp_terms = rms_backward(
        hidden, gain_mlp.astype(jnp.float32), inv_second, grad_normed_mlp
    )
    grad_hidden = grad_rows + grad_hidden_part
    grad_branch_low = grad_hidden.astype(jnp.bfloat16)
    grad_mixed_low = (
        back_product(grad_branch_low, w_output)
        .astype(jnp.bfloat16)
        .reshape(seqs_here, per_device, width)
    )
    heads_grad = lax.all_to_all(grad_mixed_low, "seq", split_axis=2, concat_axis=1, tiled=True)
    query_index, key_index, query_seg, key_seg = masks_for(
        lengths, blk_index, per_device, blk_count, seq_count
    )
    grad_heads_query, grad_keys_all, grad_values_all = lax.map(
        lambda operands: attend_backward(operands, query_index, key_index, kv_local),
        (heads_query, keys_all, values_all, heads_grad, log_total, query_seg, key_seg),
    )
    grad_key_own, grad_value_own = (
        lax.psum_scatter(
            grad_keys_all.astype(jnp.bfloat16), "blk", scatter_dimension=1, tiled=True
        ).astype(jnp.float32),
        lax.psum_scatter(
            grad_values_all.astype(jnp.bfloat16), "blk", scatter_dimension=1, tiled=True
        ).astype(jnp.float32),
    )
    token_query, token_key, token_value = (
        lax.all_to_all(grad_heads_query, "seq", split_axis=1, concat_axis=2, tiled=True),
        lax.all_to_all(
            grad_key_own.astype(jnp.bfloat16), "seq", split_axis=1, concat_axis=2, tiled=True
        ),
        lax.all_to_all(
            grad_value_own.astype(jnp.bfloat16), "seq", split_axis=1, concat_axis=2, tiled=True
        ),
    )
    grad_key_sum = jnp.sum(
        token_key.astype(jnp.float32).reshape(token_rows, KV_HEADS, copies, HEAD_DIM), axis=2
    )
    grad_value_sum = jnp.sum(
        token_value.astype(jnp.float32).reshape(token_rows, KV_HEADS, copies, HEAD_DIM), axis=2
    )
    grad_query_low = (
        rotate(token_query.astype(jnp.float32).reshape(token_rows, HEADS, HEAD_DIM), position, -1.0)
        .astype(jnp.bfloat16)
        .reshape(token_rows, width)
    )
    grad_key_low = (
        rotate(grad_key_sum, position, -1.0)
        .astype(jnp.bfloat16)
        .reshape(token_rows, KV_HEADS * HEAD_DIM)
    )
    grad_value_low = grad_value_sum.astype(jnp.bfloat16).reshape(token_rows, KV_HEADS * HEAD_DIM)
    grad_normed = (
        back_product(grad_query_low, w_query)
        + back_product(grad_key_low, w_key)
        + back_product(grad_value_low, w_value)
    )
    grad_in_part, gain_attn_terms = rms_backward(
        flat_in, gain_attn.astype(jnp.float32), inv_first, grad_normed
    )
    grad_input = (grad_hidden + grad_in_part).reshape(upstream.shape)
    weight_rows = (
        gain_attn_terms,
        normed_low,
        grad_query_low,
        grad_key_low,
        grad_value_low,
        token_mixed,
        grad_branch_low,
        gain_mlp_terms,
        normed_mlp_low,
        grad_gate_low,
        grad_up_low,
        act_low,
        grad_out_low,
    )
    return (grad_input, weight_rows)


def weight_term(inputs_low, outputs_low):
    if outputs_low is None:
        return jnp.sum(inputs_low, axis=0)
    return lax.dot_general(
        inputs_low, outputs_low, (((0,), (0,)), ((), ())), preferred_element_type=jnp.float32
    )


def shards(
    inputs,
    cotangent,
    doc_lengths,
    attention_gain,
    w_query,
    w_key,
    w_value,
    w_output,
    mlp_gain,
    w_gate,
    w_up,
    w_down,
):
    at_first = lax.axis_index("section") == 0
    seq_count = lax.axis_size("seq")
    blk_count = lax.axis_size("blk")
    blk_index = lax.axis_index("blk")
    shard_id = lax.axis_index("seq") * blk_count + blk_index
    placing = (shard_id, blk_index, seq_count, blk_count)
    micro_count = inputs.shape[0]
    local_shards = (
        attention_gain[0],
        w_query[0],
        w_key[0],
        w_value[0],
        w_output[0],
        mlp_gain[0],
        w_gate[0],
        w_up[0],
        w_down[0],
    )
    weights = (
        lax.all_gather(local_shards[0], "blk", axis=0, tiled=True),
        lax.all_gather(local_shards[1], "blk", axis=0, tiled=True),
        lax.all_gather(local_shards[2], "blk", axis=0, tiled=True),
        lax.all_gather(local_shards[3], "blk", axis=0, tiled=True),
        lax.all_gather(local_shards[4], "blk", axis=0, tiled=True),
        lax.all_gather(local_shards[5], "blk", axis=0, tiled=True),
        lax.all_gather(local_shards[6], "blk", axis=0, tiled=True),
        lax.all_gather(local_shards[7], "blk", axis=0, tiled=True),
        lax.all_gather(local_shards[8], "blk", axis=0, tiled=True),
    )
    received = jnp.zeros(inputs.shape[1:], jnp.bfloat16)
    saved_states = []
    section_outs = []
    for tick_index in range(micro_count + 1):
        fresh_input = inputs[min(tick_index, micro_count - 1)]
        section_in = jnp.where(at_first, fresh_input, received).astype(jnp.float32)
        lengths = jnp.where(
            at_first,
            doc_lengths[min(tick_index, micro_count - 1)],
            doc_lengths[max(tick_index - 1, 0)],
        )
        result, saved_state = layer_forward(section_in, lengths, weights, placing)
        result_low = result.astype(jnp.bfloat16)
        if tick_index < micro_count:
            received = passed_along(result_low, "section", 1)
        saved_states.append(saved_state)
        section_outs.append(result_low)
    weights = (
        lax.all_gather(local_shards[0], "blk", axis=0, tiled=True),
        lax.all_gather(local_shards[1], "blk", axis=0, tiled=True),
        lax.all_gather(local_shards[2], "blk", axis=0, tiled=True),
        lax.all_gather(local_shards[3], "blk", axis=0, tiled=True),
        lax.all_gather(local_shards[4], "blk", axis=0, tiled=True),
        lax.all_gather(local_shards[5], "blk", axis=0, tiled=True),
        lax.all_gather(local_shards[6], "blk", axis=0, tiled=True),
        lax.all_gather(local_shards[7], "blk", axis=0, tiled=True),
        lax.all_gather(local_shards[8], "blk", axis=0, tiled=True),
    )
    back_in = jnp.zeros(cotangent.shape[1:], jnp.bfloat16)
    grad_outs = []
    row_sets = []
    for tick_index in range(micro_count + 1):
        saved_state = jax.tree.map(
            lambda first_pick, second_pick: jnp.where(at_first, first_pick, second_pick),
            saved_states[max(tick_index - 1, 0)],
            saved_states[min(tick_index + 1, micro_count)],
        )
        upstream = jnp.where(at_first, back_in, cotangent[min(tick_index, micro_count - 1)]).astype(
            jnp.float32
        )
        grad_input, weight_rows = layer_backward(upstream, saved_state, weights, placing)
        grad_low = grad_input.astype(jnp.bfloat16)
        if tick_index < micro_count:
            back_in = passed_along(grad_low, "section", -1)
        grad_outs.append(grad_low)
        row_sets.append(weight_rows)
    activations = jnp.stack(
        [
            jnp.where(at_first, section_outs[index_m], section_outs[index_m + 1])
            for index_m in range(micro_count)
        ]
    )[None]
    input_grads = jnp.stack(
        [
            jnp.where(at_first, grad_outs[index_m + 1], grad_outs[index_m])
            for index_m in range(micro_count)
        ]
    )[None]
    picked = [
        jax.tree.map(
            lambda first_pick, second_pick: jnp.where(at_first, first_pick, second_pick),
            row_sets[index_m + 1],
            row_sets[index_m],
        )
        for index_m in range(micro_count)
    ]
    merged = jax.tree.map(lambda *pieces: jnp.concatenate(pieces, axis=0), *picked)
    (
        gain_attn_terms,
        normed_low,
        grad_query_low,
        grad_key_low,
        grad_value_low,
        token_mixed,
        grad_branch_low,
        gain_mlp_terms,
        normed_mlp_low,
        grad_gate_low,
        grad_up_low,
        act_low,
        grad_out_low,
    ) = merged
    grad_pairs = (
        (gain_attn_terms, None),
        (normed_low, grad_query_low),
        (normed_low, grad_key_low),
        (normed_low, grad_value_low),
        (token_mixed, grad_branch_low),
        (gain_mlp_terms, None),
        (normed_mlp_low, grad_gate_low),
        (normed_mlp_low, grad_up_low),
        (act_low, grad_out_low),
    )
    shares = tuple(
        (
            lax.psum_scatter(
                weight_term(left_side, right_side).astype(jnp.bfloat16),
                "blk",
                scatter_dimension=0,
                tiled=True,
            ).astype(jnp.float32)
            for left_side, right_side in grad_pairs
        )
    )
    shares = jax.tree.map(lambda part: part.astype(jnp.float32), lax.psum(shortened(shares), "seq"))
    return (
        activations,
        input_grads,
        shares[0][None],
        shares[1][None],
        shares[2][None],
        shares[3][None],
        shares[4][None],
        shares[5][None],
        shares[6][None],
        shares[7][None],
        shares[8][None],
    )


MESH = pl.DeviceIdType.MESH


def remote(source, target, sent, arrived, device):
    return pltpu.make_async_remote_copy(
        source, target, sent, arrived, device_id=device, device_id_type=MESH
    )


def greet(partners):
    barrier = pltpu.get_barrier_semaphore()
    for device in partners:
        pl.semaphore_signal(barrier, 1, device_id=device, device_id_type=MESH)
    pl.semaphore_wait(barrier, len(partners))


def settled(spot, semaphore, received):
    copy = remote(spot, spot, semaphore, semaphore, {"seq": lax.axis_index("seq") ^ 1})
    if received:
        copy.wait_recv()
    else:
        copy.wait_send()


CUTS = 2


def gather_steps(
    count, own, out, line_sent, line_got, side_sent, side_got, core_sent, core_got, local_done
):
    seq, b = lax.axis_index("seq"), lax.axis_index("blk")
    core, side = {"seq": seq ^ 1}, {"seq": seq ^ 2}
    base, side_base = seq * count, (seq ^ 2) * count
    cut = out.shape[1] // CUTS

    def spot(index, h):
        return out.at[index, pl.ds(h * cut, cut)]

    def begin(index, h, first):
        return own.at[pl.ds(h * cut, cut)] if first else spot(index, h)

    def along_line(j, way, h, first=False):
        device = {"blk": b + (1 if way else -1)}
        return remote(
            begin(base + j, h, first),
            spot(base + j, h),
            line_sent.at[j, way, h],
            line_got.at[j, h],
            device,
        )

    def to_side(j, h, first=False):
        return remote(
            begin(base + j, h, first),
            spot(base + j, h),
            side_sent.at[j, h],
            side_got.at[j, h],
            side,
        )

    def to_core(half, j, h, first=False):
        index = (side_base if half else base) + j
        return remote(
            begin(index, h, first),
            spot(index, h),
            core_sent.at[half, j, h],
            core_got.at[half, j, h],
            core,
        )

    local = pltpu.make_async_copy(own, out.at[base + b], local_done)
    local.start()
    for h in range(CUTS):
        to_side(b, h, True).start()
        pl.when(b > 0)(along_line(b, 0, h, True).start)
        pl.when(b < count - 1)(along_line(b, 1, h, True).start)
    for h in range(CUTS):
        to_core(0, b, h, True).start()
    yield "sent"

    def from_line(j, way):
        for h in range(CUTS):
            settled(spot(base + j, h), line_got.at[j, h], True)
            pl.when((b < count - 1) if way else (b > 0))(along_line(j, way, h).start)
            to_side(j, h).start()
        for h in range(CUTS):
            to_core(0, j, h).start()

    def from_side(j):
        for h in range(CUTS):
            settled(spot(side_base + j, h), side_got.at[j, h], True)
            to_core(1, j, h).start()

    for k in range(1, count + 1):
        if k < count:
            pl.when(b - k >= 0)(functools.partial(from_line, b - k, 1))
            pl.when(b + k < count)(functools.partial(from_line, b + k, 0))
        if k == 1:
            from_side(b)
        else:
            pl.when(b - k + 1 >= 0)(functools.partial(from_side, b - k + 1))
            pl.when(b + k - 1 < count)(functools.partial(from_side, b + k - 1))
        if k == count - 1:
            local.wait()
        yield "line" if k == count - 1 else "side" if k == count else "step"
    for half, corner in ((0, seq ^ 1), (1, seq ^ 3)):
        for j in range(count):
            for h in range(CUTS):
                settled(spot(corner * count + j, h), core_got.at[half, j, h], True)
        yield "corner" if half else "near"
    for h in range(CUTS):
        for j in range(count):
            to_side(j, h).wait_send()
            to_core(0, j, h).wait_send()
            to_core(1, j, h).wait_send()
        pl.when(b > 0)(along_line(b, 0, h).wait_send)
        pl.when(b < count - 1)(along_line(b, 1, h).wait_send)
        for k in range(1, count):
            pl.when((b - k >= 0) & (b < count - 1))(along_line(b - k, 1, h).wait_send)
            pl.when((b + k < count) & (b > 0))(along_line(b + k, 0, h).wait_send)


def gather_semaphores(count):
    dma = pltpu.SemaphoreType.DMA
    return [
        dma((count, 2, CUTS)),
        dma((count, CUTS)),
        dma((count, CUTS)),
        dma((count, CUTS)),
        dma((2, count, CUTS)),
        dma((2, count, CUTS)),
        dma,
    ]


def line_steps(count, own, out, line_sent, line_got, core_sent, core_got, local_done):
    seq, b = lax.axis_index("seq"), lax.axis_index("blk")
    core, base = {"seq": seq ^ 1}, (seq % 2) * count
    cut = out.shape[1] // CUTS

    def spot(j, h):
        return out.at[base + j, pl.ds(h * cut, cut)]

    def begin(j, h, first):
        return own.at[pl.ds(h * cut, cut)] if first else spot(j, h)

    def along_line(j, way, h, first=False):
        device = {"blk": b + (1 if way else -1)}
        return remote(
            begin(j, h, first), spot(j, h), line_sent.at[j, way, h], line_got.at[j, h], device
        )

    def to_core(j, h, first=False):
        return remote(begin(j, h, first), spot(j, h), core_sent.at[j, h], core_got.at[j, h], core)

    local = pltpu.make_async_copy(own, out.at[base + b], local_done)
    local.start()
    for h in range(CUTS):
        pl.when(b > 0)(along_line(b, 0, h, True).start)
        pl.when(b < count - 1)(along_line(b, 1, h, True).start)
        to_core(b, h, True).start()
    yield

    def from_line(j, way):
        for h in range(CUTS):
            settled(spot(j, h), line_got.at[j, h], True)
            pl.when((b < count - 1) if way else (b > 0))(along_line(j, way, h).start)
            to_core(j, h).start()

    for k in range(1, count):
        pl.when(b - k >= 0)(functools.partial(from_line, b - k, 1))
        pl.when(b + k < count)(functools.partial(from_line, b + k, 0))
        yield
    local.wait()
    for h in range(CUTS):
        for j in range(count):
            settled(out.at[(1 - seq % 2) * count + j, pl.ds(h * cut, cut)], core_got.at[j, h], True)
            to_core(j, h).wait_send()
        pl.when(b > 0)(along_line(b, 0, h).wait_send)
        pl.when(b < count - 1)(along_line(b, 1, h).wait_send)
        for k in range(1, count):
            pl.when((b - k >= 0) & (b < count - 1))(along_line(b - k, 1, h).wait_send)
            pl.when((b + k < count) & (b > 0))(along_line(b + k, 0, h).wait_send)


def line_semaphores(count):
    dma = pltpu.SemaphoreType.DMA
    return [
        dma((count, 2, CUTS)),
        dma((count, CUTS)),
        dma((count, CUTS)),
        dma((count, CUTS)),
        dma,
    ]


def advance(steps, times):
    for _ in range(times):
        next(steps, None)


def group_of(event):
    seq = lax.axis_index("seq")
    return {"line": seq, "side": seq ^ 2, "near": seq ^ 1, "corner": seq ^ 3}.get(event)


def scatter_steps(
    count,
    partial,
    deliver,
    core_slot,
    side_slot,
    line_slot,
    side_out,
    line_out,
    running,
    core_sent,
    core_got,
    side_sent,
    side_got,
    line_sent,
    line_got,
    compute=None,
):
    seq, b = lax.axis_index("seq"), lax.axis_index("blk")
    core, side = {"seq": seq ^ 1}, {"seq": seq ^ 2}
    place = far_first(b, count)
    size = partial.shape[1] // CUTS
    cuts = [pl.ds(h * size, size) for h in range(CUTS)]

    def to_core(half, k, h):
        return remote(
            partial.at[(seq ^ (1 if half else 3)) * count + place[k], cuts[h]],
            core_slot.at[half, k, cuts[h]],
            core_sent.at[half, k, h],
            core_got.at[half, k, h],
            core,
        )

    def to_side(k, h):
        return remote(
            side_out.at[k, cuts[h]],
            side_slot.at[k, cuts[h]],
            side_sent.at[k, h],
            side_got.at[k, h],
            side,
        )

    def along_line(k, way, h):
        j = place[k]
        return remote(
            line_out.at[k, cuts[h]],
            line_slot.at[way, j, cuts[h]],
            line_sent.at[k, h],
            line_got.at[way, j, h],
            {"blk": b + (1 if way else -1)},
        )

    def add_from(way, j, h):
        settled(line_slot.at[way, j, cuts[h]], line_got.at[way, j, h], True)
        running[cuts[h]] += line_slot[way, j, cuts[h]].astype(jnp.float32)

    def exchange(half):
        if compute:
            compute(seq ^ (1 if half else 3))
        for k in range(count):
            for h in range(CUTS):
                to_core(half, k, h).start()

    exchange(0)
    if compute:
        compute(seq ^ 2)
    for k in range(count):
        for h in range(CUTS):
            to_core(0, k, h).wait_recv()
            total = partial[(seq ^ 2) * count + place[k], cuts[h]].astype(jnp.float32)
            total += core_slot[0, k, cuts[h]].astype(jnp.float32)
            side_out[k, cuts[h]] = total.astype(jnp.bfloat16)
            to_side(k, h).start()
    exchange(1)
    if compute:
        compute(seq)
    yield
    for k in range(count):
        j = place[k]
        rightward, leftward = j >= b, j <= b
        for h in range(CUTS):
            to_core(1, k, h).wait_recv()
            to_side(k, h).wait_recv()
            total = partial[seq * count + j, cuts[h]].astype(jnp.float32)
            total += core_slot[1, k, cuts[h]].astype(jnp.float32)
            running[cuts[h]] = total + side_slot[k, cuts[h]].astype(jnp.float32)
            pl.when(rightward & (b > 0))(functools.partial(add_from, 1, j, h))
            pl.when(leftward & (b < count - 1))(functools.partial(add_from, 0, j, h))
            if k < count - 1:
                line_out[k, cuts[h]] = running[cuts[h]].astype(jnp.bfloat16)
                pl.when(rightward)(along_line(k, 1, h).start)
                pl.when(jnp.logical_not(rightward))(along_line(k, 0, h).start)
        if k < count - 1:
            yield
    deliver(running[...])
    yield
    for k in range(count):
        for h in range(CUTS):
            to_core(0, k, h).wait_send()
            to_core(1, k, h).wait_send()
            to_side(k, h).wait_send()
            if k < count - 1:
                settled(line_out.at[k, cuts[h]], line_sent.at[k, h], False)


def line_first_steps(
    count,
    partial,
    deliver,
    own,
    core_slot,
    line_slot,
    line_out,
    side_slot,
    running,
    own_done,
    core_sent,
    core_got,
    line_sent,
    line_got,
    side_sent,
    side_got,
):
    seq, b = lax.axis_index("seq"), lax.axis_index("blk")
    core, side = {"seq": seq ^ 1}, {"seq": seq ^ 2}
    place = far_first(b, count)

    def to_core(half, k):
        source = partial.at[(seq ^ (1 if half else 3)) * count + place[k]]
        return remote(
            source, core_slot.at[half, k], core_sent.at[half, k], core_got.at[half, k], core
        )

    def kept(half, k):
        source = partial.at[(seq if half else seq ^ 2) * count + place[k]]
        return pltpu.make_async_copy(source, own.at[half, k], own_done.at[half, k])

    def along_line(half, k, way):
        j = place[k]
        return remote(
            line_out.at[half, k],
            line_slot.at[half, way, j],
            line_sent.at[half, k],
            line_got.at[half, way, j],
            {"blk": b + (1 if way else -1)},
        )

    def add_from(half, way, j):
        settled(line_slot.at[half, way, j], line_got.at[half, way, j], True)
        running[...] += line_slot[half, way, j].astype(jnp.float32)

    to_side = remote(line_out.at[0, count - 1], side_slot.at[0], side_sent, side_got, side)
    for half in range(2):
        for k in range(count):
            kept(half, k).start()
            to_core(half, k).start()
    yield
    for k in range(count):
        j = place[k]
        rightward, leftward = j >= b, j <= b
        for half in range(2):
            kept(half, k).wait()
            to_core(half, k).wait_recv()
            running[...] = own[half, k].astype(jnp.float32) + core_slot[half, k].astype(jnp.float32)
            pl.when(rightward & (b > 0))(functools.partial(add_from, half, 1, j))
            pl.when(leftward & (b < count - 1))(functools.partial(add_from, half, 0, j))
            if half == 0 or k < count - 1:
                line_out[half, k] = running[...].astype(jnp.bfloat16)
            if k < count - 1:
                pl.when(rightward)(along_line(half, k, 1).start)
                pl.when(jnp.logical_not(rightward))(along_line(half, k, 0).start)
            elif half == 0:
                to_side.start()
            else:
                to_side.wait_recv()
                deliver(running[...] + side_slot[0].astype(jnp.float32))
            yield
    to_side.wait_send()
    for half in range(2):
        for k in range(count):
            to_core(half, k).wait_send()
            if k < count - 1:
                settled(line_out.at[half, k], line_sent.at[half, k], False)


def far_first(b, count):
    order = sorted(range(count), key=lambda j: -j)
    places = []
    for k in range(count):
        place = 0
        for own in range(count):
            by_distance = sorted(order, key=lambda j: (-abs(j - own), -j if own * 2 < count else j))
            place = jnp.where(b == own, by_distance[k], place)
        places.append(place)
    return places


def scatter_scratch(count, rows, width):
    dma = pltpu.SemaphoreType.DMA

    def slots(*places):
        return pltpu.VMEM(places + (rows, width), jnp.bfloat16)

    return [
        slots(2, count),
        slots(count),
        slots(2, count),
        slots(count),
        slots(count - 1),
        pltpu.VMEM((rows, width), jnp.float32),
        dma((2, count, CUTS)),
        dma((2, count, CUTS)),
        dma((count, CUTS)),
        dma((count, CUTS)),
        dma((count - 1, CUTS)),
        dma((2, count, CUTS)),
    ]


def run_all(fillers):
    for filler in fillers:
        filler()


def run_with(steps, fillers):
    fillers = list(fillers)
    for _ in steps:
        if fillers:
            fillers.pop(0)()
    for filler in fillers:
        filler()


def greet_group(count, more=()):
    seq, b = lax.axis_index("seq"), lax.axis_index("blk")
    greet(
        tuple(more)
        + ({"seq": seq ^ 1}, {"seq": seq ^ 2})
        + tuple({"blk": lax.rem(b + k, count)} for k in range(1, count))
    )


def carry(copies, from_section, what):
    sending = lax.axis_index("section") == from_section
    for copy in copies:
        if what == "start":
            pl.when(sending)(copy.start)
        else:
            pl.when(sending)(copy.wait_send)
            pl.when(jnp.logical_not(sending))(copy.wait_recv)


def carried(sources, targets, sent, got):
    other = {"section": 1 - lax.axis_index("section")}
    return [
        remote(source, target, sent.at[n], got.at[n], other)
        for n, (source, target) in enumerate(zip(sources, targets))
    ]


def group_rows(ref, group, count):
    value = ref[pl.ds(group * count, count)]
    return value.reshape(value.shape[0] * value.shape[1], value.shape[2])


def group_span(group, count, block):
    size = count * block
    return pl.ds(pl.multiple_of(group * size, size), size)


def lane_turn(field_in, cosine, sine):
    half_dim, lanes = HEAD_DIM // 2, field_in.shape[-1]
    lane = lax.broadcasted_iota(jnp.int32, field_in.shape, 1)
    partner = jnp.where(
        lane < half_dim,
        pltpu.roll(field_in, lanes - half_dim, 1),
        pltpu.roll(field_in, half_dim, 1),
    )
    return field_in * cosine + partner * sine


def masked_scores(query, key, first_row, start):
    scores = back_product(query, key) * HEAD_DIM ** (-0.5)
    key_index = lax.broadcasted_iota(jnp.int32, scores.shape, 1)
    query_index = first_row + lax.broadcasted_iota(jnp.int32, scores.shape, 0)
    return jnp.where((key_index >= start) & (key_index <= query_index), scores, MASKED)


def normalise(field_in, gain_row):
    inv_root = lax.rsqrt(jnp.mean(field_in * field_in, axis=-1, keepdims=True) + EPS)
    return field_in * inv_root * gain_row


PAD = 128


GAINS = HEAD_DIM
OWN_PART = HEAD_DIM + 16


def load_weights(layer, attn, twin, out, attn_vm, out_vm, sems):
    on_key = lax.axis_index("seq") % 2 == 0
    own, other = attn.at[layer, pl.ds(OWN_PART, HEAD_DIM)], twin.at[layer]

    def part(source, n, rows):
        return pltpu.make_async_copy(source, attn_vm.at[pl.ds(n * PAD, rows)], sems.at[n])

    copies = [
        part(attn.at[layer, pl.ds(0, HEAD_DIM)], 0, HEAD_DIM),
        part(attn.at[layer, pl.ds(GAINS, 16)], 3, 16),
    ]
    if out is not None:
        copies.append(
            pltpu.make_async_copy(out.at[layer], out_vm.at[pl.ds(0, HEAD_DIM)], sems.at[4])
        )
    start_all(copies)

    @pl.when(on_key)
    def _():
        part(own, 1, HEAD_DIM).start()
        part(other, 2, HEAD_DIM).start()

    @pl.when(jnp.logical_not(on_key))
    def _():
        part(other, 1, HEAD_DIM).start()
        part(own, 2, HEAD_DIM).start()

    return copies + [part(other, 1, HEAD_DIM), part(other, 2, HEAD_DIM)]


def clear_pads(attn_vm, out_vm):
    empty = jnp.zeros((PAD - HEAD_DIM, attn_vm.shape[1]), jnp.bfloat16)
    for part in range(3):
        attn_vm[part * PAD + HEAD_DIM : (part + 1) * PAD] = empty
    out_vm[HEAD_DIM:PAD] = empty


def attention_rows(heads, log_total, start, size, tokens):
    for i in range(tokens // size):
        here, seen = slice(i * size, (i + 1) * size), slice(0, (i + 1) * size)
        scores = masked_scores(heads[0, here], heads[1, seen], i * size, start[here])
        row_top = jnp.max(scores, axis=-1, keepdims=True)
        weights = jnp.exp(scores - row_top)
        total = jnp.sum(weights, axis=-1, keepdims=True)
        log_total[here] = row_top + jnp.log(total)
        weights = (weights * (1.0 / total)).astype(jnp.bfloat16)
        heads[3, here] = product(weights, heads[2, seen]).astype(jnp.bfloat16)


def project_heads(normed, attn_vm, heads, span, cosine, sine):
    mixed = back_product(normed, attn_vm[0 : 3 * PAD])
    cos_rows, sin_rows = cosine[span], sine[span]
    heads[0, span] = lane_turn(mixed[:, :PAD], cos_rows, sin_rows).astype(jnp.bfloat16)
    heads[1, span] = lane_turn(mixed[:, PAD : 2 * PAD], cos_rows, sin_rows).astype(jnp.bfloat16)
    heads[2, span] = mixed[:, 2 * PAD :].astype(jnp.bfloat16)


def keep_group(partial, group, value, count):
    block = partial.shape[1]
    partial[pl.ds(group * count, count)] = value.astype(jnp.bfloat16).reshape(count, block, -1)


def gain_of(ref, row):
    return ref[3 * PAD : 3 * PAD + 16][row : row + 1].astype(jnp.float32)


def attn_kernel(count, *refs):
    refs = iter(refs)

    def take(n):
        return [next(refs) for _ in range(n)]

    rows_in, x_own, grads_in, attn, twin, out, cosine, sine, start = take(9)
    hidden_out, normed_out, all_rows, heads, log_total, grads_all = take(6)
    rows_vm, attn_vm, out_vm, partial, grads_vm, load_done, save_done = take(7)
    gather_sems, grads_sems = take(7), take(5)
    scatter_refs = list(refs)
    block = rows_vm.shape[1]
    tokens = block * rows_vm.shape[0]
    size = count * block
    greet_group(count)
    steps = gather_steps(count, rows_in, rows_vm, *gather_sems)
    next(steps)
    clear_pads(attn_vm, out_vm)
    loads = load_weights(1, attn, twin, out, attn_vm, out_vm, load_done)
    for event in steps:
        if event == "line":
            wait_all(loads)
        group = group_of(event)
        if group is not None:
            span = group_span(group, count, block)
            normed = group_rows(rows_vm, group, count)
            project_heads(normed, attn_vm, heads, span, cosine, sine)
    grad_steps = line_steps(count, grads_in, grads_vm, *grads_sems)
    next(grad_steps)
    save = pltpu.make_async_copy(rows_vm, all_rows, save_done.at[0])
    save.start()
    attention_rows(heads, log_total, start, size, tokens)

    def project_out(group):
        mixed = heads[3, group_span(group, count, block)]
        keep_group(partial, group, product(mixed, out_vm[...]), count)

    def deliver(total):
        hidden = x_own[...].astype(jnp.float32) + total
        hidden_out[...] = hidden
        normed_out[...] = normalise(hidden, gain_of(attn_vm, 1)).astype(jnp.bfloat16)

    run_with(
        scatter_steps(count, partial, deliver, *scatter_refs, compute=project_out),
        [functools.partial(advance, grad_steps, 1)] * 3,
    )
    for _ in grad_steps:
        pass
    keep = pltpu.make_async_copy(grads_vm, grads_all, save_done.at[1])
    keep.start()
    keep.wait()
    save.wait()


def first_layer_kernel(count, *refs):
    refs = iter(refs)

    def take(n):
        return [next(refs) for _ in range(n)]

    pieces, w_gate, w_up, w_output, w_down, rows_in, grads_in, cosine, sine, start = take(10)
    attn, twin, gate_up, out, down, all_rows, wide_rows, grads_near, grads_side = take(9)
    hidden, result_out, normed_out, heads, log_total = take(5)
    raw_vm, normed_vm, rows_vm, partial, partial_two, grads_vm = take(6)
    attn_vm, out_vm, wide_vm, down_vm, units, normed_own, gain_vm = take(7)
    load_done, save_done, twin_sent, twin_got = take(4)
    spread_sems = take(5)
    first_sems, second_sems, grads_sems, side_sems = take(7), take(7), take(5), take(2)
    scatter_one, scatter_two = take(12), take(12)
    section = lax.axis_index("section")
    block, width = raw_vm.shape[1], raw_vm.shape[2]
    tokens = block * raw_vm.shape[0]
    size = count * block
    low, f32 = jnp.bfloat16, jnp.float32
    greet_group(count, ({"section": 1 - section},))
    spread = spread_steps(
        count, pieces, w_gate, w_up, w_output, w_down, attn, gate_up, out, down, *spread_sems
    )
    steps = gather_steps(count, rows_in, raw_vm, *first_sems)
    next(steps)
    next(spread)
    clear_pads(attn_vm, out_vm)
    for event in steps:
        if event == "line":
            advance(spread, 3)
    grads_across = remote(
        grads_in, grads_side, *side_sems, {"seq": lax.axis_index("seq") ^ 2}
    )
    grads_across.start()
    next(spread)
    pair = remote(
        attn.at[:, pl.ds(OWN_PART, HEAD_DIM)],
        twin,
        twin_sent,
        twin_got,
        {"seq": lax.axis_index("seq") ^ 1},
    )
    pair.start()
    pair.wait()
    gain_load = pltpu.make_async_copy(attn.at[1, pl.ds(GAINS, 16)], gain_vm, load_done.at[5])
    gain_load.start()
    wait_all(load_weights(0, attn, twin, None, attn_vm, out_vm, load_done) + [gain_load])
    for group in range(tokens // size):
        raw = raw_vm[group * count : (group + 1) * count].astype(f32)
        normed = normalise(raw, gain_of(attn_vm, 0)[None]).astype(low)
        normed_vm[group * count : (group + 1) * count] = normed
        span = slice(group * size, (group + 1) * size)
        project_heads(normed.reshape(size, width), attn_vm, heads, span, cosine, sine)
    saves = [pltpu.make_async_copy(normed_vm, all_rows, save_done.at[0])]
    saves[0].start()
    attention_rows(heads, log_total, start, size, tokens)
    next(spread)
    load = pltpu.make_async_copy(out.at[0], out_vm.at[pl.ds(0, HEAD_DIM)], load_done.at[4])
    load.start()
    load.wait()

    def project_out(group):
        mixed = heads[3, group_span(group, count, block)]
        keep_group(partial, group, product(mixed, out_vm[...]), count)

    def deliver(total):
        value = rows_in[...].astype(f32) + total
        hidden[...] = value
        normed_own[...] = normalise(value, gain_of(attn_vm, 1)).astype(low)

    def more():
        next(spread)

    run_with(scatter_steps(count, partial, deliver, *scatter_one, compute=project_out), [more] * 5)
    for number, event in enumerate(gather_steps(count, normed_own, rows_vm, *second_sems)):
        if number == 0:
            more()
    for _ in spread:
        pass
    loads = [
        pltpu.make_async_copy(gate_up.at[0], wide_vm, load_done.at[0]),
        pltpu.make_async_copy(down.at[0], down_vm, load_done.at[1]),
    ]
    start_all(loads)
    wait_all(loads)
    saves.append(pltpu.make_async_copy(rows_vm, wide_rows, save_done.at[1]))
    saves[1].start()

    def project_down(group):
        pre = product(group_rows(rows_vm, group, count), wide_vm[...])
        made = hidden_units(pre)
        units[group_span(group, count, block)] = made
        keep_group(partial_two, group, product(made, down_vm[...]), count)

    grad_steps = line_steps(count, grads_in, grads_vm, *grads_sems)
    next(grad_steps)

    def deliver_two(total):
        made = (hidden[...] + total).astype(low)
        result_out[...] = made
        gain = gain_vm[...][0:1].astype(f32)
        normed_out[...] = normalise(made.astype(f32), gain).astype(low)

    run_with(
        scatter_steps(count, partial_two, deliver_two, *scatter_two, compute=project_down),
        [functools.partial(advance, grad_steps, 1)] * 3,
    )
    for _ in grad_steps:
        pass
    saves.append(pltpu.make_async_copy(grads_vm, grads_near, save_done.at[2]))
    saves[2].start()
    grads_across.wait()
    wait_all(saves)


def spread_steps(
    count,
    pieces,
    w_gate,
    w_up,
    w_output,
    w_down,
    attn,
    gate_up,
    out,
    down,
    line_sent,
    line_got,
    cross_sent,
    cross_got,
    local_done,
):
    seq, b, section = lax.axis_index("seq"), lax.axis_index("blk"), lax.axis_index("section")
    seq_count = lax.axis_size("seq")
    other = {"section": 1 - section}
    rows, lanes = w_gate.shape[0], gate_up.shape[2] // 2
    turns = tuple(range(count // 2, 0, -1)) + tuple(range(count // 2 + 1, count))

    def source(kind, j):
        if kind == 0:
            return pieces.at[j]
        weight = w_gate if kind == 1 else w_up
        return weight.at[:, pl.ds(pl.multiple_of((j * seq_count + seq) * lanes, lanes), lanes)]

    def target(kind, j):
        if kind == 0:
            return attn.at[section, :, pl.ds(pl.multiple_of(j * rows, rows), rows)]
        return gate_up.at[
            section, pl.ds(pl.multiple_of(j * rows, rows), rows), pl.ds((kind - 1) * lanes, lanes)
        ]

    def along_line(kind, k):
        j = lax.rem(b + k, count)
        return remote(
            source(kind, j),
            target(kind, b),
            line_sent.at[kind, k],
            line_got.at[kind, k],
            {"blk": j},
        )

    def across(kind, j, slot, begin=None):
        spot = target(kind, j)
        return remote(
            spot if begin is None else begin,
            spot,
            cross_sent.at[kind, slot],
            cross_got.at[kind, slot],
            other,
        )

    def own_rows(kind):
        weight, place = (w_output, out) if kind == 3 else (w_down, down)
        size = place.shape[1]
        begin = weight.at[pl.ds(pl.multiple_of(seq * size, size), size)]
        spot = place.at[section]
        return (
            remote(begin, spot, cross_sent.at[kind, 0], cross_got.at[kind, 0], other),
            pltpu.make_async_copy(begin, spot, local_done.at[kind]),
        )

    def own_piece(kind):
        return (
            across(kind, b, 0, source(kind, b)),
            pltpu.make_async_copy(source(kind, b), target(kind, b), local_done.at[kind]),
        )

    def forward(kind, k):
        j = lax.rem(b + count - k, count)
        settled(target(kind, j), line_got.at[kind, k], True)
        across(kind, j, k).start()

    def arrived(kind):
        if kind > 2:
            wait_all(own_rows(kind))
            return
        for k in range(count):
            settled(target(kind, 0), cross_got.at[kind, k], True)
            settled(target(kind, 0), cross_sent.at[kind, k], False)
            if k:
                settled(target(kind, 0), line_sent.at[kind, k], False)
        pltpu.make_async_copy(source(kind, b), target(kind, b), local_done.at[kind]).wait()

    for k in turns:
        along_line(0, k).start()
    start_all(own_piece(0))
    yield
    for k in turns:
        forward(0, k)
        yield
    start_all(own_rows(3))
    for kind in (1, 2):
        for k in turns:
            along_line(kind, k).start()
    arrived(0)
    start_all(own_piece(1) + own_piece(2) + own_rows(4))
    yield
    arrived(3)
    yield
    for kind in (1, 2):
        for k in turns:
            forward(kind, k)
            yield
    for kind in (1, 2, 4):
        arrived(kind)


def start_all(copies):
    for copy in copies:
        copy.start()


def wait_all(copies):
    for copy in copies:
        copy.wait()


def gated(pre):
    half = pre.shape[1] // 2
    gate, up = pre[:, :half], pre[:, half:]
    sigma = jax.nn.sigmoid(gate)
    return gate, up, sigma


def hidden_units(pre):
    gate, up, sigma = gated(pre)
    return (gate * sigma * up).astype(jnp.bfloat16)


def store_gate_grads(place, span, grad_act, pre):
    gate, up, sigma = gated(pre)
    half = gate.shape[1]
    place[span, 0:half] = (grad_act * up * sigma * (1.0 + gate * (1.0 - sigma))).astype(
        jnp.bfloat16
    )
    place[span, half : 2 * half] = (grad_act * (gate * sigma)).astype(jnp.bfloat16)


def wide_grads(rows_vm, pre_grads, units, grads_vm, wide_grad, down_grad):
    tokens = pre_grads.shape[0]
    width = rows_vm.shape[2]
    step = width // 4

    def wide_part(n):
        cut = slice(n * step, (n + 1) * step)
        rows = rows_vm[:, :, cut].reshape(tokens, step)
        wide_grad[cut] = weight_term(rows, pre_grads[...]).astype(jnp.bfloat16)

    def down_part(n):
        cut = slice(n * 2 * step, (n + 1) * 2 * step)
        rows = grads_vm[:, :, cut].reshape(tokens, 2 * step)
        down_grad[:, cut] = weight_term(units[...], rows).astype(jnp.bfloat16)

    return [functools.partial(wide_part, n) for n in range(4)] + [
        functools.partial(down_part, n) for n in range(2)
    ]


def mlp_grad_sent(total, hidden, grads_own, gain, branch_out, grad_hidden_out, gain_out):
    field_in = hidden[...]
    inv_root = lax.rsqrt(jnp.mean(field_in * field_in, axis=-1, keepdims=True) + EPS)
    part, terms = rms_backward(field_in, gain[...], inv_root, total)
    grad_hidden = grads_own[...].astype(jnp.float32) + part
    grad_hidden_out[...] = grad_hidden
    branch_out[...] = grad_hidden.astype(jnp.bfloat16)
    gain_out[...] = jnp.broadcast_to(jnp.sum(terms, axis=0, keepdims=True), gain_out.shape)


def mlp_both_kernel(count, *refs):
    refs = iter(refs)

    def take(n):
        return [next(refs) for _ in range(n)]

    rows_in, hidden, gate_up, down, grads_near, grads_far, grads_own, gain = take(8)
    ahead_out, branch_out, grad_hidden_out, gain_out, wide_grad, down_grad = take(6)
    rows_vm, grads_vm, wide_vm, down_vm, units, pre_grads, partial, partial_back = take(8)
    (load_done,) = take(1)
    size = count * rows_vm.shape[1]
    half = rows_vm.shape[0] // 2
    near = lax.axis_index("seq") // 2 * half
    gather_sems = take(7)
    scatter_back = list(refs)
    block = rows_vm.shape[1]
    greet_group(count)
    steps = gather_steps(count, rows_in, rows_vm, *gather_sems)
    next(steps)
    loads = [
        pltpu.make_async_copy(gate_up.at[1], wide_vm, load_done.at[0]),
        pltpu.make_async_copy(down.at[1], down_vm, load_done.at[1]),
        pltpu.make_async_copy(grads_near, grads_vm.at[pl.ds(near, half)], load_done.at[2]),
        pltpu.make_async_copy(grads_far, grads_vm.at[pl.ds(half - near, half)], load_done.at[4]),
    ]
    start_all(loads)

    def through(group):
        span = group_span(group, count, block)
        pre = product(group_rows(rows_vm, group, count), wide_vm[...])
        units[span] = hidden_units(pre)
        grad_act = back_product(group_rows(grads_vm, group, count), down_vm[...])
        store_gate_grads(pre_grads, span, grad_act, pre)
        value = back_product(pre_grads[span], wide_vm[...])
        partial_back[pl.ds(group * count, count)] = value.astype(jnp.bfloat16).reshape(
            count, block, -1
        )

    for event in steps:
        if event == "line":
            wait_all(loads)
        group = group_of(event)
        if group is not None:
            through(group)

    def project_down(group):
        value = product(units[group * size : (group + 1) * size], down_vm[...])
        partial[group * count : (group + 1) * count] = value.astype(jnp.bfloat16).reshape(
            count, block, -1
        )

    def deliver_back(total):
        mlp_grad_sent(
            total, hidden, grads_own, gain, branch_out, grad_hidden_out, gain_out
        )

    fillers = wide_grads(rows_vm, pre_grads, units, grads_vm, wide_grad, down_grad)
    fillers += [functools.partial(project_down, group) for group in range(4)]
    run_with(
        scatter_steps(count, partial_back, deliver_back, *scatter_back),
        [functools.partial(run_all, fillers[n::4]) for n in range(4)],
    )
    save = pltpu.make_async_copy(partial, ahead_out, load_done.at[3])
    save.start()
    save.wait()


def mlp_back_kernel(count, *refs):
    refs = iter(refs)

    def take(n):
        return [next(refs) for _ in range(n)]

    grads_own, hidden, all_rows, gate_up, down, gain = take(6)
    carry_from = take(3)
    branch_out, grad_hidden_out, gain_out, wide_grad, down_grad = take(5)
    carry_to = take(3)
    rows_vm, grads_vm, wide_vm, down_vm, units, pre_vm, pre_grads, partial, load_done = take(9)
    carry_sent, carry_got = take(2)
    gather_sems = take(7)
    scatter_refs = list(refs)
    block = rows_vm.shape[1]
    greet_group(count, ({"section": 1 - lax.axis_index("section")},))
    steps = gather_steps(count, grads_own, grads_vm, *gather_sems)
    next(steps)
    copies = carried(carry_from, carry_to, carry_sent, carry_got)
    carry(copies, 0, "start")
    loads = [
        pltpu.make_async_copy(gate_up.at[0], wide_vm, load_done.at[0]),
        pltpu.make_async_copy(all_rows, rows_vm, load_done.at[1]),
        pltpu.make_async_copy(down.at[0], down_vm, load_done.at[2]),
    ]
    start_all(loads)

    def again(group):
        span = group_span(group, count, block)
        pre = product(group_rows(rows_vm, group, count), wide_vm[...])
        pre_vm[span] = pre
        units[span] = hidden_units(pre)

    def through(group):
        span = group_span(group, count, block)
        grad_act = back_product(group_rows(grads_vm, group, count), down_vm[...])
        store_gate_grads(pre_grads, span, grad_act, pre_vm[span])
        value = back_product(pre_grads[span], wide_vm[...])
        partial[pl.ds(group * count, count)] = value.astype(jnp.bfloat16).reshape(count, block, -1)

    wait_all(loads)
    for number, event in enumerate(steps):
        if number < 2:
            again(2 * number)
            again(2 * number + 1)
        group = group_of(event)
        if group is not None:
            through(group)

    def deliver(total):
        mlp_grad_sent(total, hidden, grads_own, gain, branch_out, grad_hidden_out, gain_out)

    run_with(
        scatter_steps(count, partial, deliver, *scatter_refs),
        wide_grads(rows_vm, pre_grads, units, grads_vm, wide_grad, down_grad),
    )
    carry(copies, 0, "wait")


class Parts:
    pass


def attn_back_refs(take, attn_grad=None, out_grad=None):
    r = Parts()
    r.branch_vm, r.rows_vm, r.heads, r.attn_vm, r.out_vm, r.mixed_grads, r.probs = take(7)
    r.key_grads, r.value_grads, r.joint, r.partial, r.load_done = take(5)
    r.gather_sems = take(7)
    r.scatter_refs = take(12)
    return r


def attn_back_body(count, layer, r, ins, outs, background, fillers, gathered=None):
    branch_in, grad_hidden, x_own, all_rows, heads_kept, log_total, attn, twin, out = ins[:9]
    cosine, sine, start, gain = ins[9:]
    grad_out, gain_out, attn_grad, out_grad = outs
    branch_vm, rows_vm, heads, attn_vm, out_vm = r.branch_vm, r.rows_vm, r.heads, r.attn_vm, r.out_vm
    mixed_grads, probs, key_grads, value_grads = r.mixed_grads, r.probs, r.key_grads, r.value_grads
    joint, partial, load_done = r.joint, r.partial, r.load_done
    block = rows_vm.shape[1]
    size = count * block
    tokens = block * rows_vm.shape[0]
    low, f32 = jnp.bfloat16, jnp.float32
    scale = HEAD_DIM ** (-0.5)
    steps = gather_steps(count, branch_in, branch_vm, *r.gather_sems)
    next(steps)
    background()
    clear_pads(attn_vm, out_vm)
    loads = load_weights(layer, attn, twin, out, attn_vm, out_vm, load_done)
    kept = [
        pltpu.make_async_copy(heads_kept, heads, load_done.at[5]),
        pltpu.make_async_copy(all_rows, rows_vm, load_done.at[6]),
    ]
    start_all(kept)
    key_grads[...] = jnp.zeros_like(key_grads)
    value_grads[...] = jnp.zeros_like(value_grads)
    wait_all(loads + kept)

    def spans(i):
        return slice(i * size, (i + 1) * size), slice(0, (i + 1) * size)

    def weigh(i):
        here, seen = spans(i)
        scores = masked_scores(heads[0, here], heads[1, seen], i * size, start[here])
        probs[here, seen] = jnp.exp(scores - log_total[here])

    def project(group):
        value = back_product(group_rows(branch_vm, group, count), out_vm[...])
        mixed_grads[group_span(group, count, block)] = value.astype(low)

    for number, event in enumerate(steps):
        if number < 2:
            weigh(2 * number)
            weigh(2 * number + 1)
        group = group_of(event)
        if group is not None:
            project(group)
    if gathered:
        gathered()
    for i in reversed(range(tokens // size)):
        here, seen = spans(i)
        weights = probs[here, seen]
        grads = mixed_grads[here]
        grad_weights = back_product(grads, heads[2, seen])
        centre = jnp.sum(weights * grad_weights, axis=-1, keepdims=True)
        grad_scores = (weights * (grad_weights - centre)).astype(low)
        query_grad = (product(grad_scores, heads[1, seen]) * scale).astype(low).astype(f32)
        joint[here, 0:PAD] = lane_turn(query_grad, cosine[here], -sine[here]).astype(low)
        key_grads[seen] += weight_term(grad_scores, heads[0, here])
        value_grads[seen] += weight_term(weights.astype(low), grads)
        key_grad = (key_grads[here] * scale).astype(low).astype(f32)
        joint[here, PAD : 2 * PAD] = lane_turn(key_grad, cosine[here], -sine[here]).astype(low)
        joint[here, 2 * PAD : 3 * PAD] = value_grads[here].astype(low)

    def project_back(group):
        value = product(joint[group_span(group, count, block)], attn_vm[0 : 3 * PAD])
        partial[pl.ds(group * count, count)] = value.astype(low).reshape(count, block, -1)

    def attn_part(part):
        rows = rows_vm[...].reshape(tokens, rows_vm.shape[2])
        value = weight_term(joint[:, part * PAD : (part + 1) * PAD], rows)
        attn_grad[part * HEAD_DIM : (part + 1) * HEAD_DIM] = value[0:HEAD_DIM].astype(low)

    def out_part():
        rows = branch_vm[...].reshape(tokens, branch_vm.shape[2])
        out_grad[...] = weight_term(heads[3], rows)[0:HEAD_DIM].astype(low)

    def deliver(total):
        field_in = x_own[...].astype(f32)
        inv_root = lax.rsqrt(jnp.mean(field_in * field_in, axis=-1, keepdims=True) + EPS)
        part, terms = rms_backward(field_in, gain[...], inv_root, total)
        grad_out[...] = (grad_hidden[...] + part).astype(low)
        gain_out[...] = jnp.broadcast_to(jnp.sum(terms, axis=0, keepdims=True), gain_out.shape)

    run_with(
        scatter_steps(count, partial, deliver, *r.scatter_refs, compute=project_back),
        [functools.partial(run_all, [functools.partial(attn_part, n) for n in range(3)] + [out_part])]
        + fillers,
    )


def attn_back_kernel(count, layer, *refs):
    refs = iter(refs)

    def take(n):
        return [next(refs) for _ in range(n)]

    ins, carry_from, outs, carry_to = take(13), take(1), take(4), take(1)
    r = attn_back_refs(take)
    carry_sent, carry_got = take(2)
    greet_group(count, ({"section": 1 - lax.axis_index("section")},))
    copies = carried(carry_from, carry_to, carry_sent, carry_got)

    def background():
        carry(copies, 1 - layer, "start")

    attn_back_body(count, layer, r, ins, outs, background, [])
    carry(copies, 1 - layer, "wait")


def last_kernel(count, *refs):
    refs = iter(refs)

    def take(n):
        return [next(refs) for _ in range(n)]

    ins = take(13)
    wide_one, down_one, attn_two, out_two, wide_two, down_two = take(6)
    wide_from_one, down_from_one, attn_from_one, out_from_one, ahead = take(5)
    gain_mlp_one, gain_attn_two, gain_mlp_two, between, grad_between, hidden = take(6)
    attn, out, gate, up, down, gains_out, swapped_rows, final, grad_start = take(9)
    attn_grad, out_grad, gain_attn_one, gains = take(4)
    attn_own, out_own, wide_own, down_own, attn_in, out_in, wide_in, down_in = take(8)
    attn_slot, wide_slot = take(2)
    gain_in, gain_sum, gain_line, gain_part, gain_side, gain_core = take(6)
    load_done, cross_sent, cross_got, line_sent, line_got = take(5)
    side_sent, side_got, core_sent, core_got, local_done, small_sent, small_got = take(7)
    ahead_refs = take(13)
    r = attn_back_refs(take)
    seq, b, section = lax.axis_index("seq"), lax.axis_index("blk"), lax.axis_index("section")
    at_first = section == 0
    at_second = jnp.logical_not(at_first)
    core, side, other = {"seq": seq ^ 1}, {"seq": seq ^ 2}, {"section": 1 - section}
    greet((other, core, side) + tuple({"blk": lax.rem(b + k, count)} for k in range(1, count)))
    rows, lanes = attn.shape[2], gate.shape[1] // (4 * count)
    turns = tuple(range(count // 2, 0, -1)) + tuple(range(count // 2 + 1, count)) + (0,)
    f32, low = jnp.float32, jnp.bfloat16

    def piece_rows(kind, j):
        if kind == 0:
            return (slice(None), pl.ds(pl.multiple_of(j * rows, rows), rows))
        return (pl.ds(pl.multiple_of(j * rows, rows), rows),)

    pairs = {
        0: (attn_own, attn_in, attn_grad),
        1: (wide_own, wide_in, wide_one),
        2: (out_own, out_in, out_grad),
        3: (down_own, down_in, down_one),
    }
    sources = {
        0: (attn_grad, attn_two, attn_from_one),
        1: (wide_one, wide_two, wide_from_one),
        2: (out_grad, out_two, out_from_one),
        3: (down_one, down_two, down_from_one),
    }

    def load(kind):
        one, two, from_one = sources[kind]
        own, held, _ = pairs[kind]

        @pl.when(at_first)
        def _():
            pltpu.make_async_copy(one, own, load_done.at[kind, 0]).start()

        @pl.when(at_second)
        def _():
            pltpu.make_async_copy(two, own, load_done.at[kind, 0]).start()
            pltpu.make_async_copy(from_one, held, load_done.at[kind, 1]).start()

    def loaded(kind):
        own, held, _ = pairs[kind]
        pltpu.make_async_copy(own, own, load_done.at[kind, 0]).wait()
        pl.when(at_second)(pltpu.make_async_copy(held, held, load_done.at[kind, 1]).wait)

    def cross(kind, k):
        _, held, begin = pairs[kind]
        index = piece_rows(kind, lax.rem(b + k, count)) if kind < 2 else (slice(None),)
        return remote(
            begin.at[index], held.at[index], cross_sent.at[kind, k], cross_got.at[kind, k], other
        )

    def add_up(kind, k):
        own, held, _ = pairs[kind]
        pl.when(at_first)(cross(kind, k).wait_recv)
        index = piece_rows(kind, lax.rem(b + k, count)) if kind < 2 else (slice(None),)
        held[index] = (own[index].astype(f32) + held[index].astype(f32)).astype(low)

    def along_line(kind, k):
        j = lax.rem(b + k, count)
        slot = (attn_slot if kind == 0 else wide_slot).at[k]
        source = pairs[kind][1].at[piece_rows(kind, j)]
        return remote(source, slot, line_sent.at[kind, k], line_got.at[kind, k], {"blk": j})

    def places(kind, k, of_seq):
        if kind == 2:
            size = out_in.shape[0]
            return [out.at[pl.ds(pl.multiple_of(of_seq * size, size), size)]]
        if kind == 3:
            size = down_in.shape[0]
            return [down.at[pl.ds(pl.multiple_of(of_seq * size, size), size)]]
        head = lax.rem(b + count - k, count) * 4 + of_seq
        if kind == 0:
            return [attn.at[head]]
        column = pl.ds(pl.multiple_of(head * lanes, lanes), lanes)
        return [gate.at[:, column], up.at[:, column]]

    def numbered(kind, k, of_seq):
        base = {0: k, 1: count + 2 * k, 2: 3 * count, 3: 3 * count + 1}[kind]
        return [(base + n, spot) for n, spot in enumerate(places(kind, k, of_seq))]

    def made(kind, k):
        if kind > 1:
            return [pairs[kind][1].at[:]]
        if kind == 0:
            return [attn_in.at[piece_rows(0, b)] if k == 0 else attn_slot.at[k]]
        whole = (lambda cut: wide_in.at[piece_rows(1, b) + (cut,)]) if k == 0 else (
            lambda cut: wide_slot.at[k, :, cut]
        )
        return [whole(pl.ds(0, lanes)), whole(pl.ds(lanes, lanes))]

    def sends(kind, k):
        found = []
        for (n, spot), begin in zip(numbered(kind, k, seq), made(kind, k)):
            found.append(
                (
                    remote(begin, spot, side_sent.at[n], side_got.at[n], side),
                    remote(begin, spot, core_sent.at[0, n], core_got.at[0, n], core),
                    pltpu.make_async_copy(begin, spot, local_done.at[n]),
                )
            )
        return found

    def publish(kind, k):
        for copies in sends(kind, k):
            for copy in copies:
                copy.start()

    def passes(kind, k):
        return [
            remote(spot, spot, core_sent.at[1, n], core_got.at[1, n], core)
            for n, spot in numbered(kind, k, seq ^ 2)
        ]

    def from_line(kind, k):
        along_line(kind, k).wait_recv()
        publish(kind, k)

    def from_side(kind, k):
        for n, spot in numbered(kind, k, seq ^ 2):
            settled(spot, side_got.at[n], True)
        for copy in passes(kind, k):
            copy.start()

    def small(n, source, slot, device):
        return remote(source, slot, small_sent.at[n], small_got.at[n], device)

    swap_rest = small(4 + count, between, swapped_rows.at[0], other)
    swap_final = small(4 + count, final, swapped_rows.at[0], other)
    swap_between = small(0, grad_between, swapped_rows.at[1], other)
    swap_start = small(0, grad_start, swapped_rows.at[1], other)
    pl.when(at_second)(swap_rest.start)
    pl.when(at_first)(swap_between.start)
    wide_turns = [(1, k) for k in turns]
    crossings = wide_turns + [(0, k) for k in turns] + [(2, 0), (3, 0)]

    def begin_cross(those):
        for kind, k in those:
            pl.when(at_second)(cross(kind, k).start)

    def background():
        begin_cross(crossings[:count])
        load(1)
        load(3)

    def deliver(total):
        final[...] = (hidden[...] + total).astype(low)
        pl.when(at_first)(swap_final.start)

    def later():
        load(0)
        load(2)
        begin_cross(crossings[count:])

    def share(n):
        if n == 0:
            loaded(1)
        add_up(1, turns[n])
        along_line(1, turns[n]).start()

    def gathered():
        share(0)
        share(1)

    ahead_steps = line_first_steps(count, ahead, deliver, *ahead_refs)
    attn_back_body(
        count,
        0,
        r,
        ins,
        (grad_start, gain_attn_one, attn_grad, out_grad),
        background,
        [later, functools.partial(share, 2)],
        gathered,
    )
    pl.when(at_second)(swap_start.start)
    gains[0, 0:4] = gain_attn_one[0:4]
    gains[0, 4:8] = gain_mlp_one[4:8]
    gains[1, 0:4] = gain_attn_two[0:4]
    gains[1, 4:8] = gain_mlp_two[4:8]
    gain_cross = small(1, gains.at[1 - section], gain_in.at[:], other)
    gain_cross.start()

    def gain_piece(j):
        return gain_sum.at[:, pl.ds(pl.multiple_of(j * rows, rows), rows)]

    def gain_send(k):
        j = lax.rem(b + k, count)
        return small(3 + k, gain_piece(j), gain_line.at[k], {"blk": j})

    add_up(1, 0)
    publish(1, 0)
    from_line(1, turns[0])
    from_line(1, turns[1])
    loaded(0)
    for k in turns[:-1]:
        add_up(0, k)
        along_line(0, k).start()
    add_up(0, 0)
    publish(0, 0)
    from_line(1, turns[2])
    from_side(1, 0)
    loaded(2)
    add_up(2, 0)
    publish(2, 0)
    from_side(1, turns[0])
    from_side(1, turns[1])
    for k in turns[:-1]:
        from_line(0, k)
    loaded(3)
    add_up(3, 0)
    publish(3, 0)
    next(ahead_steps)
    from_side(0, 0)
    from_side(1, turns[2])
    gain_cross.wait_recv()
    gain_sum[...] = gains[section] + gain_in[...]
    for k in range(1, count):
        gain_send(k).start()
    advance(ahead_steps, 2)
    from_side(2, 0)
    for k in range(1, count):
        gain_send(k).wait_recv()
    gain_part[...] = gain_sum[:, pl.ds(pl.multiple_of(b * rows, rows), rows)]
    for k in range(1, count):
        gain_part[...] += gain_line[k]
    gain_to_side = small(2, gain_part.at[:], gain_side.at[:], side)
    gain_to_side.start()
    advance(ahead_steps, 2)
    for k in turns[:-1]:
        from_side(0, k)
    advance(ahead_steps, 2)
    gain_to_side.wait_recv()
    gain_side[...] += gain_part[...]
    gain_to_core = small(3, gain_side.at[:], gain_core.at[:], core)
    gain_to_core.start()
    from_side(3, 0)
    for _ in ahead_steps:
        pass
    gain_to_core.wait_recv()
    gains_out[...] = gain_side[...] + gain_core[...]
    every = [(0, k) for k in range(count)] + [(1, k) for k in range(count)] + [(2, 0), (3, 0)]
    for kind, k in every:
        pl.when(at_second)(cross(kind, k).wait_send)
        if kind < 2 and k:
            along_line(kind, k).wait_send()
        for to_side, to_core, local in sends(kind, k):
            to_side.wait_send()
            to_core.wait_send()
            local.wait()
        for copy in passes(kind, k):
            copy.wait_send()
        for half, of_seq in ((0, seq ^ 1), (1, seq ^ 3)):
            for n, spot in numbered(kind, k, of_seq):
                settled(spot, core_got.at[half, n], True)
    swap_between.wait()
    swap_rest.wait()
    gain_cross.wait_send()
    for k in range(1, count):
        gain_send(k).wait_send()
    gain_to_side.wait_send()
    gain_to_core.wait_send()


def last_layer(count, operands, like, back_scratch):
    attn, out, wide, down, block, width, gain_rows = like
    low, f32 = jnp.bfloat16, jnp.float32
    seq_count = lax.axis_size("seq")
    rows = wide[0] // count
    lanes = wide[1] // 2
    parts = seq_count * count
    dma = pltpu.SemaphoreType.DMA
    vmem = pltpu.VMEM
    sends = 3 * count + 2
    heads = attn[0]
    small = (gain_rows, rows)

    def slots(*places):
        return vmem(places + (block, width), low)

    outputs = [
        ((parts, heads, rows), low, False),
        ((out[0] * seq_count, out[1]), low, False),
        ((rows, lanes * parts), low, False),
        ((rows, lanes * parts), low, False),
        ((down[0] * seq_count, down[1]), low, False),
        (small, f32, True),
        ((2, block, width), low, True),
        ((block, width), low, True),
        ((block, width), low, True),
    ]
    scratch = (
        [vmem(attn, low), vmem(out, low), vmem((gain_rows, width), f32)]
        + [vmem((2, gain_rows, width), f32)]
        + [vmem(shape, low) for shape in (attn, out, wide, down)] * 2
        + [vmem((count, heads, rows), low), vmem((count, rows, 2 * lanes), low)]
        + [vmem((gain_rows, width), f32)] * 2
        + [vmem((count,) + small, f32)]
        + [vmem(small, f32)] * 3
        + [dma((4, 2)), dma((4, count)), dma((4, count)), dma((2, count)), dma((2, count))]
        + [dma((sends,)), dma((sends,)), dma((2, sends)), dma((2, sends)), dma((sends,))]
        + [dma((5 + count,)), dma((5 + count,))]
        + [slots(2, count), slots(2, count), slots(2, 2, count), slots(2, count), slots(1)]
        + [vmem((block, width), f32)]
        + [dma((2, count)), dma((2, count)), dma((2, count)), dma((2, count))]
        + [dma((2, 2, count)), dma, dma]
        + back_scratch
    )
    attn, out, gate, up, down, gains, swapped_rows, final, grad_start = call_kernel(
        functools.partial(last_kernel, count), "last_layer_back", 3, operands, outputs, scratch
    )
    attn = attn.astype(f32)

    def heads_back(start, copies):
        part = attn[:, start : start + HEAD_DIM].reshape(-1, copies, HEAD_DIM, rows).sum(1)
        return part.reshape(-1, rows).T

    copies = HEADS // KV_HEADS
    return (
        swapped_rows,
        final,
        grad_start,
        gains,
        heads_back(0, 1),
        heads_back(HEAD_DIM, copies),
        heads_back(2 * HEAD_DIM, copies),
        out.astype(f32),
        gate.astype(f32),
        up.astype(f32),
        down.astype(f32),
    )


def call_kernel(kernel, name, number, operands, outputs, scratch):
    in_vmem = pl.BlockSpec(memory_space=pltpu.VMEM)
    anywhere = pl.BlockSpec(memory_space=pl.ANY)
    return pl.pallas_call(
        kernel,
        out_shape=[jax.ShapeDtypeStruct(shape, dtype) for shape, dtype, _ in outputs],
        in_specs=[in_vmem if near else anywhere for _, near in operands],
        out_specs=[in_vmem if near else anywhere for _, _, near in outputs],
        scratch_shapes=scratch,
        compiler_params=pltpu.CompilerParams(
            collective_id=number, has_side_effects=True, vmem_limit_bytes=56 * 2**20
        ),
        name=name,
    )(*[array for array, _ in operands])


def sliced_heads(local_shards):
    seq_index, seq_count = lax.axis_index("seq"), lax.axis_size("seq")
    count = lax.axis_size("blk")
    gain_attn, w_query, w_key, w_value, _, gain_mlp, _, _, _ = local_shards
    rows = w_query.shape[0]

    def heads_of(weight, per_blk, place):
        head = jnp.arange(count)[:, None] * per_blk + place
        column = (head * HEAD_DIM + jnp.arange(HEAD_DIM)).reshape(-1)
        chosen = jnp.arange(weight.shape[1])[:, None] == column[None, :]
        taken = lax.dot_general(
            chosen.astype(jnp.bfloat16),
            weight,
            (((0,), (1,)), ((), ())),
            preferred_element_type=jnp.float32,
        )
        return taken.astype(jnp.bfloat16).reshape(count, HEAD_DIM, rows)

    kv_per_blk = KV_HEADS // count
    kv_place = seq_index * kv_per_blk // seq_count
    gains = jnp.concatenate(
        [jnp.stack([gain_attn, gain_mlp]), jnp.zeros((14, rows), jnp.bfloat16)]
    )
    return jnp.concatenate(
        [
            heads_of(w_query, seq_count, seq_index),
            jnp.broadcast_to(gains[None], (count,) + gains.shape),
            heads_of(jnp.where(seq_index % 2 == 0, w_key, w_value), kv_per_blk, kv_place),
        ],
        axis=1,
    )


def head_shards(inputs, cotangent, doc_lengths, *params):
    section = lax.axis_index("section")
    at_first = section == 0
    seq_count, count = lax.axis_size("seq"), lax.axis_size("blk")
    low, f32 = jnp.bfloat16, jnp.float32
    vmem, dma = pltpu.VMEM, pltpu.SemaphoreType.DMA
    block, width = inputs.shape[2], inputs.shape[3]
    blocks = seq_count * count
    tokens = blocks * block
    rows_own = lax.dynamic_index_in_dim(inputs, section, 0, keepdims=False)[0]
    grads_own = lax.dynamic_index_in_dim(cotangent, section, 0, keepdims=False)[0]
    local = tuple(weight[0] for weight in params)
    pieces = sliced_heads(local)
    w_output, w_gate, w_up, w_down = local[4], local[6], local[7], local[8]
    rows = w_gate.shape[0]
    lanes = w_gate.shape[1] // blocks
    out_rows, down_rows = w_output.shape[0] // seq_count, w_down.shape[0] // seq_count
    lengths = lax.dynamic_index_in_dim(doc_lengths, section, 0, keepdims=False)[0]
    token_index = jnp.arange(tokens, dtype=jnp.int32)
    _, position = doc_info(lengths, token_index)
    start = (token_index - position)[:, None]
    half_dim = HEAD_DIM // 2
    lane = jnp.arange(PAD)
    frequency = THETA ** (-2.0 * (lane % half_dim).astype(f32) / HEAD_DIM)
    angles = position.astype(f32)[:, None] * frequency[None, :]
    sign = jnp.where(lane < half_dim, -1.0, 1.0).astype(f32)
    cosine = jnp.where(lane < HEAD_DIM, jnp.cos(angles), 0.0)
    sine = jnp.where(lane < HEAD_DIM, jnp.sin(angles) * sign, 0.0)

    def all_blocks():
        return vmem((blocks, block, width), low)

    def scatter():
        return scatter_scratch(count, block, width)

    half_blocks = vmem((blocks // 2, block, width), low)
    half = ((blocks // 2, block, width), low, False)
    own_low, own_wide = ((block, width), low, True), ((block, width), f32, True)
    every = ((blocks, block, width), low, False)
    gain_rows = ((8, width), f32, True)
    attn_outputs = [
        own_wide,
        own_low,
        every,
        ((4, tokens, PAD), low, True),
        ((tokens, 1), f32, True),
    ]
    weights_vm = [vmem((3 * PAD + 16, width), low), vmem((PAD, width), low)]
    wide_vm, down_vm = vmem((width, 2 * lanes), low), vmem((down_rows, width), low)
    tables = [(cosine, True), (sine, True), (start, True)]
    (
        attn,
        twin,
        gate_up,
        out,
        down,
        rows_one,
        wide_rows_one,
        grads_near,
        grads_side,
        hidden_one,
        between,
        normed,
        heads_one,
        total_one,
    ) = call_kernel(
        functools.partial(first_layer_kernel, count),
        "first_layer",
        2,
        [(array, False) for array in (pieces, w_gate, w_up, w_output, w_down)]
        + [(rows_own, True), (grads_own, True)]
        + tables,
        [
            ((2, pieces.shape[1], width), low, False),
            ((2, HEAD_DIM, width), low, False),
            ((2, width, 2 * lanes), low, False),
            ((2, out_rows, width), low, False),
            ((2, down_rows, width), low, False),
            every,
            every,
            half,
            ((block, width), low, False),
            own_wide,
            own_low,
            own_low,
            ((4, tokens, PAD), low, True),
            ((tokens, 1), f32, True),
        ],
        [all_blocks() for _ in range(5)]
        + [half_blocks]
        + weights_vm
        + [wide_vm, down_vm, vmem((tokens, lanes), low), vmem((block, width), low)]
        + [vmem((16, width), low), dma((6,)), dma((3,)), dma, dma]
        + [dma((3, count)), dma((3, count)), dma((5, count)), dma((5, count)), dma((5,))]
        + gather_semaphores(count) * 2
        + line_semaphores(count)
        + [dma, dma]
        + scatter()
        + scatter(),
    )
    gains = attn[:, GAINS : GAINS + 2].astype(f32)
    hidden_two, normed, rows_two, heads_two, total_two, grads_far = call_kernel(
        functools.partial(attn_kernel, count),
        "second_attention",
        4,
        [(normed, True), (between, True), (grads_side, True)]
        + [(attn, False), (twin, False), (out, False)]
        + tables,
        attn_outputs + [half],
        [all_blocks()]
        + weights_vm
        + [all_blocks(), half_blocks, dma((5,)), dma((2,))]
        + gather_semaphores(count)
        + line_semaphores(count)
        + scatter(),
    )
    wide_outputs = [((width, 2 * lanes), low, True), ((down_rows, width), low, True)]
    ahead, branch, grad_hidden, gain_mlp_two, wide_two, down_two = call_kernel(
        functools.partial(mlp_both_kernel, count),
        "second_feed_forward",
        6,
        [
            (normed, True),
            (hidden_two, True),
            (gate_up, False),
            (down, False),
            (grads_near, False),
            (grads_far, False),
            (grads_own, True),
            (gains[1, 1:2], True),
        ],
        [every, own_low, own_wide, gain_rows] + wide_outputs,
        [all_blocks(), all_blocks(), wide_vm, down_vm]
        + [vmem((tokens, lanes), low), vmem((tokens, 2 * lanes), low)]
        + [all_blocks(), all_blocks(), dma((5,))]
        + gather_semaphores(count)
        + scatter(),
    )

    wide_carried = ((width, 2 * lanes), low, False)
    rest_carried = [
        ((down_rows, width), low, False),
        ((3 * HEAD_DIM, width), low, False),
        ((HEAD_DIM, width), low, False),
    ]

    back_scratch = (
        [all_blocks(), all_blocks(), vmem((4, tokens, PAD), low)]
        + weights_vm
        + [vmem((tokens, PAD), low), vmem((tokens, tokens), f32)]
        + [vmem((tokens, PAD), f32), vmem((tokens, PAD), f32), vmem((tokens, 3 * PAD), low)]
        + [all_blocks(), dma((7,))]
        + gather_semaphores(count)
        + scatter()
    )

    def back_operands(layer, branch, grad_hidden, x_own, rows_all, heads, log_total):
        return (
            [(branch, True), (grad_hidden, True), (x_own, True)]
            + [(rows_all, False), (heads, False), (log_total, True)]
            + [(attn, False), (twin, False), (out, False)]
            + tables
            + [(gains[layer, 0:1], True)]
        )

    attn_shape, out_shape = (3 * HEAD_DIM, width), (HEAD_DIM, width)
    grad_between, gain_attn_two, attn_two, out_two, wide_from_one = call_kernel(
        functools.partial(attn_back_kernel, count, 1),
        "second_attention_back",
        8,
        back_operands(1, branch, grad_hidden, between, rows_two, heads_two, total_two)
        + [(wide_two, False)],
        [own_low, gain_rows, (attn_shape, low, True), (out_shape, low, True), wide_carried],
        back_scratch + [dma((1,)), dma((1,))],
    )
    branch, grad_hidden, gain_mlp_one, wide_one, down_one, *rest_from_one = call_kernel(
        functools.partial(mlp_back_kernel, count),
        "first_feed_forward_back",
        9,
        [
            (grad_between, True),
            (hidden_one, True),
            (wide_rows_one, False),
            (gate_up, False),
            (down, False),
            (gains[0, 1:2], True),
            (down_two, False),
            (attn_two, False),
            (out_two, False),
        ],
        [own_low, own_wide, gain_rows] + wide_outputs + rest_carried,
        [all_blocks(), all_blocks(), wide_vm, down_vm]
        + [vmem((tokens, lanes), low), vmem((tokens, 2 * lanes), f32)]
        + [vmem((tokens, 2 * lanes), low), all_blocks(), dma((3,)), dma((3,)), dma((3,))]
        + gather_semaphores(count)
        + scatter(),
    )
    down_from_one, attn_from_one, out_from_one = rest_from_one
    swapped_rows, final, grad_start, gain_sums, query, key, value, out, gate, up, down = last_layer(
        count,
        back_operands(0, branch, grad_hidden, rows_own, rows_one, heads_one, total_one)
        + [(wide_one, False), (down_one, False), (attn_two, False), (out_two, False)]
        + [(wide_two, False), (down_two, False), (wide_from_one, False), (down_from_one, False)]
        + [(attn_from_one, False), (out_from_one, False), (ahead, False)]
        + [(gain_mlp_one, True), (gain_attn_two, True), (gain_mlp_two, True)]
        + [(between, True), (grad_between, True), (hidden_two, True)],
        (
            attn_shape,
            out_shape,
            (width, 2 * lanes),
            (down_rows, width),
            block,
            width,
            gain_rows[0][0],
        ),
        back_scratch,
    )
    kept = jnp.where(
        at_first, jnp.stack([between, grad_start]), jnp.stack([final, grad_between])
    )
    pairs = jnp.where(
        at_first, jnp.stack([kept, swapped_rows], axis=1), jnp.stack([swapped_rows, kept], axis=1)
    )
    return (
        pairs[0][None, :, None],
        pairs[1][None, :, None],
        gain_sums[0][None],
        query[None],
        key[None],
        value[None],
        out[None],
        gain_sums[4][None],
        gate[None],
        up[None],
        down[None],
    )

def solution(mesh):
    placed = (
        P(None, None, ("seq", "blk"), None),
        P(None, None, ("seq", "blk"), None),
        P(),
        P("section", "blk"),
        P("section", "blk", None),
        P("section", "blk", None),
        P("section", "blk", None),
        P("section", "blk", None),
        P("section", "blk"),
        P("section", "blk", None),
        P("section", "blk", None),
        P("section", "blk", None),
    )
    one_head_each = mesh.shape["seq"] == 4 and mesh.shape["blk"] == HEADS // 4
    return jax.shard_map(
        head_shards if one_head_each else shards,
        mesh=mesh,
        in_specs=placed,
        out_specs=(
            P("section", None, None, ("seq", "blk"), None),
            P("section", None, None, ("seq", "blk"), None),
            P("section", "blk"),
            P("section", "blk", None),
            P("section", "blk", None),
            P("section", "blk", None),
            P("section", "blk", None),
            P("section", "blk"),
            P("section", "blk", None),
            P("section", "blk", None),
            P("section", "blk", None),
        ),
        check_vma=False,
    )
```

```python
import functools

import jax
import jax.numpy as jnp
from jax import lax
from jax.experimental import pallas as pl
from jax.experimental.pallas import tpu as pltpu
from jax.sharding import PartitionSpec as P

HEADS = 16
KV_HEADS = 8
HEAD_DIM = 96


EPS = 1e-05
THETA = 100000.0
MASKED = -1e30


def passed_along(value, axis, steps):
    count = lax.axis_size(axis)
    first, last = (max(0, -steps), min(count, count - steps))
    return lax.ppermute(value, axis, [(source, source + steps) for source in range(first, last)])


def shortened(value):
    return jax.tree.map(lambda a: a.astype(jnp.bfloat16) if a.dtype == jnp.float32 else a, value)


def product(left_side, right_side):
    return jnp.dot(left_side, right_side, preferred_element_type=jnp.float32)


def back_product(left_side, right_side):
    return lax.dot_general(
        left_side, right_side, (((1,), (1,)), ((), ())), preferred_element_type=jnp.float32
    )


def doc_info(lengths, token_index):
    doc_ends = jnp.cumsum(lengths, axis=-1)
    passed = (doc_ends[..., None, :] <= token_index[..., None]).astype(jnp.int32)
    segment = jnp.sum(passed, axis=-1)
    offset = jnp.sum(passed * lengths[..., None, :], axis=-1)
    return (segment, token_index - offset)


def rotate(field_in, position, turn_sign):
    half_dim = field_in.shape[-1] // 2
    frequency = THETA ** (-2.0 * jnp.arange(half_dim, dtype=jnp.float32) / field_in.shape[-1])
    angles = position.astype(jnp.float32)[:, None] * frequency
    cosine = jnp.cos(angles)[:, None, :]
    sine_part = turn_sign * jnp.sin(angles)[:, None, :]
    first_half = field_in[..., :half_dim]
    second_half = field_in[..., half_dim:]
    return jnp.concatenate(
        [
            first_half * cosine - second_half * sine_part,
            second_half * cosine + first_half * sine_part,
        ],
        axis=-1,
    )


def rms_forward(field_in, gain_row):
    inv_root = lax.rsqrt(jnp.mean(field_in * field_in, axis=-1, keepdims=True) + EPS)
    return (field_in * inv_root * gain_row, inv_root)


def rms_backward(field_in, gain_row, inv_root, grad_normed):
    scaled = gain_row * grad_normed
    grad_field = inv_root * scaled - field_in * inv_root**3 * jnp.mean(
        scaled * field_in, axis=-1, keepdims=True
    )
    return (grad_field, grad_normed * field_in * inv_root)


def token_place(block_id, row_ids, per_device, blk_count):
    return (row_ids // per_device * blk_count + block_id) * per_device + row_ids % per_device


def masks_for(lengths, blk_index, per_device, blk_count, seq_count):
    block_tokens = seq_count * per_device
    row_ids = jnp.arange(block_tokens, dtype=jnp.int32)
    query_index = token_place(blk_index, row_ids, per_device, blk_count)
    all_ids = jnp.arange(blk_count * block_tokens, dtype=jnp.int32)
    key_index = token_place(all_ids // block_tokens, all_ids % block_tokens, per_device, blk_count)
    query_seg, _ = doc_info(lengths, query_index)
    key_seg, _ = doc_info(lengths, key_index)
    return (query_index, key_index, query_seg, key_seg)


def head_scores(queries, key_rows, allowed, kv_local):
    grouped = queries.reshape(queries.shape[0], kv_local, -1, HEAD_DIM)
    key_heads = key_rows.reshape(key_rows.shape[0], kv_local, HEAD_DIM)
    scores = jnp.einsum(
        "rkgd,lkd->kgrl", grouped, key_heads, preferred_element_type=jnp.float32
    ) * HEAD_DIM ** (-0.5)
    return (jnp.where(allowed, scores, MASKED), grouped, key_heads)


def attend_forward(operands, query_index, key_index, kv_local):
    queries, key_rows, value_rows, query_seg, key_seg = operands
    allowed = (query_seg[:, None] == key_seg[None, :]) & (
        key_index[None, :] <= query_index[:, None]
    )
    scores, grouped, key_heads = head_scores(queries, key_rows, allowed, kv_local)
    row_top = jnp.max(scores, axis=-1, keepdims=True)
    log_total = row_top + jnp.log(jnp.sum(jnp.exp(scores - row_top), axis=-1, keepdims=True))
    weights_low = jnp.exp(scores - log_total).astype(jnp.bfloat16)
    value_heads = value_rows.reshape(value_rows.shape[0], kv_local, HEAD_DIM)
    mixed_heads = jnp.einsum(
        "kgrl,lkd->rkgd", weights_low, value_heads, preferred_element_type=jnp.float32
    )
    return (mixed_heads.reshape(queries.shape).astype(jnp.bfloat16), log_total)


def attend_backward(operands, query_index, key_index, kv_local):
    queries, key_rows, value_rows, grad_mixed, log_total, query_seg, key_seg = operands
    allowed = (query_seg[:, None] == key_seg[None, :]) & (
        key_index[None, :] <= query_index[:, None]
    )
    scores, grouped, key_heads = head_scores(queries, key_rows, allowed, kv_local)
    attn_probs = jnp.exp(scores - log_total)
    value_heads = value_rows.reshape(value_rows.shape[0], kv_local, HEAD_DIM)
    grad_heads = grad_mixed.reshape(grouped.shape)
    grad_values = jnp.einsum(
        "kgrl,rkgd->lkd",
        attn_probs.astype(jnp.bfloat16),
        grad_heads,
        preferred_element_type=jnp.float32,
    )
    grad_probs = jnp.einsum(
        "rkgd,lkd->kgrl", grad_heads, value_heads, preferred_element_type=jnp.float32
    )
    centre = jnp.sum(attn_probs * grad_probs, axis=-1, keepdims=True)
    grad_scores = (attn_probs * (grad_probs - centre)).astype(jnp.bfloat16)
    grad_queries = jnp.einsum(
        "kgrl,lkd->rkgd", grad_scores, key_heads, preferred_element_type=jnp.float32
    ) * HEAD_DIM ** (-0.5)
    grad_keys = jnp.einsum(
        "kgrl,rkgd->lkd", grad_scores, grouped, preferred_element_type=jnp.float32
    ) * HEAD_DIM ** (-0.5)
    return (
        grad_queries.reshape(queries.shape).astype(jnp.bfloat16),
        grad_keys.reshape(key_rows.shape),
        grad_values.reshape(value_rows.shape),
    )


def layer_forward(section_in, lengths, weights, placing):
    shard_id, blk_index, seq_count, blk_count = placing
    gain_attn, w_query, w_key, w_value, w_output, gain_mlp, w_gate, w_up, w_down = weights
    seqs_here, per_device, width = section_in.shape
    token_rows = seqs_here * per_device
    copies = max(1, seq_count // KV_HEADS)
    kv_local = KV_HEADS * copies // seq_count
    token_index = shard_id * per_device + jnp.arange(per_device, dtype=jnp.int32)
    _, position = doc_info(lengths, token_index)
    position = position.reshape(token_rows)
    flat_in = section_in.reshape(token_rows, width)
    normed, inv_first = rms_forward(flat_in, gain_attn.astype(jnp.float32))
    normed_low = normed.astype(jnp.bfloat16)
    query_pre = product(normed_low, w_query).reshape(token_rows, HEADS, HEAD_DIM)
    key_pre = product(normed_low, w_key).reshape(token_rows, KV_HEADS, HEAD_DIM)
    value_pre = product(normed_low, w_value).reshape(token_rows, KV_HEADS, HEAD_DIM)
    query_rot = (
        rotate(query_pre, position, 1.0).astype(jnp.bfloat16).reshape(seqs_here, per_device, width)
    )
    key_rot = rotate(key_pre, position, 1.0).astype(jnp.bfloat16)
    spread_shape = (token_rows, KV_HEADS, copies, HEAD_DIM)
    key_rep = jnp.broadcast_to(key_rot[:, :, None, :], spread_shape).reshape(
        seqs_here, per_device, -1
    )
    value_rep = jnp.broadcast_to(
        value_pre.astype(jnp.bfloat16)[:, :, None, :], spread_shape
    ).reshape(seqs_here, per_device, -1)
    heads_query, heads_key, heads_value = (
        lax.all_to_all(query_rot, "seq", split_axis=2, concat_axis=1, tiled=True),
        lax.all_to_all(key_rep, "seq", split_axis=2, concat_axis=1, tiled=True),
        lax.all_to_all(value_rep, "seq", split_axis=2, concat_axis=1, tiled=True),
    )
    keys_all, values_all = (
        lax.all_gather(heads_key, "blk", axis=1, tiled=True),
        lax.all_gather(heads_value, "blk", axis=1, tiled=True),
    )
    query_index, key_index, query_seg, key_seg = masks_for(
        lengths, blk_index, per_device, blk_count, seq_count
    )
    heads_mixed, log_total = lax.map(
        lambda operands: attend_forward(operands, query_index, key_index, kv_local),
        (heads_query, keys_all, values_all, query_seg, key_seg),
    )
    token_mixed = lax.all_to_all(
        heads_mixed, "seq", split_axis=1, concat_axis=2, tiled=True
    ).reshape(token_rows, width)
    hidden = flat_in + product(token_mixed, w_output)
    normed_mlp, inv_second = rms_forward(hidden, gain_mlp.astype(jnp.float32))
    normed_mlp_low = normed_mlp.astype(jnp.bfloat16)
    gate_pre = product(normed_mlp_low, w_gate)
    up_pre = product(normed_mlp_low, w_up)
    act_low = (jax.nn.silu(gate_pre) * up_pre).astype(jnp.bfloat16)
    result = hidden + product(act_low, w_down)
    saved_state = (
        flat_in,
        normed_low,
        inv_first,
        position,
        heads_query,
        keys_all,
        values_all,
        log_total,
        token_mixed,
        hidden,
        inv_second,
        normed_mlp_low,
        gate_pre,
        up_pre,
        act_low,
        lengths,
    )
    return (result.reshape(section_in.shape), saved_state)


def layer_backward(upstream, saved_state, weights, placing):
    shard_id, blk_index, seq_count, blk_count = placing
    gain_attn, w_query, w_key, w_value, w_output, gain_mlp, w_gate, w_up, w_down = weights
    (
        flat_in,
        normed_low,
        inv_first,
        position,
        heads_query,
        keys_all,
        values_all,
        log_total,
        token_mixed,
        hidden,
        inv_second,
        normed_mlp_low,
        gate_pre,
        up_pre,
        act_low,
        lengths,
    ) = saved_state
    seqs_here, per_device, width = upstream.shape
    token_rows = seqs_here * per_device
    copies = max(1, seq_count // KV_HEADS)
    kv_local = KV_HEADS * copies // seq_count
    grad_rows = upstream.reshape(token_rows, width)
    grad_out_low = grad_rows.astype(jnp.bfloat16)
    grad_act = back_product(grad_out_low, w_down)
    gate_sigmoid = jax.nn.sigmoid(gate_pre)
    grad_gate_low = (
        grad_act * up_pre * gate_sigmoid * (1.0 + gate_pre * (1.0 - gate_sigmoid))
    ).astype(jnp.bfloat16)
    grad_up_low = (grad_act * jax.nn.silu(gate_pre)).astype(jnp.bfloat16)
    grad_normed_mlp = back_product(grad_gate_low, w_gate) + back_product(grad_up_low, w_up)
    grad_hidden_part, gain_mlp_terms = rms_backward(
        hidden, gain_mlp.astype(jnp.float32), inv_second, grad_normed_mlp
    )
    grad_hidden = grad_rows + grad_hidden_part
    grad_branch_low = grad_hidden.astype(jnp.bfloat16)
    grad_mixed_low = (
        back_product(grad_branch_low, w_output)
        .astype(jnp.bfloat16)
        .reshape(seqs_here, per_device, width)
    )
    heads_grad = lax.all_to_all(grad_mixed_low, "seq", split_axis=2, concat_axis=1, tiled=True)
    query_index, key_index, query_seg, key_seg = masks_for(
        lengths, blk_index, per_device, blk_count, seq_count
    )
    grad_heads_query, grad_keys_all, grad_values_all = lax.map(
        lambda operands: attend_backward(operands, query_index, key_index, kv_local),
        (heads_query, keys_all, values_all, heads_grad, log_total, query_seg, key_seg),
    )
    grad_key_own, grad_value_own = (
        lax.psum_scatter(
            grad_keys_all.astype(jnp.bfloat16), "blk", scatter_dimension=1, tiled=True
        ).astype(jnp.float32),
        lax.psum_scatter(
            grad_values_all.astype(jnp.bfloat16), "blk", scatter_dimension=1, tiled=True
        ).astype(jnp.float32),
    )
    token_query, token_key, token_value = (
        lax.all_to_all(grad_heads_query, "seq", split_axis=1, concat_axis=2, tiled=True),
        lax.all_to_all(
            grad_key_own.astype(jnp.bfloat16), "seq", split_axis=1, concat_axis=2, tiled=True
        ),
        lax.all_to_all(
            grad_value_own.astype(jnp.bfloat16), "seq", split_axis=1, concat_axis=2, tiled=True
        ),
    )
    grad_key_sum = jnp.sum(
        token_key.astype(jnp.float32).reshape(token_rows, KV_HEADS, copies, HEAD_DIM), axis=2
    )
    grad_value_sum = jnp.sum(
        token_value.astype(jnp.float32).reshape(token_rows, KV_HEADS, copies, HEAD_DIM), axis=2
    )
    grad_query_low = (
        rotate(token_query.astype(jnp.float32).reshape(token_rows, HEADS, HEAD_DIM), position, -1.0)
        .astype(jnp.bfloat16)
        .reshape(token_rows, width)
    )
    grad_key_low = (
        rotate(grad_key_sum, position, -1.0)
        .astype(jnp.bfloat16)
        .reshape(token_rows, KV_HEADS * HEAD_DIM)
    )
    grad_value_low = grad_value_sum.astype(jnp.bfloat16).reshape(token_rows, KV_HEADS * HEAD_DIM)
    grad_normed = (
        back_product(grad_query_low, w_query)
        + back_product(grad_key_low, w_key)
        + back_product(grad_value_low, w_value)
    )
    grad_in_part, gain_attn_terms = rms_backward(
        flat_in, gain_attn.astype(jnp.float32), inv_first, grad_normed
    )
    grad_input = (grad_hidden + grad_in_part).reshape(upstream.shape)
    weight_rows = (
        gain_attn_terms,
        normed_low,
        grad_query_low,
        grad_key_low,
        grad_value_low,
        token_mixed,
        grad_branch_low,
        gain_mlp_terms,
        normed_mlp_low,
        grad_gate_low,
        grad_up_low,
        act_low,
        grad_out_low,
    )
    return (grad_input, weight_rows)


def weight_term(inputs_low, outputs_low):
    if outputs_low is None:
        return jnp.sum(inputs_low, axis=0)
    return lax.dot_general(
        inputs_low, outputs_low, (((0,), (0,)), ((), ())), preferred_element_type=jnp.float32
    )


def shards(
    inputs,
    cotangent,
    doc_lengths,
    attention_gain,
    w_query,
    w_key,
    w_value,
    w_output,
    mlp_gain,
    w_gate,
    w_up,
    w_down,
):
    at_first = lax.axis_index("section") == 0
    seq_count = lax.axis_size("seq")
    blk_count = lax.axis_size("blk")
    blk_index = lax.axis_index("blk")
    shard_id = lax.axis_index("seq") * blk_count + blk_index
    placing = (shard_id, blk_index, seq_count, blk_count)
    micro_count = inputs.shape[0]
    local_shards = (
        attention_gain[0],
        w_query[0],
        w_key[0],
        w_value[0],
        w_output[0],
        mlp_gain[0],
        w_gate[0],
        w_up[0],
        w_down[0],
    )
    weights = (
        lax.all_gather(local_shards[0], "blk", axis=0, tiled=True),
        lax.all_gather(local_shards[1], "blk", axis=0, tiled=True),
        lax.all_gather(local_shards[2], "blk", axis=0, tiled=True),
        lax.all_gather(local_shards[3], "blk", axis=0, tiled=True),
        lax.all_gather(local_shards[4], "blk", axis=0, tiled=True),
        lax.all_gather(local_shards[5], "blk", axis=0, tiled=True),
        lax.all_gather(local_shards[6], "blk", axis=0, tiled=True),
        lax.all_gather(local_shards[7], "blk", axis=0, tiled=True),
        lax.all_gather(local_shards[8], "blk", axis=0, tiled=True),
    )
    received = jnp.zeros(inputs.shape[1:], jnp.bfloat16)
    saved_states = []
    section_outs = []
    for tick_index in range(micro_count + 1):
        fresh_input = inputs[min(tick_index, micro_count - 1)]
        section_in = jnp.where(at_first, fresh_input, received).astype(jnp.float32)
        lengths = jnp.where(
            at_first,
            doc_lengths[min(tick_index, micro_count - 1)],
            doc_lengths[max(tick_index - 1, 0)],
        )
        result, saved_state = layer_forward(section_in, lengths, weights, placing)
        result_low = result.astype(jnp.bfloat16)
        if tick_index < micro_count:
            received = passed_along(result_low, "section", 1)
        saved_states.append(saved_state)
        section_outs.append(result_low)
    weights = (
        lax.all_gather(local_shards[0], "blk", axis=0, tiled=True),
        lax.all_gather(local_shards[1], "blk", axis=0, tiled=True),
        lax.all_gather(local_shards[2], "blk", axis=0, tiled=True),
        lax.all_gather(local_shards[3], "blk", axis=0, tiled=True),
        lax.all_gather(local_shards[4], "blk", axis=0, tiled=True),
        lax.all_gather(local_shards[5], "blk", axis=0, tiled=True),
        lax.all_gather(local_shards[6], "blk", axis=0, tiled=True),
        lax.all_gather(local_shards[7], "blk", axis=0, tiled=True),
        lax.all_gather(local_shards[8], "blk", axis=0, tiled=True),
    )
    back_in = jnp.zeros(cotangent.shape[1:], jnp.bfloat16)
    grad_outs = []
    row_sets = []
    for tick_index in range(micro_count + 1):
        saved_state = jax.tree.map(
            lambda first_pick, second_pick: jnp.where(at_first, first_pick, second_pick),
            saved_states[max(tick_index - 1, 0)],
            saved_states[min(tick_index + 1, micro_count)],
        )
        upstream = jnp.where(at_first, back_in, cotangent[min(tick_index, micro_count - 1)]).astype(
            jnp.float32
        )
        grad_input, weight_rows = layer_backward(upstream, saved_state, weights, placing)
        grad_low = grad_input.astype(jnp.bfloat16)
        if tick_index < micro_count:
            back_in = passed_along(grad_low, "section", -1)
        grad_outs.append(grad_low)
        row_sets.append(weight_rows)
    activations = jnp.stack(
        [
            jnp.where(at_first, section_outs[index_m], section_outs[index_m + 1])
            for index_m in range(micro_count)
        ]
    )[None]
    input_grads = jnp.stack(
        [
            jnp.where(at_first, grad_outs[index_m + 1], grad_outs[index_m])
            for index_m in range(micro_count)
        ]
    )[None]
    picked = [
        jax.tree.map(
            lambda first_pick, second_pick: jnp.where(at_first, first_pick, second_pick),
            row_sets[index_m + 1],
            row_sets[index_m],
        )
        for index_m in range(micro_count)
    ]
    merged = jax.tree.map(lambda *pieces: jnp.concatenate(pieces, axis=0), *picked)
    (
        gain_attn_terms,
        normed_low,
        grad_query_low,
        grad_key_low,
        grad_value_low,
        token_mixed,
        grad_branch_low,
        gain_mlp_terms,
        normed_mlp_low,
        grad_gate_low,
        grad_up_low,
        act_low,
        grad_out_low,
    ) = merged
    grad_pairs = (
        (gain_attn_terms, None),
        (normed_low, grad_query_low),
        (normed_low, grad_key_low),
        (normed_low, grad_value_low),
        (token_mixed, grad_branch_low),
        (gain_mlp_terms, None),
        (normed_mlp_low, grad_gate_low),
        (normed_mlp_low, grad_up_low),
        (act_low, grad_out_low),
    )
    shares = tuple(
        (
            lax.psum_scatter(
                weight_term(left_side, right_side).astype(jnp.bfloat16),
                "blk",
                scatter_dimension=0,
                tiled=True,
            ).astype(jnp.float32)
            for left_side, right_side in grad_pairs
        )
    )
    shares = jax.tree.map(lambda part: part.astype(jnp.float32), lax.psum(shortened(shares), "seq"))
    return (
        activations,
        input_grads,
        shares[0][None],
        shares[1][None],
        shares[2][None],
        shares[3][None],
        shares[4][None],
        shares[5][None],
        shares[6][None],
        shares[7][None],
        shares[8][None],
    )


MESH = pl.DeviceIdType.MESH


def remote(source, target, sent, arrived, device):
    return pltpu.make_async_remote_copy(
        source, target, sent, arrived, device_id=device, device_id_type=MESH
    )


def greet(partners):
    barrier = pltpu.get_barrier_semaphore()
    for device in partners:
        pl.semaphore_signal(barrier, 1, device_id=device, device_id_type=MESH)
    pl.semaphore_wait(barrier, len(partners))


def settled(spot, semaphore, received):
    copy = remote(spot, spot, semaphore, semaphore, {"seq": lax.axis_index("seq") ^ 1})
    if received:
        copy.wait_recv()
    else:
        copy.wait_send()


CUTS = 2


def gather_steps(
    count, own, out, line_sent, line_got, side_sent, side_got, core_sent, core_got, local_done
):
    seq, b = lax.axis_index("seq"), lax.axis_index("blk")
    core, side = {"seq": seq ^ 1}, {"seq": seq ^ 2}
    base, side_base = seq * count, (seq ^ 2) * count
    cut = out.shape[1] // CUTS

    def spot(index, h):
        return out.at[index, pl.ds(h * cut, cut)]

    def begin(index, h, first):
        return own.at[pl.ds(h * cut, cut)] if first else spot(index, h)

    def along_line(j, way, h, first=False):
        device = {"blk": b + (1 if way else -1)}
        return remote(
            begin(base + j, h, first),
            spot(base + j, h),
            line_sent.at[j, way, h],
            line_got.at[j, h],
            device,
        )

    def to_side(j, h, first=False):
        return remote(
            begin(base + j, h, first),
            spot(base + j, h),
            side_sent.at[j, h],
            side_got.at[j, h],
            side,
        )

    def to_core(half, j, h, first=False):
        index = (side_base if half else base) + j
        return remote(
            begin(index, h, first),
            spot(index, h),
            core_sent.at[half, j, h],
            core_got.at[half, j, h],
            core,
        )

    local = pltpu.make_async_copy(own, out.at[base + b], local_done)
    local.start()
    for h in range(CUTS):
        to_side(b, h, True).start()
        pl.when(b > 0)(along_line(b, 0, h, True).start)
        pl.when(b < count - 1)(along_line(b, 1, h, True).start)
    for h in range(CUTS):
        to_core(0, b, h, True).start()
    yield "sent"

    def from_line(j, way):
        for h in range(CUTS):
            settled(spot(base + j, h), line_got.at[j, h], True)
            pl.when((b < count - 1) if way else (b > 0))(along_line(j, way, h).start)
            to_side(j, h).start()
        for h in range(CUTS):
            to_core(0, j, h).start()

    def from_side(j):
        for h in range(CUTS):
            settled(spot(side_base + j, h), side_got.at[j, h], True)
            to_core(1, j, h).start()

    for k in range(1, count + 1):
        if k < count:
            pl.when(b - k >= 0)(functools.partial(from_line, b - k, 1))
            pl.when(b + k < count)(functools.partial(from_line, b + k, 0))
        if k == 1:
            from_side(b)
        else:
            pl.when(b - k + 1 >= 0)(functools.partial(from_side, b - k + 1))
            pl.when(b + k - 1 < count)(functools.partial(from_side, b + k - 1))
        if k == count - 1:
            local.wait()
        yield "line" if k == count - 1 else "side" if k == count else "step"
    for half, corner in ((0, seq ^ 1), (1, seq ^ 3)):
        for j in range(count):
            for h in range(CUTS):
                settled(spot(corner * count + j, h), core_got.at[half, j, h], True)
        yield "corner" if half else "near"
    for h in range(CUTS):
        for j in range(count):
            to_side(j, h).wait_send()
            to_core(0, j, h).wait_send()
            to_core(1, j, h).wait_send()
        pl.when(b > 0)(along_line(b, 0, h).wait_send)
        pl.when(b < count - 1)(along_line(b, 1, h).wait_send)
        for k in range(1, count):
            pl.when((b - k >= 0) & (b < count - 1))(along_line(b - k, 1, h).wait_send)
            pl.when((b + k < count) & (b > 0))(along_line(b + k, 0, h).wait_send)


def gather_semaphores(count):
    dma = pltpu.SemaphoreType.DMA
    return [
        dma((count, 2, CUTS)),
        dma((count, CUTS)),
        dma((count, CUTS)),
        dma((count, CUTS)),
        dma((2, count, CUTS)),
        dma((2, count, CUTS)),
        dma,
    ]


def line_steps(
    count, own, out, line_sent, line_got, core_sent, core_got, local_done, offset=0
):
    seq, b = lax.axis_index("seq"), lax.axis_index("blk")
    core, base = {"seq": seq ^ 1}, offset + (seq % 2) * count
    cut = out.shape[1] // CUTS

    def spot(j, h):
        return out.at[base + j, pl.ds(h * cut, cut)]

    def begin(j, h, first):
        return own.at[pl.ds(h * cut, cut)] if first else spot(j, h)

    def along_line(j, way, h, first=False):
        device = {"blk": b + (1 if way else -1)}
        return remote(
            begin(j, h, first), spot(j, h), line_sent.at[j, way, h], line_got.at[j, h], device
        )

    def to_core(j, h, first=False):
        return remote(begin(j, h, first), spot(j, h), core_sent.at[j, h], core_got.at[j, h], core)

    local = pltpu.make_async_copy(own, out.at[base + b], local_done)
    local.start()
    for h in range(CUTS):
        pl.when(b > 0)(along_line(b, 0, h, True).start)
        pl.when(b < count - 1)(along_line(b, 1, h, True).start)
        to_core(b, h, True).start()
    yield

    def from_line(j, way):
        for h in range(CUTS):
            settled(spot(j, h), line_got.at[j, h], True)
            pl.when((b < count - 1) if way else (b > 0))(along_line(j, way, h).start)
            to_core(j, h).start()

    for k in range(1, count):
        pl.when(b - k >= 0)(functools.partial(from_line, b - k, 1))
        pl.when(b + k < count)(functools.partial(from_line, b + k, 0))
        yield
    local.wait()
    for h in range(CUTS):
        for j in range(count):
            place = offset + (1 - seq % 2) * count + j
            settled(out.at[place, pl.ds(h * cut, cut)], core_got.at[j, h], True)
            to_core(j, h).wait_send()
        pl.when(b > 0)(along_line(b, 0, h).wait_send)
        pl.when(b < count - 1)(along_line(b, 1, h).wait_send)
        for k in range(1, count):
            pl.when((b - k >= 0) & (b < count - 1))(along_line(b - k, 1, h).wait_send)
            pl.when((b + k < count) & (b > 0))(along_line(b + k, 0, h).wait_send)


def line_semaphores(count):
    dma = pltpu.SemaphoreType.DMA
    return [
        dma((count, 2, CUTS)),
        dma((count, CUTS)),
        dma((count, CUTS)),
        dma((count, CUTS)),
        dma,
    ]


def advance(steps, times):
    for _ in range(times):
        next(steps, None)


def group_of(event):
    seq = lax.axis_index("seq")
    return {"line": seq, "side": seq ^ 2, "near": seq ^ 1, "corner": seq ^ 3}.get(event)


def scatter_steps(
    count,
    partial,
    deliver,
    core_slot,
    side_slot,
    line_slot,
    side_out,
    line_out,
    running,
    core_sent,
    core_got,
    side_sent,
    side_got,
    line_sent,
    line_got,
    compute=None,
):
    seq, b = lax.axis_index("seq"), lax.axis_index("blk")
    core, side = {"seq": seq ^ 1}, {"seq": seq ^ 2}
    place = far_first(b, count)
    size = partial.shape[1] // CUTS
    cuts = [pl.ds(h * size, size) for h in range(CUTS)]

    def to_core(half, k, h):
        return remote(
            partial.at[(seq ^ (1 if half else 3)) * count + place[k], cuts[h]],
            core_slot.at[half, k, cuts[h]],
            core_sent.at[half, k, h],
            core_got.at[half, k, h],
            core,
        )

    def to_side(k, h):
        return remote(
            side_out.at[k, cuts[h]],
            side_slot.at[k, cuts[h]],
            side_sent.at[k, h],
            side_got.at[k, h],
            side,
        )

    def along_line(k, way, h):
        j = place[k]
        return remote(
            line_out.at[k, cuts[h]],
            line_slot.at[way, j, cuts[h]],
            line_sent.at[k, h],
            line_got.at[way, j, h],
            {"blk": b + (1 if way else -1)},
        )

    def add_from(way, j, h):
        settled(line_slot.at[way, j, cuts[h]], line_got.at[way, j, h], True)
        running[cuts[h]] += line_slot[way, j, cuts[h]].astype(jnp.float32)

    def exchange(half):
        if compute:
            compute(seq ^ (1 if half else 3))
        for k in range(count):
            for h in range(CUTS):
                to_core(half, k, h).start()

    exchange(0)
    if compute:
        compute(seq ^ 2)
    for k in range(count):
        for h in range(CUTS):
            to_core(0, k, h).wait_recv()
            total = partial[(seq ^ 2) * count + place[k], cuts[h]].astype(jnp.float32)
            total += core_slot[0, k, cuts[h]].astype(jnp.float32)
            side_out[k, cuts[h]] = total.astype(jnp.bfloat16)
            to_side(k, h).start()
    exchange(1)
    if compute:
        compute(seq)
    yield
    for k in range(count):
        j = place[k]
        rightward, leftward = j >= b, j <= b
        for h in range(CUTS):
            to_core(1, k, h).wait_recv()
            to_side(k, h).wait_recv()
            total = partial[seq * count + j, cuts[h]].astype(jnp.float32)
            total += core_slot[1, k, cuts[h]].astype(jnp.float32)
            running[cuts[h]] = total + side_slot[k, cuts[h]].astype(jnp.float32)
            pl.when(rightward & (b > 0))(functools.partial(add_from, 1, j, h))
            pl.when(leftward & (b < count - 1))(functools.partial(add_from, 0, j, h))
            if k < count - 1:
                line_out[k, cuts[h]] = running[cuts[h]].astype(jnp.bfloat16)
                pl.when(rightward)(along_line(k, 1, h).start)
                pl.when(jnp.logical_not(rightward))(along_line(k, 0, h).start)
        if k < count - 1:
            yield
    deliver(running[...])
    yield
    for k in range(count):
        for h in range(CUTS):
            to_core(0, k, h).wait_send()
            to_core(1, k, h).wait_send()
            to_side(k, h).wait_send()
            if k < count - 1:
                settled(line_out.at[k, cuts[h]], line_sent.at[k, h], False)


def line_first_steps(
    count,
    partial,
    deliver,
    own,
    core_slot,
    line_slot,
    line_out,
    side_slot,
    running,
    own_done,
    core_sent,
    core_got,
    line_sent,
    line_got,
    side_sent,
    side_got,
):
    seq, b = lax.axis_index("seq"), lax.axis_index("blk")
    core, side = {"seq": seq ^ 1}, {"seq": seq ^ 2}
    place = far_first(b, count)

    def to_core(half, k):
        source = partial.at[(seq ^ (1 if half else 3)) * count + place[k]]
        return remote(
            source, core_slot.at[half, k], core_sent.at[half, k], core_got.at[half, k], core
        )

    def kept(half, k):
        source = partial.at[(seq if half else seq ^ 2) * count + place[k]]
        return pltpu.make_async_copy(source, own.at[half, k], own_done.at[half, k])

    def along_line(half, k, way):
        j = place[k]
        return remote(
            line_out.at[half, k],
            line_slot.at[half, way, j],
            line_sent.at[half, k],
            line_got.at[half, way, j],
            {"blk": b + (1 if way else -1)},
        )

    def add_from(half, way, j):
        settled(line_slot.at[half, way, j], line_got.at[half, way, j], True)
        running[...] += line_slot[half, way, j].astype(jnp.float32)

    to_side = remote(line_out.at[0, count - 1], side_slot.at[0], side_sent, side_got, side)
    for half in range(2):
        for k in range(count):
            kept(half, k).start()
            to_core(half, k).start()
    yield
    for k in range(count):
        j = place[k]
        rightward, leftward = j >= b, j <= b
        for half in range(2):
            kept(half, k).wait()
            to_core(half, k).wait_recv()
            running[...] = own[half, k].astype(jnp.float32) + core_slot[half, k].astype(jnp.float32)
            pl.when(rightward & (b > 0))(functools.partial(add_from, half, 1, j))
            pl.when(leftward & (b < count - 1))(functools.partial(add_from, half, 0, j))
            if half == 0 or k < count - 1:
                line_out[half, k] = running[...].astype(jnp.bfloat16)
            if k < count - 1:
                pl.when(rightward)(along_line(half, k, 1).start)
                pl.when(jnp.logical_not(rightward))(along_line(half, k, 0).start)
            elif half == 0:
                to_side.start()
            else:
                to_side.wait_recv()
                deliver(running[...] + side_slot[0].astype(jnp.float32))
            yield
    to_side.wait_send()
    for half in range(2):
        for k in range(count):
            to_core(half, k).wait_send()
            if k < count - 1:
                settled(line_out.at[half, k], line_sent.at[half, k], False)


def far_first(b, count):
    order = sorted(range(count), key=lambda j: -j)
    places = []
    for k in range(count):
        place = 0
        for own in range(count):
            by_distance = sorted(order, key=lambda j: (-abs(j - own), -j if own * 2 < count else j))
            place = jnp.where(b == own, by_distance[k], place)
        places.append(place)
    return places


def scatter_scratch(count, rows, width):
    dma = pltpu.SemaphoreType.DMA

    def slots(*places):
        return pltpu.VMEM(places + (rows, width), jnp.bfloat16)

    return [
        slots(2, count),
        slots(count),
        slots(2, count),
        slots(count),
        slots(count - 1),
        pltpu.VMEM((rows, width), jnp.float32),
        dma((2, count, CUTS)),
        dma((2, count, CUTS)),
        dma((count, CUTS)),
        dma((count, CUTS)),
        dma((count - 1, CUTS)),
        dma((2, count, CUTS)),
    ]


def run_all(fillers):
    for filler in fillers:
        filler()


def run_with(steps, fillers):
    fillers = list(fillers)
    for _ in steps:
        if fillers:
            fillers.pop(0)()
    for filler in fillers:
        filler()


def greet_group(count, more=()):
    seq, b = lax.axis_index("seq"), lax.axis_index("blk")
    greet(
        tuple(more)
        + ({"seq": seq ^ 1}, {"seq": seq ^ 2})
        + tuple({"blk": lax.rem(b + k, count)} for k in range(1, count))
    )


def carry(copies, from_section, what):
    sending = lax.axis_index("section") == from_section
    for copy in copies:
        if what == "start":
            pl.when(sending)(copy.start)
        else:
            pl.when(sending)(copy.wait_send)
            pl.when(jnp.logical_not(sending))(copy.wait_recv)


def carried(sources, targets, sent, got):
    other = {"section": 1 - lax.axis_index("section")}
    return [
        remote(source, target, sent.at[n], got.at[n], other)
        for n, (source, target) in enumerate(zip(sources, targets))
    ]


def group_rows(ref, group, count):
    value = ref[pl.ds(group * count, count)]
    return value.reshape(value.shape[0] * value.shape[1], value.shape[2])


def group_span(group, count, block):
    size = count * block
    return pl.ds(pl.multiple_of(group * size, size), size)


def lane_turn(field_in, cosine, sine):
    half_dim, lanes = HEAD_DIM // 2, field_in.shape[-1]
    lane = lax.broadcasted_iota(jnp.int32, field_in.shape, 1)
    partner = jnp.where(
        lane < half_dim,
        pltpu.roll(field_in, lanes - half_dim, 1),
        pltpu.roll(field_in, half_dim, 1),
    )
    return field_in * cosine + partner * sine


def masked_scores(query, key, first_row, start):
    scores = back_product(query, key) * HEAD_DIM ** (-0.5)
    key_index = lax.broadcasted_iota(jnp.int32, scores.shape, 1)
    query_index = first_row + lax.broadcasted_iota(jnp.int32, scores.shape, 0)
    return jnp.where((key_index >= start) & (key_index <= query_index), scores, MASKED)


def normalise(field_in, gain_row):
    inv_root = lax.rsqrt(jnp.mean(field_in * field_in, axis=-1, keepdims=True) + EPS)
    return field_in * inv_root * gain_row


PAD = 128


GAINS = HEAD_DIM
OWN_PART = HEAD_DIM + 16


def load_weights(layer, attn, twin, out, attn_vm, out_vm, sems):
    on_key = lax.axis_index("seq") % 2 == 0
    own, other = attn.at[layer, pl.ds(OWN_PART, HEAD_DIM)], twin.at[layer]

    def part(source, n, rows):
        return pltpu.make_async_copy(source, attn_vm.at[pl.ds(n * PAD, rows)], sems.at[n])

    copies = [
        part(attn.at[layer, pl.ds(0, HEAD_DIM)], 0, HEAD_DIM),
        part(attn.at[layer, pl.ds(GAINS, 16)], 3, 16),
    ]
    if out is not None:
        copies.append(
            pltpu.make_async_copy(out.at[layer], out_vm.at[pl.ds(0, HEAD_DIM)], sems.at[4])
        )
    start_all(copies)

    @pl.when(on_key)
    def _():
        part(own, 1, HEAD_DIM).start()
        part(other, 2, HEAD_DIM).start()

    @pl.when(jnp.logical_not(on_key))
    def _():
        part(other, 1, HEAD_DIM).start()
        part(own, 2, HEAD_DIM).start()

    return copies + [part(other, 1, HEAD_DIM), part(other, 2, HEAD_DIM)]


def clear_pads(attn_vm, out_vm):
    empty = jnp.zeros((PAD - HEAD_DIM, attn_vm.shape[1]), jnp.bfloat16)
    for part in range(3):
        attn_vm[part * PAD + HEAD_DIM : (part + 1) * PAD] = empty
    out_vm[HEAD_DIM:PAD] = empty


def attention_rows(heads, log_total, start, size, tokens):
    for i in range(tokens // size):
        here, seen = slice(i * size, (i + 1) * size), slice(0, (i + 1) * size)
        scores = masked_scores(heads[0, here], heads[1, seen], i * size, start[here])
        row_top = jnp.max(scores, axis=-1, keepdims=True)
        weights = jnp.exp(scores - row_top)
        total = jnp.sum(weights, axis=-1, keepdims=True)
        log_total[here] = row_top + jnp.log(total)
        weights = (weights * (1.0 / total)).astype(jnp.bfloat16)
        heads[3, here] = product(weights, heads[2, seen]).astype(jnp.bfloat16)


def project_heads(normed, attn_vm, heads, span, cosine, sine):
    mixed = back_product(normed, attn_vm[0 : 3 * PAD])
    cos_rows, sin_rows = cosine[span], sine[span]
    heads[0, span] = lane_turn(mixed[:, :PAD], cos_rows, sin_rows).astype(jnp.bfloat16)
    heads[1, span] = lane_turn(mixed[:, PAD : 2 * PAD], cos_rows, sin_rows).astype(jnp.bfloat16)
    heads[2, span] = mixed[:, 2 * PAD :].astype(jnp.bfloat16)


def keep_group(partial, group, value, count):
    block = partial.shape[1]
    partial[pl.ds(group * count, count)] = value.astype(jnp.bfloat16).reshape(count, block, -1)


def gain_of(ref, row):
    return ref[3 * PAD : 3 * PAD + 16][row : row + 1].astype(jnp.float32)


def first_layer_kernel(count, *refs):
    refs = iter(refs)

    def take(n):
        return [next(refs) for _ in range(n)]

    pieces, w_gate, w_up, w_output, w_down, rows_in, grads_in, cosine, sine, start = take(10)
    attn, twin, gate_up, out, down, all_rows, wide_rows, grads_near, grads_side = take(9)
    hidden, result_out, normed_out, heads, log_total = take(5)
    raw_vm, normed_vm, rows_vm, partial, partial_two, grads_vm = take(6)
    attn_vm, out_vm, wide_vm, down_vm, units, normed_own, gain_vm = take(7)
    load_done, save_done, twin_sent, twin_got = take(4)
    spread_sems = take(5)
    first_sems, second_sems, grads_sems, side_sems = take(7), take(7), take(5), take(2)
    scatter_one, scatter_two = take(12), take(12)
    section = lax.axis_index("section")
    block, width = raw_vm.shape[1], raw_vm.shape[2]
    tokens = block * raw_vm.shape[0]
    size = count * block
    low, f32 = jnp.bfloat16, jnp.float32
    greet_group(count, ({"section": 1 - section},))
    spread = spread_steps(
        count, pieces, w_gate, w_up, w_output, w_down, attn, gate_up, out, down, *spread_sems
    )
    steps = gather_steps(count, rows_in, raw_vm, *first_sems)
    next(steps)
    next(spread)
    clear_pads(attn_vm, out_vm)
    for event in steps:
        if event == "line":
            advance(spread, 3)
    grads_across = remote(
        grads_in, grads_side, *side_sems, {"seq": lax.axis_index("seq") ^ 2}
    )
    grads_across.start()
    next(spread)
    pair = remote(
        attn.at[:, pl.ds(OWN_PART, HEAD_DIM)],
        twin,
        twin_sent,
        twin_got,
        {"seq": lax.axis_index("seq") ^ 1},
    )
    pair.start()
    pair.wait()
    gain_load = pltpu.make_async_copy(attn.at[1, pl.ds(GAINS, 16)], gain_vm, load_done.at[5])
    gain_load.start()
    wait_all(load_weights(0, attn, twin, None, attn_vm, out_vm, load_done) + [gain_load])
    for group in range(tokens // size):
        raw = raw_vm[group * count : (group + 1) * count].astype(f32)
        normed = normalise(raw, gain_of(attn_vm, 0)[None]).astype(low)
        normed_vm[group * count : (group + 1) * count] = normed
        span = slice(group * size, (group + 1) * size)
        project_heads(normed.reshape(size, width), attn_vm, heads, span, cosine, sine)
    saves = [pltpu.make_async_copy(normed_vm, all_rows, save_done.at[0])]
    saves[0].start()
    attention_rows(heads, log_total, start, size, tokens)
    next(spread)
    load = pltpu.make_async_copy(out.at[0], out_vm.at[pl.ds(0, HEAD_DIM)], load_done.at[4])
    load.start()
    load.wait()

    def project_out(group):
        mixed = heads[3, group_span(group, count, block)]
        keep_group(partial, group, product(mixed, out_vm[...]), count)

    def deliver(total):
        value = rows_in[...].astype(f32) + total
        hidden[...] = value
        normed_own[...] = normalise(value, gain_of(attn_vm, 1)).astype(low)

    def more():
        next(spread)

    run_with(scatter_steps(count, partial, deliver, *scatter_one, compute=project_out), [more] * 5)
    for number, event in enumerate(gather_steps(count, normed_own, rows_vm, *second_sems)):
        if number == 0:
            more()
    for _ in spread:
        pass
    loads = [
        pltpu.make_async_copy(gate_up.at[0], wide_vm, load_done.at[0]),
        pltpu.make_async_copy(down.at[0], down_vm, load_done.at[1]),
    ]
    start_all(loads)
    wait_all(loads)
    saves.append(pltpu.make_async_copy(rows_vm, wide_rows, save_done.at[1]))
    saves[1].start()

    def project_down(group):
        pre = product(group_rows(rows_vm, group, count), wide_vm[...])
        made = hidden_units(pre)
        units[group_span(group, count, block)] = made
        keep_group(partial_two, group, product(made, down_vm[...]), count)

    grad_steps = line_steps(count, grads_in, grads_vm, *grads_sems)
    next(grad_steps)

    def deliver_two(total):
        made = (hidden[...] + total).astype(low)
        result_out[...] = made
        gain = gain_vm[...][0:1].astype(f32)
        normed_out[...] = normalise(made.astype(f32), gain).astype(low)

    run_with(
        scatter_steps(count, partial_two, deliver_two, *scatter_two, compute=project_down),
        [functools.partial(advance, grad_steps, 1)] * 3,
    )
    for _ in grad_steps:
        pass
    saves.append(pltpu.make_async_copy(grads_vm, grads_near, save_done.at[2]))
    saves[2].start()
    grads_across.wait()
    wait_all(saves)


def spread_steps(
    count,
    pieces,
    w_gate,
    w_up,
    w_output,
    w_down,
    attn,
    gate_up,
    out,
    down,
    line_sent,
    line_got,
    cross_sent,
    cross_got,
    local_done,
):
    seq, b, section = lax.axis_index("seq"), lax.axis_index("blk"), lax.axis_index("section")
    seq_count = lax.axis_size("seq")
    other = {"section": 1 - section}
    rows, lanes = w_gate.shape[0], gate_up.shape[2] // 2
    turns = tuple(range(count // 2, 0, -1)) + tuple(range(count // 2 + 1, count))

    def source(kind, j):
        if kind == 0:
            return pieces.at[j]
        weight = w_gate if kind == 1 else w_up
        return weight.at[:, pl.ds(pl.multiple_of((j * seq_count + seq) * lanes, lanes), lanes)]

    def target(kind, j):
        if kind == 0:
            return attn.at[section, :, pl.ds(pl.multiple_of(j * rows, rows), rows)]
        return gate_up.at[
            section, pl.ds(pl.multiple_of(j * rows, rows), rows), pl.ds((kind - 1) * lanes, lanes)
        ]

    def along_line(kind, k):
        j = lax.rem(b + k, count)
        return remote(
            source(kind, j),
            target(kind, b),
            line_sent.at[kind, k],
            line_got.at[kind, k],
            {"blk": j},
        )

    def across(kind, j, slot, begin=None):
        spot = target(kind, j)
        return remote(
            spot if begin is None else begin,
            spot,
            cross_sent.at[kind, slot],
            cross_got.at[kind, slot],
            other,
        )

    def own_rows(kind):
        weight, place = (w_output, out) if kind == 3 else (w_down, down)
        size = place.shape[1]
        begin = weight.at[pl.ds(pl.multiple_of(seq * size, size), size)]
        spot = place.at[section]
        return (
            remote(begin, spot, cross_sent.at[kind, 0], cross_got.at[kind, 0], other),
            pltpu.make_async_copy(begin, spot, local_done.at[kind]),
        )

    def own_piece(kind):
        return (
            across(kind, b, 0, source(kind, b)),
            pltpu.make_async_copy(source(kind, b), target(kind, b), local_done.at[kind]),
        )

    def forward(kind, k):
        j = lax.rem(b + count - k, count)
        settled(target(kind, j), line_got.at[kind, k], True)
        across(kind, j, k).start()

    def arrived(kind):
        if kind > 2:
            wait_all(own_rows(kind))
            return
        for k in range(count):
            settled(target(kind, 0), cross_got.at[kind, k], True)
            settled(target(kind, 0), cross_sent.at[kind, k], False)
            if k:
                settled(target(kind, 0), line_sent.at[kind, k], False)
        pltpu.make_async_copy(source(kind, b), target(kind, b), local_done.at[kind]).wait()

    for k in turns:
        along_line(0, k).start()
    start_all(own_piece(0))
    yield
    for k in turns:
        forward(0, k)
        yield
    start_all(own_rows(3))
    for kind in (1, 2):
        for k in turns:
            along_line(kind, k).start()
    arrived(0)
    start_all(own_piece(1) + own_piece(2) + own_rows(4))
    yield
    arrived(3)
    yield
    for kind in (1, 2):
        for k in turns:
            forward(kind, k)
            yield
    for kind in (1, 2, 4):
        arrived(kind)


def start_all(copies):
    for copy in copies:
        copy.start()


def wait_all(copies):
    for copy in copies:
        copy.wait()


def gated(pre):
    half = pre.shape[1] // 2
    gate, up = pre[:, :half], pre[:, half:]
    sigma = jax.nn.sigmoid(gate)
    return gate, up, sigma


def hidden_units(pre):
    gate, up, sigma = gated(pre)
    return (gate * sigma * up).astype(jnp.bfloat16)


def store_gate_grads(place, span, grad_act, pre):
    gate, up, sigma = gated(pre)
    half = gate.shape[1]
    place[span, 0:half] = (grad_act * up * sigma * (1.0 + gate * (1.0 - sigma))).astype(
        jnp.bfloat16
    )
    place[span, half : 2 * half] = (grad_act * (gate * sigma)).astype(jnp.bfloat16)


def wide_grads(rows_vm, pre_grads, units, grads_vm, wide_grad, down_grad):
    tokens = pre_grads.shape[0]
    width = rows_vm.shape[2]
    step = width // 4

    def wide_part(n):
        cut = slice(n * step, (n + 1) * step)
        rows = rows_vm[:, :, cut].reshape(tokens, step)
        wide_grad[cut] = weight_term(rows, pre_grads[...]).astype(jnp.bfloat16)

    def down_part(n):
        cut = slice(n * 2 * step, (n + 1) * 2 * step)
        rows = grads_vm[:, :, cut].reshape(tokens, 2 * step)
        down_grad[:, cut] = weight_term(units[...], rows).astype(jnp.bfloat16)

    return [functools.partial(wide_part, n) for n in range(4)] + [
        functools.partial(down_part, n) for n in range(2)
    ]


def mlp_grad_sent(total, hidden, grads_own, gain, branch_out, grad_hidden_out, gain_out):
    field_in = hidden[...]
    inv_root = lax.rsqrt(jnp.mean(field_in * field_in, axis=-1, keepdims=True) + EPS)
    part, terms = rms_backward(field_in, gain[...], inv_root, total)
    grad_hidden = grads_own[...].astype(jnp.float32) + part
    grad_hidden_out[...] = grad_hidden
    branch_out[...] = grad_hidden.astype(jnp.bfloat16)
    gain_out[...] = jnp.broadcast_to(jnp.sum(terms, axis=0, keepdims=True), gain_out.shape)


class Parts:
    pass


def attn_back_refs(take, attn_grad=None, out_grad=None):
    r = Parts()
    r.branch_vm, r.rows_vm, r.heads, r.attn_vm, r.out_vm, r.mixed_grads, r.probs = take(7)
    r.key_grads, r.value_grads, r.joint, r.partial, r.load_done = take(5)
    r.gather_sems = take(7)
    r.scatter_refs = take(12)
    return r


def attn_back_body(count, layer, r, ins, outs, background, fillers, gathered=None):
    branch_in, grad_hidden, x_own, all_rows, heads_kept, log_total, attn, twin, out = ins[:9]
    cosine, sine, start, gain = ins[9:]
    grad_out, gain_out, attn_grad, out_grad = outs
    branch_vm, rows_vm, heads, attn_vm, out_vm = r.branch_vm, r.rows_vm, r.heads, r.attn_vm, r.out_vm
    mixed_grads, probs, key_grads, value_grads = r.mixed_grads, r.probs, r.key_grads, r.value_grads
    joint, partial, load_done = r.joint, r.partial, r.load_done
    block = rows_vm.shape[1]
    size = count * block
    tokens = block * rows_vm.shape[0]
    low, f32 = jnp.bfloat16, jnp.float32
    scale = HEAD_DIM ** (-0.5)
    steps = gather_steps(count, branch_in, branch_vm, *r.gather_sems)
    next(steps)
    background()
    loads = []
    if layer is not None:
        clear_pads(attn_vm, out_vm)
        loads = load_weights(layer, attn, twin, out, attn_vm, out_vm, load_done)
        kept = [
            pltpu.make_async_copy(heads_kept, heads, load_done.at[5]),
            pltpu.make_async_copy(all_rows, rows_vm, load_done.at[6]),
        ]
        start_all(kept)
        loads += kept
    key_grads[...] = jnp.zeros_like(key_grads)
    value_grads[...] = jnp.zeros_like(value_grads)
    wait_all(loads)

    def spans(i):
        return slice(i * size, (i + 1) * size), slice(0, (i + 1) * size)

    def weigh(i):
        here, seen = spans(i)
        scores = masked_scores(heads[0, here], heads[1, seen], i * size, start[here])
        probs[here, seen] = jnp.exp(scores - log_total[here])

    def project(group):
        value = back_product(group_rows(branch_vm, group, count), out_vm[...])
        mixed_grads[group_span(group, count, block)] = value.astype(low)

    for number, event in enumerate(steps):
        if number < 2:
            weigh(2 * number)
            weigh(2 * number + 1)
        group = group_of(event)
        if group is not None:
            project(group)
    if gathered:
        gathered()
    for i in reversed(range(tokens // size)):
        here, seen = spans(i)
        weights = probs[here, seen]
        grads = mixed_grads[here]
        grad_weights = back_product(grads, heads[2, seen])
        centre = jnp.sum(weights * grad_weights, axis=-1, keepdims=True)
        grad_scores = (weights * (grad_weights - centre)).astype(low)
        query_grad = (product(grad_scores, heads[1, seen]) * scale).astype(low).astype(f32)
        joint[here, 0:PAD] = lane_turn(query_grad, cosine[here], -sine[here]).astype(low)
        key_grads[seen] += weight_term(grad_scores, heads[0, here])
        value_grads[seen] += weight_term(weights.astype(low), grads)
        key_grad = (key_grads[here] * scale).astype(low).astype(f32)
        joint[here, PAD : 2 * PAD] = lane_turn(key_grad, cosine[here], -sine[here]).astype(low)
        joint[here, 2 * PAD : 3 * PAD] = value_grads[here].astype(low)

    def project_back(group):
        value = product(joint[group_span(group, count, block)], attn_vm[0 : 3 * PAD])
        partial[pl.ds(group * count, count)] = value.astype(low).reshape(count, block, -1)

    def attn_part(part):
        rows = rows_vm[...].reshape(tokens, rows_vm.shape[2])
        value = weight_term(joint[:, part * PAD : (part + 1) * PAD], rows)
        attn_grad[part * HEAD_DIM : (part + 1) * HEAD_DIM] = value[0:HEAD_DIM].astype(low)

    def out_part():
        rows = branch_vm[...].reshape(tokens, branch_vm.shape[2])
        out_grad[...] = weight_term(heads[3], rows)[0:HEAD_DIM].astype(low)

    def deliver(total):
        field_in = x_own[...].astype(f32)
        inv_root = lax.rsqrt(jnp.mean(field_in * field_in, axis=-1, keepdims=True) + EPS)
        part, terms = rms_backward(field_in, gain[...], inv_root, total)
        grad_out[...] = (grad_hidden[...] + part).astype(low)
        gain_out[...] = jnp.broadcast_to(jnp.sum(terms, axis=0, keepdims=True), gain_out.shape)

    run_with(
        scatter_steps(count, partial, deliver, *r.scatter_refs, compute=project_back),
        [functools.partial(run_all, [functools.partial(attn_part, n) for n in range(3)] + [out_part])]
        + fillers,
    )


def middle_kernel(count, *refs):
    refs = iter(refs)

    def take(n):
        return [next(refs) for _ in range(n)]

    rows_in, between, grads_side, cosine, sine, start, attn, twin, out = take(9)
    grads_near, gate_up, down, grads_own, hidden_one, wide_rows = take(6)
    gain_mlp_two, gain_attn_two, gain_mlp_one = take(3)
    hidden, ahead, grad_between, branch_out, grad_hidden_out = take(5)
    mlp_two_sum, attn_two_sum, mlp_one_sum = take(3)
    wide_two, down_two, attn_two, out_two, wide_one, down_one = take(6)
    carried_to = take(4)
    rows_two, grads_vm, partial, wide_vm, down_vm = take(5)
    log_total, units, pre_vm, pre_grads, normed_own, branch_own, grad_hidden = take(7)
    load_done, carry_sent, carry_got = take(3)
    line_sems = take(5)
    r = attn_back_refs(take)
    rows_one, heads, attn_vm, out_vm, partial_back = (
        r.rows_vm,
        r.heads,
        r.attn_vm,
        r.out_vm,
        r.partial,
    )
    blocks, block = rows_one.shape[0], rows_one.shape[1]
    size, tokens, half = count * block, blocks * block, blocks // 2
    near = lax.axis_index("seq") // 2 * half
    greet_group(count, ({"section": 1 - lax.axis_index("section")},))
    steps = gather_steps(count, rows_in, rows_one, *r.gather_sems)
    next(steps)
    clear_pads(attn_vm, out_vm)
    loads = load_weights(1, attn, twin, out, attn_vm, out_vm, r.load_done)
    wide_loads = [
        pltpu.make_async_copy(gate_up.at[1], wide_vm, load_done.at[0]),
        pltpu.make_async_copy(down.at[1], down_vm, load_done.at[1]),
        pltpu.make_async_copy(grads_near, grads_vm.at[pl.ds(near, half)], load_done.at[2]),
    ]
    start_all(wide_loads)
    for event in steps:
        if event == "line":
            wait_all(loads)
        group = group_of(event)
        if group is not None:
            span = group_span(group, count, block)
            normed = group_rows(rows_one, group, count)
            project_heads(normed, attn_vm, heads, span, cosine, sine)
    grad_steps = line_steps(count, grads_side, grads_vm, *line_sems, offset=half - near)
    next(grad_steps)
    attention_rows(heads, log_total, start, size, tokens)

    def project_out(group):
        mixed = heads[3, group_span(group, count, block)]
        keep_group(partial, group, product(mixed, out_vm[...]), count)

    def deliver(total):
        value = between[...].astype(jnp.float32) + total
        hidden[...] = value
        normed_own[...] = normalise(value, gain_of(attn_vm, 1)).astype(jnp.bfloat16)

    run_with(
        scatter_steps(count, partial, deliver, *r.scatter_refs, compute=project_out),
        [functools.partial(advance, grad_steps, 1)] * 3,
    )
    steps = gather_steps(count, normed_own, rows_two, *r.gather_sems)
    next(steps)
    for _ in grad_steps:
        pass
    wait_all(wide_loads)

    def through(group):
        span = group_span(group, count, block)
        pre = product(group_rows(rows_two, group, count), wide_vm[...])
        units[span] = hidden_units(pre)
        grad_act = back_product(group_rows(grads_vm, group, count), down_vm[...])
        store_gate_grads(pre_grads, span, grad_act, pre)
        keep_group(partial_back, group, back_product(pre_grads[span], wide_vm[...]), count)

    for event in steps:
        group = group_of(event)
        if group is not None:
            through(group)

    def project_down(group):
        value = product(units[group * size : (group + 1) * size], down_vm[...])
        partial[group * count : (group + 1) * count] = value.astype(jnp.bfloat16).reshape(
            count, block, -1
        )

    def deliver_two(total):
        mlp_grad_sent(
            total, hidden, grads_own, gain_mlp_two, branch_own, grad_hidden, mlp_two_sum
        )

    fillers = wide_grads(rows_two, pre_grads, units, grads_vm, wide_two, down_two)
    fillers += [functools.partial(project_down, group) for group in range(4)]
    run_with(
        scatter_steps(count, partial_back, deliver_two, *r.scatter_refs),
        [functools.partial(run_all, fillers[n::4]) for n in range(4)],
    )
    save = pltpu.make_async_copy(partial, ahead, load_done.at[3])
    save.start()
    copies = carried(
        (wide_two, down_two, attn_two, out_two), carried_to, carry_sent, carry_got
    )

    def background():
        carry(copies[:2], 0, "start")
        wide_loads[0] = pltpu.make_async_copy(gate_up.at[0], wide_vm, load_done.at[0])
        wide_loads[1] = pltpu.make_async_copy(down.at[0], down_vm, load_done.at[1])
        wide_loads[2] = pltpu.make_async_copy(wide_rows, rows_two, load_done.at[2])
        start_all(wide_loads)

    attn_back_body(
        count,
        None,
        r,
        (branch_own, grad_hidden, between, None, None, log_total, None, None, None)
        + (cosine, sine, start, gain_attn_two),
        (grad_between, attn_two_sum, attn_two, out_two),
        background,
        [],
    )
    carry(copies[2:], 0, "start")
    steps = gather_steps(count, grad_between, grads_vm, *r.gather_sems)
    next(steps)
    wait_all(wide_loads)

    def again(group):
        span = group_span(group, count, block)
        pre = product(group_rows(rows_two, group, count), wide_vm[...])
        pre_vm[span] = pre
        units[span] = hidden_units(pre)

    def through_one(group):
        span = group_span(group, count, block)
        grad_act = back_product(group_rows(grads_vm, group, count), down_vm[...])
        store_gate_grads(pre_grads, span, grad_act, pre_vm[span])
        keep_group(partial_back, group, back_product(pre_grads[span], wide_vm[...]), count)

    for number, event in enumerate(steps):
        if number < 2:
            again(2 * number)
            again(2 * number + 1)
        group = group_of(event)
        if group is not None:
            through_one(group)

    def deliver_one(total):
        mlp_grad_sent(
            total, hidden_one, grad_between, gain_mlp_one, branch_out, grad_hidden_out, mlp_one_sum
        )

    run_with(
        scatter_steps(count, partial_back, deliver_one, *r.scatter_refs),
        wide_grads(rows_two, pre_grads, units, grads_vm, wide_one, down_one),
    )
    carry(copies, 0, "wait")
    save.wait()


def last_kernel(count, *refs):
    refs = iter(refs)

    def take(n):
        return [next(refs) for _ in range(n)]

    ins = take(13)
    wide_one, down_one, attn_two, out_two, wide_two, down_two = take(6)
    wide_from_one, down_from_one, attn_from_one, out_from_one, ahead = take(5)
    gain_mlp_one, gain_attn_two, gain_mlp_two, between, grad_between, hidden = take(6)
    attn, out, gate, up, down, gains_out, rows_out, grads_out = take(8)
    final, grad_start = take(2)
    attn_grad, out_grad, gain_attn_one, gains = take(4)
    attn_own, out_own, wide_own, down_own, attn_in, out_in, wide_in, down_in = take(8)
    attn_slot, wide_slot = take(2)
    gain_in, gain_sum, gain_line, gain_part, gain_side, gain_core = take(6)
    load_done, cross_sent, cross_got, line_sent, line_got = take(5)
    side_sent, side_got, core_sent, core_got, local_done, small_sent, small_got = take(7)
    ahead_refs = take(13)
    r = attn_back_refs(take)
    seq, b, section = lax.axis_index("seq"), lax.axis_index("blk"), lax.axis_index("section")
    at_first = section == 0
    at_second = jnp.logical_not(at_first)
    core, side, other = {"seq": seq ^ 1}, {"seq": seq ^ 2}, {"section": 1 - section}
    greet((other, core, side) + tuple({"blk": lax.rem(b + k, count)} for k in range(1, count)))
    rows, lanes = attn.shape[2], gate.shape[1] // (4 * count)
    turns = tuple(range(count // 2, 0, -1)) + tuple(range(count // 2 + 1, count)) + (0,)
    f32, low = jnp.float32, jnp.bfloat16

    def piece_rows(kind, j):
        if kind == 0:
            return (slice(None), pl.ds(pl.multiple_of(j * rows, rows), rows))
        return (pl.ds(pl.multiple_of(j * rows, rows), rows),)

    pairs = {
        0: (attn_own, attn_in, attn_grad),
        1: (wide_own, wide_in, wide_one),
        2: (out_own, out_in, out_grad),
        3: (down_own, down_in, down_one),
    }
    sources = {
        0: (attn_grad, attn_two, attn_from_one),
        1: (wide_one, wide_two, wide_from_one),
        2: (out_grad, out_two, out_from_one),
        3: (down_one, down_two, down_from_one),
    }

    def load(kind):
        one, two, from_one = sources[kind]
        own, held, _ = pairs[kind]

        @pl.when(at_first)
        def _():
            pltpu.make_async_copy(one, own, load_done.at[kind, 0]).start()

        @pl.when(at_second)
        def _():
            pltpu.make_async_copy(two, own, load_done.at[kind, 0]).start()
            pltpu.make_async_copy(from_one, held, load_done.at[kind, 1]).start()

    def loaded(kind):
        own, held, _ = pairs[kind]
        pltpu.make_async_copy(own, own, load_done.at[kind, 0]).wait()
        pl.when(at_second)(pltpu.make_async_copy(held, held, load_done.at[kind, 1]).wait)

    def cross(kind, k):
        _, held, begin = pairs[kind]
        index = piece_rows(kind, lax.rem(b + k, count)) if kind < 2 else (slice(None),)
        return remote(
            begin.at[index], held.at[index], cross_sent.at[kind, k], cross_got.at[kind, k], other
        )

    def add_up(kind, k):
        own, held, _ = pairs[kind]
        pl.when(at_first)(cross(kind, k).wait_recv)
        index = piece_rows(kind, lax.rem(b + k, count)) if kind < 2 else (slice(None),)
        held[index] = (own[index].astype(f32) + held[index].astype(f32)).astype(low)

    def along_line(kind, k):
        j = lax.rem(b + k, count)
        slot = (attn_slot if kind == 0 else wide_slot).at[k]
        source = pairs[kind][1].at[piece_rows(kind, j)]
        return remote(source, slot, line_sent.at[kind, k], line_got.at[kind, k], {"blk": j})

    def places(kind, k, of_seq):
        if kind == 2:
            size = out_in.shape[0]
            return [out.at[pl.ds(pl.multiple_of(of_seq * size, size), size)]]
        if kind == 3:
            size = down_in.shape[0]
            return [down.at[pl.ds(pl.multiple_of(of_seq * size, size), size)]]
        head = lax.rem(b + count - k, count) * 4 + of_seq
        if kind == 0:
            return [attn.at[head]]
        column = pl.ds(pl.multiple_of(head * lanes, lanes), lanes)
        return [gate.at[:, column], up.at[:, column]]

    def numbered(kind, k, of_seq):
        base = {0: k, 1: count + 2 * k, 2: 3 * count, 3: 3 * count + 1}[kind]
        return [(base + n, spot) for n, spot in enumerate(places(kind, k, of_seq))]

    def made(kind, k):
        if kind > 1:
            return [pairs[kind][1].at[:]]
        if kind == 0:
            return [attn_in.at[piece_rows(0, b)] if k == 0 else attn_slot.at[k]]
        whole = (lambda cut: wide_in.at[piece_rows(1, b) + (cut,)]) if k == 0 else (
            lambda cut: wide_slot.at[k, :, cut]
        )
        return [whole(pl.ds(0, lanes)), whole(pl.ds(lanes, lanes))]

    def sends(kind, k):
        found = []
        for (n, spot), begin in zip(numbered(kind, k, seq), made(kind, k)):
            found.append(
                (
                    remote(begin, spot, side_sent.at[n], side_got.at[n], side),
                    remote(begin, spot, core_sent.at[0, n], core_got.at[0, n], core),
                    pltpu.make_async_copy(begin, spot, local_done.at[n]),
                )
            )
        return found

    def publish(kind, k):
        for copies in sends(kind, k):
            for copy in copies:
                copy.start()

    def passes(kind, k):
        return [
            remote(spot, spot, core_sent.at[1, n], core_got.at[1, n], core)
            for n, spot in numbered(kind, k, seq ^ 2)
        ]

    def from_line(kind, k):
        along_line(kind, k).wait_recv()
        publish(kind, k)

    def from_side(kind, k):
        for n, spot in numbered(kind, k, seq ^ 2):
            settled(spot, side_got.at[n], True)
        for copy in passes(kind, k):
            copy.start()

    def small(n, source, slot, device):
        return remote(source, slot, small_sent.at[n], small_got.at[n], device)

    swap_rest = small(4 + count, between, rows_out.at[section], other)
    swap_final = small(4 + count, final, rows_out.at[section], other)
    swap_between = small(0, grad_between, grads_out.at[section], other)
    swap_start = small(0, grad_start, grads_out.at[section], other)
    pl.when(at_second)(swap_rest.start)
    pl.when(at_first)(swap_between.start)
    wide_turns = [(1, k) for k in turns]
    crossings = wide_turns + [(0, k) for k in turns] + [(2, 0), (3, 0)]

    def begin_cross(those):
        for kind, k in those:
            pl.when(at_second)(cross(kind, k).start)

    def background():
        begin_cross(crossings[:count])
        load(1)
        load(3)

    def deliver(total):
        final[...] = (hidden[...] + total).astype(low)
        pl.when(at_first)(swap_final.start)
        rows_out[section] = jnp.where(at_first, between[...], final[...])

    def later():
        load(0)
        load(2)
        begin_cross(crossings[count:])

    def share(n):
        if n == 0:
            loaded(1)
        add_up(1, turns[n])
        along_line(1, turns[n]).start()

    def gathered():
        share(0)
        share(1)

    def early():
        add_up(1, 0)
        publish(1, 0)

    ahead_steps = line_first_steps(count, ahead, deliver, *ahead_refs)
    attn_back_body(
        count,
        0,
        r,
        ins,
        (grad_start, gain_attn_one, attn_grad, out_grad),
        background,
        [later, functools.partial(share, 2), early],
        gathered,
    )
    pl.when(at_second)(swap_start.start)
    grads_out[section] = jnp.where(at_first, grad_start[...], grad_between[...])
    gains[0, 0:4] = gain_attn_one[0:4]
    gains[0, 4:8] = gain_mlp_one[4:8]
    gains[1, 0:4] = gain_attn_two[0:4]
    gains[1, 4:8] = gain_mlp_two[4:8]
    gain_cross = small(1, gains.at[1 - section], gain_in.at[:], other)
    gain_cross.start()

    def gain_piece(j):
        return gain_sum.at[:, pl.ds(pl.multiple_of(j * rows, rows), rows)]

    def gain_send(k):
        j = lax.rem(b + k, count)
        return small(3 + k, gain_piece(j), gain_line.at[k], {"blk": j})

    loaded(0)
    for k in turns[:-1]:
        add_up(0, k)
        along_line(0, k).start()
    from_line(1, turns[0])
    add_up(0, 0)
    publish(0, 0)
    from_line(1, turns[1])
    from_side(1, 0)
    loaded(2)
    add_up(2, 0)
    publish(2, 0)
    from_line(1, turns[2])
    next(ahead_steps)
    from_side(1, turns[0])
    from_side(0, 0)
    loaded(3)
    add_up(3, 0)
    publish(3, 0)
    for k in turns[:-1]:
        from_line(0, k)
    from_side(1, turns[1])
    gain_cross.wait_recv()
    gain_sum[...] = gains[section] + gain_in[...]
    for k in range(1, count):
        gain_send(k).start()
    advance(ahead_steps, 2)
    from_side(2, 0)
    from_side(1, turns[2])
    for k in range(1, count):
        gain_send(k).wait_recv()
    gain_part[...] = gain_sum[:, pl.ds(pl.multiple_of(b * rows, rows), rows)]
    for k in range(1, count):
        gain_part[...] += gain_line[k]
    gain_to_side = small(2, gain_part.at[:], gain_side.at[:], side)
    gain_to_side.start()
    advance(ahead_steps, 4)
    from_side(3, 0)
    gain_to_side.wait_recv()
    gain_side[...] += gain_part[...]
    gain_to_core = small(3, gain_side.at[:], gain_core.at[:], core)
    gain_to_core.start()
    for _ in ahead_steps:
        pass
    for k in turns[:-1]:
        from_side(0, k)
    gain_to_core.wait_recv()
    gains_out[...] = gain_side[...] + gain_core[...]
    every = [(0, k) for k in range(count)] + [(1, k) for k in range(count)] + [(2, 0), (3, 0)]
    for kind, k in every:
        pl.when(at_second)(cross(kind, k).wait_send)
        if kind < 2 and k:
            along_line(kind, k).wait_send()
        for to_side, to_core, local in sends(kind, k):
            to_side.wait_send()
            to_core.wait_send()
            local.wait()
        for copy in passes(kind, k):
            copy.wait_send()
        for half, of_seq in ((0, seq ^ 1), (1, seq ^ 3)):
            for n, spot in numbered(kind, k, of_seq):
                settled(spot, core_got.at[half, n], True)
    swap_between.wait()
    swap_rest.wait()
    gain_cross.wait_send()
    for k in range(1, count):
        gain_send(k).wait_send()
    gain_to_side.wait_send()
    gain_to_core.wait_send()


def widen_kernel(pieces, attn, out, gate, up, down, query, key, value, out_f, gate_f, up_f, down_f):
    f32 = jnp.float32
    out_f[...] = out[...].astype(f32)
    gate_f[...] = gate[...].astype(f32)
    up_f[...] = up[...].astype(f32)
    down_f[...] = down[...].astype(f32)

    @pl.when(pl.program_id(0) < pieces)
    def _():
        parts, _, lanes = attn.shape
        copies = HEADS // KV_HEADS

        def heads(n):
            return attn[:, n * HEAD_DIM : (n + 1) * HEAD_DIM].astype(f32)

        query[...] = heads(0).reshape(parts * HEAD_DIM, lanes).T
        for n, place in ((1, key), (2, value)):
            total = heads(n).reshape(parts // copies, copies, HEAD_DIM, lanes).sum(1)
            place[...] = total.reshape(parts // copies * HEAD_DIM, lanes).T


def widen(attn, out, gate, up, down):
    f32 = jnp.float32
    parts, heads, rows = attn.shape
    lanes = 128
    pieces = rows // lanes
    steps = 8
    width = parts * HEAD_DIM
    narrow = width * KV_HEADS // HEADS

    def rows_of(array):
        return pl.BlockSpec((array.shape[0] // steps, array.shape[1]), lambda i: (i, 0))

    def turned(columns):
        return pl.BlockSpec((lanes, columns), lambda i: (jnp.minimum(i, pieces - 1), 0))

    flat = [out, gate, up, down]
    taken = pl.BlockSpec((parts, heads, lanes), lambda i: (0, 0, jnp.minimum(i, pieces - 1)))
    shapes = [(rows, width), (rows, narrow), (rows, narrow)] + [array.shape for array in flat]
    return pl.pallas_call(
        functools.partial(widen_kernel, pieces),
        grid=(steps,),
        out_shape=[jax.ShapeDtypeStruct(shape, f32) for shape in shapes],
        in_specs=[taken] + [rows_of(array) for array in flat],
        out_specs=[turned(width), turned(narrow), turned(narrow)]
        + [rows_of(array) for array in flat],
        compiler_params=pltpu.CompilerParams(vmem_limit_bytes=48 * 2**20),
        name="widen_gradients",
    )(attn, out, gate, up, down)


def last_layer(count, operands, like, back_scratch):
    attn, out, wide, down, block, width, gain_rows = like
    low, f32 = jnp.bfloat16, jnp.float32
    seq_count = lax.axis_size("seq")
    rows = wide[0] // count
    lanes = wide[1] // 2
    parts = seq_count * count
    dma = pltpu.SemaphoreType.DMA
    vmem = pltpu.VMEM
    sends = 3 * count + 2
    heads = attn[0]
    small = (gain_rows, rows)

    def slots(*places):
        return vmem(places + (block, width), low)

    outputs = [
        ((parts, heads, rows), low, False),
        ((out[0] * seq_count, out[1]), low, False),
        ((rows, lanes * parts), low, False),
        ((rows, lanes * parts), low, False),
        ((down[0] * seq_count, down[1]), low, False),
        (small, f32, True),
        ((2, block, width), low, True),
        ((2, block, width), low, True),
    ]
    scratch = (
        [vmem((block, width), low), vmem((block, width), low)]
        + [vmem(attn, low), vmem(out, low), vmem((gain_rows, width), f32)]
        + [vmem((2, gain_rows, width), f32)]
        + [vmem(shape, low) for shape in (attn, out, wide, down)] * 2
        + [vmem((count, heads, rows), low), vmem((count, rows, 2 * lanes), low)]
        + [vmem((gain_rows, width), f32)] * 2
        + [vmem((count,) + small, f32)]
        + [vmem(small, f32)] * 3
        + [dma((4, 2)), dma((4, count)), dma((4, count)), dma((2, count)), dma((2, count))]
        + [dma((sends,)), dma((sends,)), dma((2, sends)), dma((2, sends)), dma((sends,))]
        + [dma((5 + count,)), dma((5 + count,))]
        + [slots(2, count), slots(2, count), slots(2, 2, count), slots(2, count), slots(1)]
        + [vmem((block, width), f32)]
        + [dma((2, count)), dma((2, count)), dma((2, count)), dma((2, count))]
        + [dma((2, 2, count)), dma, dma]
        + back_scratch
    )
    attn, out, gate, up, down, gains, rows_out, grads_out = call_kernel(
        functools.partial(last_kernel, count), "last_layer_back", 3, operands, outputs, scratch
    )
    query, key, value, out, gate, up, down = widen(attn, out, gate, up, down)
    return rows_out, grads_out, gains, query, key, value, out, gate, up, down


def call_kernel(kernel, name, number, operands, outputs, scratch):
    in_vmem = pl.BlockSpec(memory_space=pltpu.VMEM)
    anywhere = pl.BlockSpec(memory_space=pl.ANY)
    return pl.pallas_call(
        kernel,
        out_shape=[jax.ShapeDtypeStruct(shape, dtype) for shape, dtype, _ in outputs],
        in_specs=[in_vmem if near else anywhere for _, near in operands],
        out_specs=[in_vmem if near else anywhere for _, _, near in outputs],
        scratch_shapes=scratch,
        compiler_params=pltpu.CompilerParams(
            collective_id=number, has_side_effects=True, vmem_limit_bytes=56 * 2**20
        ),
        name=name,
    )(*[array for array, _ in operands])


def sliced_heads(local_shards):
    seq_index, seq_count = lax.axis_index("seq"), lax.axis_size("seq")
    count = lax.axis_size("blk")
    gain_attn, w_query, w_key, w_value, _, gain_mlp, _, _, _ = local_shards
    rows = w_query.shape[0]

    def heads_of(weight, per_blk, place):
        head = jnp.arange(count)[:, None] * per_blk + place
        column = (head * HEAD_DIM + jnp.arange(HEAD_DIM)).reshape(-1)
        chosen = jnp.arange(weight.shape[1])[:, None] == column[None, :]
        taken = lax.dot_general(
            chosen.astype(jnp.bfloat16),
            weight,
            (((0,), (1,)), ((), ())),
            preferred_element_type=jnp.float32,
        )
        return taken.astype(jnp.bfloat16).reshape(count, HEAD_DIM, rows)

    kv_per_blk = KV_HEADS // count
    kv_place = seq_index * kv_per_blk // seq_count
    gains = jnp.concatenate(
        [jnp.stack([gain_attn, gain_mlp]), jnp.zeros((14, rows), jnp.bfloat16)]
    )
    return jnp.concatenate(
        [
            heads_of(w_query, seq_count, seq_index),
            jnp.broadcast_to(gains[None], (count,) + gains.shape),
            heads_of(jnp.where(seq_index % 2 == 0, w_key, w_value), kv_per_blk, kv_place),
        ],
        axis=1,
    )


def head_shards(inputs, cotangent, doc_lengths, *params):
    section = lax.axis_index("section")
    at_first = section == 0
    seq_count, count = lax.axis_size("seq"), lax.axis_size("blk")
    low, f32 = jnp.bfloat16, jnp.float32
    vmem, dma = pltpu.VMEM, pltpu.SemaphoreType.DMA
    block, width = inputs.shape[2], inputs.shape[3]
    blocks = seq_count * count
    tokens = blocks * block
    rows_own = lax.dynamic_index_in_dim(inputs, section, 0, keepdims=False)[0]
    grads_own = lax.dynamic_index_in_dim(cotangent, section, 0, keepdims=False)[0]
    local = tuple(weight[0] for weight in params)
    pieces = sliced_heads(local)
    w_output, w_gate, w_up, w_down = local[4], local[6], local[7], local[8]
    rows = w_gate.shape[0]
    lanes = w_gate.shape[1] // blocks
    out_rows, down_rows = w_output.shape[0] // seq_count, w_down.shape[0] // seq_count
    lengths = lax.dynamic_index_in_dim(doc_lengths, section, 0, keepdims=False)[0]
    token_index = jnp.arange(tokens, dtype=jnp.int32)
    _, position = doc_info(lengths, token_index)
    start = (token_index - position)[:, None]
    half_dim = HEAD_DIM // 2
    lane = jnp.arange(PAD)
    frequency = THETA ** (-2.0 * (lane % half_dim).astype(f32) / HEAD_DIM)
    angles = position.astype(f32)[:, None] * frequency[None, :]
    sign = jnp.where(lane < half_dim, -1.0, 1.0).astype(f32)
    cosine = jnp.where(lane < HEAD_DIM, jnp.cos(angles), 0.0)
    sine = jnp.where(lane < HEAD_DIM, jnp.sin(angles) * sign, 0.0)

    def all_blocks():
        return vmem((blocks, block, width), low)

    def scatter():
        return scatter_scratch(count, block, width)

    half_blocks = vmem((blocks // 2, block, width), low)
    half = ((blocks // 2, block, width), low, False)
    own_low, own_wide = ((block, width), low, True), ((block, width), f32, True)
    every = ((blocks, block, width), low, False)
    gain_rows = ((8, width), f32, True)
    weights_vm = [vmem((3 * PAD + 16, width), low), vmem((PAD, width), low)]
    wide_vm, down_vm = vmem((width, 2 * lanes), low), vmem((down_rows, width), low)
    tables = [(cosine, True), (sine, True), (start, True)]
    (
        attn,
        twin,
        gate_up,
        out,
        down,
        rows_one,
        wide_rows_one,
        grads_near,
        grads_side,
        hidden_one,
        between,
        normed,
        heads_one,
        total_one,
    ) = call_kernel(
        functools.partial(first_layer_kernel, count),
        "first_layer",
        2,
        [(array, False) for array in (pieces, w_gate, w_up, w_output, w_down)]
        + [(rows_own, True), (grads_own, True)]
        + tables,
        [
            ((2, pieces.shape[1], width), low, False),
            ((2, HEAD_DIM, width), low, False),
            ((2, width, 2 * lanes), low, False),
            ((2, out_rows, width), low, False),
            ((2, down_rows, width), low, False),
            every,
            every,
            half,
            ((block, width), low, False),
            own_wide,
            own_low,
            own_low,
            ((4, tokens, PAD), low, True),
            ((tokens, 1), f32, True),
        ],
        [all_blocks() for _ in range(5)]
        + [half_blocks]
        + weights_vm
        + [wide_vm, down_vm, vmem((tokens, lanes), low), vmem((block, width), low)]
        + [vmem((16, width), low), dma((6,)), dma((3,)), dma, dma]
        + [dma((3, count)), dma((3, count)), dma((5, count)), dma((5, count)), dma((5,))]
        + gather_semaphores(count) * 2
        + line_semaphores(count)
        + [dma, dma]
        + scatter()
        + scatter(),
    )
    gains = attn[:, GAINS : GAINS + 2].astype(f32)
    back_scratch = (
        [all_blocks(), all_blocks(), vmem((4, tokens, PAD), low)]
        + weights_vm
        + [vmem((tokens, PAD), low), vmem((tokens, tokens), f32)]
        + [vmem((tokens, PAD), f32), vmem((tokens, PAD), f32), vmem((tokens, 3 * PAD), low)]
        + [all_blocks(), dma((7,))]
        + gather_semaphores(count)
        + scatter()
    )
    attn_shape, out_shape = (3 * HEAD_DIM, width), (HEAD_DIM, width)
    wide_shape, down_shape = (width, 2 * lanes), (down_rows, width)
    (
        hidden_two,
        ahead,
        grad_between,
        branch,
        grad_hidden,
        gain_mlp_two,
        gain_attn_two,
        gain_mlp_one,
        wide_two,
        down_two,
        attn_two,
        out_two,
        wide_one,
        down_one,
        wide_from_one,
        down_from_one,
        attn_from_one,
        out_from_one,
    ) = call_kernel(
        functools.partial(middle_kernel, count),
        "second_layer",
        4,
        [(normed, True), (between, True), (grads_side, True)]
        + tables
        + [(attn, False), (twin, False), (out, False)]
        + [(grads_near, False), (gate_up, False), (down, False)]
        + [(grads_own, True), (hidden_one, True), (wide_rows_one, False)]
        + [(gains[1, 1:2], True), (gains[1, 0:1], True), (gains[0, 1:2], True)],
        [own_wide, every, own_low, own_low, own_wide, gain_rows, gain_rows, gain_rows]
        + [(wide_shape, low, True), (down_shape, low, True)]
        + [(attn_shape, low, True), (out_shape, low, True)]
        + [(wide_shape, low, True), (down_shape, low, True)]
        + [(shape, low, False) for shape in (wide_shape, down_shape, attn_shape, out_shape)],
        [all_blocks(), all_blocks(), all_blocks(), wide_vm, down_vm]
        + [vmem((tokens, 1), f32), vmem((tokens, lanes), low), vmem((tokens, 2 * lanes), f32)]
        + [vmem((tokens, 2 * lanes), low), vmem((block, width), low), vmem((block, width), low)]
        + [vmem((block, width), f32), dma((4,)), dma((4,)), dma((4,))]
        + line_semaphores(count)
        + back_scratch,
    )
    back_operands = (
        [(branch, True), (grad_hidden, True), (rows_own, True)]
        + [(rows_one, False), (heads_one, False), (total_one, True)]
        + [(attn, False), (twin, False), (out, False)]
        + tables
        + [(gains[0, 0:1], True)]
    )
    rows_out, grads_out, gain_sums, query, key, value, out, gate, up, down = last_layer(
        count,
        back_operands
        + [(wide_one, False), (down_one, False), (attn_two, False), (out_two, False)]
        + [(wide_two, False), (down_two, False), (wide_from_one, False), (down_from_one, False)]
        + [(attn_from_one, False), (out_from_one, False), (ahead, False)]
        + [(gain_mlp_one, True), (gain_attn_two, True), (gain_mlp_two, True)]
        + [(between, True), (grad_between, True), (hidden_two, True)],
        (
            attn_shape,
            out_shape,
            wide_shape,
            down_shape,
            block,
            width,
            gain_rows[0][0],
        ),
        back_scratch,
    )
    return (
        rows_out[None, :, None],
        grads_out[None, :, None],
        gain_sums[0][None],
        query[None],
        key[None],
        value[None],
        out[None],
        gain_sums[4][None],
        gate[None],
        up[None],
        down[None],
    )

def solution(mesh):
    placed = (
        P(None, None, ("seq", "blk"), None),
        P(None, None, ("seq", "blk"), None),
        P(),
        P("section", "blk"),
        P("section", "blk", None),
        P("section", "blk", None),
        P("section", "blk", None),
        P("section", "blk", None),
        P("section", "blk"),
        P("section", "blk", None),
        P("section", "blk", None),
        P("section", "blk", None),
    )
    one_head_each = mesh.shape["seq"] == 4 and mesh.shape["blk"] == HEADS // 4
    return jax.shard_map(
        head_shards if one_head_each else shards,
        mesh=mesh,
        in_specs=placed,
        out_specs=(
            P("section", None, None, ("seq", "blk"), None),
            P("section", None, None, ("seq", "blk"), None),
            P("section", "blk"),
            P("section", "blk", None),
            P("section", "blk", None),
            P("section", "blk", None),
            P("section", "blk", None),
            P("section", "blk"),
            P("section", "blk", None),
            P("section", "blk", None),
            P("section", "blk", None),
        ),
        check_vma=False,
    )
```

```python
import functools

import jax
import jax.numpy as jnp
from jax import lax
from jax.experimental import pallas as pl
from jax.experimental.pallas import tpu as pltpu
from jax.sharding import PartitionSpec as P

HEADS = 16
KV_HEADS = 8
HEAD_DIM = 96


EPS = 1e-05
THETA = 100000.0
MASKED = -1e30


def passed_along(value, axis, steps):
    count = lax.axis_size(axis)
    first, last = (max(0, -steps), min(count, count - steps))
    return lax.ppermute(value, axis, [(source, source + steps) for source in range(first, last)])


def shortened(value):
    return jax.tree.map(lambda a: a.astype(jnp.bfloat16) if a.dtype == jnp.float32 else a, value)


def product(left_side, right_side):
    return jnp.dot(left_side, right_side, preferred_element_type=jnp.float32)


def back_product(left_side, right_side):
    return lax.dot_general(
        left_side, right_side, (((1,), (1,)), ((), ())), preferred_element_type=jnp.float32
    )


def doc_info(lengths, token_index):
    doc_ends = jnp.cumsum(lengths, axis=-1)
    passed = (doc_ends[..., None, :] <= token_index[..., None]).astype(jnp.int32)
    segment = jnp.sum(passed, axis=-1)
    offset = jnp.sum(passed * lengths[..., None, :], axis=-1)
    return (segment, token_index - offset)


def rotate(field_in, position, turn_sign):
    half_dim = field_in.shape[-1] // 2
    frequency = THETA ** (-2.0 * jnp.arange(half_dim, dtype=jnp.float32) / field_in.shape[-1])
    angles = position.astype(jnp.float32)[:, None] * frequency
    cosine = jnp.cos(angles)[:, None, :]
    sine_part = turn_sign * jnp.sin(angles)[:, None, :]
    first_half = field_in[..., :half_dim]
    second_half = field_in[..., half_dim:]
    return jnp.concatenate(
        [
            first_half * cosine - second_half * sine_part,
            second_half * cosine + first_half * sine_part,
        ],
        axis=-1,
    )


def rms_forward(field_in, gain_row):
    inv_root = lax.rsqrt(jnp.mean(field_in * field_in, axis=-1, keepdims=True) + EPS)
    return (field_in * inv_root * gain_row, inv_root)


def rms_backward(field_in, gain_row, inv_root, grad_normed):
    scaled = gain_row * grad_normed
    grad_field = inv_root * scaled - field_in * inv_root**3 * jnp.mean(
        scaled * field_in, axis=-1, keepdims=True
    )
    return (grad_field, grad_normed * field_in * inv_root)


def token_place(block_id, row_ids, per_device, blk_count):
    return (row_ids // per_device * blk_count + block_id) * per_device + row_ids % per_device


def masks_for(lengths, blk_index, per_device, blk_count, seq_count):
    block_tokens = seq_count * per_device
    row_ids = jnp.arange(block_tokens, dtype=jnp.int32)
    query_index = token_place(blk_index, row_ids, per_device, blk_count)
    all_ids = jnp.arange(blk_count * block_tokens, dtype=jnp.int32)
    key_index = token_place(all_ids // block_tokens, all_ids % block_tokens, per_device, blk_count)
    query_seg, _ = doc_info(lengths, query_index)
    key_seg, _ = doc_info(lengths, key_index)
    return (query_index, key_index, query_seg, key_seg)


def head_scores(queries, key_rows, allowed, kv_local):
    grouped = queries.reshape(queries.shape[0], kv_local, -1, HEAD_DIM)
    key_heads = key_rows.reshape(key_rows.shape[0], kv_local, HEAD_DIM)
    scores = jnp.einsum(
        "rkgd,lkd->kgrl", grouped, key_heads, preferred_element_type=jnp.float32
    ) * HEAD_DIM ** (-0.5)
    return (jnp.where(allowed, scores, MASKED), grouped, key_heads)


def attend_forward(operands, query_index, key_index, kv_local):
    queries, key_rows, value_rows, query_seg, key_seg = operands
    allowed = (query_seg[:, None] == key_seg[None, :]) & (
        key_index[None, :] <= query_index[:, None]
    )
    scores, grouped, key_heads = head_scores(queries, key_rows, allowed, kv_local)
    row_top = jnp.max(scores, axis=-1, keepdims=True)
    log_total = row_top + jnp.log(jnp.sum(jnp.exp(scores - row_top), axis=-1, keepdims=True))
    weights_low = jnp.exp(scores - log_total).astype(jnp.bfloat16)
    value_heads = value_rows.reshape(value_rows.shape[0], kv_local, HEAD_DIM)
    mixed_heads = jnp.einsum(
        "kgrl,lkd->rkgd", weights_low, value_heads, preferred_element_type=jnp.float32
    )
    return (mixed_heads.reshape(queries.shape).astype(jnp.bfloat16), log_total)


def attend_backward(operands, query_index, key_index, kv_local):
    queries, key_rows, value_rows, grad_mixed, log_total, query_seg, key_seg = operands
    allowed = (query_seg[:, None] == key_seg[None, :]) & (
        key_index[None, :] <= query_index[:, None]
    )
    scores, grouped, key_heads = head_scores(queries, key_rows, allowed, kv_local)
    attn_probs = jnp.exp(scores - log_total)
    value_heads = value_rows.reshape(value_rows.shape[0], kv_local, HEAD_DIM)
    grad_heads = grad_mixed.reshape(grouped.shape)
    grad_values = jnp.einsum(
        "kgrl,rkgd->lkd",
        attn_probs.astype(jnp.bfloat16),
        grad_heads,
        preferred_element_type=jnp.float32,
    )
    grad_probs = jnp.einsum(
        "rkgd,lkd->kgrl", grad_heads, value_heads, preferred_element_type=jnp.float32
    )
    centre = jnp.sum(attn_probs * grad_probs, axis=-1, keepdims=True)
    grad_scores = (attn_probs * (grad_probs - centre)).astype(jnp.bfloat16)
    grad_queries = jnp.einsum(
        "kgrl,lkd->rkgd", grad_scores, key_heads, preferred_element_type=jnp.float32
    ) * HEAD_DIM ** (-0.5)
    grad_keys = jnp.einsum(
        "kgrl,rkgd->lkd", grad_scores, grouped, preferred_element_type=jnp.float32
    ) * HEAD_DIM ** (-0.5)
    return (
        grad_queries.reshape(queries.shape).astype(jnp.bfloat16),
        grad_keys.reshape(key_rows.shape),
        grad_values.reshape(value_rows.shape),
    )


def layer_forward(section_in, lengths, weights, placing):
    shard_id, blk_index, seq_count, blk_count = placing
    gain_attn, w_query, w_key, w_value, w_output, gain_mlp, w_gate, w_up, w_down = weights
    seqs_here, per_device, width = section_in.shape
    token_rows = seqs_here * per_device
    copies = max(1, seq_count // KV_HEADS)
    kv_local = KV_HEADS * copies // seq_count
    token_index = shard_id * per_device + jnp.arange(per_device, dtype=jnp.int32)
    _, position = doc_info(lengths, token_index)
    position = position.reshape(token_rows)
    flat_in = section_in.reshape(token_rows, width)
    normed, inv_first = rms_forward(flat_in, gain_attn.astype(jnp.float32))
    normed_low = normed.astype(jnp.bfloat16)
    query_pre = product(normed_low, w_query).reshape(token_rows, HEADS, HEAD_DIM)
    key_pre = product(normed_low, w_key).reshape(token_rows, KV_HEADS, HEAD_DIM)
    value_pre = product(normed_low, w_value).reshape(token_rows, KV_HEADS, HEAD_DIM)
    query_rot = (
        rotate(query_pre, position, 1.0).astype(jnp.bfloat16).reshape(seqs_here, per_device, width)
    )
    key_rot = rotate(key_pre, position, 1.0).astype(jnp.bfloat16)
    spread_shape = (token_rows, KV_HEADS, copies, HEAD_DIM)
    key_rep = jnp.broadcast_to(key_rot[:, :, None, :], spread_shape).reshape(
        seqs_here, per_device, -1
    )
    value_rep = jnp.broadcast_to(
        value_pre.astype(jnp.bfloat16)[:, :, None, :], spread_shape
    ).reshape(seqs_here, per_device, -1)
    heads_query, heads_key, heads_value = (
        lax.all_to_all(query_rot, "seq", split_axis=2, concat_axis=1, tiled=True),
        lax.all_to_all(key_rep, "seq", split_axis=2, concat_axis=1, tiled=True),
        lax.all_to_all(value_rep, "seq", split_axis=2, concat_axis=1, tiled=True),
    )
    keys_all, values_all = (
        lax.all_gather(heads_key, "blk", axis=1, tiled=True),
        lax.all_gather(heads_value, "blk", axis=1, tiled=True),
    )
    query_index, key_index, query_seg, key_seg = masks_for(
        lengths, blk_index, per_device, blk_count, seq_count
    )
    heads_mixed, log_total = lax.map(
        lambda operands: attend_forward(operands, query_index, key_index, kv_local),
        (heads_query, keys_all, values_all, query_seg, key_seg),
    )
    token_mixed = lax.all_to_all(
        heads_mixed, "seq", split_axis=1, concat_axis=2, tiled=True
    ).reshape(token_rows, width)
    hidden = flat_in + product(token_mixed, w_output)
    normed_mlp, inv_second = rms_forward(hidden, gain_mlp.astype(jnp.float32))
    normed_mlp_low = normed_mlp.astype(jnp.bfloat16)
    gate_pre = product(normed_mlp_low, w_gate)
    up_pre = product(normed_mlp_low, w_up)
    act_low = (jax.nn.silu(gate_pre) * up_pre).astype(jnp.bfloat16)
    result = hidden + product(act_low, w_down)
    saved_state = (
        flat_in,
        normed_low,
        inv_first,
        position,
        heads_query,
        keys_all,
        values_all,
        log_total,
        token_mixed,
        hidden,
        inv_second,
        normed_mlp_low,
        gate_pre,
        up_pre,
        act_low,
        lengths,
    )
    return (result.reshape(section_in.shape), saved_state)


def layer_backward(upstream, saved_state, weights, placing):
    shard_id, blk_index, seq_count, blk_count = placing
    gain_attn, w_query, w_key, w_value, w_output, gain_mlp, w_gate, w_up, w_down = weights
    (
        flat_in,
        normed_low,
        inv_first,
        position,
        heads_query,
        keys_all,
        values_all,
        log_total,
        token_mixed,
        hidden,
        inv_second,
        normed_mlp_low,
        gate_pre,
        up_pre,
        act_low,
        lengths,
    ) = saved_state
    seqs_here, per_device, width = upstream.shape
    token_rows = seqs_here * per_device
    copies = max(1, seq_count // KV_HEADS)
    kv_local = KV_HEADS * copies // seq_count
    grad_rows = upstream.reshape(token_rows, width)
    grad_out_low = grad_rows.astype(jnp.bfloat16)
    grad_act = back_product(grad_out_low, w_down)
    gate_sigmoid = jax.nn.sigmoid(gate_pre)
    grad_gate_low = (
        grad_act * up_pre * gate_sigmoid * (1.0 + gate_pre * (1.0 - gate_sigmoid))
    ).astype(jnp.bfloat16)
    grad_up_low = (grad_act * jax.nn.silu(gate_pre)).astype(jnp.bfloat16)
    grad_normed_mlp = back_product(grad_gate_low, w_gate) + back_product(grad_up_low, w_up)
    grad_hidden_part, gain_mlp_terms = rms_backward(
        hidden, gain_mlp.astype(jnp.float32), inv_second, grad_normed_mlp
    )
    grad_hidden = grad_rows + grad_hidden_part
    grad_branch_low = grad_hidden.astype(jnp.bfloat16)
    grad_mixed_low = (
        back_product(grad_branch_low, w_output)
        .astype(jnp.bfloat16)
        .reshape(seqs_here, per_device, width)
    )
    heads_grad = lax.all_to_all(grad_mixed_low, "seq", split_axis=2, concat_axis=1, tiled=True)
    query_index, key_index, query_seg, key_seg = masks_for(
        lengths, blk_index, per_device, blk_count, seq_count
    )
    grad_heads_query, grad_keys_all, grad_values_all = lax.map(
        lambda operands: attend_backward(operands, query_index, key_index, kv_local),
        (heads_query, keys_all, values_all, heads_grad, log_total, query_seg, key_seg),
    )
    grad_key_own, grad_value_own = (
        lax.psum_scatter(
            grad_keys_all.astype(jnp.bfloat16), "blk", scatter_dimension=1, tiled=True
        ).astype(jnp.float32),
        lax.psum_scatter(
            grad_values_all.astype(jnp.bfloat16), "blk", scatter_dimension=1, tiled=True
        ).astype(jnp.float32),
    )
    token_query, token_key, token_value = (
        lax.all_to_all(grad_heads_query, "seq", split_axis=1, concat_axis=2, tiled=True),
        lax.all_to_all(
            grad_key_own.astype(jnp.bfloat16), "seq", split_axis=1, concat_axis=2, tiled=True
        ),
        lax.all_to_all(
            grad_value_own.astype(jnp.bfloat16), "seq", split_axis=1, concat_axis=2, tiled=True
        ),
    )
    grad_key_sum = jnp.sum(
        token_key.astype(jnp.float32).reshape(token_rows, KV_HEADS, copies, HEAD_DIM), axis=2
    )
    grad_value_sum = jnp.sum(
        token_value.astype(jnp.float32).reshape(token_rows, KV_HEADS, copies, HEAD_DIM), axis=2
    )
    grad_query_low = (
        rotate(token_query.astype(jnp.float32).reshape(token_rows, HEADS, HEAD_DIM), position, -1.0)
        .astype(jnp.bfloat16)
        .reshape(token_rows, width)
    )
    grad_key_low = (
        rotate(grad_key_sum, position, -1.0)
        .astype(jnp.bfloat16)
        .reshape(token_rows, KV_HEADS * HEAD_DIM)
    )
    grad_value_low = grad_value_sum.astype(jnp.bfloat16).reshape(token_rows, KV_HEADS * HEAD_DIM)
    grad_normed = (
        back_product(grad_query_low, w_query)
        + back_product(grad_key_low, w_key)
        + back_product(grad_value_low, w_value)
    )
    grad_in_part, gain_attn_terms = rms_backward(
        flat_in, gain_attn.astype(jnp.float32), inv_first, grad_normed
    )
    grad_input = (grad_hidden + grad_in_part).reshape(upstream.shape)
    weight_rows = (
        gain_attn_terms,
        normed_low,
        grad_query_low,
        grad_key_low,
        grad_value_low,
        token_mixed,
        grad_branch_low,
        gain_mlp_terms,
        normed_mlp_low,
        grad_gate_low,
        grad_up_low,
        act_low,
        grad_out_low,
    )
    return (grad_input, weight_rows)


def weight_term(inputs_low, outputs_low):
    if outputs_low is None:
        return jnp.sum(inputs_low, axis=0)
    return lax.dot_general(
        inputs_low, outputs_low, (((0,), (0,)), ((), ())), preferred_element_type=jnp.float32
    )


def shards(
    inputs,
    cotangent,
    doc_lengths,
    attention_gain,
    w_query,
    w_key,
    w_value,
    w_output,
    mlp_gain,
    w_gate,
    w_up,
    w_down,
):
    at_first = lax.axis_index("section") == 0
    seq_count = lax.axis_size("seq")
    blk_count = lax.axis_size("blk")
    blk_index = lax.axis_index("blk")
    shard_id = lax.axis_index("seq") * blk_count + blk_index
    placing = (shard_id, blk_index, seq_count, blk_count)
    micro_count = inputs.shape[0]
    local_shards = (
        attention_gain[0],
        w_query[0],
        w_key[0],
        w_value[0],
        w_output[0],
        mlp_gain[0],
        w_gate[0],
        w_up[0],
        w_down[0],
    )
    weights = (
        lax.all_gather(local_shards[0], "blk", axis=0, tiled=True),
        lax.all_gather(local_shards[1], "blk", axis=0, tiled=True),
        lax.all_gather(local_shards[2], "blk", axis=0, tiled=True),
        lax.all_gather(local_shards[3], "blk", axis=0, tiled=True),
        lax.all_gather(local_shards[4], "blk", axis=0, tiled=True),
        lax.all_gather(local_shards[5], "blk", axis=0, tiled=True),
        lax.all_gather(local_shards[6], "blk", axis=0, tiled=True),
        lax.all_gather(local_shards[7], "blk", axis=0, tiled=True),
        lax.all_gather(local_shards[8], "blk", axis=0, tiled=True),
    )
    received = jnp.zeros(inputs.shape[1:], jnp.bfloat16)
    saved_states = []
    section_outs = []
    for tick_index in range(micro_count + 1):
        fresh_input = inputs[min(tick_index, micro_count - 1)]
        section_in = jnp.where(at_first, fresh_input, received).astype(jnp.float32)
        lengths = jnp.where(
            at_first,
            doc_lengths[min(tick_index, micro_count - 1)],
            doc_lengths[max(tick_index - 1, 0)],
        )
        result, saved_state = layer_forward(section_in, lengths, weights, placing)
        result_low = result.astype(jnp.bfloat16)
        if tick_index < micro_count:
            received = passed_along(result_low, "section", 1)
        saved_states.append(saved_state)
        section_outs.append(result_low)
    weights = (
        lax.all_gather(local_shards[0], "blk", axis=0, tiled=True),
        lax.all_gather(local_shards[1], "blk", axis=0, tiled=True),
        lax.all_gather(local_shards[2], "blk", axis=0, tiled=True),
        lax.all_gather(local_shards[3], "blk", axis=0, tiled=True),
        lax.all_gather(local_shards[4], "blk", axis=0, tiled=True),
        lax.all_gather(local_shards[5], "blk", axis=0, tiled=True),
        lax.all_gather(local_shards[6], "blk", axis=0, tiled=True),
        lax.all_gather(local_shards[7], "blk", axis=0, tiled=True),
        lax.all_gather(local_shards[8], "blk", axis=0, tiled=True),
    )
    back_in = jnp.zeros(cotangent.shape[1:], jnp.bfloat16)
    grad_outs = []
    row_sets = []
    for tick_index in range(micro_count + 1):
        saved_state = jax.tree.map(
            lambda first_pick, second_pick: jnp.where(at_first, first_pick, second_pick),
            saved_states[max(tick_index - 1, 0)],
            saved_states[min(tick_index + 1, micro_count)],
        )
        upstream = jnp.where(at_first, back_in, cotangent[min(tick_index, micro_count - 1)]).astype(
            jnp.float32
        )
        grad_input, weight_rows = layer_backward(upstream, saved_state, weights, placing)
        grad_low = grad_input.astype(jnp.bfloat16)
        if tick_index < micro_count:
            back_in = passed_along(grad_low, "section", -1)
        grad_outs.append(grad_low)
        row_sets.append(weight_rows)
    activations = jnp.stack(
        [
            jnp.where(at_first, section_outs[index_m], section_outs[index_m + 1])
            for index_m in range(micro_count)
        ]
    )[None]
    input_grads = jnp.stack(
        [
            jnp.where(at_first, grad_outs[index_m + 1], grad_outs[index_m])
            for index_m in range(micro_count)
        ]
    )[None]
    picked = [
        jax.tree.map(
            lambda first_pick, second_pick: jnp.where(at_first, first_pick, second_pick),
            row_sets[index_m + 1],
            row_sets[index_m],
        )
        for index_m in range(micro_count)
    ]
    merged = jax.tree.map(lambda *pieces: jnp.concatenate(pieces, axis=0), *picked)
    (
        gain_attn_terms,
        normed_low,
        grad_query_low,
        grad_key_low,
        grad_value_low,
        token_mixed,
        grad_branch_low,
        gain_mlp_terms,
        normed_mlp_low,
        grad_gate_low,
        grad_up_low,
        act_low,
        grad_out_low,
    ) = merged
    grad_pairs = (
        (gain_attn_terms, None),
        (normed_low, grad_query_low),
        (normed_low, grad_key_low),
        (normed_low, grad_value_low),
        (token_mixed, grad_branch_low),
        (gain_mlp_terms, None),
        (normed_mlp_low, grad_gate_low),
        (normed_mlp_low, grad_up_low),
        (act_low, grad_out_low),
    )
    shares = tuple(
        (
            lax.psum_scatter(
                weight_term(left_side, right_side).astype(jnp.bfloat16),
                "blk",
                scatter_dimension=0,
                tiled=True,
            ).astype(jnp.float32)
            for left_side, right_side in grad_pairs
        )
    )
    shares = jax.tree.map(lambda part: part.astype(jnp.float32), lax.psum(shortened(shares), "seq"))
    return (
        activations,
        input_grads,
        shares[0][None],
        shares[1][None],
        shares[2][None],
        shares[3][None],
        shares[4][None],
        shares[5][None],
        shares[6][None],
        shares[7][None],
        shares[8][None],
    )


MESH = pl.DeviceIdType.MESH


def remote(source, target, sent, arrived, device):
    return pltpu.make_async_remote_copy(
        source, target, sent, arrived, device_id=device, device_id_type=MESH
    )


def greet(partners):
    barrier = pltpu.get_barrier_semaphore()
    for device in partners:
        pl.semaphore_signal(barrier, 1, device_id=device, device_id_type=MESH)
    pl.semaphore_wait(barrier, len(partners))


def settled(spot, semaphore, received):
    copy = remote(spot, spot, semaphore, semaphore, {"seq": lax.axis_index("seq") ^ 1})
    if received:
        copy.wait_recv()
    else:
        copy.wait_send()


CUTS = 2


def gather_steps(
    count, own, out, line_sent, line_got, side_sent, side_got, core_sent, core_got, local_done
):
    seq, b = lax.axis_index("seq"), lax.axis_index("blk")
    core, side = {"seq": seq ^ 1}, {"seq": seq ^ 2}
    base, side_base = seq * count, (seq ^ 2) * count
    cut = out.shape[1] // CUTS

    def spot(index, h):
        return out.at[index, pl.ds(h * cut, cut)]

    def begin(index, h, first):
        return own.at[pl.ds(h * cut, cut)] if first else spot(index, h)

    def along_line(j, way, h, first=False):
        device = {"blk": b + (1 if way else -1)}
        return remote(
            begin(base + j, h, first),
            spot(base + j, h),
            line_sent.at[j, way, h],
            line_got.at[j, h],
            device,
        )

    def to_side(j, h, first=False):
        return remote(
            begin(base + j, h, first),
            spot(base + j, h),
            side_sent.at[j, h],
            side_got.at[j, h],
            side,
        )

    def to_core(half, j, h, first=False):
        index = (side_base if half else base) + j
        return remote(
            begin(index, h, first),
            spot(index, h),
            core_sent.at[half, j, h],
            core_got.at[half, j, h],
            core,
        )

    local = pltpu.make_async_copy(own, out.at[base + b], local_done)
    local.start()
    for h in range(CUTS):
        to_side(b, h, True).start()
        pl.when(b > 0)(along_line(b, 0, h, True).start)
        pl.when(b < count - 1)(along_line(b, 1, h, True).start)
    for h in range(CUTS):
        to_core(0, b, h, True).start()
    yield "sent"

    def from_line(j, way):
        for h in range(CUTS):
            settled(spot(base + j, h), line_got.at[j, h], True)
            pl.when((b < count - 1) if way else (b > 0))(along_line(j, way, h).start)
            to_side(j, h).start()
        for h in range(CUTS):
            to_core(0, j, h).start()

    def from_side(j):
        for h in range(CUTS):
            settled(spot(side_base + j, h), side_got.at[j, h], True)
            to_core(1, j, h).start()

    for k in range(1, count + 1):
        if k < count:
            pl.when(b - k >= 0)(functools.partial(from_line, b - k, 1))
            pl.when(b + k < count)(functools.partial(from_line, b + k, 0))
        if k == 1:
            from_side(b)
        else:
            pl.when(b - k + 1 >= 0)(functools.partial(from_side, b - k + 1))
            pl.when(b + k - 1 < count)(functools.partial(from_side, b + k - 1))
        if k == count - 1:
            local.wait()
        yield "line" if k == count - 1 else "side" if k == count else "step"
    for half, corner in ((0, seq ^ 1), (1, seq ^ 3)):
        for j in range(count):
            for h in range(CUTS):
                settled(spot(corner * count + j, h), core_got.at[half, j, h], True)
        yield "corner" if half else "near"
    yield "done"
    for h in range(CUTS):
        for j in range(count):
            to_side(j, h).wait_send()
            to_core(0, j, h).wait_send()
            to_core(1, j, h).wait_send()
        pl.when(b > 0)(along_line(b, 0, h).wait_send)
        pl.when(b < count - 1)(along_line(b, 1, h).wait_send)
        for k in range(1, count):
            pl.when((b - k >= 0) & (b < count - 1))(along_line(b - k, 1, h).wait_send)
            pl.when((b + k < count) & (b > 0))(along_line(b + k, 0, h).wait_send)


def gather_semaphores(count):
    dma = pltpu.SemaphoreType.DMA
    return [
        dma((count, 2, CUTS)),
        dma((count, CUTS)),
        dma((count, CUTS)),
        dma((count, CUTS)),
        dma((2, count, CUTS)),
        dma((2, count, CUTS)),
        dma,
    ]


def line_steps(
    count, own, out, line_sent, line_got, core_sent, core_got, local_done, offset=0
):
    seq, b = lax.axis_index("seq"), lax.axis_index("blk")
    core, base = {"seq": seq ^ 1}, offset + (seq % 2) * count
    cut = out.shape[1] // CUTS

    def spot(j, h):
        return out.at[base + j, pl.ds(h * cut, cut)]

    def begin(j, h, first):
        return own.at[pl.ds(h * cut, cut)] if first else spot(j, h)

    def along_line(j, way, h, first=False):
        device = {"blk": b + (1 if way else -1)}
        return remote(
            begin(j, h, first), spot(j, h), line_sent.at[j, way, h], line_got.at[j, h], device
        )

    def to_core(j, h, first=False):
        return remote(begin(j, h, first), spot(j, h), core_sent.at[j, h], core_got.at[j, h], core)

    local = pltpu.make_async_copy(own, out.at[base + b], local_done)
    local.start()
    for h in range(CUTS):
        pl.when(b > 0)(along_line(b, 0, h, True).start)
        pl.when(b < count - 1)(along_line(b, 1, h, True).start)
        to_core(b, h, True).start()
    yield

    def from_line(j, way):
        for h in range(CUTS):
            settled(spot(j, h), line_got.at[j, h], True)
            pl.when((b < count - 1) if way else (b > 0))(along_line(j, way, h).start)
            to_core(j, h).start()

    for k in range(1, count):
        pl.when(b - k >= 0)(functools.partial(from_line, b - k, 1))
        pl.when(b + k < count)(functools.partial(from_line, b + k, 0))
        yield
    local.wait()
    for h in range(CUTS):
        for j in range(count):
            place = offset + (1 - seq % 2) * count + j
            settled(out.at[place, pl.ds(h * cut, cut)], core_got.at[j, h], True)
            to_core(j, h).wait_send()
        pl.when(b > 0)(along_line(b, 0, h).wait_send)
        pl.when(b < count - 1)(along_line(b, 1, h).wait_send)
        for k in range(1, count):
            pl.when((b - k >= 0) & (b < count - 1))(along_line(b - k, 1, h).wait_send)
            pl.when((b + k < count) & (b > 0))(along_line(b + k, 0, h).wait_send)


def line_semaphores(count):
    dma = pltpu.SemaphoreType.DMA
    return [
        dma((count, 2, CUTS)),
        dma((count, CUTS)),
        dma((count, CUTS)),
        dma((count, CUTS)),
        dma,
    ]


def advance(steps, times):
    for _ in range(times):
        next(steps, None)


def until_done(steps):
    for event in steps:
        if event == "done":
            return
        yield event


def all_but_last(compute):
    groups = []

    def some(group):
        groups.append(group)
        if len(groups) < 4:
            compute(group)

    return some


def group_of(event):
    seq = lax.axis_index("seq")
    return {"line": seq, "side": seq ^ 2, "near": seq ^ 1, "corner": seq ^ 3}.get(event)


def scatter_steps(
    count,
    partial,
    deliver,
    core_slot,
    side_slot,
    line_slot,
    side_out,
    line_out,
    running,
    core_sent,
    core_got,
    side_sent,
    side_got,
    line_sent,
    line_got,
    compute=None,
):
    seq, b = lax.axis_index("seq"), lax.axis_index("blk")
    core, side = {"seq": seq ^ 1}, {"seq": seq ^ 2}
    place = far_first(b, count)
    size = partial.shape[1] // CUTS
    cuts = [pl.ds(h * size, size) for h in range(CUTS)]

    def to_core(half, k, h):
        return remote(
            partial.at[(seq ^ (1 if half else 3)) * count + place[k], cuts[h]],
            core_slot.at[half, k, cuts[h]],
            core_sent.at[half, k, h],
            core_got.at[half, k, h],
            core,
        )

    def to_side(k, h):
        return remote(
            side_out.at[k, cuts[h]],
            side_slot.at[k, cuts[h]],
            side_sent.at[k, h],
            side_got.at[k, h],
            side,
        )

    def along_line(k, way, h):
        j = place[k]
        return remote(
            line_out.at[k, cuts[h]],
            line_slot.at[way, j, cuts[h]],
            line_sent.at[k, h],
            line_got.at[way, j, h],
            {"blk": b + (1 if way else -1)},
        )

    def add_from(way, j, h):
        settled(line_slot.at[way, j, cuts[h]], line_got.at[way, j, h], True)
        running[cuts[h]] += line_slot[way, j, cuts[h]].astype(jnp.float32)

    def exchange(half):
        if compute:
            compute(seq ^ (1 if half else 3))
        for k in range(count):
            for h in range(CUTS):
                to_core(half, k, h).start()

    exchange(0)
    if compute:
        compute(seq ^ 2)
    for k in range(count):
        for h in range(CUTS):
            to_core(0, k, h).wait_recv()
            total = partial[(seq ^ 2) * count + place[k], cuts[h]].astype(jnp.float32)
            total += core_slot[0, k, cuts[h]].astype(jnp.float32)
            side_out[k, cuts[h]] = total.astype(jnp.bfloat16)
            to_side(k, h).start()
    exchange(1)
    if compute:
        compute(seq)
    yield
    for k in range(count):
        j = place[k]
        rightward, leftward = j >= b, j <= b
        for h in range(CUTS):
            to_core(1, k, h).wait_recv()
            to_side(k, h).wait_recv()
            total = partial[seq * count + j, cuts[h]].astype(jnp.float32)
            total += core_slot[1, k, cuts[h]].astype(jnp.float32)
            running[cuts[h]] = total + side_slot[k, cuts[h]].astype(jnp.float32)
            pl.when(rightward & (b > 0))(functools.partial(add_from, 1, j, h))
            pl.when(leftward & (b < count - 1))(functools.partial(add_from, 0, j, h))
            if k < count - 1:
                line_out[k, cuts[h]] = running[cuts[h]].astype(jnp.bfloat16)
                pl.when(rightward)(along_line(k, 1, h).start)
                pl.when(jnp.logical_not(rightward))(along_line(k, 0, h).start)
        if k < count - 1:
            yield
    deliver(running[...])
    yield
    for k in range(count):
        for h in range(CUTS):
            to_core(0, k, h).wait_send()
            to_core(1, k, h).wait_send()
            to_side(k, h).wait_send()
            if k < count - 1:
                settled(line_out.at[k, cuts[h]], line_sent.at[k, h], False)


def line_first_steps(
    count,
    partial,
    deliver,
    own,
    core_slot,
    line_slot,
    line_out,
    side_slot,
    running,
    own_done,
    core_sent,
    core_got,
    line_sent,
    line_got,
    side_sent,
    side_got,
):
    seq, b = lax.axis_index("seq"), lax.axis_index("blk")
    core, side = {"seq": seq ^ 1}, {"seq": seq ^ 2}
    place = far_first(b, count)

    def to_core(half, k):
        source = partial.at[(seq ^ (1 if half else 3)) * count + place[k]]
        return remote(
            source, core_slot.at[half, k], core_sent.at[half, k], core_got.at[half, k], core
        )

    def kept(half, k):
        source = partial.at[(seq if half else seq ^ 2) * count + place[k]]
        return pltpu.make_async_copy(source, own.at[half, k], own_done.at[half, k])

    def along_line(half, k, way):
        j = place[k]
        return remote(
            line_out.at[half, k],
            line_slot.at[half, way, j],
            line_sent.at[half, k],
            line_got.at[half, way, j],
            {"blk": b + (1 if way else -1)},
        )

    def add_from(half, way, j):
        settled(line_slot.at[half, way, j], line_got.at[half, way, j], True)
        running[...] += line_slot[half, way, j].astype(jnp.float32)

    to_side = remote(line_out.at[0, count - 1], side_slot.at[0], side_sent, side_got, side)
    for half in range(2):
        for k in range(count):
            kept(half, k).start()
            to_core(half, k).start()
    yield
    for k in range(count):
        j = place[k]
        rightward, leftward = j >= b, j <= b
        for half in range(2):
            kept(half, k).wait()
            to_core(half, k).wait_recv()
            running[...] = own[half, k].astype(jnp.float32) + core_slot[half, k].astype(jnp.float32)
            pl.when(rightward & (b > 0))(functools.partial(add_from, half, 1, j))
            pl.when(leftward & (b < count - 1))(functools.partial(add_from, half, 0, j))
            if half == 0 or k < count - 1:
                line_out[half, k] = running[...].astype(jnp.bfloat16)
            if k < count - 1:
                pl.when(rightward)(along_line(half, k, 1).start)
                pl.when(jnp.logical_not(rightward))(along_line(half, k, 0).start)
            elif half == 0:
                to_side.start()
            else:
                to_side.wait_recv()
                deliver(running[...] + side_slot[0].astype(jnp.float32))
            yield
    to_side.wait_send()
    for half in range(2):
        for k in range(count):
            to_core(half, k).wait_send()
            if k < count - 1:
                settled(line_out.at[half, k], line_sent.at[half, k], False)


def far_first(b, count):
    order = sorted(range(count), key=lambda j: -j)
    places = []
    for k in range(count):
        place = 0
        for own in range(count):
            by_distance = sorted(order, key=lambda j: (-abs(j - own), -j if own * 2 < count else j))
            place = jnp.where(b == own, by_distance[k], place)
        places.append(place)
    return places


def scatter_scratch(count, rows, width):
    dma = pltpu.SemaphoreType.DMA

    def slots(*places):
        return pltpu.VMEM(places + (rows, width), jnp.bfloat16)

    return [
        slots(2, count),
        slots(count),
        slots(2, count),
        slots(count),
        slots(count - 1),
        pltpu.VMEM((rows, width), jnp.float32),
        dma((2, count, CUTS)),
        dma((2, count, CUTS)),
        dma((count, CUTS)),
        dma((count, CUTS)),
        dma((count - 1, CUTS)),
        dma((2, count, CUTS)),
    ]


def run_all(fillers):
    for filler in fillers:
        filler()


def run_with(steps, fillers):
    fillers = list(fillers)
    for _ in steps:
        if fillers:
            fillers.pop(0)()
    for filler in fillers:
        filler()


def greet_group(count, more=()):
    seq, b = lax.axis_index("seq"), lax.axis_index("blk")
    greet(
        tuple(more)
        + ({"seq": seq ^ 1}, {"seq": seq ^ 2})
        + tuple({"blk": lax.rem(b + k, count)} for k in range(1, count))
    )


def carry(copies, from_section, what):
    sending = lax.axis_index("section") == from_section
    for copy in copies:
        if what == "start":
            pl.when(sending)(copy.start)
        else:
            pl.when(sending)(copy.wait_send)
            pl.when(jnp.logical_not(sending))(copy.wait_recv)


def carried(sources, targets, sent, got):
    other = {"section": 1 - lax.axis_index("section")}
    return [
        remote(source, target, sent.at[n], got.at[n], other)
        for n, (source, target) in enumerate(zip(sources, targets))
    ]


def group_rows(ref, group, count):
    value = ref[pl.ds(group * count, count)]
    return value.reshape(value.shape[0] * value.shape[1], value.shape[2])


def group_span(group, count, block):
    size = count * block
    return pl.ds(pl.multiple_of(group * size, size), size)


def lane_turn(field_in, cosine, sine):
    half_dim, lanes = HEAD_DIM // 2, field_in.shape[-1]
    lane = lax.broadcasted_iota(jnp.int32, field_in.shape, 1)
    partner = jnp.where(
        lane < half_dim,
        pltpu.roll(field_in, lanes - half_dim, 1),
        pltpu.roll(field_in, half_dim, 1),
    )
    return field_in * cosine + partner * sine


def masked_scores(query, key, first_row, start):
    scores = back_product(query, key) * HEAD_DIM ** (-0.5)
    key_index = lax.broadcasted_iota(jnp.int32, scores.shape, 1)
    query_index = first_row + lax.broadcasted_iota(jnp.int32, scores.shape, 0)
    return jnp.where((key_index >= start) & (key_index <= query_index), scores, MASKED)


def normalise(field_in, gain_row):
    inv_root = lax.rsqrt(jnp.mean(field_in * field_in, axis=-1, keepdims=True) + EPS)
    return field_in * inv_root * gain_row


PAD = 128


GAINS = HEAD_DIM
OWN_PART = HEAD_DIM + 16


def load_weights(layer, attn, twin, out, attn_vm, out_vm, sems):
    on_key = lax.axis_index("seq") % 2 == 0
    own, other = attn.at[layer, pl.ds(OWN_PART, HEAD_DIM)], twin.at[layer]

    def part(source, n, rows):
        return pltpu.make_async_copy(source, attn_vm.at[pl.ds(n * PAD, rows)], sems.at[n])

    copies = [
        part(attn.at[layer, pl.ds(0, HEAD_DIM)], 0, HEAD_DIM),
        part(attn.at[layer, pl.ds(GAINS, 16)], 3, 16),
    ]
    if out is not None:
        copies.append(
            pltpu.make_async_copy(out.at[layer], out_vm.at[pl.ds(0, HEAD_DIM)], sems.at[4])
        )
    start_all(copies)

    @pl.when(on_key)
    def _():
        part(own, 1, HEAD_DIM).start()
        part(other, 2, HEAD_DIM).start()

    @pl.when(jnp.logical_not(on_key))
    def _():
        part(other, 1, HEAD_DIM).start()
        part(own, 2, HEAD_DIM).start()

    return copies + [part(other, 1, HEAD_DIM), part(other, 2, HEAD_DIM)]


def clear_pads(attn_vm, out_vm):
    empty = jnp.zeros((PAD - HEAD_DIM, attn_vm.shape[1]), jnp.bfloat16)
    for part in range(3):
        attn_vm[part * PAD + HEAD_DIM : (part + 1) * PAD] = empty
    out_vm[HEAD_DIM:PAD] = empty


def attention_rows(heads, log_total, start, size, tokens):
    for i in range(tokens // size):
        here, seen = slice(i * size, (i + 1) * size), slice(0, (i + 1) * size)
        scores = masked_scores(heads[0, here], heads[1, seen], i * size, start[here])
        row_top = jnp.max(scores, axis=-1, keepdims=True)
        weights = jnp.exp(scores - row_top)
        total = jnp.sum(weights, axis=-1, keepdims=True)
        log_total[here] = row_top + jnp.log(total)
        weights = (weights * (1.0 / total)).astype(jnp.bfloat16)
        heads[3, here] = product(weights, heads[2, seen]).astype(jnp.bfloat16)


def project_heads(normed, attn_vm, heads, span, cosine, sine):
    mixed = back_product(normed, attn_vm[0 : 3 * PAD])
    cos_rows, sin_rows = cosine[span], sine[span]
    heads[0, span] = lane_turn(mixed[:, :PAD], cos_rows, sin_rows).astype(jnp.bfloat16)
    heads[1, span] = lane_turn(mixed[:, PAD : 2 * PAD], cos_rows, sin_rows).astype(jnp.bfloat16)
    heads[2, span] = mixed[:, 2 * PAD :].astype(jnp.bfloat16)


def keep_group(partial, group, value, count):
    block = partial.shape[1]
    partial[pl.ds(group * count, count)] = value.astype(jnp.bfloat16).reshape(count, block, -1)


def gain_of(ref, row):
    return ref[3 * PAD : 3 * PAD + 16][row : row + 1].astype(jnp.float32)


def first_layer_kernel(count, *refs):
    refs = iter(refs)

    def take(n):
        return [next(refs) for _ in range(n)]

    pieces, w_gate, w_up, w_output, w_down, rows_in, grads_in, cosine, sine, start = take(10)
    attn, twin, gate_up, out, down, all_rows, wide_rows, grads_near, grads_side = take(9)
    hidden, result_out, normed_out, heads, log_total = take(5)
    raw_vm, normed_vm, rows_vm, partial, partial_two, grads_vm = take(6)
    attn_vm, out_vm, wide_vm, down_vm, units, normed_own, gain_vm = take(7)
    load_done, save_done, twin_sent, twin_got = take(4)
    spread_sems = take(5)
    first_sems, second_sems, grads_sems, side_sems = take(7), take(7), take(5), take(2)
    scatter_one, scatter_two = take(12), take(12)
    section = lax.axis_index("section")
    block, width = raw_vm.shape[1], raw_vm.shape[2]
    tokens = block * raw_vm.shape[0]
    size = count * block
    low, f32 = jnp.bfloat16, jnp.float32
    greet_group(count, ({"section": 1 - section},))
    spread = spread_steps(
        count, pieces, w_gate, w_up, w_output, w_down, attn, gate_up, out, down, *spread_sems
    )
    steps = gather_steps(count, rows_in, raw_vm, *first_sems)
    next(steps)
    next(spread)
    clear_pads(attn_vm, out_vm)
    for event in until_done(steps):
        if event == "line":
            advance(spread, 3)
    grads_across = remote(
        grads_in, grads_side, *side_sems, {"seq": lax.axis_index("seq") ^ 2}
    )
    grads_across.start()
    next(spread)
    pair = remote(
        attn.at[:, pl.ds(OWN_PART, HEAD_DIM)],
        twin,
        twin_sent,
        twin_got,
        {"seq": lax.axis_index("seq") ^ 1},
    )
    pair.start()
    pair.wait()
    gain_load = pltpu.make_async_copy(attn.at[1, pl.ds(GAINS, 16)], gain_vm, load_done.at[5])
    gain_load.start()
    wait_all(load_weights(0, attn, twin, None, attn_vm, out_vm, load_done) + [gain_load])
    for group in range(tokens // size):
        raw = raw_vm[group * count : (group + 1) * count].astype(f32)
        normed = normalise(raw, gain_of(attn_vm, 0)[None]).astype(low)
        normed_vm[group * count : (group + 1) * count] = normed
        span = slice(group * size, (group + 1) * size)
        project_heads(normed.reshape(size, width), attn_vm, heads, span, cosine, sine)
    saves = [pltpu.make_async_copy(normed_vm, all_rows, save_done.at[0])]
    saves[0].start()
    attention_rows(heads, log_total, start, size, tokens)
    next(spread)
    load = pltpu.make_async_copy(out.at[0], out_vm.at[pl.ds(0, HEAD_DIM)], load_done.at[4])
    load.start()
    load.wait()

    def project_out(group):
        mixed = heads[3, group_span(group, count, block)]
        keep_group(partial, group, product(mixed, out_vm[...]), count)

    def deliver(total):
        value = rows_in[...].astype(f32) + total
        hidden[...] = value
        normed_own[...] = normalise(value, gain_of(attn_vm, 1)).astype(low)

    def more():
        next(spread)

    run_with(scatter_steps(count, partial, deliver, *scatter_one, compute=project_out), [more] * 5)
    for _ in steps:
        pass
    steps = gather_steps(count, normed_own, rows_vm, *second_sems)
    for number, event in enumerate(until_done(steps)):
        if number == 0:
            more()
    for _ in spread:
        pass
    loads = [
        pltpu.make_async_copy(gate_up.at[0], wide_vm, load_done.at[0]),
        pltpu.make_async_copy(down.at[0], down_vm, load_done.at[1]),
    ]
    start_all(loads)
    wait_all(loads)
    saves.append(pltpu.make_async_copy(rows_vm, wide_rows, save_done.at[1]))
    saves[1].start()

    def project_down(group):
        pre = product(group_rows(rows_vm, group, count), wide_vm[...])
        made = hidden_units(pre)
        units[group_span(group, count, block)] = made
        keep_group(partial_two, group, product(made, down_vm[...]), count)

    grad_steps = line_steps(count, grads_in, grads_vm, *grads_sems)
    next(grad_steps)

    def deliver_two(total):
        made = (hidden[...] + total).astype(low)
        result_out[...] = made
        gain = gain_vm[...][0:1].astype(f32)
        normed_out[...] = normalise(made.astype(f32), gain).astype(low)

    run_with(
        scatter_steps(count, partial_two, deliver_two, *scatter_two, compute=project_down),
        [functools.partial(advance, grad_steps, 1)] * 3,
    )
    for _ in grad_steps:
        pass
    for _ in steps:
        pass
    saves.append(pltpu.make_async_copy(grads_vm, grads_near, save_done.at[2]))
    saves[2].start()
    grads_across.wait()
    wait_all(saves)


def spread_steps(
    count,
    pieces,
    w_gate,
    w_up,
    w_output,
    w_down,
    attn,
    gate_up,
    out,
    down,
    line_sent,
    line_got,
    cross_sent,
    cross_got,
    local_done,
):
    seq, b, section = lax.axis_index("seq"), lax.axis_index("blk"), lax.axis_index("section")
    seq_count = lax.axis_size("seq")
    other = {"section": 1 - section}
    rows, lanes = w_gate.shape[0], gate_up.shape[2] // 2
    turns = tuple(range(count // 2, 0, -1)) + tuple(range(count // 2 + 1, count))

    def source(kind, j):
        if kind == 0:
            return pieces.at[j]
        weight = w_gate if kind == 1 else w_up
        return weight.at[:, pl.ds(pl.multiple_of((j * seq_count + seq) * lanes, lanes), lanes)]

    def target(kind, j):
        if kind == 0:
            return attn.at[section, :, pl.ds(pl.multiple_of(j * rows, rows), rows)]
        return gate_up.at[
            section, pl.ds(pl.multiple_of(j * rows, rows), rows), pl.ds((kind - 1) * lanes, lanes)
        ]

    def along_line(kind, k):
        j = lax.rem(b + k, count)
        return remote(
            source(kind, j),
            target(kind, b),
            line_sent.at[kind, k],
            line_got.at[kind, k],
            {"blk": j},
        )

    def across(kind, j, slot, begin=None):
        spot = target(kind, j)
        return remote(
            spot if begin is None else begin,
            spot,
            cross_sent.at[kind, slot],
            cross_got.at[kind, slot],
            other,
        )

    def own_rows(kind):
        weight, place = (w_output, out) if kind == 3 else (w_down, down)
        size = place.shape[1]
        begin = weight.at[pl.ds(pl.multiple_of(seq * size, size), size)]
        spot = place.at[section]
        return (
            remote(begin, spot, cross_sent.at[kind, 0], cross_got.at[kind, 0], other),
            pltpu.make_async_copy(begin, spot, local_done.at[kind]),
        )

    def own_piece(kind):
        return (
            across(kind, b, 0, source(kind, b)),
            pltpu.make_async_copy(source(kind, b), target(kind, b), local_done.at[kind]),
        )

    def forward(kind, k):
        j = lax.rem(b + count - k, count)
        settled(target(kind, j), line_got.at[kind, k], True)
        across(kind, j, k).start()

    def arrived(kind):
        if kind > 2:
            wait_all(own_rows(kind))
            return
        for k in range(count):
            settled(target(kind, 0), cross_got.at[kind, k], True)
            settled(target(kind, 0), cross_sent.at[kind, k], False)
            if k:
                settled(target(kind, 0), line_sent.at[kind, k], False)
        pltpu.make_async_copy(source(kind, b), target(kind, b), local_done.at[kind]).wait()

    for k in turns:
        along_line(0, k).start()
    start_all(own_piece(0))
    yield
    for k in turns:
        forward(0, k)
        yield
    start_all(own_rows(3))
    for kind in (1, 2):
        for k in turns:
            along_line(kind, k).start()
    arrived(0)
    start_all(own_piece(1) + own_piece(2) + own_rows(4))
    yield
    arrived(3)
    yield
    for kind in (1, 2):
        for k in turns:
            forward(kind, k)
            yield
    for kind in (1, 2, 4):
        arrived(kind)


def start_all(copies):
    for copy in copies:
        copy.start()


def wait_all(copies):
    for copy in copies:
        copy.wait()


def gated(pre):
    half = pre.shape[1] // 2
    gate, up = pre[:, :half], pre[:, half:]
    sigma = jax.nn.sigmoid(gate)
    return gate, up, sigma


def hidden_units(pre):
    gate, up, sigma = gated(pre)
    return (gate * sigma * up).astype(jnp.bfloat16)


def store_gate_grads(place, span, grad_act, pre):
    gate, up, sigma = gated(pre)
    half = gate.shape[1]
    place[span, 0:half] = (grad_act * up * sigma * (1.0 + gate * (1.0 - sigma))).astype(
        jnp.bfloat16
    )
    place[span, half : 2 * half] = (grad_act * (gate * sigma)).astype(jnp.bfloat16)


def wide_grads(rows_vm, pre_grads, units, grads_vm, wide_grad, down_grad):
    tokens = pre_grads.shape[0]
    width = rows_vm.shape[2]
    step = width // 4

    def wide_part(n):
        cut = slice(n * step, (n + 1) * step)
        rows = rows_vm[:, :, cut].reshape(tokens, step)
        wide_grad[cut] = weight_term(rows, pre_grads[...]).astype(jnp.bfloat16)

    def down_part(n):
        cut = slice(n * 2 * step, (n + 1) * 2 * step)
        rows = grads_vm[:, :, cut].reshape(tokens, 2 * step)
        down_grad[:, cut] = weight_term(units[...], rows).astype(jnp.bfloat16)

    return [functools.partial(wide_part, n) for n in range(4)] + [
        functools.partial(down_part, n) for n in range(2)
    ]


def mlp_grad_sent(total, hidden, grads_own, gain, branch_out, grad_hidden_out, gain_out):
    field_in = hidden[...]
    inv_root = lax.rsqrt(jnp.mean(field_in * field_in, axis=-1, keepdims=True) + EPS)
    part, terms = rms_backward(field_in, gain[...], inv_root, total)
    grad_hidden = grads_own[...].astype(jnp.float32) + part
    grad_hidden_out[...] = grad_hidden
    branch_out[...] = grad_hidden.astype(jnp.bfloat16)
    gain_out[...] = jnp.broadcast_to(jnp.sum(terms, axis=0, keepdims=True), gain_out.shape)


class Parts:
    pass


def attn_back_refs(take, attn_grad=None, out_grad=None):
    r = Parts()
    r.branch_vm, r.rows_vm, r.heads, r.attn_vm, r.out_vm, r.mixed_grads, r.probs = take(7)
    r.key_grads, r.value_grads, r.joint, r.partial, r.load_done = take(5)
    r.gather_sems = take(7)
    r.scatter_refs = take(12)
    return r


def attn_back_body(
    count, layer, r, ins, outs, background, fillers, gathered=None, spare=None
):
    branch_in, grad_hidden, x_own, all_rows, heads_kept, log_total, attn, twin, out = ins[:9]
    cosine, sine, start, gain = ins[9:]
    grad_out, gain_out, attn_grad, out_grad = outs
    branch_vm, rows_vm, heads, attn_vm, out_vm = r.branch_vm, r.rows_vm, r.heads, r.attn_vm, r.out_vm
    mixed_grads, probs, key_grads, value_grads = r.mixed_grads, r.probs, r.key_grads, r.value_grads
    joint, partial, load_done = r.joint, r.partial, r.load_done
    block = rows_vm.shape[1]
    size = count * block
    tokens = block * rows_vm.shape[0]
    low, f32 = jnp.bfloat16, jnp.float32
    scale = HEAD_DIM ** (-0.5)
    steps = gather_steps(count, branch_in, branch_vm, *r.gather_sems)
    next(steps)
    background()
    loads = []
    if layer is not None:
        clear_pads(attn_vm, out_vm)
        loads = load_weights(layer, attn, twin, out, attn_vm, out_vm, load_done)
        kept = [
            pltpu.make_async_copy(heads_kept, heads, load_done.at[5]),
            pltpu.make_async_copy(all_rows, rows_vm, load_done.at[6]),
        ]
        start_all(kept)
        loads += kept
    key_grads[...] = jnp.zeros_like(key_grads)
    value_grads[...] = jnp.zeros_like(value_grads)
    wait_all(loads)

    def spans(i):
        return slice(i * size, (i + 1) * size), slice(0, (i + 1) * size)

    def weigh(i):
        here, seen = spans(i)
        scores = masked_scores(heads[0, here], heads[1, seen], i * size, start[here])
        probs[here, seen] = jnp.exp(scores - log_total[here])

    def project(group):
        value = back_product(group_rows(branch_vm, group, count), out_vm[...])
        mixed_grads[group_span(group, count, block)] = value.astype(low)

    for number, event in enumerate(until_done(steps)):
        if number < 2:
            weigh(2 * number)
            weigh(2 * number + 1)
        group = group_of(event)
        if group is not None:
            project(group)
    if gathered:
        gathered()
    for i in reversed(range(tokens // size)):
        here, seen = spans(i)
        weights = probs[here, seen]
        grads = mixed_grads[here]
        grad_weights = back_product(grads, heads[2, seen])
        centre = jnp.sum(weights * grad_weights, axis=-1, keepdims=True)
        grad_scores = (weights * (grad_weights - centre)).astype(low)
        query_grad = (product(grad_scores, heads[1, seen]) * scale).astype(low).astype(f32)
        joint[here, 0:PAD] = lane_turn(query_grad, cosine[here], -sine[here]).astype(low)
        key_grads[seen] += weight_term(grad_scores, heads[0, here])
        value_grads[seen] += weight_term(weights.astype(low), grads)
        key_grad = (key_grads[here] * scale).astype(low).astype(f32)
        joint[here, PAD : 2 * PAD] = lane_turn(key_grad, cosine[here], -sine[here]).astype(low)
        joint[here, 2 * PAD : 3 * PAD] = value_grads[here].astype(low)

    def project_back(group):
        value = product(joint[group_span(group, count, block)], attn_vm[0 : 3 * PAD])
        partial[pl.ds(group * count, count)] = value.astype(low).reshape(count, block, -1)

    def attn_part(part):
        rows = rows_vm[...].reshape(tokens, rows_vm.shape[2])
        value = weight_term(joint[:, part * PAD : (part + 1) * PAD], rows)
        attn_grad[part * HEAD_DIM : (part + 1) * HEAD_DIM] = value[0:HEAD_DIM].astype(low)

    def out_part():
        rows = branch_vm[...].reshape(tokens, branch_vm.shape[2])
        out_grad[...] = weight_term(heads[3], rows)[0:HEAD_DIM].astype(low)

    def deliver(total):
        field_in = x_own[...].astype(f32)
        inv_root = lax.rsqrt(jnp.mean(field_in * field_in, axis=-1, keepdims=True) + EPS)
        part, terms = rms_backward(field_in, gain[...], inv_root, total)
        grad_out[...] = (grad_hidden[...] + part).astype(low)
        gain_out[...] = jnp.broadcast_to(jnp.sum(terms, axis=0, keepdims=True), gain_out.shape)

    parts = [functools.partial(attn_part, n) for n in range(3)] + [out_part]
    if spare:
        parts.append(spare)
    run_with(
        scatter_steps(count, partial, deliver, *r.scatter_refs, compute=project_back),
        [functools.partial(run_all, parts)] + fillers,
    )
    for _ in steps:
        pass


def middle_kernel(count, *refs):
    refs = iter(refs)

    def take(n):
        return [next(refs) for _ in range(n)]

    rows_in, between, grads_side, cosine, sine, start, attn, twin, out = take(9)
    grads_near, gate_up, down, grads_own, hidden_one, wide_rows = take(6)
    gain_mlp_two, gain_attn_two, gain_mlp_one = take(3)
    hidden, ahead, grad_between, branch_out, grad_hidden_out = take(5)
    mlp_two_sum, attn_two_sum, mlp_one_sum = take(3)
    wide_two, down_two, attn_two, out_two, wide_one, down_one = take(6)
    carried_to = take(4)
    rows_two, grads_vm, partial, wide_vm, down_vm = take(5)
    log_total, units, pre_vm, pre_grads, normed_own, branch_own, grad_hidden = take(7)
    load_done, carry_sent, carry_got = take(3)
    line_sems = take(5)
    r = attn_back_refs(take)
    rows_one, heads, attn_vm, out_vm, partial_back = (
        r.rows_vm,
        r.heads,
        r.attn_vm,
        r.out_vm,
        r.partial,
    )
    blocks, block = rows_one.shape[0], rows_one.shape[1]
    size, tokens, half = count * block, blocks * block, blocks // 2
    near = lax.axis_index("seq") // 2 * half
    greet_group(count, ({"section": 1 - lax.axis_index("section")},))
    steps = gather_steps(count, rows_in, rows_one, *r.gather_sems)
    next(steps)
    clear_pads(attn_vm, out_vm)
    loads = load_weights(1, attn, twin, out, attn_vm, out_vm, r.load_done)
    wide_loads = [
        pltpu.make_async_copy(gate_up.at[1], wide_vm, load_done.at[0]),
        pltpu.make_async_copy(down.at[1], down_vm, load_done.at[1]),
        pltpu.make_async_copy(grads_near, grads_vm.at[pl.ds(near, half)], load_done.at[2]),
    ]
    start_all(wide_loads)
    for event in until_done(steps):
        if event == "line":
            wait_all(loads)
        group = group_of(event)
        if group is not None:
            span = group_span(group, count, block)
            normed = group_rows(rows_one, group, count)
            project_heads(normed, attn_vm, heads, span, cosine, sine)
    grad_steps = line_steps(count, grads_side, grads_vm, *line_sems, offset=half - near)
    next(grad_steps)
    attention_rows(heads, log_total, start, size, tokens)

    def project_out(group):
        mixed = heads[3, group_span(group, count, block)]
        keep_group(partial, group, product(mixed, out_vm[...]), count)

    def deliver(total):
        value = between[...].astype(jnp.float32) + total
        hidden[...] = value
        normed_own[...] = normalise(value, gain_of(attn_vm, 1)).astype(jnp.bfloat16)

    run_with(
        scatter_steps(count, partial, deliver, *r.scatter_refs, compute=project_out),
        [functools.partial(advance, grad_steps, 1)] * 3,
    )
    for _ in steps:
        pass
    steps = gather_steps(count, normed_own, rows_two, *r.gather_sems)
    next(steps)
    for _ in grad_steps:
        pass
    wait_all(wide_loads)

    def through(group):
        span = group_span(group, count, block)
        pre = product(group_rows(rows_two, group, count), wide_vm[...])
        units[span] = hidden_units(pre)
        grad_act = back_product(group_rows(grads_vm, group, count), down_vm[...])
        store_gate_grads(pre_grads, span, grad_act, pre)
        keep_group(partial_back, group, back_product(pre_grads[span], wide_vm[...]), count)

    for event in until_done(steps):
        if event == "line":
            through(group_of(event))

    def project_down(group):
        value = product(units[group * size : (group + 1) * size], down_vm[...])
        partial[group * count : (group + 1) * count] = value.astype(jnp.bfloat16).reshape(
            count, block, -1
        )

    def deliver_two(total):
        mlp_grad_sent(
            total, hidden, grads_own, gain_mlp_two, branch_own, grad_hidden, mlp_two_sum
        )

    fillers = wide_grads(rows_two, pre_grads, units, grads_vm, wide_two, down_two)
    fillers += [functools.partial(project_down, group) for group in range(4)]
    run_with(
        scatter_steps(
            count, partial_back, deliver_two, *r.scatter_refs, compute=all_but_last(through)
        ),
        [functools.partial(run_all, fillers[n::4]) for n in range(4)],
    )
    for _ in steps:
        pass
    save = pltpu.make_async_copy(partial, ahead, load_done.at[3])
    save.start()
    copies = carried(
        (wide_two, down_two, attn_two, out_two), carried_to, carry_sent, carry_got
    )

    def background():
        carry(copies[:2], 0, "start")
        wide_loads[0] = pltpu.make_async_copy(gate_up.at[0], wide_vm, load_done.at[0])
        wide_loads[1] = pltpu.make_async_copy(down.at[0], down_vm, load_done.at[1])
        wide_loads[2] = pltpu.make_async_copy(wide_rows, rows_two, load_done.at[2])
        start_all(wide_loads)

    attn_back_body(
        count,
        None,
        r,
        (branch_own, grad_hidden, between, None, None, log_total, None, None, None)
        + (cosine, sine, start, gain_attn_two),
        (grad_between, attn_two_sum, attn_two, out_two),
        background,
        [],
    )
    carry(copies[2:], 0, "start")
    steps = gather_steps(count, grad_between, grads_vm, *r.gather_sems)
    next(steps)
    wait_all(wide_loads)

    def again(group):
        span = group_span(group, count, block)
        pre = product(group_rows(rows_two, group, count), wide_vm[...])
        pre_vm[span] = pre
        units[span] = hidden_units(pre)

    def through_one(group):
        span = group_span(group, count, block)
        grad_act = back_product(group_rows(grads_vm, group, count), down_vm[...])
        store_gate_grads(pre_grads, span, grad_act, pre_vm[span])
        keep_group(partial_back, group, back_product(pre_grads[span], wide_vm[...]), count)

    for number, event in enumerate(until_done(steps)):
        if number < 2:
            again(2 * number)
            again(2 * number + 1)
        if event == "line":
            through_one(group_of(event))

    def deliver_one(total):
        mlp_grad_sent(
            total, hidden_one, grad_between, gain_mlp_one, branch_out, grad_hidden_out, mlp_one_sum
        )

    run_with(
        scatter_steps(
            count, partial_back, deliver_one, *r.scatter_refs, compute=all_but_last(through_one)
        ),
        wide_grads(rows_two, pre_grads, units, grads_vm, wide_one, down_one),
    )
    for _ in steps:
        pass
    carry(copies, 0, "wait")
    save.wait()


def last_kernel(count, *refs):
    refs = iter(refs)

    def take(n):
        return [next(refs) for _ in range(n)]

    ins = take(13)
    wide_one, down_one, attn_two, out_two, wide_two, down_two = take(6)
    wide_from_one, down_from_one, attn_from_one, out_from_one, ahead = take(5)
    gain_mlp_one, gain_attn_two, gain_mlp_two, between, grad_between, hidden = take(6)
    attn, out, gate, up, down, gains_out, rows_out, grads_out = take(8)
    final, grad_start = take(2)
    attn_grad, out_grad, gain_attn_one, gains = take(4)
    attn_own, out_own, wide_own, down_own, attn_in, out_in, wide_in, down_in = take(8)
    attn_slot, wide_slot = take(2)
    gain_in, gain_sum, gain_line, gain_part, gain_side, gain_core = take(6)
    load_done, cross_sent, cross_got, line_sent, line_got = take(5)
    side_sent, side_got, core_sent, core_got, local_done, small_sent, small_got = take(7)
    ahead_refs = take(13)
    r = attn_back_refs(take)
    seq, b, section = lax.axis_index("seq"), lax.axis_index("blk"), lax.axis_index("section")
    at_first = section == 0
    at_second = jnp.logical_not(at_first)
    core, side, other = {"seq": seq ^ 1}, {"seq": seq ^ 2}, {"section": 1 - section}
    greet((other, core, side) + tuple({"blk": lax.rem(b + k, count)} for k in range(1, count)))
    rows, lanes = attn.shape[2], gate.shape[1] // (4 * count)
    turns = tuple(range(count // 2, 0, -1)) + tuple(range(count // 2 + 1, count)) + (0,)
    f32, low = jnp.float32, jnp.bfloat16

    def piece_rows(kind, j):
        if kind == 0:
            return (slice(None), pl.ds(pl.multiple_of(j * rows, rows), rows))
        return (pl.ds(pl.multiple_of(j * rows, rows), rows),)

    pairs = {
        0: (attn_own, attn_in, attn_grad),
        1: (wide_own, wide_in, wide_one),
        2: (out_own, out_in, out_grad),
        3: (down_own, down_in, down_one),
    }
    sources = {
        0: (attn_grad, attn_two, attn_from_one),
        1: (wide_one, wide_two, wide_from_one),
        2: (out_grad, out_two, out_from_one),
        3: (down_one, down_two, down_from_one),
    }

    def load(kind):
        one, two, from_one = sources[kind]
        own, held, _ = pairs[kind]

        @pl.when(at_first)
        def _():
            pltpu.make_async_copy(one, own, load_done.at[kind, 0]).start()

        @pl.when(at_second)
        def _():
            pltpu.make_async_copy(two, own, load_done.at[kind, 0]).start()
            pltpu.make_async_copy(from_one, held, load_done.at[kind, 1]).start()

    def loaded(kind):
        own, held, _ = pairs[kind]
        pltpu.make_async_copy(own, own, load_done.at[kind, 0]).wait()
        pl.when(at_second)(pltpu.make_async_copy(held, held, load_done.at[kind, 1]).wait)

    def cross(kind, k):
        _, held, begin = pairs[kind]
        index = piece_rows(kind, lax.rem(b + k, count)) if kind < 2 else (slice(None),)
        return remote(
            begin.at[index], held.at[index], cross_sent.at[kind, k], cross_got.at[kind, k], other
        )

    def add_up(kind, k):
        own, held, _ = pairs[kind]
        pl.when(at_first)(cross(kind, k).wait_recv)
        index = piece_rows(kind, lax.rem(b + k, count)) if kind < 2 else (slice(None),)
        held[index] = (own[index].astype(f32) + held[index].astype(f32)).astype(low)

    def along_line(kind, k):
        j = lax.rem(b + k, count)
        slot = (attn_slot if kind == 0 else wide_slot).at[k]
        source = pairs[kind][1].at[piece_rows(kind, j)]
        return remote(source, slot, line_sent.at[kind, k], line_got.at[kind, k], {"blk": j})

    def places(kind, k, of_seq):
        if kind == 2:
            size = out_in.shape[0]
            return [out.at[pl.ds(pl.multiple_of(of_seq * size, size), size)]]
        if kind == 3:
            size = down_in.shape[0]
            return [down.at[pl.ds(pl.multiple_of(of_seq * size, size), size)]]
        head = lax.rem(b + count - k, count) * 4 + of_seq
        if kind == 0:
            return [attn.at[head]]
        column = pl.ds(pl.multiple_of(head * lanes, lanes), lanes)
        return [gate.at[:, column], up.at[:, column]]

    def numbered(kind, k, of_seq):
        base = {0: k, 1: count + 2 * k, 2: 3 * count, 3: 3 * count + 1}[kind]
        return [(base + n, spot) for n, spot in enumerate(places(kind, k, of_seq))]

    def made(kind, k):
        if kind > 1:
            return [pairs[kind][1].at[:]]
        if kind == 0:
            return [attn_in.at[piece_rows(0, b)] if k == 0 else attn_slot.at[k]]
        whole = (lambda cut: wide_in.at[piece_rows(1, b) + (cut,)]) if k == 0 else (
            lambda cut: wide_slot.at[k, :, cut]
        )
        return [whole(pl.ds(0, lanes)), whole(pl.ds(lanes, lanes))]

    def sends(kind, k):
        found = []
        for (n, spot), begin in zip(numbered(kind, k, seq), made(kind, k)):
            found.append(
                (
                    remote(begin, spot, side_sent.at[n], side_got.at[n], side),
                    remote(begin, spot, core_sent.at[0, n], core_got.at[0, n], core),
                    pltpu.make_async_copy(begin, spot, local_done.at[n]),
                )
            )
        return found

    def publish(kind, k):
        for copies in sends(kind, k):
            for copy in copies:
                copy.start()

    def passes(kind, k):
        return [
            remote(spot, spot, core_sent.at[1, n], core_got.at[1, n], core)
            for n, spot in numbered(kind, k, seq ^ 2)
        ]

    def from_line(kind, k):
        along_line(kind, k).wait_recv()
        publish(kind, k)

    def from_side(kind, k):
        for n, spot in numbered(kind, k, seq ^ 2):
            settled(spot, side_got.at[n], True)
        for copy in passes(kind, k):
            copy.start()

    def small(n, source, slot, device):
        return remote(source, slot, small_sent.at[n], small_got.at[n], device)

    swap_rest = small(4 + count, between, rows_out.at[section], other)
    swap_final = small(4 + count, final, rows_out.at[section], other)
    swap_between = small(0, grad_between, grads_out.at[section], other)
    swap_start = small(0, grad_start, grads_out.at[section], other)
    pl.when(at_second)(swap_rest.start)
    pl.when(at_first)(swap_between.start)
    wide_turns = [(1, k) for k in turns]
    crossings = [(3, 0)] + wide_turns + [(0, k) for k in turns] + [(2, 0)]

    def begin_cross(those):
        for kind, k in those:
            pl.when(at_second)(cross(kind, k).start)

    def background():
        begin_cross(crossings[: count + 1])
        load(3)
        load(1)

    def deliver(total):
        final[...] = (hidden[...] + total).astype(low)
        pl.when(at_first)(swap_final.start)
        rows_out[section] = jnp.where(at_first, between[...], final[...])

    def later():
        load(0)
        load(2)
        begin_cross(crossings[count + 1 :])

    def share(n):
        if n == 0:
            loaded(1)
        add_up(1, turns[n])
        along_line(1, turns[n]).start()

    def gathered():
        loaded(3)
        add_up(3, 0)
        publish(3, 0)

    def spare():
        later()
        share(0)

    def early():
        add_up(1, 0)
        publish(1, 0)

    ahead_steps = line_first_steps(count, ahead, deliver, *ahead_refs)
    attn_back_body(
        count,
        0,
        r,
        ins,
        (grad_start, gain_attn_one, attn_grad, out_grad),
        background,
        [functools.partial(share, 1), functools.partial(share, 2), early],
        gathered,
        spare,
    )
    pl.when(at_second)(swap_start.start)
    grads_out[section] = jnp.where(at_first, grad_start[...], grad_between[...])
    gains[0, 0:4] = gain_attn_one[0:4]
    gains[0, 4:8] = gain_mlp_one[4:8]
    gains[1, 0:4] = gain_attn_two[0:4]
    gains[1, 4:8] = gain_mlp_two[4:8]
    gain_cross = small(1, gains.at[1 - section], gain_in.at[:], other)
    gain_cross.start()

    def gain_piece(j):
        return gain_sum.at[:, pl.ds(pl.multiple_of(j * rows, rows), rows)]

    def gain_send(k):
        j = lax.rem(b + k, count)
        return small(3 + k, gain_piece(j), gain_line.at[k], {"blk": j})

    loaded(0)
    for k in turns[:-1]:
        add_up(0, k)
        along_line(0, k).start()
    from_line(1, turns[0])
    add_up(0, 0)
    publish(0, 0)
    from_line(1, turns[1])
    from_side(1, 0)
    loaded(2)
    add_up(2, 0)
    publish(2, 0)
    from_line(1, turns[2])
    next(ahead_steps)
    from_side(3, 0)
    from_side(1, turns[0])
    for k in turns[:-1]:
        from_line(0, k)
    from_side(0, 0)
    from_side(1, turns[1])
    gain_cross.wait_recv()
    gain_sum[...] = gains[section] + gain_in[...]
    for k in range(1, count):
        gain_send(k).start()
    advance(ahead_steps, 2)
    from_side(2, 0)
    from_side(1, turns[2])
    for k in range(1, count):
        gain_send(k).wait_recv()
    gain_part[...] = gain_sum[:, pl.ds(pl.multiple_of(b * rows, rows), rows)]
    for k in range(1, count):
        gain_part[...] += gain_line[k]
    gain_to_side = small(2, gain_part.at[:], gain_side.at[:], side)
    gain_to_side.start()
    advance(ahead_steps, 4)
    gain_to_side.wait_recv()
    gain_side[...] += gain_part[...]
    gain_to_core = small(3, gain_side.at[:], gain_core.at[:], core)
    gain_to_core.start()
    for _ in ahead_steps:
        pass
    for k in turns[:-1]:
        from_side(0, k)
    gain_to_core.wait_recv()
    gains_out[...] = gain_side[...] + gain_core[...]
    every = [(0, k) for k in range(count)] + [(1, k) for k in range(count)] + [(2, 0), (3, 0)]
    for kind, k in every:
        pl.when(at_second)(cross(kind, k).wait_send)
        if kind < 2 and k:
            along_line(kind, k).wait_send()
        for to_side, to_core, local in sends(kind, k):
            to_side.wait_send()
            to_core.wait_send()
            local.wait()
        for copy in passes(kind, k):
            copy.wait_send()
        for half, of_seq in ((0, seq ^ 1), (1, seq ^ 3)):
            for n, spot in numbered(kind, k, of_seq):
                settled(spot, core_got.at[half, n], True)
    swap_between.wait()
    swap_rest.wait()
    gain_cross.wait_send()
    for k in range(1, count):
        gain_send(k).wait_send()
    gain_to_side.wait_send()
    gain_to_core.wait_send()


def widen_kernel(pieces, *refs):
    attn, out, gate, up, down, rows_in, grads_in, gains = refs[:8]
    query, key, value, out_f, gate_f, up_f, down_f = refs[8:15]
    rows_out, grads_out, gain_attn, gain_mlp = refs[15:]
    f32 = jnp.float32
    out_f[...] = out[...].astype(f32)
    gate_f[...] = gate[...].astype(f32)
    up_f[...] = up[...].astype(f32)
    down_f[...] = down[...].astype(f32)

    @pl.when(pl.program_id(0) == 0)
    def _():
        rows_out[...] = rows_in[...]
        grads_out[...] = grads_in[...]
        gain_attn[...] = gains[0:1]
        gain_mlp[...] = gains[4:5]

    @pl.when(pl.program_id(0) < pieces)
    def _():
        parts, _, lanes = attn.shape
        copies = HEADS // KV_HEADS

        def heads(n):
            return attn[:, n * HEAD_DIM : (n + 1) * HEAD_DIM].astype(f32)

        query[...] = heads(0).reshape(parts * HEAD_DIM, lanes).T
        for n, place in ((1, key), (2, value)):
            total = heads(n).reshape(parts // copies, copies, HEAD_DIM, lanes).sum(1)
            place[...] = total.reshape(parts // copies * HEAD_DIM, lanes).T


def widen(attn, out, gate, up, down, rows_out, grads_out, gains):
    f32 = jnp.float32
    parts, heads, rows = attn.shape
    lanes = 128
    pieces = rows // lanes
    steps = 8
    width = parts * HEAD_DIM
    narrow = width * KV_HEADS // HEADS

    def rows_of(array):
        return pl.BlockSpec((array.shape[0] // steps, array.shape[1]), lambda i: (i, 0))

    def turned(columns):
        return pl.BlockSpec((lanes, columns), lambda i: (jnp.minimum(i, pieces - 1), 0))

    def whole(shape):
        return pl.BlockSpec(shape, lambda i: (0,) * len(shape))

    flat = [out, gate, up, down]
    swaps = [whole(rows_out.shape), whole(grads_out.shape)]
    gain = jax.ShapeDtypeStruct((1, rows), f32)
    taken = pl.BlockSpec((parts, heads, lanes), lambda i: (0, 0, jnp.minimum(i, pieces - 1)))
    shapes = [(rows, width), (rows, narrow), (rows, narrow)] + [array.shape for array in flat]
    return pl.pallas_call(
        functools.partial(widen_kernel, pieces),
        grid=(steps,),
        out_shape=[jax.ShapeDtypeStruct(shape, f32) for shape in shapes]
        + [jax.ShapeDtypeStruct(array.shape, array.dtype) for array in (rows_out, grads_out)]
        + [gain, gain],
        in_specs=[taken] + [rows_of(array) for array in flat] + swaps + [whole(gains.shape)],
        out_specs=[turned(width), turned(narrow), turned(narrow)]
        + [rows_of(array) for array in flat]
        + swaps
        + [whole((1, rows)), whole((1, rows))],
        compiler_params=pltpu.CompilerParams(vmem_limit_bytes=60 * 2**20),
        name="widen_gradients",
    )(attn, out, gate, up, down, rows_out, grads_out, gains)


def last_layer(count, operands, like, back_scratch):
    attn, out, wide, down, block, width, gain_rows = like
    low, f32 = jnp.bfloat16, jnp.float32
    seq_count = lax.axis_size("seq")
    rows = wide[0] // count
    lanes = wide[1] // 2
    parts = seq_count * count
    dma = pltpu.SemaphoreType.DMA
    vmem = pltpu.VMEM
    sends = 3 * count + 2
    heads = attn[0]
    small = (gain_rows, rows)

    def slots(*places):
        return vmem(places + (block, width), low)

    outputs = [
        ((parts, heads, rows), low, False),
        ((out[0] * seq_count, out[1]), low, False),
        ((rows, lanes * parts), low, False),
        ((rows, lanes * parts), low, False),
        ((down[0] * seq_count, down[1]), low, False),
        (small, f32, True),
        ((2, block, width), low, True),
        ((2, block, width), low, True),
    ]
    scratch = (
        [vmem((block, width), low), vmem((block, width), low)]
        + [vmem(attn, low), vmem(out, low), vmem((gain_rows, width), f32)]
        + [vmem((2, gain_rows, width), f32)]
        + [vmem(shape, low) for shape in (attn, out, wide, down)] * 2
        + [vmem((count, heads, rows), low), vmem((count, rows, 2 * lanes), low)]
        + [vmem((gain_rows, width), f32)] * 2
        + [vmem((count,) + small, f32)]
        + [vmem(small, f32)] * 3
        + [dma((4, 2)), dma((4, count)), dma((4, count)), dma((2, count)), dma((2, count))]
        + [dma((sends,)), dma((sends,)), dma((2, sends)), dma((2, sends)), dma((sends,))]
        + [dma((5 + count,)), dma((5 + count,))]
        + [slots(2, count), slots(2, count), slots(2, 2, count), slots(2, count), slots(1)]
        + [vmem((block, width), f32)]
        + [dma((2, count)), dma((2, count)), dma((2, count)), dma((2, count))]
        + [dma((2, 2, count)), dma, dma]
        + back_scratch
    )
    attn, out, gate, up, down, gains, rows_out, grads_out = call_kernel(
        functools.partial(last_kernel, count), "last_layer_back", 3, operands, outputs, scratch
    )
    return widen(attn, out, gate, up, down, rows_out, grads_out, gains)


def call_kernel(kernel, name, number, operands, outputs, scratch):
    in_vmem = pl.BlockSpec(memory_space=pltpu.VMEM)
    anywhere = pl.BlockSpec(memory_space=pl.ANY)
    return pl.pallas_call(
        kernel,
        out_shape=[jax.ShapeDtypeStruct(shape, dtype) for shape, dtype, _ in outputs],
        in_specs=[in_vmem if near else anywhere for _, near in operands],
        out_specs=[in_vmem if near else anywhere for _, _, near in outputs],
        scratch_shapes=scratch,
        compiler_params=pltpu.CompilerParams(
            collective_id=number, has_side_effects=True, vmem_limit_bytes=56 * 2**20
        ),
        name=name,
    )(*[array for array, _ in operands])


def sliced_heads(local_shards):
    seq_index, seq_count = lax.axis_index("seq"), lax.axis_size("seq")
    count = lax.axis_size("blk")
    gain_attn, w_query, w_key, w_value, _, gain_mlp, _, _, _ = local_shards
    rows = w_query.shape[0]

    def heads_of(weight, per_blk, place):
        head = jnp.arange(count)[:, None] * per_blk + place
        column = (head * HEAD_DIM + jnp.arange(HEAD_DIM)).reshape(-1)
        chosen = jnp.arange(weight.shape[1])[:, None] == column[None, :]
        taken = lax.dot_general(
            chosen.astype(jnp.bfloat16),
            weight,
            (((0,), (1,)), ((), ())),
            preferred_element_type=jnp.float32,
        )
        return taken.astype(jnp.bfloat16).reshape(count, HEAD_DIM, rows)

    kv_per_blk = KV_HEADS // count
    kv_place = seq_index * kv_per_blk // seq_count
    gains = jnp.concatenate(
        [jnp.stack([gain_attn, gain_mlp]), jnp.zeros((14, rows), jnp.bfloat16)]
    )
    return jnp.concatenate(
        [
            heads_of(w_query, seq_count, seq_index),
            jnp.broadcast_to(gains[None], (count,) + gains.shape),
            heads_of(jnp.where(seq_index % 2 == 0, w_key, w_value), kv_per_blk, kv_place),
        ],
        axis=1,
    )


def head_shards(inputs, cotangent, doc_lengths, *params):
    section = lax.axis_index("section")
    at_first = section == 0
    seq_count, count = lax.axis_size("seq"), lax.axis_size("blk")
    low, f32 = jnp.bfloat16, jnp.float32
    vmem, dma = pltpu.VMEM, pltpu.SemaphoreType.DMA
    block, width = inputs.shape[2], inputs.shape[3]
    blocks = seq_count * count
    tokens = blocks * block
    rows_own = lax.dynamic_index_in_dim(inputs, section, 0, keepdims=False)[0]
    grads_own = lax.dynamic_index_in_dim(cotangent, section, 0, keepdims=False)[0]
    local = tuple(weight[0] for weight in params)
    pieces = sliced_heads(local)
    w_output, w_gate, w_up, w_down = local[4], local[6], local[7], local[8]
    rows = w_gate.shape[0]
    lanes = w_gate.shape[1] // blocks
    out_rows, down_rows = w_output.shape[0] // seq_count, w_down.shape[0] // seq_count
    lengths = lax.dynamic_index_in_dim(doc_lengths, section, 0, keepdims=False)[0]
    token_index = jnp.arange(tokens, dtype=jnp.int32)
    _, position = doc_info(lengths, token_index)
    start = (token_index - position)[:, None]
    half_dim = HEAD_DIM // 2
    lane = jnp.arange(PAD)
    frequency = THETA ** (-2.0 * (lane % half_dim).astype(f32) / HEAD_DIM)
    angles = position.astype(f32)[:, None] * frequency[None, :]
    sign = jnp.where(lane < half_dim, -1.0, 1.0).astype(f32)
    cosine = jnp.where(lane < HEAD_DIM, jnp.cos(angles), 0.0)
    sine = jnp.where(lane < HEAD_DIM, jnp.sin(angles) * sign, 0.0)

    def all_blocks():
        return vmem((blocks, block, width), low)

    def scatter():
        return scatter_scratch(count, block, width)

    half_blocks = vmem((blocks // 2, block, width), low)
    half = ((blocks // 2, block, width), low, False)
    own_low, own_wide = ((block, width), low, True), ((block, width), f32, True)
    every = ((blocks, block, width), low, False)
    gain_rows = ((8, width), f32, True)
    weights_vm = [vmem((3 * PAD + 16, width), low), vmem((PAD, width), low)]
    wide_vm, down_vm = vmem((width, 2 * lanes), low), vmem((down_rows, width), low)
    tables = [(cosine, True), (sine, True), (start, True)]
    (
        attn,
        twin,
        gate_up,
        out,
        down,
        rows_one,
        wide_rows_one,
        grads_near,
        grads_side,
        hidden_one,
        between,
        normed,
        heads_one,
        total_one,
    ) = call_kernel(
        functools.partial(first_layer_kernel, count),
        "first_layer",
        2,
        [(array, False) for array in (pieces, w_gate, w_up, w_output, w_down)]
        + [(rows_own, True), (grads_own, True)]
        + tables,
        [
            ((2, pieces.shape[1], width), low, False),
            ((2, HEAD_DIM, width), low, False),
            ((2, width, 2 * lanes), low, False),
            ((2, out_rows, width), low, False),
            ((2, down_rows, width), low, False),
            every,
            every,
            half,
            ((block, width), low, False),
            own_wide,
            own_low,
            own_low,
            ((4, tokens, PAD), low, True),
            ((tokens, 1), f32, True),
        ],
        [all_blocks() for _ in range(5)]
        + [half_blocks]
        + weights_vm
        + [wide_vm, down_vm, vmem((tokens, lanes), low), vmem((block, width), low)]
        + [vmem((16, width), low), dma((6,)), dma((3,)), dma, dma]
        + [dma((3, count)), dma((3, count)), dma((5, count)), dma((5, count)), dma((5,))]
        + gather_semaphores(count) * 2
        + line_semaphores(count)
        + [dma, dma]
        + scatter()
        + scatter(),
    )
    gains = attn[:, GAINS : GAINS + 2].astype(f32)
    back_scratch = (
        [all_blocks(), all_blocks(), vmem((4, tokens, PAD), low)]
        + weights_vm
        + [vmem((tokens, PAD), low), vmem((tokens, tokens), f32)]
        + [vmem((tokens, PAD), f32), vmem((tokens, PAD), f32), vmem((tokens, 3 * PAD), low)]
        + [all_blocks(), dma((7,))]
        + gather_semaphores(count)
        + scatter()
    )
    attn_shape, out_shape = (3 * HEAD_DIM, width), (HEAD_DIM, width)
    wide_shape, down_shape = (width, 2 * lanes), (down_rows, width)
    (
        hidden_two,
        ahead,
        grad_between,
        branch,
        grad_hidden,
        gain_mlp_two,
        gain_attn_two,
        gain_mlp_one,
        wide_two,
        down_two,
        attn_two,
        out_two,
        wide_one,
        down_one,
        wide_from_one,
        down_from_one,
        attn_from_one,
        out_from_one,
    ) = call_kernel(
        functools.partial(middle_kernel, count),
        "second_layer",
        4,
        [(normed, True), (between, True), (grads_side, True)]
        + tables
        + [(attn, False), (twin, False), (out, False)]
        + [(grads_near, False), (gate_up, False), (down, False)]
        + [(grads_own, True), (hidden_one, True), (wide_rows_one, False)]
        + [(gains[1, 1:2], True), (gains[1, 0:1], True), (gains[0, 1:2], True)],
        [own_wide, every, own_low, own_low, own_wide, gain_rows, gain_rows, gain_rows]
        + [(wide_shape, low, True), (down_shape, low, True)]
        + [(attn_shape, low, True), (out_shape, low, True)]
        + [(wide_shape, low, True), (down_shape, low, True)]
        + [(shape, low, False) for shape in (wide_shape, down_shape, attn_shape, out_shape)],
        [all_blocks(), all_blocks(), all_blocks(), wide_vm, down_vm]
        + [vmem((tokens, 1), f32), vmem((tokens, lanes), low), vmem((tokens, 2 * lanes), f32)]
        + [vmem((tokens, 2 * lanes), low), vmem((block, width), low), vmem((block, width), low)]
        + [vmem((block, width), f32), dma((4,)), dma((4,)), dma((4,))]
        + line_semaphores(count)
        + back_scratch,
    )
    back_operands = (
        [(branch, True), (grad_hidden, True), (rows_own, True)]
        + [(rows_one, False), (heads_one, False), (total_one, True)]
        + [(attn, False), (twin, False), (out, False)]
        + tables
        + [(gains[0, 0:1], True)]
    )
    query, key, value, out, gate, up, down, *swapped, gain_attn, gain_mlp = last_layer(
        count,
        back_operands
        + [(wide_one, False), (down_one, False), (attn_two, False), (out_two, False)]
        + [(wide_two, False), (down_two, False), (wide_from_one, False), (down_from_one, False)]
        + [(attn_from_one, False), (out_from_one, False), (ahead, False)]
        + [(gain_mlp_one, True), (gain_attn_two, True), (gain_mlp_two, True)]
        + [(between, True), (grad_between, True), (hidden_two, True)],
        (
            attn_shape,
            out_shape,
            wide_shape,
            down_shape,
            block,
            width,
            gain_rows[0][0],
        ),
        back_scratch,
    )
    return (
        swapped[0][None, :, None],
        swapped[1][None, :, None],
        gain_attn,
        query[None],
        key[None],
        value[None],
        out[None],
        gain_mlp,
        gate[None],
        up[None],
        down[None],
    )

def solution(mesh):
    placed = (
        P(None, None, ("seq", "blk"), None),
        P(None, None, ("seq", "blk"), None),
        P(),
        P("section", "blk"),
        P("section", "blk", None),
        P("section", "blk", None),
        P("section", "blk", None),
        P("section", "blk", None),
        P("section", "blk"),
        P("section", "blk", None),
        P("section", "blk", None),
        P("section", "blk", None),
    )
    one_head_each = mesh.shape["seq"] == 4 and mesh.shape["blk"] == HEADS // 4
    return jax.shard_map(
        head_shards if one_head_each else shards,
        mesh=mesh,
        in_specs=placed,
        out_specs=(
            P("section", None, None, ("seq", "blk"), None),
            P("section", None, None, ("seq", "blk"), None),
            P("section", "blk"),
            P("section", "blk", None),
            P("section", "blk", None),
            P("section", "blk", None),
            P("section", "blk", None),
            P("section", "blk"),
            P("section", "blk", None),
            P("section", "blk", None),
            P("section", "blk", None),
        ),
        check_vma=False,
    )
```

```python
import functools

import jax
import jax.numpy as jnp
from jax import lax
from jax.experimental import pallas as pl
from jax.experimental.pallas import tpu as pltpu
from jax.sharding import PartitionSpec as P

HEADS = 16
KV_HEADS = 8
HEAD_DIM = 96


EPS = 1e-05
THETA = 100000.0
MASKED = -1e30


def passed_along(value, axis, steps):
    count = lax.axis_size(axis)
    first, last = (max(0, -steps), min(count, count - steps))
    return lax.ppermute(value, axis, [(source, source + steps) for source in range(first, last)])


def shortened(value):
    return jax.tree.map(lambda a: a.astype(jnp.bfloat16) if a.dtype == jnp.float32 else a, value)


def product(left_side, right_side):
    return jnp.dot(left_side, right_side, preferred_element_type=jnp.float32)


def back_product(left_side, right_side):
    return lax.dot_general(
        left_side, right_side, (((1,), (1,)), ((), ())), preferred_element_type=jnp.float32
    )


def doc_info(lengths, token_index):
    doc_ends = jnp.cumsum(lengths, axis=-1)
    passed = (doc_ends[..., None, :] <= token_index[..., None]).astype(jnp.int32)
    segment = jnp.sum(passed, axis=-1)
    offset = jnp.sum(passed * lengths[..., None, :], axis=-1)
    return (segment, token_index - offset)


def rotate(field_in, position, turn_sign):
    half_dim = field_in.shape[-1] // 2
    frequency = THETA ** (-2.0 * jnp.arange(half_dim, dtype=jnp.float32) / field_in.shape[-1])
    angles = position.astype(jnp.float32)[:, None] * frequency
    cosine = jnp.cos(angles)[:, None, :]
    sine_part = turn_sign * jnp.sin(angles)[:, None, :]
    first_half = field_in[..., :half_dim]
    second_half = field_in[..., half_dim:]
    return jnp.concatenate(
        [
            first_half * cosine - second_half * sine_part,
            second_half * cosine + first_half * sine_part,
        ],
        axis=-1,
    )


def rms_forward(field_in, gain_row):
    inv_root = lax.rsqrt(jnp.mean(field_in * field_in, axis=-1, keepdims=True) + EPS)
    return (field_in * inv_root * gain_row, inv_root)


def rms_backward(field_in, gain_row, inv_root, grad_normed):
    scaled = gain_row * grad_normed
    grad_field = inv_root * scaled - field_in * inv_root**3 * jnp.mean(
        scaled * field_in, axis=-1, keepdims=True
    )
    return (grad_field, grad_normed * field_in * inv_root)


def token_place(block_id, row_ids, per_device, blk_count):
    return (row_ids // per_device * blk_count + block_id) * per_device + row_ids % per_device


def masks_for(lengths, blk_index, per_device, blk_count, seq_count):
    block_tokens = seq_count * per_device
    row_ids = jnp.arange(block_tokens, dtype=jnp.int32)
    query_index = token_place(blk_index, row_ids, per_device, blk_count)
    all_ids = jnp.arange(blk_count * block_tokens, dtype=jnp.int32)
    key_index = token_place(all_ids // block_tokens, all_ids % block_tokens, per_device, blk_count)
    query_seg, _ = doc_info(lengths, query_index)
    key_seg, _ = doc_info(lengths, key_index)
    return (query_index, key_index, query_seg, key_seg)


def head_scores(queries, key_rows, allowed, kv_local):
    grouped = queries.reshape(queries.shape[0], kv_local, -1, HEAD_DIM)
    key_heads = key_rows.reshape(key_rows.shape[0], kv_local, HEAD_DIM)
    scores = jnp.einsum(
        "rkgd,lkd->kgrl", grouped, key_heads, preferred_element_type=jnp.float32
    ) * HEAD_DIM ** (-0.5)
    return (jnp.where(allowed, scores, MASKED), grouped, key_heads)


def attend_forward(operands, query_index, key_index, kv_local):
    queries, key_rows, value_rows, query_seg, key_seg = operands
    allowed = (query_seg[:, None] == key_seg[None, :]) & (
        key_index[None, :] <= query_index[:, None]
    )
    scores, grouped, key_heads = head_scores(queries, key_rows, allowed, kv_local)
    row_top = jnp.max(scores, axis=-1, keepdims=True)
    log_total = row_top + jnp.log(jnp.sum(jnp.exp(scores - row_top), axis=-1, keepdims=True))
    weights_low = jnp.exp(scores - log_total).astype(jnp.bfloat16)
    value_heads = value_rows.reshape(value_rows.shape[0], kv_local, HEAD_DIM)
    mixed_heads = jnp.einsum(
        "kgrl,lkd->rkgd", weights_low, value_heads, preferred_element_type=jnp.float32
    )
    return (mixed_heads.reshape(queries.shape).astype(jnp.bfloat16), log_total)


def attend_backward(operands, query_index, key_index, kv_local):
    queries, key_rows, value_rows, grad_mixed, log_total, query_seg, key_seg = operands
    allowed = (query_seg[:, None] == key_seg[None, :]) & (
        key_index[None, :] <= query_index[:, None]
    )
    scores, grouped, key_heads = head_scores(queries, key_rows, allowed, kv_local)
    attn_probs = jnp.exp(scores - log_total)
    value_heads = value_rows.reshape(value_rows.shape[0], kv_local, HEAD_DIM)
    grad_heads = grad_mixed.reshape(grouped.shape)
    grad_values = jnp.einsum(
        "kgrl,rkgd->lkd",
        attn_probs.astype(jnp.bfloat16),
        grad_heads,
        preferred_element_type=jnp.float32,
    )
    grad_probs = jnp.einsum(
        "rkgd,lkd->kgrl", grad_heads, value_heads, preferred_element_type=jnp.float32
    )
    centre = jnp.sum(attn_probs * grad_probs, axis=-1, keepdims=True)
    grad_scores = (attn_probs * (grad_probs - centre)).astype(jnp.bfloat16)
    grad_queries = jnp.einsum(
        "kgrl,lkd->rkgd", grad_scores, key_heads, preferred_element_type=jnp.float32
    ) * HEAD_DIM ** (-0.5)
    grad_keys = jnp.einsum(
        "kgrl,rkgd->lkd", grad_scores, grouped, preferred_element_type=jnp.float32
    ) * HEAD_DIM ** (-0.5)
    return (
        grad_queries.reshape(queries.shape).astype(jnp.bfloat16),
        grad_keys.reshape(key_rows.shape),
        grad_values.reshape(value_rows.shape),
    )


def layer_forward(section_in, lengths, weights, placing):
    shard_id, blk_index, seq_count, blk_count = placing
    gain_attn, w_query, w_key, w_value, w_output, gain_mlp, w_gate, w_up, w_down = weights
    seqs_here, per_device, width = section_in.shape
    token_rows = seqs_here * per_device
    copies = max(1, seq_count // KV_HEADS)
    kv_local = KV_HEADS * copies // seq_count
    token_index = shard_id * per_device + jnp.arange(per_device, dtype=jnp.int32)
    _, position = doc_info(lengths, token_index)
    position = position.reshape(token_rows)
    flat_in = section_in.reshape(token_rows, width)
    normed, inv_first = rms_forward(flat_in, gain_attn.astype(jnp.float32))
    normed_low = normed.astype(jnp.bfloat16)
    query_pre = product(normed_low, w_query).reshape(token_rows, HEADS, HEAD_DIM)
    key_pre = product(normed_low, w_key).reshape(token_rows, KV_HEADS, HEAD_DIM)
    value_pre = product(normed_low, w_value).reshape(token_rows, KV_HEADS, HEAD_DIM)
    query_rot = (
        rotate(query_pre, position, 1.0).astype(jnp.bfloat16).reshape(seqs_here, per_device, width)
    )
    key_rot = rotate(key_pre, position, 1.0).astype(jnp.bfloat16)
    spread_shape = (token_rows, KV_HEADS, copies, HEAD_DIM)
    key_rep = jnp.broadcast_to(key_rot[:, :, None, :], spread_shape).reshape(
        seqs_here, per_device, -1
    )
    value_rep = jnp.broadcast_to(
        value_pre.astype(jnp.bfloat16)[:, :, None, :], spread_shape
    ).reshape(seqs_here, per_device, -1)
    heads_query, heads_key, heads_value = (
        lax.all_to_all(query_rot, "seq", split_axis=2, concat_axis=1, tiled=True),
        lax.all_to_all(key_rep, "seq", split_axis=2, concat_axis=1, tiled=True),
        lax.all_to_all(value_rep, "seq", split_axis=2, concat_axis=1, tiled=True),
    )
    keys_all, values_all = (
        lax.all_gather(heads_key, "blk", axis=1, tiled=True),
        lax.all_gather(heads_value, "blk", axis=1, tiled=True),
    )
    query_index, key_index, query_seg, key_seg = masks_for(
        lengths, blk_index, per_device, blk_count, seq_count
    )
    heads_mixed, log_total = lax.map(
        lambda operands: attend_forward(operands, query_index, key_index, kv_local),
        (heads_query, keys_all, values_all, query_seg, key_seg),
    )
    token_mixed = lax.all_to_all(
        heads_mixed, "seq", split_axis=1, concat_axis=2, tiled=True
    ).reshape(token_rows, width)
    hidden = flat_in + product(token_mixed, w_output)
    normed_mlp, inv_second = rms_forward(hidden, gain_mlp.astype(jnp.float32))
    normed_mlp_low = normed_mlp.astype(jnp.bfloat16)
    gate_pre = product(normed_mlp_low, w_gate)
    up_pre = product(normed_mlp_low, w_up)
    act_low = (jax.nn.silu(gate_pre) * up_pre).astype(jnp.bfloat16)
    result = hidden + product(act_low, w_down)
    saved_state = (
        flat_in,
        normed_low,
        inv_first,
        position,
        heads_query,
        keys_all,
        values_all,
        log_total,
        token_mixed,
        hidden,
        inv_second,
        normed_mlp_low,
        gate_pre,
        up_pre,
        act_low,
        lengths,
    )
    return (result.reshape(section_in.shape), saved_state)


def layer_backward(upstream, saved_state, weights, placing):
    shard_id, blk_index, seq_count, blk_count = placing
    gain_attn, w_query, w_key, w_value, w_output, gain_mlp, w_gate, w_up, w_down = weights
    (
        flat_in,
        normed_low,
        inv_first,
        position,
        heads_query,
        keys_all,
        values_all,
        log_total,
        token_mixed,
        hidden,
        inv_second,
        normed_mlp_low,
        gate_pre,
        up_pre,
        act_low,
        lengths,
    ) = saved_state
    seqs_here, per_device, width = upstream.shape
    token_rows = seqs_here * per_device
    copies = max(1, seq_count // KV_HEADS)
    kv_local = KV_HEADS * copies // seq_count
    grad_rows = upstream.reshape(token_rows, width)
    grad_out_low = grad_rows.astype(jnp.bfloat16)
    grad_act = back_product(grad_out_low, w_down)
    gate_sigmoid = jax.nn.sigmoid(gate_pre)
    grad_gate_low = (
        grad_act * up_pre * gate_sigmoid * (1.0 + gate_pre * (1.0 - gate_sigmoid))
    ).astype(jnp.bfloat16)
    grad_up_low = (grad_act * jax.nn.silu(gate_pre)).astype(jnp.bfloat16)
    grad_normed_mlp = back_product(grad_gate_low, w_gate) + back_product(grad_up_low, w_up)
    grad_hidden_part, gain_mlp_terms = rms_backward(
        hidden, gain_mlp.astype(jnp.float32), inv_second, grad_normed_mlp
    )
    grad_hidden = grad_rows + grad_hidden_part
    grad_branch_low = grad_hidden.astype(jnp.bfloat16)
    grad_mixed_low = (
        back_product(grad_branch_low, w_output)
        .astype(jnp.bfloat16)
        .reshape(seqs_here, per_device, width)
    )
    heads_grad = lax.all_to_all(grad_mixed_low, "seq", split_axis=2, concat_axis=1, tiled=True)
    query_index, key_index, query_seg, key_seg = masks_for(
        lengths, blk_index, per_device, blk_count, seq_count
    )
    grad_heads_query, grad_keys_all, grad_values_all = lax.map(
        lambda operands: attend_backward(operands, query_index, key_index, kv_local),
        (heads_query, keys_all, values_all, heads_grad, log_total, query_seg, key_seg),
    )
    grad_key_own, grad_value_own = (
        lax.psum_scatter(
            grad_keys_all.astype(jnp.bfloat16), "blk", scatter_dimension=1, tiled=True
        ).astype(jnp.float32),
        lax.psum_scatter(
            grad_values_all.astype(jnp.bfloat16), "blk", scatter_dimension=1, tiled=True
        ).astype(jnp.float32),
    )
    token_query, token_key, token_value = (
        lax.all_to_all(grad_heads_query, "seq", split_axis=1, concat_axis=2, tiled=True),
        lax.all_to_all(
            grad_key_own.astype(jnp.bfloat16), "seq", split_axis=1, concat_axis=2, tiled=True
        ),
        lax.all_to_all(
            grad_value_own.astype(jnp.bfloat16), "seq", split_axis=1, concat_axis=2, tiled=True
        ),
    )
    grad_key_sum = jnp.sum(
        token_key.astype(jnp.float32).reshape(token_rows, KV_HEADS, copies, HEAD_DIM), axis=2
    )
    grad_value_sum = jnp.sum(
        token_value.astype(jnp.float32).reshape(token_rows, KV_HEADS, copies, HEAD_DIM), axis=2
    )
    grad_query_low = (
        rotate(token_query.astype(jnp.float32).reshape(token_rows, HEADS, HEAD_DIM), position, -1.0)
        .astype(jnp.bfloat16)
        .reshape(token_rows, width)
    )
    grad_key_low = (
        rotate(grad_key_sum, position, -1.0)
        .astype(jnp.bfloat16)
        .reshape(token_rows, KV_HEADS * HEAD_DIM)
    )
    grad_value_low = grad_value_sum.astype(jnp.bfloat16).reshape(token_rows, KV_HEADS * HEAD_DIM)
    grad_normed = (
        back_product(grad_query_low, w_query)
        + back_product(grad_key_low, w_key)
        + back_product(grad_value_low, w_value)
    )
    grad_in_part, gain_attn_terms = rms_backward(
        flat_in, gain_attn.astype(jnp.float32), inv_first, grad_normed
    )
    grad_input = (grad_hidden + grad_in_part).reshape(upstream.shape)
    weight_rows = (
        gain_attn_terms,
        normed_low,
        grad_query_low,
        grad_key_low,
        grad_value_low,
        token_mixed,
        grad_branch_low,
        gain_mlp_terms,
        normed_mlp_low,
        grad_gate_low,
        grad_up_low,
        act_low,
        grad_out_low,
    )
    return (grad_input, weight_rows)


def weight_term(inputs_low, outputs_low):
    if outputs_low is None:
        return jnp.sum(inputs_low, axis=0)
    return lax.dot_general(
        inputs_low, outputs_low, (((0,), (0,)), ((), ())), preferred_element_type=jnp.float32
    )


def shards(
    inputs,
    cotangent,
    doc_lengths,
    attention_gain,
    w_query,
    w_key,
    w_value,
    w_output,
    mlp_gain,
    w_gate,
    w_up,
    w_down,
):
    at_first = lax.axis_index("section") == 0
    seq_count = lax.axis_size("seq")
    blk_count = lax.axis_size("blk")
    blk_index = lax.axis_index("blk")
    shard_id = lax.axis_index("seq") * blk_count + blk_index
    placing = (shard_id, blk_index, seq_count, blk_count)
    micro_count = inputs.shape[0]
    local_shards = (
        attention_gain[0],
        w_query[0],
        w_key[0],
        w_value[0],
        w_output[0],
        mlp_gain[0],
        w_gate[0],
        w_up[0],
        w_down[0],
    )
    weights = (
        lax.all_gather(local_shards[0], "blk", axis=0, tiled=True),
        lax.all_gather(local_shards[1], "blk", axis=0, tiled=True),
        lax.all_gather(local_shards[2], "blk", axis=0, tiled=True),
        lax.all_gather(local_shards[3], "blk", axis=0, tiled=True),
        lax.all_gather(local_shards[4], "blk", axis=0, tiled=True),
        lax.all_gather(local_shards[5], "blk", axis=0, tiled=True),
        lax.all_gather(local_shards[6], "blk", axis=0, tiled=True),
        lax.all_gather(local_shards[7], "blk", axis=0, tiled=True),
        lax.all_gather(local_shards[8], "blk", axis=0, tiled=True),
    )
    received = jnp.zeros(inputs.shape[1:], jnp.bfloat16)
    saved_states = []
    section_outs = []
    for tick_index in range(micro_count + 1):
        fresh_input = inputs[min(tick_index, micro_count - 1)]
        section_in = jnp.where(at_first, fresh_input, received).astype(jnp.float32)
        lengths = jnp.where(
            at_first,
            doc_lengths[min(tick_index, micro_count - 1)],
            doc_lengths[max(tick_index - 1, 0)],
        )
        result, saved_state = layer_forward(section_in, lengths, weights, placing)
        result_low = result.astype(jnp.bfloat16)
        if tick_index < micro_count:
            received = passed_along(result_low, "section", 1)
        saved_states.append(saved_state)
        section_outs.append(result_low)
    weights = (
        lax.all_gather(local_shards[0], "blk", axis=0, tiled=True),
        lax.all_gather(local_shards[1], "blk", axis=0, tiled=True),
        lax.all_gather(local_shards[2], "blk", axis=0, tiled=True),
        lax.all_gather(local_shards[3], "blk", axis=0, tiled=True),
        lax.all_gather(local_shards[4], "blk", axis=0, tiled=True),
        lax.all_gather(local_shards[5], "blk", axis=0, tiled=True),
        lax.all_gather(local_shards[6], "blk", axis=0, tiled=True),
        lax.all_gather(local_shards[7], "blk", axis=0, tiled=True),
        lax.all_gather(local_shards[8], "blk", axis=0, tiled=True),
    )
    back_in = jnp.zeros(cotangent.shape[1:], jnp.bfloat16)
    grad_outs = []
    row_sets = []
    for tick_index in range(micro_count + 1):
        saved_state = jax.tree.map(
            lambda first_pick, second_pick: jnp.where(at_first, first_pick, second_pick),
            saved_states[max(tick_index - 1, 0)],
            saved_states[min(tick_index + 1, micro_count)],
        )
        upstream = jnp.where(at_first, back_in, cotangent[min(tick_index, micro_count - 1)]).astype(
            jnp.float32
        )
        grad_input, weight_rows = layer_backward(upstream, saved_state, weights, placing)
        grad_low = grad_input.astype(jnp.bfloat16)
        if tick_index < micro_count:
            back_in = passed_along(grad_low, "section", -1)
        grad_outs.append(grad_low)
        row_sets.append(weight_rows)
    activations = jnp.stack(
        [
            jnp.where(at_first, section_outs[index_m], section_outs[index_m + 1])
            for index_m in range(micro_count)
        ]
    )[None]
    input_grads = jnp.stack(
        [
            jnp.where(at_first, grad_outs[index_m + 1], grad_outs[index_m])
            for index_m in range(micro_count)
        ]
    )[None]
    picked = [
        jax.tree.map(
            lambda first_pick, second_pick: jnp.where(at_first, first_pick, second_pick),
            row_sets[index_m + 1],
            row_sets[index_m],
        )
        for index_m in range(micro_count)
    ]
    merged = jax.tree.map(lambda *pieces: jnp.concatenate(pieces, axis=0), *picked)
    (
        gain_attn_terms,
        normed_low,
        grad_query_low,
        grad_key_low,
        grad_value_low,
        token_mixed,
        grad_branch_low,
        gain_mlp_terms,
        normed_mlp_low,
        grad_gate_low,
        grad_up_low,
        act_low,
        grad_out_low,
    ) = merged
    grad_pairs = (
        (gain_attn_terms, None),
        (normed_low, grad_query_low),
        (normed_low, grad_key_low),
        (normed_low, grad_value_low),
        (token_mixed, grad_branch_low),
        (gain_mlp_terms, None),
        (normed_mlp_low, grad_gate_low),
        (normed_mlp_low, grad_up_low),
        (act_low, grad_out_low),
    )
    shares = tuple(
        (
            lax.psum_scatter(
                weight_term(left_side, right_side).astype(jnp.bfloat16),
                "blk",
                scatter_dimension=0,
                tiled=True,
            ).astype(jnp.float32)
            for left_side, right_side in grad_pairs
        )
    )
    shares = jax.tree.map(lambda part: part.astype(jnp.float32), lax.psum(shortened(shares), "seq"))
    return (
        activations,
        input_grads,
        shares[0][None],
        shares[1][None],
        shares[2][None],
        shares[3][None],
        shares[4][None],
        shares[5][None],
        shares[6][None],
        shares[7][None],
        shares[8][None],
    )


MESH = pl.DeviceIdType.MESH


def remote(source, target, sent, arrived, device):
    return pltpu.make_async_remote_copy(
        source, target, sent, arrived, device_id=device, device_id_type=MESH
    )


def greet(partners):
    barrier = pltpu.get_barrier_semaphore()
    for device in partners:
        pl.semaphore_signal(barrier, 1, device_id=device, device_id_type=MESH)
    pl.semaphore_wait(barrier, len(partners))


def settled(spot, semaphore, received):
    copy = remote(spot, spot, semaphore, semaphore, {"seq": lax.axis_index("seq") ^ 1})
    if received:
        copy.wait_recv()
    else:
        copy.wait_send()


CUTS = 2


def gather_steps(
    count, own, out, line_sent, line_got, side_sent, side_got, core_sent, core_got, local_done
):
    seq, b = lax.axis_index("seq"), lax.axis_index("blk")
    core, side = {"seq": seq ^ 1}, {"seq": seq ^ 2}
    base, side_base = seq * count, (seq ^ 2) * count
    cut = out.shape[1] // CUTS

    def spot(index, h):
        return out.at[index, pl.ds(h * cut, cut)]

    def begin(index, h, first):
        return own.at[pl.ds(h * cut, cut)] if first else spot(index, h)

    def along_line(j, way, h, first=False):
        device = {"blk": b + (1 if way else -1)}
        return remote(
            begin(base + j, h, first),
            spot(base + j, h),
            line_sent.at[j, way, h],
            line_got.at[j, h],
            device,
        )

    def to_side(j, h, first=False):
        return remote(
            begin(base + j, h, first),
            spot(base + j, h),
            side_sent.at[j, h],
            side_got.at[j, h],
            side,
        )

    def to_core(half, j, h, first=False):
        index = (side_base if half else base) + j
        return remote(
            begin(index, h, first),
            spot(index, h),
            core_sent.at[half, j, h],
            core_got.at[half, j, h],
            core,
        )

    local = pltpu.make_async_copy(own, out.at[base + b], local_done)
    local.start()
    for h in range(CUTS):
        to_side(b, h, True).start()
        pl.when(b > 0)(along_line(b, 0, h, True).start)
        pl.when(b < count - 1)(along_line(b, 1, h, True).start)
    for h in range(CUTS):
        to_core(0, b, h, True).start()
    yield "sent"

    def from_line(j, way):
        for h in range(CUTS):
            settled(spot(base + j, h), line_got.at[j, h], True)
            pl.when((b < count - 1) if way else (b > 0))(along_line(j, way, h).start)
            to_side(j, h).start()
        for h in range(CUTS):
            to_core(0, j, h).start()

    def from_side(j):
        for h in range(CUTS):
            settled(spot(side_base + j, h), side_got.at[j, h], True)
            to_core(1, j, h).start()

    for k in range(1, count + 1):
        if k < count:
            pl.when(b - k >= 0)(functools.partial(from_line, b - k, 1))
            pl.when(b + k < count)(functools.partial(from_line, b + k, 0))
        if k == 1:
            from_side(b)
        else:
            pl.when(b - k + 1 >= 0)(functools.partial(from_side, b - k + 1))
            pl.when(b + k - 1 < count)(functools.partial(from_side, b + k - 1))
        if k == count - 1:
            local.wait()
        yield "line" if k == count - 1 else "side" if k == count else "step"
    for half, corner in ((0, seq ^ 1), (1, seq ^ 3)):
        for j in range(count):
            for h in range(CUTS):
                settled(spot(corner * count + j, h), core_got.at[half, j, h], True)
        yield "corner" if half else "near"
    yield "done"
    for h in range(CUTS):
        for j in range(count):
            to_side(j, h).wait_send()
            to_core(0, j, h).wait_send()
            to_core(1, j, h).wait_send()
        pl.when(b > 0)(along_line(b, 0, h).wait_send)
        pl.when(b < count - 1)(along_line(b, 1, h).wait_send)
        for k in range(1, count):
            pl.when((b - k >= 0) & (b < count - 1))(along_line(b - k, 1, h).wait_send)
            pl.when((b + k < count) & (b > 0))(along_line(b + k, 0, h).wait_send)


def gather_semaphores(count):
    dma = pltpu.SemaphoreType.DMA
    return [
        dma((count, 2, CUTS)),
        dma((count, CUTS)),
        dma((count, CUTS)),
        dma((count, CUTS)),
        dma((2, count, CUTS)),
        dma((2, count, CUTS)),
        dma,
    ]


def line_steps(
    count, own, out, line_sent, line_got, core_sent, core_got, local_done, offset=0
):
    seq, b = lax.axis_index("seq"), lax.axis_index("blk")
    core, base = {"seq": seq ^ 1}, offset + (seq % 2) * count
    cut = out.shape[1] // CUTS

    def spot(j, h):
        return out.at[base + j, pl.ds(h * cut, cut)]

    def begin(j, h, first):
        return own.at[pl.ds(h * cut, cut)] if first else spot(j, h)

    def along_line(j, way, h, first=False):
        device = {"blk": b + (1 if way else -1)}
        return remote(
            begin(j, h, first), spot(j, h), line_sent.at[j, way, h], line_got.at[j, h], device
        )

    def to_core(j, h, first=False):
        return remote(begin(j, h, first), spot(j, h), core_sent.at[j, h], core_got.at[j, h], core)

    local = pltpu.make_async_copy(own, out.at[base + b], local_done)
    local.start()
    for h in range(CUTS):
        pl.when(b > 0)(along_line(b, 0, h, True).start)
        pl.when(b < count - 1)(along_line(b, 1, h, True).start)
        to_core(b, h, True).start()
    yield

    def from_line(j, way):
        for h in range(CUTS):
            settled(spot(j, h), line_got.at[j, h], True)
            pl.when((b < count - 1) if way else (b > 0))(along_line(j, way, h).start)
            to_core(j, h).start()

    for k in range(1, count):
        pl.when(b - k >= 0)(functools.partial(from_line, b - k, 1))
        pl.when(b + k < count)(functools.partial(from_line, b + k, 0))
        yield
    local.wait()
    for h in range(CUTS):
        for j in range(count):
            place = offset + (1 - seq % 2) * count + j
            settled(out.at[place, pl.ds(h * cut, cut)], core_got.at[j, h], True)
            to_core(j, h).wait_send()
        pl.when(b > 0)(along_line(b, 0, h).wait_send)
        pl.when(b < count - 1)(along_line(b, 1, h).wait_send)
        for k in range(1, count):
            pl.when((b - k >= 0) & (b < count - 1))(along_line(b - k, 1, h).wait_send)
            pl.when((b + k < count) & (b > 0))(along_line(b + k, 0, h).wait_send)


def line_semaphores(count):
    dma = pltpu.SemaphoreType.DMA
    return [
        dma((count, 2, CUTS)),
        dma((count, CUTS)),
        dma((count, CUTS)),
        dma((count, CUTS)),
        dma,
    ]


def advance(steps, times):
    for _ in range(times):
        next(steps, None)


def until_done(steps):
    for event in steps:
        if event == "done":
            return
        yield event


def all_but_last(compute):
    groups = []

    def some(group):
        groups.append(group)
        if len(groups) < 4:
            compute(group)

    return some


def group_of(event):
    seq = lax.axis_index("seq")
    return {"line": seq, "side": seq ^ 2, "near": seq ^ 1, "corner": seq ^ 3}.get(event)


def scatter_steps(
    count,
    partial,
    deliver,
    core_slot,
    side_slot,
    line_slot,
    side_out,
    line_out,
    running,
    core_sent,
    core_got,
    side_sent,
    side_got,
    line_sent,
    line_got,
    compute=None,
):
    seq, b = lax.axis_index("seq"), lax.axis_index("blk")
    core, side = {"seq": seq ^ 1}, {"seq": seq ^ 2}
    place = far_first(b, count)
    size = partial.shape[1] // CUTS
    cuts = [pl.ds(h * size, size) for h in range(CUTS)]

    def to_core(half, k, h):
        return remote(
            partial.at[(seq ^ (1 if half else 3)) * count + place[k], cuts[h]],
            core_slot.at[half, k, cuts[h]],
            core_sent.at[half, k, h],
            core_got.at[half, k, h],
            core,
        )

    def to_side(k, h):
        return remote(
            side_out.at[k, cuts[h]],
            side_slot.at[k, cuts[h]],
            side_sent.at[k, h],
            side_got.at[k, h],
            side,
        )

    def along_line(k, way, h):
        j = place[k]
        return remote(
            line_out.at[k, cuts[h]],
            line_slot.at[way, j, cuts[h]],
            line_sent.at[k, h],
            line_got.at[way, j, h],
            {"blk": b + (1 if way else -1)},
        )

    def add_from(way, j, h):
        settled(line_slot.at[way, j, cuts[h]], line_got.at[way, j, h], True)
        running[cuts[h]] += line_slot[way, j, cuts[h]].astype(jnp.float32)

    def exchange(half):
        if compute:
            compute(seq ^ (1 if half else 3))
        for k in range(count):
            for h in range(CUTS):
                to_core(half, k, h).start()

    exchange(0)
    if compute:
        compute(seq ^ 2)
    for k in range(count):
        for h in range(CUTS):
            to_core(0, k, h).wait_recv()
            total = partial[(seq ^ 2) * count + place[k], cuts[h]].astype(jnp.float32)
            total += core_slot[0, k, cuts[h]].astype(jnp.float32)
            side_out[k, cuts[h]] = total.astype(jnp.bfloat16)
            to_side(k, h).start()
    exchange(1)
    if compute:
        compute(seq)
    yield
    for k in range(count):
        j = place[k]
        rightward, leftward = j >= b, j <= b
        for h in range(CUTS):
            to_core(1, k, h).wait_recv()
            to_side(k, h).wait_recv()
            total = partial[seq * count + j, cuts[h]].astype(jnp.float32)
            total += core_slot[1, k, cuts[h]].astype(jnp.float32)
            running[cuts[h]] = total + side_slot[k, cuts[h]].astype(jnp.float32)
            pl.when(rightward & (b > 0))(functools.partial(add_from, 1, j, h))
            pl.when(leftward & (b < count - 1))(functools.partial(add_from, 0, j, h))
            if k < count - 1:
                line_out[k, cuts[h]] = running[cuts[h]].astype(jnp.bfloat16)
                pl.when(rightward)(along_line(k, 1, h).start)
                pl.when(jnp.logical_not(rightward))(along_line(k, 0, h).start)
        if k < count - 1:
            yield
    deliver(running[...])
    yield
    for k in range(count):
        for h in range(CUTS):
            to_core(0, k, h).wait_send()
            to_core(1, k, h).wait_send()
            to_side(k, h).wait_send()
            if k < count - 1:
                settled(line_out.at[k, cuts[h]], line_sent.at[k, h], False)


def line_first_steps(
    count,
    partial,
    deliver,
    own,
    core_slot,
    line_slot,
    line_out,
    side_slot,
    running,
    own_done,
    core_sent,
    core_got,
    line_sent,
    line_got,
    side_sent,
    side_got,
):
    seq, b = lax.axis_index("seq"), lax.axis_index("blk")
    core, side = {"seq": seq ^ 1}, {"seq": seq ^ 2}
    place = far_first(b, count)

    def to_core(half, k):
        source = partial.at[(seq ^ (1 if half else 3)) * count + place[k]]
        return remote(
            source, core_slot.at[half, k], core_sent.at[half, k], core_got.at[half, k], core
        )

    def kept(half, k):
        source = partial.at[(seq if half else seq ^ 2) * count + place[k]]
        return pltpu.make_async_copy(source, own.at[half, k], own_done.at[half, k])

    def along_line(half, k, way):
        j = place[k]
        return remote(
            line_out.at[half, k],
            line_slot.at[half, way, j],
            line_sent.at[half, k],
            line_got.at[half, way, j],
            {"blk": b + (1 if way else -1)},
        )

    def add_from(half, way, j):
        settled(line_slot.at[half, way, j], line_got.at[half, way, j], True)
        running[...] += line_slot[half, way, j].astype(jnp.float32)

    to_side = remote(line_out.at[0, count - 1], side_slot.at[0], side_sent, side_got, side)
    for half in range(2):
        for k in range(count):
            kept(half, k).start()
            to_core(half, k).start()
    yield
    for k in range(count):
        j = place[k]
        rightward, leftward = j >= b, j <= b
        for half in range(2):
            kept(half, k).wait()
            to_core(half, k).wait_recv()
            running[...] = own[half, k].astype(jnp.float32) + core_slot[half, k].astype(jnp.float32)
            pl.when(rightward & (b > 0))(functools.partial(add_from, half, 1, j))
            pl.when(leftward & (b < count - 1))(functools.partial(add_from, half, 0, j))
            if half == 0 or k < count - 1:
                line_out[half, k] = running[...].astype(jnp.bfloat16)
            if k < count - 1:
                pl.when(rightward)(along_line(half, k, 1).start)
                pl.when(jnp.logical_not(rightward))(along_line(half, k, 0).start)
            elif half == 0:
                to_side.start()
            else:
                to_side.wait_recv()
                deliver(running[...] + side_slot[0].astype(jnp.float32))
            yield
    to_side.wait_send()
    for half in range(2):
        for k in range(count):
            to_core(half, k).wait_send()
            if k < count - 1:
                settled(line_out.at[half, k], line_sent.at[half, k], False)


def far_first(b, count):
    order = sorted(range(count), key=lambda j: -j)
    places = []
    for k in range(count):
        place = 0
        for own in range(count):
            by_distance = sorted(order, key=lambda j: (-abs(j - own), -j if own * 2 < count else j))
            place = jnp.where(b == own, by_distance[k], place)
        places.append(place)
    return places


def scatter_scratch(count, rows, width):
    dma = pltpu.SemaphoreType.DMA

    def slots(*places):
        return pltpu.VMEM(places + (rows, width), jnp.bfloat16)

    return [
        slots(2, count),
        slots(count),
        slots(2, count),
        slots(count),
        slots(count - 1),
        pltpu.VMEM((rows, width), jnp.float32),
        dma((2, count, CUTS)),
        dma((2, count, CUTS)),
        dma((count, CUTS)),
        dma((count, CUTS)),
        dma((count - 1, CUTS)),
        dma((2, count, CUTS)),
    ]


def run_all(fillers):
    for filler in fillers:
        filler()


def run_with(steps, fillers):
    fillers = list(fillers)
    for _ in steps:
        if fillers:
            fillers.pop(0)()
    for filler in fillers:
        filler()


def greet_group(count, more=()):
    seq, b = lax.axis_index("seq"), lax.axis_index("blk")
    greet(
        tuple(more)
        + ({"seq": seq ^ 1}, {"seq": seq ^ 2})
        + tuple({"blk": lax.rem(b + k, count)} for k in range(1, count))
    )


def carry(copies, from_section, what):
    sending = lax.axis_index("section") == from_section
    for copy in copies:
        if what == "start":
            pl.when(sending)(copy.start)
        else:
            pl.when(sending)(copy.wait_send)
            pl.when(jnp.logical_not(sending))(copy.wait_recv)


def carried(sources, targets, sent, got):
    other = {"section": 1 - lax.axis_index("section")}
    return [
        remote(source, target, sent.at[n], got.at[n], other)
        for n, (source, target) in enumerate(zip(sources, targets))
    ]


def group_rows(ref, group, count):
    value = ref[pl.ds(group * count, count)]
    return value.reshape(value.shape[0] * value.shape[1], value.shape[2])


def group_span(group, count, block):
    size = count * block
    return pl.ds(pl.multiple_of(group * size, size), size)


def lane_turn(field_in, cosine, sine):
    half_dim, lanes = HEAD_DIM // 2, field_in.shape[-1]
    lane = lax.broadcasted_iota(jnp.int32, field_in.shape, 1)
    partner = jnp.where(
        lane < half_dim,
        pltpu.roll(field_in, lanes - half_dim, 1),
        pltpu.roll(field_in, half_dim, 1),
    )
    return field_in * cosine + partner * sine


def masked_scores(query, key, first_row, start):
    scores = back_product(query, key) * HEAD_DIM ** (-0.5)
    key_index = lax.broadcasted_iota(jnp.int32, scores.shape, 1)
    query_index = first_row + lax.broadcasted_iota(jnp.int32, scores.shape, 0)
    return jnp.where((key_index >= start) & (key_index <= query_index), scores, MASKED)


def normalise(field_in, gain_row):
    inv_root = lax.rsqrt(jnp.mean(field_in * field_in, axis=-1, keepdims=True) + EPS)
    return field_in * inv_root * gain_row


PAD = 128


GAINS = HEAD_DIM
OWN_PART = HEAD_DIM + 16


def load_weights(layer, attn, twin, out, attn_vm, out_vm, sems):
    on_key = lax.axis_index("seq") % 2 == 0
    own, other = attn.at[layer, pl.ds(OWN_PART, HEAD_DIM)], twin.at[layer]

    def part(source, n, rows):
        return pltpu.make_async_copy(source, attn_vm.at[pl.ds(n * PAD, rows)], sems.at[n])

    copies = [
        part(attn.at[layer, pl.ds(0, HEAD_DIM)], 0, HEAD_DIM),
        part(attn.at[layer, pl.ds(GAINS, 16)], 3, 16),
    ]
    if out is not None:
        copies.append(
            pltpu.make_async_copy(out.at[layer], out_vm.at[pl.ds(0, HEAD_DIM)], sems.at[4])
        )
    start_all(copies)

    @pl.when(on_key)
    def _():
        part(own, 1, HEAD_DIM).start()
        part(other, 2, HEAD_DIM).start()

    @pl.when(jnp.logical_not(on_key))
    def _():
        part(other, 1, HEAD_DIM).start()
        part(own, 2, HEAD_DIM).start()

    return copies + [part(other, 1, HEAD_DIM), part(other, 2, HEAD_DIM)]


def clear_pads(attn_vm, out_vm):
    empty = jnp.zeros((PAD - HEAD_DIM, attn_vm.shape[1]), jnp.bfloat16)
    for part in range(3):
        attn_vm[part * PAD + HEAD_DIM : (part + 1) * PAD] = empty
    out_vm[HEAD_DIM:PAD] = empty


def attention_rows(heads, log_total, start, size, tokens):
    for i in range(tokens // size):
        here, seen = slice(i * size, (i + 1) * size), slice(0, (i + 1) * size)
        scores = masked_scores(heads[0, here], heads[1, seen], i * size, start[here])
        row_top = jnp.max(scores, axis=-1, keepdims=True)
        weights = jnp.exp(scores - row_top)
        total = jnp.sum(weights, axis=-1, keepdims=True)
        log_total[here] = row_top + jnp.log(total)
        weights = (weights * (1.0 / total)).astype(jnp.bfloat16)
        heads[3, here] = product(weights, heads[2, seen]).astype(jnp.bfloat16)


def project_heads(normed, attn_vm, heads, span, cosine, sine):
    mixed = back_product(normed, attn_vm[0 : 3 * PAD])
    cos_rows, sin_rows = cosine[span], sine[span]
    heads[0, span] = lane_turn(mixed[:, :PAD], cos_rows, sin_rows).astype(jnp.bfloat16)
    heads[1, span] = lane_turn(mixed[:, PAD : 2 * PAD], cos_rows, sin_rows).astype(jnp.bfloat16)
    heads[2, span] = mixed[:, 2 * PAD :].astype(jnp.bfloat16)


def keep_group(partial, group, value, count):
    block = partial.shape[1]
    partial[pl.ds(group * count, count)] = value.astype(jnp.bfloat16).reshape(count, block, -1)


def gain_of(ref, row):
    return ref[3 * PAD : 3 * PAD + 16][row : row + 1].astype(jnp.float32)


def fill_tables(lengths, frequency, cosine, sine, start):
    section = lax.axis_index("section")
    token = lax.broadcasted_iota(jnp.int32, start.shape, 0)
    end, begin = 0, jnp.zeros(start.shape, jnp.int32)
    for n in range(lengths.shape[2]):
        length = lengths[section, 0, n]
        end = end + length
        begin = begin + jnp.where(end <= token, length, 0)
    start[...] = begin
    lane = lax.broadcasted_iota(jnp.int32, cosine.shape, 1)
    angles = (token - begin).astype(jnp.float32) * frequency[...]
    cosine[...] = jnp.where(lane < HEAD_DIM, jnp.cos(angles), 0.0)
    turned = jnp.where(lane < HEAD_DIM, jnp.sin(angles), 0.0)
    sine[...] = jnp.where(lane < HEAD_DIM // 2, -turned, turned)


def first_layer_kernel(count, *refs):
    refs = iter(refs)

    def take(n):
        return [next(refs) for _ in range(n)]

    w_query, w_key, w_value, w_gate, w_up, w_output, w_down = take(7)
    gain_attn, gain_mlp, inputs, cotangent, lengths, frequency = take(6)
    attn, twin, gate_up, out, down, all_rows, wide_rows, grads_near, grads_side = take(9)
    cosine, sine, start = take(3)
    hidden, result_out, normed_out, heads, log_total = take(5)
    raw_vm, normed_vm, rows_vm, partial, partial_two, grads_vm = take(6)
    attn_vm, out_vm, wide_vm, down_vm, units, normed_own, gain_vm = take(7)
    pieces, query_vm, other_vm, query_turned, other_turned, weights_done = take(6)
    load_done, save_done, twin_sent, twin_got = take(4)
    spread_sems = take(5)
    first_sems, second_sems, grads_sems, side_sems = take(7), take(7), take(5), take(2)
    scatter_one, scatter_two = take(12), take(12)
    section = lax.axis_index("section")
    block, width = raw_vm.shape[1], raw_vm.shape[2]
    tokens = block * raw_vm.shape[0]
    size = count * block
    low, f32 = jnp.bfloat16, jnp.float32
    seq = lax.axis_index("seq")
    rows_in, grads_in = inputs.at[section, 0], cotangent.at[section, 0]
    query_load = pltpu.make_async_copy(w_query, query_vm, weights_done.at[0])
    query_load.start()
    key_load = pltpu.make_async_copy(w_key, other_vm, weights_done.at[1])
    value_load = pltpu.make_async_copy(w_value, other_vm, weights_done.at[1])
    pl.when(seq % 2 == 0)(key_load.start)
    pl.when(seq % 2 == 1)(value_load.start)
    greet_group(count, ({"section": 1 - section},))
    steps = gather_steps(count, rows_in, raw_vm, *first_sems)
    next(steps)
    query_load.wait()
    key_load.wait()
    query_turned[...] = query_vm[...].astype(f32).T.astype(low)
    other_turned[...] = other_vm[...].astype(f32).T.astype(low)
    row = lax.broadcasted_iota(jnp.int32, (16, gain_attn.shape[1]), 0)
    own_gains = jnp.where(row == 0, gain_attn[...], jnp.where(row == 1, gain_mlp[...], 0))
    per_blk = other_turned.shape[0] // HEAD_DIM // count
    for j in range(count):
        head = j * 4 + seq
        other_head = j * per_blk + seq * per_blk // 4
        for place, turned, index in (
            (0, query_turned, head),
            (OWN_PART, other_turned, other_head),
        ):
            rows = pl.ds(pl.multiple_of(index * HEAD_DIM, 16), HEAD_DIM)
            pieces[j, place : place + HEAD_DIM] = turned[rows]
        pieces[j, GAINS : GAINS + 16] = own_gains.astype(low)
    spread = spread_steps(
        count, pieces, w_gate, w_up, w_output, w_down, attn, gate_up, out, down, *spread_sems
    )
    next(spread)
    fill_tables(lengths, frequency, cosine, sine, start)
    clear_pads(attn_vm, out_vm)
    for event in until_done(steps):
        if event == "line":
            advance(spread, 3)
    grads_across = remote(
        grads_in, grads_side, *side_sems, {"seq": lax.axis_index("seq") ^ 2}
    )
    grads_across.start()
    next(spread)
    pair = remote(
        attn.at[:, pl.ds(OWN_PART, HEAD_DIM)],
        twin,
        twin_sent,
        twin_got,
        {"seq": lax.axis_index("seq") ^ 1},
    )
    pair.start()
    pair.wait()
    gain_load = pltpu.make_async_copy(attn.at[1, pl.ds(GAINS, 16)], gain_vm, load_done.at[5])
    gain_load.start()
    wait_all(load_weights(0, attn, twin, None, attn_vm, out_vm, load_done) + [gain_load])
    for group in range(tokens // size):
        raw = raw_vm[group * count : (group + 1) * count].astype(f32)
        normed = normalise(raw, gain_of(attn_vm, 0)[None]).astype(low)
        normed_vm[group * count : (group + 1) * count] = normed
        span = slice(group * size, (group + 1) * size)
        project_heads(normed.reshape(size, width), attn_vm, heads, span, cosine, sine)
    saves = [pltpu.make_async_copy(normed_vm, all_rows, save_done.at[0])]
    saves[0].start()
    attention_rows(heads, log_total, start, size, tokens)
    next(spread)
    load = pltpu.make_async_copy(out.at[0], out_vm.at[pl.ds(0, HEAD_DIM)], load_done.at[4])
    load.start()
    load.wait()

    def project_out(group):
        mixed = heads[3, group_span(group, count, block)]
        keep_group(partial, group, product(mixed, out_vm[...]), count)

    def deliver(total):
        value = rows_in[...].astype(f32) + total
        hidden[...] = value
        normed_own[...] = normalise(value, gain_of(attn_vm, 1)).astype(low)

    def more():
        next(spread)

    run_with(scatter_steps(count, partial, deliver, *scatter_one, compute=project_out), [more] * 5)
    for _ in steps:
        pass
    steps = gather_steps(count, normed_own, rows_vm, *second_sems)
    for number, event in enumerate(until_done(steps)):
        if number == 0:
            more()
    for _ in spread:
        pass
    loads = [
        pltpu.make_async_copy(gate_up.at[0], wide_vm, load_done.at[0]),
        pltpu.make_async_copy(down.at[0], down_vm, load_done.at[1]),
    ]
    start_all(loads)
    wait_all(loads)
    saves.append(pltpu.make_async_copy(rows_vm, wide_rows, save_done.at[1]))
    saves[1].start()

    def project_down(group):
        pre = product(group_rows(rows_vm, group, count), wide_vm[...])
        made = hidden_units(pre)
        units[group_span(group, count, block)] = made
        keep_group(partial_two, group, product(made, down_vm[...]), count)

    grad_steps = line_steps(count, grads_in, grads_vm, *grads_sems)
    next(grad_steps)

    def deliver_two(total):
        made = (hidden[...] + total).astype(low)
        result_out[...] = made
        gain = gain_vm[...][0:1].astype(f32)
        normed_out[...] = normalise(made.astype(f32), gain).astype(low)

    run_with(
        scatter_steps(count, partial_two, deliver_two, *scatter_two, compute=project_down),
        [functools.partial(advance, grad_steps, 1)] * 3,
    )
    for _ in grad_steps:
        pass
    for _ in steps:
        pass
    saves.append(pltpu.make_async_copy(grads_vm, grads_near, save_done.at[2]))
    saves[2].start()
    grads_across.wait()
    wait_all(saves)


def spread_steps(
    count,
    pieces,
    w_gate,
    w_up,
    w_output,
    w_down,
    attn,
    gate_up,
    out,
    down,
    line_sent,
    line_got,
    cross_sent,
    cross_got,
    local_done,
):
    seq, b, section = lax.axis_index("seq"), lax.axis_index("blk"), lax.axis_index("section")
    seq_count = lax.axis_size("seq")
    other = {"section": 1 - section}
    rows, lanes = w_gate.shape[0], gate_up.shape[2] // 2
    turns = tuple(range(count // 2, 0, -1)) + tuple(range(count // 2 + 1, count))

    def source(kind, j):
        if kind == 0:
            return pieces.at[j]
        weight = w_gate if kind == 1 else w_up
        return weight.at[:, pl.ds(pl.multiple_of((j * seq_count + seq) * lanes, lanes), lanes)]

    def target(kind, j):
        if kind == 0:
            return attn.at[section, :, pl.ds(pl.multiple_of(j * rows, rows), rows)]
        return gate_up.at[
            section, pl.ds(pl.multiple_of(j * rows, rows), rows), pl.ds((kind - 1) * lanes, lanes)
        ]

    def along_line(kind, k):
        j = lax.rem(b + k, count)
        return remote(
            source(kind, j),
            target(kind, b),
            line_sent.at[kind, k],
            line_got.at[kind, k],
            {"blk": j},
        )

    def across(kind, j, slot, begin=None):
        spot = target(kind, j)
        return remote(
            spot if begin is None else begin,
            spot,
            cross_sent.at[kind, slot],
            cross_got.at[kind, slot],
            other,
        )

    def own_rows(kind):
        weight, place = (w_output, out) if kind == 3 else (w_down, down)
        size = place.shape[1]
        begin = weight.at[pl.ds(pl.multiple_of(seq * size, size), size)]
        spot = place.at[section]
        return (
            remote(begin, spot, cross_sent.at[kind, 0], cross_got.at[kind, 0], other),
            pltpu.make_async_copy(begin, spot, local_done.at[kind]),
        )

    def own_piece(kind):
        return (
            across(kind, b, 0, source(kind, b)),
            pltpu.make_async_copy(source(kind, b), target(kind, b), local_done.at[kind]),
        )

    def forward(kind, k):
        j = lax.rem(b + count - k, count)
        settled(target(kind, j), line_got.at[kind, k], True)
        across(kind, j, k).start()

    def arrived(kind):
        if kind > 2:
            wait_all(own_rows(kind))
            return
        for k in range(count):
            settled(target(kind, 0), cross_got.at[kind, k], True)
            settled(target(kind, 0), cross_sent.at[kind, k], False)
            if k:
                settled(target(kind, 0), line_sent.at[kind, k], False)
        pltpu.make_async_copy(source(kind, b), target(kind, b), local_done.at[kind]).wait()

    for k in turns:
        along_line(0, k).start()
    start_all(own_piece(0))
    yield
    for k in turns:
        forward(0, k)
        yield
    start_all(own_rows(3))
    for kind in (1, 2):
        for k in turns:
            along_line(kind, k).start()
    arrived(0)
    start_all(own_piece(1) + own_piece(2) + own_rows(4))
    yield
    arrived(3)
    yield
    for kind in (1, 2):
        for k in turns:
            forward(kind, k)
            yield
    for kind in (1, 2, 4):
        arrived(kind)


def start_all(copies):
    for copy in copies:
        copy.start()


def wait_all(copies):
    for copy in copies:
        copy.wait()


def gated(pre):
    half = pre.shape[1] // 2
    gate, up = pre[:, :half], pre[:, half:]
    sigma = jax.nn.sigmoid(gate)
    return gate, up, sigma


def hidden_units(pre):
    gate, up, sigma = gated(pre)
    return (gate * sigma * up).astype(jnp.bfloat16)


def store_gate_grads(place, span, grad_act, pre):
    gate, up, sigma = gated(pre)
    half = gate.shape[1]
    place[span, 0:half] = (grad_act * up * sigma * (1.0 + gate * (1.0 - sigma))).astype(
        jnp.bfloat16
    )
    place[span, half : 2 * half] = (grad_act * (gate * sigma)).astype(jnp.bfloat16)


def wide_grads(rows_vm, pre_grads, units, grads_vm, wide_grad, down_grad):
    tokens = pre_grads.shape[0]
    width = rows_vm.shape[2]
    step = width // 4

    def wide_part(n):
        cut = slice(n * step, (n + 1) * step)
        rows = rows_vm[:, :, cut].reshape(tokens, step)
        wide_grad[cut] = weight_term(rows, pre_grads[...]).astype(jnp.bfloat16)

    def down_part(n):
        cut = slice(n * 2 * step, (n + 1) * 2 * step)
        rows = grads_vm[:, :, cut].reshape(tokens, 2 * step)
        down_grad[:, cut] = weight_term(units[...], rows).astype(jnp.bfloat16)

    return [functools.partial(wide_part, n) for n in range(4)] + [
        functools.partial(down_part, n) for n in range(2)
    ]


def mlp_grad_sent(total, hidden, grads_own, gain, branch_out, grad_hidden_out, gain_out):
    field_in = hidden[...]
    inv_root = lax.rsqrt(jnp.mean(field_in * field_in, axis=-1, keepdims=True) + EPS)
    part, terms = rms_backward(field_in, gain[...], inv_root, total)
    grad_hidden = grads_own[...].astype(jnp.float32) + part
    grad_hidden_out[...] = grad_hidden
    branch_out[...] = grad_hidden.astype(jnp.bfloat16)
    gain_out[...] = jnp.broadcast_to(jnp.sum(terms, axis=0, keepdims=True), gain_out.shape)


class Parts:
    pass


def attn_back_refs(take, attn_grad=None, out_grad=None):
    r = Parts()
    r.branch_vm, r.rows_vm, r.heads, r.attn_vm, r.out_vm, r.mixed_grads, r.probs = take(7)
    r.key_grads, r.value_grads, r.joint, r.partial, r.load_done = take(5)
    r.gather_sems = take(7)
    r.scatter_refs = take(12)
    return r


def attn_back_body(
    count, layer, r, ins, outs, background, fillers, gathered=None, spare=None
):
    branch_in, grad_hidden, x_own, all_rows, heads_kept, log_total, attn, twin, out = ins[:9]
    cosine, sine, start, gain = ins[9:]
    grad_out, gain_out, attn_grad, out_grad = outs
    branch_vm, rows_vm, heads, attn_vm, out_vm = r.branch_vm, r.rows_vm, r.heads, r.attn_vm, r.out_vm
    mixed_grads, probs, key_grads, value_grads = r.mixed_grads, r.probs, r.key_grads, r.value_grads
    joint, partial, load_done = r.joint, r.partial, r.load_done
    block = rows_vm.shape[1]
    size = count * block
    tokens = block * rows_vm.shape[0]
    low, f32 = jnp.bfloat16, jnp.float32
    scale = HEAD_DIM ** (-0.5)
    steps = gather_steps(count, branch_in, branch_vm, *r.gather_sems)
    next(steps)
    background()
    loads = []
    if layer is not None:
        clear_pads(attn_vm, out_vm)
        loads = load_weights(layer, attn, twin, out, attn_vm, out_vm, load_done)
        kept = [
            pltpu.make_async_copy(heads_kept, heads, load_done.at[5]),
            pltpu.make_async_copy(all_rows, rows_vm, load_done.at[6]),
        ]
        start_all(kept)
        loads += kept
    key_grads[...] = jnp.zeros_like(key_grads)
    value_grads[...] = jnp.zeros_like(value_grads)
    wait_all(loads)

    def spans(i):
        return slice(i * size, (i + 1) * size), slice(0, (i + 1) * size)

    def weigh(i):
        here, seen = spans(i)
        scores = masked_scores(heads[0, here], heads[1, seen], i * size, start[here])
        probs[here, seen] = jnp.exp(scores - log_total[here])

    def project(group):
        value = back_product(group_rows(branch_vm, group, count), out_vm[...])
        mixed_grads[group_span(group, count, block)] = value.astype(low)

    for number, event in enumerate(until_done(steps)):
        if number < 2:
            weigh(2 * number)
            weigh(2 * number + 1)
        group = group_of(event)
        if group is not None:
            project(group)
    if gathered:
        gathered()
    for i in reversed(range(tokens // size)):
        here, seen = spans(i)
        weights = probs[here, seen]
        grads = mixed_grads[here]
        grad_weights = back_product(grads, heads[2, seen])
        centre = jnp.sum(weights * grad_weights, axis=-1, keepdims=True)
        grad_scores = (weights * (grad_weights - centre)).astype(low)
        query_grad = (product(grad_scores, heads[1, seen]) * scale).astype(low).astype(f32)
        joint[here, 0:PAD] = lane_turn(query_grad, cosine[here], -sine[here]).astype(low)
        key_grads[seen] += weight_term(grad_scores, heads[0, here])
        value_grads[seen] += weight_term(weights.astype(low), grads)
        key_grad = (key_grads[here] * scale).astype(low).astype(f32)
        joint[here, PAD : 2 * PAD] = lane_turn(key_grad, cosine[here], -sine[here]).astype(low)
        joint[here, 2 * PAD : 3 * PAD] = value_grads[here].astype(low)

    def project_back(group):
        value = product(joint[group_span(group, count, block)], attn_vm[0 : 3 * PAD])
        partial[pl.ds(group * count, count)] = value.astype(low).reshape(count, block, -1)

    def attn_part(part):
        rows = rows_vm[...].reshape(tokens, rows_vm.shape[2])
        value = weight_term(joint[:, part * PAD : (part + 1) * PAD], rows)
        attn_grad[part * HEAD_DIM : (part + 1) * HEAD_DIM] = value[0:HEAD_DIM].astype(low)

    def out_part():
        rows = branch_vm[...].reshape(tokens, branch_vm.shape[2])
        out_grad[...] = weight_term(heads[3], rows)[0:HEAD_DIM].astype(low)

    def deliver(total):
        field_in = x_own[...].astype(f32)
        inv_root = lax.rsqrt(jnp.mean(field_in * field_in, axis=-1, keepdims=True) + EPS)
        part, terms = rms_backward(field_in, gain[...], inv_root, total)
        grad_out[...] = (grad_hidden[...] + part).astype(low)
        gain_out[...] = jnp.broadcast_to(jnp.sum(terms, axis=0, keepdims=True), gain_out.shape)

    parts = [functools.partial(attn_part, n) for n in range(3)] + [out_part]
    if spare:
        parts.append(spare)
    run_with(
        scatter_steps(count, partial, deliver, *r.scatter_refs, compute=project_back),
        [functools.partial(run_all, parts)] + fillers,
    )
    for _ in steps:
        pass


def middle_kernel(count, *refs):
    refs = iter(refs)

    def take(n):
        return [next(refs) for _ in range(n)]

    rows_in, between, grads_side, cosine, sine, start, attn, twin, out = take(9)
    grads_near, gate_up, down, cotangent, hidden_one, wide_rows = take(6)
    grads_own = cotangent.at[lax.axis_index("section"), 0]
    gain_mlp_two, gain_attn_two, gain_mlp_one = take(3)
    hidden, ahead, grad_between, branch_out, grad_hidden_out = take(5)
    mlp_two_sum, attn_two_sum, mlp_one_sum = take(3)
    wide_two, down_two, attn_two, out_two, wide_one, down_one = take(6)
    carried_to = take(4)
    rows_two, grads_vm, partial, wide_vm, down_vm = take(5)
    log_total, units, pre_vm, pre_grads, normed_own, branch_own, grad_hidden = take(7)
    load_done, carry_sent, carry_got = take(3)
    line_sems = take(5)
    r = attn_back_refs(take)
    rows_one, heads, attn_vm, out_vm, partial_back = (
        r.rows_vm,
        r.heads,
        r.attn_vm,
        r.out_vm,
        r.partial,
    )
    blocks, block = rows_one.shape[0], rows_one.shape[1]
    size, tokens, half = count * block, blocks * block, blocks // 2
    near = lax.axis_index("seq") // 2 * half
    greet_group(count, ({"section": 1 - lax.axis_index("section")},))
    steps = gather_steps(count, rows_in, rows_one, *r.gather_sems)
    next(steps)
    clear_pads(attn_vm, out_vm)
    loads = load_weights(1, attn, twin, out, attn_vm, out_vm, r.load_done)
    wide_loads = [
        pltpu.make_async_copy(gate_up.at[1], wide_vm, load_done.at[0]),
        pltpu.make_async_copy(down.at[1], down_vm, load_done.at[1]),
        pltpu.make_async_copy(grads_near, grads_vm.at[pl.ds(near, half)], load_done.at[2]),
    ]
    start_all(wide_loads)
    for event in until_done(steps):
        if event == "line":
            wait_all(loads)
        group = group_of(event)
        if group is not None:
            span = group_span(group, count, block)
            normed = group_rows(rows_one, group, count)
            project_heads(normed, attn_vm, heads, span, cosine, sine)
    grad_steps = line_steps(count, grads_side, grads_vm, *line_sems, offset=half - near)
    next(grad_steps)
    attention_rows(heads, log_total, start, size, tokens)

    def project_out(group):
        mixed = heads[3, group_span(group, count, block)]
        keep_group(partial, group, product(mixed, out_vm[...]), count)

    def deliver(total):
        value = between[...].astype(jnp.float32) + total
        hidden[...] = value
        normed_own[...] = normalise(value, gain_of(attn_vm, 1)).astype(jnp.bfloat16)

    run_with(
        scatter_steps(count, partial, deliver, *r.scatter_refs, compute=project_out),
        [functools.partial(advance, grad_steps, 1)] * 3,
    )
    for _ in steps:
        pass
    steps = gather_steps(count, normed_own, rows_two, *r.gather_sems)
    next(steps)
    for _ in grad_steps:
        pass
    wait_all(wide_loads)

    def through(group):
        span = group_span(group, count, block)
        pre = product(group_rows(rows_two, group, count), wide_vm[...])
        units[span] = hidden_units(pre)
        grad_act = back_product(group_rows(grads_vm, group, count), down_vm[...])
        store_gate_grads(pre_grads, span, grad_act, pre)
        keep_group(partial_back, group, back_product(pre_grads[span], wide_vm[...]), count)

    for event in until_done(steps):
        if event == "line":
            through(group_of(event))

    def project_down(group):
        value = product(units[group * size : (group + 1) * size], down_vm[...])
        partial[group * count : (group + 1) * count] = value.astype(jnp.bfloat16).reshape(
            count, block, -1
        )

    def deliver_two(total):
        mlp_grad_sent(
            total, hidden, grads_own, gain_mlp_two, branch_own, grad_hidden, mlp_two_sum
        )

    fillers = wide_grads(rows_two, pre_grads, units, grads_vm, wide_two, down_two)
    fillers += [functools.partial(project_down, group) for group in range(4)]
    run_with(
        scatter_steps(
            count, partial_back, deliver_two, *r.scatter_refs, compute=all_but_last(through)
        ),
        [functools.partial(run_all, fillers[n::4]) for n in range(4)],
    )
    for _ in steps:
        pass
    save = pltpu.make_async_copy(partial, ahead, load_done.at[3])
    save.start()
    copies = carried(
        (wide_two, down_two, attn_two, out_two), carried_to, carry_sent, carry_got
    )

    def background():
        carry(copies[:2], 0, "start")
        wide_loads[0] = pltpu.make_async_copy(gate_up.at[0], wide_vm, load_done.at[0])
        wide_loads[1] = pltpu.make_async_copy(down.at[0], down_vm, load_done.at[1])
        wide_loads[2] = pltpu.make_async_copy(wide_rows, rows_two, load_done.at[2])
        start_all(wide_loads)

    attn_back_body(
        count,
        None,
        r,
        (branch_own, grad_hidden, between, None, None, log_total, None, None, None)
        + (cosine, sine, start, gain_attn_two),
        (grad_between, attn_two_sum, attn_two, out_two),
        background,
        [],
    )
    carry(copies[2:], 0, "start")
    steps = gather_steps(count, grad_between, grads_vm, *r.gather_sems)
    next(steps)
    wait_all(wide_loads)

    def again(group):
        span = group_span(group, count, block)
        pre = product(group_rows(rows_two, group, count), wide_vm[...])
        pre_vm[span] = pre
        units[span] = hidden_units(pre)

    def through_one(group):
        span = group_span(group, count, block)
        grad_act = back_product(group_rows(grads_vm, group, count), down_vm[...])
        store_gate_grads(pre_grads, span, grad_act, pre_vm[span])
        keep_group(partial_back, group, back_product(pre_grads[span], wide_vm[...]), count)

    for number, event in enumerate(until_done(steps)):
        if number < 2:
            again(2 * number)
            again(2 * number + 1)
        if event == "line":
            through_one(group_of(event))

    def deliver_one(total):
        mlp_grad_sent(
            total, hidden_one, grad_between, gain_mlp_one, branch_out, grad_hidden_out, mlp_one_sum
        )

    run_with(
        scatter_steps(
            count, partial_back, deliver_one, *r.scatter_refs, compute=all_but_last(through_one)
        ),
        wide_grads(rows_two, pre_grads, units, grads_vm, wide_one, down_one),
    )
    for _ in steps:
        pass
    carry(copies, 0, "wait")
    save.wait()


def last_kernel(count, *refs):
    refs = iter(refs)

    def take(n):
        return [next(refs) for _ in range(n)]

    ins = take(13)
    ins[2] = ins[2].at[lax.axis_index("section"), 0]
    wide_one, down_one, attn_two, out_two, wide_two, down_two = take(6)
    wide_from_one, down_from_one, attn_from_one, out_from_one, ahead = take(5)
    gain_mlp_one, gain_attn_two, gain_mlp_two, between, grad_between, hidden = take(6)
    attn, out, gate, up, down, gains_out, rows_out, grads_out = take(8)
    final, grad_start = take(2)
    attn_grad, out_grad, gain_attn_one, gains = take(4)
    attn_own, out_own, wide_own, down_own, attn_in, out_in, wide_in, down_in = take(8)
    attn_slot, wide_slot = take(2)
    gain_in, gain_sum, gain_line, gain_part, gain_side, gain_core = take(6)
    load_done, cross_sent, cross_got, line_sent, line_got = take(5)
    side_sent, side_got, core_sent, core_got, local_done, small_sent, small_got = take(7)
    ahead_refs = take(13)
    r = attn_back_refs(take)
    seq, b, section = lax.axis_index("seq"), lax.axis_index("blk"), lax.axis_index("section")
    at_first = section == 0
    at_second = jnp.logical_not(at_first)
    core, side, other = {"seq": seq ^ 1}, {"seq": seq ^ 2}, {"section": 1 - section}
    greet((other, core, side) + tuple({"blk": lax.rem(b + k, count)} for k in range(1, count)))
    rows, lanes = attn.shape[2], gate.shape[1] // (4 * count)
    turns = tuple(range(count // 2, 0, -1)) + tuple(range(count // 2 + 1, count)) + (0,)
    f32, low = jnp.float32, jnp.bfloat16

    def piece_rows(kind, j):
        if kind == 0:
            return (slice(None), pl.ds(pl.multiple_of(j * rows, rows), rows))
        return (pl.ds(pl.multiple_of(j * rows, rows), rows),)

    pairs = {
        0: (attn_own, attn_in, attn_grad),
        1: (wide_own, wide_in, wide_one),
        2: (out_own, out_in, out_grad),
        3: (down_own, down_in, down_one),
    }
    sources = {
        0: (attn_grad, attn_two, attn_from_one),
        1: (wide_one, wide_two, wide_from_one),
        2: (out_grad, out_two, out_from_one),
        3: (down_one, down_two, down_from_one),
    }

    def load(kind):
        one, two, from_one = sources[kind]
        own, held, _ = pairs[kind]

        @pl.when(at_first)
        def _():
            pltpu.make_async_copy(one, own, load_done.at[kind, 0]).start()

        @pl.when(at_second)
        def _():
            pltpu.make_async_copy(two, own, load_done.at[kind, 0]).start()
            pltpu.make_async_copy(from_one, held, load_done.at[kind, 1]).start()

    def loaded(kind):
        own, held, _ = pairs[kind]
        pltpu.make_async_copy(own, own, load_done.at[kind, 0]).wait()
        pl.when(at_second)(pltpu.make_async_copy(held, held, load_done.at[kind, 1]).wait)

    def cross(kind, k):
        _, held, begin = pairs[kind]
        index = piece_rows(kind, lax.rem(b + k, count)) if kind < 2 else (slice(None),)
        return remote(
            begin.at[index], held.at[index], cross_sent.at[kind, k], cross_got.at[kind, k], other
        )

    def add_up(kind, k):
        own, held, _ = pairs[kind]
        pl.when(at_first)(cross(kind, k).wait_recv)
        index = piece_rows(kind, lax.rem(b + k, count)) if kind < 2 else (slice(None),)
        held[index] = (own[index].astype(f32) + held[index].astype(f32)).astype(low)

    def along_line(kind, k):
        j = lax.rem(b + k, count)
        slot = (attn_slot if kind == 0 else wide_slot).at[k]
        source = pairs[kind][1].at[piece_rows(kind, j)]
        return remote(source, slot, line_sent.at[kind, k], line_got.at[kind, k], {"blk": j})

    def places(kind, k, of_seq):
        if kind == 2:
            size = out_in.shape[0]
            return [out.at[pl.ds(pl.multiple_of(of_seq * size, size), size)]]
        if kind == 3:
            size = down_in.shape[0]
            return [down.at[pl.ds(pl.multiple_of(of_seq * size, size), size)]]
        head = lax.rem(b + count - k, count) * 4 + of_seq
        if kind == 0:
            return [attn.at[head]]
        column = pl.ds(pl.multiple_of(head * lanes, lanes), lanes)
        return [gate.at[:, column], up.at[:, column]]

    def numbered(kind, k, of_seq):
        base = {0: k, 1: count + 2 * k, 2: 3 * count, 3: 3 * count + 1}[kind]
        return [(base + n, spot) for n, spot in enumerate(places(kind, k, of_seq))]

    def made(kind, k):
        if kind > 1:
            return [pairs[kind][1].at[:]]
        if kind == 0:
            return [attn_in.at[piece_rows(0, b)] if k == 0 else attn_slot.at[k]]
        whole = (lambda cut: wide_in.at[piece_rows(1, b) + (cut,)]) if k == 0 else (
            lambda cut: wide_slot.at[k, :, cut]
        )
        return [whole(pl.ds(0, lanes)), whole(pl.ds(lanes, lanes))]

    def sends(kind, k):
        found = []
        for (n, spot), begin in zip(numbered(kind, k, seq), made(kind, k)):
            found.append(
                (
                    remote(begin, spot, side_sent.at[n], side_got.at[n], side),
                    remote(begin, spot, core_sent.at[0, n], core_got.at[0, n], core),
                    pltpu.make_async_copy(begin, spot, local_done.at[n]),
                )
            )
        return found

    def publish(kind, k):
        for copies in sends(kind, k):
            for copy in copies:
                copy.start()

    def passes(kind, k):
        return [
            remote(spot, spot, core_sent.at[1, n], core_got.at[1, n], core)
            for n, spot in numbered(kind, k, seq ^ 2)
        ]

    def from_line(kind, k):
        along_line(kind, k).wait_recv()
        publish(kind, k)

    def from_side(kind, k):
        for n, spot in numbered(kind, k, seq ^ 2):
            settled(spot, side_got.at[n], True)
        for copy in passes(kind, k):
            copy.start()

    def small(n, source, slot, device):
        return remote(source, slot, small_sent.at[n], small_got.at[n], device)

    swap_rest = small(4 + count, between, rows_out.at[section], other)
    swap_final = small(4 + count, final, rows_out.at[section], other)
    swap_between = small(0, grad_between, grads_out.at[section], other)
    swap_start = small(0, grad_start, grads_out.at[section], other)
    pl.when(at_second)(swap_rest.start)
    pl.when(at_first)(swap_between.start)
    wide_turns = [(1, k) for k in turns]
    crossings = [(3, 0)] + wide_turns + [(0, k) for k in turns] + [(2, 0)]

    def begin_cross(those):
        for kind, k in those:
            pl.when(at_second)(cross(kind, k).start)

    def background():
        begin_cross(crossings[: count + 1])
        load(3)
        load(1)

    def deliver(total):
        final[...] = (hidden[...] + total).astype(low)
        pl.when(at_first)(swap_final.start)
        rows_out[section] = jnp.where(at_first, between[...], final[...])

    def later():
        load(0)
        load(2)
        begin_cross(crossings[count + 1 :])

    def share(n):
        if n == 0:
            loaded(1)
        add_up(1, turns[n])
        along_line(1, turns[n]).start()

    def gathered():
        loaded(3)
        add_up(3, 0)
        publish(3, 0)

    def spare():
        later()
        share(0)

    def early():
        add_up(1, 0)
        publish(1, 0)

    ahead_steps = line_first_steps(count, ahead, deliver, *ahead_refs)
    attn_back_body(
        count,
        0,
        r,
        ins,
        (grad_start, gain_attn_one, attn_grad, out_grad),
        background,
        [functools.partial(share, 1), functools.partial(share, 2), early],
        gathered,
        spare,
    )
    pl.when(at_second)(swap_start.start)
    grads_out[section] = jnp.where(at_first, grad_start[...], grad_between[...])
    gains[0, 0:4] = gain_attn_one[0:4]
    gains[0, 4:8] = gain_mlp_one[4:8]
    gains[1, 0:4] = gain_attn_two[0:4]
    gains[1, 4:8] = gain_mlp_two[4:8]
    gain_cross = small(1, gains.at[1 - section], gain_in.at[:], other)
    gain_cross.start()

    def gain_piece(j):
        return gain_sum.at[:, pl.ds(pl.multiple_of(j * rows, rows), rows)]

    def gain_send(k):
        j = lax.rem(b + k, count)
        return small(3 + k, gain_piece(j), gain_line.at[k], {"blk": j})

    loaded(0)
    for k in turns[:-1]:
        add_up(0, k)
        along_line(0, k).start()
    from_line(1, turns[0])
    add_up(0, 0)
    publish(0, 0)
    from_line(1, turns[1])
    from_side(1, 0)
    loaded(2)
    add_up(2, 0)
    publish(2, 0)
    from_line(1, turns[2])
    next(ahead_steps)
    from_side(3, 0)
    from_side(1, turns[0])
    for k in turns[:-1]:
        from_line(0, k)
    from_side(0, 0)
    from_side(1, turns[1])
    gain_cross.wait_recv()
    gain_sum[...] = gains[section] + gain_in[...]
    for k in range(1, count):
        gain_send(k).start()
    advance(ahead_steps, 2)
    from_side(2, 0)
    from_side(1, turns[2])
    for k in range(1, count):
        gain_send(k).wait_recv()
    gain_part[...] = gain_sum[:, pl.ds(pl.multiple_of(b * rows, rows), rows)]
    for k in range(1, count):
        gain_part[...] += gain_line[k]
    gain_to_side = small(2, gain_part.at[:], gain_side.at[:], side)
    gain_to_side.start()
    advance(ahead_steps, 4)
    gain_to_side.wait_recv()
    gain_side[...] += gain_part[...]
    gain_to_core = small(3, gain_side.at[:], gain_core.at[:], core)
    gain_to_core.start()
    for _ in ahead_steps:
        pass
    for k in turns[:-1]:
        from_side(0, k)
    gain_to_core.wait_recv()
    gains_out[...] = gain_side[...] + gain_core[...]
    every = [(0, k) for k in range(count)] + [(1, k) for k in range(count)] + [(2, 0), (3, 0)]
    for kind, k in every:
        pl.when(at_second)(cross(kind, k).wait_send)
        if kind < 2 and k:
            along_line(kind, k).wait_send()
        for to_side, to_core, local in sends(kind, k):
            to_side.wait_send()
            to_core.wait_send()
            local.wait()
        for copy in passes(kind, k):
            copy.wait_send()
        for half, of_seq in ((0, seq ^ 1), (1, seq ^ 3)):
            for n, spot in numbered(kind, k, of_seq):
                settled(spot, core_got.at[half, n], True)
    swap_between.wait()
    swap_rest.wait()
    gain_cross.wait_send()
    for k in range(1, count):
        gain_send(k).wait_send()
    gain_to_side.wait_send()
    gain_to_core.wait_send()


def widen_kernel(pieces, *refs):
    attn, out, gate, up, down, rows_in, grads_in, gains = refs[:8]
    query, key, value, out_f, gate_f, up_f, down_f = refs[8:15]
    rows_out, grads_out, gain_attn, gain_mlp = refs[15:]
    f32 = jnp.float32
    out_f[...] = out[...].astype(f32)
    gate_f[...] = gate[...].astype(f32)
    up_f[...] = up[...].astype(f32)
    down_f[...] = down[...].astype(f32)

    @pl.when(pl.program_id(0) == 0)
    def _():
        rows_out[...] = rows_in[...]
        grads_out[...] = grads_in[...]
        gain_attn[...] = gains[0:1]
        gain_mlp[...] = gains[4:5]

    @pl.when(pl.program_id(0) < pieces)
    def _():
        parts, _, lanes = attn.shape
        copies = HEADS // KV_HEADS

        def heads(n):
            return attn[:, n * HEAD_DIM : (n + 1) * HEAD_DIM].astype(f32)

        query[...] = heads(0).reshape(parts * HEAD_DIM, lanes).T
        for n, place in ((1, key), (2, value)):
            total = heads(n).reshape(parts // copies, copies, HEAD_DIM, lanes).sum(1)
            place[...] = total.reshape(parts // copies * HEAD_DIM, lanes).T


def widen(attn, out, gate, up, down, rows_out, grads_out, gains):
    f32 = jnp.float32
    parts, heads, rows = attn.shape
    lanes = 128
    pieces = rows // lanes
    steps = 8
    width = parts * HEAD_DIM
    narrow = width * KV_HEADS // HEADS

    def rows_of(array):
        return pl.BlockSpec((array.shape[0] // steps, array.shape[1]), lambda i: (i, 0))

    def turned(columns):
        return pl.BlockSpec((lanes, columns), lambda i: (jnp.minimum(i, pieces - 1), 0))

    def whole(shape):
        return pl.BlockSpec(shape, lambda i: (0,) * len(shape))

    flat = [out, gate, up, down]
    swaps = [whole(rows_out.shape), whole(grads_out.shape)]
    gain = jax.ShapeDtypeStruct((1, rows), f32)
    taken = pl.BlockSpec((parts, heads, lanes), lambda i: (0, 0, jnp.minimum(i, pieces - 1)))
    shapes = [(rows, width), (rows, narrow), (rows, narrow)] + [array.shape for array in flat]
    return pl.pallas_call(
        functools.partial(widen_kernel, pieces),
        grid=(steps,),
        out_shape=[jax.ShapeDtypeStruct(shape, f32) for shape in shapes]
        + [jax.ShapeDtypeStruct(array.shape, array.dtype) for array in (rows_out, grads_out)]
        + [gain, gain],
        in_specs=[taken] + [rows_of(array) for array in flat] + swaps + [whole(gains.shape)],
        out_specs=[turned(width), turned(narrow), turned(narrow)]
        + [rows_of(array) for array in flat]
        + swaps
        + [whole((1, rows)), whole((1, rows))],
        compiler_params=pltpu.CompilerParams(vmem_limit_bytes=60 * 2**20),
        name="widen_gradients",
    )(attn, out, gate, up, down, rows_out, grads_out, gains)


def last_layer(count, operands, like, back_scratch):
    attn, out, wide, down, block, width, gain_rows = like
    low, f32 = jnp.bfloat16, jnp.float32
    seq_count = lax.axis_size("seq")
    rows = wide[0] // count
    lanes = wide[1] // 2
    parts = seq_count * count
    dma = pltpu.SemaphoreType.DMA
    vmem = pltpu.VMEM
    sends = 3 * count + 2
    heads = attn[0]
    small = (gain_rows, rows)

    def slots(*places):
        return vmem(places + (block, width), low)

    outputs = [
        ((parts, heads, rows), low, False),
        ((out[0] * seq_count, out[1]), low, False),
        ((rows, lanes * parts), low, False),
        ((rows, lanes * parts), low, False),
        ((down[0] * seq_count, down[1]), low, False),
        (small, f32, True),
        ((2, block, width), low, True),
        ((2, block, width), low, True),
    ]
    scratch = (
        [vmem((block, width), low), vmem((block, width), low)]
        + [vmem(attn, low), vmem(out, low), vmem((gain_rows, width), f32)]
        + [vmem((2, gain_rows, width), f32)]
        + [vmem(shape, low) for shape in (attn, out, wide, down)] * 2
        + [vmem((count, heads, rows), low), vmem((count, rows, 2 * lanes), low)]
        + [vmem((gain_rows, width), f32)] * 2
        + [vmem((count,) + small, f32)]
        + [vmem(small, f32)] * 3
        + [dma((4, 2)), dma((4, count)), dma((4, count)), dma((2, count)), dma((2, count))]
        + [dma((sends,)), dma((sends,)), dma((2, sends)), dma((2, sends)), dma((sends,))]
        + [dma((5 + count,)), dma((5 + count,))]
        + [slots(2, count), slots(2, count), slots(2, 2, count), slots(2, count), slots(1)]
        + [vmem((block, width), f32)]
        + [dma((2, count)), dma((2, count)), dma((2, count)), dma((2, count))]
        + [dma((2, 2, count)), dma, dma]
        + back_scratch
    )
    attn, out, gate, up, down, gains, rows_out, grads_out = call_kernel(
        functools.partial(last_kernel, count), "last_layer_back", 3, operands, outputs, scratch
    )
    return widen(attn, out, gate, up, down, rows_out, grads_out, gains)


def call_kernel(kernel, name, number, operands, outputs, scratch):
    in_vmem = pl.BlockSpec(memory_space=pltpu.VMEM)
    anywhere = pl.BlockSpec(memory_space=pl.ANY)
    places = {True: in_vmem, False: anywhere, None: pl.BlockSpec(memory_space=pltpu.SMEM)}
    return pl.pallas_call(
        kernel,
        out_shape=[jax.ShapeDtypeStruct(shape, dtype) for shape, dtype, _ in outputs],
        in_specs=[places[near] for _, near in operands],
        out_specs=[in_vmem if near else anywhere for _, _, near in outputs],
        scratch_shapes=scratch,
        compiler_params=pltpu.CompilerParams(
            collective_id=number, has_side_effects=True, vmem_limit_bytes=56 * 2**20
        ),
        name=name,
    )(*[array for array, _ in operands])


def head_shards(inputs, cotangent, doc_lengths, *params):
    seq_count, count = lax.axis_size("seq"), lax.axis_size("blk")
    low, f32 = jnp.bfloat16, jnp.float32
    vmem, dma = pltpu.VMEM, pltpu.SemaphoreType.DMA
    block, width = inputs.shape[2], inputs.shape[3]
    blocks = seq_count * count
    tokens = blocks * block
    local = tuple(weight[0] for weight in params)
    piece_shape = (count, 2 * HEAD_DIM + 16, local[1].shape[0])
    w_output, w_gate, w_up, w_down = local[4], local[6], local[7], local[8]
    rows = w_gate.shape[0]
    lanes = w_gate.shape[1] // blocks
    out_rows, down_rows = w_output.shape[0] // seq_count, w_down.shape[0] // seq_count
    lane = jnp.arange(PAD) % (HEAD_DIM // 2)
    frequency = (THETA ** (-2.0 * lane.astype(f32) / HEAD_DIM))[None]

    def all_blocks():
        return vmem((blocks, block, width), low)

    def scatter():
        return scatter_scratch(count, block, width)

    half_blocks = vmem((blocks // 2, block, width), low)
    half = ((blocks // 2, block, width), low, False)
    own_low, own_wide = ((block, width), low, True), ((block, width), f32, True)
    every = ((blocks, block, width), low, False)
    gain_rows = ((8, width), f32, True)
    weights_vm = [vmem((3 * PAD + 16, width), low), vmem((PAD, width), low)]
    wide_vm, down_vm = vmem((width, 2 * lanes), low), vmem((down_rows, width), low)
    (
        attn,
        twin,
        gate_up,
        out,
        down,
        rows_one,
        wide_rows_one,
        grads_near,
        grads_side,
        cosine,
        sine,
        start,
        hidden_one,
        between,
        normed,
        heads_one,
        total_one,
    ) = call_kernel(
        functools.partial(first_layer_kernel, count),
        "first_layer",
        2,
        [(array, False) for array in local[1:4] + (w_gate, w_up, w_output, w_down)]
        + [(local[0][None], True), (local[5][None], True)]
        + [(inputs, True), (cotangent, True), (doc_lengths, None), (frequency, True)],
        [
            ((2, piece_shape[1], width), low, False),
            ((2, HEAD_DIM, width), low, False),
            ((2, width, 2 * lanes), low, False),
            ((2, out_rows, width), low, False),
            ((2, down_rows, width), low, False),
            every,
            every,
            half,
            ((block, width), low, False),
            ((tokens, PAD), f32, True),
            ((tokens, PAD), f32, True),
            ((tokens, 1), jnp.int32, True),
            own_wide,
            own_low,
            own_low,
            ((4, tokens, PAD), low, True),
            ((tokens, 1), f32, True),
        ],
        [all_blocks() for _ in range(5)]
        + [half_blocks]
        + weights_vm
        + [wide_vm, down_vm, vmem((tokens, lanes), low), vmem((block, width), low)]
        + [vmem((16, width), low), vmem(piece_shape, low)]
        + [vmem(local[1].shape, low), vmem(local[2].shape, low)]
        + [vmem(local[1].shape[::-1], low), vmem(local[2].shape[::-1], low), dma((2,))]
        + [dma((6,)), dma((3,)), dma, dma]
        + [dma((3, count)), dma((3, count)), dma((5, count)), dma((5, count)), dma((5,))]
        + gather_semaphores(count) * 2
        + line_semaphores(count)
        + [dma, dma]
        + scatter()
        + scatter(),
    )
    tables = [(cosine, True), (sine, True), (start, True)]
    gains = attn[:, GAINS : GAINS + 2].astype(f32)
    back_scratch = (
        [all_blocks(), all_blocks(), vmem((4, tokens, PAD), low)]
        + weights_vm
        + [vmem((tokens, PAD), low), vmem((tokens, tokens), f32)]
        + [vmem((tokens, PAD), f32), vmem((tokens, PAD), f32), vmem((tokens, 3 * PAD), low)]
        + [all_blocks(), dma((7,))]
        + gather_semaphores(count)
        + scatter()
    )
    attn_shape, out_shape = (3 * HEAD_DIM, width), (HEAD_DIM, width)
    wide_shape, down_shape = (width, 2 * lanes), (down_rows, width)
    (
        hidden_two,
        ahead,
        grad_between,
        branch,
        grad_hidden,
        gain_mlp_two,
        gain_attn_two,
        gain_mlp_one,
        wide_two,
        down_two,
        attn_two,
        out_two,
        wide_one,
        down_one,
        wide_from_one,
        down_from_one,
        attn_from_one,
        out_from_one,
    ) = call_kernel(
        functools.partial(middle_kernel, count),
        "second_layer",
        4,
        [(normed, True), (between, True), (grads_side, True)]
        + tables
        + [(attn, False), (twin, False), (out, False)]
        + [(grads_near, False), (gate_up, False), (down, False)]
        + [(cotangent, True), (hidden_one, True), (wide_rows_one, False)]
        + [(gains[1, 1:2], True), (gains[1, 0:1], True), (gains[0, 1:2], True)],
        [own_wide, every, own_low, own_low, own_wide, gain_rows, gain_rows, gain_rows]
        + [(wide_shape, low, True), (down_shape, low, True)]
        + [(attn_shape, low, True), (out_shape, low, True)]
        + [(wide_shape, low, True), (down_shape, low, True)]
        + [(shape, low, False) for shape in (wide_shape, down_shape, attn_shape, out_shape)],
        [all_blocks(), all_blocks(), all_blocks(), wide_vm, down_vm]
        + [vmem((tokens, 1), f32), vmem((tokens, lanes), low), vmem((tokens, 2 * lanes), f32)]
        + [vmem((tokens, 2 * lanes), low), vmem((block, width), low), vmem((block, width), low)]
        + [vmem((block, width), f32), dma((4,)), dma((4,)), dma((4,))]
        + line_semaphores(count)
        + back_scratch,
    )
    back_operands = (
        [(branch, True), (grad_hidden, True), (inputs, True)]
        + [(rows_one, False), (heads_one, False), (total_one, True)]
        + [(attn, False), (twin, False), (out, False)]
        + tables
        + [(gains[0, 0:1], True)]
    )
    query, key, value, out, gate, up, down, *swapped, gain_attn, gain_mlp = last_layer(
        count,
        back_operands
        + [(wide_one, False), (down_one, False), (attn_two, False), (out_two, False)]
        + [(wide_two, False), (down_two, False), (wide_from_one, False), (down_from_one, False)]
        + [(attn_from_one, False), (out_from_one, False), (ahead, False)]
        + [(gain_mlp_one, True), (gain_attn_two, True), (gain_mlp_two, True)]
        + [(between, True), (grad_between, True), (hidden_two, True)],
        (
            attn_shape,
            out_shape,
            wide_shape,
            down_shape,
            block,
            width,
            gain_rows[0][0],
        ),
        back_scratch,
    )
    return (
        swapped[0][None, :, None],
        swapped[1][None, :, None],
        gain_attn,
        query[None],
        key[None],
        value[None],
        out[None],
        gain_mlp,
        gate[None],
        up[None],
        down[None],
    )

def solution(mesh):
    placed = (
        P(None, None, ("seq", "blk"), None),
        P(None, None, ("seq", "blk"), None),
        P(),
        P("section", "blk"),
        P("section", "blk", None),
        P("section", "blk", None),
        P("section", "blk", None),
        P("section", "blk", None),
        P("section", "blk"),
        P("section", "blk", None),
        P("section", "blk", None),
        P("section", "blk", None),
    )
    one_head_each = mesh.shape["seq"] == 4 and mesh.shape["blk"] == HEADS // 4
    return jax.shard_map(
        head_shards if one_head_each else shards,
        mesh=mesh,
        in_specs=placed,
        out_specs=(
            P("section", None, None, ("seq", "blk"), None),
            P("section", None, None, ("seq", "blk"), None),
            P("section", "blk"),
            P("section", "blk", None),
            P("section", "blk", None),
            P("section", "blk", None),
            P("section", "blk", None),
            P("section", "blk"),
            P("section", "blk", None),
            P("section", "blk", None),
            P("section", "blk", None),
        ),
        check_vma=False,
    )
```

```python
import functools

import jax
import jax.numpy as jnp
from jax import lax
from jax.experimental import pallas as pl
from jax.experimental.pallas import tpu as pltpu
from jax.sharding import PartitionSpec as P

HEADS = 16
KV_HEADS = 8
HEAD_DIM = 96


EPS = 1e-05
THETA = 100000.0
MASKED = -1e30


def passed_along(value, axis, steps):
    count = lax.axis_size(axis)
    first, last = (max(0, -steps), min(count, count - steps))
    return lax.ppermute(value, axis, [(source, source + steps) for source in range(first, last)])


def shortened(value):
    return jax.tree.map(lambda a: a.astype(jnp.bfloat16) if a.dtype == jnp.float32 else a, value)


def product(left_side, right_side):
    return jnp.dot(left_side, right_side, preferred_element_type=jnp.float32)


def back_product(left_side, right_side):
    return lax.dot_general(
        left_side, right_side, (((1,), (1,)), ((), ())), preferred_element_type=jnp.float32
    )


def doc_info(lengths, token_index):
    doc_ends = jnp.cumsum(lengths, axis=-1)
    passed = (doc_ends[..., None, :] <= token_index[..., None]).astype(jnp.int32)
    segment = jnp.sum(passed, axis=-1)
    offset = jnp.sum(passed * lengths[..., None, :], axis=-1)
    return (segment, token_index - offset)


def rotate(field_in, position, turn_sign):
    half_dim = field_in.shape[-1] // 2
    frequency = THETA ** (-2.0 * jnp.arange(half_dim, dtype=jnp.float32) / field_in.shape[-1])
    angles = position.astype(jnp.float32)[:, None] * frequency
    cosine = jnp.cos(angles)[:, None, :]
    sine_part = turn_sign * jnp.sin(angles)[:, None, :]
    first_half = field_in[..., :half_dim]
    second_half = field_in[..., half_dim:]
    return jnp.concatenate(
        [
            first_half * cosine - second_half * sine_part,
            second_half * cosine + first_half * sine_part,
        ],
        axis=-1,
    )


def rms_forward(field_in, gain_row):
    inv_root = lax.rsqrt(jnp.mean(field_in * field_in, axis=-1, keepdims=True) + EPS)
    return (field_in * inv_root * gain_row, inv_root)


def rms_backward(field_in, gain_row, inv_root, grad_normed):
    scaled = gain_row * grad_normed
    grad_field = inv_root * scaled - field_in * inv_root**3 * jnp.mean(
        scaled * field_in, axis=-1, keepdims=True
    )
    return (grad_field, grad_normed * field_in * inv_root)


def token_place(block_id, row_ids, per_device, blk_count):
    return (row_ids // per_device * blk_count + block_id) * per_device + row_ids % per_device


def masks_for(lengths, blk_index, per_device, blk_count, seq_count):
    block_tokens = seq_count * per_device
    row_ids = jnp.arange(block_tokens, dtype=jnp.int32)
    query_index = token_place(blk_index, row_ids, per_device, blk_count)
    all_ids = jnp.arange(blk_count * block_tokens, dtype=jnp.int32)
    key_index = token_place(all_ids // block_tokens, all_ids % block_tokens, per_device, blk_count)
    query_seg, _ = doc_info(lengths, query_index)
    key_seg, _ = doc_info(lengths, key_index)
    return (query_index, key_index, query_seg, key_seg)


def head_scores(queries, key_rows, allowed, kv_local):
    grouped = queries.reshape(queries.shape[0], kv_local, -1, HEAD_DIM)
    key_heads = key_rows.reshape(key_rows.shape[0], kv_local, HEAD_DIM)
    scores = jnp.einsum(
        "rkgd,lkd->kgrl", grouped, key_heads, preferred_element_type=jnp.float32
    ) * HEAD_DIM ** (-0.5)
    return (jnp.where(allowed, scores, MASKED), grouped, key_heads)


def attend_forward(operands, query_index, key_index, kv_local):
    queries, key_rows, value_rows, query_seg, key_seg = operands
    allowed = (query_seg[:, None] == key_seg[None, :]) & (
        key_index[None, :] <= query_index[:, None]
    )
    scores, grouped, key_heads = head_scores(queries, key_rows, allowed, kv_local)
    row_top = jnp.max(scores, axis=-1, keepdims=True)
    log_total = row_top + jnp.log(jnp.sum(jnp.exp(scores - row_top), axis=-1, keepdims=True))
    weights_low = jnp.exp(scores - log_total).astype(jnp.bfloat16)
    value_heads = value_rows.reshape(value_rows.shape[0], kv_local, HEAD_DIM)
    mixed_heads = jnp.einsum(
        "kgrl,lkd->rkgd", weights_low, value_heads, preferred_element_type=jnp.float32
    )
    return (mixed_heads.reshape(queries.shape).astype(jnp.bfloat16), log_total)


def attend_backward(operands, query_index, key_index, kv_local):
    queries, key_rows, value_rows, grad_mixed, log_total, query_seg, key_seg = operands
    allowed = (query_seg[:, None] == key_seg[None, :]) & (
        key_index[None, :] <= query_index[:, None]
    )
    scores, grouped, key_heads = head_scores(queries, key_rows, allowed, kv_local)
    attn_probs = jnp.exp(scores - log_total)
    value_heads = value_rows.reshape(value_rows.shape[0], kv_local, HEAD_DIM)
    grad_heads = grad_mixed.reshape(grouped.shape)
    grad_values = jnp.einsum(
        "kgrl,rkgd->lkd",
        attn_probs.astype(jnp.bfloat16),
        grad_heads,
        preferred_element_type=jnp.float32,
    )
    grad_probs = jnp.einsum(
        "rkgd,lkd->kgrl", grad_heads, value_heads, preferred_element_type=jnp.float32
    )
    centre = jnp.sum(attn_probs * grad_probs, axis=-1, keepdims=True)
    grad_scores = (attn_probs * (grad_probs - centre)).astype(jnp.bfloat16)
    grad_queries = jnp.einsum(
        "kgrl,lkd->rkgd", grad_scores, key_heads, preferred_element_type=jnp.float32
    ) * HEAD_DIM ** (-0.5)
    grad_keys = jnp.einsum(
        "kgrl,rkgd->lkd", grad_scores, grouped, preferred_element_type=jnp.float32
    ) * HEAD_DIM ** (-0.5)
    return (
        grad_queries.reshape(queries.shape).astype(jnp.bfloat16),
        grad_keys.reshape(key_rows.shape),
        grad_values.reshape(value_rows.shape),
    )


def layer_forward(section_in, lengths, weights, placing):
    shard_id, blk_index, seq_count, blk_count = placing
    gain_attn, w_query, w_key, w_value, w_output, gain_mlp, w_gate, w_up, w_down = weights
    seqs_here, per_device, width = section_in.shape
    token_rows = seqs_here * per_device
    copies = max(1, seq_count // KV_HEADS)
    kv_local = KV_HEADS * copies // seq_count
    token_index = shard_id * per_device + jnp.arange(per_device, dtype=jnp.int32)
    _, position = doc_info(lengths, token_index)
    position = position.reshape(token_rows)
    flat_in = section_in.reshape(token_rows, width)
    normed, inv_first = rms_forward(flat_in, gain_attn.astype(jnp.float32))
    normed_low = normed.astype(jnp.bfloat16)
    query_pre = product(normed_low, w_query).reshape(token_rows, HEADS, HEAD_DIM)
    key_pre = product(normed_low, w_key).reshape(token_rows, KV_HEADS, HEAD_DIM)
    value_pre = product(normed_low, w_value).reshape(token_rows, KV_HEADS, HEAD_DIM)
    query_rot = (
        rotate(query_pre, position, 1.0).astype(jnp.bfloat16).reshape(seqs_here, per_device, width)
    )
    key_rot = rotate(key_pre, position, 1.0).astype(jnp.bfloat16)
    spread_shape = (token_rows, KV_HEADS, copies, HEAD_DIM)
    key_rep = jnp.broadcast_to(key_rot[:, :, None, :], spread_shape).reshape(
        seqs_here, per_device, -1
    )
    value_rep = jnp.broadcast_to(
        value_pre.astype(jnp.bfloat16)[:, :, None, :], spread_shape
    ).reshape(seqs_here, per_device, -1)
    heads_query, heads_key, heads_value = (
        lax.all_to_all(query_rot, "seq", split_axis=2, concat_axis=1, tiled=True),
        lax.all_to_all(key_rep, "seq", split_axis=2, concat_axis=1, tiled=True),
        lax.all_to_all(value_rep, "seq", split_axis=2, concat_axis=1, tiled=True),
    )
    keys_all, values_all = (
        lax.all_gather(heads_key, "blk", axis=1, tiled=True),
        lax.all_gather(heads_value, "blk", axis=1, tiled=True),
    )
    query_index, key_index, query_seg, key_seg = masks_for(
        lengths, blk_index, per_device, blk_count, seq_count
    )
    heads_mixed, log_total = lax.map(
        lambda operands: attend_forward(operands, query_index, key_index, kv_local),
        (heads_query, keys_all, values_all, query_seg, key_seg),
    )
    token_mixed = lax.all_to_all(
        heads_mixed, "seq", split_axis=1, concat_axis=2, tiled=True
    ).reshape(token_rows, width)
    hidden = flat_in + product(token_mixed, w_output)
    normed_mlp, inv_second = rms_forward(hidden, gain_mlp.astype(jnp.float32))
    normed_mlp_low = normed_mlp.astype(jnp.bfloat16)
    gate_pre = product(normed_mlp_low, w_gate)
    up_pre = product(normed_mlp_low, w_up)
    act_low = (jax.nn.silu(gate_pre) * up_pre).astype(jnp.bfloat16)
    result = hidden + product(act_low, w_down)
    saved_state = (
        flat_in,
        normed_low,
        inv_first,
        position,
        heads_query,
        keys_all,
        values_all,
        log_total,
        token_mixed,
        hidden,
        inv_second,
        normed_mlp_low,
        gate_pre,
        up_pre,
        act_low,
        lengths,
    )
    return (result.reshape(section_in.shape), saved_state)


def layer_backward(upstream, saved_state, weights, placing):
    shard_id, blk_index, seq_count, blk_count = placing
    gain_attn, w_query, w_key, w_value, w_output, gain_mlp, w_gate, w_up, w_down = weights
    (
        flat_in,
        normed_low,
        inv_first,
        position,
        heads_query,
        keys_all,
        values_all,
        log_total,
        token_mixed,
        hidden,
        inv_second,
        normed_mlp_low,
        gate_pre,
        up_pre,
        act_low,
        lengths,
    ) = saved_state
    seqs_here, per_device, width = upstream.shape
    token_rows = seqs_here * per_device
    copies = max(1, seq_count // KV_HEADS)
    kv_local = KV_HEADS * copies // seq_count
    grad_rows = upstream.reshape(token_rows, width)
    grad_out_low = grad_rows.astype(jnp.bfloat16)
    grad_act = back_product(grad_out_low, w_down)
    gate_sigmoid = jax.nn.sigmoid(gate_pre)
    grad_gate_low = (
        grad_act * up_pre * gate_sigmoid * (1.0 + gate_pre * (1.0 - gate_sigmoid))
    ).astype(jnp.bfloat16)
    grad_up_low = (grad_act * jax.nn.silu(gate_pre)).astype(jnp.bfloat16)
    grad_normed_mlp = back_product(grad_gate_low, w_gate) + back_product(grad_up_low, w_up)
    grad_hidden_part, gain_mlp_terms = rms_backward(
        hidden, gain_mlp.astype(jnp.float32), inv_second, grad_normed_mlp
    )
    grad_hidden = grad_rows + grad_hidden_part
    grad_branch_low = grad_hidden.astype(jnp.bfloat16)
    grad_mixed_low = (
        back_product(grad_branch_low, w_output)
        .astype(jnp.bfloat16)
        .reshape(seqs_here, per_device, width)
    )
    heads_grad = lax.all_to_all(grad_mixed_low, "seq", split_axis=2, concat_axis=1, tiled=True)
    query_index, key_index, query_seg, key_seg = masks_for(
        lengths, blk_index, per_device, blk_count, seq_count
    )
    grad_heads_query, grad_keys_all, grad_values_all = lax.map(
        lambda operands: attend_backward(operands, query_index, key_index, kv_local),
        (heads_query, keys_all, values_all, heads_grad, log_total, query_seg, key_seg),
    )
    grad_key_own, grad_value_own = (
        lax.psum_scatter(
            grad_keys_all.astype(jnp.bfloat16), "blk", scatter_dimension=1, tiled=True
        ).astype(jnp.float32),
        lax.psum_scatter(
            grad_values_all.astype(jnp.bfloat16), "blk", scatter_dimension=1, tiled=True
        ).astype(jnp.float32),
    )
    token_query, token_key, token_value = (
        lax.all_to_all(grad_heads_query, "seq", split_axis=1, concat_axis=2, tiled=True),
        lax.all_to_all(
            grad_key_own.astype(jnp.bfloat16), "seq", split_axis=1, concat_axis=2, tiled=True
        ),
        lax.all_to_all(
            grad_value_own.astype(jnp.bfloat16), "seq", split_axis=1, concat_axis=2, tiled=True
        ),
    )
    grad_key_sum = jnp.sum(
        token_key.astype(jnp.float32).reshape(token_rows, KV_HEADS, copies, HEAD_DIM), axis=2
    )
    grad_value_sum = jnp.sum(
        token_value.astype(jnp.float32).reshape(token_rows, KV_HEADS, copies, HEAD_DIM), axis=2
    )
    grad_query_low = (
        rotate(token_query.astype(jnp.float32).reshape(token_rows, HEADS, HEAD_DIM), position, -1.0)
        .astype(jnp.bfloat16)
        .reshape(token_rows, width)
    )
    grad_key_low = (
        rotate(grad_key_sum, position, -1.0)
        .astype(jnp.bfloat16)
        .reshape(token_rows, KV_HEADS * HEAD_DIM)
    )
    grad_value_low = grad_value_sum.astype(jnp.bfloat16).reshape(token_rows, KV_HEADS * HEAD_DIM)
    grad_normed = (
        back_product(grad_query_low, w_query)
        + back_product(grad_key_low, w_key)
        + back_product(grad_value_low, w_value)
    )
    grad_in_part, gain_attn_terms = rms_backward(
        flat_in, gain_attn.astype(jnp.float32), inv_first, grad_normed
    )
    grad_input = (grad_hidden + grad_in_part).reshape(upstream.shape)
    weight_rows = (
        gain_attn_terms,
        normed_low,
        grad_query_low,
        grad_key_low,
        grad_value_low,
        token_mixed,
        grad_branch_low,
        gain_mlp_terms,
        normed_mlp_low,
        grad_gate_low,
        grad_up_low,
        act_low,
        grad_out_low,
    )
    return (grad_input, weight_rows)


def weight_term(inputs_low, outputs_low):
    if outputs_low is None:
        return jnp.sum(inputs_low, axis=0)
    return lax.dot_general(
        inputs_low, outputs_low, (((0,), (0,)), ((), ())), preferred_element_type=jnp.float32
    )


def shards(
    inputs,
    cotangent,
    doc_lengths,
    attention_gain,
    w_query,
    w_key,
    w_value,
    w_output,
    mlp_gain,
    w_gate,
    w_up,
    w_down,
):
    at_first = lax.axis_index("section") == 0
    seq_count = lax.axis_size("seq")
    blk_count = lax.axis_size("blk")
    blk_index = lax.axis_index("blk")
    shard_id = lax.axis_index("seq") * blk_count + blk_index
    placing = (shard_id, blk_index, seq_count, blk_count)
    micro_count = inputs.shape[0]
    local_shards = (
        attention_gain[0],
        w_query[0],
        w_key[0],
        w_value[0],
        w_output[0],
        mlp_gain[0],
        w_gate[0],
        w_up[0],
        w_down[0],
    )
    weights = (
        lax.all_gather(local_shards[0], "blk", axis=0, tiled=True),
        lax.all_gather(local_shards[1], "blk", axis=0, tiled=True),
        lax.all_gather(local_shards[2], "blk", axis=0, tiled=True),
        lax.all_gather(local_shards[3], "blk", axis=0, tiled=True),
        lax.all_gather(local_shards[4], "blk", axis=0, tiled=True),
        lax.all_gather(local_shards[5], "blk", axis=0, tiled=True),
        lax.all_gather(local_shards[6], "blk", axis=0, tiled=True),
        lax.all_gather(local_shards[7], "blk", axis=0, tiled=True),
        lax.all_gather(local_shards[8], "blk", axis=0, tiled=True),
    )
    received = jnp.zeros(inputs.shape[1:], jnp.bfloat16)
    saved_states = []
    section_outs = []
    for tick_index in range(micro_count + 1):
        fresh_input = inputs[min(tick_index, micro_count - 1)]
        section_in = jnp.where(at_first, fresh_input, received).astype(jnp.float32)
        lengths = jnp.where(
            at_first,
            doc_lengths[min(tick_index, micro_count - 1)],
            doc_lengths[max(tick_index - 1, 0)],
        )
        result, saved_state = layer_forward(section_in, lengths, weights, placing)
        result_low = result.astype(jnp.bfloat16)
        if tick_index < micro_count:
            received = passed_along(result_low, "section", 1)
        saved_states.append(saved_state)
        section_outs.append(result_low)
    weights = (
        lax.all_gather(local_shards[0], "blk", axis=0, tiled=True),
        lax.all_gather(local_shards[1], "blk", axis=0, tiled=True),
        lax.all_gather(local_shards[2], "blk", axis=0, tiled=True),
        lax.all_gather(local_shards[3], "blk", axis=0, tiled=True),
        lax.all_gather(local_shards[4], "blk", axis=0, tiled=True),
        lax.all_gather(local_shards[5], "blk", axis=0, tiled=True),
        lax.all_gather(local_shards[6], "blk", axis=0, tiled=True),
        lax.all_gather(local_shards[7], "blk", axis=0, tiled=True),
        lax.all_gather(local_shards[8], "blk", axis=0, tiled=True),
    )
    back_in = jnp.zeros(cotangent.shape[1:], jnp.bfloat16)
    grad_outs = []
    row_sets = []
    for tick_index in range(micro_count + 1):
        saved_state = jax.tree.map(
            lambda first_pick, second_pick: jnp.where(at_first, first_pick, second_pick),
            saved_states[max(tick_index - 1, 0)],
            saved_states[min(tick_index + 1, micro_count)],
        )
        upstream = jnp.where(at_first, back_in, cotangent[min(tick_index, micro_count - 1)]).astype(
            jnp.float32
        )
        grad_input, weight_rows = layer_backward(upstream, saved_state, weights, placing)
        grad_low = grad_input.astype(jnp.bfloat16)
        if tick_index < micro_count:
            back_in = passed_along(grad_low, "section", -1)
        grad_outs.append(grad_low)
        row_sets.append(weight_rows)
    activations = jnp.stack(
        [
            jnp.where(at_first, section_outs[index_m], section_outs[index_m + 1])
            for index_m in range(micro_count)
        ]
    )[None]
    input_grads = jnp.stack(
        [
            jnp.where(at_first, grad_outs[index_m + 1], grad_outs[index_m])
            for index_m in range(micro_count)
        ]
    )[None]
    picked = [
        jax.tree.map(
            lambda first_pick, second_pick: jnp.where(at_first, first_pick, second_pick),
            row_sets[index_m + 1],
            row_sets[index_m],
        )
        for index_m in range(micro_count)
    ]
    merged = jax.tree.map(lambda *pieces: jnp.concatenate(pieces, axis=0), *picked)
    (
        gain_attn_terms,
        normed_low,
        grad_query_low,
        grad_key_low,
        grad_value_low,
        token_mixed,
        grad_branch_low,
        gain_mlp_terms,
        normed_mlp_low,
        grad_gate_low,
        grad_up_low,
        act_low,
        grad_out_low,
    ) = merged
    grad_pairs = (
        (gain_attn_terms, None),
        (normed_low, grad_query_low),
        (normed_low, grad_key_low),
        (normed_low, grad_value_low),
        (token_mixed, grad_branch_low),
        (gain_mlp_terms, None),
        (normed_mlp_low, grad_gate_low),
        (normed_mlp_low, grad_up_low),
        (act_low, grad_out_low),
    )
    shares = tuple(
        (
            lax.psum_scatter(
                weight_term(left_side, right_side).astype(jnp.bfloat16),
                "blk",
                scatter_dimension=0,
                tiled=True,
            ).astype(jnp.float32)
            for left_side, right_side in grad_pairs
        )
    )
    shares = jax.tree.map(lambda part: part.astype(jnp.float32), lax.psum(shortened(shares), "seq"))
    return (
        activations,
        input_grads,
        shares[0][None],
        shares[1][None],
        shares[2][None],
        shares[3][None],
        shares[4][None],
        shares[5][None],
        shares[6][None],
        shares[7][None],
        shares[8][None],
    )


MESH = pl.DeviceIdType.MESH


def remote(source, target, sent, arrived, device):
    return pltpu.make_async_remote_copy(
        source, target, sent, arrived, device_id=device, device_id_type=MESH
    )


def greet(partners):
    barrier = pltpu.get_barrier_semaphore()
    for device in partners:
        pl.semaphore_signal(barrier, 1, device_id=device, device_id_type=MESH)
    pl.semaphore_wait(barrier, len(partners))


def settled(spot, semaphore, received):
    copy = remote(spot, spot, semaphore, semaphore, {"seq": lax.axis_index("seq") ^ 1})
    if received:
        copy.wait_recv()
    else:
        copy.wait_send()


CUTS = 2


def gather_steps(
    count, own, out, line_sent, line_got, side_sent, side_got, core_sent, core_got, local_done
):
    seq, b = lax.axis_index("seq"), lax.axis_index("blk")
    core, side = {"seq": seq ^ 1}, {"seq": seq ^ 2}
    base, side_base = seq * count, (seq ^ 2) * count
    cut = out.shape[1] // CUTS

    def spot(index, h):
        return out.at[index, pl.ds(h * cut, cut)]

    def begin(index, h, first):
        return own.at[pl.ds(h * cut, cut)] if first else spot(index, h)

    def along_line(j, way, h, first=False):
        device = {"blk": b + (1 if way else -1)}
        return remote(
            begin(base + j, h, first),
            spot(base + j, h),
            line_sent.at[j, way, h],
            line_got.at[j, h],
            device,
        )

    def to_side(j, h, first=False):
        return remote(
            begin(base + j, h, first),
            spot(base + j, h),
            side_sent.at[j, h],
            side_got.at[j, h],
            side,
        )

    def to_core(half, j, h, first=False):
        index = (side_base if half else base) + j
        return remote(
            begin(index, h, first),
            spot(index, h),
            core_sent.at[half, j, h],
            core_got.at[half, j, h],
            core,
        )

    local = pltpu.make_async_copy(own, out.at[base + b], local_done)
    local.start()
    for h in range(CUTS):
        to_side(b, h, True).start()
        pl.when(b > 0)(along_line(b, 0, h, True).start)
        pl.when(b < count - 1)(along_line(b, 1, h, True).start)
    for h in range(CUTS):
        to_core(0, b, h, True).start()
    yield "sent"

    def from_line(j, way):
        for h in range(CUTS):
            settled(spot(base + j, h), line_got.at[j, h], True)
            pl.when((b < count - 1) if way else (b > 0))(along_line(j, way, h).start)
            to_side(j, h).start()
        for h in range(CUTS):
            to_core(0, j, h).start()

    def from_side(j):
        for h in range(CUTS):
            settled(spot(side_base + j, h), side_got.at[j, h], True)
            to_core(1, j, h).start()

    for k in range(1, count + 1):
        if k < count:
            pl.when(b - k >= 0)(functools.partial(from_line, b - k, 1))
            pl.when(b + k < count)(functools.partial(from_line, b + k, 0))
        if k == 1:
            from_side(b)
        else:
            pl.when(b - k + 1 >= 0)(functools.partial(from_side, b - k + 1))
            pl.when(b + k - 1 < count)(functools.partial(from_side, b + k - 1))
        if k == count - 1:
            local.wait()
        yield "line" if k == count - 1 else "side" if k == count else "step"
    for half, corner in ((0, seq ^ 1), (1, seq ^ 3)):
        for j in range(count):
            for h in range(CUTS):
                settled(spot(corner * count + j, h), core_got.at[half, j, h], True)
        yield "corner" if half else "near"
    yield "done"
    for h in range(CUTS):
        for j in range(count):
            to_side(j, h).wait_send()
            to_core(0, j, h).wait_send()
            to_core(1, j, h).wait_send()
        pl.when(b > 0)(along_line(b, 0, h).wait_send)
        pl.when(b < count - 1)(along_line(b, 1, h).wait_send)
        for k in range(1, count):
            pl.when((b - k >= 0) & (b < count - 1))(along_line(b - k, 1, h).wait_send)
            pl.when((b + k < count) & (b > 0))(along_line(b + k, 0, h).wait_send)


def gather_semaphores(count):
    dma = pltpu.SemaphoreType.DMA
    return [
        dma((count, 2, CUTS)),
        dma((count, CUTS)),
        dma((count, CUTS)),
        dma((count, CUTS)),
        dma((2, count, CUTS)),
        dma((2, count, CUTS)),
        dma,
    ]


def line_steps(
    count, own, out, line_sent, line_got, core_sent, core_got, local_done, offset=0
):
    seq, b = lax.axis_index("seq"), lax.axis_index("blk")
    core, base = {"seq": seq ^ 1}, offset + (seq % 2) * count
    cut = out.shape[1] // CUTS

    def spot(j, h):
        return out.at[base + j, pl.ds(h * cut, cut)]

    def begin(j, h, first):
        return own.at[pl.ds(h * cut, cut)] if first else spot(j, h)

    def along_line(j, way, h, first=False):
        device = {"blk": b + (1 if way else -1)}
        return remote(
            begin(j, h, first), spot(j, h), line_sent.at[j, way, h], line_got.at[j, h], device
        )

    def to_core(j, h, first=False):
        return remote(begin(j, h, first), spot(j, h), core_sent.at[j, h], core_got.at[j, h], core)

    local = pltpu.make_async_copy(own, out.at[base + b], local_done)
    local.start()
    for h in range(CUTS):
        pl.when(b > 0)(along_line(b, 0, h, True).start)
        pl.when(b < count - 1)(along_line(b, 1, h, True).start)
        to_core(b, h, True).start()
    yield

    def from_line(j, way):
        for h in range(CUTS):
            settled(spot(j, h), line_got.at[j, h], True)
            pl.when((b < count - 1) if way else (b > 0))(along_line(j, way, h).start)
            to_core(j, h).start()

    for k in range(1, count):
        pl.when(b - k >= 0)(functools.partial(from_line, b - k, 1))
        pl.when(b + k < count)(functools.partial(from_line, b + k, 0))
        yield
    local.wait()
    for h in range(CUTS):
        for j in range(count):
            place = offset + (1 - seq % 2) * count + j
            settled(out.at[place, pl.ds(h * cut, cut)], core_got.at[j, h], True)
            to_core(j, h).wait_send()
        pl.when(b > 0)(along_line(b, 0, h).wait_send)
        pl.when(b < count - 1)(along_line(b, 1, h).wait_send)
        for k in range(1, count):
            pl.when((b - k >= 0) & (b < count - 1))(along_line(b - k, 1, h).wait_send)
            pl.when((b + k < count) & (b > 0))(along_line(b + k, 0, h).wait_send)


def line_semaphores(count):
    dma = pltpu.SemaphoreType.DMA
    return [
        dma((count, 2, CUTS)),
        dma((count, CUTS)),
        dma((count, CUTS)),
        dma((count, CUTS)),
        dma,
    ]


def advance(steps, times):
    for _ in range(times):
        next(steps, None)


def until_done(steps):
    for event in steps:
        if event == "done":
            return
        yield event


def all_but_last(compute):
    groups = []

    def some(group):
        groups.append(group)
        if len(groups) < 4:
            compute(group)

    return some


def group_of(event):
    seq = lax.axis_index("seq")
    return {"line": seq, "side": seq ^ 2, "near": seq ^ 1, "corner": seq ^ 3}.get(event)


def scatter_steps(
    count,
    partial,
    deliver,
    core_slot,
    side_slot,
    line_slot,
    side_out,
    line_out,
    running,
    core_sent,
    core_got,
    side_sent,
    side_got,
    line_sent,
    line_got,
    compute=None,
):
    seq, b = lax.axis_index("seq"), lax.axis_index("blk")
    core, side = {"seq": seq ^ 1}, {"seq": seq ^ 2}
    place = far_first(b, count)
    size = partial.shape[1] // CUTS
    cuts = [pl.ds(h * size, size) for h in range(CUTS)]

    def to_core(half, k, h):
        return remote(
            partial.at[(seq ^ (1 if half else 3)) * count + place[k], cuts[h]],
            core_slot.at[half, k, cuts[h]],
            core_sent.at[half, k, h],
            core_got.at[half, k, h],
            core,
        )

    def to_side(k, h):
        return remote(
            side_out.at[k, cuts[h]],
            side_slot.at[k, cuts[h]],
            side_sent.at[k, h],
            side_got.at[k, h],
            side,
        )

    def along_line(k, way, h):
        j = place[k]
        return remote(
            line_out.at[k, cuts[h]],
            line_slot.at[way, j, cuts[h]],
            line_sent.at[k, h],
            line_got.at[way, j, h],
            {"blk": b + (1 if way else -1)},
        )

    def add_from(way, j, h):
        settled(line_slot.at[way, j, cuts[h]], line_got.at[way, j, h], True)
        running[cuts[h]] += line_slot[way, j, cuts[h]].astype(jnp.float32)

    def exchange(half):
        if compute:
            compute(seq ^ (1 if half else 3))
        for k in range(count):
            for h in range(CUTS):
                to_core(half, k, h).start()

    exchange(0)
    if compute:
        compute(seq ^ 2)
    for k in range(count):
        for h in range(CUTS):
            to_core(0, k, h).wait_recv()
            total = partial[(seq ^ 2) * count + place[k], cuts[h]].astype(jnp.float32)
            total += core_slot[0, k, cuts[h]].astype(jnp.float32)
            side_out[k, cuts[h]] = total.astype(jnp.bfloat16)
            to_side(k, h).start()
    exchange(1)
    if compute:
        compute(seq)
    yield
    for k in range(count):
        j = place[k]
        rightward, leftward = j >= b, j <= b
        for h in range(CUTS):
            to_core(1, k, h).wait_recv()
            to_side(k, h).wait_recv()
            total = partial[seq * count + j, cuts[h]].astype(jnp.float32)
            total += core_slot[1, k, cuts[h]].astype(jnp.float32)
            running[cuts[h]] = total + side_slot[k, cuts[h]].astype(jnp.float32)
            pl.when(rightward & (b > 0))(functools.partial(add_from, 1, j, h))
            pl.when(leftward & (b < count - 1))(functools.partial(add_from, 0, j, h))
            if k < count - 1:
                line_out[k, cuts[h]] = running[cuts[h]].astype(jnp.bfloat16)
                pl.when(rightward)(along_line(k, 1, h).start)
                pl.when(jnp.logical_not(rightward))(along_line(k, 0, h).start)
        if k < count - 1:
            yield
    deliver(running[...])
    yield
    for k in range(count):
        for h in range(CUTS):
            to_core(0, k, h).wait_send()
            to_core(1, k, h).wait_send()
            to_side(k, h).wait_send()
            if k < count - 1:
                settled(line_out.at[k, cuts[h]], line_sent.at[k, h], False)


def line_first_steps(
    count,
    partial,
    deliver,
    own,
    core_slot,
    line_slot,
    line_out,
    side_slot,
    running,
    own_done,
    core_sent,
    core_got,
    line_sent,
    line_got,
    side_sent,
    side_got,
):
    seq, b = lax.axis_index("seq"), lax.axis_index("blk")
    core, side = {"seq": seq ^ 1}, {"seq": seq ^ 2}
    place = far_first(b, count)

    def to_core(half, k):
        source = partial.at[(seq ^ (1 if half else 3)) * count + place[k]]
        return remote(
            source, core_slot.at[half, k], core_sent.at[half, k], core_got.at[half, k], core
        )

    def kept(half, k):
        source = partial.at[(seq if half else seq ^ 2) * count + place[k]]
        return pltpu.make_async_copy(source, own.at[half, k], own_done.at[half, k])

    def along_line(half, k, way):
        j = place[k]
        return remote(
            line_out.at[half, k],
            line_slot.at[half, way, j],
            line_sent.at[half, k],
            line_got.at[half, way, j],
            {"blk": b + (1 if way else -1)},
        )

    def add_from(half, way, j):
        settled(line_slot.at[half, way, j], line_got.at[half, way, j], True)
        running[...] += line_slot[half, way, j].astype(jnp.float32)

    to_side = remote(line_out.at[0, count - 1], side_slot.at[0], side_sent, side_got, side)
    for half in range(2):
        for k in range(count):
            kept(half, k).start()
            to_core(half, k).start()
    yield
    for k in range(count):
        j = place[k]
        rightward, leftward = j >= b, j <= b
        for half in range(2):
            kept(half, k).wait()
            to_core(half, k).wait_recv()
            running[...] = own[half, k].astype(jnp.float32) + core_slot[half, k].astype(jnp.float32)
            pl.when(rightward & (b > 0))(functools.partial(add_from, half, 1, j))
            pl.when(leftward & (b < count - 1))(functools.partial(add_from, half, 0, j))
            if half == 0 or k < count - 1:
                line_out[half, k] = running[...].astype(jnp.bfloat16)
            if k < count - 1:
                pl.when(rightward)(along_line(half, k, 1).start)
                pl.when(jnp.logical_not(rightward))(along_line(half, k, 0).start)
            elif half == 0:
                to_side.start()
            else:
                to_side.wait_recv()
                deliver(running[...] + side_slot[0].astype(jnp.float32))
            yield
    to_side.wait_send()
    for half in range(2):
        for k in range(count):
            to_core(half, k).wait_send()
            if k < count - 1:
                settled(line_out.at[half, k], line_sent.at[half, k], False)


def far_first(b, count):
    order = sorted(range(count), key=lambda j: -j)
    places = []
    for k in range(count):
        place = 0
        for own in range(count):
            by_distance = sorted(order, key=lambda j: (-abs(j - own), -j if own * 2 < count else j))
            place = jnp.where(b == own, by_distance[k], place)
        places.append(place)
    return places


def scatter_scratch(count, rows, width):
    dma = pltpu.SemaphoreType.DMA

    def slots(*places):
        return pltpu.VMEM(places + (rows, width), jnp.bfloat16)

    return [
        slots(2, count),
        slots(count),
        slots(2, count),
        slots(count),
        slots(count - 1),
        pltpu.VMEM((rows, width), jnp.float32),
        dma((2, count, CUTS)),
        dma((2, count, CUTS)),
        dma((count, CUTS)),
        dma((count, CUTS)),
        dma((count - 1, CUTS)),
        dma((2, count, CUTS)),
    ]


def run_all(fillers):
    for filler in fillers:
        filler()


def run_with(steps, fillers):
    fillers = list(fillers)
    for _ in steps:
        if fillers:
            fillers.pop(0)()
    for filler in fillers:
        filler()


def greet_group(count, more=()):
    seq, b = lax.axis_index("seq"), lax.axis_index("blk")
    greet(
        tuple(more)
        + ({"seq": seq ^ 1}, {"seq": seq ^ 2})
        + tuple({"blk": lax.rem(b + k, count)} for k in range(1, count))
    )


def carry(copies, from_section, what):
    sending = lax.axis_index("section") == from_section
    for copy in copies:
        if what == "start":
            pl.when(sending)(copy.start)
        else:
            pl.when(sending)(copy.wait_send)
            pl.when(jnp.logical_not(sending))(copy.wait_recv)


def carried(sources, targets, sent, got):
    other = {"section": 1 - lax.axis_index("section")}
    return [
        remote(source, target, sent.at[n], got.at[n], other)
        for n, (source, target) in enumerate(zip(sources, targets))
    ]


def group_rows(ref, group, count):
    value = ref[pl.ds(group * count, count)]
    return value.reshape(value.shape[0] * value.shape[1], value.shape[2])


def group_span(group, count, block):
    size = count * block
    return pl.ds(pl.multiple_of(group * size, size), size)


def lane_turn(field_in, cosine, sine):
    half_dim, lanes = HEAD_DIM // 2, field_in.shape[-1]
    lane = lax.broadcasted_iota(jnp.int32, field_in.shape, 1)
    partner = jnp.where(
        lane < half_dim,
        pltpu.roll(field_in, lanes - half_dim, 1),
        pltpu.roll(field_in, half_dim, 1),
    )
    return field_in * cosine + partner * sine


def masked_scores(query, key, first_row, start):
    scores = back_product(query, key) * HEAD_DIM ** (-0.5)
    key_index = lax.broadcasted_iota(jnp.int32, scores.shape, 1)
    query_index = first_row + lax.broadcasted_iota(jnp.int32, scores.shape, 0)
    return jnp.where((key_index >= start) & (key_index <= query_index), scores, MASKED)


def normalise(field_in, gain_row):
    inv_root = lax.rsqrt(jnp.mean(field_in * field_in, axis=-1, keepdims=True) + EPS)
    return field_in * inv_root * gain_row


PAD = 128


GAINS = HEAD_DIM
OWN_PART = HEAD_DIM + 16


def load_weights(layer, attn, twin, out, attn_vm, out_vm, sems):
    on_key = lax.axis_index("seq") % 2 == 0
    own, other = attn.at[layer, pl.ds(OWN_PART, HEAD_DIM)], twin.at[layer]

    def part(source, n, rows):
        return pltpu.make_async_copy(source, attn_vm.at[pl.ds(n * PAD, rows)], sems.at[n])

    copies = [
        part(attn.at[layer, pl.ds(0, HEAD_DIM)], 0, HEAD_DIM),
        part(attn.at[layer, pl.ds(GAINS, 16)], 3, 16),
    ]
    if out is not None:
        copies.append(
            pltpu.make_async_copy(out.at[layer], out_vm.at[pl.ds(0, HEAD_DIM)], sems.at[4])
        )
    start_all(copies)

    @pl.when(on_key)
    def _():
        part(own, 1, HEAD_DIM).start()
        part(other, 2, HEAD_DIM).start()

    @pl.when(jnp.logical_not(on_key))
    def _():
        part(other, 1, HEAD_DIM).start()
        part(own, 2, HEAD_DIM).start()

    return copies + [part(other, 1, HEAD_DIM), part(other, 2, HEAD_DIM)]


def clear_pads(attn_vm, out_vm):
    empty = jnp.zeros((PAD - HEAD_DIM, attn_vm.shape[1]), jnp.bfloat16)
    for part in range(3):
        attn_vm[part * PAD + HEAD_DIM : (part + 1) * PAD] = empty
    out_vm[HEAD_DIM:PAD] = empty


def attention_rows(heads, log_total, start, size, tokens):
    for i in range(tokens // size):
        here, seen = slice(i * size, (i + 1) * size), slice(0, (i + 1) * size)
        scores = masked_scores(heads[0, here], heads[1, seen], i * size, start[here])
        row_top = jnp.max(scores, axis=-1, keepdims=True)
        weights = jnp.exp(scores - row_top)
        total = jnp.sum(weights, axis=-1, keepdims=True)
        log_total[here] = row_top + jnp.log(total)
        weights = (weights * (1.0 / total)).astype(jnp.bfloat16)
        heads[3, here] = product(weights, heads[2, seen]).astype(jnp.bfloat16)


def project_heads(normed, attn_vm, heads, span, cosine, sine):
    mixed = back_product(normed, attn_vm[0 : 3 * PAD])
    cos_rows, sin_rows = cosine[span], sine[span]
    heads[0, span] = lane_turn(mixed[:, :PAD], cos_rows, sin_rows).astype(jnp.bfloat16)
    heads[1, span] = lane_turn(mixed[:, PAD : 2 * PAD], cos_rows, sin_rows).astype(jnp.bfloat16)
    heads[2, span] = mixed[:, 2 * PAD :].astype(jnp.bfloat16)


def keep_group(partial, group, value, count):
    block = partial.shape[1]
    partial[pl.ds(group * count, count)] = value.astype(jnp.bfloat16).reshape(count, block, -1)


def gain_of(ref, row):
    return ref[3 * PAD : 3 * PAD + 16][row : row + 1].astype(jnp.float32)


def fill_tables(lengths, frequency, cosine, sine, start):
    section = lax.axis_index("section")
    token = lax.broadcasted_iota(jnp.int32, start.shape, 0)
    end, begin = 0, jnp.zeros(start.shape, jnp.int32)
    for n in range(lengths.shape[2]):
        length = lengths[section, 0, n]
        end = end + length
        begin = begin + jnp.where(end <= token, length, 0)
    start[...] = begin
    lane = lax.broadcasted_iota(jnp.int32, cosine.shape, 1)
    angles = (token - begin).astype(jnp.float32) * frequency[...]
    cosine[...] = jnp.where(lane < HEAD_DIM, jnp.cos(angles), 0.0)
    turned = jnp.where(lane < HEAD_DIM, jnp.sin(angles), 0.0)
    sine[...] = jnp.where(lane < HEAD_DIM // 2, -turned, turned)


def first_layer_kernel(count, *refs):
    refs = iter(refs)

    def take(n):
        return [next(refs) for _ in range(n)]

    w_query, w_key, w_value, w_gate, w_up, w_output, w_down = take(7)
    gain_attn, gain_mlp, inputs, cotangent, lengths, frequency = take(6)
    attn, twin, gate_up, out, down, all_rows, wide_rows, grads_near, grads_side = take(9)
    cosine, sine, start = take(3)
    gain_rows = take(4)
    hidden, result_out, normed_out, heads, log_total = take(5)
    raw_vm, normed_vm, rows_vm, partial, partial_two, grads_vm = take(6)
    attn_vm, out_vm, wide_vm, down_vm, units, normed_own, gain_vm = take(7)
    pieces, query_vm, other_vm, query_turned, other_turned, weights_done = take(6)
    load_done, save_done, twin_sent, twin_got = take(4)
    spread_sems = take(5)
    first_sems, second_sems, grads_sems, side_sems = take(7), take(7), take(5), take(2)
    scatter_one, scatter_two = take(12), take(12)
    section = lax.axis_index("section")
    block, width = raw_vm.shape[1], raw_vm.shape[2]
    tokens = block * raw_vm.shape[0]
    size = count * block
    low, f32 = jnp.bfloat16, jnp.float32
    seq = lax.axis_index("seq")
    rows_in, grads_in = inputs.at[section, 0], cotangent.at[section, 0]
    query_load = pltpu.make_async_copy(w_query, query_vm, weights_done.at[0])
    query_load.start()
    key_load = pltpu.make_async_copy(w_key, other_vm, weights_done.at[1])
    value_load = pltpu.make_async_copy(w_value, other_vm, weights_done.at[1])
    pl.when(seq % 2 == 0)(key_load.start)
    pl.when(seq % 2 == 1)(value_load.start)
    greet_group(count, ({"section": 1 - section},))
    steps = gather_steps(count, rows_in, raw_vm, *first_sems)
    next(steps)
    query_load.wait()
    key_load.wait()
    query_turned[...] = query_vm[...].astype(f32).T.astype(low)
    other_turned[...] = other_vm[...].astype(f32).T.astype(low)
    row = lax.broadcasted_iota(jnp.int32, (16, gain_attn.shape[1]), 0)
    own_gains = jnp.where(row == 0, gain_attn[...], jnp.where(row == 1, gain_mlp[...], 0))
    per_blk = other_turned.shape[0] // HEAD_DIM // count
    for j in range(count):
        head = j * 4 + seq
        other_head = j * per_blk + seq * per_blk // 4
        for place, turned, index in (
            (0, query_turned, head),
            (OWN_PART, other_turned, other_head),
        ):
            rows = pl.ds(pl.multiple_of(index * HEAD_DIM, 16), HEAD_DIM)
            pieces[j, place : place + HEAD_DIM] = turned[rows]
        pieces[j, GAINS : GAINS + 16] = own_gains.astype(low)
    spread = spread_steps(
        count, pieces, w_gate, w_up, w_output, w_down, attn, gate_up, out, down, *spread_sems
    )
    next(spread)
    fill_tables(lengths, frequency, cosine, sine, start)
    clear_pads(attn_vm, out_vm)
    for event in until_done(steps):
        if event == "side":
            advance(spread, 3)
    grads_across = remote(
        grads_in, grads_side, *side_sems, {"seq": lax.axis_index("seq") ^ 2}
    )
    grads_across.start()
    next(spread)
    pair = remote(
        attn.at[:, pl.ds(OWN_PART, HEAD_DIM)],
        twin,
        twin_sent,
        twin_got,
        {"seq": lax.axis_index("seq") ^ 1},
    )
    pair.start()
    pair.wait()
    gain_load = pltpu.make_async_copy(attn.at[1, pl.ds(GAINS, 16)], gain_vm, load_done.at[5])
    gain_load.start()
    wait_all(load_weights(0, attn, twin, None, attn_vm, out_vm, load_done) + [gain_load])
    for group in range(tokens // size):
        raw = raw_vm[group * count : (group + 1) * count].astype(f32)
        normed = normalise(raw, gain_of(attn_vm, 0)[None]).astype(low)
        normed_vm[group * count : (group + 1) * count] = normed
        span = slice(group * size, (group + 1) * size)
        project_heads(normed.reshape(size, width), attn_vm, heads, span, cosine, sine)
    saves = [pltpu.make_async_copy(normed_vm, all_rows, save_done.at[0])]
    saves[0].start()
    attention_rows(heads, log_total, start, size, tokens)
    next(spread)
    load = pltpu.make_async_copy(out.at[0], out_vm.at[pl.ds(0, HEAD_DIM)], load_done.at[4])
    load.start()
    load.wait()

    def project_out(group):
        mixed = heads[3, group_span(group, count, block)]
        keep_group(partial, group, product(mixed, out_vm[...]), count)

    def deliver(total):
        value = rows_in[...].astype(f32) + total
        hidden[...] = value
        normed_own[...] = normalise(value, gain_of(attn_vm, 1)).astype(low)

    def more():
        next(spread)

    run_with(scatter_steps(count, partial, deliver, *scatter_one, compute=project_out), [more] * 5)
    for _ in steps:
        pass
    steps = gather_steps(count, normed_own, rows_vm, *second_sems)
    for number, event in enumerate(until_done(steps)):
        if number == 0:
            more()
    for _ in spread:
        pass
    loads = [
        pltpu.make_async_copy(gate_up.at[0], wide_vm, load_done.at[0]),
        pltpu.make_async_copy(down.at[0], down_vm, load_done.at[1]),
    ]
    start_all(loads)
    wait_all(loads)
    saves.append(pltpu.make_async_copy(rows_vm, wide_rows, save_done.at[1]))
    saves[1].start()

    def project_down(group):
        pre = product(group_rows(rows_vm, group, count), wide_vm[...])
        made = hidden_units(pre)
        units[group_span(group, count, block)] = made
        keep_group(partial_two, group, product(made, down_vm[...]), count)

    grad_steps = line_steps(count, grads_in, grads_vm, *grads_sems)
    next(grad_steps)

    for n in range(2):
        gain_rows[n][...] = gain_of(attn_vm, n)

    def deliver_two(total):
        made = (hidden[...] + total).astype(low)
        result_out[...] = made
        gain = gain_vm[...][0:1].astype(f32)
        gain_rows[2][...] = gain
        gain_rows[3][...] = gain_vm[...][1:2].astype(f32)
        normed_out[...] = normalise(made.astype(f32), gain).astype(low)

    run_with(
        scatter_steps(count, partial_two, deliver_two, *scatter_two, compute=project_down),
        [functools.partial(advance, grad_steps, 1)] * 3,
    )
    for _ in grad_steps:
        pass
    for _ in steps:
        pass
    saves.append(pltpu.make_async_copy(grads_vm, grads_near, save_done.at[2]))
    saves[2].start()
    grads_across.wait()
    wait_all(saves)


def spread_steps(
    count,
    pieces,
    w_gate,
    w_up,
    w_output,
    w_down,
    attn,
    gate_up,
    out,
    down,
    line_sent,
    line_got,
    cross_sent,
    cross_got,
    local_done,
):
    seq, b, section = lax.axis_index("seq"), lax.axis_index("blk"), lax.axis_index("section")
    seq_count = lax.axis_size("seq")
    other = {"section": 1 - section}
    rows, lanes = w_gate.shape[0], gate_up.shape[2] // 2
    turns = tuple(range(count // 2, 0, -1)) + tuple(range(count // 2 + 1, count))

    def source(kind, j):
        if kind == 0:
            return pieces.at[j]
        weight = w_gate if kind == 1 else w_up
        return weight.at[:, pl.ds(pl.multiple_of((j * seq_count + seq) * lanes, lanes), lanes)]

    def target(kind, j):
        if kind == 0:
            return attn.at[section, :, pl.ds(pl.multiple_of(j * rows, rows), rows)]
        return gate_up.at[
            section, pl.ds(pl.multiple_of(j * rows, rows), rows), pl.ds((kind - 1) * lanes, lanes)
        ]

    def along_line(kind, k):
        j = lax.rem(b + k, count)
        return remote(
            source(kind, j),
            target(kind, b),
            line_sent.at[kind, k],
            line_got.at[kind, k],
            {"blk": j},
        )

    def across(kind, j, slot, begin=None):
        spot = target(kind, j)
        return remote(
            spot if begin is None else begin,
            spot,
            cross_sent.at[kind, slot],
            cross_got.at[kind, slot],
            other,
        )

    def own_rows(kind):
        weight, place = (w_output, out) if kind == 3 else (w_down, down)
        size = place.shape[1]
        begin = weight.at[pl.ds(pl.multiple_of(seq * size, size), size)]
        spot = place.at[section]
        return (
            remote(begin, spot, cross_sent.at[kind, 0], cross_got.at[kind, 0], other),
            pltpu.make_async_copy(begin, spot, local_done.at[kind]),
        )

    def own_piece(kind):
        return (
            across(kind, b, 0, source(kind, b)),
            pltpu.make_async_copy(source(kind, b), target(kind, b), local_done.at[kind]),
        )

    def forward(kind, k):
        j = lax.rem(b + count - k, count)
        settled(target(kind, j), line_got.at[kind, k], True)
        across(kind, j, k).start()

    def arrived(kind):
        if kind > 2:
            wait_all(own_rows(kind))
            return
        for k in range(count):
            settled(target(kind, 0), cross_got.at[kind, k], True)
            settled(target(kind, 0), cross_sent.at[kind, k], False)
            if k:
                settled(target(kind, 0), line_sent.at[kind, k], False)
        pltpu.make_async_copy(source(kind, b), target(kind, b), local_done.at[kind]).wait()

    for k in turns:
        along_line(0, k).start()
    start_all(own_piece(0))
    yield
    for k in turns:
        forward(0, k)
        yield
    start_all(own_rows(3))
    for kind in (1, 2):
        for k in turns:
            along_line(kind, k).start()
    arrived(0)
    start_all(own_piece(1) + own_piece(2) + own_rows(4))
    yield
    arrived(3)
    yield
    for kind in (1, 2):
        for k in turns:
            forward(kind, k)
            yield
    for kind in (1, 2, 4):
        arrived(kind)


def start_all(copies):
    for copy in copies:
        copy.start()


def wait_all(copies):
    for copy in copies:
        copy.wait()


def gated(pre):
    half = pre.shape[1] // 2
    gate, up = pre[:, :half], pre[:, half:]
    sigma = jax.nn.sigmoid(gate)
    return gate, up, sigma


def hidden_units(pre):
    gate, up, sigma = gated(pre)
    return (gate * sigma * up).astype(jnp.bfloat16)


def store_gate_grads(place, span, grad_act, pre):
    gate, up, sigma = gated(pre)
    half = gate.shape[1]
    place[span, 0:half] = (grad_act * up * sigma * (1.0 + gate * (1.0 - sigma))).astype(
        jnp.bfloat16
    )
    place[span, half : 2 * half] = (grad_act * (gate * sigma)).astype(jnp.bfloat16)


def wide_grads(rows_vm, pre_grads, units, grads_vm, wide_grad, down_grad):
    tokens = pre_grads.shape[0]
    width = rows_vm.shape[2]
    step = width // 4

    def wide_part(n):
        cut = slice(n * step, (n + 1) * step)
        rows = rows_vm[:, :, cut].reshape(tokens, step)
        wide_grad[cut] = weight_term(rows, pre_grads[...]).astype(jnp.bfloat16)

    def down_part(n):
        cut = slice(n * 2 * step, (n + 1) * 2 * step)
        rows = grads_vm[:, :, cut].reshape(tokens, 2 * step)
        down_grad[:, cut] = weight_term(units[...], rows).astype(jnp.bfloat16)

    return [functools.partial(wide_part, n) for n in range(4)] + [
        functools.partial(down_part, n) for n in range(2)
    ]


def mlp_grad_sent(total, hidden, grads_own, gain, branch_out, grad_hidden_out, gain_out):
    field_in = hidden[...]
    inv_root = lax.rsqrt(jnp.mean(field_in * field_in, axis=-1, keepdims=True) + EPS)
    part, terms = rms_backward(field_in, gain[...], inv_root, total)
    grad_hidden = grads_own[...].astype(jnp.float32) + part
    grad_hidden_out[...] = grad_hidden
    branch_out[...] = grad_hidden.astype(jnp.bfloat16)
    gain_out[...] = jnp.broadcast_to(jnp.sum(terms, axis=0, keepdims=True), gain_out.shape)


class Parts:
    pass


def attn_back_refs(take, attn_grad=None, out_grad=None):
    r = Parts()
    r.branch_vm, r.rows_vm, r.heads, r.attn_vm, r.out_vm, r.mixed_grads, r.probs = take(7)
    r.key_grads, r.value_grads, r.joint, r.partial, r.load_done = take(5)
    r.gather_sems = take(7)
    r.scatter_refs = take(12)
    return r


def attn_back_body(
    count, layer, r, ins, outs, background, fillers, gathered=None, spare=None
):
    branch_in, grad_hidden, x_own, all_rows, heads_kept, log_total, attn, twin, out = ins[:9]
    cosine, sine, start, gain = ins[9:]
    grad_out, gain_out, attn_grad, out_grad = outs
    branch_vm, rows_vm, heads, attn_vm, out_vm = r.branch_vm, r.rows_vm, r.heads, r.attn_vm, r.out_vm
    mixed_grads, probs, key_grads, value_grads = r.mixed_grads, r.probs, r.key_grads, r.value_grads
    joint, partial, load_done = r.joint, r.partial, r.load_done
    block = rows_vm.shape[1]
    size = count * block
    tokens = block * rows_vm.shape[0]
    low, f32 = jnp.bfloat16, jnp.float32
    scale = HEAD_DIM ** (-0.5)
    steps = gather_steps(count, branch_in, branch_vm, *r.gather_sems)
    next(steps)
    background()
    loads = []
    if layer is not None:
        clear_pads(attn_vm, out_vm)
        loads = load_weights(layer, attn, twin, out, attn_vm, out_vm, load_done)
        kept = [
            pltpu.make_async_copy(heads_kept, heads, load_done.at[5]),
            pltpu.make_async_copy(all_rows, rows_vm, load_done.at[6]),
        ]
        start_all(kept)
        loads += kept
    key_grads[...] = jnp.zeros_like(key_grads)
    value_grads[...] = jnp.zeros_like(value_grads)
    wait_all(loads)

    def spans(i):
        return slice(i * size, (i + 1) * size), slice(0, (i + 1) * size)

    def weigh(i):
        here, seen = spans(i)
        scores = masked_scores(heads[0, here], heads[1, seen], i * size, start[here])
        probs[here, seen] = jnp.exp(scores - log_total[here])

    def project(group):
        value = back_product(group_rows(branch_vm, group, count), out_vm[...])
        mixed_grads[group_span(group, count, block)] = value.astype(low)

    for number, event in enumerate(until_done(steps)):
        if number < 2:
            weigh(2 * number)
            weigh(2 * number + 1)
        group = group_of(event)
        if group is not None:
            project(group)
    if gathered:
        gathered()
    for i in reversed(range(tokens // size)):
        here, seen = spans(i)
        weights = probs[here, seen]
        grads = mixed_grads[here]
        grad_weights = back_product(grads, heads[2, seen])
        centre = jnp.sum(weights * grad_weights, axis=-1, keepdims=True)
        grad_scores = (weights * (grad_weights - centre)).astype(low)
        query_grad = (product(grad_scores, heads[1, seen]) * scale).astype(low).astype(f32)
        joint[here, 0:PAD] = lane_turn(query_grad, cosine[here], -sine[here]).astype(low)
        key_grads[seen] += weight_term(grad_scores, heads[0, here])
        value_grads[seen] += weight_term(weights.astype(low), grads)
        key_grad = (key_grads[here] * scale).astype(low).astype(f32)
        joint[here, PAD : 2 * PAD] = lane_turn(key_grad, cosine[here], -sine[here]).astype(low)
        joint[here, 2 * PAD : 3 * PAD] = value_grads[here].astype(low)

    def project_back(group):
        value = product(joint[group_span(group, count, block)], attn_vm[0 : 3 * PAD])
        partial[pl.ds(group * count, count)] = value.astype(low).reshape(count, block, -1)

    def attn_part(part):
        rows = rows_vm[...].reshape(tokens, rows_vm.shape[2])
        value = weight_term(joint[:, part * PAD : (part + 1) * PAD], rows)
        attn_grad[part * HEAD_DIM : (part + 1) * HEAD_DIM] = value[0:HEAD_DIM].astype(low)

    def out_part():
        rows = branch_vm[...].reshape(tokens, branch_vm.shape[2])
        out_grad[...] = weight_term(heads[3], rows)[0:HEAD_DIM].astype(low)

    def deliver(total):
        field_in = x_own[...].astype(f32)
        inv_root = lax.rsqrt(jnp.mean(field_in * field_in, axis=-1, keepdims=True) + EPS)
        part, terms = rms_backward(field_in, gain[...], inv_root, total)
        grad_out[...] = (grad_hidden[...] + part).astype(low)
        gain_out[...] = jnp.broadcast_to(jnp.sum(terms, axis=0, keepdims=True), gain_out.shape)

    parts = [functools.partial(attn_part, n) for n in range(3)] + [out_part]
    if spare:
        parts.append(spare)
    run_with(
        scatter_steps(count, partial, deliver, *r.scatter_refs, compute=project_back),
        [functools.partial(run_all, parts)] + fillers,
    )
    for _ in steps:
        pass


def middle_kernel(count, *refs):
    refs = iter(refs)

    def take(n):
        return [next(refs) for _ in range(n)]

    rows_in, between, grads_side, cosine, sine, start, attn, twin, out = take(9)
    grads_near, gate_up, down, cotangent, hidden_one, wide_rows = take(6)
    grads_own = cotangent.at[lax.axis_index("section"), 0]
    gain_mlp_two, gain_attn_two, gain_mlp_one = take(3)
    hidden, ahead, grad_between, branch_out, grad_hidden_out = take(5)
    mlp_two_sum, attn_two_sum, mlp_one_sum = take(3)
    grads_kept = take(6)
    carried_to = take(4)
    rows_two, grads_vm, partial, wide_vm, down_vm = take(5)
    log_total, units, pre_vm, pre_grads, normed_own, branch_own, grad_hidden = take(7)
    load_done, carry_sent, carry_got, keep_done = take(4)
    wide_two, down_two, attn_two, out_two, wide_one, down_one = take(6)
    line_sems = take(5)
    r = attn_back_refs(take)
    rows_one, heads, attn_vm, out_vm, partial_back = (
        r.rows_vm,
        r.heads,
        r.attn_vm,
        r.out_vm,
        r.partial,
    )
    blocks, block = rows_one.shape[0], rows_one.shape[1]
    size, tokens, half = count * block, blocks * block, blocks // 2
    near = lax.axis_index("seq") // 2 * half
    greet_group(count, ({"section": 1 - lax.axis_index("section")},))
    steps = gather_steps(count, rows_in, rows_one, *r.gather_sems)
    next(steps)
    clear_pads(attn_vm, out_vm)
    loads = load_weights(1, attn, twin, out, attn_vm, out_vm, r.load_done)
    wide_loads = [
        pltpu.make_async_copy(gate_up.at[1], wide_vm, load_done.at[0]),
        pltpu.make_async_copy(down.at[1], down_vm, load_done.at[1]),
        pltpu.make_async_copy(grads_near, grads_vm.at[pl.ds(near, half)], load_done.at[2]),
    ]
    start_all(wide_loads)
    for event in until_done(steps):
        if event == "line":
            wait_all(loads)
        group = group_of(event)
        if group is not None:
            span = group_span(group, count, block)
            normed = group_rows(rows_one, group, count)
            project_heads(normed, attn_vm, heads, span, cosine, sine)
    grad_steps = line_steps(count, grads_side, grads_vm, *line_sems, offset=half - near)
    next(grad_steps)
    attention_rows(heads, log_total, start, size, tokens)

    def project_out(group):
        mixed = heads[3, group_span(group, count, block)]
        keep_group(partial, group, product(mixed, out_vm[...]), count)

    def deliver(total):
        value = between[...].astype(jnp.float32) + total
        hidden[...] = value
        normed_own[...] = normalise(value, gain_of(attn_vm, 1)).astype(jnp.bfloat16)

    run_with(
        scatter_steps(count, partial, deliver, *r.scatter_refs, compute=project_out),
        [functools.partial(advance, grad_steps, 1)] * 3,
    )
    for _ in steps:
        pass
    steps = gather_steps(count, normed_own, rows_two, *r.gather_sems)
    next(steps)
    for _ in grad_steps:
        pass
    wait_all(wide_loads)

    def through(group):
        span = group_span(group, count, block)
        pre = product(group_rows(rows_two, group, count), wide_vm[...])
        units[span] = hidden_units(pre)
        grad_act = back_product(group_rows(grads_vm, group, count), down_vm[...])
        store_gate_grads(pre_grads, span, grad_act, pre)
        keep_group(partial_back, group, back_product(pre_grads[span], wide_vm[...]), count)

    for event in until_done(steps):
        if event == "line":
            through(group_of(event))

    def project_down(group):
        value = product(units[group * size : (group + 1) * size], down_vm[...])
        partial[group * count : (group + 1) * count] = value.astype(jnp.bfloat16).reshape(
            count, block, -1
        )

    def deliver_two(total):
        mlp_grad_sent(
            total, hidden, grads_own, gain_mlp_two, branch_own, grad_hidden, mlp_two_sum
        )

    fillers = wide_grads(rows_two, pre_grads, units, grads_vm, wide_two, down_two)
    fillers += [functools.partial(project_down, group) for group in range(4)]
    run_with(
        scatter_steps(
            count, partial_back, deliver_two, *r.scatter_refs, compute=all_but_last(through)
        ),
        [functools.partial(run_all, fillers[n::4]) for n in range(4)],
    )
    for _ in steps:
        pass
    save = pltpu.make_async_copy(partial, ahead, load_done.at[3])
    save.start()
    copies = carried(
        (wide_two, down_two, attn_two, out_two), carried_to, carry_sent, carry_got
    )

    made = (wide_two, down_two, attn_two, out_two, wide_one, down_one)
    keeps = [
        pltpu.make_async_copy(begin, end, keep_done.at[n])
        for n, (begin, end) in enumerate(zip(made, grads_kept))
    ]

    def background():
        carry(copies[:2], 0, "start")
        start_all(keeps[:2])
        wide_loads[0] = pltpu.make_async_copy(gate_up.at[0], wide_vm, load_done.at[0])
        wide_loads[1] = pltpu.make_async_copy(down.at[0], down_vm, load_done.at[1])
        wide_loads[2] = pltpu.make_async_copy(wide_rows, rows_two, load_done.at[2])
        start_all(wide_loads)

    attn_back_body(
        count,
        None,
        r,
        (branch_own, grad_hidden, between, None, None, log_total, None, None, None)
        + (cosine, sine, start, gain_attn_two),
        (grad_between, attn_two_sum, attn_two, out_two),
        background,
        [],
    )
    carry(copies[2:], 0, "start")
    start_all(keeps[2:4])
    steps = gather_steps(count, grad_between, grads_vm, *r.gather_sems)
    next(steps)
    wait_all(wide_loads)

    def again(group):
        span = group_span(group, count, block)
        pre = product(group_rows(rows_two, group, count), wide_vm[...])
        pre_vm[span] = pre
        units[span] = hidden_units(pre)

    def through_one(group):
        span = group_span(group, count, block)
        grad_act = back_product(group_rows(grads_vm, group, count), down_vm[...])
        store_gate_grads(pre_grads, span, grad_act, pre_vm[span])
        keep_group(partial_back, group, back_product(pre_grads[span], wide_vm[...]), count)

    for number, event in enumerate(until_done(steps)):
        if number < 2:
            again(2 * number)
            again(2 * number + 1)
        if event == "line":
            through_one(group_of(event))

    def deliver_one(total):
        mlp_grad_sent(
            total, hidden_one, grad_between, gain_mlp_one, branch_out, grad_hidden_out, mlp_one_sum
        )

    run_with(
        scatter_steps(
            count, partial_back, deliver_one, *r.scatter_refs, compute=all_but_last(through_one)
        ),
        wide_grads(rows_two, pre_grads, units, grads_vm, wide_one, down_one),
    )
    for _ in steps:
        pass
    start_all(keeps[4:])
    carry(copies, 0, "wait")
    save.wait()
    wait_all(keeps)


def last_kernel(count, *refs):
    refs = iter(refs)

    def take(n):
        return [next(refs) for _ in range(n)]

    ins = take(13)
    ins[2] = ins[2].at[lax.axis_index("section"), 0]
    wide_one, down_one, attn_two, out_two, wide_two, down_two = take(6)
    wide_from_one, down_from_one, attn_from_one, out_from_one, ahead = take(5)
    gain_mlp_one, gain_attn_two, gain_mlp_two, between, grad_between, hidden = take(6)
    attn, out, gate, up, down, gains_out, rows_out, grads_out = take(8)
    final, grad_start = take(2)
    attn_grad, out_grad, gain_attn_one, gains = take(4)
    attn_own, out_own, wide_own, down_own, attn_in, out_in, wide_in, down_in = take(8)
    attn_slot, wide_slot = take(2)
    gain_in, gain_sum, gain_line, gain_part, gain_side, gain_core = take(6)
    load_done, cross_sent, cross_got, line_sent, line_got = take(5)
    side_sent, side_got, core_sent, core_got, local_done, small_sent, small_got = take(7)
    ahead_refs = take(13)
    r = attn_back_refs(take)
    seq, b, section = lax.axis_index("seq"), lax.axis_index("blk"), lax.axis_index("section")
    at_first = section == 0
    at_second = jnp.logical_not(at_first)
    core, side, other = {"seq": seq ^ 1}, {"seq": seq ^ 2}, {"section": 1 - section}
    greet((other, core, side) + tuple({"blk": lax.rem(b + k, count)} for k in range(1, count)))
    rows, lanes = attn.shape[2], gate.shape[1] // (4 * count)
    turns = tuple(range(count // 2, 0, -1)) + tuple(range(count // 2 + 1, count)) + (0,)
    f32, low = jnp.float32, jnp.bfloat16

    def piece_rows(kind, j):
        if kind == 0:
            return (slice(None), pl.ds(pl.multiple_of(j * rows, rows), rows))
        return (pl.ds(pl.multiple_of(j * rows, rows), rows),)

    pairs = {
        0: (attn_own, attn_in, attn_grad),
        1: (wide_own, wide_in, wide_one),
        2: (out_own, out_in, out_grad),
        3: (down_own, down_in, down_one),
    }
    sources = {
        0: (attn_grad, attn_two, attn_from_one),
        1: (wide_one, wide_two, wide_from_one),
        2: (out_grad, out_two, out_from_one),
        3: (down_one, down_two, down_from_one),
    }

    def load(kind):
        one, two, from_one = sources[kind]
        own, held, _ = pairs[kind]

        @pl.when(at_first)
        def _():
            pltpu.make_async_copy(one, own, load_done.at[kind, 0]).start()

        @pl.when(at_second)
        def _():
            pltpu.make_async_copy(two, own, load_done.at[kind, 0]).start()
            pltpu.make_async_copy(from_one, held, load_done.at[kind, 1]).start()

    def loaded(kind):
        own, held, _ = pairs[kind]
        pltpu.make_async_copy(own, own, load_done.at[kind, 0]).wait()
        pl.when(at_second)(pltpu.make_async_copy(held, held, load_done.at[kind, 1]).wait)

    def cross(kind, k):
        _, held, begin = pairs[kind]
        index = piece_rows(kind, lax.rem(b + k, count)) if kind < 2 else (slice(None),)
        return remote(
            begin.at[index], held.at[index], cross_sent.at[kind, k], cross_got.at[kind, k], other
        )

    def add_up(kind, k):
        own, held, _ = pairs[kind]
        pl.when(at_first)(cross(kind, k).wait_recv)
        index = piece_rows(kind, lax.rem(b + k, count)) if kind < 2 else (slice(None),)
        held[index] = (own[index].astype(f32) + held[index].astype(f32)).astype(low)

    def along_line(kind, k):
        j = lax.rem(b + k, count)
        slot = (attn_slot if kind == 0 else wide_slot).at[k]
        source = pairs[kind][1].at[piece_rows(kind, j)]
        return remote(source, slot, line_sent.at[kind, k], line_got.at[kind, k], {"blk": j})

    def places(kind, k, of_seq):
        if kind == 2:
            size = out_in.shape[0]
            return [out.at[pl.ds(pl.multiple_of(of_seq * size, size), size)]]
        if kind == 3:
            size = down_in.shape[0]
            return [down.at[pl.ds(pl.multiple_of(of_seq * size, size), size)]]
        head = lax.rem(b + count - k, count) * 4 + of_seq
        if kind == 0:
            return [attn.at[head]]
        column = pl.ds(pl.multiple_of(head * lanes, lanes), lanes)
        return [gate.at[:, column], up.at[:, column]]

    def numbered(kind, k, of_seq):
        base = {0: k, 1: count + 2 * k, 2: 3 * count, 3: 3 * count + 1}[kind]
        return [(base + n, spot) for n, spot in enumerate(places(kind, k, of_seq))]

    def made(kind, k):
        if kind > 1:
            return [pairs[kind][1].at[:]]
        if kind == 0:
            return [attn_in.at[piece_rows(0, b)] if k == 0 else attn_slot.at[k]]
        whole = (lambda cut: wide_in.at[piece_rows(1, b) + (cut,)]) if k == 0 else (
            lambda cut: wide_slot.at[k, :, cut]
        )
        return [whole(pl.ds(0, lanes)), whole(pl.ds(lanes, lanes))]

    def sends(kind, k):
        found = []
        for (n, spot), begin in zip(numbered(kind, k, seq), made(kind, k)):
            found.append(
                (
                    remote(begin, spot, side_sent.at[n], side_got.at[n], side),
                    remote(begin, spot, core_sent.at[0, n], core_got.at[0, n], core),
                    pltpu.make_async_copy(begin, spot, local_done.at[n]),
                )
            )
        return found

    def publish(kind, k):
        for copies in sends(kind, k):
            for copy in copies:
                copy.start()

    def passes(kind, k):
        return [
            remote(spot, spot, core_sent.at[1, n], core_got.at[1, n], core)
            for n, spot in numbered(kind, k, seq ^ 2)
        ]

    def from_line(kind, k):
        along_line(kind, k).wait_recv()
        publish(kind, k)

    def from_side(kind, k):
        for n, spot in numbered(kind, k, seq ^ 2):
            settled(spot, side_got.at[n], True)
        for copy in passes(kind, k):
            copy.start()

    def small(n, source, slot, device):
        return remote(source, slot, small_sent.at[n], small_got.at[n], device)

    swap_rest = small(4 + count, between, rows_out.at[section], other)
    swap_final = small(4 + count, final, rows_out.at[section], other)
    swap_between = small(0, grad_between, grads_out.at[section], other)
    swap_start = small(0, grad_start, grads_out.at[section], other)
    pl.when(at_second)(swap_rest.start)
    pl.when(at_first)(swap_between.start)
    wide_turns = [(1, k) for k in turns]
    crossings = [(3, 0)] + wide_turns + [(0, k) for k in turns] + [(2, 0)]

    def begin_cross(those):
        for kind, k in those:
            pl.when(at_second)(cross(kind, k).start)

    def background():
        begin_cross(crossings[: count + 1])
        load(3)
        load(1)

    def deliver(total):
        final[...] = (hidden[...] + total).astype(low)
        pl.when(at_first)(swap_final.start)
        rows_out[section] = jnp.where(at_first, between[...], final[...])

    def later():
        load(0)
        load(2)
        begin_cross(crossings[count + 1 :])

    def share(n):
        if n == 0:
            loaded(1)
        add_up(1, turns[n])
        along_line(1, turns[n]).start()

    def gathered():
        loaded(3)
        add_up(3, 0)
        publish(3, 0)

    def spare():
        later()
        share(0)

    def early():
        add_up(1, 0)
        publish(1, 0)

    ahead_steps = line_first_steps(count, ahead, deliver, *ahead_refs)
    attn_back_body(
        count,
        0,
        r,
        ins,
        (grad_start, gain_attn_one, attn_grad, out_grad),
        background,
        [functools.partial(share, 1), functools.partial(share, 2), early],
        gathered,
        spare,
    )
    pl.when(at_second)(swap_start.start)
    grads_out[section] = jnp.where(at_first, grad_start[...], grad_between[...])
    gains[0, 0:4] = gain_attn_one[0:4]
    gains[0, 4:8] = gain_mlp_one[4:8]
    gains[1, 0:4] = gain_attn_two[0:4]
    gains[1, 4:8] = gain_mlp_two[4:8]
    gain_cross = small(1, gains.at[1 - section], gain_in.at[:], other)
    gain_cross.start()

    def gain_piece(j):
        return gain_sum.at[:, pl.ds(pl.multiple_of(j * rows, rows), rows)]

    def gain_send(k):
        j = lax.rem(b + k, count)
        return small(3 + k, gain_piece(j), gain_line.at[k], {"blk": j})

    loaded(0)
    for k in turns[:-1]:
        add_up(0, k)
        along_line(0, k).start()
    from_line(1, turns[0])
    add_up(0, 0)
    publish(0, 0)
    from_line(1, turns[1])
    from_side(1, 0)
    loaded(2)
    add_up(2, 0)
    publish(2, 0)
    from_line(1, turns[2])
    next(ahead_steps)
    from_side(3, 0)
    from_side(1, turns[0])
    for k in turns[:-1]:
        from_line(0, k)
    from_side(0, 0)
    from_side(1, turns[1])
    gain_cross.wait_recv()
    gain_sum[...] = gains[section] + gain_in[...]
    for k in range(1, count):
        gain_send(k).start()
    advance(ahead_steps, 2)
    from_side(2, 0)
    from_side(1, turns[2])
    for k in range(1, count):
        gain_send(k).wait_recv()
    gain_part[...] = gain_sum[:, pl.ds(pl.multiple_of(b * rows, rows), rows)]
    for k in range(1, count):
        gain_part[...] += gain_line[k]
    gain_to_side = small(2, gain_part.at[:], gain_side.at[:], side)
    gain_to_side.start()
    advance(ahead_steps, 4)
    gain_to_side.wait_recv()
    gain_side[...] += gain_part[...]
    gain_to_core = small(3, gain_side.at[:], gain_core.at[:], core)
    gain_to_core.start()
    for _ in ahead_steps:
        pass
    for k in turns[:-1]:
        from_side(0, k)
    gain_to_core.wait_recv()
    gains_out[...] = gain_side[...] + gain_core[...]
    every = [(0, k) for k in range(count)] + [(1, k) for k in range(count)] + [(2, 0), (3, 0)]
    for kind, k in every:
        pl.when(at_second)(cross(kind, k).wait_send)
        if kind < 2 and k:
            along_line(kind, k).wait_send()
        for to_side, to_core, local in sends(kind, k):
            to_side.wait_send()
            to_core.wait_send()
            local.wait()
        for copy in passes(kind, k):
            copy.wait_send()
        for half, of_seq in ((0, seq ^ 1), (1, seq ^ 3)):
            for n, spot in numbered(kind, k, of_seq):
                settled(spot, core_got.at[half, n], True)
    swap_between.wait()
    swap_rest.wait()
    gain_cross.wait_send()
    for k in range(1, count):
        gain_send(k).wait_send()
    gain_to_side.wait_send()
    gain_to_core.wait_send()


def widen_kernel(pieces, *refs):
    attn, out, gate, up, down, rows_in, grads_in, gains = refs[:8]
    query, key, value, out_f, gate_f, up_f, down_f = refs[8:15]
    rows_out, grads_out, gain_attn, gain_mlp = refs[15:]
    f32 = jnp.float32
    out_f[...] = out[...].astype(f32)
    gate_f[...] = gate[...].astype(f32)
    up_f[...] = up[...].astype(f32)
    down_f[...] = down[...].astype(f32)

    @pl.when(pl.program_id(0) == 0)
    def _():
        rows_out[...] = rows_in[...]
        grads_out[...] = grads_in[...]
        gain_attn[...] = gains[0:1]
        gain_mlp[...] = gains[4:5]

    @pl.when(pl.program_id(0) < pieces)
    def _():
        parts, _, lanes = attn.shape
        copies = HEADS // KV_HEADS

        def heads(n):
            return attn[:, n * HEAD_DIM : (n + 1) * HEAD_DIM].astype(f32)

        query[...] = heads(0).reshape(parts * HEAD_DIM, lanes).T
        for n, place in ((1, key), (2, value)):
            total = heads(n).reshape(parts // copies, copies, HEAD_DIM, lanes).sum(1)
            place[...] = total.reshape(parts // copies * HEAD_DIM, lanes).T


def widen(attn, out, gate, up, down, rows_out, grads_out, gains):
    f32 = jnp.float32
    parts, heads, rows = attn.shape
    lanes = 128
    pieces = rows // lanes
    steps = 8
    width = parts * HEAD_DIM
    narrow = width * KV_HEADS // HEADS

    def rows_of(array):
        return pl.BlockSpec((array.shape[0] // steps, array.shape[1]), lambda i: (i, 0))

    def turned(columns):
        return pl.BlockSpec((lanes, columns), lambda i: (jnp.minimum(i, pieces - 1), 0))

    def whole(shape):
        return pl.BlockSpec(shape, lambda i: (0,) * len(shape))

    flat = [out, gate, up, down]
    swaps = [whole(rows_out.shape), whole(grads_out.shape)]
    gain = jax.ShapeDtypeStruct((1, rows), f32)
    taken = pl.BlockSpec((parts, heads, lanes), lambda i: (0, 0, jnp.minimum(i, pieces - 1)))
    shapes = [(rows, width), (rows, narrow), (rows, narrow)] + [array.shape for array in flat]
    return pl.pallas_call(
        functools.partial(widen_kernel, pieces),
        grid=(steps,),
        out_shape=[jax.ShapeDtypeStruct(shape, f32) for shape in shapes]
        + [jax.ShapeDtypeStruct(array.shape, array.dtype) for array in (rows_out, grads_out)]
        + [gain, gain],
        in_specs=[taken] + [rows_of(array) for array in flat] + swaps + [whole(gains.shape)],
        out_specs=[turned(width), turned(narrow), turned(narrow)]
        + [rows_of(array) for array in flat]
        + swaps
        + [whole((1, rows)), whole((1, rows))],
        compiler_params=pltpu.CompilerParams(vmem_limit_bytes=60 * 2**20),
        name="widen_gradients",
    )(attn, out, gate, up, down, rows_out, grads_out, gains)


def last_layer(count, operands, like, back_scratch):
    attn, out, wide, down, block, width, gain_rows = like
    low, f32 = jnp.bfloat16, jnp.float32
    seq_count = lax.axis_size("seq")
    rows = wide[0] // count
    lanes = wide[1] // 2
    parts = seq_count * count
    dma = pltpu.SemaphoreType.DMA
    vmem = pltpu.VMEM
    sends = 3 * count + 2
    heads = attn[0]
    small = (gain_rows, rows)

    def slots(*places):
        return vmem(places + (block, width), low)

    outputs = [
        ((parts, heads, rows), low, False),
        ((out[0] * seq_count, out[1]), low, False),
        ((rows, lanes * parts), low, False),
        ((rows, lanes * parts), low, False),
        ((down[0] * seq_count, down[1]), low, False),
        (small, f32, True),
        ((2, block, width), low, True),
        ((2, block, width), low, True),
    ]
    scratch = (
        [vmem((block, width), low), vmem((block, width), low)]
        + [vmem(attn, low), vmem(out, low), vmem((gain_rows, width), f32)]
        + [vmem((2, gain_rows, width), f32)]
        + [vmem(shape, low) for shape in (attn, out, wide, down)] * 2
        + [vmem((count, heads, rows), low), vmem((count, rows, 2 * lanes), low)]
        + [vmem((gain_rows, width), f32)] * 2
        + [vmem((count,) + small, f32)]
        + [vmem(small, f32)] * 3
        + [dma((4, 2)), dma((4, count)), dma((4, count)), dma((2, count)), dma((2, count))]
        + [dma((sends,)), dma((sends,)), dma((2, sends)), dma((2, sends)), dma((sends,))]
        + [dma((5 + count,)), dma((5 + count,))]
        + [slots(2, count), slots(2, count), slots(2, 2, count), slots(2, count), slots(1)]
        + [vmem((block, width), f32)]
        + [dma((2, count)), dma((2, count)), dma((2, count)), dma((2, count))]
        + [dma((2, 2, count)), dma, dma]
        + back_scratch
    )
    attn, out, gate, up, down, gains, rows_out, grads_out = call_kernel(
        functools.partial(last_kernel, count), "last_layer_back", 3, operands, outputs, scratch
    )
    return widen(attn, out, gate, up, down, rows_out, grads_out, gains)


def call_kernel(kernel, name, number, operands, outputs, scratch):
    in_vmem = pl.BlockSpec(memory_space=pltpu.VMEM)
    anywhere = pl.BlockSpec(memory_space=pl.ANY)
    places = {True: in_vmem, False: anywhere, None: pl.BlockSpec(memory_space=pltpu.SMEM)}
    return pl.pallas_call(
        kernel,
        out_shape=[jax.ShapeDtypeStruct(shape, dtype) for shape, dtype, _ in outputs],
        in_specs=[places[near] for _, near in operands],
        out_specs=[in_vmem if near else anywhere for _, _, near in outputs],
        scratch_shapes=scratch,
        compiler_params=pltpu.CompilerParams(
            collective_id=number, has_side_effects=True, vmem_limit_bytes=56 * 2**20
        ),
        name=name,
    )(*[array for array, _ in operands])


def head_shards(inputs, cotangent, doc_lengths, *params):
    seq_count, count = lax.axis_size("seq"), lax.axis_size("blk")
    low, f32 = jnp.bfloat16, jnp.float32
    vmem, dma = pltpu.VMEM, pltpu.SemaphoreType.DMA
    block, width = inputs.shape[2], inputs.shape[3]
    blocks = seq_count * count
    tokens = blocks * block
    local = tuple(weight[0] for weight in params)
    piece_shape = (count, 2 * HEAD_DIM + 16, local[1].shape[0])
    w_output, w_gate, w_up, w_down = local[4], local[6], local[7], local[8]
    rows = w_gate.shape[0]
    lanes = w_gate.shape[1] // blocks
    out_rows, down_rows = w_output.shape[0] // seq_count, w_down.shape[0] // seq_count
    lane = jnp.arange(PAD) % (HEAD_DIM // 2)
    frequency = (THETA ** (-2.0 * lane.astype(f32) / HEAD_DIM))[None]

    def all_blocks():
        return vmem((blocks, block, width), low)

    def scatter():
        return scatter_scratch(count, block, width)

    half_blocks = vmem((blocks // 2, block, width), low)
    half = ((blocks // 2, block, width), low, False)
    own_low, own_wide = ((block, width), low, True), ((block, width), f32, True)
    every = ((blocks, block, width), low, False)
    gain_rows, one_row = ((8, width), f32, True), ((1, width), f32, True)
    weights_vm = [vmem((3 * PAD + 16, width), low), vmem((PAD, width), low)]
    wide_vm, down_vm = vmem((width, 2 * lanes), low), vmem((down_rows, width), low)
    (
        attn,
        twin,
        gate_up,
        out,
        down,
        rows_one,
        wide_rows_one,
        grads_near,
        grads_side,
        cosine,
        sine,
        start,
        gain_attn_first,
        gain_mlp_first,
        gain_attn_second,
        gain_mlp_second,
        hidden_one,
        between,
        normed,
        heads_one,
        total_one,
    ) = call_kernel(
        functools.partial(first_layer_kernel, count),
        "first_layer",
        2,
        [(array, False) for array in local[1:4] + (w_gate, w_up, w_output, w_down)]
        + [(local[0][None], True), (local[5][None], True)]
        + [(inputs, True), (cotangent, True), (doc_lengths, None), (frequency, True)],
        [
            ((2, piece_shape[1], width), low, False),
            ((2, HEAD_DIM, width), low, False),
            ((2, width, 2 * lanes), low, False),
            ((2, out_rows, width), low, False),
            ((2, down_rows, width), low, False),
            every,
            every,
            half,
            ((block, width), low, False),
            ((tokens, PAD), f32, True),
            ((tokens, PAD), f32, True),
            ((tokens, 1), jnp.int32, True),
            one_row,
            one_row,
            one_row,
            one_row,
            own_wide,
            own_low,
            own_low,
            ((4, tokens, PAD), low, True),
            ((tokens, 1), f32, True),
        ],
        [all_blocks() for _ in range(5)]
        + [half_blocks]
        + weights_vm
        + [wide_vm, down_vm, vmem((tokens, lanes), low), vmem((block, width), low)]
        + [vmem((16, width), low), vmem(piece_shape, low)]
        + [vmem(local[1].shape, low), vmem(local[2].shape, low)]
        + [vmem(local[1].shape[::-1], low), vmem(local[2].shape[::-1], low), dma((2,))]
        + [dma((6,)), dma((3,)), dma, dma]
        + [dma((3, count)), dma((3, count)), dma((5, count)), dma((5, count)), dma((5,))]
        + gather_semaphores(count) * 2
        + line_semaphores(count)
        + [dma, dma]
        + scatter()
        + scatter(),
    )
    tables = [(cosine, True), (sine, True), (start, True)]
    back_scratch = (
        [all_blocks(), all_blocks(), vmem((4, tokens, PAD), low)]
        + weights_vm
        + [vmem((tokens, PAD), low), vmem((tokens, tokens), f32)]
        + [vmem((tokens, PAD), f32), vmem((tokens, PAD), f32), vmem((tokens, 3 * PAD), low)]
        + [all_blocks(), dma((7,))]
        + gather_semaphores(count)
        + scatter()
    )
    attn_shape, out_shape = (3 * HEAD_DIM, width), (HEAD_DIM, width)
    wide_shape, down_shape = (width, 2 * lanes), (down_rows, width)
    kept_shapes = [wide_shape, down_shape, attn_shape, out_shape, wide_shape, down_shape]
    (
        hidden_two,
        ahead,
        grad_between,
        branch,
        grad_hidden,
        gain_mlp_two,
        gain_attn_two,
        gain_mlp_one,
        wide_two,
        down_two,
        attn_two,
        out_two,
        wide_one,
        down_one,
        wide_from_one,
        down_from_one,
        attn_from_one,
        out_from_one,
    ) = call_kernel(
        functools.partial(middle_kernel, count),
        "second_layer",
        4,
        [(normed, True), (between, True), (grads_side, True)]
        + tables
        + [(attn, False), (twin, False), (out, False)]
        + [(grads_near, False), (gate_up, False), (down, False)]
        + [(cotangent, True), (hidden_one, True), (wide_rows_one, False)]
        + [(gain_mlp_second, True), (gain_attn_second, True), (gain_mlp_first, True)],
        [own_wide, every, own_low, own_low, own_wide, gain_rows, gain_rows, gain_rows]
        + [(shape, low, False) for shape in kept_shapes]
        + [(shape, low, False) for shape in (wide_shape, down_shape, attn_shape, out_shape)],
        [all_blocks(), all_blocks(), all_blocks(), wide_vm, down_vm]
        + [vmem((tokens, 1), f32), vmem((tokens, lanes), low), vmem((tokens, 2 * lanes), f32)]
        + [vmem((tokens, 2 * lanes), low), vmem((block, width), low), vmem((block, width), low)]
        + [vmem((block, width), f32), dma((4,)), dma((4,)), dma((4,)), dma((6,))]
        + [vmem(shape, low) for shape in kept_shapes]
        + line_semaphores(count)
        + back_scratch,
    )
    back_operands = (
        [(branch, True), (grad_hidden, True), (inputs, True)]
        + [(rows_one, False), (heads_one, False), (total_one, True)]
        + [(attn, False), (twin, False), (out, False)]
        + tables
        + [(gain_attn_first, True)]
    )
    query, key, value, out, gate, up, down, *swapped, gain_attn, gain_mlp = last_layer(
        count,
        back_operands
        + [(wide_one, False), (down_one, False), (attn_two, False), (out_two, False)]
        + [(wide_two, False), (down_two, False), (wide_from_one, False), (down_from_one, False)]
        + [(attn_from_one, False), (out_from_one, False), (ahead, False)]
        + [(gain_mlp_one, True), (gain_attn_two, True), (gain_mlp_two, True)]
        + [(between, True), (grad_between, True), (hidden_two, True)],
        (
            attn_shape,
            out_shape,
            wide_shape,
            down_shape,
            block,
            width,
            gain_rows[0][0],
        ),
        back_scratch,
    )
    return (
        swapped[0][None, :, None],
        swapped[1][None, :, None],
        gain_attn,
        query[None],
        key[None],
        value[None],
        out[None],
        gain_mlp,
        gate[None],
        up[None],
        down[None],
    )

def solution(mesh):
    placed = (
        P(None, None, ("seq", "blk"), None),
        P(None, None, ("seq", "blk"), None),
        P(),
        P("section", "blk"),
        P("section", "blk", None),
        P("section", "blk", None),
        P("section", "blk", None),
        P("section", "blk", None),
        P("section", "blk"),
        P("section", "blk", None),
        P("section", "blk", None),
        P("section", "blk", None),
    )
    one_head_each = mesh.shape["seq"] == 4 and mesh.shape["blk"] == HEADS // 4
    return jax.shard_map(
        head_shards if one_head_each else shards,
        mesh=mesh,
        in_specs=placed,
        out_specs=(
            P("section", None, None, ("seq", "blk"), None),
            P("section", None, None, ("seq", "blk"), None),
            P("section", "blk"),
            P("section", "blk", None),
            P("section", "blk", None),
            P("section", "blk", None),
            P("section", "blk", None),
            P("section", "blk"),
            P("section", "blk", None),
            P("section", "blk", None),
            P("section", "blk", None),
        ),
        check_vma=False,
    )
```

```python
import functools

import jax
import jax.numpy as jnp
from jax import lax
from jax.experimental import pallas as pl
from jax.experimental.pallas import tpu as pltpu
from jax.sharding import PartitionSpec as P

HEADS = 16
KV_HEADS = 8
HEAD_DIM = 96


EPS = 1e-05
THETA = 100000.0
MASKED = -1e30


def passed_along(value, axis, steps):
    count = lax.axis_size(axis)
    first, last = (max(0, -steps), min(count, count - steps))
    return lax.ppermute(value, axis, [(source, source + steps) for source in range(first, last)])


def shortened(value):
    return jax.tree.map(lambda a: a.astype(jnp.bfloat16) if a.dtype == jnp.float32 else a, value)


def product(left_side, right_side):
    return jnp.dot(left_side, right_side, preferred_element_type=jnp.float32)


def back_product(left_side, right_side):
    return lax.dot_general(
        left_side, right_side, (((1,), (1,)), ((), ())), preferred_element_type=jnp.float32
    )


def doc_info(lengths, token_index):
    doc_ends = jnp.cumsum(lengths, axis=-1)
    passed = (doc_ends[..., None, :] <= token_index[..., None]).astype(jnp.int32)
    segment = jnp.sum(passed, axis=-1)
    offset = jnp.sum(passed * lengths[..., None, :], axis=-1)
    return (segment, token_index - offset)


def rotate(field_in, position, turn_sign):
    half_dim = field_in.shape[-1] // 2
    frequency = THETA ** (-2.0 * jnp.arange(half_dim, dtype=jnp.float32) / field_in.shape[-1])
    angles = position.astype(jnp.float32)[:, None] * frequency
    cosine = jnp.cos(angles)[:, None, :]
    sine_part = turn_sign * jnp.sin(angles)[:, None, :]
    first_half = field_in[..., :half_dim]
    second_half = field_in[..., half_dim:]
    return jnp.concatenate(
        [
            first_half * cosine - second_half * sine_part,
            second_half * cosine + first_half * sine_part,
        ],
        axis=-1,
    )


def rms_forward(field_in, gain_row):
    inv_root = lax.rsqrt(jnp.mean(field_in * field_in, axis=-1, keepdims=True) + EPS)
    return (field_in * inv_root * gain_row, inv_root)


def rms_backward(field_in, gain_row, inv_root, grad_normed):
    scaled = gain_row * grad_normed
    grad_field = inv_root * scaled - field_in * inv_root**3 * jnp.mean(
        scaled * field_in, axis=-1, keepdims=True
    )
    return (grad_field, grad_normed * field_in * inv_root)


def token_place(block_id, row_ids, per_device, blk_count):
    return (row_ids // per_device * blk_count + block_id) * per_device + row_ids % per_device


def masks_for(lengths, blk_index, per_device, blk_count, seq_count):
    block_tokens = seq_count * per_device
    row_ids = jnp.arange(block_tokens, dtype=jnp.int32)
    query_index = token_place(blk_index, row_ids, per_device, blk_count)
    all_ids = jnp.arange(blk_count * block_tokens, dtype=jnp.int32)
    key_index = token_place(all_ids // block_tokens, all_ids % block_tokens, per_device, blk_count)
    query_seg, _ = doc_info(lengths, query_index)
    key_seg, _ = doc_info(lengths, key_index)
    return (query_index, key_index, query_seg, key_seg)


def head_scores(queries, key_rows, allowed, kv_local):
    grouped = queries.reshape(queries.shape[0], kv_local, -1, HEAD_DIM)
    key_heads = key_rows.reshape(key_rows.shape[0], kv_local, HEAD_DIM)
    scores = jnp.einsum(
        "rkgd,lkd->kgrl", grouped, key_heads, preferred_element_type=jnp.float32
    ) * HEAD_DIM ** (-0.5)
    return (jnp.where(allowed, scores, MASKED), grouped, key_heads)


def attend_forward(operands, query_index, key_index, kv_local):
    queries, key_rows, value_rows, query_seg, key_seg = operands
    allowed = (query_seg[:, None] == key_seg[None, :]) & (
        key_index[None, :] <= query_index[:, None]
    )
    scores, grouped, key_heads = head_scores(queries, key_rows, allowed, kv_local)
    row_top = jnp.max(scores, axis=-1, keepdims=True)
    log_total = row_top + jnp.log(jnp.sum(jnp.exp(scores - row_top), axis=-1, keepdims=True))
    weights_low = jnp.exp(scores - log_total).astype(jnp.bfloat16)
    value_heads = value_rows.reshape(value_rows.shape[0], kv_local, HEAD_DIM)
    mixed_heads = jnp.einsum(
        "kgrl,lkd->rkgd", weights_low, value_heads, preferred_element_type=jnp.float32
    )
    return (mixed_heads.reshape(queries.shape).astype(jnp.bfloat16), log_total)


def attend_backward(operands, query_index, key_index, kv_local):
    queries, key_rows, value_rows, grad_mixed, log_total, query_seg, key_seg = operands
    allowed = (query_seg[:, None] == key_seg[None, :]) & (
        key_index[None, :] <= query_index[:, None]
    )
    scores, grouped, key_heads = head_scores(queries, key_rows, allowed, kv_local)
    attn_probs = jnp.exp(scores - log_total)
    value_heads = value_rows.reshape(value_rows.shape[0], kv_local, HEAD_DIM)
    grad_heads = grad_mixed.reshape(grouped.shape)
    grad_values = jnp.einsum(
        "kgrl,rkgd->lkd",
        attn_probs.astype(jnp.bfloat16),
        grad_heads,
        preferred_element_type=jnp.float32,
    )
    grad_probs = jnp.einsum(
        "rkgd,lkd->kgrl", grad_heads, value_heads, preferred_element_type=jnp.float32
    )
    centre = jnp.sum(attn_probs * grad_probs, axis=-1, keepdims=True)
    grad_scores = (attn_probs * (grad_probs - centre)).astype(jnp.bfloat16)
    grad_queries = jnp.einsum(
        "kgrl,lkd->rkgd", grad_scores, key_heads, preferred_element_type=jnp.float32
    ) * HEAD_DIM ** (-0.5)
    grad_keys = jnp.einsum(
        "kgrl,rkgd->lkd", grad_scores, grouped, preferred_element_type=jnp.float32
    ) * HEAD_DIM ** (-0.5)
    return (
        grad_queries.reshape(queries.shape).astype(jnp.bfloat16),
        grad_keys.reshape(key_rows.shape),
        grad_values.reshape(value_rows.shape),
    )


def layer_forward(section_in, lengths, weights, placing):
    shard_id, blk_index, seq_count, blk_count = placing
    gain_attn, w_query, w_key, w_value, w_output, gain_mlp, w_gate, w_up, w_down = weights
    seqs_here, per_device, width = section_in.shape
    token_rows = seqs_here * per_device
    copies = max(1, seq_count // KV_HEADS)
    kv_local = KV_HEADS * copies // seq_count
    token_index = shard_id * per_device + jnp.arange(per_device, dtype=jnp.int32)
    _, position = doc_info(lengths, token_index)
    position = position.reshape(token_rows)
    flat_in = section_in.reshape(token_rows, width)
    normed, inv_first = rms_forward(flat_in, gain_attn.astype(jnp.float32))
    normed_low = normed.astype(jnp.bfloat16)
    query_pre = product(normed_low, w_query).reshape(token_rows, HEADS, HEAD_DIM)
    key_pre = product(normed_low, w_key).reshape(token_rows, KV_HEADS, HEAD_DIM)
    value_pre = product(normed_low, w_value).reshape(token_rows, KV_HEADS, HEAD_DIM)
    query_rot = (
        rotate(query_pre, position, 1.0).astype(jnp.bfloat16).reshape(seqs_here, per_device, width)
    )
    key_rot = rotate(key_pre, position, 1.0).astype(jnp.bfloat16)
    spread_shape = (token_rows, KV_HEADS, copies, HEAD_DIM)
    key_rep = jnp.broadcast_to(key_rot[:, :, None, :], spread_shape).reshape(
        seqs_here, per_device, -1
    )
    value_rep = jnp.broadcast_to(
        value_pre.astype(jnp.bfloat16)[:, :, None, :], spread_shape
    ).reshape(seqs_here, per_device, -1)
    heads_query, heads_key, heads_value = (
        lax.all_to_all(query_rot, "seq", split_axis=2, concat_axis=1, tiled=True),
        lax.all_to_all(key_rep, "seq", split_axis=2, concat_axis=1, tiled=True),
        lax.all_to_all(value_rep, "seq", split_axis=2, concat_axis=1, tiled=True),
    )
    keys_all, values_all = (
        lax.all_gather(heads_key, "blk", axis=1, tiled=True),
        lax.all_gather(heads_value, "blk", axis=1, tiled=True),
    )
    query_index, key_index, query_seg, key_seg = masks_for(
        lengths, blk_index, per_device, blk_count, seq_count
    )
    heads_mixed, log_total = lax.map(
        lambda operands: attend_forward(operands, query_index, key_index, kv_local),
        (heads_query, keys_all, values_all, query_seg, key_seg),
    )
    token_mixed = lax.all_to_all(
        heads_mixed, "seq", split_axis=1, concat_axis=2, tiled=True
    ).reshape(token_rows, width)
    hidden = flat_in + product(token_mixed, w_output)
    normed_mlp, inv_second = rms_forward(hidden, gain_mlp.astype(jnp.float32))
    normed_mlp_low = normed_mlp.astype(jnp.bfloat16)
    gate_pre = product(normed_mlp_low, w_gate)
    up_pre = product(normed_mlp_low, w_up)
    act_low = (jax.nn.silu(gate_pre) * up_pre).astype(jnp.bfloat16)
    result = hidden + product(act_low, w_down)
    saved_state = (
        flat_in,
        normed_low,
        inv_first,
        position,
        heads_query,
        keys_all,
        values_all,
        log_total,
        token_mixed,
        hidden,
        inv_second,
        normed_mlp_low,
        gate_pre,
        up_pre,
        act_low,
        lengths,
    )
    return (result.reshape(section_in.shape), saved_state)


def layer_backward(upstream, saved_state, weights, placing):
    shard_id, blk_index, seq_count, blk_count = placing
    gain_attn, w_query, w_key, w_value, w_output, gain_mlp, w_gate, w_up, w_down = weights
    (
        flat_in,
        normed_low,
        inv_first,
        position,
        heads_query,
        keys_all,
        values_all,
        log_total,
        token_mixed,
        hidden,
        inv_second,
        normed_mlp_low,
        gate_pre,
        up_pre,
        act_low,
        lengths,
    ) = saved_state
    seqs_here, per_device, width = upstream.shape
    token_rows = seqs_here * per_device
    copies = max(1, seq_count // KV_HEADS)
    kv_local = KV_HEADS * copies // seq_count
    grad_rows = upstream.reshape(token_rows, width)
    grad_out_low = grad_rows.astype(jnp.bfloat16)
    grad_act = back_product(grad_out_low, w_down)
    gate_sigmoid = jax.nn.sigmoid(gate_pre)
    grad_gate_low = (
        grad_act * up_pre * gate_sigmoid * (1.0 + gate_pre * (1.0 - gate_sigmoid))
    ).astype(jnp.bfloat16)
    grad_up_low = (grad_act * jax.nn.silu(gate_pre)).astype(jnp.bfloat16)
    grad_normed_mlp = back_product(grad_gate_low, w_gate) + back_product(grad_up_low, w_up)
    grad_hidden_part, gain_mlp_terms = rms_backward(
        hidden, gain_mlp.astype(jnp.float32), inv_second, grad_normed_mlp
    )
    grad_hidden = grad_rows + grad_hidden_part
    grad_branch_low = grad_hidden.astype(jnp.bfloat16)
    grad_mixed_low = (
        back_product(grad_branch_low, w_output)
        .astype(jnp.bfloat16)
        .reshape(seqs_here, per_device, width)
    )
    heads_grad = lax.all_to_all(grad_mixed_low, "seq", split_axis=2, concat_axis=1, tiled=True)
    query_index, key_index, query_seg, key_seg = masks_for(
        lengths, blk_index, per_device, blk_count, seq_count
    )
    grad_heads_query, grad_keys_all, grad_values_all = lax.map(
        lambda operands: attend_backward(operands, query_index, key_index, kv_local),
        (heads_query, keys_all, values_all, heads_grad, log_total, query_seg, key_seg),
    )
    grad_key_own, grad_value_own = (
        lax.psum_scatter(
            grad_keys_all.astype(jnp.bfloat16), "blk", scatter_dimension=1, tiled=True
        ).astype(jnp.float32),
        lax.psum_scatter(
            grad_values_all.astype(jnp.bfloat16), "blk", scatter_dimension=1, tiled=True
        ).astype(jnp.float32),
    )
    token_query, token_key, token_value = (
        lax.all_to_all(grad_heads_query, "seq", split_axis=1, concat_axis=2, tiled=True),
        lax.all_to_all(
            grad_key_own.astype(jnp.bfloat16), "seq", split_axis=1, concat_axis=2, tiled=True
        ),
        lax.all_to_all(
            grad_value_own.astype(jnp.bfloat16), "seq", split_axis=1, concat_axis=2, tiled=True
        ),
    )
    grad_key_sum = jnp.sum(
        token_key.astype(jnp.float32).reshape(token_rows, KV_HEADS, copies, HEAD_DIM), axis=2
    )
    grad_value_sum = jnp.sum(
        token_value.astype(jnp.float32).reshape(token_rows, KV_HEADS, copies, HEAD_DIM), axis=2
    )
    grad_query_low = (
        rotate(token_query.astype(jnp.float32).reshape(token_rows, HEADS, HEAD_DIM), position, -1.0)
        .astype(jnp.bfloat16)
        .reshape(token_rows, width)
    )
    grad_key_low = (
        rotate(grad_key_sum, position, -1.0)
        .astype(jnp.bfloat16)
        .reshape(token_rows, KV_HEADS * HEAD_DIM)
    )
    grad_value_low = grad_value_sum.astype(jnp.bfloat16).reshape(token_rows, KV_HEADS * HEAD_DIM)
    grad_normed = (
        back_product(grad_query_low, w_query)
        + back_product(grad_key_low, w_key)
        + back_product(grad_value_low, w_value)
    )
    grad_in_part, gain_attn_terms = rms_backward(
        flat_in, gain_attn.astype(jnp.float32), inv_first, grad_normed
    )
    grad_input = (grad_hidden + grad_in_part).reshape(upstream.shape)
    weight_rows = (
        gain_attn_terms,
        normed_low,
        grad_query_low,
        grad_key_low,
        grad_value_low,
        token_mixed,
        grad_branch_low,
        gain_mlp_terms,
        normed_mlp_low,
        grad_gate_low,
        grad_up_low,
        act_low,
        grad_out_low,
    )
    return (grad_input, weight_rows)


def weight_term(inputs_low, outputs_low):
    if outputs_low is None:
        return jnp.sum(inputs_low, axis=0)
    return lax.dot_general(
        inputs_low, outputs_low, (((0,), (0,)), ((), ())), preferred_element_type=jnp.float32
    )


def shards(
    inputs,
    cotangent,
    doc_lengths,
    attention_gain,
    w_query,
    w_key,
    w_value,
    w_output,
    mlp_gain,
    w_gate,
    w_up,
    w_down,
):
    at_first = lax.axis_index("section") == 0
    seq_count = lax.axis_size("seq")
    blk_count = lax.axis_size("blk")
    blk_index = lax.axis_index("blk")
    shard_id = lax.axis_index("seq") * blk_count + blk_index
    placing = (shard_id, blk_index, seq_count, blk_count)
    micro_count = inputs.shape[0]
    local_shards = (
        attention_gain[0],
        w_query[0],
        w_key[0],
        w_value[0],
        w_output[0],
        mlp_gain[0],
        w_gate[0],
        w_up[0],
        w_down[0],
    )
    weights = (
        lax.all_gather(local_shards[0], "blk", axis=0, tiled=True),
        lax.all_gather(local_shards[1], "blk", axis=0, tiled=True),
        lax.all_gather(local_shards[2], "blk", axis=0, tiled=True),
        lax.all_gather(local_shards[3], "blk", axis=0, tiled=True),
        lax.all_gather(local_shards[4], "blk", axis=0, tiled=True),
        lax.all_gather(local_shards[5], "blk", axis=0, tiled=True),
        lax.all_gather(local_shards[6], "blk", axis=0, tiled=True),
        lax.all_gather(local_shards[7], "blk", axis=0, tiled=True),
        lax.all_gather(local_shards[8], "blk", axis=0, tiled=True),
    )
    received = jnp.zeros(inputs.shape[1:], jnp.bfloat16)
    saved_states = []
    section_outs = []
    for tick_index in range(micro_count + 1):
        fresh_input = inputs[min(tick_index, micro_count - 1)]
        section_in = jnp.where(at_first, fresh_input, received).astype(jnp.float32)
        lengths = jnp.where(
            at_first,
            doc_lengths[min(tick_index, micro_count - 1)],
            doc_lengths[max(tick_index - 1, 0)],
        )
        result, saved_state = layer_forward(section_in, lengths, weights, placing)
        result_low = result.astype(jnp.bfloat16)
        if tick_index < micro_count:
            received = passed_along(result_low, "section", 1)
        saved_states.append(saved_state)
        section_outs.append(result_low)
    weights = (
        lax.all_gather(local_shards[0], "blk", axis=0, tiled=True),
        lax.all_gather(local_shards[1], "blk", axis=0, tiled=True),
        lax.all_gather(local_shards[2], "blk", axis=0, tiled=True),
        lax.all_gather(local_shards[3], "blk", axis=0, tiled=True),
        lax.all_gather(local_shards[4], "blk", axis=0, tiled=True),
        lax.all_gather(local_shards[5], "blk", axis=0, tiled=True),
        lax.all_gather(local_shards[6], "blk", axis=0, tiled=True),
        lax.all_gather(local_shards[7], "blk", axis=0, tiled=True),
        lax.all_gather(local_shards[8], "blk", axis=0, tiled=True),
    )
    back_in = jnp.zeros(cotangent.shape[1:], jnp.bfloat16)
    grad_outs = []
    row_sets = []
    for tick_index in range(micro_count + 1):
        saved_state = jax.tree.map(
            lambda first_pick, second_pick: jnp.where(at_first, first_pick, second_pick),
            saved_states[max(tick_index - 1, 0)],
            saved_states[min(tick_index + 1, micro_count)],
        )
        upstream = jnp.where(at_first, back_in, cotangent[min(tick_index, micro_count - 1)]).astype(
            jnp.float32
        )
        grad_input, weight_rows = layer_backward(upstream, saved_state, weights, placing)
        grad_low = grad_input.astype(jnp.bfloat16)
        if tick_index < micro_count:
            back_in = passed_along(grad_low, "section", -1)
        grad_outs.append(grad_low)
        row_sets.append(weight_rows)
    activations = jnp.stack(
        [
            jnp.where(at_first, section_outs[index_m], section_outs[index_m + 1])
            for index_m in range(micro_count)
        ]
    )[None]
    input_grads = jnp.stack(
        [
            jnp.where(at_first, grad_outs[index_m + 1], grad_outs[index_m])
            for index_m in range(micro_count)
        ]
    )[None]
    picked = [
        jax.tree.map(
            lambda first_pick, second_pick: jnp.where(at_first, first_pick, second_pick),
            row_sets[index_m + 1],
            row_sets[index_m],
        )
        for index_m in range(micro_count)
    ]
    merged = jax.tree.map(lambda *pieces: jnp.concatenate(pieces, axis=0), *picked)
    (
        gain_attn_terms,
        normed_low,
        grad_query_low,
        grad_key_low,
        grad_value_low,
        token_mixed,
        grad_branch_low,
        gain_mlp_terms,
        normed_mlp_low,
        grad_gate_low,
        grad_up_low,
        act_low,
        grad_out_low,
    ) = merged
    grad_pairs = (
        (gain_attn_terms, None),
        (normed_low, grad_query_low),
        (normed_low, grad_key_low),
        (normed_low, grad_value_low),
        (token_mixed, grad_branch_low),
        (gain_mlp_terms, None),
        (normed_mlp_low, grad_gate_low),
        (normed_mlp_low, grad_up_low),
        (act_low, grad_out_low),
    )
    shares = tuple(
        (
            lax.psum_scatter(
                weight_term(left_side, right_side).astype(jnp.bfloat16),
                "blk",
                scatter_dimension=0,
                tiled=True,
            ).astype(jnp.float32)
            for left_side, right_side in grad_pairs
        )
    )
    shares = jax.tree.map(lambda part: part.astype(jnp.float32), lax.psum(shortened(shares), "seq"))
    return (
        activations,
        input_grads,
        shares[0][None],
        shares[1][None],
        shares[2][None],
        shares[3][None],
        shares[4][None],
        shares[5][None],
        shares[6][None],
        shares[7][None],
        shares[8][None],
    )


MESH = pl.DeviceIdType.MESH


def remote(source, target, sent, arrived, device):
    return pltpu.make_async_remote_copy(
        source, target, sent, arrived, device_id=device, device_id_type=MESH
    )


def greet(partners):
    barrier = pltpu.get_barrier_semaphore()
    for device in partners:
        pl.semaphore_signal(barrier, 1, device_id=device, device_id_type=MESH)
    pl.semaphore_wait(barrier, len(partners))


def settled(spot, semaphore, received):
    copy = remote(spot, spot, semaphore, semaphore, {"seq": lax.axis_index("seq") ^ 1})
    if received:
        copy.wait_recv()
    else:
        copy.wait_send()


CUTS = 2


def gather_steps(
    count, own, out, line_sent, line_got, side_sent, side_got, core_sent, core_got, local_done
):
    seq, b = lax.axis_index("seq"), lax.axis_index("blk")
    core, side = {"seq": seq ^ 1}, {"seq": seq ^ 2}
    base, side_base = seq * count, (seq ^ 2) * count
    cut = out.shape[1] // CUTS

    def spot(index, h):
        return out.at[index, pl.ds(h * cut, cut)]

    def begin(index, h, first):
        return own.at[pl.ds(h * cut, cut)] if first else spot(index, h)

    def along_line(j, way, h, first=False):
        device = {"blk": b + (1 if way else -1)}
        return remote(
            begin(base + j, h, first),
            spot(base + j, h),
            line_sent.at[j, way, h],
            line_got.at[j, h],
            device,
        )

    def to_side(j, h, first=False):
        return remote(
            begin(base + j, h, first),
            spot(base + j, h),
            side_sent.at[j, h],
            side_got.at[j, h],
            side,
        )

    def to_core(half, j, h, first=False):
        index = (side_base if half else base) + j
        return remote(
            begin(index, h, first),
            spot(index, h),
            core_sent.at[half, j, h],
            core_got.at[half, j, h],
            core,
        )

    local = pltpu.make_async_copy(own, out.at[base + b], local_done)
    local.start()
    for h in range(CUTS):
        to_side(b, h, True).start()
        pl.when(b > 0)(along_line(b, 0, h, True).start)
        pl.when(b < count - 1)(along_line(b, 1, h, True).start)
    for h in range(CUTS):
        to_core(0, b, h, True).start()
    yield "sent"

    def from_line(j, way):
        for h in range(CUTS):
            settled(spot(base + j, h), line_got.at[j, h], True)
            pl.when((b < count - 1) if way else (b > 0))(along_line(j, way, h).start)
            to_side(j, h).start()
        for h in range(CUTS):
            to_core(0, j, h).start()

    def from_side(j):
        for h in range(CUTS):
            settled(spot(side_base + j, h), side_got.at[j, h], True)
            to_core(1, j, h).start()

    for k in range(1, count + 1):
        if k < count:
            pl.when(b - k >= 0)(functools.partial(from_line, b - k, 1))
            pl.when(b + k < count)(functools.partial(from_line, b + k, 0))
        if k == 1:
            from_side(b)
        else:
            pl.when(b - k + 1 >= 0)(functools.partial(from_side, b - k + 1))
            pl.when(b + k - 1 < count)(functools.partial(from_side, b + k - 1))
        if k == count - 1:
            local.wait()
        yield "line" if k == count - 1 else "side" if k == count else "step"
    for half, corner in ((0, seq ^ 1), (1, seq ^ 3)):
        for j in range(count):
            for h in range(CUTS):
                settled(spot(corner * count + j, h), core_got.at[half, j, h], True)
        yield "corner" if half else "near"
    yield "done"
    for h in range(CUTS):
        for j in range(count):
            to_side(j, h).wait_send()
            to_core(0, j, h).wait_send()
            to_core(1, j, h).wait_send()
        pl.when(b > 0)(along_line(b, 0, h).wait_send)
        pl.when(b < count - 1)(along_line(b, 1, h).wait_send)
        for k in range(1, count):
            pl.when((b - k >= 0) & (b < count - 1))(along_line(b - k, 1, h).wait_send)
            pl.when((b + k < count) & (b > 0))(along_line(b + k, 0, h).wait_send)


def gather_semaphores(count):
    dma = pltpu.SemaphoreType.DMA
    return [
        dma((count, 2, CUTS)),
        dma((count, CUTS)),
        dma((count, CUTS)),
        dma((count, CUTS)),
        dma((2, count, CUTS)),
        dma((2, count, CUTS)),
        dma,
    ]


def line_steps(
    count, own, out, line_sent, line_got, core_sent, core_got, local_done, offset=0
):
    seq, b = lax.axis_index("seq"), lax.axis_index("blk")
    core, base = {"seq": seq ^ 1}, offset + (seq % 2) * count
    cut = out.shape[1] // CUTS

    def spot(j, h):
        return out.at[base + j, pl.ds(h * cut, cut)]

    def begin(j, h, first):
        return own.at[pl.ds(h * cut, cut)] if first else spot(j, h)

    def along_line(j, way, h, first=False):
        device = {"blk": b + (1 if way else -1)}
        return remote(
            begin(j, h, first), spot(j, h), line_sent.at[j, way, h], line_got.at[j, h], device
        )

    def to_core(j, h, first=False):
        return remote(begin(j, h, first), spot(j, h), core_sent.at[j, h], core_got.at[j, h], core)

    local = pltpu.make_async_copy(own, out.at[base + b], local_done)
    local.start()
    for h in range(CUTS):
        pl.when(b > 0)(along_line(b, 0, h, True).start)
        pl.when(b < count - 1)(along_line(b, 1, h, True).start)
        to_core(b, h, True).start()
    yield

    def from_line(j, way):
        for h in range(CUTS):
            settled(spot(j, h), line_got.at[j, h], True)
            pl.when((b < count - 1) if way else (b > 0))(along_line(j, way, h).start)
            to_core(j, h).start()

    for k in range(1, count):
        pl.when(b - k >= 0)(functools.partial(from_line, b - k, 1))
        pl.when(b + k < count)(functools.partial(from_line, b + k, 0))
        yield
    local.wait()
    for h in range(CUTS):
        for j in range(count):
            place = offset + (1 - seq % 2) * count + j
            settled(out.at[place, pl.ds(h * cut, cut)], core_got.at[j, h], True)
            to_core(j, h).wait_send()
        pl.when(b > 0)(along_line(b, 0, h).wait_send)
        pl.when(b < count - 1)(along_line(b, 1, h).wait_send)
        for k in range(1, count):
            pl.when((b - k >= 0) & (b < count - 1))(along_line(b - k, 1, h).wait_send)
            pl.when((b + k < count) & (b > 0))(along_line(b + k, 0, h).wait_send)


def line_semaphores(count):
    dma = pltpu.SemaphoreType.DMA
    return [
        dma((count, 2, CUTS)),
        dma((count, CUTS)),
        dma((count, CUTS)),
        dma((count, CUTS)),
        dma,
    ]


def advance(steps, times):
    for _ in range(times):
        next(steps, None)


def until_done(steps):
    for event in steps:
        if event == "done":
            return
        yield event


def all_but_last(compute):
    groups = []

    def some(group):
        groups.append(group)
        if len(groups) < 4:
            compute(group)

    return some


def group_of(event):
    seq = lax.axis_index("seq")
    return {"line": seq, "side": seq ^ 2, "near": seq ^ 1, "corner": seq ^ 3}.get(event)


def scatter_steps(
    count,
    partial,
    deliver,
    core_slot,
    side_slot,
    line_slot,
    side_out,
    line_out,
    running,
    core_sent,
    core_got,
    side_sent,
    side_got,
    line_sent,
    line_got,
    compute=None,
):
    seq, b = lax.axis_index("seq"), lax.axis_index("blk")
    core, side = {"seq": seq ^ 1}, {"seq": seq ^ 2}
    place = far_first(b, count)
    size = partial.shape[1] // CUTS
    cuts = [pl.ds(h * size, size) for h in range(CUTS)]

    def to_core(half, k, h):
        return remote(
            partial.at[(seq ^ (1 if half else 3)) * count + place[k], cuts[h]],
            core_slot.at[half, k, cuts[h]],
            core_sent.at[half, k, h],
            core_got.at[half, k, h],
            core,
        )

    def to_side(k, h):
        return remote(
            side_out.at[k, cuts[h]],
            side_slot.at[k, cuts[h]],
            side_sent.at[k, h],
            side_got.at[k, h],
            side,
        )

    def along_line(k, way, h):
        j = place[k]
        return remote(
            line_out.at[k, cuts[h]],
            line_slot.at[way, j, cuts[h]],
            line_sent.at[k, h],
            line_got.at[way, j, h],
            {"blk": b + (1 if way else -1)},
        )

    def add_from(way, j, h):
        settled(line_slot.at[way, j, cuts[h]], line_got.at[way, j, h], True)
        running[cuts[h]] += line_slot[way, j, cuts[h]].astype(jnp.float32)

    def exchange(half):
        if compute:
            compute(seq ^ (1 if half else 3))
        for k in range(count):
            for h in range(CUTS):
                to_core(half, k, h).start()

    exchange(0)
    if compute:
        compute(seq ^ 2)
    for k in range(count):
        for h in range(CUTS):
            to_core(0, k, h).wait_recv()
            total = partial[(seq ^ 2) * count + place[k], cuts[h]].astype(jnp.float32)
            total += core_slot[0, k, cuts[h]].astype(jnp.float32)
            side_out[k, cuts[h]] = total.astype(jnp.bfloat16)
            to_side(k, h).start()
    exchange(1)
    if compute:
        compute(seq)
    yield
    for k in range(count):
        j = place[k]
        rightward, leftward = j >= b, j <= b
        for h in range(CUTS):
            to_core(1, k, h).wait_recv()
            to_side(k, h).wait_recv()
            total = partial[seq * count + j, cuts[h]].astype(jnp.float32)
            total += core_slot[1, k, cuts[h]].astype(jnp.float32)
            running[cuts[h]] = total + side_slot[k, cuts[h]].astype(jnp.float32)
            pl.when(rightward & (b > 0))(functools.partial(add_from, 1, j, h))
            pl.when(leftward & (b < count - 1))(functools.partial(add_from, 0, j, h))
            if k < count - 1:
                line_out[k, cuts[h]] = running[cuts[h]].astype(jnp.bfloat16)
                pl.when(rightward)(along_line(k, 1, h).start)
                pl.when(jnp.logical_not(rightward))(along_line(k, 0, h).start)
        if k < count - 1:
            yield
    deliver(running[...])
    yield
    for k in range(count):
        for h in range(CUTS):
            to_core(0, k, h).wait_send()
            to_core(1, k, h).wait_send()
            to_side(k, h).wait_send()
            if k < count - 1:
                settled(line_out.at[k, cuts[h]], line_sent.at[k, h], False)


def line_first_steps(
    count,
    partial,
    deliver,
    own,
    core_slot,
    line_slot,
    line_out,
    side_slot,
    running,
    own_done,
    core_sent,
    core_got,
    line_sent,
    line_got,
    side_sent,
    side_got,
):
    seq, b = lax.axis_index("seq"), lax.axis_index("blk")
    core, side = {"seq": seq ^ 1}, {"seq": seq ^ 2}
    place = far_first(b, count)

    def to_core(half, k):
        source = partial.at[(seq ^ (1 if half else 3)) * count + place[k]]
        return remote(
            source, core_slot.at[half, k], core_sent.at[half, k], core_got.at[half, k], core
        )

    def kept(half, k):
        source = partial.at[(seq if half else seq ^ 2) * count + place[k]]
        return pltpu.make_async_copy(source, own.at[half, k], own_done.at[half, k])

    def along_line(half, k, way):
        j = place[k]
        return remote(
            line_out.at[half, k],
            line_slot.at[half, way, j],
            line_sent.at[half, k],
            line_got.at[half, way, j],
            {"blk": b + (1 if way else -1)},
        )

    def add_from(half, way, j):
        settled(line_slot.at[half, way, j], line_got.at[half, way, j], True)
        running[...] += line_slot[half, way, j].astype(jnp.float32)

    to_side = remote(line_out.at[0, count - 1], side_slot.at[0], side_sent, side_got, side)
    for half in range(2):
        for k in range(count):
            kept(half, k).start()
            to_core(half, k).start()
    yield
    for k in range(count):
        j = place[k]
        rightward, leftward = j >= b, j <= b
        for half in range(2):
            kept(half, k).wait()
            to_core(half, k).wait_recv()
            running[...] = own[half, k].astype(jnp.float32) + core_slot[half, k].astype(jnp.float32)
            pl.when(rightward & (b > 0))(functools.partial(add_from, half, 1, j))
            pl.when(leftward & (b < count - 1))(functools.partial(add_from, half, 0, j))
            if half == 0 or k < count - 1:
                line_out[half, k] = running[...].astype(jnp.bfloat16)
            if k < count - 1:
                pl.when(rightward)(along_line(half, k, 1).start)
                pl.when(jnp.logical_not(rightward))(along_line(half, k, 0).start)
            elif half == 0:
                to_side.start()
            else:
                to_side.wait_recv()
                deliver(running[...] + side_slot[0].astype(jnp.float32))
            yield
    to_side.wait_send()
    for half in range(2):
        for k in range(count):
            to_core(half, k).wait_send()
            if k < count - 1:
                settled(line_out.at[half, k], line_sent.at[half, k], False)


def far_first(b, count):
    order = sorted(range(count), key=lambda j: -j)
    places = []
    for k in range(count):
        place = 0
        for own in range(count):
            by_distance = sorted(order, key=lambda j: (-abs(j - own), -j if own * 2 < count else j))
            place = jnp.where(b == own, by_distance[k], place)
        places.append(place)
    return places


def scatter_scratch(count, rows, width):
    dma = pltpu.SemaphoreType.DMA

    def slots(*places):
        return pltpu.VMEM(places + (rows, width), jnp.bfloat16)

    return [
        slots(2, count),
        slots(count),
        slots(2, count),
        slots(count),
        slots(count - 1),
        pltpu.VMEM((rows, width), jnp.float32),
        dma((2, count, CUTS)),
        dma((2, count, CUTS)),
        dma((count, CUTS)),
        dma((count, CUTS)),
        dma((count - 1, CUTS)),
        dma((2, count, CUTS)),
    ]


def run_all(fillers):
    for filler in fillers:
        filler()


def run_with(steps, fillers):
    fillers = list(fillers)
    for _ in steps:
        if fillers:
            fillers.pop(0)()
    for filler in fillers:
        filler()


def greet_group(count, more=()):
    seq, b = lax.axis_index("seq"), lax.axis_index("blk")
    greet(
        tuple(more)
        + ({"seq": seq ^ 1}, {"seq": seq ^ 2})
        + tuple({"blk": lax.rem(b + k, count)} for k in range(1, count))
    )


def carry(copies, from_section, what):
    sending = lax.axis_index("section") == from_section
    for copy in copies:
        if what == "start":
            pl.when(sending)(copy.start)
        else:
            pl.when(sending)(copy.wait_send)
            pl.when(jnp.logical_not(sending))(copy.wait_recv)


def carried(sources, targets, sent, got):
    other = {"section": 1 - lax.axis_index("section")}
    return [
        remote(source, target, sent.at[n], got.at[n], other)
        for n, (source, target) in enumerate(zip(sources, targets))
    ]


def group_rows(ref, group, count):
    value = ref[pl.ds(group * count, count)]
    return value.reshape(value.shape[0] * value.shape[1], value.shape[2])


def group_span(group, count, block):
    size = count * block
    return pl.ds(pl.multiple_of(group * size, size), size)


def lane_turn(field_in, cosine, sine):
    half_dim, lanes = HEAD_DIM // 2, field_in.shape[-1]
    lane = lax.broadcasted_iota(jnp.int32, field_in.shape, 1)
    partner = jnp.where(
        lane < half_dim,
        pltpu.roll(field_in, lanes - half_dim, 1),
        pltpu.roll(field_in, half_dim, 1),
    )
    return field_in * cosine + partner * sine


def masked_scores(query, key, first_row, start):
    scores = back_product(query, key) * HEAD_DIM ** (-0.5)
    key_index = lax.broadcasted_iota(jnp.int32, scores.shape, 1)
    query_index = first_row + lax.broadcasted_iota(jnp.int32, scores.shape, 0)
    return jnp.where((key_index >= start) & (key_index <= query_index), scores, MASKED)


def normalise(field_in, gain_row):
    inv_root = lax.rsqrt(jnp.mean(field_in * field_in, axis=-1, keepdims=True) + EPS)
    return field_in * inv_root * gain_row


PAD = 128


GAINS = HEAD_DIM
OWN_PART = HEAD_DIM + 16


def load_weights(layer, attn, twin, out, attn_vm, out_vm, sems):
    on_key = lax.axis_index("seq") % 2 == 0
    own, other = attn.at[layer, pl.ds(OWN_PART, HEAD_DIM)], twin.at[layer]

    def part(source, n, rows):
        return pltpu.make_async_copy(source, attn_vm.at[pl.ds(n * PAD, rows)], sems.at[n])

    copies = [
        part(attn.at[layer, pl.ds(0, HEAD_DIM)], 0, HEAD_DIM),
        part(attn.at[layer, pl.ds(GAINS, 16)], 3, 16),
    ]
    if out is not None:
        copies.append(
            pltpu.make_async_copy(out.at[layer], out_vm.at[pl.ds(0, HEAD_DIM)], sems.at[4])
        )
    start_all(copies)

    @pl.when(on_key)
    def _():
        part(own, 1, HEAD_DIM).start()
        part(other, 2, HEAD_DIM).start()

    @pl.when(jnp.logical_not(on_key))
    def _():
        part(other, 1, HEAD_DIM).start()
        part(own, 2, HEAD_DIM).start()

    return copies + [part(other, 1, HEAD_DIM), part(other, 2, HEAD_DIM)]


def clear_pads(attn_vm, out_vm):
    empty = jnp.zeros((PAD - HEAD_DIM, attn_vm.shape[1]), jnp.bfloat16)
    for part in range(3):
        attn_vm[part * PAD + HEAD_DIM : (part + 1) * PAD] = empty
    out_vm[HEAD_DIM:PAD] = empty


def attention_rows(heads, log_total, start, size, tokens):
    for i in range(tokens // size):
        here, seen = slice(i * size, (i + 1) * size), slice(0, (i + 1) * size)
        scores = masked_scores(heads[0, here], heads[1, seen], i * size, start[here])
        row_top = jnp.max(scores, axis=-1, keepdims=True)
        weights = jnp.exp(scores - row_top)
        total = jnp.sum(weights, axis=-1, keepdims=True)
        log_total[here] = row_top + jnp.log(total)
        weights = (weights * (1.0 / total)).astype(jnp.bfloat16)
        heads[3, here] = product(weights, heads[2, seen]).astype(jnp.bfloat16)


def project_heads(normed, attn_vm, heads, span, cosine, sine):
    mixed = back_product(normed, attn_vm[0 : 3 * PAD])
    cos_rows, sin_rows = cosine[span], sine[span]
    heads[0, span] = lane_turn(mixed[:, :PAD], cos_rows, sin_rows).astype(jnp.bfloat16)
    heads[1, span] = lane_turn(mixed[:, PAD : 2 * PAD], cos_rows, sin_rows).astype(jnp.bfloat16)
    heads[2, span] = mixed[:, 2 * PAD :].astype(jnp.bfloat16)


def keep_group(partial, group, value, count):
    block = partial.shape[1]
    partial[pl.ds(group * count, count)] = value.astype(jnp.bfloat16).reshape(count, block, -1)


def gain_of(ref, row):
    return ref[3 * PAD : 3 * PAD + 16][row : row + 1].astype(jnp.float32)


def fill_tables(lengths, frequency, cosine, sine, start):
    section = lax.axis_index("section")
    token = lax.broadcasted_iota(jnp.int32, start.shape, 0)
    end, begin = 0, jnp.zeros(start.shape, jnp.int32)
    for n in range(lengths.shape[2]):
        length = lengths[section, 0, n]
        end = end + length
        begin = begin + jnp.where(end <= token, length, 0)
    start[...] = begin
    lane = lax.broadcasted_iota(jnp.int32, cosine.shape, 1)
    angles = (token - begin).astype(jnp.float32) * frequency[...]
    cosine[...] = jnp.where(lane < HEAD_DIM, jnp.cos(angles), 0.0)
    turned = jnp.where(lane < HEAD_DIM, jnp.sin(angles), 0.0)
    sine[...] = jnp.where(lane < HEAD_DIM // 2, -turned, turned)


def first_layer_kernel(count, *refs):
    refs = iter(refs)

    def take(n):
        return [next(refs) for _ in range(n)]

    w_query, w_key, w_value, w_gate, w_up, w_output, w_down = take(7)
    gain_attn, gain_mlp, inputs, cotangent, lengths, frequency = take(6)
    attn, twin, gate_up, out, down, all_rows, wide_rows, grads_near, grads_side = take(9)
    cosine, sine, start = take(3)
    gain_rows = take(4)
    hidden, result_out, normed_out, heads, log_total = take(5)
    raw_vm, normed_vm, rows_vm, partial, partial_two, grads_vm = take(6)
    attn_vm, out_vm, wide_vm, down_vm, units, normed_own, gain_vm = take(7)
    pieces, query_vm, other_vm, query_turned, other_turned, weights_done = take(6)
    roots, load_done, save_done, twin_sent, twin_got = take(5)
    spread_sems = take(5)
    first_sems, second_sems, grads_sems, side_sems = take(7), take(7), take(5), take(2)
    scatter_one, scatter_two = take(12), take(12)
    section = lax.axis_index("section")
    block, width = raw_vm.shape[1], raw_vm.shape[2]
    tokens = block * raw_vm.shape[0]
    size = count * block
    low, f32 = jnp.bfloat16, jnp.float32
    seq = lax.axis_index("seq")
    rows_in, grads_in = inputs.at[section, 0], cotangent.at[section, 0]
    query_load = pltpu.make_async_copy(w_query, query_vm, weights_done.at[0])
    query_load.start()
    key_load = pltpu.make_async_copy(w_key, other_vm, weights_done.at[1])
    value_load = pltpu.make_async_copy(w_value, other_vm, weights_done.at[1])
    pl.when(seq % 2 == 0)(key_load.start)
    pl.when(seq % 2 == 1)(value_load.start)
    greet_group(count, ({"section": 1 - section},))
    steps = gather_steps(count, rows_in, raw_vm, *first_sems)
    next(steps)
    query_load.wait()
    key_load.wait()
    query_turned[...] = query_vm[...].astype(f32).T.astype(low)
    other_turned[...] = other_vm[...].astype(f32).T.astype(low)
    row = lax.broadcasted_iota(jnp.int32, (16, gain_attn.shape[1]), 0)
    own_gains = jnp.where(row == 0, gain_attn[...], jnp.where(row == 1, gain_mlp[...], 0))
    per_blk = other_turned.shape[0] // HEAD_DIM // count
    for j in range(count):
        head = j * 4 + seq
        other_head = j * per_blk + seq * per_blk // 4
        for place, turned, index in (
            (0, query_turned, head),
            (OWN_PART, other_turned, other_head),
        ):
            rows = pl.ds(pl.multiple_of(index * HEAD_DIM, 16), HEAD_DIM)
            pieces[j, place : place + HEAD_DIM] = turned[rows]
        pieces[j, GAINS : GAINS + 16] = own_gains.astype(low)
    spread = spread_steps(
        count, pieces, w_gate, w_up, w_output, w_down, attn, gate_up, out, down, *spread_sems
    )
    next(spread)
    fill_tables(lengths, frequency, cosine, sine, start)
    clear_pads(attn_vm, out_vm)
    for event in until_done(steps):
        if event == "side":
            advance(spread, 3)
        group = group_of(event)
        if group is not None:
            span = pl.ds(group * count, count)
            raw = raw_vm[span].astype(f32)
            roots[span] = lax.rsqrt(jnp.mean(raw * raw, axis=-1, keepdims=True) + EPS)
    grads_across = remote(
        grads_in, grads_side, *side_sems, {"seq": lax.axis_index("seq") ^ 2}
    )
    grads_across.start()
    next(spread)
    pair = remote(
        attn.at[:, pl.ds(OWN_PART, HEAD_DIM)],
        twin,
        twin_sent,
        twin_got,
        {"seq": lax.axis_index("seq") ^ 1},
    )
    pair.start()
    pair.wait()
    gain_load = pltpu.make_async_copy(attn.at[1, pl.ds(GAINS, 16)], gain_vm, load_done.at[5])
    gain_load.start()
    wait_all(load_weights(0, attn, twin, None, attn_vm, out_vm, load_done) + [gain_load])
    for group in range(tokens // size):
        raw = raw_vm[group * count : (group + 1) * count].astype(f32)
        root = roots[group * count : (group + 1) * count]
        normed = (raw * root * gain_of(attn_vm, 0)[None]).astype(low)
        normed_vm[group * count : (group + 1) * count] = normed
        span = slice(group * size, (group + 1) * size)
        project_heads(normed.reshape(size, width), attn_vm, heads, span, cosine, sine)
    saves = [pltpu.make_async_copy(normed_vm, all_rows, save_done.at[0])]
    saves[0].start()
    attention_rows(heads, log_total, start, size, tokens)
    next(spread)
    load = pltpu.make_async_copy(out.at[0], out_vm.at[pl.ds(0, HEAD_DIM)], load_done.at[4])
    load.start()
    load.wait()

    def project_out(group):
        mixed = heads[3, group_span(group, count, block)]
        keep_group(partial, group, product(mixed, out_vm[...]), count)

    def deliver(total):
        value = rows_in[...].astype(f32) + total
        hidden[...] = value
        normed_own[...] = normalise(value, gain_of(attn_vm, 1)).astype(low)

    def more():
        next(spread)

    run_with(scatter_steps(count, partial, deliver, *scatter_one, compute=project_out), [more] * 5)
    for _ in steps:
        pass
    steps = gather_steps(count, normed_own, rows_vm, *second_sems)
    for number, event in enumerate(until_done(steps)):
        if number == 0:
            more()
    for _ in spread:
        pass
    loads = [
        pltpu.make_async_copy(gate_up.at[0], wide_vm, load_done.at[0]),
        pltpu.make_async_copy(down.at[0], down_vm, load_done.at[1]),
    ]
    start_all(loads)
    wait_all(loads)
    saves.append(pltpu.make_async_copy(rows_vm, wide_rows, save_done.at[1]))
    saves[1].start()

    def project_down(group):
        pre = product(group_rows(rows_vm, group, count), wide_vm[...])
        made = hidden_units(pre)
        units[group_span(group, count, block)] = made
        keep_group(partial_two, group, product(made, down_vm[...]), count)

    grad_steps = line_steps(count, grads_in, grads_vm, *grads_sems)
    next(grad_steps)

    for n in range(2):
        gain_rows[n][...] = gain_of(attn_vm, n)

    def deliver_two(total):
        made = (hidden[...] + total).astype(low)
        result_out[...] = made
        gain = gain_vm[...][0:1].astype(f32)
        gain_rows[2][...] = gain
        gain_rows[3][...] = gain_vm[...][1:2].astype(f32)
        normed_out[...] = normalise(made.astype(f32), gain).astype(low)

    run_with(
        scatter_steps(count, partial_two, deliver_two, *scatter_two, compute=project_down),
        [functools.partial(advance, grad_steps, 1)] * 3,
    )
    for _ in grad_steps:
        pass
    for _ in steps:
        pass
    saves.append(pltpu.make_async_copy(grads_vm, grads_near, save_done.at[2]))
    saves[2].start()
    grads_across.wait()
    wait_all(saves)


def spread_steps(
    count,
    pieces,
    w_gate,
    w_up,
    w_output,
    w_down,
    attn,
    gate_up,
    out,
    down,
    line_sent,
    line_got,
    cross_sent,
    cross_got,
    local_done,
):
    seq, b, section = lax.axis_index("seq"), lax.axis_index("blk"), lax.axis_index("section")
    seq_count = lax.axis_size("seq")
    other = {"section": 1 - section}
    rows, lanes = w_gate.shape[0], gate_up.shape[2] // 2
    turns = tuple(range(count // 2, 0, -1)) + tuple(range(count // 2 + 1, count))

    def source(kind, j):
        if kind == 0:
            return pieces.at[j]
        weight = w_gate if kind == 1 else w_up
        return weight.at[:, pl.ds(pl.multiple_of((j * seq_count + seq) * lanes, lanes), lanes)]

    def target(kind, j):
        if kind == 0:
            return attn.at[section, :, pl.ds(pl.multiple_of(j * rows, rows), rows)]
        return gate_up.at[
            section, pl.ds(pl.multiple_of(j * rows, rows), rows), pl.ds((kind - 1) * lanes, lanes)
        ]

    def along_line(kind, k):
        j = lax.rem(b + k, count)
        return remote(
            source(kind, j),
            target(kind, b),
            line_sent.at[kind, k],
            line_got.at[kind, k],
            {"blk": j},
        )

    def across(kind, j, slot, begin=None):
        spot = target(kind, j)
        return remote(
            spot if begin is None else begin,
            spot,
            cross_sent.at[kind, slot],
            cross_got.at[kind, slot],
            other,
        )

    def own_rows(kind):
        weight, place = (w_output, out) if kind == 3 else (w_down, down)
        size = place.shape[1]
        begin = weight.at[pl.ds(pl.multiple_of(seq * size, size), size)]
        spot = place.at[section]
        return (
            remote(begin, spot, cross_sent.at[kind, 0], cross_got.at[kind, 0], other),
            pltpu.make_async_copy(begin, spot, local_done.at[kind]),
        )

    def own_piece(kind):
        return (
            across(kind, b, 0, source(kind, b)),
            pltpu.make_async_copy(source(kind, b), target(kind, b), local_done.at[kind]),
        )

    def forward(kind, k):
        j = lax.rem(b + count - k, count)
        settled(target(kind, j), line_got.at[kind, k], True)
        across(kind, j, k).start()

    def arrived(kind):
        if kind > 2:
            wait_all(own_rows(kind))
            return
        for k in range(count):
            settled(target(kind, 0), cross_got.at[kind, k], True)
            settled(target(kind, 0), cross_sent.at[kind, k], False)
            if k:
                settled(target(kind, 0), line_sent.at[kind, k], False)
        pltpu.make_async_copy(source(kind, b), target(kind, b), local_done.at[kind]).wait()

    for k in turns:
        along_line(0, k).start()
    start_all(own_piece(0))
    yield
    for k in turns:
        forward(0, k)
        yield
    start_all(own_rows(3))
    for kind in (1, 2):
        for k in turns:
            along_line(kind, k).start()
    arrived(0)
    start_all(own_piece(1) + own_piece(2) + own_rows(4))
    yield
    arrived(3)
    yield
    for kind in (1, 2):
        for k in turns:
            forward(kind, k)
            yield
    for kind in (1, 2, 4):
        arrived(kind)


def start_all(copies):
    for copy in copies:
        copy.start()


def wait_all(copies):
    for copy in copies:
        copy.wait()


def gated(pre):
    half = pre.shape[1] // 2
    gate, up = pre[:, :half], pre[:, half:]
    sigma = jax.nn.sigmoid(gate)
    return gate, up, sigma


def hidden_units(pre):
    gate, up, sigma = gated(pre)
    return (gate * sigma * up).astype(jnp.bfloat16)


def store_gate_grads(place, span, grad_act, pre):
    gate, up, sigma = gated(pre)
    half = gate.shape[1]
    place[span, 0:half] = (grad_act * up * sigma * (1.0 + gate * (1.0 - sigma))).astype(
        jnp.bfloat16
    )
    place[span, half : 2 * half] = (grad_act * (gate * sigma)).astype(jnp.bfloat16)


def wide_grads(rows_vm, pre_grads, units, grads_vm, wide_grad, down_grad):
    tokens = pre_grads.shape[0]
    width = rows_vm.shape[2]
    step = width // 4

    def wide_part(n):
        cut = slice(n * step, (n + 1) * step)
        rows = rows_vm[:, :, cut].reshape(tokens, step)
        wide_grad[cut] = weight_term(rows, pre_grads[...]).astype(jnp.bfloat16)

    def down_part(n):
        cut = slice(n * 2 * step, (n + 1) * 2 * step)
        rows = grads_vm[:, :, cut].reshape(tokens, 2 * step)
        down_grad[:, cut] = weight_term(units[...], rows).astype(jnp.bfloat16)

    return [functools.partial(wide_part, n) for n in range(4)] + [
        functools.partial(down_part, n) for n in range(2)
    ]


def mlp_grad_sent(total, hidden, grads_own, gain, branch_out, grad_hidden_out, gain_out):
    field_in = hidden[...]
    inv_root = lax.rsqrt(jnp.mean(field_in * field_in, axis=-1, keepdims=True) + EPS)
    part, terms = rms_backward(field_in, gain[...], inv_root, total)
    grad_hidden = grads_own[...].astype(jnp.float32) + part
    grad_hidden_out[...] = grad_hidden
    branch_out[...] = grad_hidden.astype(jnp.bfloat16)
    gain_out[...] = jnp.broadcast_to(jnp.sum(terms, axis=0, keepdims=True), gain_out.shape)


class Parts:
    pass


def attn_back_refs(take, attn_grad=None, out_grad=None):
    r = Parts()
    r.branch_vm, r.rows_vm, r.heads, r.attn_vm, r.out_vm, r.mixed_grads, r.probs = take(7)
    r.key_grads, r.value_grads, r.joint, r.partial, r.load_done = take(5)
    r.gather_sems = take(7)
    r.scatter_refs = take(12)
    return r


def attn_back_body(
    count, layer, r, ins, outs, background, fillers, gathered=None, spare=None
):
    branch_in, grad_hidden, x_own, all_rows, heads_kept, log_total, attn, twin, out = ins[:9]
    cosine, sine, start, gain = ins[9:]
    grad_out, gain_out, attn_grad, out_grad = outs
    branch_vm, rows_vm, heads, attn_vm, out_vm = r.branch_vm, r.rows_vm, r.heads, r.attn_vm, r.out_vm
    mixed_grads, probs, key_grads, value_grads = r.mixed_grads, r.probs, r.key_grads, r.value_grads
    joint, partial, load_done = r.joint, r.partial, r.load_done
    block = rows_vm.shape[1]
    size = count * block
    tokens = block * rows_vm.shape[0]
    low, f32 = jnp.bfloat16, jnp.float32
    scale = HEAD_DIM ** (-0.5)
    steps = gather_steps(count, branch_in, branch_vm, *r.gather_sems)
    next(steps)
    background()
    loads = []
    if layer is not None:
        clear_pads(attn_vm, out_vm)
        loads = load_weights(layer, attn, twin, out, attn_vm, out_vm, load_done)
        kept = [
            pltpu.make_async_copy(heads_kept, heads, load_done.at[5]),
            pltpu.make_async_copy(all_rows, rows_vm, load_done.at[6]),
        ]
        start_all(kept)
        loads += kept
    key_grads[...] = jnp.zeros_like(key_grads)
    value_grads[...] = jnp.zeros_like(value_grads)
    wait_all(loads)

    def spans(i):
        return slice(i * size, (i + 1) * size), slice(0, (i + 1) * size)

    def weigh(i):
        here, seen = spans(i)
        scores = masked_scores(heads[0, here], heads[1, seen], i * size, start[here])
        probs[here, seen] = jnp.exp(scores - log_total[here])

    def project(group):
        value = back_product(group_rows(branch_vm, group, count), out_vm[...])
        mixed_grads[group_span(group, count, block)] = value.astype(low)

    for number, event in enumerate(until_done(steps)):
        if number < 2:
            weigh(2 * number)
            weigh(2 * number + 1)
        group = group_of(event)
        if group is not None:
            project(group)
    if gathered:
        gathered()
    for i in reversed(range(tokens // size)):
        here, seen = spans(i)
        weights = probs[here, seen]
        grads = mixed_grads[here]
        grad_weights = back_product(grads, heads[2, seen])
        centre = jnp.sum(weights * grad_weights, axis=-1, keepdims=True)
        grad_scores = (weights * (grad_weights - centre)).astype(low)
        query_grad = (product(grad_scores, heads[1, seen]) * scale).astype(low).astype(f32)
        joint[here, 0:PAD] = lane_turn(query_grad, cosine[here], -sine[here]).astype(low)
        key_grads[seen] += weight_term(grad_scores, heads[0, here])
        value_grads[seen] += weight_term(weights.astype(low), grads)
        key_grad = (key_grads[here] * scale).astype(low).astype(f32)
        joint[here, PAD : 2 * PAD] = lane_turn(key_grad, cosine[here], -sine[here]).astype(low)
        joint[here, 2 * PAD : 3 * PAD] = value_grads[here].astype(low)

    def project_back(group):
        value = product(joint[group_span(group, count, block)], attn_vm[0 : 3 * PAD])
        partial[pl.ds(group * count, count)] = value.astype(low).reshape(count, block, -1)

    def attn_part(part):
        rows = rows_vm[...].reshape(tokens, rows_vm.shape[2])
        value = weight_term(joint[:, part * PAD : (part + 1) * PAD], rows)
        attn_grad[part * HEAD_DIM : (part + 1) * HEAD_DIM] = value[0:HEAD_DIM].astype(low)

    def out_part():
        rows = branch_vm[...].reshape(tokens, branch_vm.shape[2])
        out_grad[...] = weight_term(heads[3], rows)[0:HEAD_DIM].astype(low)

    def deliver(total):
        field_in = x_own[...].astype(f32)
        inv_root = lax.rsqrt(jnp.mean(field_in * field_in, axis=-1, keepdims=True) + EPS)
        part, terms = rms_backward(field_in, gain[...], inv_root, total)
        grad_out[...] = (grad_hidden[...] + part).astype(low)
        gain_out[...] = jnp.broadcast_to(jnp.sum(terms, axis=0, keepdims=True), gain_out.shape)

    parts = [functools.partial(attn_part, n) for n in range(3)] + [out_part]
    if spare:
        parts.append(spare)
    run_with(
        scatter_steps(count, partial, deliver, *r.scatter_refs, compute=project_back),
        [functools.partial(run_all, parts)] + fillers,
    )
    for _ in steps:
        pass


def middle_kernel(count, *refs):
    refs = iter(refs)

    def take(n):
        return [next(refs) for _ in range(n)]

    rows_in, between, grads_side, cosine, sine, start, attn, twin, out = take(9)
    grads_near, gate_up, down, cotangent, hidden_one, wide_rows = take(6)
    grads_own = cotangent.at[lax.axis_index("section"), 0]
    gain_mlp_two, gain_attn_two, gain_mlp_one = take(3)
    hidden, ahead, grad_between, branch_out, grad_hidden_out = take(5)
    mlp_two_sum, attn_two_sum, mlp_one_sum = take(3)
    grads_kept = take(6)
    carried_to = take(4)
    rows_two, grads_vm, partial, wide_vm, down_vm = take(5)
    log_total, units, pre_vm, pre_grads, normed_own, branch_own, grad_hidden = take(7)
    load_done, carry_sent, carry_got, keep_done = take(4)
    wide_two, down_two, attn_two, out_two, wide_one, down_one = take(6)
    line_sems = take(5)
    r = attn_back_refs(take)
    rows_one, heads, attn_vm, out_vm, partial_back = (
        r.rows_vm,
        r.heads,
        r.attn_vm,
        r.out_vm,
        r.partial,
    )
    blocks, block = rows_one.shape[0], rows_one.shape[1]
    size, tokens, half = count * block, blocks * block, blocks // 2
    near = lax.axis_index("seq") // 2 * half
    greet_group(count, ({"section": 1 - lax.axis_index("section")},))
    steps = gather_steps(count, rows_in, rows_one, *r.gather_sems)
    next(steps)
    clear_pads(attn_vm, out_vm)
    loads = load_weights(1, attn, twin, out, attn_vm, out_vm, r.load_done)
    wide_loads = [
        pltpu.make_async_copy(gate_up.at[1], wide_vm, load_done.at[0]),
        pltpu.make_async_copy(down.at[1], down_vm, load_done.at[1]),
        pltpu.make_async_copy(grads_near, grads_vm.at[pl.ds(near, half)], load_done.at[2]),
    ]
    start_all(wide_loads)
    for event in until_done(steps):
        if event == "line":
            wait_all(loads)
        group = group_of(event)
        if group is not None:
            span = group_span(group, count, block)
            normed = group_rows(rows_one, group, count)
            project_heads(normed, attn_vm, heads, span, cosine, sine)
    grad_steps = line_steps(count, grads_side, grads_vm, *line_sems, offset=half - near)
    next(grad_steps)
    attention_rows(heads, log_total, start, size, tokens)

    def project_out(group):
        mixed = heads[3, group_span(group, count, block)]
        keep_group(partial, group, product(mixed, out_vm[...]), count)

    def deliver(total):
        value = between[...].astype(jnp.float32) + total
        hidden[...] = value
        normed_own[...] = normalise(value, gain_of(attn_vm, 1)).astype(jnp.bfloat16)

    run_with(
        scatter_steps(count, partial, deliver, *r.scatter_refs, compute=project_out),
        [functools.partial(advance, grad_steps, 1)] * 3,
    )
    for _ in steps:
        pass
    steps = gather_steps(count, normed_own, rows_two, *r.gather_sems)
    next(steps)
    for _ in grad_steps:
        pass
    wait_all(wide_loads)

    def through(group):
        span = group_span(group, count, block)
        pre = product(group_rows(rows_two, group, count), wide_vm[...])
        units[span] = hidden_units(pre)
        grad_act = back_product(group_rows(grads_vm, group, count), down_vm[...])
        store_gate_grads(pre_grads, span, grad_act, pre)
        keep_group(partial_back, group, back_product(pre_grads[span], wide_vm[...]), count)

    for event in until_done(steps):
        if event == "line":
            through(group_of(event))

    def project_down(group):
        value = product(units[group * size : (group + 1) * size], down_vm[...])
        partial[group * count : (group + 1) * count] = value.astype(jnp.bfloat16).reshape(
            count, block, -1
        )

    def deliver_two(total):
        mlp_grad_sent(
            total, hidden, grads_own, gain_mlp_two, branch_own, grad_hidden, mlp_two_sum
        )

    fillers = wide_grads(rows_two, pre_grads, units, grads_vm, wide_two, down_two)
    fillers += [functools.partial(project_down, group) for group in range(4)]
    run_with(
        scatter_steps(
            count, partial_back, deliver_two, *r.scatter_refs, compute=all_but_last(through)
        ),
        [functools.partial(run_all, fillers[n::4]) for n in range(4)],
    )
    for _ in steps:
        pass
    save = pltpu.make_async_copy(partial, ahead, load_done.at[3])
    save.start()
    copies = carried(
        (wide_two, down_two, attn_two, out_two), carried_to, carry_sent, carry_got
    )

    made = (wide_two, down_two, attn_two, out_two, wide_one, down_one)
    keeps = [
        pltpu.make_async_copy(begin, end, keep_done.at[n])
        for n, (begin, end) in enumerate(zip(made, grads_kept))
    ]

    def background():
        carry(copies[:2], 0, "start")
        start_all(keeps[:2])
        wide_loads[0] = pltpu.make_async_copy(gate_up.at[0], wide_vm, load_done.at[0])
        wide_loads[1] = pltpu.make_async_copy(down.at[0], down_vm, load_done.at[1])
        wide_loads[2] = pltpu.make_async_copy(wide_rows, rows_two, load_done.at[2])
        start_all(wide_loads)

    attn_back_body(
        count,
        None,
        r,
        (branch_own, grad_hidden, between, None, None, log_total, None, None, None)
        + (cosine, sine, start, gain_attn_two),
        (grad_between, attn_two_sum, attn_two, out_two),
        background,
        [],
    )
    carry(copies[2:], 0, "start")
    start_all(keeps[2:4])
    steps = gather_steps(count, grad_between, grads_vm, *r.gather_sems)
    next(steps)
    wait_all(wide_loads)

    def again(group):
        span = group_span(group, count, block)
        pre = product(group_rows(rows_two, group, count), wide_vm[...])
        pre_vm[span] = pre
        units[span] = hidden_units(pre)

    def through_one(group):
        span = group_span(group, count, block)
        grad_act = back_product(group_rows(grads_vm, group, count), down_vm[...])
        store_gate_grads(pre_grads, span, grad_act, pre_vm[span])
        keep_group(partial_back, group, back_product(pre_grads[span], wide_vm[...]), count)

    for number, event in enumerate(until_done(steps)):
        if number < 2:
            again(2 * number)
            again(2 * number + 1)
        if event == "line":
            through_one(group_of(event))

    def deliver_one(total):
        mlp_grad_sent(
            total, hidden_one, grad_between, gain_mlp_one, branch_out, grad_hidden_out, mlp_one_sum
        )

    run_with(
        scatter_steps(
            count, partial_back, deliver_one, *r.scatter_refs, compute=all_but_last(through_one)
        ),
        wide_grads(rows_two, pre_grads, units, grads_vm, wide_one, down_one),
    )
    for _ in steps:
        pass
    start_all(keeps[4:])
    carry(copies, 0, "wait")
    save.wait()
    wait_all(keeps)


def last_kernel(count, *refs):
    refs = iter(refs)

    def take(n):
        return [next(refs) for _ in range(n)]

    ins = take(13)
    ins[2] = ins[2].at[lax.axis_index("section"), 0]
    wide_one, down_one, attn_two, out_two, wide_two, down_two = take(6)
    wide_from_one, down_from_one, attn_from_one, out_from_one, ahead = take(5)
    gain_mlp_one, gain_attn_two, gain_mlp_two, between, grad_between, hidden = take(6)
    attn, out, gate, up, down, gains_out, rows_out, grads_out = take(8)
    final, grad_start = take(2)
    attn_grad, out_grad, gain_attn_one, gains = take(4)
    attn_own, out_own, wide_own, down_own, attn_in, out_in, wide_in, down_in = take(8)
    attn_slot, wide_slot = take(2)
    gain_in, gain_sum, gain_line, gain_part, gain_side, gain_core = take(6)
    load_done, cross_sent, cross_got, line_sent, line_got = take(5)
    side_sent, side_got, core_sent, core_got, local_done, small_sent, small_got = take(7)
    ahead_refs = take(13)
    r = attn_back_refs(take)
    seq, b, section = lax.axis_index("seq"), lax.axis_index("blk"), lax.axis_index("section")
    at_first = section == 0
    at_second = jnp.logical_not(at_first)
    core, side, other = {"seq": seq ^ 1}, {"seq": seq ^ 2}, {"section": 1 - section}
    greet((other, core, side) + tuple({"blk": lax.rem(b + k, count)} for k in range(1, count)))
    rows, lanes = attn.shape[2], gate.shape[1] // (4 * count)
    turns = tuple(range(count // 2, 0, -1)) + tuple(range(count // 2 + 1, count)) + (0,)
    f32, low = jnp.float32, jnp.bfloat16

    def piece_rows(kind, j):
        if kind == 0:
            return (slice(None), pl.ds(pl.multiple_of(j * rows, rows), rows))
        return (pl.ds(pl.multiple_of(j * rows, rows), rows),)

    pairs = {
        0: (attn_own, attn_in, attn_grad),
        1: (wide_own, wide_in, wide_one),
        2: (out_own, out_in, out_grad),
        3: (down_own, down_in, down_one),
    }
    sources = {
        0: (attn_grad, attn_two, attn_from_one),
        1: (wide_one, wide_two, wide_from_one),
        2: (out_grad, out_two, out_from_one),
        3: (down_one, down_two, down_from_one),
    }

    def load(kind):
        one, two, from_one = sources[kind]
        own, held, _ = pairs[kind]

        @pl.when(at_first)
        def _():
            pltpu.make_async_copy(one, own, load_done.at[kind, 0]).start()

        @pl.when(at_second)
        def _():
            pltpu.make_async_copy(two, own, load_done.at[kind, 0]).start()
            pltpu.make_async_copy(from_one, held, load_done.at[kind, 1]).start()

    def loaded(kind):
        own, held, _ = pairs[kind]
        pltpu.make_async_copy(own, own, load_done.at[kind, 0]).wait()
        pl.when(at_second)(pltpu.make_async_copy(held, held, load_done.at[kind, 1]).wait)

    def cross(kind, k):
        _, held, begin = pairs[kind]
        index = piece_rows(kind, lax.rem(b + k, count)) if kind < 2 else (slice(None),)
        return remote(
            begin.at[index], held.at[index], cross_sent.at[kind, k], cross_got.at[kind, k], other
        )

    def add_up(kind, k):
        own, held, _ = pairs[kind]
        pl.when(at_first)(cross(kind, k).wait_recv)
        index = piece_rows(kind, lax.rem(b + k, count)) if kind < 2 else (slice(None),)
        held[index] = (own[index].astype(f32) + held[index].astype(f32)).astype(low)

    def along_line(kind, k):
        j = lax.rem(b + k, count)
        slot = (attn_slot if kind == 0 else wide_slot).at[k]
        source = pairs[kind][1].at[piece_rows(kind, j)]
        return remote(source, slot, line_sent.at[kind, k], line_got.at[kind, k], {"blk": j})

    def places(kind, k, of_seq):
        if kind == 2:
            size = out_in.shape[0]
            return [out.at[pl.ds(pl.multiple_of(of_seq * size, size), size)]]
        if kind == 3:
            size = down_in.shape[0]
            return [down.at[pl.ds(pl.multiple_of(of_seq * size, size), size)]]
        head = lax.rem(b + count - k, count) * 4 + of_seq
        if kind == 0:
            return [attn.at[head]]
        column = pl.ds(pl.multiple_of(head * lanes, lanes), lanes)
        return [gate.at[:, column], up.at[:, column]]

    def numbered(kind, k, of_seq):
        base = {0: k, 1: count + 2 * k, 2: 3 * count, 3: 3 * count + 1}[kind]
        return [(base + n, spot) for n, spot in enumerate(places(kind, k, of_seq))]

    def made(kind, k):
        if kind > 1:
            return [pairs[kind][1].at[:]]
        if kind == 0:
            return [attn_in.at[piece_rows(0, b)] if k == 0 else attn_slot.at[k]]
        whole = (lambda cut: wide_in.at[piece_rows(1, b) + (cut,)]) if k == 0 else (
            lambda cut: wide_slot.at[k, :, cut]
        )
        return [whole(pl.ds(0, lanes)), whole(pl.ds(lanes, lanes))]

    def sends(kind, k):
        found = []
        for (n, spot), begin in zip(numbered(kind, k, seq), made(kind, k)):
            found.append(
                (
                    remote(begin, spot, side_sent.at[n], side_got.at[n], side),
                    remote(begin, spot, core_sent.at[0, n], core_got.at[0, n], core),
                    pltpu.make_async_copy(begin, spot, local_done.at[n]),
                )
            )
        return found

    def publish(kind, k):
        for copies in sends(kind, k):
            for copy in copies:
                copy.start()

    def passes(kind, k):
        return [
            remote(spot, spot, core_sent.at[1, n], core_got.at[1, n], core)
            for n, spot in numbered(kind, k, seq ^ 2)
        ]

    def from_line(kind, k):
        along_line(kind, k).wait_recv()
        publish(kind, k)

    def from_side(kind, k):
        for n, spot in numbered(kind, k, seq ^ 2):
            settled(spot, side_got.at[n], True)
        for copy in passes(kind, k):
            copy.start()

    def small(n, source, slot, device):
        return remote(source, slot, small_sent.at[n], small_got.at[n], device)

    swap_rest = small(4 + count, between, rows_out.at[section], other)
    swap_final = small(4 + count, final, rows_out.at[section], other)
    swap_between = small(0, grad_between, grads_out.at[section], other)
    swap_start = small(0, grad_start, grads_out.at[section], other)
    pl.when(at_second)(swap_rest.start)
    pl.when(at_first)(swap_between.start)
    wide_turns = [(1, k) for k in turns]
    crossings = [(3, 0)] + wide_turns + [(0, k) for k in turns] + [(2, 0)]

    def begin_cross(those):
        for kind, k in those:
            pl.when(at_second)(cross(kind, k).start)

    def background():
        begin_cross(crossings[: count + 1])
        load(3)
        load(1)

    def deliver(total):
        final[...] = (hidden[...] + total).astype(low)
        pl.when(at_first)(swap_final.start)
        rows_out[section] = jnp.where(at_first, between[...], final[...])

    def later():
        load(0)
        load(2)
        begin_cross(crossings[count + 1 :])

    def share(n):
        if n == 0:
            loaded(1)
        add_up(1, turns[n])
        along_line(1, turns[n]).start()

    def gathered():
        loaded(3)
        add_up(3, 0)
        publish(3, 0)

    def spare():
        later()
        share(0)

    def early():
        add_up(1, 0)
        publish(1, 0)

    ahead_steps = line_first_steps(count, ahead, deliver, *ahead_refs)
    attn_back_body(
        count,
        0,
        r,
        ins,
        (grad_start, gain_attn_one, attn_grad, out_grad),
        background,
        [functools.partial(share, 1), functools.partial(share, 2), early],
        gathered,
        spare,
    )
    pl.when(at_second)(swap_start.start)
    grads_out[section] = jnp.where(at_first, grad_start[...], grad_between[...])
    gains[0, 0:4] = gain_attn_one[0:4]
    gains[0, 4:8] = gain_mlp_one[4:8]
    gains[1, 0:4] = gain_attn_two[0:4]
    gains[1, 4:8] = gain_mlp_two[4:8]
    gain_cross = small(1, gains.at[1 - section], gain_in.at[:], other)
    gain_cross.start()

    def gain_piece(j):
        return gain_sum.at[:, pl.ds(pl.multiple_of(j * rows, rows), rows)]

    def gain_send(k):
        j = lax.rem(b + k, count)
        return small(3 + k, gain_piece(j), gain_line.at[k], {"blk": j})

    loaded(0)
    for k in turns[:-1]:
        add_up(0, k)
        along_line(0, k).start()
    from_line(1, turns[0])
    add_up(0, 0)
    publish(0, 0)
    from_line(1, turns[1])
    from_side(1, 0)
    loaded(2)
    add_up(2, 0)
    publish(2, 0)
    from_line(1, turns[2])
    next(ahead_steps)
    from_side(3, 0)
    from_side(1, turns[0])
    for k in turns[:-1]:
        from_line(0, k)
    from_side(0, 0)
    from_side(1, turns[1])
    gain_cross.wait_recv()
    gain_sum[...] = gains[section] + gain_in[...]
    for k in range(1, count):
        gain_send(k).start()
    advance(ahead_steps, 2)
    from_side(2, 0)
    from_side(1, turns[2])
    for k in range(1, count):
        gain_send(k).wait_recv()
    gain_part[...] = gain_sum[:, pl.ds(pl.multiple_of(b * rows, rows), rows)]
    for k in range(1, count):
        gain_part[...] += gain_line[k]
    gain_to_side = small(2, gain_part.at[:], gain_side.at[:], side)
    gain_to_side.start()
    advance(ahead_steps, 4)
    gain_to_side.wait_recv()
    gain_side[...] += gain_part[...]
    gain_to_core = small(3, gain_side.at[:], gain_core.at[:], core)
    gain_to_core.start()
    for _ in ahead_steps:
        pass
    for k in turns[:-1]:
        from_side(0, k)
    gain_to_core.wait_recv()
    gains_out[...] = gain_side[...] + gain_core[...]
    every = [(0, k) for k in range(count)] + [(1, k) for k in range(count)] + [(2, 0), (3, 0)]
    for kind, k in every:
        pl.when(at_second)(cross(kind, k).wait_send)
        if kind < 2 and k:
            along_line(kind, k).wait_send()
        for to_side, to_core, local in sends(kind, k):
            to_side.wait_send()
            to_core.wait_send()
            local.wait()
        for copy in passes(kind, k):
            copy.wait_send()
        for half, of_seq in ((0, seq ^ 1), (1, seq ^ 3)):
            for n, spot in numbered(kind, k, of_seq):
                settled(spot, core_got.at[half, n], True)
    swap_between.wait()
    swap_rest.wait()
    gain_cross.wait_send()
    for k in range(1, count):
        gain_send(k).wait_send()
    gain_to_side.wait_send()
    gain_to_core.wait_send()


def widen_kernel(pieces, *refs):
    attn, out, gate, up, down, rows_in, grads_in, gains = refs[:8]
    query, key, value, out_f, gate_f, up_f, down_f = refs[8:15]
    rows_out, grads_out, gain_attn, gain_mlp = refs[15:]
    f32 = jnp.float32
    out_f[...] = out[...].astype(f32)
    gate_f[...] = gate[...].astype(f32)
    up_f[...] = up[...].astype(f32)
    down_f[...] = down[...].astype(f32)

    @pl.when(pl.program_id(0) == 0)
    def _():
        rows_out[...] = rows_in[...]
        grads_out[...] = grads_in[...]
        gain_attn[...] = gains[0:1]
        gain_mlp[...] = gains[4:5]

    @pl.when(pl.program_id(0) < pieces)
    def _():
        parts, _, lanes = attn.shape
        copies = HEADS // KV_HEADS

        def heads(n):
            return attn[:, n * HEAD_DIM : (n + 1) * HEAD_DIM].astype(f32)

        query[...] = heads(0).reshape(parts * HEAD_DIM, lanes).T
        for n, place in ((1, key), (2, value)):
            total = heads(n).reshape(parts // copies, copies, HEAD_DIM, lanes).sum(1)
            place[...] = total.reshape(parts // copies * HEAD_DIM, lanes).T


def widen(attn, out, gate, up, down, rows_out, grads_out, gains):
    f32 = jnp.float32
    parts, heads, rows = attn.shape
    lanes = 128
    pieces = rows // lanes
    steps = 8
    width = parts * HEAD_DIM
    narrow = width * KV_HEADS // HEADS

    def rows_of(array):
        return pl.BlockSpec((array.shape[0] // steps, array.shape[1]), lambda i: (i, 0))

    def turned(columns):
        return pl.BlockSpec((lanes, columns), lambda i: (jnp.minimum(i, pieces - 1), 0))

    def whole(shape):
        return pl.BlockSpec(shape, lambda i: (0,) * len(shape))

    flat = [out, gate, up, down]
    swaps = [whole(rows_out.shape), whole(grads_out.shape)]
    gain = jax.ShapeDtypeStruct((1, rows), f32)
    taken = pl.BlockSpec((parts, heads, lanes), lambda i: (0, 0, jnp.minimum(i, pieces - 1)))
    shapes = [(rows, width), (rows, narrow), (rows, narrow)] + [array.shape for array in flat]
    return pl.pallas_call(
        functools.partial(widen_kernel, pieces),
        grid=(steps,),
        out_shape=[jax.ShapeDtypeStruct(shape, f32) for shape in shapes]
        + [jax.ShapeDtypeStruct(array.shape, array.dtype) for array in (rows_out, grads_out)]
        + [gain, gain],
        in_specs=[taken] + [rows_of(array) for array in flat] + swaps + [whole(gains.shape)],
        out_specs=[turned(width), turned(narrow), turned(narrow)]
        + [rows_of(array) for array in flat]
        + swaps
        + [whole((1, rows)), whole((1, rows))],
        compiler_params=pltpu.CompilerParams(vmem_limit_bytes=60 * 2**20),
        name="widen_gradients",
    )(attn, out, gate, up, down, rows_out, grads_out, gains)


def last_layer(count, operands, like, back_scratch):
    attn, out, wide, down, block, width, gain_rows = like
    low, f32 = jnp.bfloat16, jnp.float32
    seq_count = lax.axis_size("seq")
    rows = wide[0] // count
    lanes = wide[1] // 2
    parts = seq_count * count
    dma = pltpu.SemaphoreType.DMA
    vmem = pltpu.VMEM
    sends = 3 * count + 2
    heads = attn[0]
    small = (gain_rows, rows)

    def slots(*places):
        return vmem(places + (block, width), low)

    outputs = [
        ((parts, heads, rows), low, False),
        ((out[0] * seq_count, out[1]), low, False),
        ((rows, lanes * parts), low, False),
        ((rows, lanes * parts), low, False),
        ((down[0] * seq_count, down[1]), low, False),
        (small, f32, True),
        ((2, block, width), low, True),
        ((2, block, width), low, True),
    ]
    scratch = (
        [vmem((block, width), low), vmem((block, width), low)]
        + [vmem(attn, low), vmem(out, low), vmem((gain_rows, width), f32)]
        + [vmem((2, gain_rows, width), f32)]
        + [vmem(shape, low) for shape in (attn, out, wide, down)] * 2
        + [vmem((count, heads, rows), low), vmem((count, rows, 2 * lanes), low)]
        + [vmem((gain_rows, width), f32)] * 2
        + [vmem((count,) + small, f32)]
        + [vmem(small, f32)] * 3
        + [dma((4, 2)), dma((4, count)), dma((4, count)), dma((2, count)), dma((2, count))]
        + [dma((sends,)), dma((sends,)), dma((2, sends)), dma((2, sends)), dma((sends,))]
        + [dma((5 + count,)), dma((5 + count,))]
        + [slots(2, count), slots(2, count), slots(2, 2, count), slots(2, count), slots(1)]
        + [vmem((block, width), f32)]
        + [dma((2, count)), dma((2, count)), dma((2, count)), dma((2, count))]
        + [dma((2, 2, count)), dma, dma]
        + back_scratch
    )
    attn, out, gate, up, down, gains, rows_out, grads_out = call_kernel(
        functools.partial(last_kernel, count), "last_layer_back", 3, operands, outputs, scratch
    )
    return widen(attn, out, gate, up, down, rows_out, grads_out, gains)


def call_kernel(kernel, name, number, operands, outputs, scratch):
    in_vmem = pl.BlockSpec(memory_space=pltpu.VMEM)
    anywhere = pl.BlockSpec(memory_space=pl.ANY)
    places = {True: in_vmem, False: anywhere, None: pl.BlockSpec(memory_space=pltpu.SMEM)}
    return pl.pallas_call(
        kernel,
        out_shape=[jax.ShapeDtypeStruct(shape, dtype) for shape, dtype, _ in outputs],
        in_specs=[places[near] for _, near in operands],
        out_specs=[in_vmem if near else anywhere for _, _, near in outputs],
        scratch_shapes=scratch,
        compiler_params=pltpu.CompilerParams(
            collective_id=number, has_side_effects=True, vmem_limit_bytes=56 * 2**20
        ),
        name=name,
    )(*[array for array, _ in operands])


def head_shards(inputs, cotangent, doc_lengths, *params):
    seq_count, count = lax.axis_size("seq"), lax.axis_size("blk")
    low, f32 = jnp.bfloat16, jnp.float32
    vmem, dma = pltpu.VMEM, pltpu.SemaphoreType.DMA
    block, width = inputs.shape[2], inputs.shape[3]
    blocks = seq_count * count
    tokens = blocks * block
    local = tuple(weight[0] for weight in params)
    piece_shape = (count, 2 * HEAD_DIM + 16, local[1].shape[0])
    w_output, w_gate, w_up, w_down = local[4], local[6], local[7], local[8]
    rows = w_gate.shape[0]
    lanes = w_gate.shape[1] // blocks
    out_rows, down_rows = w_output.shape[0] // seq_count, w_down.shape[0] // seq_count
    lane = jnp.arange(PAD) % (HEAD_DIM // 2)
    frequency = (THETA ** (-2.0 * lane.astype(f32) / HEAD_DIM))[None]

    def all_blocks():
        return vmem((blocks, block, width), low)

    def scatter():
        return scatter_scratch(count, block, width)

    half_blocks = vmem((blocks // 2, block, width), low)
    half = ((blocks // 2, block, width), low, False)
    own_low, own_wide = ((block, width), low, True), ((block, width), f32, True)
    every = ((blocks, block, width), low, False)
    gain_rows, one_row = ((8, width), f32, True), ((1, width), f32, True)
    weights_vm = [vmem((3 * PAD + 16, width), low), vmem((PAD, width), low)]
    wide_vm, down_vm = vmem((width, 2 * lanes), low), vmem((down_rows, width), low)
    (
        attn,
        twin,
        gate_up,
        out,
        down,
        rows_one,
        wide_rows_one,
        grads_near,
        grads_side,
        cosine,
        sine,
        start,
        gain_attn_first,
        gain_mlp_first,
        gain_attn_second,
        gain_mlp_second,
        hidden_one,
        between,
        normed,
        heads_one,
        total_one,
    ) = call_kernel(
        functools.partial(first_layer_kernel, count),
        "first_layer",
        2,
        [(array, False) for array in local[1:4] + (w_gate, w_up, w_output, w_down)]
        + [(local[0][None], True), (local[5][None], True)]
        + [(inputs, True), (cotangent, True), (doc_lengths, None), (frequency, True)],
        [
            ((2, piece_shape[1], width), low, False),
            ((2, HEAD_DIM, width), low, False),
            ((2, width, 2 * lanes), low, False),
            ((2, out_rows, width), low, False),
            ((2, down_rows, width), low, False),
            every,
            every,
            half,
            ((block, width), low, False),
            ((tokens, PAD), f32, True),
            ((tokens, PAD), f32, True),
            ((tokens, 1), jnp.int32, True),
            one_row,
            one_row,
            one_row,
            one_row,
            own_wide,
            own_low,
            own_low,
            ((4, tokens, PAD), low, True),
            ((tokens, 1), f32, True),
        ],
        [all_blocks() for _ in range(5)]
        + [half_blocks]
        + weights_vm
        + [wide_vm, down_vm, vmem((tokens, lanes), low), vmem((block, width), low)]
        + [vmem((16, width), low), vmem(piece_shape, low)]
        + [vmem(local[1].shape, low), vmem(local[2].shape, low)]
        + [vmem(local[1].shape[::-1], low), vmem(local[2].shape[::-1], low), dma((2,))]
        + [vmem((blocks, block, 1), f32), dma((6,)), dma((3,)), dma, dma]
        + [dma((3, count)), dma((3, count)), dma((5, count)), dma((5, count)), dma((5,))]
        + gather_semaphores(count) * 2
        + line_semaphores(count)
        + [dma, dma]
        + scatter()
        + scatter(),
    )
    tables = [(cosine, True), (sine, True), (start, True)]
    back_scratch = (
        [all_blocks(), all_blocks(), vmem((4, tokens, PAD), low)]
        + weights_vm
        + [vmem((tokens, PAD), low), vmem((tokens, tokens), f32)]
        + [vmem((tokens, PAD), f32), vmem((tokens, PAD), f32), vmem((tokens, 3 * PAD), low)]
        + [all_blocks(), dma((7,))]
        + gather_semaphores(count)
        + scatter()
    )
    attn_shape, out_shape = (3 * HEAD_DIM, width), (HEAD_DIM, width)
    wide_shape, down_shape = (width, 2 * lanes), (down_rows, width)
    kept_shapes = [wide_shape, down_shape, attn_shape, out_shape, wide_shape, down_shape]
    (
        hidden_two,
        ahead,
        grad_between,
        branch,
        grad_hidden,
        gain_mlp_two,
        gain_attn_two,
        gain_mlp_one,
        wide_two,
        down_two,
        attn_two,
        out_two,
        wide_one,
        down_one,
        wide_from_one,
        down_from_one,
        attn_from_one,
        out_from_one,
    ) = call_kernel(
        functools.partial(middle_kernel, count),
        "second_layer",
        4,
        [(normed, True), (between, True), (grads_side, True)]
        + tables
        + [(attn, False), (twin, False), (out, False)]
        + [(grads_near, False), (gate_up, False), (down, False)]
        + [(cotangent, True), (hidden_one, True), (wide_rows_one, False)]
        + [(gain_mlp_second, True), (gain_attn_second, True), (gain_mlp_first, True)],
        [own_wide, every, own_low, own_low, own_wide, gain_rows, gain_rows, gain_rows]
        + [(shape, low, False) for shape in kept_shapes]
        + [(shape, low, False) for shape in (wide_shape, down_shape, attn_shape, out_shape)],
        [all_blocks(), all_blocks(), all_blocks(), wide_vm, down_vm]
        + [vmem((tokens, 1), f32), vmem((tokens, lanes), low), vmem((tokens, 2 * lanes), f32)]
        + [vmem((tokens, 2 * lanes), low), vmem((block, width), low), vmem((block, width), low)]
        + [vmem((block, width), f32), dma((4,)), dma((4,)), dma((4,)), dma((6,))]
        + [vmem(shape, low) for shape in kept_shapes]
        + line_semaphores(count)
        + back_scratch,
    )
    back_operands = (
        [(branch, True), (grad_hidden, True), (inputs, True)]
        + [(rows_one, False), (heads_one, False), (total_one, True)]
        + [(attn, False), (twin, False), (out, False)]
        + tables
        + [(gain_attn_first, True)]
    )
    query, key, value, out, gate, up, down, *swapped, gain_attn, gain_mlp = last_layer(
        count,
        back_operands
        + [(wide_one, False), (down_one, False), (attn_two, False), (out_two, False)]
        + [(wide_two, False), (down_two, False), (wide_from_one, False), (down_from_one, False)]
        + [(attn_from_one, False), (out_from_one, False), (ahead, False)]
        + [(gain_mlp_one, True), (gain_attn_two, True), (gain_mlp_two, True)]
        + [(between, True), (grad_between, True), (hidden_two, True)],
        (
            attn_shape,
            out_shape,
            wide_shape,
            down_shape,
            block,
            width,
            gain_rows[0][0],
        ),
        back_scratch,
    )
    return (
        swapped[0][None, :, None],
        swapped[1][None, :, None],
        gain_attn,
        query[None],
        key[None],
        value[None],
        out[None],
        gain_mlp,
        gate[None],
        up[None],
        down[None],
    )

def solution(mesh):
    placed = (
        P(None, None, ("seq", "blk"), None),
        P(None, None, ("seq", "blk"), None),
        P(),
        P("section", "blk"),
        P("section", "blk", None),
        P("section", "blk", None),
        P("section", "blk", None),
        P("section", "blk", None),
        P("section", "blk"),
        P("section", "blk", None),
        P("section", "blk", None),
        P("section", "blk", None),
    )
    one_head_each = mesh.shape["seq"] == 4 and mesh.shape["blk"] == HEADS // 4
    return jax.shard_map(
        head_shards if one_head_each else shards,
        mesh=mesh,
        in_specs=placed,
        out_specs=(
            P("section", None, None, ("seq", "blk"), None),
            P("section", None, None, ("seq", "blk"), None),
            P("section", "blk"),
            P("section", "blk", None),
            P("section", "blk", None),
            P("section", "blk", None),
            P("section", "blk", None),
            P("section", "blk"),
            P("section", "blk", None),
            P("section", "blk", None),
            P("section", "blk", None),
        ),
        check_vma=False,
    )
```
